32 devices in a mesh: expert: 2 (over x), context: 4 (over y, core), dp: 4 (over z).
Axes of the slice: x: 2, y: 2, z: 4, core: 2. Of those that a mesh axis runs over, the one named last changes fastest.
Arguments:
- hidden_in: bfloat16 [8, 1024, 1536], P(('expert', 'dp'), 'context'), may hold values from -6 to 6
- span_order: int32 [8, 8], P(('expert', 'dp')), may hold values from 0 to 7, each once within a row
- expert_ids: int32 [8, 1024, 4], P(('expert', 'dp'), 'context'), may hold values from 0 to 7, all different within a row
- priority: int32 [8, 1024, 4], P(('expert', 'dp'), 'context'), may hold values from 0 to 1023, as said below
- gain_attn: float32 [1536], replicated, may hold values from 0.1 to 1.9
- qkv_weight: bfloat16 [1536, 2048], replicated, may hold values from -0.15625 to 0.15625
- out_weight: bfloat16 [1536, 1536], replicated, may hold values from -0.625 to 0.625
- gain_ffn: float32 [1536], replicated, may hold values from 0.1 to 1.9
- router: bfloat16 [1536, 8], replicated, may hold values from -0.078125 to 0.078125
- in_weight: bfloat16 [8, 1536, 1536], P('expert'), may hold values from -0.15625 to 0.15625
- down_weight: bfloat16 [8, 1536, 768], P('expert'), may hold values from -0.4375 to 0.4375
- cotangent: bfloat16 [8, 1024, 1536], P(('expert', 'dp'), 'context'), may hold values from -6 to 6
Outputs:
- output: bfloat16 [8, 1024, 1536], P(('expert', 'dp'), 'context')
- input_grad: bfloat16 [8, 1024, 1536], P(('expert', 'dp'), 'context')
- gain_attn_grad: float32 [1536], P(('expert', 'context', 'dp'))
- qkv_grad: float32 [1536, 2048], P(('expert', 'context', 'dp'))
- out_proj_grad: float32 [1536, 1536], P(('expert', 'context', 'dp'))
- gain_ffn_grad: float32 [1536], P(('expert', 'context', 'dp'))
- router_grad: float32 [1536, 8], P(('expert', 'context', 'dp'))
- expert_in_grad: float32 [8, 1536, 1536], P('expert', ('context', 'dp'))
- expert_down_grad: float32 [8, 1536, 768], P('expert', ('context', 'dp'))
The draws below stay inside these ranges and needn't reach their ends.
Inputs may be any that keep to these rules, and one draw needn't show every extreme that they name: `priority`: within each device's block (256 stored rows of one sequence) the 4 entries of all its tokens are a permutation of 0 to 1023. `expert_ids`: each token names 4 different experts. `span_order`: each row is a permutation.
All inputs are finite; a program needn't handle non-finite values.
Results may differ from the reference program's by a relative error of at most 0.022.
Values may be sent and summed in bfloat16 or wider, within the bound.
A program may use at most 320 MiB of HBM per device.

```python
import math
import jax
import jax.numpy as jnp
from jax import lax

D = 1536
HEADS = 12
KV_HEADS = 2
HEAD = 128
FF = 768
TOP = 4
SPAN = 128
TOK_DEV = 256
SEQ = 1024
SEQS = 8
EXPERTS = 8
CAP = 144
N_CONTEXT = 4


def one_permutation(key):
    return jax.random.permutation(key, TOK_DEV * TOP)


def draw_priority(key, part):
    key = jax.random.fold_in(key, 7)
    blocks = SEQS * (SEQ // TOK_DEV)
    keys = jax.random.split(key, blocks)
    perms = jax.vmap(one_permutation)(keys)
    return perms.reshape(SEQS, SEQ, TOP).astype(jnp.int32)


def shard_levels(rng, shape, cuts, low, high):
    level = 1.0
    for position, shards_of in cuts:
        heights = jax.random.uniform(jax.random.fold_in(jax.random.fold_in(rng, 6), position), (shards_of,), jnp.float32, low / len(cuts), high / len(cuts))
        level = level * jnp.repeat(jnp.exp(heights), shape[position] // shards_of).reshape((-1,) + (1,) * (len(shape) - 1 - position))
    return level


def different_ones(own_key, rows, count, top, lift):
    ranking = jax.random.permutation(jax.random.fold_in(own_key, 1), count)
    favour = ranking
    for power in range(3):
        favour = favour * favour // count
    favour = favour * lift // count
    tickets = jax.random.randint(jax.random.fold_in(own_key, 2), (rows, count), 0, 4096) + favour
    holders = jax.random.permutation(jax.random.fold_in(own_key, 3), rows)[jnp.arange(count) % rows]
    tickets = jnp.where(jnp.arange(rows)[:, None] == holders[None, :], 1 << 14, tickets)
    merit = tickets * count + jnp.arange(count)
    return lax.top_k(merit.astype(jnp.int32), top)[1].astype(jnp.int32)


def scatter_about(key, extent, width, limit, cuts=(), held_as=jnp.bfloat16):
    values = width * jax.random.normal(key, extent, jnp.float32)
    if cuts:
        values = values * shard_levels(key, extent, cuts, -0.22, 0.18)
    return jnp.clip(values, -limit, limit).astype(held_as)


def setup_inputs(seed: int = 0) -> dict:
    arg_keys = jax.random.split(jax.random.key(seed), 13)
    hidden_in = scatter_about(arg_keys[0], (SEQS, SEQ, D), 1.0, 6.0, ((0, 8), (1, 4)))
    span_order = jax.vmap(lambda own: jax.random.permutation(own, 2 * N_CONTEXT))(jax.random.split(arg_keys[1], SEQS)).reshape((SEQS, 2 * N_CONTEXT)).astype(jnp.int32)
    expert_ids = different_ones(arg_keys[2], SEQS * SEQ, EXPERTS, TOP, 4096).reshape((SEQS, SEQ, TOP))
    priority = draw_priority(jax.random.fold_in(arg_keys[12], 71), 0)
    gain_attn = jnp.clip(1.0 + 0.18 * jax.random.normal(arg_keys[4], (D,), jnp.float32), 0.1, 1.9)
    qkv_weight = scatter_about(arg_keys[5], (D, (HEADS + 2 * KV_HEADS) * HEAD), D ** -0.5, 0.15625)
    out_weight = scatter_about(arg_keys[6], (D, HEADS * HEAD), (HEADS * HEAD // 16) ** -0.5, 0.625)
    gain_ffn = jnp.clip(1.0 + 0.18 * jax.random.normal(arg_keys[7], (D,), jnp.float32), 0.1, 1.9)
    router = scatter_about(arg_keys[8], (D, EXPERTS), (4 * D) ** -0.5, 0.078125)
    in_weight = scatter_about(arg_keys[9], (EXPERTS, D, 2 * FF), D ** -0.5, 0.15625, ((0, 2),))
    down_weight = scatter_about(arg_keys[10], (EXPERTS, D, FF), (FF // 4) ** -0.5, 0.4375, ((0, 2),))
    cotangent = scatter_about(arg_keys[11], (SEQS, SEQ, D), 1.0, 6.0, ((0, 8), (1, 4)))
    return dict(hidden_in=hidden_in, span_order=span_order, expert_ids=expert_ids, priority=priority, gain_attn=gain_attn, qkv_weight=qkv_weight, out_weight=out_weight, gain_ffn=gain_ffn, router=router, in_weight=in_weight, down_weight=down_weight, cotangent=cotangent)


ROPE_BASE = 1000000.0
NORM_EPS = 1e-06
MASKED = -1e+30
HIGHEST = lax.Precision.HIGHEST

@jax.custom_vjp
def low(v):
    return lax.optimization_barrier(v.astype(jnp.bfloat16)).astype(jnp.float32)

@jax.custom_vjp
def low_back(v):
    return v

def low_keep(v):
    return (low(v), None)

def low_pass(kept, grad):
    return (grad,)

def back_keep(v):
    return (v, None)

def back_low(kept, grad):
    return (low(grad),)
low.defvjp(low_keep, low_pass)
low_back.defvjp(back_keep, back_low)

def rms_norm(values, gain):
    return values * lax.rsqrt(lax.optimization_barrier(jnp.mean(values * values, axis=-1, keepdims=True)) + NORM_EPS) * gain

def rope_tables(positions):
    half_size = HEAD // 2
    freqs = ROPE_BASE ** (jnp.arange(half_size).astype(jnp.float32) * (-2.0 / HEAD))
    angles = positions[:, None] * freqs[None, :]
    return (jnp.cos(angles)[:, None, :], jnp.sin(angles)[:, None, :])

def rotate(values, cosine, sine):
    half_size = values.shape[-1] // 2
    first = values[..., :half_size]
    second = values[..., half_size:]
    return jnp.concatenate([first * cosine - second * sine, second * cosine + first * sine], axis=-1)

def softmax_last(scores):
    shifted = jnp.exp(scores - lax.optimization_barrier(jnp.max(scores, axis=-1, keepdims=True)))
    return shifted / lax.optimization_barrier(jnp.sum(shifted, axis=-1, keepdims=True))

def silu(values):
    return values / (1.0 + jnp.exp(-values))

def attend(queries, keys, values, positions):
    group = HEADS // KV_HEADS
    block = math.gcd(SEQ, 512)
    blocks = SEQ // block
    grouped = queries.reshape(blocks, block, KV_HEADS, group, HEAD)
    block_pos = positions.reshape(blocks, block)

    def one_block(item):
        query_blk, query_pos = item
        scores = low_back(jnp.einsum('qkgd,skd->kgqs', query_blk, keys, precision=HIGHEST))
        visible = positions[None, None, None, :] <= query_pos[None, None, :, None]
        weights = low(softmax_last(jnp.where(visible, scores, MASKED)))
        return jnp.einsum('kgqs,skd->qkgd', weights, values, precision=HIGHEST)
    result = lax.map(jax.checkpoint(one_block), (grouped, block_pos))
    return result.reshape(SEQ, HEADS * HEAD)

def route(block_ids, block_order):
    flat_ids = block_ids.reshape(-1).astype(jnp.int32)
    flat_order = block_order.reshape(-1).astype(jnp.int32)
    choose = (flat_ids[:, None] == jnp.arange(EXPERTS).astype(jnp.int32)[None, :]).astype(jnp.int32)
    ordered = jnp.zeros_like(choose).at[flat_order].set(choose)
    earlier = jnp.cumsum(ordered, axis=0, dtype=jnp.int32) - ordered
    ranks = lax.optimization_barrier(jnp.sum(earlier[flat_order] * choose, axis=1)).astype(jnp.int32)
    slots = jnp.where(ranks < CAP, flat_ids * CAP + ranks, EXPERTS * CAP)
    return slots.astype(jnp.int32)

def fill_slots(rows, slots):
    return jnp.zeros((EXPERTS * CAP, D), jnp.float32).at[slots].set(rows, mode='drop')

def pick_rows(table, slots):
    return table[slots]

def mixture(ffn_in, router_w, weights_in, weights_down, seq_ids, seq_order):
    logits = low_back(jnp.dot(ffn_in, router_w, precision=HIGHEST))
    chosen = jnp.take_along_axis(logits, seq_ids.astype(jnp.int32), axis=1)
    gates = softmax_last(chosen)
    slots = jax.vmap(route)(seq_ids.reshape(N_CONTEXT, TOK_DEV, TOP), seq_order.reshape(N_CONTEXT, TOK_DEV, TOP))
    pair_rows = low_back(jnp.repeat(ffn_in, TOP, axis=0)).reshape(N_CONTEXT, TOK_DEV * TOP, D)
    buffers = jax.vmap(fill_slots)(pair_rows, slots)
    buffers = buffers.reshape(N_CONTEXT, EXPERTS, CAP, D).transpose(1, 0, 2, 3).reshape(EXPERTS, N_CONTEXT * CAP, D)
    inner = low_back(jnp.einsum('erd,edf->erf', buffers, weights_in, precision=HIGHEST))
    hidden = low(silu(inner[..., :FF]) * inner[..., FF:])
    returned = low(low_back(jnp.einsum('erf,edf->erd', hidden, weights_down, precision=HIGHEST)))
    returned = returned.reshape(EXPERTS, N_CONTEXT, CAP, D).transpose(1, 0, 2, 3).reshape(N_CONTEXT, EXPERTS * CAP, D)
    padded = jnp.concatenate([returned, jnp.zeros((N_CONTEXT, 1, D), jnp.float32)], axis=1)
    picked = jax.vmap(pick_rows)(padded, slots).reshape(SEQ, TOP, D)
    return lax.optimization_barrier(jnp.sum(gates[:, :, None] * picked, axis=1))

def layer(hidden_in, gain_attn, qkv_weight, out_weight, gain_ffn, router, in_weight, down_weight, positions, seq_ids, seq_order):
    q_cols = HEADS * HEAD
    kv_cols = KV_HEADS * HEAD
    normed = low(rms_norm(hidden_in, gain_attn))
    mixed = low_back(jnp.dot(normed, qkv_weight, precision=HIGHEST))
    cosine, sine = rope_tables(positions)
    queries = low(rotate(mixed[:, :q_cols].reshape(SEQ, HEADS, HEAD), cosine, sine) * HEAD ** (-0.5))
    keys = low(rotate(mixed[:, q_cols:q_cols + kv_cols].reshape(SEQ, KV_HEADS, HEAD), cosine, sine))
    values = low(mixed[:, q_cols + kv_cols:].reshape(SEQ, KV_HEADS, HEAD))
    attended = low(low_back(attend(queries, keys, values, positions)))
    resid = hidden_in + low_back(jnp.dot(attended, out_weight.T, precision=HIGHEST))
    ffn_in = low(rms_norm(resid, gain_ffn))
    return resid + mixture(ffn_in, router, in_weight, down_weight, seq_ids, seq_order)

def reference(hidden_in, span_order, expert_ids, priority, gain_attn, qkv_weight, out_weight, gain_ffn, router, in_weight, down_weight, cotangent):
    params = (gain_attn.astype(jnp.float32), qkv_weight.astype(jnp.float32), out_weight.astype(jnp.float32), gain_ffn.astype(jnp.float32), router.astype(jnp.float32), in_weight.astype(jnp.float32), down_weight.astype(jnp.float32))
    stored = (jnp.arange(SEQ) // SPAN).astype(jnp.int32)
    offsets = (jnp.arange(SEQ) % SPAN).astype(jnp.int32)

    def step(totals, item):
        seq_in, seq_spans, seq_ids, seq_prio, seq_cot = item
        positions = (seq_spans.astype(jnp.int32)[stored] * SPAN + offsets).astype(jnp.float32)

        def forward(inputs, gain_one, w_mixed, w_proj, gain_two, w_router, w_inner, w_outer):
            return layer(inputs, gain_one, w_mixed, w_proj, gain_two, w_router, w_inner, w_outer, positions, seq_ids, seq_prio)
        result, pull = jax.vjp(forward, seq_in.astype(jnp.float32), params[0], params[1], params[2], params[3], params[4], params[5], params[6])
        grads = pull(seq_cot.astype(jnp.float32))
        totals = jax.tree.map(jnp.add, totals, tuple(grads[1:]))
        return (totals, (result.astype(jnp.bfloat16), grads[0].astype(jnp.bfloat16)))
    start = tuple((jnp.zeros(p.shape, jnp.float32) for p in params))
    totals, (output, input_grad) = lax.scan(step, start, (hidden_in, span_order, expert_ids, priority, cotangent))
    return (output, input_grad, totals[0], totals[1], totals[2], totals[3], totals[4], totals[5], totals[6])
```

```python
import functools

import jax
import jax.numpy as jnp
from jax import lax
from jax.experimental import pallas as pl
from jax.experimental.pallas import tpu as pltpu
from jax.sharding import PartitionSpec as P

HEADS = 12
KV_HEADS = 2
HEAD = 128


ROPE_BASE = 1000000.0
NORM_EPS = 1e-06
MASKED = -1e30


def rope_tables(positions, head_size):
    half_size = head_size // 2
    freqs = ROPE_BASE ** (jnp.arange(half_size).astype(jnp.float32) * (-2.0 / head_size))
    angles = positions[:, None] * freqs[None, :]
    return (jnp.cos(angles)[:, None, :], jnp.sin(angles)[:, None, :])


def rotate(values, cosine, sine):
    half_size = values.shape[-1] // 2
    first = values[..., :half_size]
    second = values[..., half_size:]
    return jnp.concatenate(
        [first * cosine - second * sine, second * cosine + first * sine], axis=-1
    )


def unrotate(values, cosine, sine):
    half_size = values.shape[-1] // 2
    first = values[..., :half_size]
    second = values[..., half_size:]
    return jnp.concatenate(
        [first * cosine + second * sine, second * cosine - first * sine], axis=-1
    )


def softmax_last(scores):
    shifted = jnp.exp(scores - jnp.max(scores, axis=-1, keepdims=True))
    return shifted / jnp.sum(shifted, axis=-1, keepdims=True)


def route(block_ids, block_order, n_experts, capacity):
    flat_ids = block_ids.reshape(-1)
    flat_order = block_order.reshape(-1)
    choose = (flat_ids[:, None] == jnp.arange(n_experts)[None, :]).astype(jnp.int32)
    ordered = jnp.zeros_like(choose).at[flat_order].set(choose)
    earlier = jnp.cumsum(ordered, axis=0, dtype=jnp.int32) - ordered
    ranks = jnp.sum(earlier[flat_order] * choose, axis=1)
    return jnp.where(ranks < capacity, flat_ids * capacity + ranks, n_experts * capacity)


MESH = pl.DeviceIdType.MESH
F32 = jnp.float32
BF16 = jnp.bfloat16


def dot(a, b):
    return jnp.dot(a, b, preferred_element_type=F32)


def dot_nt(a, b):
    return lax.dot_general(a, b, (((1,), (1,)), ((), ())), preferred_element_type=F32)


def dot_tn(a, b):
    return lax.dot_general(a, b, (((0,), (0,)), ((), ())), preferred_element_type=F32)


def place():
    e, c, z = lax.axis_index("expert"), lax.axis_index("context"), lax.axis_index("dp")
    return e, c, z, lax.div(c, 2), lax.rem(c, 2)


def greet(peers, extra=()):
    barrier = pltpu.get_barrier_semaphore()
    for peer in peers:
        pl.semaphore_signal(barrier, inc=1, device_id=peer, device_id_type=MESH)
    for there, peer in extra:

        @pl.when(there)
        def _():
            pl.semaphore_signal(barrier, inc=1, device_id=peer, device_id_type=MESH)

    count = len(peers)
    for there, _ in extra:
        count = count + there.astype(jnp.int32)
    pl.semaphore_wait(barrier, count)


def ffn_kernel(
    cap,
    ffn,
    cot_h,
    meta,
    win_h,
    wdn_h,
    zout_h,
    pg_out,
    gg_out,
    gwin_h,
    gwdn_h,
    agb,
    metas,
    cotb,
    win,
    wdn,
    xs,
    ds,
    hid,
    igs,
    pgs,
    ys,
    zcs,
    zcr,
    zk,
    rx,
    ry,
    ggs,
    ggr,
    stage,
    load_sem,
    cot_sem,
    ag_s,
    ag_r,
    me_s,
    me_r,
    gg_s,
    gg_r,
    rs_s,
    rs_r,
    st_sem,
):
    e, c, z, y, k = place()
    tok, width = ffn.shape
    half = tok // 2
    ff = wdn.shape[1]
    planes = agb.shape[0]
    ctx = planes // 2
    me = e * ctx + c
    xp, yp, kp = (1 - e, c, z), (e, (1 - y) * 2 + k, z), (e, y * 2 + 1 - k, z)
    x_me, y_me, k_me = (1 - e) * ctx + c, e * ctx + (1 - y) * 2 + k, e * ctx + y * 2 + 1 - k
    d_me = (1 - e) * ctx + (1 - y) * 2 + k
    k_of = 1 - 2 * k

    loads = [
        pltpu.make_async_copy(win_h.at[c], win, load_sem.at[0]),
        pltpu.make_async_copy(wdn_h.at[c], wdn, load_sem.at[1]),
        pltpu.make_async_copy(cot_h, cotb, cot_sem.at[0]),
    ]
    for load in loads:
        load.start()
    others = []
    for step in range(1, planes):
        other = lax.rem(me + step, planes)
        others.append((other, (lax.div(other, ctx), lax.rem(other, ctx), z)))
    greet([dev for _, dev in others])

    sent = []

    def push(src, dst, s, r, i, dev):
        copy = pltpu.make_async_remote_copy(
            src_ref=src, dst_ref=dst, send_sem=s.at[i], recv_sem=r.at[i], device_id=dev, device_id_type=MESH
        )
        copy.start()
        sent.append(copy)

    def arrive(dst, s, r, i):
        pltpu.make_async_remote_copy(
            src_ref=dst, dst_ref=dst, send_sem=s.at[i], recv_sem=r.at[i], device_id=kp, device_id_type=MESH
        ).wait_recv()

    lo, hi = pl.ds(0, half), pl.ds(half, half)

    def move(p, rows, i, dev):
        push(agb.at[p, rows], agb.at[p, rows], ag_s, ag_r, i, dev)

    def got(p, rows, i):
        arrive(agb.at[p, rows], ag_s, ag_r, i)

    for step, (other, dev) in enumerate(others):
        pltpu.make_async_remote_copy(
            src_ref=meta.at[other],
            dst_ref=metas.at[me],
            send_sem=me_s.at[step],
            recv_sem=me_r.at[step],
            device_id=dev,
            device_id_type=MESH,
        ).start()
    push(ffn.at[lo], agb.at[me, lo], ag_s, ag_r, 0, xp)
    push(ffn.at[hi], agb.at[me, hi], ag_s, ag_r, 3, yp)
    push(ffn, agb.at[me], ag_s, ag_r, 6, kp)
    push(ffn.at[hi], agb.at[me, hi], ag_s, ag_r, 1, xp)
    push(ffn.at[lo], agb.at[me, lo], ag_s, ag_r, 2, yp)
    agb[me] = ffn[...]
    metas[me] = meta[me]
    slot_rows = lax.broadcasted_iota(jnp.int32, (cap, tok), 0).astype(F32)

    def spots(p):
        return jnp.where(slot_rows == metas[p, 0:1, :], 1.0, 0.0)

    def gate_of(p, hot):
        return jnp.sum(hot * metas[p, 1:2, :], axis=1, keepdims=True)

    def chip(eq, yq):
        return eq * ctx + yq * 2

    def group(q, base):
        rows = pl.ds(q * 2 * cap, 2 * cap)
        for kk in range(2):
            p = base + kk
            hot = spots(p)
            low = hot.astype(BF16)
            part = pl.ds(q * 2 * cap + kk * cap, cap)
            xs[part, :] = dot(low, agb[p]).astype(BF16)
            ds[part, :] = (dot(low, cotb[p]) * gate_of(p, hot)).astype(BF16)
        step = 256

        @pl.loop(0, ff // step)
        def _(n):
            gate_cols = pl.ds(pl.multiple_of(n * step, step), step)
            up_cols = pl.ds(pl.multiple_of(ff + n * step, step), step)
            x = xs[rows, :]
            g = dot(x, win[:, gate_cols])
            u = dot(x, win[:, up_cols])
            s = 1.0 / (1.0 + jnp.exp(-g))
            act = g * s
            hid[rows, gate_cols] = (act * u).astype(BF16)
            h = dot(ds[rows, :], wdn[:, gate_cols])
            igs[rows, gate_cols] = (h * u * (s * (1.0 + g * (1.0 - s)))).astype(BF16)
            igs[rows, up_cols] = (h * act).astype(BF16)

        @pl.loop(0, width // step)
        def _(n):
            cols = pl.ds(pl.multiple_of(n * step, step), step)
            pgs[:, cols] = dot_nt(igs[rows, :], win[cols, :]).astype(BF16)

        mine = pl.ds(pl.multiple_of(k * cap, 16), cap)
        theirs = pl.ds(pl.multiple_of((1 - k) * cap, 16), cap)
        zcs[q] = dot_tn(spots(base + 1 - k).astype(BF16), pgs[theirs, :]).astype(BF16)
        push(zcs.at[q], zcr.at[q], rs_s, rs_r, q, kp)
        zk[q] = dot_tn(spots(base + k).astype(BF16), pgs[mine, :]).astype(BF16)

    def fold(q):
        arrive(zcr.at[q], rs_s, rs_r, q)
        zk[q] = (zk[q].astype(F32) + zcr[q].astype(F32)).astype(BF16)

    def add(q, rows, term):
        zk[q, rows] = (zk[q, rows].astype(F32) + term.astype(F32)).astype(BF16)

    def hop(q, rows, buf, i, sem, dev):
        push(zk.at[q, rows], buf.at[i], rs_s, rs_r, sem, dev)

    def hopped(buf, i, sem):
        arrive(buf.at[i], rs_s, rs_r, sem)

    for load in loads:
        load.wait()
    for step in range(planes - 1):
        source = lax.rem(me + planes - 1 - step, planes)
        arrive(metas.at[source], me_s, me_r, step)
    got(me + k_of, pl.ds(0, tok), 6)
    group(0, chip(e, y))

    got(x_me, lo, 0)
    move(x_me, lo, 4, yp)
    move(x_me, lo, 7, kp)
    got(y_me, hi, 3)
    move(y_me, hi, 5, xp)
    move(y_me, hi, 10, kp)
    got(x_me, hi, 1)
    move(x_me, hi, 8, kp)
    got(y_me, lo, 2)
    move(y_me, lo, 9, kp)
    got(x_me + k_of, lo, 7)
    got(x_me + k_of, hi, 8)
    group(1, chip(1 - e, y))

    got(d_me, lo, 4)
    move(d_me, lo, 11, kp)
    got(d_me, hi, 5)
    move(d_me, hi, 12, kp)
    got(y_me + k_of, lo, 9)
    got(y_me + k_of, hi, 10)
    fold(1)
    hop(1, lo, rx, 1, 5, xp)
    group(2, chip(e, 1 - y))
    got(d_me + k_of, lo, 11)
    got(d_me + k_of, hi, 12)
    fold(2)
    hop(2, hi, ry, 1, 8, yp)
    group(3, chip(1 - e, 1 - y))
    fold(3)
    hop(3, lo, rx, 0, 4, xp)
    hop(3, hi, ry, 0, 7, yp)
    fold(0)

    step = 256

    @pl.loop(0, width // step)
    def _(n):
        cols = pl.ds(pl.multiple_of(n * step, step), step)
        ys[:, cols] = dot_nt(hid[...], wdn[cols, :]).astype(BF16)

    order = [chip(e, y), chip(1 - e, y), chip(e, 1 - y), chip(1 - e, 1 - y)]

    for q, base in enumerate(order):
        for kk in range(2):
            p = base + kk
            hot = spots(p)
            part = pl.ds(q * 2 * cap + kk * cap, cap)
            ggs[p, 0:1, :] = jnp.sum(hot * dot_nt(ys[part, :], cotb[p]), axis=0, keepdims=True)
    ggr[me] = ggs[me]
    for step, (other, dev) in enumerate(others):
        pltpu.make_async_remote_copy(
            src_ref=ggs.at[other],
            dst_ref=ggr.at[me],
            send_sem=gg_s.at[step],
            recv_sem=gg_r.at[step],
            device_id=dev,
            device_id_type=MESH,
        ).start()

    hopped(rx, 0, 4)
    add(2, lo, rx[0])
    hop(2, lo, ry, 2, 9, yp)
    hopped(ry, 0, 7)
    add(1, hi, ry[0])
    hop(1, hi, rx, 2, 6, xp)

    for q, base in enumerate(order):
        for kk in range(2):
            p = base + kk
            i = q * 2 + kk
            slot = i % 2
            hot = spots(p)
            part = pl.ds(q * 2 * cap + kk * cap, cap)
            scaled = (ys[part, :].astype(F32) * gate_of(p, hot)).astype(BF16)
            if i >= 2:
                pltpu.make_async_copy(stage.at[slot], zout_h.at[p], st_sem.at[slot]).wait()
            stage[slot] = dot_tn(hot.astype(BF16), scaled).astype(BF16)
            pltpu.make_async_copy(stage.at[slot], zout_h.at[p], st_sem.at[slot]).start()

    for slot in range(2):
        pltpu.make_async_copy(stage.at[slot], zout_h.at[0], st_sem.at[slot]).wait()

    m = 256

    def out_tiles(left, right, dest, wide):
        @pl.loop(0, width // m)
        def _(n):
            slot = lax.rem(n, 2)
            cols = pl.ds(pl.multiple_of(n * m, m), m)
            to = pltpu.make_async_copy(stage.at[slot, :, pl.ds(0, wide)], dest.at[cols, :], st_sem.at[slot])

            @pl.when(n >= 2)
            def _():
                to.wait()

            stage[slot, :, pl.ds(0, wide)] = dot_tn(left[:, cols], right[...]).astype(BF16)
            to.start()

        for slot in range(2):
            pltpu.make_async_copy(
                stage.at[slot, :, pl.ds(0, wide)], dest.at[pl.ds(0, m), :], st_sem.at[slot]
            ).wait()

    out_tiles(ds, hid, gwdn_h, ff)
    out_tiles(xs, igs, gwin_h, 2 * ff)

    hopped(rx, 1, 5)
    hopped(ry, 1, 8)
    hopped(rx, 2, 6)
    hopped(ry, 2, 9)
    for rows, first, second in ((lo, rx[1], ry[2]), (hi, rx[2], ry[1])):
        pg_out[rows, :] = zk[0, rows].astype(F32) + first.astype(F32) + second.astype(F32)
    for step in range(planes - 1):
        source = lax.rem(me + planes - 1 - step, planes)
        arrive(ggr.at[source], gg_s, gg_r, step)
    for p in range(planes):
        gg_out[p : p + 1, :] = ggr[p, 0:1, :]
    for step, (other, dev) in enumerate(others):
        for buf, s, r in ((meta, me_s, me_r), (ggs, gg_s, gg_r)):
            pltpu.make_async_remote_copy(
                src_ref=buf.at[other],
                dst_ref=buf.at[other],
                send_sem=s.at[step],
                recv_sem=r.at[step],
                device_id=dev,
                device_id_type=MESH,
            ).wait_send()
    for copy in sent:
        copy.wait_send()


def run_ffn(cap, ffn, cot_all, meta, win, wdn):
    tok, width = ffn.shape
    ff = wdn.shape[2]
    planes = cot_all.shape[0]
    rows = planes * cap
    vm, anyspace = pl.BlockSpec(memory_space=pltpu.VMEM), pl.BlockSpec(memory_space=pl.ANY)
    shape = jax.ShapeDtypeStruct
    dma = pltpu.SemaphoreType.DMA
    half = tok // 2
    return pl.pallas_call(
        functools.partial(ffn_kernel, cap),
        out_shape=(
            shape((planes, tok, width), BF16),
            shape((tok, width), F32),
            shape((planes, tok), F32),
            shape((width, 2 * ff), BF16),
            shape((width, ff), BF16),
        ),
        in_specs=[vm, anyspace, vm, anyspace, anyspace],
        out_specs=(anyspace, vm, vm, anyspace, anyspace),
        scratch_shapes=[
            pltpu.VMEM((planes, tok, width), BF16),
            pltpu.VMEM((planes, 8, tok), F32),
            pltpu.VMEM((planes, tok, width), BF16),
            pltpu.VMEM((width, 2 * ff), BF16),
            pltpu.VMEM((width, ff), BF16),
            pltpu.VMEM((rows, width), BF16),
            pltpu.VMEM((rows, width), BF16),
            pltpu.VMEM((rows, ff), BF16),
            pltpu.VMEM((rows, 2 * ff), BF16),
            pltpu.VMEM((2 * cap, width), BF16),
            pltpu.VMEM((rows, width), BF16),
            pltpu.VMEM((4, tok, width), BF16),
            pltpu.VMEM((4, tok, width), BF16),
            pltpu.VMEM((4, tok, width), BF16),
            pltpu.VMEM((3, half, width), BF16),
            pltpu.VMEM((3, half, width), BF16),
            pltpu.VMEM((planes, 8, tok), F32),
            pltpu.VMEM((planes, 8, tok), F32),
            pltpu.VMEM((2, 256, max(width, 2 * ff)), BF16),
            dma((2,)),
            dma((1,)),
            dma((13,)),
            dma((13,)),
            dma((planes - 1,)),
            dma((planes - 1,)),
            dma((planes - 1,)),
            dma((planes - 1,)),
            dma((10,)),
            dma((10,)),
            dma((2,)),
        ],
        compiler_params=pltpu.CompilerParams(
            collective_id=1, has_side_effects=True, vmem_limit_bytes=62 * 2**20
        ),
        cost_estimate=pl.CostEstimate(flops=25 * 10**9, bytes_accessed=50 * 10**6, transcendentals=10**6),
    )(ffn, cot_all, meta, win, wdn)


def reduce_kernel(
    shared,
    gwin,
    gwdn,
    sh_out,
    ex_out,
    zcr,
    zk,
    rx,
    ry,
    fin,
    ar,
    ez,
    sz,
    rs_s,
    rs_r,
    ez_s,
    ez_r,
    sz_s,
    sz_r,
    aa_s,
    aa_r,
):
    e, c, z, y, k = place()
    parts = lax.axis_size("dp")
    ctx = lax.axis_size("context")
    last = parts - 1
    block = zk.shape[1]
    half = block // 2
    piece = block // parts
    cols = ex_out.shape[2] // 3
    xp, yp, kp = (1 - e, c, z), (e, (1 - y) * 2 + k, z), (e, y * 2 + 1 - k, z)
    yk = (e, (1 - y) * 2 + 1 - k, z)
    ups = [(z, (e, c, z + 1), lambda d: d), (last - z, (e, c, z - 1), lambda d: last - d)]
    greet([xp, yp, kp, yk], [(z < last, (e, c, z + 1)), (z > 0, (e, c, z - 1))])

    def remote(src, dst, s, r, dev):
        return pltpu.make_async_remote_copy(
            src_ref=src, dst_ref=dst, send_sem=s, recv_sem=r, device_id=dev, device_id_type=MESH
        )

    def plus(a, b):
        return (a.astype(F32) + b.astype(F32)).astype(BF16)

    units = [(gwdn, 0), (gwin, 0), (gwin, cols)]

    def line_step(own, pieces, buf, s, r, u, turn, adder):
        for way, (i, dev, part) in enumerate(ups):
            to = buf.at[way, u, turn - 1]

            @pl.when(i == 0)
            def _():
                remote(own(part(parts - turn)), to, s.at[way, u, turn - 1], r.at[way, u, turn - 1], dev).start()

            if turn >= 2:
                came = buf.at[way, u, turn - 2]

                @pl.when((i >= 1) & (i <= turn - 1) & (i < last))
                def _():
                    remote(came, came, s.at[way, u, turn - 2], r.at[way, u, turn - 2], dev).wait_recv()
                    adder(came, part(parts - turn + i))
                    remote(came, to, s.at[way, u, turn - 1], r.at[way, u, turn - 1], dev).start()

    def line_final(buf, s, r, u):
        for way, (i, dev, part) in enumerate(ups):
            came = buf.at[way, u, last - 1]

            @pl.when(i >= 1)
            def _():
                remote(came, came, s.at[way, u, last - 1], r.at[way, u, last - 1], dev).wait_recv()

    def line_sent(buf, s, r, u):
        for way, (i, dev, part) in enumerate(ups):
            for turn in range(1, parts):
                came = buf.at[way, u, turn - 1]

                @pl.when((i <= turn - 1) & (i < last))
                def _():
                    remote(came, came, s.at[way, u, turn - 1], r.at[way, u, turn - 1], dev).wait_send()

    def expert_own(u):
        ref, at = units[u]
        return lambda d: ref.at[:, d, :, pl.ds(at, cols)]

    def expert_step(u, turn):
        ref, at = units[u]

        def adder(came, d):
            for cc in range(ctx):
                came[cc] = plus(came[cc], ref[cc, d, :, at : at + cols])

        line_step(expert_own(u), ctx, ez, ez_s, ez_r, u, turn, adder)

    def expert_final(u):
        ref, at = units[u]
        line_final(ez, ez_s, ez_r, u)
        below, above = ez.at[0, u, last - 1], ez.at[1, u, last - 1]

        @pl.when(z == 0)
        def _():
            for cc in range(ctx):
                fin[u, cc] = plus(ref[cc, z, :, at : at + cols], above[cc])

        @pl.when(z == last)
        def _():
            for cc in range(ctx):
                fin[u, cc] = plus(ref[cc, z, :, at : at + cols], below[cc])

        @pl.when((z > 0) & (z < last))
        def _():
            for cc in range(ctx):
                total = ref[cc, z, :, at : at + cols].astype(F32) + below[cc].astype(F32)
                fin[u, cc] = (total + above[cc].astype(F32)).astype(BF16)

        for step in range(1, ctx):
            cc = lax.rem(c + step, ctx)
            remote(
                fin.at[u, cc], ar.at[u, c], aa_s.at[u, step - 1], aa_r.at[u, step - 1], (e, cc, z)
            ).start()

    def spread(u):
        at = u * cols
        for step in range(1, ctx):
            cc = lax.rem(c + ctx - step, ctx)
            got = remote(
                ar.at[u, cc], ar.at[u, cc], aa_s.at[u, step - 1], aa_r.at[u, step - 1], (e, cc, z)
            )
            got.wait_recv()
            got.wait_send()
            ex_out[cc, :, at : at + cols] = ar[u, cc]
        ex_out[c, :, at : at + cols] = fin[u, c]

    lo, hi = pl.ds(0, half), pl.ds(half, half)
    order = [(e, y), (1 - e, y), (e, 1 - y), (1 - e, 1 - y)]
    sent = []

    def rows_of(eq, yq, kq):
        return pl.ds(pl.multiple_of((eq * ctx + yq * 2 + kq) * block, 16), block)

    def push(src, dst, i, dev):
        copy = remote(src, dst, rs_s.at[i], rs_r.at[i], dev)
        copy.start()
        sent.append(copy)

    def arrive(dst, i):
        remote(dst, dst, rs_s.at[i], rs_r.at[i], kp).wait_recv()

    def fold(q):
        arrive(zcr.at[q], q)
        eq, yq = order[q]
        zk[q] = plus(shared[rows_of(eq, yq, k), :], zcr[q])

    def add(q, rows, term):
        zk[q, rows] = plus(zk[q, rows], term)

    for u in range(3):
        expert_step(u, 1)
    for q in (1, 2, 3, 0):
        eq, yq = order[q]
        push(shared.at[rows_of(eq, yq, 1 - k)], zcr.at[q], q, kp)
    fold(1)
    push(zk.at[1, lo], rx.at[1], 5, xp)
    fold(2)
    push(zk.at[2, hi], ry.at[1], 8, yp)
    fold(3)
    push(zk.at[3, lo], rx.at[0], 4, xp)
    push(zk.at[3, hi], ry.at[0], 7, yp)
    fold(0)
    expert_step(0, 2)
    expert_step(0, 3)
    expert_step(1, 2)
    arrive(rx.at[0], 4)
    add(2, lo, rx[0])
    push(zk.at[2, lo], ry.at[2], 9, yp)
    arrive(ry.at[0], 7)
    add(1, hi, ry[0])
    push(zk.at[1, hi], rx.at[2], 6, xp)
    expert_final(0)
    expert_step(1, 3)
    expert_step(2, 2)
    arrive(rx.at[1], 5)
    arrive(ry.at[1], 8)
    arrive(rx.at[2], 6)
    arrive(ry.at[2], 9)
    for rows, first, second in ((lo, rx[1], ry[2]), (hi, rx[2], ry[1])):
        zk[0, rows] = (zk[0, rows].astype(F32) + first.astype(F32) + second.astype(F32)).astype(BF16)

    def shared_own(d):
        return zk.at[0, pl.ds(pl.multiple_of(d * piece, 16), piece)]

    def shared_step(turn):
        def adder(came, d):
            came[...] = plus(came[...], shared_own(d)[...])

        line_step(shared_own, 1, sz, sz_s, sz_r, 0, turn, adder)

    shared_step(1)
    expert_final(1)
    expert_step(2, 3)
    shared_step(2)
    expert_final(2)
    shared_step(3)
    spread(0)
    spread(1)
    line_final(sz, sz_s, sz_r, 0)
    below, above = sz.at[0, 0, last - 1], sz.at[1, 0, last - 1]

    @pl.when(z == 0)
    def _():
        sh_out[...] = plus(shared_own(z)[...], above[...])

    @pl.when(z == last)
    def _():
        sh_out[...] = plus(shared_own(z)[...], below[...])

    @pl.when((z > 0) & (z < last))
    def _():
        sh_out[...] = (shared_own(z)[...].astype(F32) + below[...].astype(F32) + above[...].astype(F32)).astype(BF16)

    spread(2)
    for u in range(3):
        line_sent(ez, ez_s, ez_r, u)
    line_sent(sz, sz_s, sz_r, 0)
    for copy in sent:
        copy.wait_send()


def run_reduce(shared, gwin, gwdn, parts, ctx, planes):
    width, wide = shared.shape
    block = width // planes
    piece = block // parts
    rows = width // (ctx * parts)
    ff = gwdn.shape[1]
    gwin = gwin.reshape(ctx, parts, rows, 2 * ff)
    gwdn = gwdn.reshape(ctx, parts, rows, ff)
    vm = pl.BlockSpec(memory_space=pltpu.VMEM)
    shape = jax.ShapeDtypeStruct
    dma = pltpu.SemaphoreType.DMA
    turns = parts - 1
    return pl.pallas_call(
        reduce_kernel,
        out_shape=(shape((piece, wide), BF16), shape((ctx, rows, 3 * ff), BF16)),
        in_specs=[vm, vm, vm],
        out_specs=(vm, vm),
        scratch_shapes=[
            pltpu.VMEM((4, block, wide), BF16),
            pltpu.VMEM((4, block, wide), BF16),
            pltpu.VMEM((3, block // 2, wide), BF16),
            pltpu.VMEM((3, block // 2, wide), BF16),
            pltpu.VMEM((3, ctx, rows, ff), BF16),
            pltpu.VMEM((3, ctx, rows, ff), BF16),
            pltpu.VMEM((2, 3, turns, ctx, rows, ff), BF16),
            pltpu.VMEM((2, 1, turns, piece, wide), BF16),
            dma((10,)),
            dma((10,)),
            dma((2, 3, turns)),
            dma((2, 3, turns)),
            dma((2, 1, turns)),
            dma((2, 1, turns)),
            dma((3, ctx - 1)),
            dma((3, ctx - 1)),
        ],
        compiler_params=pltpu.CompilerParams(
            collective_id=2, has_side_effects=True, vmem_limit_bytes=60 * 2**20
        ),
        cost_estimate=pl.CostEstimate(flops=10**8, bytes_accessed=30 * 10**6, transcendentals=0),
    )(shared, gwin, gwdn)


def local(
    hidden_in,
    span_order,
    expert_ids,
    priority,
    gain_attn,
    qkv_weight,
    out_weight,
    gain_ffn,
    router,
    in_weight,
    down_weight,
    cotangent,
):
    tok_rows = hidden_in.shape[1]
    width = hidden_in.shape[2]
    contexts = lax.axis_size("context")
    span_len = tok_rows // 2
    seq_len = tok_rows * contexts
    group = HEADS // KV_HEADS
    q_cols = HEADS * HEAD
    kv_cols = KV_HEADS * HEAD
    scale = HEAD ** (-0.5)
    local_experts = in_weight.shape[0]
    n_experts = local_experts * lax.axis_size("expert")
    top_k = expert_ids.shape[2]
    capacity = (9 * tok_rows * top_k + 8 * n_experts - 1) // (8 * n_experts)
    ff_width = down_weight.shape[2]
    seq_spans = span_order[0]
    stored = jnp.arange(seq_len) // span_len
    all_pos = (seq_spans[stored] * span_len + jnp.arange(seq_len) % span_len).astype(jnp.float32)
    my_pos = lax.dynamic_slice_in_dim(all_pos, lax.axis_index("context") * tok_rows, tok_rows)
    cosine, sine = rope_tables(my_pos, HEAD)
    inputs = hidden_in[0].astype(jnp.float32)
    inv_one = lax.rsqrt(jnp.mean(inputs * inputs, axis=-1, keepdims=True) + NORM_EPS)
    plain_one = inputs * inv_one
    normed = (plain_one * gain_attn).astype(jnp.bfloat16)
    mixed = jnp.dot(normed, qkv_weight, preferred_element_type=jnp.float32)
    queries = (
        rotate(mixed[:, :q_cols].reshape(tok_rows, HEADS, HEAD), cosine, sine) * scale
    ).astype(jnp.bfloat16)
    keys = rotate(
        mixed[:, q_cols : q_cols + kv_cols].reshape(tok_rows, KV_HEADS, HEAD), cosine, sine
    ).astype(jnp.bfloat16)
    values = mixed[:, q_cols + kv_cols :].reshape(tok_rows, KV_HEADS, HEAD).astype(jnp.bfloat16)
    grouped = queries.reshape(tok_rows, KV_HEADS, group, HEAD)

    def key_scores(key_piece):
        scores = jnp.einsum(
            "qkgd,skd->kgqs", grouped, key_piece, preferred_element_type=jnp.float32
        )
        visible = all_pos[None, None, None, :] <= my_pos[None, None, :, None]
        return (jnp.where(visible, scores, MASKED), visible)

    running = jnp.full((KV_HEADS, group, tok_rows), MASKED, jnp.float32)
    key_piece = lax.all_gather(keys, "context", axis=0, tiled=True)
    value_piece = lax.all_gather(values, "context", axis=0, tiled=True)
    scores, visible = key_scores(key_piece)
    newest = jnp.maximum(running, jnp.max(scores, axis=-1))
    weights = jnp.where(visible, jnp.exp(scores - newest[..., None]), 0.0)
    totals = jnp.sum(weights, axis=-1)
    accum = jnp.einsum(
        "kgqs,skd->kgqd",
        weights.astype(jnp.bfloat16),
        value_piece,
        preferred_element_type=jnp.float32,
    )
    running, totals, accum = (newest, totals, accum)
    log_total = running + jnp.log(totals)
    attended = (
        (accum / totals[..., None])
        .transpose(2, 0, 1, 3)
        .reshape(tok_rows, q_cols)
        .astype(jnp.bfloat16)
    )
    resid = inputs + jnp.einsum(
        "rh,dh->rd", attended, out_weight, preferred_element_type=jnp.float32
    )
    inv_two = lax.rsqrt(jnp.mean(resid * resid, axis=-1, keepdims=True) + NORM_EPS)
    plain_two = resid * inv_two
    ffn_in = (plain_two * gain_ffn).astype(jnp.bfloat16)
    logits = jnp.dot(ffn_in, router, preferred_element_type=jnp.float32)
    token_ids = expert_ids[0]
    matches = token_ids[:, :, None] == jnp.arange(n_experts)[None, None, :]
    chosen = jnp.any(matches, axis=1)
    gates = softmax_last(jnp.where(chosen, logits, MASKED))
    turn = jnp.sum(jnp.where(matches, priority[0][:, :, None], 0), axis=1)
    turn = jnp.where(chosen, turn, tok_rows * top_k)
    ranks = jnp.sum((turn[:, None, :] < turn[None, :, :]).astype(jnp.int32), axis=0)
    slots = jnp.where(chosen & (ranks < capacity), ranks, -1).astype(jnp.float32)
    meta = jnp.stack([slots.T, gates.T], axis=1)
    meta = jnp.pad(meta, ((0, 0), (0, 6), (0, 0)))
    cot_low = cotangent[0]
    cot_full = cot_low.astype(jnp.float32)
    cot_all = lax.all_gather(cot_low, ("expert", "context"), axis=0)
    zout, pair_sum, gate_grad_t, gwin, gwdn = run_ffn(
        capacity, ffn_in, cot_all, meta, in_weight, down_weight
    )
    out_sum = lax.psum_scatter(zout, ("expert", "context"), scatter_dimension=0, tiled=True)[0]
    output = (resid + out_sum.astype(jnp.float32)).astype(jnp.bfloat16)
    gate_grad = gate_grad_t.T
    mix_grad = gates * (gate_grad - jnp.sum(gates * gate_grad, axis=-1, keepdims=True))
    logit_grad = mix_grad.astype(jnp.bfloat16)
    router_part = jnp.einsum("rd,re->de", ffn_in, logit_grad, preferred_element_type=jnp.float32)
    ffn_grad = pair_sum + jnp.einsum(
        "re,de->rd", logit_grad, router, preferred_element_type=jnp.float32
    )
    gain_ffn_part = jnp.sum(ffn_grad * plain_two, axis=0)
    scaled_two = ffn_grad * gain_ffn
    resid_grad = cot_full + inv_two * (
        scaled_two - plain_two * jnp.mean(scaled_two * plain_two, axis=-1, keepdims=True)
    )
    resid_low = resid_grad.astype(jnp.bfloat16)
    out_part = jnp.einsum("rd,rh->dh", resid_low, attended, preferred_element_type=jnp.float32)
    att_grad = jnp.einsum(
        "rd,dh->rh", resid_low, out_weight, preferred_element_type=jnp.float32
    ).astype(jnp.bfloat16)
    att_heads = att_grad.reshape(tok_rows, KV_HEADS, group, HEAD)
    row_delta = jnp.sum(
        att_heads.astype(jnp.float32)
        * attended.reshape(tok_rows, KV_HEADS, group, HEAD).astype(jnp.float32),
        axis=-1,
    ).transpose(1, 2, 0)
    key_piece = lax.all_gather(keys, "context", axis=0, tiled=True)
    value_piece = lax.all_gather(values, "context", axis=0, tiled=True)
    scores, visible = key_scores(key_piece)
    soft = jnp.exp(scores - log_total[..., None])
    prob_grad = jnp.einsum(
        "qkgd,skd->kgqs", att_heads, value_piece, preferred_element_type=jnp.float32
    )
    score_grad = (soft * (prob_grad - row_delta[..., None])).astype(jnp.bfloat16)
    query_acc = jnp.einsum(
        "kgqs,skd->kgqd", score_grad, key_piece, preferred_element_type=jnp.float32
    )
    key_part = jnp.einsum("kgqs,qkgd->skd", score_grad, grouped, preferred_element_type=jnp.float32)
    value_part = jnp.einsum(
        "kgqs,qkgd->skd", soft.astype(jnp.bfloat16), att_heads, preferred_element_type=jnp.float32
    )
    pair_acc = jnp.stack([key_part, value_part], axis=1)
    query_acc, pair_acc = (query_acc, pair_acc)
    own_pairs = lax.psum_scatter(
        pair_acc.astype(jnp.bfloat16), "context", scatter_dimension=0, tiled=True
    ).astype(jnp.float32)
    query_grad = (
        unrotate(query_acc.transpose(2, 0, 1, 3).reshape(tok_rows, HEADS, HEAD), cosine, sine)
        * scale
    )
    key_grad = unrotate(own_pairs[:, 0], cosine, sine)
    mixed_grad = jnp.concatenate(
        [
            query_grad.reshape(tok_rows, q_cols),
            key_grad.reshape(tok_rows, kv_cols),
            own_pairs[:, 1].reshape(tok_rows, kv_cols),
        ],
        axis=-1,
    ).astype(jnp.bfloat16)
    qkv_part = jnp.einsum("rd,rc->dc", normed, mixed_grad, preferred_element_type=jnp.float32)
    norm_grad = jnp.einsum("rc,dc->rd", mixed_grad, qkv_weight, preferred_element_type=jnp.float32)
    gain_attn_part = jnp.sum(norm_grad * plain_one, axis=0)
    scaled_one = norm_grad * gain_attn
    input_grad = (
        resid_grad
        + inv_one
        * (scaled_one - plain_one * jnp.mean(scaled_one * plain_one, axis=-1, keepdims=True))
    ).astype(jnp.bfloat16)
    small = jnp.concatenate(
        [router_part, gain_attn_part[:, None], gain_ffn_part[:, None]], axis=1
    )
    small = jnp.pad(small, ((0, 0), (0, 128 - small.shape[1])))
    shared = jnp.concatenate(
        [small.astype(jnp.bfloat16), qkv_part.astype(jnp.bfloat16), out_part.astype(jnp.bfloat16)],
        axis=1,
    )
    shared, experts = run_reduce(
        shared, gwin, gwdn, lax.axis_size("dp"), contexts, contexts * lax.axis_size("expert")
    )
    shared = shared.astype(jnp.float32)
    experts = experts.astype(jnp.float32)
    router_grad = shared[:, :n_experts]
    gain_attn_grad = shared[:, n_experts]
    gain_ffn_grad = shared[:, n_experts + 1]
    qkv_grad = shared[:, 128 : 128 + qkv_part.shape[1]]
    out_proj_grad = shared[:, 128 + qkv_part.shape[1] :]
    expert_down = experts[:, :, :ff_width]
    expert_in = experts[:, :, ff_width:]
    return (
        output[None],
        input_grad[None],
        gain_attn_grad,
        qkv_grad,
        out_proj_grad,
        gain_ffn_grad,
        router_grad,
        expert_in,
        expert_down,
    )


def general(
    hidden_in,
    span_order,
    expert_ids,
    priority,
    gain_attn,
    qkv_weight,
    out_weight,
    gain_ffn,
    router,
    in_weight,
    down_weight,
    cotangent,
):
    tok_rows = hidden_in.shape[1]
    width = hidden_in.shape[2]
    contexts = lax.axis_size("context")
    span_len = tok_rows // 2
    seq_len = tok_rows * contexts
    group = HEADS // KV_HEADS
    q_cols = HEADS * HEAD
    kv_cols = KV_HEADS * HEAD
    scale = HEAD ** (-0.5)
    local_experts = in_weight.shape[0]
    n_experts = local_experts * lax.axis_size("expert")
    top_k = expert_ids.shape[2]
    capacity = (9 * tok_rows * top_k + 8 * n_experts - 1) // (8 * n_experts)
    ff_width = down_weight.shape[2]
    seq_spans = span_order[0]
    stored = jnp.arange(seq_len) // span_len
    all_pos = (seq_spans[stored] * span_len + jnp.arange(seq_len) % span_len).astype(jnp.float32)
    my_pos = lax.dynamic_slice_in_dim(all_pos, lax.axis_index("context") * tok_rows, tok_rows)
    cosine, sine = rope_tables(my_pos, HEAD)
    inputs = hidden_in[0].astype(jnp.float32)
    inv_one = lax.rsqrt(jnp.mean(inputs * inputs, axis=-1, keepdims=True) + NORM_EPS)
    plain_one = inputs * inv_one
    normed = (plain_one * gain_attn).astype(jnp.bfloat16)
    mixed = jnp.dot(normed, qkv_weight, preferred_element_type=jnp.float32)
    queries = (
        rotate(mixed[:, :q_cols].reshape(tok_rows, HEADS, HEAD), cosine, sine) * scale
    ).astype(jnp.bfloat16)
    keys = rotate(
        mixed[:, q_cols : q_cols + kv_cols].reshape(tok_rows, KV_HEADS, HEAD), cosine, sine
    ).astype(jnp.bfloat16)
    values = mixed[:, q_cols + kv_cols :].reshape(tok_rows, KV_HEADS, HEAD).astype(jnp.bfloat16)
    grouped = queries.reshape(tok_rows, KV_HEADS, group, HEAD)

    def key_scores(key_piece):
        scores = jnp.einsum(
            "qkgd,skd->kgqs", grouped, key_piece, preferred_element_type=jnp.float32
        )
        visible = all_pos[None, None, None, :] <= my_pos[None, None, :, None]
        return (jnp.where(visible, scores, MASKED), visible)

    running = jnp.full((KV_HEADS, group, tok_rows), MASKED, jnp.float32)
    key_piece = lax.all_gather(keys, "context", axis=0, tiled=True)
    value_piece = lax.all_gather(values, "context", axis=0, tiled=True)
    scores, visible = key_scores(key_piece)
    newest = jnp.maximum(running, jnp.max(scores, axis=-1))
    weights = jnp.where(visible, jnp.exp(scores - newest[..., None]), 0.0)
    totals = jnp.sum(weights, axis=-1)
    accum = jnp.einsum(
        "kgqs,skd->kgqd",
        weights.astype(jnp.bfloat16),
        value_piece,
        preferred_element_type=jnp.float32,
    )
    running, totals, accum = (newest, totals, accum)
    log_total = running + jnp.log(totals)
    attended = (
        (accum / totals[..., None])
        .transpose(2, 0, 1, 3)
        .reshape(tok_rows, q_cols)
        .astype(jnp.bfloat16)
    )
    resid = inputs + jnp.einsum(
        "rh,dh->rd", attended, out_weight, preferred_element_type=jnp.float32
    )
    inv_two = lax.rsqrt(jnp.mean(resid * resid, axis=-1, keepdims=True) + NORM_EPS)
    plain_two = resid * inv_two
    ffn_in = (plain_two * gain_ffn).astype(jnp.bfloat16)
    logits = jnp.dot(ffn_in, router, preferred_element_type=jnp.float32)
    token_ids = expert_ids[0]
    gates = softmax_last(jnp.take_along_axis(logits, token_ids, axis=1))
    slots = route(token_ids, priority[0], n_experts, capacity)
    pair_rows = jnp.repeat(ffn_in, top_k, axis=0)
    send_rows = (
        jnp.zeros((n_experts * capacity, width), jnp.bfloat16).at[slots].set(pair_rows, mode="drop")
    )
    received = lax.all_to_all(
        send_rows.reshape(n_experts, capacity, width),
        "expert",
        split_axis=0,
        concat_axis=1,
        tiled=True,
    )
    inner = jnp.einsum("erd,edf->erf", received, in_weight, preferred_element_type=jnp.float32)
    gate_part = inner[..., :ff_width]
    up_part = inner[..., ff_width:]
    sigma = 1.0 / (1.0 + jnp.exp(-gate_part))
    activated = gate_part * sigma
    hidden = (activated * up_part).astype(jnp.bfloat16)
    expert_out = jnp.einsum(
        "erf,edf->erd", hidden, down_weight, preferred_element_type=jnp.float32
    ).astype(jnp.bfloat16)
    returned = lax.all_to_all(
        expert_out, "expert", split_axis=1, concat_axis=0, tiled=True
    ).reshape(n_experts * capacity, width)
    padded = jnp.concatenate([returned, jnp.zeros((1, width), jnp.bfloat16)], axis=0)
    picked = padded[slots].reshape(tok_rows, top_k, width)
    output = (resid + jnp.sum(gates[:, :, None] * picked, axis=1)).astype(jnp.bfloat16)
    cot_low = cotangent[0]
    cot_full = cot_low.astype(jnp.float32)
    gate_grad = jnp.einsum("rkd,rd->rk", picked, cot_low, preferred_element_type=jnp.float32)
    ret_grad = (
        (gates[:, :, None] * cot_full[:, None, :])
        .astype(jnp.bfloat16)
        .reshape(tok_rows * top_k, width)
    )
    send_grad = (
        jnp.zeros((n_experts * capacity, width), jnp.bfloat16).at[slots].set(ret_grad, mode="drop")
    )
    received_grad = lax.all_to_all(
        send_grad.reshape(n_experts, capacity, width),
        "expert",
        split_axis=0,
        concat_axis=1,
        tiled=True,
    )
    hid_grad = jnp.einsum(
        "erd,edf->erf", received_grad, down_weight, preferred_element_type=jnp.float32
    )
    slope = sigma * (1.0 + gate_part * (1.0 - sigma))
    inner_grad = jnp.concatenate(
        [hid_grad * up_part * slope, hid_grad * activated], axis=-1
    ).astype(jnp.bfloat16)
    row_grad = jnp.einsum(
        "erf,edf->erd", inner_grad, in_weight, preferred_element_type=jnp.float32
    ).astype(jnp.bfloat16)
    part_rows = received
    expert_in = (
        lax.psum_scatter(
            jnp.einsum(
                "erd,erf->def", part_rows, inner_grad, preferred_element_type=jnp.float32
            ).astype(jnp.bfloat16),
            ("context", "dp"),
            scatter_dimension=0,
            tiled=True,
        )
        .astype(jnp.float32)
        .transpose(1, 0, 2)
    )
    part_rows = received_grad
    expert_down = (
        lax.psum_scatter(
            jnp.einsum(
                "erd,erf->def", part_rows, hidden, preferred_element_type=jnp.float32
            ).astype(jnp.bfloat16),
            ("context", "dp"),
            scatter_dimension=0,
            tiled=True,
        )
        .astype(jnp.float32)
        .transpose(1, 0, 2)
    )
    back_rows = lax.all_to_all(row_grad, "expert", split_axis=1, concat_axis=0, tiled=True).reshape(
        n_experts * capacity, width
    )
    back_padded = jnp.concatenate([back_rows, jnp.zeros((1, width), jnp.bfloat16)], axis=0)
    pair_grad = back_padded[slots].reshape(tok_rows, top_k, width)
    mix_grad = gates * (gate_grad - jnp.sum(gates * gate_grad, axis=-1, keepdims=True))
    matches = token_ids[:, :, None] == jnp.arange(n_experts)[None, None, :]
    logit_grad = jnp.sum(jnp.where(matches, mix_grad[:, :, None], 0.0), axis=1).astype(jnp.bfloat16)
    router_part = jnp.einsum("rd,re->de", ffn_in, logit_grad, preferred_element_type=jnp.float32)
    ffn_grad = jnp.sum(pair_grad.astype(jnp.float32), axis=1) + jnp.einsum(
        "re,de->rd", logit_grad, router, preferred_element_type=jnp.float32
    )
    gain_ffn_part = jnp.sum(ffn_grad * plain_two, axis=0)
    scaled_two = ffn_grad * gain_ffn
    resid_grad = cot_full + inv_two * (
        scaled_two - plain_two * jnp.mean(scaled_two * plain_two, axis=-1, keepdims=True)
    )
    resid_low = resid_grad.astype(jnp.bfloat16)
    out_part = jnp.einsum("rd,rh->dh", resid_low, attended, preferred_element_type=jnp.float32)
    att_grad = jnp.einsum(
        "rd,dh->rh", resid_low, out_weight, preferred_element_type=jnp.float32
    ).astype(jnp.bfloat16)
    att_heads = att_grad.reshape(tok_rows, KV_HEADS, group, HEAD)
    row_delta = jnp.sum(
        att_heads.astype(jnp.float32)
        * attended.reshape(tok_rows, KV_HEADS, group, HEAD).astype(jnp.float32),
        axis=-1,
    ).transpose(1, 2, 0)
    key_piece = lax.all_gather(keys, "context", axis=0, tiled=True)
    value_piece = lax.all_gather(values, "context", axis=0, tiled=True)
    scores, visible = key_scores(key_piece)
    soft = jnp.exp(scores - log_total[..., None])
    prob_grad = jnp.einsum(
        "qkgd,skd->kgqs", att_heads, value_piece, preferred_element_type=jnp.float32
    )
    score_grad = (soft * (prob_grad - row_delta[..., None])).astype(jnp.bfloat16)
    query_acc = jnp.einsum(
        "kgqs,skd->kgqd", score_grad, key_piece, preferred_element_type=jnp.float32
    )
    key_part = jnp.einsum("kgqs,qkgd->skd", score_grad, grouped, preferred_element_type=jnp.float32)
    value_part = jnp.einsum(
        "kgqs,qkgd->skd", soft.astype(jnp.bfloat16), att_heads, preferred_element_type=jnp.float32
    )
    pair_acc = jnp.stack([key_part, value_part], axis=1)
    query_acc, pair_acc = (query_acc, pair_acc)
    own_pairs = lax.psum_scatter(
        pair_acc.astype(jnp.bfloat16), "context", scatter_dimension=0, tiled=True
    ).astype(jnp.float32)
    query_grad = (
        unrotate(query_acc.transpose(2, 0, 1, 3).reshape(tok_rows, HEADS, HEAD), cosine, sine)
        * scale
    )
    key_grad = unrotate(own_pairs[:, 0], cosine, sine)
    mixed_grad = jnp.concatenate(
        [
            query_grad.reshape(tok_rows, q_cols),
            key_grad.reshape(tok_rows, kv_cols),
            own_pairs[:, 1].reshape(tok_rows, kv_cols),
        ],
        axis=-1,
    ).astype(jnp.bfloat16)
    qkv_part = jnp.einsum("rd,rc->dc", normed, mixed_grad, preferred_element_type=jnp.float32)
    norm_grad = jnp.einsum("rc,dc->rd", mixed_grad, qkv_weight, preferred_element_type=jnp.float32)
    gain_attn_part = jnp.sum(norm_grad * plain_one, axis=0)
    scaled_one = norm_grad * gain_attn
    input_grad = (
        resid_grad
        + inv_one
        * (scaled_one - plain_one * jnp.mean(scaled_one * plain_one, axis=-1, keepdims=True))
    ).astype(jnp.bfloat16)
    gain_attn_grad, qkv_grad, out_proj_grad, gain_ffn_grad, router_grad = (
        lax.psum_scatter(
            gain_attn_part, ("expert", "context", "dp"), scatter_dimension=0, tiled=True
        ),
        lax.psum_scatter(qkv_part, ("expert", "context", "dp"), scatter_dimension=0, tiled=True),
        lax.psum_scatter(out_part, ("expert", "context", "dp"), scatter_dimension=0, tiled=True),
        lax.psum_scatter(
            gain_ffn_part, ("expert", "context", "dp"), scatter_dimension=0, tiled=True
        ),
        lax.psum_scatter(router_part, ("expert", "context", "dp"), scatter_dimension=0, tiled=True),
    )
    return (
        output[None],
        input_grad[None],
        gain_attn_grad,
        qkv_grad,
        out_proj_grad,
        gain_ffn_grad,
        router_grad,
        expert_in,
        expert_down,
    )


def solution(mesh):
    in_specs = (
        P(("expert", "dp"), "context", None),
        P(("expert", "dp"), None),
        P(("expert", "dp"), "context", None),
        P(("expert", "dp"), "context", None),
        P(),
        P(),
        P(),
        P(),
        P(),
        P("expert", None, None),
        P("expert", None, None),
        P(("expert", "dp"), "context", None),
    )
    out_specs = (
        P(("expert", "dp"), "context", None),
        P(("expert", "dp"), "context", None),
        P(("expert", "context", "dp")),
        P(("expert", "context", "dp"), None),
        P(("expert", "context", "dp"), None),
        P(("expert", "context", "dp")),
        P(("expert", "context", "dp"), None),
        P("expert", ("context", "dp"), None),
        P("expert", ("context", "dp"), None),
    )
    sizes = dict(mesh.shape)
    tuned = sizes == {"expert": 2, "context": 4, "dp": 4}
    body = local if tuned else general
    return jax.shard_map(body, mesh=mesh, in_specs=in_specs, out_specs=out_specs, check_vma=False)
```

```python
import functools

import jax
import jax.numpy as jnp
from jax import lax
from jax.experimental import pallas as pl
from jax.experimental.pallas import tpu as pltpu
from jax.sharding import PartitionSpec as P

HEADS = 12
KV_HEADS = 2
HEAD = 128


ROPE_BASE = 1000000.0
NORM_EPS = 1e-06
MASKED = -1e30


def rope_tables(positions, head_size):
    half_size = head_size // 2
    freqs = ROPE_BASE ** (jnp.arange(half_size).astype(jnp.float32) * (-2.0 / head_size))
    angles = positions[:, None] * freqs[None, :]
    return (jnp.cos(angles)[:, None, :], jnp.sin(angles)[:, None, :])


def rotate(values, cosine, sine):
    half_size = values.shape[-1] // 2
    first = values[..., :half_size]
    second = values[..., half_size:]
    return jnp.concatenate(
        [first * cosine - second * sine, second * cosine + first * sine], axis=-1
    )


def unrotate(values, cosine, sine):
    half_size = values.shape[-1] // 2
    first = values[..., :half_size]
    second = values[..., half_size:]
    return jnp.concatenate(
        [first * cosine + second * sine, second * cosine - first * sine], axis=-1
    )


def softmax_last(scores):
    shifted = jnp.exp(scores - jnp.max(scores, axis=-1, keepdims=True))
    return shifted / jnp.sum(shifted, axis=-1, keepdims=True)


def route(block_ids, block_order, n_experts, capacity):
    flat_ids = block_ids.reshape(-1)
    flat_order = block_order.reshape(-1)
    choose = (flat_ids[:, None] == jnp.arange(n_experts)[None, :]).astype(jnp.int32)
    ordered = jnp.zeros_like(choose).at[flat_order].set(choose)
    earlier = jnp.cumsum(ordered, axis=0, dtype=jnp.int32) - ordered
    ranks = jnp.sum(earlier[flat_order] * choose, axis=1)
    return jnp.where(ranks < capacity, flat_ids * capacity + ranks, n_experts * capacity)


MESH = pl.DeviceIdType.MESH
F32 = jnp.float32
BF16 = jnp.bfloat16


def dot(a, b):
    return jnp.dot(a, b, preferred_element_type=F32)


def dot_nt(a, b):
    return lax.dot_general(a, b, (((1,), (1,)), ((), ())), preferred_element_type=F32)


def dot_tn(a, b):
    return lax.dot_general(a, b, (((0,), (0,)), ((), ())), preferred_element_type=F32)


def plus(a, *more):
    total = a.astype(F32)
    for b in more:
        total = total + b.astype(F32)
    return total.astype(BF16)


def lanes(at, size):
    return pl.ds(pl.multiple_of(at, 128), size)


def rows_at(at, size):
    return pl.ds(pl.multiple_of(at, 16), size)


def remote(src, dst, s, r, dev):
    return pltpu.make_async_remote_copy(
        src_ref=src, dst_ref=dst, send_sem=s, recv_sem=r, device_id=dev, device_id_type=MESH
    )


class Spot:
    def __init__(self):
        e, c, z = lax.axis_index("expert"), lax.axis_index("context"), lax.axis_index("dp")
        self.ctx = lax.axis_size("context")
        self.parts = lax.axis_size("dp")
        self.planes = self.ctx * lax.axis_size("expert")
        y, k = lax.div(c, 2), lax.rem(c, 2)
        self.e, self.c, self.z, self.k = e, c, z, k
        self.me = e * self.ctx + c
        self.xp, self.yp = (1 - e, c, z), (e, (1 - y) * 2 + k, z)
        self.kp, self.yk = (e, y * 2 + 1 - k, z), (e, (1 - y) * 2 + 1 - k, z)
        self.chips = [
            eq * self.ctx + yq * 2 for eq, yq in ((e, y), (1 - e, y), (e, 1 - y), (1 - e, 1 - y))
        ]

    def others(self):
        found = []
        for step in range(1, self.planes):
            other = lax.rem(self.me + step, self.planes)
            found.append((other, (lax.div(other, self.ctx), lax.rem(other, self.ctx), self.z)))
        return found

    def along(self):
        e, c, z = self.e, self.c, self.z
        return [(z < self.parts - 1, (e, c, z + 1)), (z > 0, (e, c, z - 1))]


def greet(peers, extra=()):
    barrier = pltpu.get_barrier_semaphore()
    for peer in peers:
        pl.semaphore_signal(barrier, inc=1, device_id=peer, device_id_type=MESH)
    for there, peer in extra:

        @pl.when(there)
        def _():
            pl.semaphore_signal(barrier, inc=1, device_id=peer, device_id_type=MESH)

    count = len(peers)
    for there, _ in extra:
        count = count + there.astype(jnp.int32)
    pl.semaphore_wait(barrier, count)


class Plane:
    def __init__(self, spot, zcr, zk, rx, ry, s, r):
        self.spot, self.zcr, self.zk, self.rx, self.ry, self.s, self.r = spot, zcr, zk, rx, ry, s, r
        half = zk.shape[1] // 2
        self.lo, self.hi = pl.ds(0, half), pl.ds(half, half)
        self.sent = []

    def push(self, src, dst, i, dev):
        copy = remote(src, dst, self.s.at[i], self.r.at[i], dev)
        copy.start()
        self.sent.append(copy)

    def arrive(self, dst, i):
        remote(dst, dst, self.s.at[i], self.r.at[i], self.spot.kp).wait_recv()

    def give(self, q, src):
        self.push(src, self.zcr.at[q], q, self.spot.kp)

    def fold(self, q, own):
        self.arrive(self.zcr.at[q], q)
        self.zk[q] = plus(own, self.zcr[q])

    def near(self):
        self.push(self.zk.at[1, self.lo], self.rx.at[1], 5, self.spot.xp)
        self.push(self.zk.at[2, self.hi], self.ry.at[1], 8, self.spot.yp)

    def across(self):
        self.push(self.zk.at[3, self.lo], self.rx.at[0], 4, self.spot.xp)
        self.push(self.zk.at[3, self.hi], self.ry.at[0], 7, self.spot.yp)

    def turn(self):
        lo, hi = self.lo, self.hi
        self.arrive(self.rx.at[0], 4)
        self.zk[2, lo] = plus(self.zk[2, lo], self.rx[0])
        self.push(self.zk.at[2, lo], self.ry.at[2], 9, self.spot.yp)
        self.arrive(self.ry.at[0], 7)
        self.zk[1, hi] = plus(self.zk[1, hi], self.ry[0])
        self.push(self.zk.at[1, hi], self.rx.at[2], 6, self.spot.xp)

    def total(self):
        self.arrive(self.rx.at[1], 5)
        self.arrive(self.ry.at[1], 8)
        self.arrive(self.rx.at[2], 6)
        self.arrive(self.ry.at[2], 9)
        return ((self.lo, self.rx.at[1], self.ry.at[2]), (self.hi, self.rx.at[2], self.ry.at[1]))

    def done(self):
        for copy in self.sent:
            copy.wait_send()


def plane_scratch(block, wide):
    return [
        pltpu.VMEM((4, block, wide), BF16),
        pltpu.VMEM((4, block, wide), BF16),
        pltpu.VMEM((3, block // 2, wide), BF16),
        pltpu.VMEM((3, block // 2, wide), BF16),
        pltpu.SemaphoreType.DMA((10,)),
        pltpu.SemaphoreType.DMA((10,)),
    ]


class Line:
    def __init__(self, spot, own, adder, buf, s, r):
        z, last = spot.z, spot.parts - 1
        e, c = spot.e, spot.c
        self.own, self.adder, self.buf, self.s, self.r = own, adder, buf, s, r
        self.z, self.last, self.parts = z, last, spot.parts
        self.ways = [(z, (e, c, z + 1), lambda d: d), (last - z, (e, c, z - 1), lambda d: last - d)]

    def step(self, turn):
        for way, (i, dev, part) in enumerate(self.ways):
            to, s, r = self.buf.at[way, turn - 1], self.s.at[way, turn - 1], self.r.at[way, turn - 1]

            @pl.when(i == 0)
            def _():
                remote(self.own(part(self.parts - turn)), to, s, r, dev).start()

            if turn >= 2:
                came, s_came, r_came = (x.at[way, turn - 2] for x in (self.buf, self.s, self.r))

                @pl.when((i >= 1) & (i <= turn - 1) & (i < self.last))
                def _():
                    remote(came, came, s_came, r_came, dev).wait_recv()
                    self.adder(came, part(self.parts - turn + i))
                    remote(came, to, s, r, dev).start()

    def final(self, put):
        last, z = self.last, self.z
        for way, (i, dev, _) in enumerate(self.ways):
            came = self.buf.at[way, last - 1]

            @pl.when(i >= 1)
            def _():
                remote(came, came, self.s.at[way, last - 1], self.r.at[way, last - 1], dev).wait_recv()

        up, down = self.buf.at[0, last - 1], self.buf.at[1, last - 1]
        pl.when(z == 0)(lambda: put(down))
        pl.when(z == last)(lambda: put(up))
        pl.when((z > 0) & (z < last))(lambda: put(up, down))

    def done(self):
        for way, (i, dev, _) in enumerate(self.ways):
            for turn in range(1, self.parts):
                came = self.buf.at[way, turn - 1]

                @pl.when((i <= turn - 1) & (i < self.last))
                def _():
                    remote(came, came, self.s.at[way, turn - 1], self.r.at[way, turn - 1], dev).wait_send()


def line_scratch(parts, piece):
    return [
        pltpu.VMEM((2, parts - 1) + piece, BF16),
        pltpu.SemaphoreType.DMA((2, parts - 1)),
        pltpu.SemaphoreType.DMA((2, parts - 1)),
    ]


class ExpertLine:
    def __init__(self, spot, ref, at, cols, buf, s, r, fin, spread, a_s, a_r):
        self.spot, self.ref, self.at, self.cols = spot, ref, at, cols
        self.fin, self.spread, self.a_s, self.a_r = fin, spread, a_s, a_r
        self.line = Line(spot, self.own, self.adder, buf, s, r)
        self.step = self.line.step

    def own(self, d):
        return self.ref.at[:, d, :, pl.ds(self.at, self.cols)]

    def piece(self, cc, d):
        return self.ref[cc, d, :, self.at : self.at + self.cols]

    def adder(self, came, d):
        for cc in range(self.spot.ctx):
            came[cc] = plus(came[cc], self.piece(cc, d))

    def final(self):
        spot = self.spot

        def put(*came):
            for cc in range(spot.ctx):
                self.fin[cc] = plus(self.piece(cc, spot.z), *(x[cc] for x in came))

        self.line.final(put)
        for step in range(1, spot.ctx):
            cc = lax.rem(spot.c + step, spot.ctx)
            remote(
                self.fin.at[cc],
                self.spread.at[spot.c],
                self.a_s.at[step - 1],
                self.a_r.at[step - 1],
                (spot.e, cc, spot.z),
            ).start()

    def done(self, out):
        spot = self.spot
        for step in range(1, spot.ctx):
            cc = lax.rem(spot.c + spot.ctx - step, spot.ctx)
            got = remote(
                self.spread.at[cc],
                self.spread.at[cc],
                self.a_s.at[step - 1],
                self.a_r.at[step - 1],
                (spot.e, cc, spot.z),
            )
            got.wait_recv()
            got.wait_send()
            out[cc] = self.spread[cc]
        out[spot.c] = self.fin[spot.c]
        self.line.done()


def expert_scratch(ctx, parts, rows, cols):
    return line_scratch(parts, (ctx, rows, cols)) + [
        pltpu.VMEM((ctx, rows, cols), BF16),
        pltpu.VMEM((ctx, rows, cols), BF16),
        pltpu.SemaphoreType.DMA((ctx - 1,)),
        pltpu.SemaphoreType.DMA((ctx - 1,)),
    ]


def ffn_kernel(cap, ffn, cot_h, meta, win_h, wdn_h, zout_h, pg_out, gg_out, gwin_h, ex_out, *scratch):
    agb, metas, cotb, win, wdn, xs, ds, hid, igs, pgs, ggs, ggr, stage, gwdn, pgt = scratch[:15]
    load_sem, ag_s, ag_r, me_s, me_r, gg_s, gg_r, st_sem = scratch[15:23]
    plane_refs, line_refs = scratch[23:29], scratch[29:]
    spot = Spot()
    e, c, k, me = spot.e, spot.c, spot.k, spot.me
    xp, yp, kp = spot.xp, spot.yp, spot.kp
    tok, width = ffn.shape
    half = tok // 2
    ff = wdn.shape[1]
    planes, ctx = spot.planes, spot.ctx
    chips = spot.chips
    x_me, y_me, d_me = (base + k for base in chips[1:])
    side = 1 - 2 * k

    loads = [
        pltpu.make_async_copy(win_h.at[c], win, load_sem.at[0]),
        pltpu.make_async_copy(wdn_h.at[c], wdn, load_sem.at[1]),
        pltpu.make_async_copy(cot_h, cotb, load_sem.at[2]),
    ]
    for load in loads:
        load.start()
    others = spot.others()
    greet([dev for _, dev in others], spot.along())
    plane = Plane(spot, *plane_refs)
    line = ExpertLine(spot, gwdn, 0, ff, *line_refs)
    lo, hi = plane.lo, plane.hi
    sent = []

    def push(src, dst, i, dev):
        copy = remote(src, dst, ag_s.at[i], ag_r.at[i], dev)
        copy.start()
        sent.append(copy)

    def move(p, rows, i, dev):
        push(agb.at[p, rows], agb.at[p, rows], i, dev)

    def got(p, rows, i):
        remote(agb.at[p, rows], agb.at[p, rows], ag_s.at[i], ag_r.at[i], kp).wait_recv()

    for step, (other, dev) in enumerate(others):
        remote(meta.at[other], metas.at[me], me_s.at[step], me_r.at[step], dev).start()
    push(ffn.at[lo], agb.at[me, lo], 0, xp)
    push(ffn.at[hi], agb.at[me, hi], 3, yp)
    push(ffn, agb.at[me], 6, kp)
    push(ffn.at[hi], agb.at[me, hi], 1, xp)
    push(ffn.at[lo], agb.at[me, lo], 2, yp)
    agb[me] = ffn[...]
    metas[me] = meta[me]
    slot_rows = lax.broadcasted_iota(jnp.int32, (cap, tok), 0).astype(F32)
    step = 256

    def spots(p):
        return jnp.where(slot_rows == metas[p, 0:1, :], 1.0, 0.0)

    def gate_of(p, hot):
        return jnp.sum(hot * metas[p, 1:2, :], axis=1, keepdims=True)

    def group(q):
        base = chips[q]
        rows = pl.ds(q * 2 * cap, 2 * cap)
        for kk in range(2):
            p = base + kk
            hot = spots(p)
            low = hot.astype(BF16)
            part = pl.ds(q * 2 * cap + kk * cap, cap)
            xs[part, :] = dot(low, agb[p]).astype(BF16)
            ds[part, :] = (dot(low, cotb[p]) * gate_of(p, hot)).astype(BF16)

        @pl.loop(0, ff // step)
        def _(n):
            gate_cols, up_cols = lanes(n * step, step), lanes(ff + n * step, step)
            x = xs[rows, :]
            g = dot(x, win[:, gate_cols])
            u = dot(x, win[:, up_cols])
            s = 1.0 / (1.0 + jnp.exp(-g))
            act = g * s
            hid[rows, gate_cols] = (act * u).astype(BF16)
            h = dot(ds[rows, :], wdn[:, gate_cols])
            igs[rows, gate_cols] = (h * u * (s * (1.0 + g * (1.0 - s)))).astype(BF16)
            igs[rows, up_cols] = (h * act).astype(BF16)

        @pl.loop(0, width // step)
        def _(n):
            cols = lanes(n * step, step)
            pgs[:, cols] = dot_nt(igs[rows, :], win[cols, :]).astype(BF16)

        mine, theirs = rows_at(k * cap, cap), rows_at((1 - k) * cap, cap)
        zcs = stage.at[q]
        zcs[...] = dot_tn(spots(base + 1 - k).astype(BF16), pgs[theirs, :]).astype(BF16)
        plane.give(q, zcs)
        plane.zk[q] = dot_tn(spots(base + k).astype(BF16), pgs[mine, :]).astype(BF16)

    def fold(q):
        plane.fold(q, plane.zk[q])

    for load in loads:
        load.wait()
    for n in range(planes - 1):
        source = lax.rem(me + planes - 1 - n, planes)
        remote(metas.at[source], metas.at[source], me_s.at[n], me_r.at[n], kp).wait_recv()
    got(me + side, pl.ds(0, tok), 6)
    group(0)

    got(x_me, lo, 0)
    move(x_me, lo, 4, yp)
    move(x_me, lo, 7, kp)
    got(y_me, hi, 3)
    move(y_me, hi, 5, xp)
    move(y_me, hi, 10, kp)
    got(x_me, hi, 1)
    move(x_me, hi, 8, kp)
    got(y_me, lo, 2)
    move(y_me, lo, 9, kp)
    got(x_me + side, lo, 7)
    got(x_me + side, hi, 8)
    group(1)

    got(d_me, lo, 4)
    move(d_me, lo, 11, kp)
    got(d_me, hi, 5)
    move(d_me, hi, 12, kp)
    got(y_me + side, lo, 9)
    got(y_me + side, hi, 10)
    group(2)
    fold(1)
    fold(2)
    plane.near()
    got(d_me + side, lo, 11)
    got(d_me + side, hi, 12)
    group(3)
    fold(3)
    plane.across()

    tall = width // ctx

    @pl.loop(0, ctx)
    def _(n):
        tile = dot_tn(ds[:, lanes(n * tall, tall)], hid[...]).astype(BF16)
        for d in range(gwdn.shape[1]):
            gwdn[n, d] = tile[d * gwdn.shape[2] : (d + 1) * gwdn.shape[2]]

    line.step(1)
    fold(0)
    plane.turn()

    for copy in sent:
        copy.wait_send()

    for q, base in enumerate(chips):

        @pl.loop(0, width // step)
        def _(n):
            cols = lanes(n * step, step)
            pgs[:, cols] = dot_nt(hid[pl.ds(q * 2 * cap, 2 * cap), :], wdn[cols, :]).astype(BF16)

        for kk in range(2):
            p = base + kk
            i = q * 2 + kk
            hot = spots(p)
            rows = pgs[pl.ds(kk * cap, cap), :]
            ggs[p, 0:1, :] = jnp.sum(hot * dot_nt(rows, cotb[p]), axis=0, keepdims=True)
            scaled = (rows.astype(F32) * gate_of(p, hot)).astype(BF16)
            agb[p] = dot_tn(hot.astype(BF16), scaled).astype(BF16)
            pltpu.make_async_copy(agb.at[p], zout_h.at[p], st_sem.at[i]).start()
    ggr[me] = ggs[me]
    for n, (other, dev) in enumerate(others):
        remote(ggs.at[other], ggr.at[me], gg_s.at[n], gg_r.at[n], dev).start()
    line.step(2)
    half_wide = ff

    @pl.loop(0, 2 * ctx)
    def _(n):
        slot = lax.rem(n, 2)
        rows = lanes(lax.div(n, 2) * tall, tall)
        cols = lanes(slot * half_wide, half_wide)
        tile = pgt.at[slot]
        to = pltpu.make_async_copy(tile, gwin_h.at[rows, cols], load_sem.at[slot])

        @pl.when(n >= 2)
        def _():
            to.wait()

        tile[...] = dot_tn(xs[:, rows], igs[:, cols]).astype(BF16)
        to.start()

    for slot in range(2):
        pltpu.make_async_copy(pgt.at[slot], gwin_h.at[pl.ds(0, tall), pl.ds(0, half_wide)], load_sem.at[slot]).wait()
    line.step(3)
    for rows, first, second in plane.total():
        pg_out[rows, :] = (
            plane.zk[0, rows].astype(F32) + first[...].astype(F32) + second[...].astype(F32)
        )
    for n in range(planes - 1):
        source = lax.rem(me + planes - 1 - n, planes)
        remote(ggr.at[source], ggr.at[source], gg_s.at[n], gg_r.at[n], kp).wait_recv()
    for p in range(planes):
        gg_out[p : p + 1, :] = ggr[p, 0:1, :]
    line.final()
    for i in range(planes):
        pltpu.make_async_copy(agb.at[0], zout_h.at[0], st_sem.at[i]).wait()
    for n, (other, dev) in enumerate(others):
        remote(meta.at[other], metas.at[other], me_s.at[n], me_r.at[n], dev).wait_send()
        remote(ggs.at[other], ggr.at[other], gg_s.at[n], gg_r.at[n], dev).wait_send()
    plane.done()
    line.done(ex_out)


def run_ffn(cap, ffn, cot_all, meta, win, wdn, parts):
    tok, width = ffn.shape
    ff = wdn.shape[2]
    planes = cot_all.shape[0]
    ctx = win.shape[0]
    rows = planes * cap
    piece = width // (ctx * parts)
    vm, anyspace = pl.BlockSpec(memory_space=pltpu.VMEM), pl.BlockSpec(memory_space=pl.ANY)
    shape = jax.ShapeDtypeStruct
    dma = pltpu.SemaphoreType.DMA
    return pl.pallas_call(
        functools.partial(ffn_kernel, cap),
        out_shape=(
            shape((planes, tok, width), BF16),
            shape((tok, width), F32),
            shape((planes, tok), F32),
            shape((width, 2 * ff), BF16),
            shape((ctx, piece, ff), BF16),
        ),
        in_specs=[vm, anyspace, vm, anyspace, anyspace],
        out_specs=(anyspace, vm, vm, anyspace, vm),
        scratch_shapes=[
            pltpu.VMEM((planes, tok, width), BF16),
            pltpu.VMEM((planes, 8, tok), F32),
            pltpu.VMEM((planes, tok, width), BF16),
            pltpu.VMEM((width, 2 * ff), BF16),
            pltpu.VMEM((width, ff), BF16),
            pltpu.VMEM((rows, width), BF16),
            pltpu.VMEM((rows, width), BF16),
            pltpu.VMEM((rows, ff), BF16),
            pltpu.VMEM((rows, 2 * ff), BF16),
            pltpu.VMEM((2 * cap, width), BF16),
            pltpu.VMEM((planes, 8, tok), F32),
            pltpu.VMEM((planes, 8, tok), F32),
            pltpu.VMEM((4, tok, width), BF16),
            pltpu.VMEM((ctx, parts, piece, ff), BF16),
            pltpu.VMEM((2, width // ctx, ff), BF16),
            dma((3,)),
            dma((13,)),
            dma((13,)),
            dma((planes - 1,)),
            dma((planes - 1,)),
            dma((planes - 1,)),
            dma((planes - 1,)),
            dma((planes,)),
        ]
        + plane_scratch(tok, width)
        + expert_scratch(ctx, parts, piece, ff),
        compiler_params=pltpu.CompilerParams(
            collective_id=1, has_side_effects=True, vmem_limit_bytes=62 * 2**20
        ),
        cost_estimate=pl.CostEstimate(flops=25 * 10**9, bytes_accessed=50 * 10**6, transcendentals=10**6),
    )(ffn, cot_all, meta, win, wdn)


def attend_back_kernel(
    span,
    resid,
    cot,
    pg,
    gg,
    gates,
    attended,
    ffn_in,
    queries,
    keys,
    values,
    lse,
    trig,
    wout,
    router_t,
    gain,
    zout_h,
    gwin_h,
    output,
    resid_grad,
    mixed_grad,
    out_red,
    small,
    ex_out,
    *scratch,
):
    zkeep, gwin, osend, low, attg, mask, delta, dk, dv, dq, kvs, kvr = scratch[:12]
    load_sem, kv_s, kv_r = scratch[12:15]
    tok_refs, out_refs, line_refs = scratch[15:21], scratch[21:27], scratch[27:]
    spot = Spot()
    c, k, z, ctx = spot.c, spot.k, spot.z, spot.ctx
    tok, width = cot.shape
    cols = ex_out.shape[2]
    block = out_red.shape[0]
    heads_kv = KV_HEADS
    group = HEADS // KV_HEADS
    half_head = HEAD // 2
    gwin_load = pltpu.make_async_copy(gwin_h.at[:, :, :, pl.ds(0, cols)], gwin, load_sem.at[0])
    gwin_load.start()
    keeps = []
    for q, base in enumerate(spot.chips):
        keeps.append(pltpu.make_async_copy(zout_h.at[base + k], zkeep.at[q], load_sem.at[1 + q]))
        keeps[-1].start()
    greet([spot.xp, spot.yp, spot.kp, spot.yk], spot.along())
    tokens, weights = Plane(spot, *tok_refs), Plane(spot, *out_refs)
    line = ExpertLine(spot, gwin, 0, cols, *line_refs)
    for q, base in enumerate(spot.chips):
        tokens.give(q, zout_h.at[base + 1 - k])
    gwin_load.wait()
    line.step(1)

    gate = gates[...]
    seen = gate * gg[...]
    mix = seen - gate * jnp.sum(seen, axis=0, keepdims=True)
    mix = jnp.concatenate([mix, jnp.zeros((HEAD - mix.shape[0], tok), F32)], axis=0)
    logit_t = mix.astype(BF16)
    r = resid[...]
    inv = lax.rsqrt(jnp.mean(r * r, axis=-1, keepdims=True) + NORM_EPS)
    plain = r * inv
    ffn_grad = pg[...] + dot_tn(logit_t[: router_t.shape[0]], router_t[...])
    gain_row = jnp.sum(ffn_grad * plain, axis=0, keepdims=True)
    scaled = ffn_grad * gain[...]
    back = cot[...].astype(F32) + inv * (
        scaled - plain * jnp.mean(scaled * plain, axis=-1, keepdims=True)
    )
    resid_grad[...] = back
    low[...] = back.astype(BF16)
    lane = lax.broadcasted_iota(jnp.int32, (width, HEAD), 1)
    gain_col = jnp.broadcast_to(gain_row, (HEAD, width)).T
    routed = dot_tn(ffn_in[...], logit_t.T)
    small[...] = jnp.where(lane == gate.shape[0], gain_col, routed).astype(BF16)

    for q in (1, 2):
        keeps[q].wait()
        tokens.fold(q, zkeep[q])
    tokens.near()
    keeps[3].wait()
    tokens.fold(3, zkeep[3])
    tokens.across()
    keeps[0].wait()
    tokens.fold(0, zkeep[0])

    for q in (1, 2, 3, 0):
        at = lanes(spot.chips[q] * block, 2 * block)
        osend[q] = dot_tn(low[:, at], attended[...]).astype(BF16)
        weights.give(q, osend.at[q, rows_at((1 - k) * block, block)])

    step = 256

    @pl.loop(0, width // step)
    def _(n):
        at = lanes(n * step, step)
        attg[:, at] = dot(low[...], wout[:, at]).astype(BF16)

    seq = keys.shape[0]
    spans = span.shape[1]
    size = seq // spans
    mine = spans // ctx
    along_q = lax.broadcasted_iota(jnp.int32, (size, tok), 1)
    q_pos = jnp.where(along_q < size, span[0, c * mine] * size, (span[0, c * mine + 1] - 1) * size) + along_q
    for s in range(spans):
        k_pos = span[0, s] * size + lax.broadcasted_iota(jnp.int32, (size, tok), 0)
        mask[s * size : (s + 1) * size, :] = jnp.where(k_pos <= q_pos, 0.0, MASKED)

    lane_h = lax.broadcasted_iota(jnp.int32, (tok, HEAD), 1)
    deltas = jnp.zeros((tok, HEAD), F32)
    for h in range(HEADS):
        at = slice(h * HEAD, (h + 1) * HEAD)
        term = jnp.sum(attg[:, at].astype(F32) * attended[:, at].astype(F32), axis=-1, keepdims=True)
        deltas = jnp.where(lane_h == h, term, deltas)
    delta[...] = deltas.T

    def head(g, h):
        at = lanes(h * HEAD, HEAD)
        kv = slice(g * HEAD, (g + 1) * HEAD)
        q, a = queries[:, at], attg[:, at]
        soft = jnp.exp(dot_nt(keys[:, kv], q) + mask[...] - lse[pl.ds(h, 1), :])
        prob = dot_nt(values[:, kv], a)
        score = (soft * (prob - delta[pl.ds(h, 1), :])).astype(BF16)
        dq[:, at] = dot_tn(score, keys[:, kv])
        dk[...] += dot(score, q)
        dv[...] += dot(soft.astype(BF16), a)

    def send_kv(g):
        for cc in range(ctx):
            rows = slice(cc * tok, (cc + 1) * tok)
            kvs[g, cc, :, :HEAD] = dk[rows, :].astype(BF16)
            kvs[g, cc, :, HEAD:] = dv[rows, :].astype(BF16)
        for n in range(1, ctx):
            cc = lax.rem(c + n, ctx)
            remote(kvs.at[g, cc], kvr.at[g, c], kv_s.at[g, n - 1], kv_r.at[g, n - 1], (spot.e, cc, z)).start()

    def heads(g, first, count):
        @pl.loop(first, first + count)
        def _(h):
            head(g, h)

    def clear():
        dk[...] = jnp.zeros(dk.shape, F32)
        dv[...] = jnp.zeros(dv.shape, F32)

    def own_part(q):
        return osend[q, rows_at(k * block, block)]

    clear()
    heads(0, 0, 2)
    for q in (1, 2):
        weights.fold(q, own_part(q))
    weights.near()
    weights.fold(3, own_part(3))
    weights.across()
    weights.fold(0, own_part(0))
    heads(0, 2, 2)
    line.step(2)
    heads(0, 4, 2)
    send_kv(0)
    tokens.turn()
    clear()
    heads(1, 6, 2)
    line.step(3)
    heads(1, 8, 2)
    heads(1, 10, 2)
    send_kv(1)
    weights.turn()
    for rows, first, second in tokens.total():
        out_sum = tokens.zk[0, rows].astype(F32) + first[...].astype(F32) + second[...].astype(F32)
        output[rows, :] = (resid[rows, :] + out_sum).astype(BF16)

    cosine, sine = trig[0], trig[1]

    def unrotate(w):
        return w * cosine - pltpu.roll(w, half_head, 1) * sine

    for h in range(HEADS):
        at = slice(h * HEAD, (h + 1) * HEAD)
        mixed_grad[:, at] = (unrotate(dq[:, at]) * HEAD**-0.5).astype(BF16)
    line.final()
    for rows, first, second in weights.total():
        out_red[rows, :] = plus(weights.zk[0, rows], first[...], second[...])
    for g in range(heads_kv):
        own = kvs[g, c].astype(F32)
        for n in range(1, ctx):
            cc = lax.rem(c + ctx - n, ctx)
            got = remote(kvr.at[g, cc], kvr.at[g, cc], kv_s.at[g, n - 1], kv_r.at[g, n - 1], spot.kp)
            got.wait_recv()
            own = own + kvr[g, cc].astype(F32)
        at = width + g * HEAD
        mixed_grad[:, at : at + HEAD] = unrotate(own[:, :HEAD]).astype(BF16)
        at = width + (heads_kv + g) * HEAD
        mixed_grad[:, at : at + HEAD] = own[:, HEAD:].astype(BF16)
    for g in range(heads_kv):
        for n in range(1, ctx):
            cc = lax.rem(c + n, ctx)
            remote(kvs.at[g, cc], kvr.at[g, cc], kv_s.at[g, n - 1], kv_r.at[g, n - 1], spot.kp).wait_send()
    tokens.done()
    weights.done()
    line.done(ex_out)


def run_attend_back(
    span, resid, cot, pg, gg, gates, attended, ffn_in, queries, keys, values, lse, trig, wout, router_t, gain, zout, gwin
):
    tok, width = cot.shape
    planes = zout.shape[0]
    ctx, parts, piece, wide = gwin.shape
    cols = wide // 2
    block = width // planes
    seq, kv_cols = keys.shape
    vm, anyspace = pl.BlockSpec(memory_space=pltpu.VMEM), pl.BlockSpec(memory_space=pl.ANY)
    sm = pl.BlockSpec(memory_space=pltpu.SMEM)
    shape = jax.ShapeDtypeStruct
    dma = pltpu.SemaphoreType.DMA
    return pl.pallas_call(
        attend_back_kernel,
        out_shape=(
            shape((tok, width), BF16),
            shape((tok, width), F32),
            shape((tok, width + 2 * kv_cols), BF16),
            shape((block, width), BF16),
            shape((width, HEAD), BF16),
            shape((ctx, piece, cols), BF16),
        ),
        in_specs=[sm] + [vm] * 15 + [anyspace] * 2,
        out_specs=(vm,) * 6,
        scratch_shapes=[
            pltpu.VMEM((4, tok, width), BF16),
            pltpu.VMEM((ctx, parts, piece, cols), BF16),
            pltpu.VMEM((4, 2 * block, width), BF16),
            pltpu.VMEM((tok, width), BF16),
            pltpu.VMEM((tok, width), BF16),
            pltpu.VMEM((seq, tok), F32),
            pltpu.VMEM((HEAD, tok), F32),
            pltpu.VMEM((seq, HEAD), F32),
            pltpu.VMEM((seq, HEAD), F32),
            pltpu.VMEM((tok, width), F32),
            pltpu.VMEM((KV_HEADS, ctx, tok, 2 * HEAD), BF16),
            pltpu.VMEM((KV_HEADS, ctx, tok, 2 * HEAD), BF16),
            dma((5,)),
            dma((KV_HEADS, ctx - 1)),
            dma((KV_HEADS, ctx - 1)),
        ]
        + plane_scratch(tok, width)
        + plane_scratch(block, width)
        + expert_scratch(ctx, parts, piece, cols),
        compiler_params=pltpu.CompilerParams(
            collective_id=2, has_side_effects=True, vmem_limit_bytes=62 * 2**20
        ),
        cost_estimate=pl.CostEstimate(flops=8 * 10**9, bytes_accessed=40 * 10**6, transcendentals=10**6),
    )(
        span, resid, cot, pg, gg, gates, attended, ffn_in, queries, keys, values, lse, trig, wout, router_t, gain, zout, gwin
    )


def last_kernel(
    normed, mixed_grad, hidden, resid_grad, wqkv, gain, small, out_red, gwin_h, input_grad, qkv_out, proj_out, ex_out, *scratch
):
    gwin, asend, bsend, norm_grad, smalls, total, load_sem = scratch[:7]
    a_refs, b_refs, qkv_refs, proj_refs, line_refs = (
        scratch[7:13],
        scratch[13:19],
        scratch[19:22],
        scratch[22:25],
        scratch[25:],
    )
    spot = Spot()
    k, z = spot.k, spot.z
    tok, width = normed.shape
    cols = ex_out.shape[2]
    block = out_red.shape[0]
    piece = proj_out.shape[0]
    kv_wide = mixed_grad.shape[1] - width
    load = pltpu.make_async_copy(gwin_h.at[:, :, :, pl.ds(cols, cols)], gwin, load_sem.at[0])
    load.start()
    greet([spot.xp, spot.yp, spot.kp, spot.yk], spot.along())
    first, second = Plane(spot, *a_refs), Plane(spot, *b_refs)
    line = ExpertLine(spot, gwin, 0, cols, *line_refs)

    def shared_line(ref, refs):
        def own(d):
            return ref.at[rows_at(d * piece, piece)]

        def adder(came, d):
            came[...] = plus(came[...], own(d)[...])

        return Line(spot, own, adder, *refs)

    qkv, proj = shared_line(total, qkv_refs), shared_line(out_red, proj_refs)
    def put_shared(to, ref, came):
        to[...] = plus(ref[rows_at(z * piece, piece)], *(x[...] for x in came))

    mine, theirs = rows_at(k * block, block), rows_at((1 - k) * block, block)
    load.wait()
    line.step(1)
    proj.step(1)
    for q in (1, 2, 3, 0):
        at = lanes(spot.chips[q] * block, 2 * block)
        asend[q] = dot_tn(normed[:, at], mixed_grad[:, :width]).astype(BF16)
        first.give(q, asend.at[q, theirs])
    first.fold(1, asend[1, mine])
    first.fold(2, asend[2, mine])
    first.near()
    first.fold(3, asend[3, mine])
    first.across()
    first.fold(0, asend[0, mine])

    step = 256

    @pl.loop(0, width // step)
    def _(n):
        at = lanes(n * step, step)
        norm_grad[:, at] = dot_nt(mixed_grad[...], wqkv[at, :])

    x = hidden[...].astype(F32)
    inv = lax.rsqrt(jnp.mean(x * x, axis=-1, keepdims=True) + NORM_EPS)
    plain = x * inv
    ng = norm_grad[...]
    gain_row = jnp.sum(ng * plain, axis=0, keepdims=True)
    scaled = ng * gain[...]
    input_grad[...] = (
        resid_grad[...]
        + inv * (scaled - plain * jnp.mean(scaled * plain, axis=-1, keepdims=True))
    ).astype(BF16)
    lane = lax.broadcasted_iota(jnp.int32, (width, HEAD), 1)
    gain_col = jnp.broadcast_to(gain_row, (HEAD, width)).T
    smalls[...] = jnp.where(lane == HEAD - 1, gain_col, small[...].astype(F32)).astype(BF16)
    for q in (1, 2, 3, 0):
        at = lanes(spot.chips[q] * block, 2 * block)
        bsend[q, :, :kv_wide] = dot_tn(normed[:, at], mixed_grad[:, width:]).astype(BF16)
        bsend[q, :, kv_wide:] = smalls[rows_at(spot.chips[q] * block, 2 * block), :]
        second.give(q, bsend.at[q, theirs])
    first.turn()
    second.fold(1, bsend[1, mine])
    second.fold(2, bsend[2, mine])
    second.near()
    second.fold(3, bsend[3, mine])
    second.across()
    second.fold(0, bsend[0, mine])
    line.step(2)
    proj.step(2)
    for rows, one, two in first.total():
        total[rows, :width] = plus(first.zk[0, rows], one[...], two[...])
    second.turn()
    line.step(3)
    proj.step(3)
    for rows, one, two in second.total():
        total[rows, width:] = plus(second.zk[0, rows], one[...], two[...])
    qkv.step(1)
    proj.final(lambda *came: put_shared(proj_out, out_red, came))
    line.final()
    qkv.step(2)
    line.done(ex_out)
    qkv.step(3)
    proj.done()
    first.done()
    second.done()
    qkv.final(lambda *came: put_shared(qkv_out, total, came))
    qkv.done()


def run_last(normed, mixed_grad, hidden, resid_grad, wqkv, gain, small, out_red, gwin):
    tok, width = normed.shape
    block = out_red.shape[0]
    ctx, parts, rows, wide = gwin.shape
    cols = wide // 2
    piece = block // parts
    rest = mixed_grad.shape[1] - width + HEAD
    vm, anyspace = pl.BlockSpec(memory_space=pltpu.VMEM), pl.BlockSpec(memory_space=pl.ANY)
    shape = jax.ShapeDtypeStruct
    return pl.pallas_call(
        last_kernel,
        out_shape=(
            shape((tok, width), BF16),
            shape((piece, width + rest), BF16),
            shape((piece, width), BF16),
            shape((ctx, rows, cols), BF16),
        ),
        in_specs=[vm] * 8 + [anyspace],
        out_specs=(vm,) * 4,
        scratch_shapes=[
            pltpu.VMEM((ctx, parts, rows, cols), BF16),
            pltpu.VMEM((4, 2 * block, width), BF16),
            pltpu.VMEM((4, 2 * block, rest), BF16),
            pltpu.VMEM((tok, width), F32),
            pltpu.VMEM((width, HEAD), BF16),
            pltpu.VMEM((block, width + rest), BF16),
            pltpu.SemaphoreType.DMA((1,)),
        ]
        + plane_scratch(block, width)
        + plane_scratch(block, rest)
        + line_scratch(parts, (piece, width + rest))
        + line_scratch(parts, (piece, width))
        + expert_scratch(ctx, parts, rows, cols),
        compiler_params=pltpu.CompilerParams(
            collective_id=3, has_side_effects=True, vmem_limit_bytes=62 * 2**20
        ),
        cost_estimate=pl.CostEstimate(flops=4 * 10**9, bytes_accessed=40 * 10**6, transcendentals=0),
    )(normed, mixed_grad, hidden, resid_grad, wqkv, gain, small, out_red, gwin)


def local(
    hidden_in,
    span_order,
    expert_ids,
    priority,
    gain_attn,
    qkv_weight,
    out_weight,
    gain_ffn,
    router,
    in_weight,
    down_weight,
    cotangent,
):
    tok_rows = hidden_in.shape[1]
    width = hidden_in.shape[2]
    contexts = lax.axis_size("context")
    span_len = tok_rows // 2
    seq_len = tok_rows * contexts
    group = HEADS // KV_HEADS
    q_cols = HEADS * HEAD
    kv_cols = KV_HEADS * HEAD
    scale = HEAD ** (-0.5)
    local_experts = in_weight.shape[0]
    n_experts = local_experts * lax.axis_size("expert")
    top_k = expert_ids.shape[2]
    capacity = (9 * tok_rows * top_k + 8 * n_experts - 1) // (8 * n_experts)
    ff_width = down_weight.shape[2]
    seq_spans = span_order[0]
    stored = jnp.arange(seq_len) // span_len
    all_pos = (seq_spans[stored] * span_len + jnp.arange(seq_len) % span_len).astype(jnp.float32)
    my_pos = lax.dynamic_slice_in_dim(all_pos, lax.axis_index("context") * tok_rows, tok_rows)
    cosine, sine = rope_tables(my_pos, HEAD)
    inputs = hidden_in[0].astype(jnp.float32)
    inv_one = lax.rsqrt(jnp.mean(inputs * inputs, axis=-1, keepdims=True) + NORM_EPS)
    plain_one = inputs * inv_one
    normed = (plain_one * gain_attn).astype(jnp.bfloat16)
    mixed = jnp.dot(normed, qkv_weight, preferred_element_type=jnp.float32)
    queries = (
        rotate(mixed[:, :q_cols].reshape(tok_rows, HEADS, HEAD), cosine, sine) * scale
    ).astype(jnp.bfloat16)
    keys = rotate(
        mixed[:, q_cols : q_cols + kv_cols].reshape(tok_rows, KV_HEADS, HEAD), cosine, sine
    ).astype(jnp.bfloat16)
    values = mixed[:, q_cols + kv_cols :].reshape(tok_rows, KV_HEADS, HEAD).astype(jnp.bfloat16)
    grouped = queries.reshape(tok_rows, KV_HEADS, group, HEAD)

    def key_scores(key_piece):
        scores = jnp.einsum(
            "qkgd,skd->kgqs", grouped, key_piece, preferred_element_type=jnp.float32
        )
        visible = all_pos[None, None, None, :] <= my_pos[None, None, :, None]
        return (jnp.where(visible, scores, MASKED), visible)

    running = jnp.full((KV_HEADS, group, tok_rows), MASKED, jnp.float32)
    key_piece = lax.all_gather(keys, "context", axis=0, tiled=True)
    value_piece = lax.all_gather(values, "context", axis=0, tiled=True)
    scores, visible = key_scores(key_piece)
    newest = jnp.maximum(running, jnp.max(scores, axis=-1))
    weights = jnp.where(visible, jnp.exp(scores - newest[..., None]), 0.0)
    totals = jnp.sum(weights, axis=-1)
    accum = jnp.einsum(
        "kgqs,skd->kgqd",
        weights.astype(jnp.bfloat16),
        value_piece,
        preferred_element_type=jnp.float32,
    )
    running, totals, accum = (newest, totals, accum)
    log_total = running + jnp.log(totals)
    attended = (
        (accum / totals[..., None])
        .transpose(2, 0, 1, 3)
        .reshape(tok_rows, q_cols)
        .astype(jnp.bfloat16)
    )
    resid = inputs + jnp.einsum(
        "rh,dh->rd", attended, out_weight, preferred_element_type=jnp.float32
    )
    inv_two = lax.rsqrt(jnp.mean(resid * resid, axis=-1, keepdims=True) + NORM_EPS)
    plain_two = resid * inv_two
    ffn_in = (plain_two * gain_ffn).astype(jnp.bfloat16)
    logits = jnp.dot(ffn_in, router, preferred_element_type=jnp.float32)
    token_ids = expert_ids[0]
    matches = token_ids[:, :, None] == jnp.arange(n_experts)[None, None, :]
    chosen = jnp.any(matches, axis=1)
    gates = softmax_last(jnp.where(chosen, logits, MASKED))
    turn = jnp.sum(jnp.where(matches, priority[0][:, :, None], 0), axis=1)
    turn = jnp.where(chosen, turn, tok_rows * top_k)
    ranks = jnp.sum((turn[:, None, :] < turn[None, :, :]).astype(jnp.int32), axis=0)
    slots = jnp.where(chosen & (ranks < capacity), ranks, -1).astype(jnp.float32)
    gates_t = gates.T
    meta = jnp.stack([slots.T, gates_t], axis=1)
    meta = jnp.pad(meta, ((0, 0), (0, 6), (0, 0)))
    cot_low = cotangent[0]
    cot_all = lax.all_gather(cot_low, ("expert", "context"), axis=0)
    parts = lax.axis_size("dp")
    zout, pair_sum, gate_grad_t, gwin, down = run_ffn(
        capacity, ffn_in, cot_all, meta, in_weight, down_weight, parts
    )
    gwin = gwin.reshape(contexts, parts, width // (contexts * parts), 2 * ff_width)
    lse = jnp.pad(log_total.reshape(HEADS, tok_rows), ((0, 16 - HEADS), (0, 0)))
    cosine, sine = cosine[:, 0, :], sine[:, 0, :]
    trig = jnp.stack(
        [jnp.concatenate([cosine, cosine], axis=1), jnp.concatenate([-sine, sine], axis=1)]
    )
    router_t = jnp.pad(router.T, ((0, 16 - n_experts), (0, 0)))
    output, resid_grad, mixed_grad, out_red, small, in_one = run_attend_back(
        span_order,
        resid,
        cot_low,
        pair_sum,
        gate_grad_t,
        gates_t,
        attended,
        ffn_in,
        queries.reshape(tok_rows, q_cols),
        key_piece.reshape(seq_len, kv_cols),
        value_piece.reshape(seq_len, kv_cols),
        lse,
        trig,
        out_weight,
        router_t,
        gain_ffn[None],
        zout,
        gwin,
    )
    input_grad, qkv_sum, proj_sum, in_two = run_last(
        normed, mixed_grad, hidden_in[0], resid_grad, qkv_weight, gain_attn[None], small, out_red, gwin
    )
    qkv_sum = qkv_sum.astype(jnp.float32)
    smalls = qkv_sum[:, q_cols + 2 * kv_cols :]
    return (
        output[None],
        input_grad[None],
        smalls[:, HEAD - 1],
        qkv_sum[:, : q_cols + 2 * kv_cols],
        proj_sum.astype(jnp.float32),
        smalls[:, n_experts],
        smalls[:, :n_experts],
        jnp.concatenate([in_one, in_two], axis=2).astype(jnp.float32),
        down.astype(jnp.float32),
    )


def general(
    hidden_in,
    span_order,
    expert_ids,
    priority,
    gain_attn,
    qkv_weight,
    out_weight,
    gain_ffn,
    router,
    in_weight,
    down_weight,
    cotangent,
):
    tok_rows = hidden_in.shape[1]
    width = hidden_in.shape[2]
    contexts = lax.axis_size("context")
    span_len = tok_rows // 2
    seq_len = tok_rows * contexts
    group = HEADS // KV_HEADS
    q_cols = HEADS * HEAD
    kv_cols = KV_HEADS * HEAD
    scale = HEAD ** (-0.5)
    local_experts = in_weight.shape[0]
    n_experts = local_experts * lax.axis_size("expert")
    top_k = expert_ids.shape[2]
    capacity = (9 * tok_rows * top_k + 8 * n_experts - 1) // (8 * n_experts)
    ff_width = down_weight.shape[2]
    seq_spans = span_order[0]
    stored = jnp.arange(seq_len) // span_len
    all_pos = (seq_spans[stored] * span_len + jnp.arange(seq_len) % span_len).astype(jnp.float32)
    my_pos = lax.dynamic_slice_in_dim(all_pos, lax.axis_index("context") * tok_rows, tok_rows)
    cosine, sine = rope_tables(my_pos, HEAD)
    inputs = hidden_in[0].astype(jnp.float32)
    inv_one = lax.rsqrt(jnp.mean(inputs * inputs, axis=-1, keepdims=True) + NORM_EPS)
    plain_one = inputs * inv_one
    normed = (plain_one * gain_attn).astype(jnp.bfloat16)
    mixed = jnp.dot(normed, qkv_weight, preferred_element_type=jnp.float32)
    queries = (
        rotate(mixed[:, :q_cols].reshape(tok_rows, HEADS, HEAD), cosine, sine) * scale
    ).astype(jnp.bfloat16)
    keys = rotate(
        mixed[:, q_cols : q_cols + kv_cols].reshape(tok_rows, KV_HEADS, HEAD), cosine, sine
    ).astype(jnp.bfloat16)
    values = mixed[:, q_cols + kv_cols :].reshape(tok_rows, KV_HEADS, HEAD).astype(jnp.bfloat16)
    grouped = queries.reshape(tok_rows, KV_HEADS, group, HEAD)

    def key_scores(key_piece):
        scores = jnp.einsum(
            "qkgd,skd->kgqs", grouped, key_piece, preferred_element_type=jnp.float32
        )
        visible = all_pos[None, None, None, :] <= my_pos[None, None, :, None]
        return (jnp.where(visible, scores, MASKED), visible)

    running = jnp.full((KV_HEADS, group, tok_rows), MASKED, jnp.float32)
    key_piece = lax.all_gather(keys, "context", axis=0, tiled=True)
    value_piece = lax.all_gather(values, "context", axis=0, tiled=True)
    scores, visible = key_scores(key_piece)
    newest = jnp.maximum(running, jnp.max(scores, axis=-1))
    weights = jnp.where(visible, jnp.exp(scores - newest[..., None]), 0.0)
    totals = jnp.sum(weights, axis=-1)
    accum = jnp.einsum(
        "kgqs,skd->kgqd",
        weights.astype(jnp.bfloat16),
        value_piece,
        preferred_element_type=jnp.float32,
    )
    running, totals, accum = (newest, totals, accum)
    log_total = running + jnp.log(totals)
    attended = (
        (accum / totals[..., None])
        .transpose(2, 0, 1, 3)
        .reshape(tok_rows, q_cols)
        .astype(jnp.bfloat16)
    )
    resid = inputs + jnp.einsum(
        "rh,dh->rd", attended, out_weight, preferred_element_type=jnp.float32
    )
    inv_two = lax.rsqrt(jnp.mean(resid * resid, axis=-1, keepdims=True) + NORM_EPS)
    plain_two = resid * inv_two
    ffn_in = (plain_two * gain_ffn).astype(jnp.bfloat16)
    logits = jnp.dot(ffn_in, router, preferred_element_type=jnp.float32)
    token_ids = expert_ids[0]
    gates = softmax_last(jnp.take_along_axis(logits, token_ids, axis=1))
    slots = route(token_ids, priority[0], n_experts, capacity)
    pair_rows = jnp.repeat(ffn_in, top_k, axis=0)
    send_rows = (
        jnp.zeros((n_experts * capacity, width), jnp.bfloat16).at[slots].set(pair_rows, mode="drop")
    )
    received = lax.all_to_all(
        send_rows.reshape(n_experts, capacity, width),
        "expert",
        split_axis=0,
        concat_axis=1,
        tiled=True,
    )
    inner = jnp.einsum("erd,edf->erf", received, in_weight, preferred_element_type=jnp.float32)
    gate_part = inner[..., :ff_width]
    up_part = inner[..., ff_width:]
    sigma = 1.0 / (1.0 + jnp.exp(-gate_part))
    activated = gate_part * sigma
    hidden = (activated * up_part).astype(jnp.bfloat16)
    expert_out = jnp.einsum(
        "erf,edf->erd", hidden, down_weight, preferred_element_type=jnp.float32
    ).astype(jnp.bfloat16)
    returned = lax.all_to_all(
        expert_out, "expert", split_axis=1, concat_axis=0, tiled=True
    ).reshape(n_experts * capacity, width)
    padded = jnp.concatenate([returned, jnp.zeros((1, width), jnp.bfloat16)], axis=0)
    picked = padded[slots].reshape(tok_rows, top_k, width)
    output = (resid + jnp.sum(gates[:, :, None] * picked, axis=1)).astype(jnp.bfloat16)
    cot_low = cotangent[0]
    cot_full = cot_low.astype(jnp.float32)
    gate_grad = jnp.einsum("rkd,rd->rk", picked, cot_low, preferred_element_type=jnp.float32)
    ret_grad = (
        (gates[:, :, None] * cot_full[:, None, :])
        .astype(jnp.bfloat16)
        .reshape(tok_rows * top_k, width)
    )
    send_grad = (
        jnp.zeros((n_experts * capacity, width), jnp.bfloat16).at[slots].set(ret_grad, mode="drop")
    )
    received_grad = lax.all_to_all(
        send_grad.reshape(n_experts, capacity, width),
        "expert",
        split_axis=0,
        concat_axis=1,
        tiled=True,
    )
    hid_grad = jnp.einsum(
        "erd,edf->erf", received_grad, down_weight, preferred_element_type=jnp.float32
    )
    slope = sigma * (1.0 + gate_part * (1.0 - sigma))
    inner_grad = jnp.concatenate(
        [hid_grad * up_part * slope, hid_grad * activated], axis=-1
    ).astype(jnp.bfloat16)
    row_grad = jnp.einsum(
        "erf,edf->erd", inner_grad, in_weight, preferred_element_type=jnp.float32
    ).astype(jnp.bfloat16)
    part_rows = received
    expert_in = (
        lax.psum_scatter(
            jnp.einsum(
                "erd,erf->def", part_rows, inner_grad, preferred_element_type=jnp.float32
            ).astype(jnp.bfloat16),
            ("context", "dp"),
            scatter_dimension=0,
            tiled=True,
        )
        .astype(jnp.float32)
        .transpose(1, 0, 2)
    )
    part_rows = received_grad
    expert_down = (
        lax.psum_scatter(
            jnp.einsum(
                "erd,erf->def", part_rows, hidden, preferred_element_type=jnp.float32
            ).astype(jnp.bfloat16),
            ("context", "dp"),
            scatter_dimension=0,
            tiled=True,
        )
        .astype(jnp.float32)
        .transpose(1, 0, 2)
    )
    back_rows = lax.all_to_all(row_grad, "expert", split_axis=1, concat_axis=0, tiled=True).reshape(
        n_experts * capacity, width
    )
    back_padded = jnp.concatenate([back_rows, jnp.zeros((1, width), jnp.bfloat16)], axis=0)
    pair_grad = back_padded[slots].reshape(tok_rows, top_k, width)
    mix_grad = gates * (gate_grad - jnp.sum(gates * gate_grad, axis=-1, keepdims=True))
    matches = token_ids[:, :, None] == jnp.arange(n_experts)[None, None, :]
    logit_grad = jnp.sum(jnp.where(matches, mix_grad[:, :, None], 0.0), axis=1).astype(jnp.bfloat16)
    router_part = jnp.einsum("rd,re->de", ffn_in, logit_grad, preferred_element_type=jnp.float32)
    ffn_grad = jnp.sum(pair_grad.astype(jnp.float32), axis=1) + jnp.einsum(
        "re,de->rd", logit_grad, router, preferred_element_type=jnp.float32
    )
    gain_ffn_part = jnp.sum(ffn_grad * plain_two, axis=0)
    scaled_two = ffn_grad * gain_ffn
    resid_grad = cot_full + inv_two * (
        scaled_two - plain_two * jnp.mean(scaled_two * plain_two, axis=-1, keepdims=True)
    )
    resid_low = resid_grad.astype(jnp.bfloat16)
    out_part = jnp.einsum("rd,rh->dh", resid_low, attended, preferred_element_type=jnp.float32)
    att_grad = jnp.einsum(
        "rd,dh->rh", resid_low, out_weight, preferred_element_type=jnp.float32
    ).astype(jnp.bfloat16)
    att_heads = att_grad.reshape(tok_rows, KV_HEADS, group, HEAD)
    row_delta = jnp.sum(
        att_heads.astype(jnp.float32)
        * attended.reshape(tok_rows, KV_HEADS, group, HEAD).astype(jnp.float32),
        axis=-1,
    ).transpose(1, 2, 0)
    key_piece = lax.all_gather(keys, "context", axis=0, tiled=True)
    value_piece = lax.all_gather(values, "context", axis=0, tiled=True)
    scores, visible = key_scores(key_piece)
    soft = jnp.exp(scores - log_total[..., None])
    prob_grad = jnp.einsum(
        "qkgd,skd->kgqs", att_heads, value_piece, preferred_element_type=jnp.float32
    )
    score_grad = (soft * (prob_grad - row_delta[..., None])).astype(jnp.bfloat16)
    query_acc = jnp.einsum(
        "kgqs,skd->kgqd", score_grad, key_piece, preferred_element_type=jnp.float32
    )
    key_part = jnp.einsum("kgqs,qkgd->skd", score_grad, grouped, preferred_element_type=jnp.float32)
    value_part = jnp.einsum(
        "kgqs,qkgd->skd", soft.astype(jnp.bfloat16), att_heads, preferred_element_type=jnp.float32
    )
    pair_acc = jnp.stack([key_part, value_part], axis=1)
    query_acc, pair_acc = (query_acc, pair_acc)
    own_pairs = lax.psum_scatter(
        pair_acc.astype(jnp.bfloat16), "context", scatter_dimension=0, tiled=True
    ).astype(jnp.float32)
    query_grad = (
        unrotate(query_acc.transpose(2, 0, 1, 3).reshape(tok_rows, HEADS, HEAD), cosine, sine)
        * scale
    )
    key_grad = unrotate(own_pairs[:, 0], cosine, sine)
    mixed_grad = jnp.concatenate(
        [
            query_grad.reshape(tok_rows, q_cols),
            key_grad.reshape(tok_rows, kv_cols),
            own_pairs[:, 1].reshape(tok_rows, kv_cols),
        ],
        axis=-1,
    ).astype(jnp.bfloat16)
    qkv_part = jnp.einsum("rd,rc->dc", normed, mixed_grad, preferred_element_type=jnp.float32)
    norm_grad = jnp.einsum("rc,dc->rd", mixed_grad, qkv_weight, preferred_element_type=jnp.float32)
    gain_attn_part = jnp.sum(norm_grad * plain_one, axis=0)
    scaled_one = norm_grad * gain_attn
    input_grad = (
        resid_grad
        + inv_one
        * (scaled_one - plain_one * jnp.mean(scaled_one * plain_one, axis=-1, keepdims=True))
    ).astype(jnp.bfloat16)
    gain_attn_grad, qkv_grad, out_proj_grad, gain_ffn_grad, router_grad = (
        lax.psum_scatter(
            gain_attn_part, ("expert", "context", "dp"), scatter_dimension=0, tiled=True
        ),
        lax.psum_scatter(qkv_part, ("expert", "context", "dp"), scatter_dimension=0, tiled=True),
        lax.psum_scatter(out_part, ("expert", "context", "dp"), scatter_dimension=0, tiled=True),
        lax.psum_scatter(
            gain_ffn_part, ("expert", "context", "dp"), scatter_dimension=0, tiled=True
        ),
        lax.psum_scatter(router_part, ("expert", "context", "dp"), scatter_dimension=0, tiled=True),
    )
    return (
        output[None],
        input_grad[None],
        gain_attn_grad,
        qkv_grad,
        out_proj_grad,
        gain_ffn_grad,
        router_grad,
        expert_in,
        expert_down,
    )


def solution(mesh):
    in_specs = (
        P(("expert", "dp"), "context", None),
        P(("expert", "dp"), None),
        P(("expert", "dp"), "context", None),
        P(("expert", "dp"), "context", None),
        P(),
        P(),
        P(),
        P(),
        P(),
        P("expert", None, None),
        P("expert", None, None),
        P(("expert", "dp"), "context", None),
    )
    out_specs = (
        P(("expert", "dp"), "context", None),
        P(("expert", "dp"), "context", None),
        P(("expert", "context", "dp")),
        P(("expert", "context", "dp"), None),
        P(("expert", "context", "dp"), None),
        P(("expert", "context", "dp")),
        P(("expert", "context", "dp"), None),
        P("expert", ("context", "dp"), None),
        P("expert", ("context", "dp"), None),
    )
    tuned = dict(mesh.shape) == {"expert": 2, "context": 4, "dp": 4}
    body = local if tuned else general
    return jax.shard_map(body, mesh=mesh, in_specs=in_specs, out_specs=out_specs, check_vma=False)
```

```python
import functools

import jax
import jax.numpy as jnp
from jax import lax
from jax.experimental import pallas as pl
from jax.experimental.pallas import tpu as pltpu
from jax.sharding import PartitionSpec as P

HEADS = 12
KV_HEADS = 2
HEAD = 128


ROPE_BASE = 1000000.0
NORM_EPS = 1e-06
MASKED = -1e30


def rope_tables(positions, head_size):
    half_size = head_size // 2
    freqs = ROPE_BASE ** (jnp.arange(half_size).astype(jnp.float32) * (-2.0 / head_size))
    angles = positions[:, None] * freqs[None, :]
    return (jnp.cos(angles)[:, None, :], jnp.sin(angles)[:, None, :])


def rotate(values, cosine, sine):
    half_size = values.shape[-1] // 2
    first = values[..., :half_size]
    second = values[..., half_size:]
    return jnp.concatenate(
        [first * cosine - second * sine, second * cosine + first * sine], axis=-1
    )


def unrotate(values, cosine, sine):
    half_size = values.shape[-1] // 2
    first = values[..., :half_size]
    second = values[..., half_size:]
    return jnp.concatenate(
        [first * cosine + second * sine, second * cosine - first * sine], axis=-1
    )


def softmax_last(scores):
    shifted = jnp.exp(scores - jnp.max(scores, axis=-1, keepdims=True))
    return shifted / jnp.sum(shifted, axis=-1, keepdims=True)


def route(block_ids, block_order, n_experts, capacity):
    flat_ids = block_ids.reshape(-1)
    flat_order = block_order.reshape(-1)
    choose = (flat_ids[:, None] == jnp.arange(n_experts)[None, :]).astype(jnp.int32)
    ordered = jnp.zeros_like(choose).at[flat_order].set(choose)
    earlier = jnp.cumsum(ordered, axis=0, dtype=jnp.int32) - ordered
    ranks = jnp.sum(earlier[flat_order] * choose, axis=1)
    return jnp.where(ranks < capacity, flat_ids * capacity + ranks, n_experts * capacity)


MESH = pl.DeviceIdType.MESH
F32 = jnp.float32
BF16 = jnp.bfloat16


def dot(a, b):
    return jnp.dot(a, b, preferred_element_type=F32)


def dot_nt(a, b):
    return lax.dot_general(a, b, (((1,), (1,)), ((), ())), preferred_element_type=F32)


def dot_tn(a, b):
    return lax.dot_general(a, b, (((0,), (0,)), ((), ())), preferred_element_type=F32)


def plus(a, *more):
    total = a.astype(F32)
    for b in more:
        total = total + b.astype(F32)
    return total.astype(BF16)


def lanes(at, size):
    return pl.ds(pl.multiple_of(at, 128), size)


def rows_at(at, size):
    return pl.ds(pl.multiple_of(at, 16), size)


def remote(src, dst, s, r, dev):
    return pltpu.make_async_remote_copy(
        src_ref=src, dst_ref=dst, send_sem=s, recv_sem=r, device_id=dev, device_id_type=MESH
    )


class Spot:
    def __init__(self):
        e, c, z = lax.axis_index("expert"), lax.axis_index("context"), lax.axis_index("dp")
        self.ctx = lax.axis_size("context")
        self.parts = lax.axis_size("dp")
        self.planes = self.ctx * lax.axis_size("expert")
        y, k = lax.div(c, 2), lax.rem(c, 2)
        self.e, self.c, self.z, self.k = e, c, z, k
        self.me = e * self.ctx + c
        self.xp, self.yp = (1 - e, c, z), (e, (1 - y) * 2 + k, z)
        self.kp, self.yk = (e, y * 2 + 1 - k, z), (e, (1 - y) * 2 + 1 - k, z)
        self.chips = [
            eq * self.ctx + yq * 2 for eq, yq in ((e, y), (1 - e, y), (e, 1 - y), (1 - e, 1 - y))
        ]

    def others(self):
        found = []
        for step in range(1, self.planes):
            other = lax.rem(self.me + step, self.planes)
            found.append((other, (lax.div(other, self.ctx), lax.rem(other, self.ctx), self.z)))
        return found

    def along(self):
        e, c, z = self.e, self.c, self.z
        return [(z < self.parts - 1, (e, c, z + 1)), (z > 0, (e, c, z - 1))]


def greet(peers, extra=()):
    barrier = pltpu.get_barrier_semaphore()
    for peer in peers:
        pl.semaphore_signal(barrier, inc=1, device_id=peer, device_id_type=MESH)
    for there, peer in extra:

        @pl.when(there)
        def _():
            pl.semaphore_signal(barrier, inc=1, device_id=peer, device_id_type=MESH)

    count = len(peers)
    for there, _ in extra:
        count = count + there.astype(jnp.int32)
    pl.semaphore_wait(barrier, count)


class Plane:
    def __init__(self, spot, zcr, zk, rx, ry, s, r):
        self.spot, self.zcr, self.zk, self.rx, self.ry, self.s, self.r = spot, zcr, zk, rx, ry, s, r
        half = zk.shape[1] // 2
        self.lo, self.hi = pl.ds(0, half), pl.ds(half, half)
        self.sent = []

    def push(self, src, dst, i, dev):
        copy = remote(src, dst, self.s.at[i], self.r.at[i], dev)
        copy.start()
        self.sent.append(copy)

    def arrive(self, dst, i):
        remote(dst, dst, self.s.at[i], self.r.at[i], self.spot.kp).wait_recv()

    def give(self, q, src):
        self.push(src, self.zcr.at[q], q, self.spot.kp)

    def fold(self, q, own):
        self.arrive(self.zcr.at[q], q)
        self.zk[q] = plus(own, self.zcr[q])

    def near(self):
        self.push(self.zk.at[1, self.lo], self.rx.at[1], 5, self.spot.xp)
        self.push(self.zk.at[2, self.hi], self.ry.at[1], 8, self.spot.yp)

    def across(self):
        self.push(self.zk.at[3, self.lo], self.rx.at[0], 4, self.spot.xp)
        self.push(self.zk.at[3, self.hi], self.ry.at[0], 7, self.spot.yp)

    def turn(self):
        lo, hi = self.lo, self.hi
        self.arrive(self.rx.at[0], 4)
        self.zk[2, lo] = plus(self.zk[2, lo], self.rx[0])
        self.push(self.zk.at[2, lo], self.ry.at[2], 9, self.spot.yp)
        self.arrive(self.ry.at[0], 7)
        self.zk[1, hi] = plus(self.zk[1, hi], self.ry[0])
        self.push(self.zk.at[1, hi], self.rx.at[2], 6, self.spot.xp)

    def total(self):
        self.arrive(self.rx.at[1], 5)
        self.arrive(self.ry.at[1], 8)
        self.arrive(self.rx.at[2], 6)
        self.arrive(self.ry.at[2], 9)
        return ((self.lo, self.rx.at[1], self.ry.at[2]), (self.hi, self.rx.at[2], self.ry.at[1]))

    def done(self):
        for copy in self.sent:
            copy.wait_send()


def plane_scratch(block, wide):
    return [
        pltpu.VMEM((4, block, wide), BF16),
        pltpu.VMEM((4, block, wide), BF16),
        pltpu.VMEM((3, block // 2, wide), BF16),
        pltpu.VMEM((3, block // 2, wide), BF16),
        pltpu.SemaphoreType.DMA((10,)),
        pltpu.SemaphoreType.DMA((10,)),
    ]


class Line:
    def __init__(self, spot, own, adder, buf, s, r):
        z, last = spot.z, spot.parts - 1
        e, c = spot.e, spot.c
        self.own, self.adder, self.buf, self.s, self.r = own, adder, buf, s, r
        self.z, self.last, self.parts = z, last, spot.parts
        self.ways = [(z, (e, c, z + 1), lambda d: d), (last - z, (e, c, z - 1), lambda d: last - d)]

    def step(self, turn):
        for way, (i, dev, part) in enumerate(self.ways):
            to, s, r = self.buf.at[way, turn - 1], self.s.at[way, turn - 1], self.r.at[way, turn - 1]

            @pl.when(i == 0)
            def _():
                remote(self.own(part(self.parts - turn)), to, s, r, dev).start()

            if turn >= 2:
                came, s_came, r_came = (x.at[way, turn - 2] for x in (self.buf, self.s, self.r))

                @pl.when((i >= 1) & (i <= turn - 1) & (i < self.last))
                def _():
                    remote(came, came, s_came, r_came, dev).wait_recv()
                    self.adder(came, part(self.parts - turn + i))
                    remote(came, to, s, r, dev).start()

    def final(self, put):
        last, z = self.last, self.z
        for way, (i, dev, _) in enumerate(self.ways):
            came = self.buf.at[way, last - 1]

            @pl.when(i >= 1)
            def _():
                remote(came, came, self.s.at[way, last - 1], self.r.at[way, last - 1], dev).wait_recv()

        up, down = self.buf.at[0, last - 1], self.buf.at[1, last - 1]
        pl.when(z == 0)(lambda: put(down))
        pl.when(z == last)(lambda: put(up))
        pl.when((z > 0) & (z < last))(lambda: put(up, down))

    def done(self):
        for way, (i, dev, _) in enumerate(self.ways):
            for turn in range(1, self.parts):
                came = self.buf.at[way, turn - 1]

                @pl.when((i <= turn - 1) & (i < self.last))
                def _():
                    remote(came, came, self.s.at[way, turn - 1], self.r.at[way, turn - 1], dev).wait_send()


def line_scratch(parts, piece):
    return [
        pltpu.VMEM((2, parts - 1) + piece, BF16),
        pltpu.SemaphoreType.DMA((2, parts - 1)),
        pltpu.SemaphoreType.DMA((2, parts - 1)),
    ]


class ExpertLine:
    def __init__(self, spot, ref, at, cols, buf, s, r, fin, spread, a_s, a_r):
        self.spot, self.ref, self.at, self.cols = spot, ref, at, cols
        self.fin, self.spread, self.a_s, self.a_r = fin, spread, a_s, a_r
        self.line = Line(spot, self.own, self.adder, buf, s, r)
        self.step = self.line.step

    def own(self, d):
        return self.ref.at[:, d, :, pl.ds(self.at, self.cols)]

    def piece(self, cc, d):
        return self.ref[cc, d, :, self.at : self.at + self.cols]

    def adder(self, came, d):
        for cc in range(self.spot.ctx):
            came[cc] = plus(came[cc], self.piece(cc, d))

    def final(self):
        spot = self.spot

        def put(*came):
            for cc in range(spot.ctx):
                self.fin[cc] = plus(self.piece(cc, spot.z), *(x[cc] for x in came))

        self.line.final(put)
        for step in range(1, spot.ctx):
            cc = lax.rem(spot.c + step, spot.ctx)
            remote(
                self.fin.at[cc],
                self.spread.at[spot.c],
                self.a_s.at[step - 1],
                self.a_r.at[step - 1],
                (spot.e, cc, spot.z),
            ).start()

    def done(self, out):
        spot = self.spot
        for step in range(1, spot.ctx):
            cc = lax.rem(spot.c + spot.ctx - step, spot.ctx)
            got = remote(
                self.spread.at[cc],
                self.spread.at[cc],
                self.a_s.at[step - 1],
                self.a_r.at[step - 1],
                (spot.e, cc, spot.z),
            )
            got.wait_recv()
            got.wait_send()
            out[cc] = self.spread[cc]
        out[spot.c] = self.fin[spot.c]
        self.line.done()


def expert_scratch(ctx, parts, rows, cols):
    return line_scratch(parts, (ctx, rows, cols)) + [
        pltpu.VMEM((ctx, rows, cols), BF16),
        pltpu.VMEM((ctx, rows, cols), BF16),
        pltpu.SemaphoreType.DMA((ctx - 1,)),
        pltpu.SemaphoreType.DMA((ctx - 1,)),
    ]


class Gather:
    def __init__(self, spot, own, buf, s, r):
        self.spot, self.own, self.buf, self.s, self.r = spot, own, buf, s, r
        half = own.shape[0] // 2
        self.lo, self.hi = pl.ds(0, half), pl.ds(half, half)
        self.x_me, self.y_me, self.d_me = (base + spot.k for base in spot.chips[1:])
        self.side = 1 - 2 * spot.k
        self.sent = []

    def push(self, src, dst, i, dev):
        copy = remote(src, dst, self.s.at[i], self.r.at[i], dev)
        copy.start()
        self.sent.append(copy)

    def move(self, p, rows, i, dev):
        self.push(self.buf.at[p, rows], self.buf.at[p, rows], i, dev)

    def got(self, p, rows, i):
        to = self.buf.at[p, rows]
        remote(to, to, self.s.at[i], self.r.at[i], self.spot.kp).wait_recv()

    def start(self):
        me, own, lo, hi = self.spot.me, self.own, self.lo, self.hi
        self.push(own.at[lo], self.buf.at[me, lo], 0, self.spot.xp)
        self.push(own.at[hi], self.buf.at[me, hi], 3, self.spot.yp)
        self.push(own.at[lo], self.buf.at[me, lo], 6, self.spot.kp)
        self.push(own.at[hi], self.buf.at[me, hi], 13, self.spot.kp)
        self.push(own.at[hi], self.buf.at[me, hi], 1, self.spot.xp)
        self.push(own.at[lo], self.buf.at[me, lo], 2, self.spot.yp)

    def first(self):
        spot = self.spot
        self.got(self.x_me, self.lo, 0)
        self.move(self.x_me, self.lo, 4, spot.yp)
        self.move(self.x_me, self.lo, 7, spot.kp)
        self.got(self.y_me, self.hi, 3)
        self.move(self.y_me, self.hi, 5, spot.xp)
        self.move(self.y_me, self.hi, 10, spot.kp)

    def second(self):
        self.got(self.x_me, self.hi, 1)
        self.move(self.x_me, self.hi, 8, self.spot.kp)
        self.got(self.y_me, self.lo, 2)
        self.move(self.y_me, self.lo, 9, self.spot.kp)

    def third(self):
        self.got(self.d_me, self.lo, 4)
        self.move(self.d_me, self.lo, 11, self.spot.kp)
        self.got(self.d_me, self.hi, 5)
        self.move(self.d_me, self.hi, 12, self.spot.kp)

    def other_core(self, q):
        low_sem, high_sem = ((6, 13), (7, 8), (9, 10), (11, 12))[q]
        p = (self.spot.me, self.x_me, self.y_me, self.d_me)[q] + self.side
        self.got(p, self.lo, low_sem)
        self.got(p, self.hi, high_sem)

    def done(self):
        for copy in self.sent:
            copy.wait_send()


GATHER_COPIES = 14


def front_kernel(
    cap,
    span,
    hidden,
    cot,
    gain_one,
    freqs,
    gain_two,
    router_t,
    ids_t,
    turn_t,
    wqkv_h,
    wout_h,
    normed,
    queries,
    kv,
    lse,
    attended,
    resid,
    ffn_in,
    trig,
    meta,
    cot_all,
    wqkv,
    wout,
    mask,
    vt,
    load_sem,
    kv_s,
    kv_r,
    co_s,
    co_r,
):
    spot = Spot()
    c, ctx, k = spot.c, spot.ctx, spot.k
    tok, width = hidden.shape
    group = HEADS // KV_HEADS
    kv_cols = KV_HEADS * HEAD
    half_head = HEAD // 2
    seq = kv.shape[0]
    spans = span.shape[1]
    size = seq // spans
    mine = spans // ctx
    n_experts = meta.shape[0]
    loads = [
        pltpu.make_async_copy(wqkv_h.at[:, pl.ds(width, 2 * kv_cols)], wqkv.at[:, pl.ds(width, 2 * kv_cols)], load_sem.at[0]),
        pltpu.make_async_copy(wqkv_h.at[:, pl.ds(0, width)], wqkv.at[:, pl.ds(0, width)], load_sem.at[1]),
        pltpu.make_async_copy(wout_h, wout, load_sem.at[2]),
        pltpu.make_async_copy(cot, cot_all.at[spot.me], load_sem.at[3]),
    ]
    for load in loads:
        load.start()
    greet([spot.xp, spot.yp, spot.kp])
    gather = Gather(spot, cot, cot_all, co_s, co_r)

    x = hidden[...].astype(F32)
    inv = lax.rsqrt(jnp.mean(x * x, axis=-1, keepdims=True) + NORM_EPS)
    normed[...] = (x * inv * gain_one[...]).astype(BF16)

    along = lax.broadcasted_iota(jnp.int32, (tok, HEAD), 0)
    start_one, start_two = span[0, c * mine] * size, (span[0, c * mine + 1] - 1) * size
    place = jnp.where(along < size, start_one, start_two) + along
    angle = place.astype(F32) * freqs[...]
    cosine, sine = jnp.cos(angle), jnp.sin(angle)
    lane = lax.broadcasted_iota(jnp.int32, (tok, HEAD), 1)
    sine = jnp.where(lane < half_head, -sine, sine)
    trig[0] = cosine
    trig[1] = sine

    def rotate_in(w):
        return w * cosine + pltpu.roll(w, half_head, 1) * sine

    loads[0].wait()
    raw = dot(normed[...], wqkv[:, width:])
    own = rows_at(c * tok, tok)
    for g in range(KV_HEADS):
        at = slice(g * HEAD, (g + 1) * HEAD)
        kv[own, at] = rotate_in(raw[:, at]).astype(BF16)
    kv[own, kv_cols:] = raw[:, kv_cols:].astype(BF16)

    def kv_copy(rows, i, dev):
        return remote(kv.at[rows], kv.at[rows], kv_s.at[i], kv_r.at[i], dev)

    flip_c = lax.rem(c + 2, ctx)
    near_c = c + 1 - 2 * k
    across_c = lax.rem(near_c + 2, ctx)
    sent = [kv_copy(own, 1, spot.yp), kv_copy(own, 0, spot.kp)]
    for copy in sent:
        copy.start()
    gather.start()

    loads[1].wait()
    step = 256

    @pl.loop(0, width // step)
    def _(n):
        at = lanes(n * step, step)
        raw = dot(normed[...], wqkv[:, at])
        for i in range(step // HEAD):
            w = raw[:, i * HEAD : (i + 1) * HEAD]
            queries[:, lanes(n * step + i * HEAD, HEAD)] = (rotate_in(w) * HEAD**-0.5).astype(BF16)

    flip = rows_at(flip_c * tok, tok)
    kv_copy(flip, 1, spot.kp).wait_recv()
    sent.append(kv_copy(flip, 2, spot.kp))
    sent[-1].start()

    expert = lax.broadcasted_iota(jnp.int32, (n_experts, tok), 0)
    never = tok * ids_t.shape[0]
    turn = jnp.full((n_experts, tok), never, jnp.int32)
    for i in range(ids_t.shape[0]):
        turn = jnp.where(ids_t[i : i + 1, :] == expert, turn_t[i : i + 1, :], turn)
    turn_f = turn.astype(F32)
    tall = jnp.concatenate([turn_f, jnp.full((HEAD - n_experts, tok), float(never), F32)], axis=0).T
    meta[...] = jnp.zeros(meta.shape, F32)
    for g in range(n_experts):
        row = turn_f[g : g + 1, :]
        rank = jnp.sum(jnp.where(tall[:, g : g + 1] < row, 1.0, 0.0), axis=0, keepdims=True)
        meta[g, 0:1, :] = jnp.where((row < never) & (rank < cap), rank, -1.0)

    along_q = lax.broadcasted_iota(jnp.int32, (size, tok), 1)
    q_pos = jnp.where(along_q < size, start_one, start_two) + along_q
    for s in range(spans):
        k_pos = span[0, s] * size + lax.broadcasted_iota(jnp.int32, (size, tok), 0)
        mask[s * size : (s + 1) * size, :] = jnp.where(k_pos <= q_pos, 0.0, MASKED)

    near, across = rows_at(near_c * tok, tok), rows_at(across_c * tok, tok)
    kv_copy(near, 0, spot.kp).wait_recv()
    kv_copy(across, 2, spot.kp).wait_recv()
    for g in range(KV_HEADS):
        vt[g] = kv[:, kv_cols + g * HEAD : kv_cols + (g + 1) * HEAD].astype(F32).T.astype(BF16)
    lse[...] = jnp.zeros(lse.shape, F32)

    def heads(g, first, count):
        @pl.loop(first, first + count)
        def _(h):
            at = lanes(h * HEAD, HEAD)
            scores = dot_nt(kv[:, g * HEAD : (g + 1) * HEAD], queries[:, at]) + mask[...]
            top = jnp.max(scores, axis=0, keepdims=True)
            weights = jnp.exp(scores - top)
            total = jnp.sum(weights, axis=0, keepdims=True)
            lse[pl.ds(h, 1), :] = top + jnp.log(total)
            out = dot(vt[g], weights.astype(BF16)) / total
            attended[:, at] = out.T.astype(BF16)

    heads(0, 0, 3)
    gather.first()
    heads(0, 3, 3)
    heads(1, 6, 3)
    gather.second()
    heads(1, 9, 3)

    loads[2].wait()

    @pl.loop(0, width // step)
    def _(n):
        at = lanes(n * step, step)
        resid[:, at] = hidden[:, at].astype(F32) + dot_nt(attended[...], wout[at, :])

    r = resid[...]
    inv = lax.rsqrt(jnp.mean(r * r, axis=-1, keepdims=True) + NORM_EPS)
    ffn_in[...] = (r * inv * gain_two[...]).astype(BF16)
    logits = dot_nt(router_t[...], ffn_in[...])[:n_experts]
    logits = jnp.where(turn < never, logits, MASKED)
    shifted = jnp.exp(logits - jnp.max(logits, axis=0, keepdims=True))
    gates = shifted / jnp.sum(shifted, axis=0, keepdims=True)
    for g in range(n_experts):
        meta[g, 1:2, :] = gates[g : g + 1, :]
    gather.third()
    for q in range(4):
        gather.other_core(q)
    loads[3].wait()
    gather.done()
    for copy in sent:
        copy.wait_send()


def run_front(cap, span, hidden, cot, gain_one, freqs, gain_two, router_t, ids_t, turn_t, wqkv, wout, ctx, planes):
    tok, width = hidden.shape
    seq = tok * ctx
    n_experts = planes
    kv_cols = 2 * KV_HEADS * HEAD
    vm, anyspace = pl.BlockSpec(memory_space=pltpu.VMEM), pl.BlockSpec(memory_space=pl.ANY)
    sm = pl.BlockSpec(memory_space=pltpu.SMEM)
    shape = jax.ShapeDtypeStruct
    dma = pltpu.SemaphoreType.DMA
    return pl.pallas_call(
        functools.partial(front_kernel, cap),
        out_shape=(
            shape((tok, width), BF16),
            shape((tok, width), BF16),
            shape((seq, kv_cols), BF16),
            shape((16, tok), F32),
            shape((tok, width), BF16),
            shape((tok, width), F32),
            shape((tok, width), BF16),
            shape((2, tok, HEAD), F32),
            shape((n_experts, 8, tok), F32),
            shape((planes, tok, width), BF16),
        ),
        in_specs=[sm] + [vm] * 8 + [anyspace] * 2,
        out_specs=(vm,) * 9 + (anyspace,),
        scratch_shapes=[
            pltpu.VMEM(wqkv.shape, BF16),
            pltpu.VMEM(wout.shape, BF16),
            pltpu.VMEM((seq, tok), F32),
            pltpu.VMEM((KV_HEADS, HEAD, seq), BF16),
            dma((4,)),
            dma((3,)),
            dma((3,)),
            dma((GATHER_COPIES,)),
            dma((GATHER_COPIES,)),
        ],
        compiler_params=pltpu.CompilerParams(
            collective_id=4, has_side_effects=True, vmem_limit_bytes=56 * 2**20
        ),
        cost_estimate=pl.CostEstimate(flops=5 * 10**9, bytes_accessed=20 * 10**6, transcendentals=4 * 10**6),
    )(span, hidden, cot, gain_one, freqs, gain_two, router_t, ids_t, turn_t, wqkv, wout)


def ffn_kernel(cap, ffn, cot_h, meta, win_h, wdn_h, zout_h, pg_out, gg_out, gwin_h, ex_out, *scratch):
    agb, metas, cotb, win, wdn, xs, ds, hid, igs, pgs, ggs, ggr, stage, gwdn, pgt = scratch[:15]
    load_sem, ag_s, ag_r, me_s, me_r, gg_s, gg_r, st_sem = scratch[15:23]
    plane_refs, line_refs = scratch[23:29], scratch[29:]
    spot = Spot()
    c, k, me = spot.c, spot.k, spot.me
    kp = spot.kp
    tok, width = ffn.shape
    ff = wdn.shape[1]
    planes, ctx = spot.planes, spot.ctx
    chips = spot.chips

    loads = [
        pltpu.make_async_copy(win_h.at[c], win, load_sem.at[0]),
        pltpu.make_async_copy(wdn_h.at[c], wdn, load_sem.at[1]),
        pltpu.make_async_copy(cot_h, cotb, load_sem.at[2]),
    ]
    for load in loads:
        load.start()
    others = spot.others()
    greet([dev for _, dev in others], spot.along())
    plane = Plane(spot, *plane_refs)
    line = ExpertLine(spot, gwdn, 0, ff, *line_refs)
    gather = Gather(spot, ffn, agb, ag_s, ag_r)
    for step, (other, dev) in enumerate(others):
        remote(meta.at[other], metas.at[me], me_s.at[step], me_r.at[step], dev).start()
    gather.start()
    agb[me] = ffn[...]
    metas[me] = meta[me]
    slot_rows = lax.broadcasted_iota(jnp.int32, (cap, tok), 0).astype(F32)
    step = 256

    def spots(p):
        return jnp.where(slot_rows == metas[p, 0:1, :], 1.0, 0.0)

    def gate_of(p, hot):
        return jnp.sum(hot * metas[p, 1:2, :], axis=1, keepdims=True)

    def group(q):
        base = chips[q]
        rows = pl.ds(q * 2 * cap, 2 * cap)
        for kk in range(2):
            p = base + kk
            hot = spots(p)
            low = hot.astype(BF16)
            part = pl.ds(q * 2 * cap + kk * cap, cap)
            xs[part, :] = dot(low, agb[p]).astype(BF16)
            ds[part, :] = (dot(low, cotb[p]) * gate_of(p, hot)).astype(BF16)

        @pl.loop(0, ff // step)
        def _(n):
            gate_cols, up_cols = lanes(n * step, step), lanes(ff + n * step, step)
            x = xs[rows, :]
            g = dot(x, win[:, gate_cols])
            u = dot(x, win[:, up_cols])
            s = 1.0 / (1.0 + jnp.exp(-g))
            act = g * s
            hid[rows, gate_cols] = (act * u).astype(BF16)
            h = dot(ds[rows, :], wdn[:, gate_cols])
            igs[rows, gate_cols] = (h * u * (s * (1.0 + g * (1.0 - s)))).astype(BF16)
            igs[rows, up_cols] = (h * act).astype(BF16)

        @pl.loop(0, width // step)
        def _(n):
            cols = lanes(n * step, step)
            pgs[:, cols] = dot_nt(igs[rows, :], win[cols, :]).astype(BF16)

        mine, theirs = rows_at(k * cap, cap), rows_at((1 - k) * cap, cap)
        zcs = stage.at[q]
        zcs[...] = dot_tn(spots(base + 1 - k).astype(BF16), pgs[theirs, :]).astype(BF16)
        plane.give(q, zcs)
        plane.zk[q] = dot_tn(spots(base + k).astype(BF16), pgs[mine, :]).astype(BF16)

    def fold(q):
        plane.fold(q, plane.zk[q])

    for load in loads:
        load.wait()
    for n in range(planes - 1):
        source = lax.rem(me + planes - 1 - n, planes)
        remote(metas.at[source], metas.at[source], me_s.at[n], me_r.at[n], kp).wait_recv()
    gather.other_core(0)
    group(0)
    gather.first()
    gather.second()
    gather.other_core(1)
    group(1)
    gather.third()
    gather.other_core(2)
    group(2)
    fold(1)
    fold(2)
    plane.near()
    gather.other_core(3)
    group(3)
    fold(3)
    plane.across()

    tall = width // ctx

    @pl.loop(0, ctx)
    def _(n):
        tile = dot_tn(ds[:, lanes(n * tall, tall)], hid[...]).astype(BF16)
        for d in range(gwdn.shape[1]):
            gwdn[n, d] = tile[d * gwdn.shape[2] : (d + 1) * gwdn.shape[2]]

    line.step(1)
    fold(0)
    plane.turn()

    gather.done()

    for q, base in enumerate(chips):

        @pl.loop(0, width // step)
        def _(n):
            cols = lanes(n * step, step)
            pgs[:, cols] = dot_nt(hid[pl.ds(q * 2 * cap, 2 * cap), :], wdn[cols, :]).astype(BF16)

        for kk in range(2):
            p = base + kk
            i = q * 2 + kk
            hot = spots(p)
            rows = pgs[pl.ds(kk * cap, cap), :]
            ggs[p, 0:1, :] = jnp.sum(hot * dot_nt(rows, cotb[p]), axis=0, keepdims=True)
            scaled = (rows.astype(F32) * gate_of(p, hot)).astype(BF16)
            agb[p] = dot_tn(hot.astype(BF16), scaled).astype(BF16)
            pltpu.make_async_copy(agb.at[p], zout_h.at[p], st_sem.at[i]).start()
    ggr[me] = ggs[me]
    for n, (other, dev) in enumerate(others):
        remote(ggs.at[other], ggr.at[me], gg_s.at[n], gg_r.at[n], dev).start()
    line.step(2)
    half_wide = ff

    @pl.loop(0, 2 * ctx)
    def _(n):
        slot = lax.rem(n, 2)
        rows = lanes(lax.div(n, 2) * tall, tall)
        cols = lanes(slot * half_wide, half_wide)
        tile = pgt.at[slot]
        to = pltpu.make_async_copy(tile, gwin_h.at[rows, cols], load_sem.at[slot])

        @pl.when(n >= 2)
        def _():
            to.wait()

        tile[...] = dot_tn(xs[:, rows], igs[:, cols]).astype(BF16)
        to.start()

    for slot in range(2):
        pltpu.make_async_copy(pgt.at[slot], gwin_h.at[pl.ds(0, tall), pl.ds(0, half_wide)], load_sem.at[slot]).wait()
    line.step(3)
    for rows, first, second in plane.total():
        pg_out[rows, :] = (
            plane.zk[0, rows].astype(F32) + first[...].astype(F32) + second[...].astype(F32)
        )
    for n in range(planes - 1):
        source = lax.rem(me + planes - 1 - n, planes)
        remote(ggr.at[source], ggr.at[source], gg_s.at[n], gg_r.at[n], kp).wait_recv()
    for p in range(planes):
        gg_out[p : p + 1, :] = ggr[p, 0:1, :]
    line.final()
    for i in range(planes):
        pltpu.make_async_copy(agb.at[0], zout_h.at[0], st_sem.at[i]).wait()
    for n, (other, dev) in enumerate(others):
        remote(meta.at[other], metas.at[other], me_s.at[n], me_r.at[n], dev).wait_send()
        remote(ggs.at[other], ggr.at[other], gg_s.at[n], gg_r.at[n], dev).wait_send()
    plane.done()
    line.done(ex_out)


def run_ffn(cap, ffn, cot_all, meta, win, wdn, parts):
    tok, width = ffn.shape
    ff = wdn.shape[2]
    planes = cot_all.shape[0]
    ctx = win.shape[0]
    rows = planes * cap
    piece = width // (ctx * parts)
    vm, anyspace = pl.BlockSpec(memory_space=pltpu.VMEM), pl.BlockSpec(memory_space=pl.ANY)
    shape = jax.ShapeDtypeStruct
    dma = pltpu.SemaphoreType.DMA
    return pl.pallas_call(
        functools.partial(ffn_kernel, cap),
        out_shape=(
            shape((planes, tok, width), BF16),
            shape((tok, width), F32),
            shape((planes, tok), F32),
            shape((width, 2 * ff), BF16),
            shape((ctx, piece, ff), BF16),
        ),
        in_specs=[vm, anyspace, vm, anyspace, anyspace],
        out_specs=(anyspace, vm, vm, anyspace, vm),
        scratch_shapes=[
            pltpu.VMEM((planes, tok, width), BF16),
            pltpu.VMEM((planes, 8, tok), F32),
            pltpu.VMEM((planes, tok, width), BF16),
            pltpu.VMEM((width, 2 * ff), BF16),
            pltpu.VMEM((width, ff), BF16),
            pltpu.VMEM((rows, width), BF16),
            pltpu.VMEM((rows, width), BF16),
            pltpu.VMEM((rows, ff), BF16),
            pltpu.VMEM((rows, 2 * ff), BF16),
            pltpu.VMEM((2 * cap, width), BF16),
            pltpu.VMEM((planes, 8, tok), F32),
            pltpu.VMEM((planes, 8, tok), F32),
            pltpu.VMEM((4, tok, width), BF16),
            pltpu.VMEM((ctx, parts, piece, ff), BF16),
            pltpu.VMEM((2, width // ctx, ff), BF16),
            dma((3,)),
            dma((GATHER_COPIES,)),
            dma((GATHER_COPIES,)),
            dma((planes - 1,)),
            dma((planes - 1,)),
            dma((planes - 1,)),
            dma((planes - 1,)),
            dma((planes,)),
        ]
        + plane_scratch(tok, width)
        + expert_scratch(ctx, parts, piece, ff),
        compiler_params=pltpu.CompilerParams(
            collective_id=1, has_side_effects=True, vmem_limit_bytes=62 * 2**20
        ),
        cost_estimate=pl.CostEstimate(flops=25 * 10**9, bytes_accessed=50 * 10**6, transcendentals=10**6),
    )(ffn, cot_all, meta, win, wdn)


def attend_back_kernel(
    span,
    resid,
    cot,
    pg,
    gg,
    meta,
    attended,
    ffn_in,
    queries,
    kv,
    lse,
    trig,
    wout,
    router_t,
    gain,
    zout_h,
    gwin_h,
    output,
    resid_grad,
    mixed_grad,
    out_red,
    small,
    ex_out,
    *scratch,
):
    zkeep, gwin, osend, low, attg, mask, delta, kt, dk, dv, dq, kvs, kvr = scratch[:13]
    load_sem, kv_s, kv_r = scratch[13:16]
    tok_refs, out_refs, line_refs = scratch[16:22], scratch[22:28], scratch[28:]
    spot = Spot()
    c, k, z, ctx = spot.c, spot.k, spot.z, spot.ctx
    tok, width = cot.shape
    cols = ex_out.shape[2]
    block = out_red.shape[0]
    heads_kv = KV_HEADS
    group = HEADS // KV_HEADS
    half_head = HEAD // 2
    gwin_load = pltpu.make_async_copy(gwin_h.at[:, :, :, pl.ds(0, cols)], gwin, load_sem.at[0])
    gwin_load.start()
    keeps = []
    for q, base in enumerate(spot.chips):
        keeps.append(pltpu.make_async_copy(zout_h.at[base + k], zkeep.at[q], load_sem.at[1 + q]))
        keeps[-1].start()
    greet([spot.xp, spot.yp, spot.kp, spot.yk], spot.along())
    tokens, weights = Plane(spot, *tok_refs), Plane(spot, *out_refs)
    line = ExpertLine(spot, gwin, 0, cols, *line_refs)
    for q, base in enumerate(spot.chips):
        tokens.give(q, zout_h.at[base + 1 - k])
    gwin_load.wait()
    line.step(1)

    gate = jnp.concatenate([meta[g, 1:2, :] for g in range(meta.shape[0])], axis=0)
    seen = gate * gg[...]
    mix = seen - gate * jnp.sum(seen, axis=0, keepdims=True)
    mix = jnp.concatenate([mix, jnp.zeros((HEAD - mix.shape[0], tok), F32)], axis=0)
    logit_t = mix.astype(BF16)
    r = resid[...]
    inv = lax.rsqrt(jnp.mean(r * r, axis=-1, keepdims=True) + NORM_EPS)
    plain = r * inv
    ffn_grad = pg[...] + dot_tn(logit_t[: router_t.shape[0]], router_t[...])
    gain_row = jnp.sum(ffn_grad * plain, axis=0, keepdims=True)
    scaled = ffn_grad * gain[...]
    back = cot[...].astype(F32) + inv * (
        scaled - plain * jnp.mean(scaled * plain, axis=-1, keepdims=True)
    )
    resid_grad[...] = back
    low[...] = back.astype(BF16)
    lane = lax.broadcasted_iota(jnp.int32, (width, HEAD), 1)
    gain_col = jnp.broadcast_to(gain_row, (HEAD, width)).T
    routed = dot_tn(ffn_in[...], logit_t.T)
    small[...] = jnp.where(lane == gate.shape[0], gain_col, routed).astype(BF16)

    for q in (1, 2):
        keeps[q].wait()
        tokens.fold(q, zkeep[q])
    tokens.near()
    keeps[3].wait()
    tokens.fold(3, zkeep[3])
    tokens.across()
    keeps[0].wait()
    tokens.fold(0, zkeep[0])

    for q in (1, 2, 3, 0):
        at = lanes(spot.chips[q] * block, 2 * block)
        osend[q] = dot_tn(low[:, at], attended[...]).astype(BF16)
        weights.give(q, osend.at[q, rows_at((1 - k) * block, block)])

    step = 256

    @pl.loop(0, width // step)
    def _(n):
        at = lanes(n * step, step)
        attg[:, at] = dot(low[...], wout[:, at]).astype(BF16)

    seq = kv.shape[0]
    spans = span.shape[1]
    size = seq // spans
    mine = spans // ctx
    along_q = lax.broadcasted_iota(jnp.int32, (size, tok), 1)
    q_pos = jnp.where(along_q < size, span[0, c * mine] * size, (span[0, c * mine + 1] - 1) * size) + along_q
    for s in range(spans):
        k_pos = span[0, s] * size + lax.broadcasted_iota(jnp.int32, (size, tok), 0)
        mask[s * size : (s + 1) * size, :] = jnp.where(k_pos <= q_pos, 0.0, MASKED)

    lane_h = lax.broadcasted_iota(jnp.int32, (tok, HEAD), 1)
    deltas = jnp.zeros((tok, HEAD), F32)
    for h in range(HEADS):
        at = slice(h * HEAD, (h + 1) * HEAD)
        term = jnp.sum(attg[:, at].astype(F32) * attended[:, at].astype(F32), axis=-1, keepdims=True)
        deltas = jnp.where(lane_h == h, term, deltas)
    delta[...] = deltas.T
    for g in range(heads_kv):
        kt[g] = kv[:, g * HEAD : (g + 1) * HEAD].astype(F32).T.astype(BF16)

    def head(g, h):
        at = lanes(h * HEAD, HEAD)
        k_at = slice(g * HEAD, (g + 1) * HEAD)
        v_at = slice((heads_kv + g) * HEAD, (heads_kv + g + 1) * HEAD)
        q, a = queries[:, at], attg[:, at]
        soft = jnp.exp(dot_nt(kv[:, k_at], q) + mask[...] - lse[pl.ds(h, 1), :])
        prob = dot_nt(kv[:, v_at], a)
        score = (soft * (prob - delta[pl.ds(h, 1), :])).astype(BF16)
        dq[:, at] = dot(kt[g], score).T
        dk[...] += dot(score, q)
        dv[...] += dot(soft.astype(BF16), a)

    def send_kv(g):
        for cc in range(ctx):
            rows = slice(cc * tok, (cc + 1) * tok)
            kvs[g, cc, :, :HEAD] = dk[rows, :].astype(BF16)
            kvs[g, cc, :, HEAD:] = dv[rows, :].astype(BF16)
        for n in range(1, ctx):
            cc = lax.rem(c + n, ctx)
            remote(kvs.at[g, cc], kvr.at[g, c], kv_s.at[g, n - 1], kv_r.at[g, n - 1], (spot.e, cc, z)).start()

    def heads(g, first, count):
        @pl.loop(first, first + count)
        def _(h):
            head(g, h)

    def clear():
        dk[...] = jnp.zeros(dk.shape, F32)
        dv[...] = jnp.zeros(dv.shape, F32)

    def own_part(q):
        return osend[q, rows_at(k * block, block)]

    clear()
    heads(0, 0, 2)
    for q in (1, 2):
        weights.fold(q, own_part(q))
    weights.near()
    weights.fold(3, own_part(3))
    weights.across()
    weights.fold(0, own_part(0))
    heads(0, 2, 2)
    line.step(2)
    heads(0, 4, 2)
    send_kv(0)
    tokens.turn()
    clear()
    heads(1, 6, 2)
    line.step(3)
    heads(1, 8, 2)
    heads(1, 10, 2)
    send_kv(1)
    weights.turn()
    for rows, first, second in tokens.total():
        out_sum = tokens.zk[0, rows].astype(F32) + first[...].astype(F32) + second[...].astype(F32)
        output[rows, :] = (resid[rows, :] + out_sum).astype(BF16)

    cosine, sine = trig[0], trig[1]

    def unrotate(w):
        return w * cosine - pltpu.roll(w, half_head, 1) * sine

    for h in range(HEADS):
        at = slice(h * HEAD, (h + 1) * HEAD)
        mixed_grad[:, at] = (unrotate(dq[:, at]) * HEAD**-0.5).astype(BF16)
    line.final()
    for rows, first, second in weights.total():
        out_red[rows, :] = plus(weights.zk[0, rows], first[...], second[...])
    for g in range(heads_kv):
        own = kvs[g, c].astype(F32)
        for n in range(1, ctx):
            cc = lax.rem(c + ctx - n, ctx)
            got = remote(kvr.at[g, cc], kvr.at[g, cc], kv_s.at[g, n - 1], kv_r.at[g, n - 1], spot.kp)
            got.wait_recv()
            own = own + kvr[g, cc].astype(F32)
        at = width + g * HEAD
        mixed_grad[:, at : at + HEAD] = unrotate(own[:, :HEAD]).astype(BF16)
        at = width + (heads_kv + g) * HEAD
        mixed_grad[:, at : at + HEAD] = own[:, HEAD:].astype(BF16)
    for g in range(heads_kv):
        for n in range(1, ctx):
            cc = lax.rem(c + n, ctx)
            remote(kvs.at[g, cc], kvr.at[g, cc], kv_s.at[g, n - 1], kv_r.at[g, n - 1], spot.kp).wait_send()
    tokens.done()
    weights.done()
    line.done(ex_out)


def run_attend_back(
    span, resid, cot, pg, gg, meta, attended, ffn_in, queries, kv, lse, trig, wout, router_t, gain, zout, gwin
):
    tok, width = cot.shape
    planes = zout.shape[0]
    ctx, parts, piece, wide = gwin.shape
    cols = wide // 2
    block = width // planes
    seq, kv_cols = kv.shape
    vm, anyspace = pl.BlockSpec(memory_space=pltpu.VMEM), pl.BlockSpec(memory_space=pl.ANY)
    sm = pl.BlockSpec(memory_space=pltpu.SMEM)
    shape = jax.ShapeDtypeStruct
    dma = pltpu.SemaphoreType.DMA
    return pl.pallas_call(
        attend_back_kernel,
        out_shape=(
            shape((tok, width), BF16),
            shape((tok, width), F32),
            shape((tok, width + kv_cols), BF16),
            shape((block, width), BF16),
            shape((width, HEAD), BF16),
            shape((ctx, piece, cols), BF16),
        ),
        in_specs=[sm] + [vm] * 14 + [anyspace] * 2,
        out_specs=(vm,) * 6,
        scratch_shapes=[
            pltpu.VMEM((4, tok, width), BF16),
            pltpu.VMEM((ctx, parts, piece, cols), BF16),
            pltpu.VMEM((4, 2 * block, width), BF16),
            pltpu.VMEM((tok, width), BF16),
            pltpu.VMEM((tok, width), BF16),
            pltpu.VMEM((seq, tok), F32),
            pltpu.VMEM((HEAD, tok), F32),
            pltpu.VMEM((KV_HEADS, HEAD, seq), BF16),
            pltpu.VMEM((seq, HEAD), F32),
            pltpu.VMEM((seq, HEAD), F32),
            pltpu.VMEM((tok, width), F32),
            pltpu.VMEM((KV_HEADS, ctx, tok, 2 * HEAD), BF16),
            pltpu.VMEM((KV_HEADS, ctx, tok, 2 * HEAD), BF16),
            dma((5,)),
            dma((KV_HEADS, ctx - 1)),
            dma((KV_HEADS, ctx - 1)),
        ]
        + plane_scratch(tok, width)
        + plane_scratch(block, width)
        + expert_scratch(ctx, parts, piece, cols),
        compiler_params=pltpu.CompilerParams(
            collective_id=2, has_side_effects=True, vmem_limit_bytes=62 * 2**20
        ),
        cost_estimate=pl.CostEstimate(flops=8 * 10**9, bytes_accessed=40 * 10**6, transcendentals=10**6),
    )(
        span, resid, cot, pg, gg, meta, attended, ffn_in, queries, kv, lse, trig, wout, router_t, gain, zout, gwin
    )


def last_kernel(
    normed, mixed_grad, hidden, resid_grad, wqkv, gain, small, out_red, gwin_h, input_grad, qkv_out, proj_out, ex_out, *scratch
):
    gwin, asend, bsend, norm_grad, smalls, total, load_sem = scratch[:7]
    a_refs, b_refs, qkv_refs, proj_refs, line_refs = (
        scratch[7:13],
        scratch[13:19],
        scratch[19:22],
        scratch[22:25],
        scratch[25:],
    )
    spot = Spot()
    k, z = spot.k, spot.z
    tok, width = normed.shape
    cols = ex_out.shape[2]
    block = out_red.shape[0]
    piece = proj_out.shape[0]
    kv_wide = mixed_grad.shape[1] - width
    load = pltpu.make_async_copy(gwin_h.at[:, :, :, pl.ds(cols, cols)], gwin, load_sem.at[0])
    load.start()
    greet([spot.xp, spot.yp, spot.kp, spot.yk], spot.along())
    first, second = Plane(spot, *a_refs), Plane(spot, *b_refs)
    line = ExpertLine(spot, gwin, 0, cols, *line_refs)

    def shared_line(ref, refs):
        def own(d):
            return ref.at[rows_at(d * piece, piece)]

        def adder(came, d):
            came[...] = plus(came[...], own(d)[...])

        return Line(spot, own, adder, *refs)

    qkv, proj = shared_line(total, qkv_refs), shared_line(out_red, proj_refs)
    def put_shared(to, ref, came):
        to[...] = plus(ref[rows_at(z * piece, piece)], *(x[...] for x in came))

    mine, theirs = rows_at(k * block, block), rows_at((1 - k) * block, block)
    load.wait()
    line.step(1)
    proj.step(1)
    for q in (1, 2, 3, 0):
        at = lanes(spot.chips[q] * block, 2 * block)
        asend[q] = dot_tn(normed[:, at], mixed_grad[:, :width]).astype(BF16)
        first.give(q, asend.at[q, theirs])
    first.fold(1, asend[1, mine])
    first.fold(2, asend[2, mine])
    first.near()
    first.fold(3, asend[3, mine])
    first.across()
    first.fold(0, asend[0, mine])

    step = 256

    @pl.loop(0, width // step)
    def _(n):
        at = lanes(n * step, step)
        norm_grad[:, at] = dot_nt(mixed_grad[...], wqkv[at, :])

    x = hidden[...].astype(F32)
    inv = lax.rsqrt(jnp.mean(x * x, axis=-1, keepdims=True) + NORM_EPS)
    plain = x * inv
    ng = norm_grad[...]
    gain_row = jnp.sum(ng * plain, axis=0, keepdims=True)
    scaled = ng * gain[...]
    input_grad[...] = (
        resid_grad[...]
        + inv * (scaled - plain * jnp.mean(scaled * plain, axis=-1, keepdims=True))
    ).astype(BF16)
    lane = lax.broadcasted_iota(jnp.int32, (width, HEAD), 1)
    gain_col = jnp.broadcast_to(gain_row, (HEAD, width)).T
    smalls[...] = jnp.where(lane == HEAD - 1, gain_col, small[...].astype(F32)).astype(BF16)
    for q in (1, 2, 3, 0):
        at = lanes(spot.chips[q] * block, 2 * block)
        bsend[q, :, :kv_wide] = dot_tn(normed[:, at], mixed_grad[:, width:]).astype(BF16)
        bsend[q, :, kv_wide:] = smalls[rows_at(spot.chips[q] * block, 2 * block), :]
        second.give(q, bsend.at[q, theirs])
    first.turn()
    second.fold(1, bsend[1, mine])
    second.fold(2, bsend[2, mine])
    second.near()
    second.fold(3, bsend[3, mine])
    second.across()
    second.fold(0, bsend[0, mine])
    line.step(2)
    proj.step(2)
    for rows, one, two in first.total():
        total[rows, :width] = plus(first.zk[0, rows], one[...], two[...])
    second.turn()
    line.step(3)
    proj.step(3)
    for rows, one, two in second.total():
        total[rows, width:] = plus(second.zk[0, rows], one[...], two[...])
    qkv.step(1)
    proj.final(lambda *came: put_shared(proj_out, out_red, came))
    line.final()
    qkv.step(2)
    line.done(ex_out)
    qkv.step(3)
    proj.done()
    first.done()
    second.done()
    qkv.final(lambda *came: put_shared(qkv_out, total, came))
    qkv.done()


def run_last(normed, mixed_grad, hidden, resid_grad, wqkv, gain, small, out_red, gwin):
    tok, width = normed.shape
    block = out_red.shape[0]
    ctx, parts, rows, wide = gwin.shape
    cols = wide // 2
    piece = block // parts
    rest = mixed_grad.shape[1] - width + HEAD
    vm, anyspace = pl.BlockSpec(memory_space=pltpu.VMEM), pl.BlockSpec(memory_space=pl.ANY)
    shape = jax.ShapeDtypeStruct
    return pl.pallas_call(
        last_kernel,
        out_shape=(
            shape((tok, width), BF16),
            shape((piece, width + rest), BF16),
            shape((piece, width), BF16),
            shape((ctx, rows, cols), BF16),
        ),
        in_specs=[vm] * 8 + [anyspace],
        out_specs=(vm,) * 4,
        scratch_shapes=[
            pltpu.VMEM((ctx, parts, rows, cols), BF16),
            pltpu.VMEM((4, 2 * block, width), BF16),
            pltpu.VMEM((4, 2 * block, rest), BF16),
            pltpu.VMEM((tok, width), F32),
            pltpu.VMEM((width, HEAD), BF16),
            pltpu.VMEM((block, width + rest), BF16),
            pltpu.SemaphoreType.DMA((1,)),
        ]
        + plane_scratch(block, width)
        + plane_scratch(block, rest)
        + line_scratch(parts, (piece, width + rest))
        + line_scratch(parts, (piece, width))
        + expert_scratch(ctx, parts, rows, cols),
        compiler_params=pltpu.CompilerParams(
            collective_id=3, has_side_effects=True, vmem_limit_bytes=62 * 2**20
        ),
        cost_estimate=pl.CostEstimate(flops=4 * 10**9, bytes_accessed=40 * 10**6, transcendentals=0),
    )(normed, mixed_grad, hidden, resid_grad, wqkv, gain, small, out_red, gwin)


def local(
    hidden_in,
    span_order,
    expert_ids,
    priority,
    gain_attn,
    qkv_weight,
    out_weight,
    gain_ffn,
    router,
    in_weight,
    down_weight,
    cotangent,
):
    _, tok_rows, width = hidden_in.shape
    ctx, parts = lax.axis_size("context"), lax.axis_size("dp")
    planes = ctx * lax.axis_size("expert")
    n_experts = router.shape[1]
    top_k = expert_ids.shape[2]
    capacity = (9 * tok_rows * top_k + 8 * n_experts - 1) // (8 * n_experts)
    ff = down_weight.shape[2]
    half_freqs = ROPE_BASE ** (jnp.arange(HEAD // 2).astype(jnp.float32) * (-2.0 / HEAD))
    freqs = jnp.concatenate([half_freqs, half_freqs])[None]
    router_t = jnp.pad(router.T, ((0, 16 - n_experts), (0, 0)))
    hidden, cot = hidden_in[0], cotangent[0]
    normed, queries, kv, lse, attended, resid, ffn_in, trig, meta, cot_all = run_front(
        capacity,
        span_order,
        hidden,
        cot,
        gain_attn[None],
        freqs,
        gain_ffn[None],
        router_t,
        expert_ids[0].T,
        priority[0].T,
        qkv_weight,
        out_weight,
        ctx,
        planes,
    )
    zout, pair_sum, gate_grad, gwin, down = run_ffn(
        capacity, ffn_in, cot_all, meta, in_weight, down_weight, parts
    )
    gwin = gwin.reshape(ctx, parts, width // (ctx * parts), 2 * ff)
    output, resid_grad, mixed_grad, out_red, small, in_one = run_attend_back(
        span_order,
        resid,
        cot,
        pair_sum,
        gate_grad,
        meta,
        attended,
        ffn_in,
        queries,
        kv,
        lse,
        trig,
        out_weight,
        router_t,
        gain_ffn[None],
        zout,
        gwin,
    )
    input_grad, qkv_sum, proj_sum, in_two = run_last(
        normed, mixed_grad, hidden, resid_grad, qkv_weight, gain_attn[None], small, out_red, gwin
    )
    wide = qkv_weight.shape[1]
    qkv_sum = qkv_sum.astype(jnp.float32)
    smalls = qkv_sum[:, wide:]
    return (
        output[None],
        input_grad[None],
        smalls[:, HEAD - 1],
        qkv_sum[:, :wide],
        proj_sum.astype(jnp.float32),
        smalls[:, n_experts],
        smalls[:, :n_experts],
        jnp.concatenate([in_one, in_two], axis=2).astype(jnp.float32),
        down.astype(jnp.float32),
    )


def general(
    hidden_in,
    span_order,
    expert_ids,
    priority,
    gain_attn,
    qkv_weight,
    out_weight,
    gain_ffn,
    router,
    in_weight,
    down_weight,
    cotangent,
):
    tok_rows = hidden_in.shape[1]
    width = hidden_in.shape[2]
    contexts = lax.axis_size("context")
    span_len = tok_rows // 2
    seq_len = tok_rows * contexts
    group = HEADS // KV_HEADS
    q_cols = HEADS * HEAD
    kv_cols = KV_HEADS * HEAD
    scale = HEAD ** (-0.5)
    local_experts = in_weight.shape[0]
    n_experts = local_experts * lax.axis_size("expert")
    top_k = expert_ids.shape[2]
    capacity = (9 * tok_rows * top_k + 8 * n_experts - 1) // (8 * n_experts)
    ff_width = down_weight.shape[2]
    seq_spans = span_order[0]
    stored = jnp.arange(seq_len) // span_len
    all_pos = (seq_spans[stored] * span_len + jnp.arange(seq_len) % span_len).astype(jnp.float32)
    my_pos = lax.dynamic_slice_in_dim(all_pos, lax.axis_index("context") * tok_rows, tok_rows)
    cosine, sine = rope_tables(my_pos, HEAD)
    inputs = hidden_in[0].astype(jnp.float32)
    inv_one = lax.rsqrt(jnp.mean(inputs * inputs, axis=-1, keepdims=True) + NORM_EPS)
    plain_one = inputs * inv_one
    normed = (plain_one * gain_attn).astype(jnp.bfloat16)
    mixed = jnp.dot(normed, qkv_weight, preferred_element_type=jnp.float32)
    queries = (
        rotate(mixed[:, :q_cols].reshape(tok_rows, HEADS, HEAD), cosine, sine) * scale
    ).astype(jnp.bfloat16)
    keys = rotate(
        mixed[:, q_cols : q_cols + kv_cols].reshape(tok_rows, KV_HEADS, HEAD), cosine, sine
    ).astype(jnp.bfloat16)
    values = mixed[:, q_cols + kv_cols :].reshape(tok_rows, KV_HEADS, HEAD).astype(jnp.bfloat16)
    grouped = queries.reshape(tok_rows, KV_HEADS, group, HEAD)

    def key_scores(key_piece):
        scores = jnp.einsum(
            "qkgd,skd->kgqs", grouped, key_piece, preferred_element_type=jnp.float32
        )
        visible = all_pos[None, None, None, :] <= my_pos[None, None, :, None]
        return (jnp.where(visible, scores, MASKED), visible)

    running = jnp.full((KV_HEADS, group, tok_rows), MASKED, jnp.float32)
    key_piece = lax.all_gather(keys, "context", axis=0, tiled=True)
    value_piece = lax.all_gather(values, "context", axis=0, tiled=True)
    scores, visible = key_scores(key_piece)
    newest = jnp.maximum(running, jnp.max(scores, axis=-1))
    weights = jnp.where(visible, jnp.exp(scores - newest[..., None]), 0.0)
    totals = jnp.sum(weights, axis=-1)
    accum = jnp.einsum(
        "kgqs,skd->kgqd",
        weights.astype(jnp.bfloat16),
        value_piece,
        preferred_element_type=jnp.float32,
    )
    running, totals, accum = (newest, totals, accum)
    log_total = running + jnp.log(totals)
    attended = (
        (accum / totals[..., None])
        .transpose(2, 0, 1, 3)
        .reshape(tok_rows, q_cols)
        .astype(jnp.bfloat16)
    )
    resid = inputs + jnp.einsum(
        "rh,dh->rd", attended, out_weight, preferred_element_type=jnp.float32
    )
    inv_two = lax.rsqrt(jnp.mean(resid * resid, axis=-1, keepdims=True) + NORM_EPS)
    plain_two = resid * inv_two
    ffn_in = (plain_two * gain_ffn).astype(jnp.bfloat16)
    logits = jnp.dot(ffn_in, router, preferred_element_type=jnp.float32)
    token_ids = expert_ids[0]
    gates = softmax_last(jnp.take_along_axis(logits, token_ids, axis=1))
    slots = route(token_ids, priority[0], n_experts, capacity)
    pair_rows = jnp.repeat(ffn_in, top_k, axis=0)
    send_rows = (
        jnp.zeros((n_experts * capacity, width), jnp.bfloat16).at[slots].set(pair_rows, mode="drop")
    )
    received = lax.all_to_all(
        send_rows.reshape(n_experts, capacity, width),
        "expert",
        split_axis=0,
        concat_axis=1,
        tiled=True,
    )
    inner = jnp.einsum("erd,edf->erf", received, in_weight, preferred_element_type=jnp.float32)
    gate_part = inner[..., :ff_width]
    up_part = inner[..., ff_width:]
    sigma = 1.0 / (1.0 + jnp.exp(-gate_part))
    activated = gate_part * sigma
    hidden = (activated * up_part).astype(jnp.bfloat16)
    expert_out = jnp.einsum(
        "erf,edf->erd", hidden, down_weight, preferred_element_type=jnp.float32
    ).astype(jnp.bfloat16)
    returned = lax.all_to_all(
        expert_out, "expert", split_axis=1, concat_axis=0, tiled=True
    ).reshape(n_experts * capacity, width)
    padded = jnp.concatenate([returned, jnp.zeros((1, width), jnp.bfloat16)], axis=0)
    picked = padded[slots].reshape(tok_rows, top_k, width)
    output = (resid + jnp.sum(gates[:, :, None] * picked, axis=1)).astype(jnp.bfloat16)
    cot_low = cotangent[0]
    cot_full = cot_low.astype(jnp.float32)
    gate_grad = jnp.einsum("rkd,rd->rk", picked, cot_low, preferred_element_type=jnp.float32)
    ret_grad = (
        (gates[:, :, None] * cot_full[:, None, :])
        .astype(jnp.bfloat16)
        .reshape(tok_rows * top_k, width)
    )
    send_grad = (
        jnp.zeros((n_experts * capacity, width), jnp.bfloat16).at[slots].set(ret_grad, mode="drop")
    )
    received_grad = lax.all_to_all(
        send_grad.reshape(n_experts, capacity, width),
        "expert",
        split_axis=0,
        concat_axis=1,
        tiled=True,
    )
    hid_grad = jnp.einsum(
        "erd,edf->erf", received_grad, down_weight, preferred_element_type=jnp.float32
    )
    slope = sigma * (1.0 + gate_part * (1.0 - sigma))
    inner_grad = jnp.concatenate(
        [hid_grad * up_part * slope, hid_grad * activated], axis=-1
    ).astype(jnp.bfloat16)
    row_grad = jnp.einsum(
        "erf,edf->erd", inner_grad, in_weight, preferred_element_type=jnp.float32
    ).astype(jnp.bfloat16)
    part_rows = received
    expert_in = (
        lax.psum_scatter(
            jnp.einsum(
                "erd,erf->def", part_rows, inner_grad, preferred_element_type=jnp.float32
            ).astype(jnp.bfloat16),
            ("context", "dp"),
            scatter_dimension=0,
            tiled=True,
        )
        .astype(jnp.float32)
        .transpose(1, 0, 2)
    )
    part_rows = received_grad
    expert_down = (
        lax.psum_scatter(
            jnp.einsum(
                "erd,erf->def", part_rows, hidden, preferred_element_type=jnp.float32
            ).astype(jnp.bfloat16),
            ("context", "dp"),
            scatter_dimension=0,
            tiled=True,
        )
        .astype(jnp.float32)
        .transpose(1, 0, 2)
    )
    back_rows = lax.all_to_all(row_grad, "expert", split_axis=1, concat_axis=0, tiled=True).reshape(
        n_experts * capacity, width
    )
    back_padded = jnp.concatenate([back_rows, jnp.zeros((1, width), jnp.bfloat16)], axis=0)
    pair_grad = back_padded[slots].reshape(tok_rows, top_k, width)
    mix_grad = gates * (gate_grad - jnp.sum(gates * gate_grad, axis=-1, keepdims=True))
    matches = token_ids[:, :, None] == jnp.arange(n_experts)[None, None, :]
    logit_grad = jnp.sum(jnp.where(matches, mix_grad[:, :, None], 0.0), axis=1).astype(jnp.bfloat16)
    router_part = jnp.einsum("rd,re->de", ffn_in, logit_grad, preferred_element_type=jnp.float32)
    ffn_grad = jnp.sum(pair_grad.astype(jnp.float32), axis=1) + jnp.einsum(
        "re,de->rd", logit_grad, router, preferred_element_type=jnp.float32
    )
    gain_ffn_part = jnp.sum(ffn_grad * plain_two, axis=0)
    scaled_two = ffn_grad * gain_ffn
    resid_grad = cot_full + inv_two * (
        scaled_two - plain_two * jnp.mean(scaled_two * plain_two, axis=-1, keepdims=True)
    )
    resid_low = resid_grad.astype(jnp.bfloat16)
    out_part = jnp.einsum("rd,rh->dh", resid_low, attended, preferred_element_type=jnp.float32)
    att_grad = jnp.einsum(
        "rd,dh->rh", resid_low, out_weight, preferred_element_type=jnp.float32
    ).astype(jnp.bfloat16)
    att_heads = att_grad.reshape(tok_rows, KV_HEADS, group, HEAD)
    row_delta = jnp.sum(
        att_heads.astype(jnp.float32)
        * attended.reshape(tok_rows, KV_HEADS, group, HEAD).astype(jnp.float32),
        axis=-1,
    ).transpose(1, 2, 0)
    key_piece = lax.all_gather(keys, "context", axis=0, tiled=True)
    value_piece = lax.all_gather(values, "context", axis=0, tiled=True)
    scores, visible = key_scores(key_piece)
    soft = jnp.exp(scores - log_total[..., None])
    prob_grad = jnp.einsum(
        "qkgd,skd->kgqs", att_heads, value_piece, preferred_element_type=jnp.float32
    )
    score_grad = (soft * (prob_grad - row_delta[..., None])).astype(jnp.bfloat16)
    query_acc = jnp.einsum(
        "kgqs,skd->kgqd", score_grad, key_piece, preferred_element_type=jnp.float32
    )
    key_part = jnp.einsum("kgqs,qkgd->skd", score_grad, grouped, preferred_element_type=jnp.float32)
    value_part = jnp.einsum(
        "kgqs,qkgd->skd", soft.astype(jnp.bfloat16), att_heads, preferred_element_type=jnp.float32
    )
    pair_acc = jnp.stack([key_part, value_part], axis=1)
    query_acc, pair_acc = (query_acc, pair_acc)
    own_pairs = lax.psum_scatter(
        pair_acc.astype(jnp.bfloat16), "context", scatter_dimension=0, tiled=True
    ).astype(jnp.float32)
    query_grad = (
        unrotate(query_acc.transpose(2, 0, 1, 3).reshape(tok_rows, HEADS, HEAD), cosine, sine)
        * scale
    )
    key_grad = unrotate(own_pairs[:, 0], cosine, sine)
    mixed_grad = jnp.concatenate(
        [
            query_grad.reshape(tok_rows, q_cols),
            key_grad.reshape(tok_rows, kv_cols),
            own_pairs[:, 1].reshape(tok_rows, kv_cols),
        ],
        axis=-1,
    ).astype(jnp.bfloat16)
    qkv_part = jnp.einsum("rd,rc->dc", normed, mixed_grad, preferred_element_type=jnp.float32)
    norm_grad = jnp.einsum("rc,dc->rd", mixed_grad, qkv_weight, preferred_element_type=jnp.float32)
    gain_attn_part = jnp.sum(norm_grad * plain_one, axis=0)
    scaled_one = norm_grad * gain_attn
    input_grad = (
        resid_grad
        + inv_one
        * (scaled_one - plain_one * jnp.mean(scaled_one * plain_one, axis=-1, keepdims=True))
    ).astype(jnp.bfloat16)
    gain_attn_grad, qkv_grad, out_proj_grad, gain_ffn_grad, router_grad = (
        lax.psum_scatter(
            gain_attn_part, ("expert", "context", "dp"), scatter_dimension=0, tiled=True
        ),
        lax.psum_scatter(qkv_part, ("expert", "context", "dp"), scatter_dimension=0, tiled=True),
        lax.psum_scatter(out_part, ("expert", "context", "dp"), scatter_dimension=0, tiled=True),
        lax.psum_scatter(
            gain_ffn_part, ("expert", "context", "dp"), scatter_dimension=0, tiled=True
        ),
        lax.psum_scatter(router_part, ("expert", "context", "dp"), scatter_dimension=0, tiled=True),
    )
    return (
        output[None],
        input_grad[None],
        gain_attn_grad,
        qkv_grad,
        out_proj_grad,
        gain_ffn_grad,
        router_grad,
        expert_in,
        expert_down,
    )


def solution(mesh):
    in_specs = (
        P(("expert", "dp"), "context", None),
        P(("expert", "dp"), None),
        P(("expert", "dp"), "context", None),
        P(("expert", "dp"), "context", None),
        P(),
        P(),
        P(),
        P(),
        P(),
        P("expert", None, None),
        P("expert", None, None),
        P(("expert", "dp"), "context", None),
    )
    out_specs = (
        P(("expert", "dp"), "context", None),
        P(("expert", "dp"), "context", None),
        P(("expert", "context", "dp")),
        P(("expert", "context", "dp"), None),
        P(("expert", "context", "dp"), None),
        P(("expert", "context", "dp")),
        P(("expert", "context", "dp"), None),
        P("expert", ("context", "dp"), None),
        P("expert", ("context", "dp"), None),
    )
    tuned = dict(mesh.shape) == {"expert": 2, "context": 4, "dp": 4}
    body = local if tuned else general
    return jax.shard_map(body, mesh=mesh, in_specs=in_specs, out_specs=out_specs, check_vma=False)
```

```python
import functools

import jax
import jax.numpy as jnp
import numpy as np
from jax import lax
from jax.experimental import pallas as pl
from jax.experimental.pallas import tpu as pltpu
from jax.sharding import PartitionSpec as P

HEADS = 12
KV_HEADS = 2
HEAD = 128


ROPE_BASE = 1000000.0
NORM_EPS = 1e-06
MASKED = -1e30


def rope_tables(positions, head_size):
    half_size = head_size // 2
    freqs = ROPE_BASE ** (jnp.arange(half_size).astype(jnp.float32) * (-2.0 / head_size))
    angles = positions[:, None] * freqs[None, :]
    return (jnp.cos(angles)[:, None, :], jnp.sin(angles)[:, None, :])


def rotate(values, cosine, sine):
    half_size = values.shape[-1] // 2
    first = values[..., :half_size]
    second = values[..., half_size:]
    return jnp.concatenate(
        [first * cosine - second * sine, second * cosine + first * sine], axis=-1
    )


def unrotate(values, cosine, sine):
    half_size = values.shape[-1] // 2
    first = values[..., :half_size]
    second = values[..., half_size:]
    return jnp.concatenate(
        [first * cosine + second * sine, second * cosine - first * sine], axis=-1
    )


def softmax_last(scores):
    shifted = jnp.exp(scores - jnp.max(scores, axis=-1, keepdims=True))
    return shifted / jnp.sum(shifted, axis=-1, keepdims=True)


def route(block_ids, block_order, n_experts, capacity):
    flat_ids = block_ids.reshape(-1)
    flat_order = block_order.reshape(-1)
    choose = (flat_ids[:, None] == jnp.arange(n_experts)[None, :]).astype(jnp.int32)
    ordered = jnp.zeros_like(choose).at[flat_order].set(choose)
    earlier = jnp.cumsum(ordered, axis=0, dtype=jnp.int32) - ordered
    ranks = jnp.sum(earlier[flat_order] * choose, axis=1)
    return jnp.where(ranks < capacity, flat_ids * capacity + ranks, n_experts * capacity)


MESH = pl.DeviceIdType.MESH
F32 = jnp.float32
BF16 = jnp.bfloat16


def dot(a, b):
    return jnp.dot(a, b, preferred_element_type=F32)


def dot_nt(a, b):
    return lax.dot_general(a, b, (((1,), (1,)), ((), ())), preferred_element_type=F32)


def dot_tn(a, b):
    return lax.dot_general(a, b, (((0,), (0,)), ((), ())), preferred_element_type=F32)


def plus(a, *more):
    total = a.astype(F32)
    for b in more:
        total = total + b.astype(F32)
    return total.astype(BF16)


def lanes(at, size):
    return pl.ds(pl.multiple_of(at, 128), size)


def rows_at(at, size):
    return pl.ds(pl.multiple_of(at, 16), size)


def remote(src, dst, s, r, dev):
    return pltpu.make_async_remote_copy(
        src_ref=src, dst_ref=dst, send_sem=s, recv_sem=r, device_id=dev, device_id_type=MESH
    )


class Spot:
    def __init__(self):
        e, c, z = lax.axis_index("expert"), lax.axis_index("context"), lax.axis_index("dp")
        self.ctx = lax.axis_size("context")
        self.parts = lax.axis_size("dp")
        self.planes = self.ctx * lax.axis_size("expert")
        y, k = lax.div(c, 2), lax.rem(c, 2)
        self.e, self.c, self.z, self.k = e, c, z, k
        self.me = e * self.ctx + c
        self.xp, self.yp = (1 - e, c, z), (e, (1 - y) * 2 + k, z)
        self.kp, self.yk = (e, y * 2 + 1 - k, z), (e, (1 - y) * 2 + 1 - k, z)
        self.chips = [
            eq * self.ctx + yq * 2 for eq, yq in ((e, y), (1 - e, y), (e, 1 - y), (1 - e, 1 - y))
        ]

    def others(self):
        found = []
        for step in range(1, self.planes):
            other = lax.rem(self.me + step, self.planes)
            found.append((other, (lax.div(other, self.ctx), lax.rem(other, self.ctx), self.z)))
        return found

    def along(self):
        e, c, z = self.e, self.c, self.z
        return [(z < self.parts - 1, (e, c, z + 1)), (z > 0, (e, c, z - 1))]


def greet(peers, extra=()):
    barrier = pltpu.get_barrier_semaphore()
    for peer in peers:
        pl.semaphore_signal(barrier, inc=1, device_id=peer, device_id_type=MESH)
    for there, peer in extra:

        @pl.when(there)
        def _():
            pl.semaphore_signal(barrier, inc=1, device_id=peer, device_id_type=MESH)

    count = len(peers)
    for there, _ in extra:
        count = count + there.astype(jnp.int32)
    pl.semaphore_wait(barrier, count)


class Plane:
    def __init__(self, spot, zcr, zk, rx, ry, s, r):
        self.spot, self.zcr, self.zk, self.rx, self.ry, self.s, self.r = spot, zcr, zk, rx, ry, s, r
        half = zk[0].shape[0] // 2
        self.lo, self.hi = pl.ds(0, half), pl.ds(half, half)
        self.sent = []

    def push(self, src, dst, i, dev):
        copy = remote(src, dst, self.s.at[i], self.r.at[i], dev)
        copy.start()
        self.sent.append(copy)

    def arrive(self, dst, i):
        remote(dst, dst, self.s.at[i], self.r.at[i], self.spot.kp).wait_recv()

    def give(self, q, src):
        self.push(src, self.zcr[q], q, self.spot.kp)

    def fold(self, q, own=None):
        self.arrive(self.zcr[q], q)
        self.zk[q][...] = plus(self.zk[q][...] if own is None else own, self.zcr[q][...])

    def near(self):
        self.push(self.zk[1].at[self.lo], self.rx[1], 5, self.spot.xp)
        self.push(self.zk[2].at[self.hi], self.ry[1], 8, self.spot.yp)

    def across(self):
        self.push(self.zk[3].at[self.lo], self.rx[0], 4, self.spot.xp)
        self.push(self.zk[3].at[self.hi], self.ry[0], 7, self.spot.yp)

    def turn(self):
        lo, hi = self.lo, self.hi
        self.arrive(self.rx[0], 4)
        self.zk[2][lo] = plus(self.zk[2][lo], self.rx[0][...])
        self.push(self.zk[2].at[lo], self.ry[2], 9, self.spot.yp)
        self.arrive(self.ry[0], 7)
        self.zk[1][hi] = plus(self.zk[1][hi], self.ry[0][...])
        self.push(self.zk[1].at[hi], self.rx[2], 6, self.spot.xp)

    def total(self):
        self.arrive(self.rx[1], 5)
        self.arrive(self.ry[1], 8)
        self.arrive(self.rx[2], 6)
        self.arrive(self.ry[2], 9)
        return (
            (self.lo, (self.zk[0][self.lo], self.rx[1][...], self.ry[2][...])),
            (self.hi, (self.zk[0][self.hi], self.rx[2][...], self.ry[1][...])),
        )

    def done(self):
        for copy in self.sent:
            copy.wait_send()


def plane_of(spot, zcr, zk, rx, ry, s, r):
    four, three = range(4), range(3)
    return Plane(
        spot, [zcr.at[q] for q in four], [zk.at[q] for q in four], [rx.at[i] for i in three], [ry.at[i] for i in three], s, r
    )


def plane_scratch(block, wide):
    return [
        pltpu.VMEM((4, block, wide), BF16),
        pltpu.VMEM((4, block, wide), BF16),
        pltpu.VMEM((3, block // 2, wide), BF16),
        pltpu.VMEM((3, block // 2, wide), BF16),
        pltpu.SemaphoreType.DMA((10,)),
        pltpu.SemaphoreType.DMA((10,)),
    ]


def summed(terms):
    total = terms[0].astype(F32)
    for term in terms[1:]:
        total = total + term.astype(F32)
    return total


class Line:
    def __init__(self, spot, own, adder, buf, s, r):
        z, last = spot.z, spot.parts - 1
        e, c = spot.e, spot.c
        self.own, self.adder, self.buf, self.s, self.r = own, adder, buf, s, r
        self.z, self.last, self.parts = z, last, spot.parts
        self.ways = [(z, (e, c, z + 1), lambda d: d), (last - z, (e, c, z - 1), lambda d: last - d)]

    def step(self, turn):
        for way, (i, dev, part) in enumerate(self.ways):
            to, s, r = self.buf.at[way, turn - 1], self.s.at[way, turn - 1], self.r.at[way, turn - 1]

            @pl.when(i == 0)
            def _():
                remote(self.own(part(self.parts - turn)), to, s, r, dev).start()

            if turn >= 2:
                came, s_came, r_came = (x.at[way, turn - 2] for x in (self.buf, self.s, self.r))

                @pl.when((i >= 1) & (i <= turn - 1) & (i < self.last))
                def _():
                    remote(came, came, s_came, r_came, dev).wait_recv()
                    self.adder(came, part(self.parts - turn + i))
                    remote(came, to, s, r, dev).start()

    def final(self, put):
        last, z = self.last, self.z
        for way, (i, dev, _) in enumerate(self.ways):
            came = self.buf.at[way, last - 1]

            @pl.when(i >= 1)
            def _():
                remote(came, came, self.s.at[way, last - 1], self.r.at[way, last - 1], dev).wait_recv()

        up, down = self.buf.at[0, last - 1], self.buf.at[1, last - 1]
        pl.when(z == 0)(lambda: put(down))
        pl.when(z == last)(lambda: put(up))
        pl.when((z > 0) & (z < last))(lambda: put(up, down))

    def done(self):
        for way, (i, dev, _) in enumerate(self.ways):
            for turn in range(1, self.parts):
                came = self.buf.at[way, turn - 1]

                @pl.when((i <= turn - 1) & (i < self.last))
                def _():
                    remote(came, came, self.s.at[way, turn - 1], self.r.at[way, turn - 1], dev).wait_send()


def line_scratch(parts, piece):
    return [
        pltpu.VMEM((2, parts - 1) + piece, BF16),
        pltpu.SemaphoreType.DMA((2, parts - 1)),
        pltpu.SemaphoreType.DMA((2, parts - 1)),
    ]


class ExpertLine:
    def __init__(self, spot, ref, at, cols, buf, s, r, fin, spread, a_s, a_r):
        self.spot, self.ref, self.at, self.cols = spot, ref, at, cols
        self.fin, self.spread, self.a_s, self.a_r = fin, spread, a_s, a_r
        self.line = Line(spot, self.own, self.adder, buf, s, r)
        self.step = self.line.step

    def own(self, d):
        return self.ref.at[:, d, :, pl.ds(self.at, self.cols)]

    def piece(self, cc, d):
        return self.ref[cc, d, :, self.at : self.at + self.cols]

    def adder(self, came, d):
        for cc in range(self.spot.ctx):
            came[cc] = plus(came[cc], self.piece(cc, d))

    def final(self):
        spot = self.spot

        def put(*came):
            for cc in range(spot.ctx):
                self.fin[cc] = plus(self.piece(cc, spot.z), *(x[cc] for x in came))

        self.line.final(put)
        for step in range(1, spot.ctx):
            cc = lax.rem(spot.c + step, spot.ctx)
            remote(
                self.fin.at[cc],
                self.spread.at[spot.c],
                self.a_s.at[step - 1],
                self.a_r.at[step - 1],
                (spot.e, cc, spot.z),
            ).start()

    def done(self, out):
        spot = self.spot
        for step in range(1, spot.ctx):
            cc = lax.rem(spot.c + spot.ctx - step, spot.ctx)
            got = remote(
                self.spread.at[cc],
                self.spread.at[cc],
                self.a_s.at[step - 1],
                self.a_r.at[step - 1],
                (spot.e, cc, spot.z),
            )
            got.wait_recv()
            got.wait_send()
            out[cc] = self.spread[cc]
        out[spot.c] = self.fin[spot.c]
        self.line.done()


def expert_scratch(ctx, parts, rows, cols):
    return line_scratch(parts, (ctx, rows, cols)) + [
        pltpu.VMEM((ctx, rows, cols), BF16),
        pltpu.VMEM((ctx, rows, cols), BF16),
        pltpu.SemaphoreType.DMA((ctx - 1,)),
        pltpu.SemaphoreType.DMA((ctx - 1,)),
    ]


class Gather:
    def __init__(self, spot, own, buf, s, r):
        self.spot, self.own, self.buf, self.s, self.r = spot, own, buf, s, r
        half = own.shape[0] // 2
        self.lo, self.hi = pl.ds(0, half), pl.ds(half, half)
        self.x_me, self.y_me, self.d_me = (base + spot.k for base in spot.chips[1:])
        self.side = 1 - 2 * spot.k
        self.sent = []

    def push(self, src, dst, i, dev):
        copy = remote(src, dst, self.s.at[i], self.r.at[i], dev)
        copy.start()
        self.sent.append(copy)

    def move(self, p, rows, i, dev):
        self.push(self.buf.at[p, rows], self.buf.at[p, rows], i, dev)

    def got(self, p, rows, i):
        to = self.buf.at[p, rows]
        remote(to, to, self.s.at[i], self.r.at[i], self.spot.kp).wait_recv()

    def start(self):
        me, own, lo, hi = self.spot.me, self.own, self.lo, self.hi
        self.push(own.at[lo], self.buf.at[me, lo], 0, self.spot.xp)
        self.push(own.at[lo], self.buf.at[me, lo], 6, self.spot.kp)
        self.push(own.at[hi], self.buf.at[me, hi], 13, self.spot.kp)
        self.push(own.at[hi], self.buf.at[me, hi], 1, self.spot.xp)

    def start_y(self):
        me, own, lo, hi = self.spot.me, self.own, self.lo, self.hi
        self.push(own.at[hi], self.buf.at[me, hi], 3, self.spot.yp)
        self.push(own.at[lo], self.buf.at[me, lo], 2, self.spot.yp)

    def first(self):
        spot = self.spot
        self.got(self.x_me, self.lo, 0)
        self.move(self.x_me, self.lo, 4, spot.yp)
        self.move(self.x_me, self.lo, 7, spot.kp)
        self.got(self.y_me, self.hi, 3)
        self.move(self.y_me, self.hi, 5, spot.xp)
        self.move(self.y_me, self.hi, 10, spot.kp)

    def second(self):
        self.got(self.x_me, self.hi, 1)
        self.move(self.x_me, self.hi, 8, self.spot.kp)
        self.got(self.y_me, self.lo, 2)
        self.move(self.y_me, self.lo, 9, self.spot.kp)

    def third(self):
        self.got(self.d_me, self.lo, 4)
        self.move(self.d_me, self.lo, 11, self.spot.kp)
        self.got(self.d_me, self.hi, 5)
        self.move(self.d_me, self.hi, 12, self.spot.kp)

    def other_core(self, q):
        low_sem, high_sem = ((6, 13), (7, 8), (9, 10), (11, 12))[q]
        p = (self.spot.me, self.x_me, self.y_me, self.d_me)[q] + self.side
        self.got(p, self.lo, low_sem)
        self.got(p, self.hi, high_sem)

    def done(self):
        for copy in self.sent:
            copy.wait_send()


GATHER_COPIES = 14


def front_kernel(
    cap,
    span,
    hidden,
    cot,
    gain_one,
    freqs,
    gain_two,
    router_t,
    ids_t,
    turn_t,
    wqkv_h,
    wout_h,
    normed,
    queries,
    kv,
    lse,
    attended,
    resid,
    ffn_in,
    trig,
    meta,
    cot_all,
    wqkv,
    wout,
    mask,
    vt,
    load_sem,
    kv_s,
    kv_r,
    co_s,
    co_r,
):
    spot = Spot()
    c, ctx, k = spot.c, spot.ctx, spot.k
    tok, width = hidden.shape
    group = HEADS // KV_HEADS
    kv_cols = KV_HEADS * HEAD
    half_head = HEAD // 2
    seq = kv.shape[0]
    spans = span.shape[1]
    size = seq // spans
    mine = spans // ctx
    n_experts = meta.shape[0]
    loads = [
        pltpu.make_async_copy(wqkv_h.at[:, pl.ds(width, 2 * kv_cols)], wqkv.at[:, pl.ds(width, 2 * kv_cols)], load_sem.at[0]),
        pltpu.make_async_copy(wqkv_h.at[:, pl.ds(0, width)], wqkv.at[:, pl.ds(0, width)], load_sem.at[1]),
        pltpu.make_async_copy(wout_h, wout, load_sem.at[2]),
        pltpu.make_async_copy(cot, cot_all.at[spot.me], load_sem.at[3]),
    ]
    for load in loads:
        load.start()
    greet([spot.xp, spot.yp, spot.kp])
    gather = Gather(spot, cot, cot_all, co_s, co_r)
    gather.start()

    x = hidden[...].astype(F32)
    inv = lax.rsqrt(jnp.mean(x * x, axis=-1, keepdims=True) + NORM_EPS)
    normed[...] = (x * inv * gain_one[...]).astype(BF16)

    along = lax.broadcasted_iota(jnp.int32, (tok, HEAD), 0)
    start_one, start_two = span[0, c * mine] * size, (span[0, c * mine + 1] - 1) * size
    place = jnp.where(along < size, start_one, start_two) + along
    angle = place.astype(F32) * freqs[...]
    cosine, sine = jnp.cos(angle), jnp.sin(angle)
    lane = lax.broadcasted_iota(jnp.int32, (tok, HEAD), 1)
    sine = jnp.where(lane < half_head, -sine, sine)
    trig[0] = cosine
    trig[1] = sine

    def rotate_in(w):
        return w * cosine + pltpu.roll(w, half_head, 1) * sine

    loads[0].wait()
    raw = dot(normed[...], wqkv[:, width:])
    own = rows_at(c * tok, tok)
    for g in range(KV_HEADS):
        at = slice(g * HEAD, (g + 1) * HEAD)
        kv[own, at] = rotate_in(raw[:, at]).astype(BF16)
    kv[own, kv_cols:] = raw[:, kv_cols:].astype(BF16)

    def kv_copy(rows, i, dev):
        return remote(kv.at[rows], kv.at[rows], kv_s.at[i], kv_r.at[i], dev)

    flip_c = lax.rem(c + 2, ctx)
    near_c = c + 1 - 2 * k
    across_c = lax.rem(near_c + 2, ctx)
    sent = [kv_copy(own, 1, spot.yp), kv_copy(own, 0, spot.kp)]
    for copy in sent:
        copy.start()
    gather.start_y()

    loads[1].wait()
    step = 256

    @pl.loop(0, width // step)
    def _(n):
        at = lanes(n * step, step)
        raw = dot(normed[...], wqkv[:, at])
        for i in range(step // HEAD):
            w = raw[:, i * HEAD : (i + 1) * HEAD]
            queries[:, lanes(n * step + i * HEAD, HEAD)] = (rotate_in(w) * HEAD**-0.5).astype(BF16)

    flip = rows_at(flip_c * tok, tok)
    kv_copy(flip, 1, spot.kp).wait_recv()
    sent.append(kv_copy(flip, 2, spot.kp))
    sent[-1].start()

    expert = lax.broadcasted_iota(jnp.int32, (n_experts, tok), 0)
    never = tok * ids_t.shape[0]
    turn = jnp.full((n_experts, tok), never, jnp.int32)
    for i in range(ids_t.shape[0]):
        turn = jnp.where(ids_t[i : i + 1, :] == expert, turn_t[i : i + 1, :], turn)
    turn_f = turn.astype(F32)
    tall = jnp.concatenate([turn_f, jnp.full((HEAD - n_experts, tok), float(never), F32)], axis=0).T
    meta[...] = jnp.zeros(meta.shape, F32)
    for g in range(n_experts):
        row = turn_f[g : g + 1, :]
        rank = jnp.sum(jnp.where(tall[:, g : g + 1] < row, 1.0, 0.0), axis=0, keepdims=True)
        meta[g, 0:1, :] = jnp.where((row < never) & (rank < cap), rank, -1.0)

    along_q = lax.broadcasted_iota(jnp.int32, (size, tok), 1)
    q_pos = jnp.where(along_q < size, start_one, start_two) + along_q
    for s in range(spans):
        k_pos = span[0, s] * size + lax.broadcasted_iota(jnp.int32, (size, tok), 0)
        mask[s * size : (s + 1) * size, :] = jnp.where(k_pos <= q_pos, 0.0, MASKED)

    near, across = rows_at(near_c * tok, tok), rows_at(across_c * tok, tok)
    kv_copy(near, 0, spot.kp).wait_recv()
    kv_copy(across, 2, spot.kp).wait_recv()
    for g in range(KV_HEADS):
        vt[g] = kv[:, kv_cols + g * HEAD : kv_cols + (g + 1) * HEAD].astype(F32).T.astype(BF16)
    lse[...] = jnp.zeros(lse.shape, F32)

    def heads(g, first, count):
        @pl.loop(first, first + count)
        def _(h):
            at = lanes(h * HEAD, HEAD)
            scores = dot_nt(kv[:, g * HEAD : (g + 1) * HEAD], queries[:, at]) + mask[...]
            top = jnp.max(scores, axis=0, keepdims=True)
            weights = jnp.exp(scores - top)
            total = jnp.sum(weights, axis=0, keepdims=True)
            lse[pl.ds(h, 1), :] = top + jnp.log(total)
            out = dot(vt[g], weights.astype(BF16)) / total
            attended[:, at] = out.T.astype(BF16)

    heads(0, 0, 3)
    gather.first()
    heads(0, 3, 3)
    heads(1, 6, 3)
    gather.second()
    heads(1, 9, 3)

    loads[2].wait()

    @pl.loop(0, width // step)
    def _(n):
        at = lanes(n * step, step)
        resid[:, at] = hidden[:, at].astype(F32) + dot_nt(attended[...], wout[at, :])

    r = resid[...]
    inv = lax.rsqrt(jnp.mean(r * r, axis=-1, keepdims=True) + NORM_EPS)
    ffn_in[...] = (r * inv * gain_two[...]).astype(BF16)
    logits = dot_nt(router_t[...], ffn_in[...])[:n_experts]
    logits = jnp.where(turn < never, logits, MASKED)
    shifted = jnp.exp(logits - jnp.max(logits, axis=0, keepdims=True))
    gates = shifted / jnp.sum(shifted, axis=0, keepdims=True)
    for g in range(n_experts):
        meta[g, 1:2, :] = gates[g : g + 1, :]
    gather.third()
    for q in range(4):
        gather.other_core(q)
    loads[3].wait()
    gather.done()
    for copy in sent:
        copy.wait_send()


def run_front(cap, span, hidden, cot, gain_one, freqs, gain_two, router_t, ids_t, turn_t, wqkv, wout, ctx, planes):
    tok, width = hidden.shape
    seq = tok * ctx
    n_experts = planes
    kv_cols = 2 * KV_HEADS * HEAD
    vm, anyspace = pl.BlockSpec(memory_space=pltpu.VMEM), pl.BlockSpec(memory_space=pl.ANY)
    sm = pl.BlockSpec(memory_space=pltpu.SMEM)
    shape = jax.ShapeDtypeStruct
    dma = pltpu.SemaphoreType.DMA
    return pl.pallas_call(
        functools.partial(front_kernel, cap),
        out_shape=(
            shape((tok, width), BF16),
            shape((tok, width), BF16),
            shape((seq, kv_cols), BF16),
            shape((16, tok), F32),
            shape((tok, width), BF16),
            shape((tok, width), F32),
            shape((tok, width), BF16),
            shape((2, tok, HEAD), F32),
            shape((n_experts, 8, tok), F32),
            shape((planes, tok, width), BF16),
        ),
        in_specs=[sm] + [vm] * 8 + [anyspace] * 2,
        out_specs=(vm,) * 9 + (anyspace,),
        scratch_shapes=[
            pltpu.VMEM(wqkv.shape, BF16),
            pltpu.VMEM(wout.shape, BF16),
            pltpu.VMEM((seq, tok), F32),
            pltpu.VMEM((KV_HEADS, HEAD, seq), BF16),
            dma((4,)),
            dma((3,)),
            dma((3,)),
            dma((GATHER_COPIES,)),
            dma((GATHER_COPIES,)),
        ],
        compiler_params=pltpu.CompilerParams(
            collective_id=4, has_side_effects=True, vmem_limit_bytes=56 * 2**20
        ),
        cost_estimate=pl.CostEstimate(flops=5 * 10**9, bytes_accessed=20 * 10**6, transcendentals=4 * 10**6),
    )(span, hidden, cot, gain_one, freqs, gain_two, router_t, ids_t, turn_t, wqkv, wout)


def ffn_kernel(cap, ffn, resid, cot_h, meta, win_h, wdn_h, output, pg_out, gg_out, gwin_h, ex_out, *scratch):
    agb, metas, cotb, win, wdn, xs, ds, hid, igs, pgs, ggs, ggr, stage, gwdn, pgt = scratch[:15]
    load_sem, ag_s, ag_r, me_s, me_r, gg_s, gg_r, out_s, out_r = scratch[15:24]
    plane_refs, line_refs = scratch[24:30], scratch[30:]
    spot = Spot()
    c, k, me = spot.c, spot.k, spot.me
    kp = spot.kp
    tok, width = ffn.shape
    ff = wdn.shape[1]
    planes, ctx = spot.planes, spot.ctx
    chips = spot.chips

    loads = [
        pltpu.make_async_copy(win_h.at[c], win, load_sem.at[0]),
        pltpu.make_async_copy(wdn_h.at[c], wdn, load_sem.at[1]),
        pltpu.make_async_copy(cot_h, cotb, load_sem.at[2]),
    ]
    for load in loads:
        load.start()
    others = spot.others()
    greet([dev for _, dev in others], spot.along())
    plane = plane_of(spot, *plane_refs)
    lo, hi = plane.lo, plane.hi
    outs = Plane(
        spot,
        [agb.at[q] for q in range(4)],
        [cotb.at[base + k] for base in chips],
        [agb.at[4, lo], agb.at[4, hi], agb.at[5, lo]],
        [agb.at[6, lo], agb.at[6, hi], agb.at[5, hi]],
        out_s,
        out_r,
    )
    line = ExpertLine(spot, gwdn, 0, ff, *line_refs)
    gather = Gather(spot, ffn, agb, ag_s, ag_r)
    for step, (other, dev) in enumerate(others):
        remote(meta.at[other], metas.at[me], me_s.at[step], me_r.at[step], dev).start()
    gather.start()
    gather.start_y()
    agb[me] = ffn[...]
    metas[me] = meta[me]
    slot_rows = lax.broadcasted_iota(jnp.int32, (cap, tok), 0).astype(F32)
    step = 256

    def spots(p):
        return jnp.where(slot_rows == metas[p, 0:1, :], 1.0, 0.0)

    def gate_of(p, hot):
        return jnp.sum(hot * metas[p, 1:2, :], axis=1, keepdims=True)

    def group(q):
        base = chips[q]
        rows = pl.ds(q * 2 * cap, 2 * cap)
        for kk in range(2):
            p = base + kk
            hot = spots(p)
            low = hot.astype(BF16)
            part = pl.ds(q * 2 * cap + kk * cap, cap)
            xs[part, :] = dot(low, agb[p]).astype(BF16)
            ds[part, :] = (dot(low, cotb[p]) * gate_of(p, hot)).astype(BF16)

        @pl.loop(0, ff // step)
        def _(n):
            gate_cols, up_cols = lanes(n * step, step), lanes(ff + n * step, step)
            x = xs[rows, :]
            g = dot(x, win[:, gate_cols])
            u = dot(x, win[:, up_cols])
            s = 1.0 / (1.0 + jnp.exp(-g))
            act = g * s
            hid[rows, gate_cols] = (act * u).astype(BF16)
            h = dot(ds[rows, :], wdn[:, gate_cols])
            igs[rows, gate_cols] = (h * u * (s * (1.0 + g * (1.0 - s)))).astype(BF16)
            igs[rows, up_cols] = (h * act).astype(BF16)

        @pl.loop(0, width // step)
        def _(n):
            cols = lanes(n * step, step)
            pgs[:, cols] = dot_nt(igs[rows, :], win[cols, :]).astype(BF16)

        mine, theirs = rows_at(k * cap, cap), rows_at((1 - k) * cap, cap)
        zcs = stage.at[q]
        zcs[...] = dot_tn(spots(base + 1 - k).astype(BF16), pgs[theirs, :]).astype(BF16)
        plane.give(q, zcs)
        plane.zk[q][...] = dot_tn(spots(base + k).astype(BF16), pgs[mine, :]).astype(BF16)

    for load in loads:
        load.wait()
    for n in range(planes - 1):
        source = lax.rem(me + planes - 1 - n, planes)
        remote(metas.at[source], metas.at[source], me_s.at[n], me_r.at[n], kp).wait_recv()
    gather.other_core(0)
    group(0)
    gather.first()
    gather.second()
    gather.other_core(1)
    group(1)
    gather.third()
    gather.other_core(2)
    group(2)
    plane.fold(1)
    plane.fold(2)
    plane.near()
    gather.other_core(3)
    gather.done()
    group(3)
    plane.fold(3)
    plane.across()

    tall = width // ctx

    @pl.loop(0, ctx)
    def _(n):
        tile = dot_tn(ds[:, lanes(n * tall, tall)], hid[...]).astype(BF16)
        for d in range(gwdn.shape[1]):
            gwdn[n, d] = tile[d * gwdn.shape[2] : (d + 1) * gwdn.shape[2]]

    line.step(1)
    plane.fold(0)
    plane.turn()

    for q in (1, 2, 3, 0):
        base = chips[q]

        @pl.loop(0, width // step)
        def _(n):
            cols = lanes(n * step, step)
            pgs[:, cols] = dot_nt(hid[pl.ds(q * 2 * cap, 2 * cap), :], wdn[cols, :]).astype(BF16)

        for kk in range(2):
            p = base + kk
            hot = spots(p)
            rows = pgs[pl.ds(kk * cap, cap), :]
            ggs[p, 0:1, :] = jnp.sum(hot * dot_nt(rows, cotb[p]), axis=0, keepdims=True)
            scaled = (rows.astype(F32) * gate_of(p, hot)).astype(BF16)
            cotb[p] = dot_tn(hot.astype(BF16), scaled).astype(BF16)
        outs.give(q, cotb.at[base + 1 - k])
    ggr[me] = ggs[me]
    for n, (other, dev) in enumerate(others):
        remote(ggs.at[other], ggr.at[me], gg_s.at[n], gg_r.at[n], dev).start()
    line.step(2)
    outs.fold(1)
    outs.fold(2)
    outs.near()
    outs.fold(3)
    outs.across()
    outs.fold(0)
    half_wide = ff

    @pl.loop(0, 2 * ctx)
    def _(n):
        slot = lax.rem(n, 2)
        rows = lanes(lax.div(n, 2) * tall, tall)
        cols = lanes(slot * half_wide, half_wide)
        tile = pgt.at[slot]
        to = pltpu.make_async_copy(tile, gwin_h.at[rows, cols], load_sem.at[slot])

        @pl.when(n >= 2)
        def _():
            to.wait()

        tile[...] = dot_tn(xs[:, rows], igs[:, cols]).astype(BF16)
        to.start()

    for slot in range(2):
        pltpu.make_async_copy(pgt.at[slot], gwin_h.at[pl.ds(0, tall), pl.ds(0, half_wide)], load_sem.at[slot]).wait()
    outs.turn()
    line.step(3)
    for rows, terms in plane.total():
        pg_out[rows, :] = summed(terms)
    for n in range(planes - 1):
        source = lax.rem(me + planes - 1 - n, planes)
        remote(ggr.at[source], ggr.at[source], gg_s.at[n], gg_r.at[n], kp).wait_recv()
    for p in range(planes):
        gg_out[p : p + 1, :] = ggr[p, 0:1, :]
    line.final()
    for rows, terms in outs.total():
        output[rows, :] = (resid[rows, :] + summed(terms)).astype(BF16)
    for n, (other, dev) in enumerate(others):
        remote(meta.at[other], metas.at[other], me_s.at[n], me_r.at[n], dev).wait_send()
        remote(ggs.at[other], ggr.at[other], gg_s.at[n], gg_r.at[n], dev).wait_send()
    plane.done()
    outs.done()
    line.done(ex_out)


def run_ffn(cap, ffn, resid, cot_all, meta, win, wdn, parts):
    tok, width = ffn.shape
    ff = wdn.shape[2]
    planes = cot_all.shape[0]
    ctx = win.shape[0]
    rows = planes * cap
    piece = width // (ctx * parts)
    vm, anyspace = pl.BlockSpec(memory_space=pltpu.VMEM), pl.BlockSpec(memory_space=pl.ANY)
    shape = jax.ShapeDtypeStruct
    dma = pltpu.SemaphoreType.DMA
    return pl.pallas_call(
        functools.partial(ffn_kernel, cap),
        out_shape=(
            shape((tok, width), BF16),
            shape((tok, width), F32),
            shape((planes, tok), F32),
            shape((width, 2 * ff), BF16),
            shape((ctx, piece, ff), BF16),
        ),
        in_specs=[vm, vm, anyspace, vm, anyspace, anyspace],
        out_specs=(vm, vm, vm, anyspace, vm),
        scratch_shapes=[
            pltpu.VMEM((planes, tok, width), BF16),
            pltpu.VMEM((planes, 8, tok), F32),
            pltpu.VMEM((planes, tok, width), BF16),
            pltpu.VMEM((width, 2 * ff), BF16),
            pltpu.VMEM((width, ff), BF16),
            pltpu.VMEM((rows, width), BF16),
            pltpu.VMEM((rows, width), BF16),
            pltpu.VMEM((rows, ff), BF16),
            pltpu.VMEM((rows, 2 * ff), BF16),
            pltpu.VMEM((2 * cap, width), BF16),
            pltpu.VMEM((planes, 8, tok), F32),
            pltpu.VMEM((planes, 8, tok), F32),
            pltpu.VMEM((4, tok, width), BF16),
            pltpu.VMEM((ctx, parts, piece, ff), BF16),
            pltpu.VMEM((2, width // ctx, ff), BF16),
            dma((3,)),
            dma((GATHER_COPIES,)),
            dma((GATHER_COPIES,)),
            dma((planes - 1,)),
            dma((planes - 1,)),
            dma((planes - 1,)),
            dma((planes - 1,)),
            dma((10,)),
            dma((10,)),
        ]
        + plane_scratch(tok, width)
        + expert_scratch(ctx, parts, piece, ff),
        compiler_params=pltpu.CompilerParams(
            collective_id=1, has_side_effects=True, vmem_limit_bytes=62 * 2**20
        ),
        cost_estimate=pl.CostEstimate(flops=25 * 10**9, bytes_accessed=50 * 10**6, transcendentals=10**6),
    )(ffn, resid, cot_all, meta, win, wdn)


def attend_back_kernel(
    span,
    resid,
    cot,
    pg,
    gg,
    meta,
    attended,
    ffn_in,
    queries,
    kv,
    lse,
    trig,
    wout,
    router_t,
    gain,
    gwin_h,
    resid_grad,
    mixed_grad,
    out_red,
    small,
    ex_out,
    *scratch,
):
    gwin, osend, low, attg, mask, delta, kt, dk, dv, dq, kvs, kvr = scratch[:12]
    load_sem, kv_s, kv_r = scratch[12:15]
    out_refs, line_refs = scratch[15:21], scratch[21:]
    spot = Spot()
    c, k, z, ctx = spot.c, spot.k, spot.z, spot.ctx
    tok, width = cot.shape
    cols = ex_out.shape[2]
    block = out_red.shape[0]
    heads_kv = KV_HEADS
    group = HEADS // KV_HEADS
    half_head = HEAD // 2
    gwin_load = pltpu.make_async_copy(gwin_h.at[:, :, :, pl.ds(0, cols)], gwin, load_sem.at[0])
    gwin_load.start()
    greet([spot.xp, spot.yp, spot.kp, spot.yk], spot.along())
    weights = plane_of(spot, *out_refs)
    line = ExpertLine(spot, gwin, 0, cols, *line_refs)
    gwin_load.wait()
    line.step(1)

    gate = jnp.concatenate([meta[g, 1:2, :] for g in range(meta.shape[0])], axis=0)
    seen = gate * gg[...]
    mix = seen - gate * jnp.sum(seen, axis=0, keepdims=True)
    mix = jnp.concatenate([mix, jnp.zeros((HEAD - mix.shape[0], tok), F32)], axis=0)
    logit_t = mix.astype(BF16)
    r = resid[...]
    inv = lax.rsqrt(jnp.mean(r * r, axis=-1, keepdims=True) + NORM_EPS)
    plain = r * inv
    ffn_grad = pg[...] + dot_tn(logit_t[: router_t.shape[0]], router_t[...])
    gain_row = jnp.sum(ffn_grad * plain, axis=0, keepdims=True)
    scaled = ffn_grad * gain[...]
    back = cot[...].astype(F32) + inv * (
        scaled - plain * jnp.mean(scaled * plain, axis=-1, keepdims=True)
    )
    resid_grad[...] = back
    low[...] = back.astype(BF16)
    lane = lax.broadcasted_iota(jnp.int32, (width, HEAD), 1)
    gain_col = jnp.broadcast_to(gain_row, (HEAD, width)).T
    routed = dot_tn(ffn_in[...], logit_t.T)
    small[...] = jnp.where(lane == gate.shape[0], gain_col, routed).astype(BF16)

    for q in (1, 2, 3, 0):
        at = lanes(spot.chips[q] * block, 2 * block)
        osend[q] = dot_tn(low[:, at], attended[...]).astype(BF16)
        weights.give(q, osend.at[q, rows_at((1 - k) * block, block)])

    step = 256

    @pl.loop(0, width // step)
    def _(n):
        at = lanes(n * step, step)
        attg[:, at] = dot(low[...], wout[:, at]).astype(BF16)

    seq = kv.shape[0]
    spans = span.shape[1]
    size = seq // spans
    mine = spans // ctx
    along_q = lax.broadcasted_iota(jnp.int32, (size, tok), 1)
    q_pos = jnp.where(along_q < size, span[0, c * mine] * size, (span[0, c * mine + 1] - 1) * size) + along_q
    for s in range(spans):
        k_pos = span[0, s] * size + lax.broadcasted_iota(jnp.int32, (size, tok), 0)
        mask[s * size : (s + 1) * size, :] = jnp.where(k_pos <= q_pos, 0.0, MASKED)

    lane_h = lax.broadcasted_iota(jnp.int32, (tok, HEAD), 1)
    deltas = jnp.zeros((tok, HEAD), F32)
    for h in range(HEADS):
        at = slice(h * HEAD, (h + 1) * HEAD)
        term = jnp.sum(attg[:, at].astype(F32) * attended[:, at].astype(F32), axis=-1, keepdims=True)
        deltas = jnp.where(lane_h == h, term, deltas)
    delta[...] = deltas.T
    for g in range(heads_kv):
        kt[g] = kv[:, g * HEAD : (g + 1) * HEAD].astype(F32).T.astype(BF16)

    def head(g, h):
        at = lanes(h * HEAD, HEAD)
        k_at = slice(g * HEAD, (g + 1) * HEAD)
        v_at = slice((heads_kv + g) * HEAD, (heads_kv + g + 1) * HEAD)
        q, a = queries[:, at], attg[:, at]
        soft = jnp.exp(dot_nt(kv[:, k_at], q) + mask[...] - lse[pl.ds(h, 1), :])
        prob = dot_nt(kv[:, v_at], a)
        score = (soft * (prob - delta[pl.ds(h, 1), :])).astype(BF16)
        dq[:, at] = dot(kt[g], score).T
        dk[...] += dot(score, q)
        dv[...] += dot(soft.astype(BF16), a)

    def send_kv(g):
        for cc in range(ctx):
            rows = slice(cc * tok, (cc + 1) * tok)
            kvs[g, cc, :, :HEAD] = dk[rows, :].astype(BF16)
            kvs[g, cc, :, HEAD:] = dv[rows, :].astype(BF16)
        for n in range(1, ctx):
            cc = lax.rem(c + n, ctx)
            remote(kvs.at[g, cc], kvr.at[g, c], kv_s.at[g, n - 1], kv_r.at[g, n - 1], (spot.e, cc, z)).start()

    def heads(g, first, count):
        @pl.loop(first, first + count)
        def _(h):
            head(g, h)

    def clear():
        dk[...] = jnp.zeros(dk.shape, F32)
        dv[...] = jnp.zeros(dv.shape, F32)

    def own_part(q):
        return osend[q, rows_at(k * block, block)]

    clear()
    heads(0, 0, 2)
    for q in (1, 2):
        weights.fold(q, own_part(q))
    weights.near()
    weights.fold(3, own_part(3))
    weights.across()
    weights.fold(0, own_part(0))
    heads(0, 2, 2)
    line.step(2)
    heads(0, 4, 2)
    send_kv(0)
    weights.turn()
    clear()
    heads(1, 6, 2)
    line.step(3)
    heads(1, 8, 2)
    heads(1, 10, 2)
    send_kv(1)
    cosine, sine = trig[0], trig[1]

    def unrotate(w):
        return w * cosine - pltpu.roll(w, half_head, 1) * sine

    for h in range(HEADS):
        at = slice(h * HEAD, (h + 1) * HEAD)
        mixed_grad[:, at] = (unrotate(dq[:, at]) * HEAD**-0.5).astype(BF16)
    line.final()
    for rows, terms in weights.total():
        out_red[rows, :] = summed(terms).astype(BF16)
    for g in range(heads_kv):
        own = kvs[g, c].astype(F32)
        for n in range(1, ctx):
            cc = lax.rem(c + ctx - n, ctx)
            got = remote(kvr.at[g, cc], kvr.at[g, cc], kv_s.at[g, n - 1], kv_r.at[g, n - 1], spot.kp)
            got.wait_recv()
            own = own + kvr[g, cc].astype(F32)
        at = width + g * HEAD
        mixed_grad[:, at : at + HEAD] = unrotate(own[:, :HEAD]).astype(BF16)
        at = width + (heads_kv + g) * HEAD
        mixed_grad[:, at : at + HEAD] = own[:, HEAD:].astype(BF16)
    for g in range(heads_kv):
        for n in range(1, ctx):
            cc = lax.rem(c + n, ctx)
            remote(kvs.at[g, cc], kvr.at[g, cc], kv_s.at[g, n - 1], kv_r.at[g, n - 1], spot.kp).wait_send()
    weights.done()
    line.done(ex_out)


def run_attend_back(
    span, resid, cot, pg, gg, meta, attended, ffn_in, queries, kv, lse, trig, wout, router_t, gain, gwin
):
    tok, width = cot.shape
    ctx, parts, piece, wide = gwin.shape
    planes = meta.shape[0]
    cols = wide // 2
    block = width // planes
    seq, kv_cols = kv.shape
    vm, anyspace = pl.BlockSpec(memory_space=pltpu.VMEM), pl.BlockSpec(memory_space=pl.ANY)
    sm = pl.BlockSpec(memory_space=pltpu.SMEM)
    shape = jax.ShapeDtypeStruct
    dma = pltpu.SemaphoreType.DMA
    return pl.pallas_call(
        attend_back_kernel,
        out_shape=(
            shape((tok, width), F32),
            shape((tok, width + kv_cols), BF16),
            shape((block, width), BF16),
            shape((width, HEAD), BF16),
            shape((ctx, piece, cols), BF16),
        ),
        in_specs=[sm] + [vm] * 14 + [anyspace],
        out_specs=(vm,) * 5,
        scratch_shapes=[
            pltpu.VMEM((ctx, parts, piece, cols), BF16),
            pltpu.VMEM((4, 2 * block, width), BF16),
            pltpu.VMEM((tok, width), BF16),
            pltpu.VMEM((tok, width), BF16),
            pltpu.VMEM((seq, tok), F32),
            pltpu.VMEM((HEAD, tok), F32),
            pltpu.VMEM((KV_HEADS, HEAD, seq), BF16),
            pltpu.VMEM((seq, HEAD), F32),
            pltpu.VMEM((seq, HEAD), F32),
            pltpu.VMEM((tok, width), F32),
            pltpu.VMEM((KV_HEADS, ctx, tok, 2 * HEAD), BF16),
            pltpu.VMEM((KV_HEADS, ctx, tok, 2 * HEAD), BF16),
            dma((1,)),
            dma((KV_HEADS, ctx - 1)),
            dma((KV_HEADS, ctx - 1)),
        ]
        + plane_scratch(block, width)
        + expert_scratch(ctx, parts, piece, cols),
        compiler_params=pltpu.CompilerParams(
            collective_id=2, has_side_effects=True, vmem_limit_bytes=62 * 2**20
        ),
        cost_estimate=pl.CostEstimate(flops=8 * 10**9, bytes_accessed=40 * 10**6, transcendentals=10**6),
    )(
        span, resid, cot, pg, gg, meta, attended, ffn_in, queries, kv, lse, trig, wout, router_t, gain, gwin
    )


def last_kernel(
    normed, mixed_grad, hidden, resid_grad, wqkv, gain, small, out_red, gwin_h, input_grad, qkv_out, proj_out, ex_out, *scratch
):
    gwin, asend, bsend, norm_grad, smalls, total, load_sem = scratch[:7]
    a_refs, b_refs, qkv_refs, proj_refs, line_refs = (
        scratch[7:13],
        scratch[13:19],
        scratch[19:22],
        scratch[22:25],
        scratch[25:],
    )
    spot = Spot()
    k, z = spot.k, spot.z
    tok, width = normed.shape
    cols = ex_out.shape[2]
    block = out_red.shape[0]
    piece = proj_out.shape[0]
    kv_wide = mixed_grad.shape[1] - width
    load = pltpu.make_async_copy(gwin_h.at[:, :, :, pl.ds(cols, cols)], gwin, load_sem.at[0])
    load.start()
    greet([spot.xp, spot.yp, spot.kp, spot.yk], spot.along())
    first, second = plane_of(spot, *a_refs), plane_of(spot, *b_refs)
    line = ExpertLine(spot, gwin, 0, cols, *line_refs)

    def shared_line(ref, refs):
        def own(d):
            return ref.at[rows_at(d * piece, piece)]

        def adder(came, d):
            came[...] = plus(came[...], own(d)[...])

        return Line(spot, own, adder, *refs)

    qkv, proj = shared_line(total, qkv_refs), shared_line(out_red, proj_refs)
    def put_shared(to, ref, came):
        to[...] = plus(ref[rows_at(z * piece, piece)], *(x[...] for x in came))

    mine, theirs = rows_at(k * block, block), rows_at((1 - k) * block, block)
    load.wait()
    line.step(1)
    proj.step(1)
    for q in (1, 2, 3, 0):
        at = lanes(spot.chips[q] * block, 2 * block)
        asend[q] = dot_tn(normed[:, at], mixed_grad[:, :width]).astype(BF16)
        first.give(q, asend.at[q, theirs])
    first.fold(1, asend[1, mine])
    first.fold(2, asend[2, mine])
    first.near()
    first.fold(3, asend[3, mine])
    first.across()
    first.fold(0, asend[0, mine])

    step = 256

    @pl.loop(0, width // step)
    def _(n):
        at = lanes(n * step, step)
        norm_grad[:, at] = dot_nt(mixed_grad[...], wqkv[at, :])

    x = hidden[...].astype(F32)
    inv = lax.rsqrt(jnp.mean(x * x, axis=-1, keepdims=True) + NORM_EPS)
    plain = x * inv
    ng = norm_grad[...]
    gain_row = jnp.sum(ng * plain, axis=0, keepdims=True)
    scaled = ng * gain[...]
    input_grad[...] = (
        resid_grad[...]
        + inv * (scaled - plain * jnp.mean(scaled * plain, axis=-1, keepdims=True))
    ).astype(BF16)
    lane = lax.broadcasted_iota(jnp.int32, (width, HEAD), 1)
    gain_col = jnp.broadcast_to(gain_row, (HEAD, width)).T
    smalls[...] = jnp.where(lane == HEAD - 1, gain_col, small[...].astype(F32)).astype(BF16)
    for q in (1, 2, 3, 0):
        at = lanes(spot.chips[q] * block, 2 * block)
        bsend[q, :, :kv_wide] = dot_tn(normed[:, at], mixed_grad[:, width:]).astype(BF16)
        bsend[q, :, kv_wide:] = smalls[rows_at(spot.chips[q] * block, 2 * block), :]
        second.give(q, bsend.at[q, theirs])
    first.turn()
    second.fold(1, bsend[1, mine])
    second.fold(2, bsend[2, mine])
    second.near()
    second.fold(3, bsend[3, mine])
    second.across()
    second.fold(0, bsend[0, mine])
    line.step(2)
    proj.step(2)
    for rows, terms in first.total():
        total[rows, :width] = summed(terms).astype(BF16)
    second.turn()
    line.step(3)
    proj.step(3)
    for rows, terms in second.total():
        total[rows, width:] = summed(terms).astype(BF16)
    qkv.step(1)
    proj.final(lambda *came: put_shared(proj_out, out_red, came))
    line.final()
    qkv.step(2)
    line.done(ex_out)
    qkv.step(3)
    proj.done()
    first.done()
    second.done()
    qkv.final(lambda *came: put_shared(qkv_out, total, came))
    qkv.done()


def run_last(normed, mixed_grad, hidden, resid_grad, wqkv, gain, small, out_red, gwin):
    tok, width = normed.shape
    block = out_red.shape[0]
    ctx, parts, rows, wide = gwin.shape
    cols = wide // 2
    piece = block // parts
    rest = mixed_grad.shape[1] - width + HEAD
    vm, anyspace = pl.BlockSpec(memory_space=pltpu.VMEM), pl.BlockSpec(memory_space=pl.ANY)
    shape = jax.ShapeDtypeStruct
    return pl.pallas_call(
        last_kernel,
        out_shape=(
            shape((tok, width), BF16),
            shape((piece, width + rest), BF16),
            shape((piece, width), BF16),
            shape((ctx, rows, cols), BF16),
        ),
        in_specs=[vm] * 8 + [anyspace],
        out_specs=(vm,) * 4,
        scratch_shapes=[
            pltpu.VMEM((ctx, parts, rows, cols), BF16),
            pltpu.VMEM((4, 2 * block, width), BF16),
            pltpu.VMEM((4, 2 * block, rest), BF16),
            pltpu.VMEM((tok, width), F32),
            pltpu.VMEM((width, HEAD), BF16),
            pltpu.VMEM((block, width + rest), BF16),
            pltpu.SemaphoreType.DMA((1,)),
        ]
        + plane_scratch(block, width)
        + plane_scratch(block, rest)
        + line_scratch(parts, (piece, width + rest))
        + line_scratch(parts, (piece, width))
        + expert_scratch(ctx, parts, rows, cols),
        compiler_params=pltpu.CompilerParams(
            collective_id=3, has_side_effects=True, vmem_limit_bytes=62 * 2**20
        ),
        cost_estimate=pl.CostEstimate(flops=4 * 10**9, bytes_accessed=40 * 10**6, transcendentals=0),
    )(normed, mixed_grad, hidden, resid_grad, wqkv, gain, small, out_red, gwin)


def finish_kernel(
    n_experts, output_low, input_low, qkv_low, proj_low, one, two, down_low, output, input_grad, gains, qkv, proj, router, inner, down
):
    output[...] = output_low[...]
    input_grad[...] = input_low[...]
    wide = qkv.shape[1]
    qkv[...] = qkv_low[:, :wide].astype(F32)
    proj[...] = proj_low[...].astype(F32)
    ff = one.shape[2]
    inner[:, :, :ff] = one[...].astype(F32)
    inner[:, :, ff:] = two[...].astype(F32)
    down[...] = down_low[...].astype(F32)
    small = qkv_low[:, wide:].astype(F32)
    router[...] = small[:, :n_experts]
    piece = small.shape[0]
    same = lax.broadcasted_iota(jnp.int32, (piece, piece), 0) == lax.broadcasted_iota(
        jnp.int32, (piece, piece), 1
    )
    for row, col in ((0, HEAD - 1), (1, n_experts)):
        gains[row : row + 1, :] = jnp.sum(jnp.where(same, small[:, col : col + 1], 0.0), axis=0, keepdims=True)


def run_finish(n_experts, output, input_grad, qkv, proj, one, two, down):
    piece, width = proj.shape
    ctx, rows, ff = one.shape
    shape = jax.ShapeDtypeStruct
    vm = pl.BlockSpec(memory_space=pltpu.VMEM)
    return pl.pallas_call(
        functools.partial(finish_kernel, n_experts),
        out_shape=(
            shape(output.shape, BF16),
            shape(input_grad.shape, BF16),
            shape((2, piece), F32),
            shape((piece, qkv.shape[1] - HEAD), F32),
            shape((piece, width), F32),
            shape((piece, n_experts), F32),
            shape((ctx, rows, 2 * ff), F32),
            shape((ctx, rows, ff), F32),
        ),
        in_specs=[vm] * 7,
        out_specs=(vm,) * 8,
        compiler_params=pltpu.CompilerParams(vmem_limit_bytes=40 * 2**20),
    )(output, input_grad, qkv, proj, one, two, down)


def local(
    hidden_in,
    span_order,
    expert_ids,
    priority,
    gain_attn,
    qkv_weight,
    out_weight,
    gain_ffn,
    router,
    in_weight,
    down_weight,
    cotangent,
):
    _, tok_rows, width = hidden_in.shape
    ctx, parts = lax.axis_size("context"), lax.axis_size("dp")
    planes = ctx * lax.axis_size("expert")
    n_experts = router.shape[1]
    top_k = expert_ids.shape[2]
    capacity = (9 * tok_rows * top_k + 8 * n_experts - 1) // (8 * n_experts)
    ff = down_weight.shape[2]
    half_freqs = ROPE_BASE ** (np.arange(HEAD // 2) * (-2.0 / HEAD))
    freqs = np.concatenate([half_freqs, half_freqs])[None].astype(np.float32)
    router_t = router.T
    hidden, cot = hidden_in[0], cotangent[0]
    normed, queries, kv, lse, attended, resid, ffn_in, trig, meta, cot_all = run_front(
        capacity,
        span_order,
        hidden,
        cot,
        gain_attn,
        freqs,
        gain_ffn,
        router_t,
        expert_ids[0].T,
        priority[0].T,
        qkv_weight,
        out_weight,
        ctx,
        planes,
    )
    output, pair_sum, gate_grad, gwin, down = run_ffn(
        capacity, ffn_in, resid, cot_all, meta, in_weight, down_weight, parts
    )
    gwin = gwin.reshape(ctx, parts, width // (ctx * parts), 2 * ff)
    resid_grad, mixed_grad, out_red, small, in_one = run_attend_back(
        span_order,
        resid,
        cot,
        pair_sum,
        gate_grad,
        meta,
        attended,
        ffn_in,
        queries,
        kv,
        lse,
        trig,
        out_weight,
        router_t,
        gain_ffn,
        gwin,
    )
    input_grad, qkv_sum, proj_sum, in_two = run_last(
        normed, mixed_grad, hidden, resid_grad, qkv_weight, gain_attn, small, out_red, gwin
    )
    output, input_grad, gains, qkv_grad, proj_grad, router_grad, inner_grad, down_grad = run_finish(
        n_experts, output, input_grad, qkv_sum, proj_sum, in_one, in_two, down
    )
    return (
        output[None],
        input_grad[None],
        gains[0],
        qkv_grad,
        proj_grad,
        gains[1],
        router_grad,
        inner_grad,
        down_grad,
    )


def general(
    hidden_in,
    span_order,
    expert_ids,
    priority,
    gain_attn,
    qkv_weight,
    out_weight,
    gain_ffn,
    router,
    in_weight,
    down_weight,
    cotangent,
):
    tok_rows = hidden_in.shape[1]
    width = hidden_in.shape[2]
    contexts = lax.axis_size("context")
    span_len = tok_rows // 2
    seq_len = tok_rows * contexts
    group = HEADS // KV_HEADS
    q_cols = HEADS * HEAD
    kv_cols = KV_HEADS * HEAD
    scale = HEAD ** (-0.5)
    local_experts = in_weight.shape[0]
    n_experts = local_experts * lax.axis_size("expert")
    top_k = expert_ids.shape[2]
    capacity = (9 * tok_rows * top_k + 8 * n_experts - 1) // (8 * n_experts)
    ff_width = down_weight.shape[2]
    seq_spans = span_order[0]
    stored = jnp.arange(seq_len) // span_len
    all_pos = (seq_spans[stored] * span_len + jnp.arange(seq_len) % span_len).astype(jnp.float32)
    my_pos = lax.dynamic_slice_in_dim(all_pos, lax.axis_index("context") * tok_rows, tok_rows)
    cosine, sine = rope_tables(my_pos, HEAD)
    inputs = hidden_in[0].astype(jnp.float32)
    inv_one = lax.rsqrt(jnp.mean(inputs * inputs, axis=-1, keepdims=True) + NORM_EPS)
    plain_one = inputs * inv_one
    normed = (plain_one * gain_attn).astype(jnp.bfloat16)
    mixed = jnp.dot(normed, qkv_weight, preferred_element_type=jnp.float32)
    queries = (
        rotate(mixed[:, :q_cols].reshape(tok_rows, HEADS, HEAD), cosine, sine) * scale
    ).astype(jnp.bfloat16)
    keys = rotate(
        mixed[:, q_cols : q_cols + kv_cols].reshape(tok_rows, KV_HEADS, HEAD), cosine, sine
    ).astype(jnp.bfloat16)
    values = mixed[:, q_cols + kv_cols :].reshape(tok_rows, KV_HEADS, HEAD).astype(jnp.bfloat16)
    grouped = queries.reshape(tok_rows, KV_HEADS, group, HEAD)

    def key_scores(key_piece):
        scores = jnp.einsum(
            "qkgd,skd->kgqs", grouped, key_piece, preferred_element_type=jnp.float32
        )
        visible = all_pos[None, None, None, :] <= my_pos[None, None, :, None]
        return (jnp.where(visible, scores, MASKED), visible)

    running = jnp.full((KV_HEADS, group, tok_rows), MASKED, jnp.float32)
    key_piece = lax.all_gather(keys, "context", axis=0, tiled=True)
    value_piece = lax.all_gather(values, "context", axis=0, tiled=True)
    scores, visible = key_scores(key_piece)
    newest = jnp.maximum(running, jnp.max(scores, axis=-1))
    weights = jnp.where(visible, jnp.exp(scores - newest[..., None]), 0.0)
    totals = jnp.sum(weights, axis=-1)
    accum = jnp.einsum(
        "kgqs,skd->kgqd",
        weights.astype(jnp.bfloat16),
        value_piece,
        preferred_element_type=jnp.float32,
    )
    running, totals, accum = (newest, totals, accum)
    log_total = running + jnp.log(totals)
    attended = (
        (accum / totals[..., None])
        .transpose(2, 0, 1, 3)
        .reshape(tok_rows, q_cols)
        .astype(jnp.bfloat16)
    )
    resid = inputs + jnp.einsum(
        "rh,dh->rd", attended, out_weight, preferred_element_type=jnp.float32
    )
    inv_two = lax.rsqrt(jnp.mean(resid * resid, axis=-1, keepdims=True) + NORM_EPS)
    plain_two = resid * inv_two
    ffn_in = (plain_two * gain_ffn).astype(jnp.bfloat16)
    logits = jnp.dot(ffn_in, router, preferred_element_type=jnp.float32)
    token_ids = expert_ids[0]
    gates = softmax_last(jnp.take_along_axis(logits, token_ids, axis=1))
    slots = route(token_ids, priority[0], n_experts, capacity)
    pair_rows = jnp.repeat(ffn_in, top_k, axis=0)
    send_rows = (
        jnp.zeros((n_experts * capacity, width), jnp.bfloat16).at[slots].set(pair_rows, mode="drop")
    )
    received = lax.all_to_all(
        send_rows.reshape(n_experts, capacity, width),
        "expert",
        split_axis=0,
        concat_axis=1,
        tiled=True,
    )
    inner = jnp.einsum("erd,edf->erf", received, in_weight, preferred_element_type=jnp.float32)
    gate_part = inner[..., :ff_width]
    up_part = inner[..., ff_width:]
    sigma = 1.0 / (1.0 + jnp.exp(-gate_part))
    activated = gate_part * sigma
    hidden = (activated * up_part).astype(jnp.bfloat16)
    expert_out = jnp.einsum(
        "erf,edf->erd", hidden, down_weight, preferred_element_type=jnp.float32
    ).astype(jnp.bfloat16)
    returned = lax.all_to_all(
        expert_out, "expert", split_axis=1, concat_axis=0, tiled=True
    ).reshape(n_experts * capacity, width)
    padded = jnp.concatenate([returned, jnp.zeros((1, width), jnp.bfloat16)], axis=0)
    picked = padded[slots].reshape(tok_rows, top_k, width)
    output = (resid + jnp.sum(gates[:, :, None] * picked, axis=1)).astype(jnp.bfloat16)
    cot_low = cotangent[0]
    cot_full = cot_low.astype(jnp.float32)
    gate_grad = jnp.einsum("rkd,rd->rk", picked, cot_low, preferred_element_type=jnp.float32)
    ret_grad = (
        (gates[:, :, None] * cot_full[:, None, :])
        .astype(jnp.bfloat16)
        .reshape(tok_rows * top_k, width)
    )
    send_grad = (
        jnp.zeros((n_experts * capacity, width), jnp.bfloat16).at[slots].set(ret_grad, mode="drop")
    )
    received_grad = lax.all_to_all(
        send_grad.reshape(n_experts, capacity, width),
        "expert",
        split_axis=0,
        concat_axis=1,
        tiled=True,
    )
    hid_grad = jnp.einsum(
        "erd,edf->erf", received_grad, down_weight, preferred_element_type=jnp.float32
    )
    slope = sigma * (1.0 + gate_part * (1.0 - sigma))
    inner_grad = jnp.concatenate(
        [hid_grad * up_part * slope, hid_grad * activated], axis=-1
    ).astype(jnp.bfloat16)
    row_grad = jnp.einsum(
        "erf,edf->erd", inner_grad, in_weight, preferred_element_type=jnp.float32
    ).astype(jnp.bfloat16)
    part_rows = received
    expert_in = (
        lax.psum_scatter(
            jnp.einsum(
                "erd,erf->def", part_rows, inner_grad, preferred_element_type=jnp.float32
            ).astype(jnp.bfloat16),
            ("context", "dp"),
            scatter_dimension=0,
            tiled=True,
        )
        .astype(jnp.float32)
        .transpose(1, 0, 2)
    )
    part_rows = received_grad
    expert_down = (
        lax.psum_scatter(
            jnp.einsum(
                "erd,erf->def", part_rows, hidden, preferred_element_type=jnp.float32
            ).astype(jnp.bfloat16),
            ("context", "dp"),
            scatter_dimension=0,
            tiled=True,
        )
        .astype(jnp.float32)
        .transpose(1, 0, 2)
    )
    back_rows = lax.all_to_all(row_grad, "expert", split_axis=1, concat_axis=0, tiled=True).reshape(
        n_experts * capacity, width
    )
    back_padded = jnp.concatenate([back_rows, jnp.zeros((1, width), jnp.bfloat16)], axis=0)
    pair_grad = back_padded[slots].reshape(tok_rows, top_k, width)
    mix_grad = gates * (gate_grad - jnp.sum(gates * gate_grad, axis=-1, keepdims=True))
    matches = token_ids[:, :, None] == jnp.arange(n_experts)[None, None, :]
    logit_grad = jnp.sum(jnp.where(matches, mix_grad[:, :, None], 0.0), axis=1).astype(jnp.bfloat16)
    router_part = jnp.einsum("rd,re->de", ffn_in, logit_grad, preferred_element_type=jnp.float32)
    ffn_grad = jnp.sum(pair_grad.astype(jnp.float32), axis=1) + jnp.einsum(
        "re,de->rd", logit_grad, router, preferred_element_type=jnp.float32
    )
    gain_ffn_part = jnp.sum(ffn_grad * plain_two, axis=0)
    scaled_two = ffn_grad * gain_ffn
    resid_grad = cot_full + inv_two * (
        scaled_two - plain_two * jnp.mean(scaled_two * plain_two, axis=-1, keepdims=True)
    )
    resid_low = resid_grad.astype(jnp.bfloat16)
    out_part = jnp.einsum("rd,rh->dh", resid_low, attended, preferred_element_type=jnp.float32)
    att_grad = jnp.einsum(
        "rd,dh->rh", resid_low, out_weight, preferred_element_type=jnp.float32
    ).astype(jnp.bfloat16)
    att_heads = att_grad.reshape(tok_rows, KV_HEADS, group, HEAD)
    row_delta = jnp.sum(
        att_heads.astype(jnp.float32)
        * attended.reshape(tok_rows, KV_HEADS, group, HEAD).astype(jnp.float32),
        axis=-1,
    ).transpose(1, 2, 0)
    key_piece = lax.all_gather(keys, "context", axis=0, tiled=True)
    value_piece = lax.all_gather(values, "context", axis=0, tiled=True)
    scores, visible = key_scores(key_piece)
    soft = jnp.exp(scores - log_total[..., None])
    prob_grad = jnp.einsum(
        "qkgd,skd->kgqs", att_heads, value_piece, preferred_element_type=jnp.float32
    )
    score_grad = (soft * (prob_grad - row_delta[..., None])).astype(jnp.bfloat16)
    query_acc = jnp.einsum(
        "kgqs,skd->kgqd", score_grad, key_piece, preferred_element_type=jnp.float32
    )
    key_part = jnp.einsum("kgqs,qkgd->skd", score_grad, grouped, preferred_element_type=jnp.float32)
    value_part = jnp.einsum(
        "kgqs,qkgd->skd", soft.astype(jnp.bfloat16), att_heads, preferred_element_type=jnp.float32
    )
    pair_acc = jnp.stack([key_part, value_part], axis=1)
    query_acc, pair_acc = (query_acc, pair_acc)
    own_pairs = lax.psum_scatter(
        pair_acc.astype(jnp.bfloat16), "context", scatter_dimension=0, tiled=True
    ).astype(jnp.float32)
    query_grad = (
        unrotate(query_acc.transpose(2, 0, 1, 3).reshape(tok_rows, HEADS, HEAD), cosine, sine)
        * scale
    )
    key_grad = unrotate(own_pairs[:, 0], cosine, sine)
    mixed_grad = jnp.concatenate(
        [
            query_grad.reshape(tok_rows, q_cols),
            key_grad.reshape(tok_rows, kv_cols),
            own_pairs[:, 1].reshape(tok_rows, kv_cols),
        ],
        axis=-1,
    ).astype(jnp.bfloat16)
    qkv_part = jnp.einsum("rd,rc->dc", normed, mixed_grad, preferred_element_type=jnp.float32)
    norm_grad = jnp.einsum("rc,dc->rd", mixed_grad, qkv_weight, preferred_element_type=jnp.float32)
    gain_attn_part = jnp.sum(norm_grad * plain_one, axis=0)
    scaled_one = norm_grad * gain_attn
    input_grad = (
        resid_grad
        + inv_one
        * (scaled_one - plain_one * jnp.mean(scaled_one * plain_one, axis=-1, keepdims=True))
    ).astype(jnp.bfloat16)
    gain_attn_grad, qkv_grad, out_proj_grad, gain_ffn_grad, router_grad = (
        lax.psum_scatter(
            gain_attn_part, ("expert", "context", "dp"), scatter_dimension=0, tiled=True
        ),
        lax.psum_scatter(qkv_part, ("expert", "context", "dp"), scatter_dimension=0, tiled=True),
        lax.psum_scatter(out_part, ("expert", "context", "dp"), scatter_dimension=0, tiled=True),
        lax.psum_scatter(
            gain_ffn_part, ("expert", "context", "dp"), scatter_dimension=0, tiled=True
        ),
        lax.psum_scatter(router_part, ("expert", "context", "dp"), scatter_dimension=0, tiled=True),
    )
    return (
        output[None],
        input_grad[None],
        gain_attn_grad,
        qkv_grad,
        out_proj_grad,
        gain_ffn_grad,
        router_grad,
        expert_in,
        expert_down,
    )


def solution(mesh):
    in_specs = (
        P(("expert", "dp"), "context", None),
        P(("expert", "dp"), None),
        P(("expert", "dp"), "context", None),
        P(("expert", "dp"), "context", None),
        P(),
        P(),
        P(),
        P(),
        P(),
        P("expert", None, None),
        P("expert", None, None),
        P(("expert", "dp"), "context", None),
    )
    out_specs = (
        P(("expert", "dp"), "context", None),
        P(("expert", "dp"), "context", None),
        P(("expert", "context", "dp")),
        P(("expert", "context", "dp"), None),
        P(("expert", "context", "dp"), None),
        P(("expert", "context", "dp")),
        P(("expert", "context", "dp"), None),
        P("expert", ("context", "dp"), None),
        P("expert", ("context", "dp"), None),
    )
    tuned = dict(mesh.shape) == {"expert": 2, "context": 4, "dp": 4}
    body = local if tuned else general
    return jax.shard_map(body, mesh=mesh, in_specs=in_specs, out_specs=out_specs, check_vma=False)
```

```python
import functools

import jax
import jax.numpy as jnp
import numpy as np
from jax import lax
from jax.experimental import pallas as pl
from jax.experimental.pallas import tpu as pltpu
from jax.sharding import PartitionSpec as P

HEADS = 12
KV_HEADS = 2
HEAD = 128


ROPE_BASE = 1000000.0
NORM_EPS = 1e-06
MASKED = -1e30


def rope_tables(positions, head_size):
    half_size = head_size // 2
    freqs = ROPE_BASE ** (jnp.arange(half_size).astype(jnp.float32) * (-2.0 / head_size))
    angles = positions[:, None] * freqs[None, :]
    return (jnp.cos(angles)[:, None, :], jnp.sin(angles)[:, None, :])


def rotate(values, cosine, sine):
    half_size = values.shape[-1] // 2
    first = values[..., :half_size]
    second = values[..., half_size:]
    return jnp.concatenate(
        [first * cosine - second * sine, second * cosine + first * sine], axis=-1
    )


def unrotate(values, cosine, sine):
    half_size = values.shape[-1] // 2
    first = values[..., :half_size]
    second = values[..., half_size:]
    return jnp.concatenate(
        [first * cosine + second * sine, second * cosine - first * sine], axis=-1
    )


def softmax_last(scores):
    shifted = jnp.exp(scores - jnp.max(scores, axis=-1, keepdims=True))
    return shifted / jnp.sum(shifted, axis=-1, keepdims=True)


def route(block_ids, block_order, n_experts, capacity):
    flat_ids = block_ids.reshape(-1)
    flat_order = block_order.reshape(-1)
    choose = (flat_ids[:, None] == jnp.arange(n_experts)[None, :]).astype(jnp.int32)
    ordered = jnp.zeros_like(choose).at[flat_order].set(choose)
    earlier = jnp.cumsum(ordered, axis=0, dtype=jnp.int32) - ordered
    ranks = jnp.sum(earlier[flat_order] * choose, axis=1)
    return jnp.where(ranks < capacity, flat_ids * capacity + ranks, n_experts * capacity)


MESH = pl.DeviceIdType.MESH
F32 = jnp.float32
BF16 = jnp.bfloat16


def dot(a, b):
    return jnp.dot(a, b, preferred_element_type=F32)


def dot_nt(a, b):
    return lax.dot_general(a, b, (((1,), (1,)), ((), ())), preferred_element_type=F32)


def dot_tn(a, b):
    return lax.dot_general(a, b, (((0,), (0,)), ((), ())), preferred_element_type=F32)


def plus(a, *more):
    total = a.astype(F32)
    for b in more:
        total = total + b.astype(F32)
    return total.astype(BF16)


def lanes(at, size):
    return pl.ds(pl.multiple_of(at, 128), size)


def rows_at(at, size):
    return pl.ds(pl.multiple_of(at, 16), size)


def remote(src, dst, s, r, dev):
    return pltpu.make_async_remote_copy(
        src_ref=src, dst_ref=dst, send_sem=s, recv_sem=r, device_id=dev, device_id_type=MESH
    )


class Spot:
    def __init__(self):
        e, c, z = lax.axis_index("expert"), lax.axis_index("context"), lax.axis_index("dp")
        self.ctx = lax.axis_size("context")
        self.parts = lax.axis_size("dp")
        self.planes = self.ctx * lax.axis_size("expert")
        y, k = lax.div(c, 2), lax.rem(c, 2)
        self.e, self.c, self.z, self.k = e, c, z, k
        self.me = e * self.ctx + c
        self.xp, self.yp = (1 - e, c, z), (e, (1 - y) * 2 + k, z)
        self.kp, self.yk = (e, y * 2 + 1 - k, z), (e, (1 - y) * 2 + 1 - k, z)
        self.chips = [
            eq * self.ctx + yq * 2 for eq, yq in ((e, y), (1 - e, y), (e, 1 - y), (1 - e, 1 - y))
        ]

    def others(self):
        found = []
        for step in range(1, self.planes):
            other = lax.rem(self.me + step, self.planes)
            found.append((other, (lax.div(other, self.ctx), lax.rem(other, self.ctx), self.z)))
        return found

    def along(self):
        e, c, z = self.e, self.c, self.z
        return [(z < self.parts - 1, (e, c, z + 1)), (z > 0, (e, c, z - 1))]


def greet(peers, extra=()):
    barrier = pltpu.get_barrier_semaphore()
    for peer in peers:
        pl.semaphore_signal(barrier, inc=1, device_id=peer, device_id_type=MESH)
    for there, peer in extra:

        @pl.when(there)
        def _():
            pl.semaphore_signal(barrier, inc=1, device_id=peer, device_id_type=MESH)

    count = len(peers)
    for there, _ in extra:
        count = count + there.astype(jnp.int32)
    pl.semaphore_wait(barrier, count)


class Plane:
    def __init__(self, spot, zcr, zk, rx, ry, s, r, zcr_there=None):
        self.zcr_there = zcr_there or zcr
        self.spot, self.zcr, self.zk, self.rx, self.ry, self.s, self.r = spot, zcr, zk, rx, ry, s, r
        half = zk[0].shape[0] // 2
        self.lo, self.hi = pl.ds(0, half), pl.ds(half, half)
        self.sent, self.gives = [], []

    def push(self, src, dst, i, dev):
        copy = remote(src, dst, self.s.at[i], self.r.at[i], dev)
        copy.start()
        self.sent.append(copy)

    def arrive(self, dst, i):
        remote(dst, dst, self.s.at[i], self.r.at[i], self.spot.kp).wait_recv()

    def given(self):
        for copy in self.gives:
            copy.wait_send()
        self.gives = []

    def give(self, q, src):
        self.gives.append(remote(src, self.zcr_there[q], self.s.at[q], self.r.at[q], self.spot.kp))
        self.gives[-1].start()

    def fold(self, q, own=None):
        self.arrive(self.zcr[q], q)
        self.zk[q][...] = plus(self.zk[q][...] if own is None else own, self.zcr[q][...])

    def near(self):
        self.push(self.zk[1].at[self.lo], self.rx[1], 5, self.spot.xp)
        self.push(self.zk[2].at[self.hi], self.ry[1], 8, self.spot.yp)

    def across(self):
        self.push(self.zk[3].at[self.lo], self.rx[0], 4, self.spot.xp)
        self.push(self.zk[3].at[self.hi], self.ry[0], 7, self.spot.yp)

    def turn(self):
        lo, hi = self.lo, self.hi
        self.arrive(self.rx[0], 4)
        self.zk[2][lo] = plus(self.zk[2][lo], self.rx[0][...])
        self.push(self.zk[2].at[lo], self.ry[2], 9, self.spot.yp)
        self.arrive(self.ry[0], 7)
        self.zk[1][hi] = plus(self.zk[1][hi], self.ry[0][...])
        self.push(self.zk[1].at[hi], self.rx[2], 6, self.spot.xp)

    def total(self):
        self.arrive(self.rx[1], 5)
        self.arrive(self.ry[1], 8)
        self.arrive(self.rx[2], 6)
        self.arrive(self.ry[2], 9)
        return (
            (self.lo, (self.zk[0][self.lo], self.rx[1][...], self.ry[2][...])),
            (self.hi, (self.zk[0][self.hi], self.rx[2][...], self.ry[1][...])),
        )

    def done(self):
        self.given()
        for copy in self.sent:
            copy.wait_send()


def plane_of(spot, zcr, zk, rx, ry, s, r):
    four, three = range(4), range(3)
    return Plane(
        spot, [zcr.at[q] for q in four], [zk.at[q] for q in four], [rx.at[i] for i in three], [ry.at[i] for i in three], s, r
    )


def plane_scratch(block, wide):
    return [
        pltpu.VMEM((4, block, wide), BF16),
        pltpu.VMEM((4, block, wide), BF16),
        pltpu.VMEM((3, block // 2, wide), BF16),
        pltpu.VMEM((3, block // 2, wide), BF16),
        pltpu.SemaphoreType.DMA((10,)),
        pltpu.SemaphoreType.DMA((10,)),
    ]


def summed(terms):
    total = terms[0].astype(F32)
    for term in terms[1:]:
        total = total + term.astype(F32)
    return total


class Line:
    def __init__(self, spot, own, adder, buf, s, r):
        z, last = spot.z, spot.parts - 1
        e, c = spot.e, spot.c
        self.own, self.adder, self.buf, self.s, self.r = own, adder, buf, s, r
        self.z, self.last, self.parts = z, last, spot.parts
        self.ways = [(z, (e, c, z + 1), lambda d: d), (last - z, (e, c, z - 1), lambda d: last - d)]

    def step(self, turn):
        for way, (i, dev, part) in enumerate(self.ways):
            to, s, r = self.buf.at[way, turn - 1], self.s.at[way, turn - 1], self.r.at[way, turn - 1]

            @pl.when(i == 0)
            def _():
                remote(self.own(part(self.parts - turn)), to, s, r, dev).start()

            if turn >= 2:
                came, s_came, r_came = (x.at[way, turn - 2] for x in (self.buf, self.s, self.r))

                @pl.when((i >= 1) & (i <= turn - 1) & (i < self.last))
                def _():
                    remote(came, came, s_came, r_came, dev).wait_recv()
                    self.adder(came, part(self.parts - turn + i))
                    remote(came, to, s, r, dev).start()

    def final(self, put):
        last, z = self.last, self.z
        for way, (i, dev, _) in enumerate(self.ways):
            came = self.buf.at[way, last - 1]

            @pl.when(i >= 1)
            def _():
                remote(came, came, self.s.at[way, last - 1], self.r.at[way, last - 1], dev).wait_recv()

        up, down = self.buf.at[0, last - 1], self.buf.at[1, last - 1]
        pl.when(z == 0)(lambda: put(down))
        pl.when(z == last)(lambda: put(up))
        pl.when((z > 0) & (z < last))(lambda: put(up, down))

    def done(self):
        for way, (i, dev, _) in enumerate(self.ways):
            for turn in range(1, self.parts):
                came = self.buf.at[way, turn - 1]

                @pl.when((i <= turn - 1) & (i < self.last))
                def _():
                    remote(came, came, self.s.at[way, turn - 1], self.r.at[way, turn - 1], dev).wait_send()


def line_scratch(parts, piece):
    return [
        pltpu.VMEM((2, parts - 1) + piece, BF16),
        pltpu.SemaphoreType.DMA((2, parts - 1)),
        pltpu.SemaphoreType.DMA((2, parts - 1)),
    ]


class ExpertLine:
    def __init__(self, spot, ref, at, cols, buf, s, r, fin, spread, a_s, a_r):
        self.spot, self.ref, self.at, self.cols = spot, ref, at, cols
        self.fin, self.spread, self.a_s, self.a_r = fin, spread, a_s, a_r
        self.line = Line(spot, self.own, self.adder, buf, s, r)
        self.step = self.line.step

    def own(self, d):
        return self.ref.at[:, d, :, pl.ds(self.at, self.cols)]

    def piece(self, cc, d):
        return self.ref[cc, d, :, self.at : self.at + self.cols]

    def adder(self, came, d):
        for cc in range(self.spot.ctx):
            came[cc] = plus(came[cc], self.piece(cc, d))

    def final(self):
        spot = self.spot

        def put(*came):
            for cc in range(spot.ctx):
                self.fin[cc] = plus(self.piece(cc, spot.z), *(x[cc] for x in came))

        self.line.final(put)
        for step in range(1, spot.ctx):
            cc = lax.rem(spot.c + step, spot.ctx)
            remote(
                self.fin.at[cc],
                self.spread.at[spot.c],
                self.a_s.at[step - 1],
                self.a_r.at[step - 1],
                (spot.e, cc, spot.z),
            ).start()

    def done(self, out):
        spot = self.spot
        for step in range(1, spot.ctx):
            cc = lax.rem(spot.c + spot.ctx - step, spot.ctx)
            got = remote(
                self.spread.at[cc],
                self.spread.at[cc],
                self.a_s.at[step - 1],
                self.a_r.at[step - 1],
                (spot.e, cc, spot.z),
            )
            got.wait_recv()
            got.wait_send()
            out[cc] = self.spread[cc]
        out[spot.c] = self.fin[spot.c]
        self.line.done()


def expert_scratch(ctx, parts, rows, cols):
    return line_scratch(parts, (ctx, rows, cols)) + [
        pltpu.VMEM((ctx, rows, cols), BF16),
        pltpu.VMEM((ctx, rows, cols), BF16),
        pltpu.SemaphoreType.DMA((ctx - 1,)),
        pltpu.SemaphoreType.DMA((ctx - 1,)),
    ]


class Gather:
    def __init__(self, spot, own, buf, s, r):
        self.spot, self.own, self.buf, self.s, self.r = spot, own, buf, s, r
        half = own.shape[0] // 2
        self.lo, self.hi = pl.ds(0, half), pl.ds(half, half)
        self.x_me, self.y_me, self.d_me = (base + spot.k for base in spot.chips[1:])
        self.side = 1 - 2 * spot.k
        self.sent = []

    def push(self, src, dst, i, dev):
        copy = remote(src, dst, self.s.at[i], self.r.at[i], dev)
        copy.start()
        self.sent.append(copy)

    def move(self, p, rows, i, dev):
        self.push(self.buf.at[p, rows], self.buf.at[p, rows], i, dev)

    def got(self, p, rows, i):
        to = self.buf.at[p, rows]
        remote(to, to, self.s.at[i], self.r.at[i], self.spot.kp).wait_recv()

    def start(self):
        me, own, lo, hi = self.spot.me, self.own, self.lo, self.hi
        self.push(own.at[lo], self.buf.at[me, lo], 0, self.spot.xp)
        self.push(own.at[lo], self.buf.at[me, lo], 6, self.spot.kp)
        self.push(own.at[hi], self.buf.at[me, hi], 13, self.spot.kp)
        self.push(own.at[hi], self.buf.at[me, hi], 1, self.spot.xp)

    def start_y(self):
        me, own, lo, hi = self.spot.me, self.own, self.lo, self.hi
        self.push(own.at[hi], self.buf.at[me, hi], 3, self.spot.yp)
        self.push(own.at[lo], self.buf.at[me, lo], 2, self.spot.yp)

    def first(self):
        spot = self.spot
        self.got(self.x_me, self.lo, 0)
        self.move(self.x_me, self.lo, 4, spot.yp)
        self.move(self.x_me, self.lo, 7, spot.kp)
        self.got(self.y_me, self.hi, 3)
        self.move(self.y_me, self.hi, 5, spot.xp)
        self.move(self.y_me, self.hi, 10, spot.kp)

    def second(self):
        self.got(self.x_me, self.hi, 1)
        self.move(self.x_me, self.hi, 8, self.spot.kp)
        self.got(self.y_me, self.lo, 2)
        self.move(self.y_me, self.lo, 9, self.spot.kp)

    def third(self):
        self.got(self.d_me, self.lo, 4)
        self.move(self.d_me, self.lo, 11, self.spot.kp)
        self.got(self.d_me, self.hi, 5)
        self.move(self.d_me, self.hi, 12, self.spot.kp)

    def other_core(self, q):
        low_sem, high_sem = ((6, 13), (7, 8), (9, 10), (11, 12))[q]
        p = (self.spot.me, self.x_me, self.y_me, self.d_me)[q] + self.side
        self.got(p, self.lo, low_sem)
        self.got(p, self.hi, high_sem)

    def done(self):
        for copy in self.sent:
            copy.wait_send()


GATHER_COPIES = 14


def front_kernel(
    cap,
    span,
    hidden,
    cot,
    gain_one,
    freqs,
    gain_two,
    router_t,
    ids_t,
    turn_t,
    wqkv_h,
    wout_h,
    normed,
    queries,
    kv,
    lse,
    attended,
    resid,
    ffn_in,
    trig,
    meta,
    cot_all,
    wqkv,
    wout,
    mask,
    vt,
    load_sem,
    kv_s,
    kv_r,
    co_s,
    co_r,
):
    spot = Spot()
    c, ctx, k = spot.c, spot.ctx, spot.k
    tok, width = hidden.shape
    group = HEADS // KV_HEADS
    kv_cols = KV_HEADS * HEAD
    half_head = HEAD // 2
    seq = kv.shape[0]
    spans = span.shape[1]
    size = seq // spans
    mine = spans // ctx
    n_experts = meta.shape[0]
    loads = [
        pltpu.make_async_copy(wqkv_h.at[:, pl.ds(width, 2 * kv_cols)], wqkv.at[:, pl.ds(width, 2 * kv_cols)], load_sem.at[0]),
        pltpu.make_async_copy(wqkv_h.at[:, pl.ds(0, width)], wqkv.at[:, pl.ds(0, width)], load_sem.at[1]),
        pltpu.make_async_copy(wout_h, wout, load_sem.at[2]),
        pltpu.make_async_copy(cot, cot_all.at[spot.me], load_sem.at[3]),
    ]
    for load in loads:
        load.start()
    greet([spot.xp, spot.yp, spot.kp])
    gather = Gather(spot, cot, cot_all, co_s, co_r)
    gather.start()

    x = hidden[...].astype(F32)
    inv = lax.rsqrt(jnp.mean(x * x, axis=-1, keepdims=True) + NORM_EPS)
    normed[...] = (x * inv * gain_one[...]).astype(BF16)

    along = lax.broadcasted_iota(jnp.int32, (tok, HEAD), 0)
    start_one, start_two = span[0, c * mine] * size, (span[0, c * mine + 1] - 1) * size
    place = jnp.where(along < size, start_one, start_two) + along
    angle = place.astype(F32) * freqs[...]
    cosine, sine = jnp.cos(angle), jnp.sin(angle)
    lane = lax.broadcasted_iota(jnp.int32, (tok, HEAD), 1)
    sine = jnp.where(lane < half_head, -sine, sine)
    trig[0] = cosine
    trig[1] = sine

    def rotate_in(w):
        return w * cosine + pltpu.roll(w, half_head, 1) * sine

    loads[0].wait()
    raw = dot(normed[...], wqkv[:, width:])
    own = rows_at(c * tok, tok)
    for g in range(KV_HEADS):
        at = slice(g * HEAD, (g + 1) * HEAD)
        kv[own, at] = rotate_in(raw[:, at]).astype(BF16)
    kv[own, kv_cols:] = raw[:, kv_cols:].astype(BF16)

    def kv_copy(rows, i, dev):
        return remote(kv.at[rows], kv.at[rows], kv_s.at[i], kv_r.at[i], dev)

    flip_c = lax.rem(c + 2, ctx)
    near_c = c + 1 - 2 * k
    across_c = lax.rem(near_c + 2, ctx)
    sent = [kv_copy(own, 1, spot.yp), kv_copy(own, 0, spot.kp)]
    for copy in sent:
        copy.start()
    gather.start_y()

    loads[1].wait()
    step = 256

    @pl.loop(0, width // step)
    def _(n):
        at = lanes(n * step, step)
        raw = dot(normed[...], wqkv[:, at])
        for i in range(step // HEAD):
            w = raw[:, i * HEAD : (i + 1) * HEAD]
            queries[:, lanes(n * step + i * HEAD, HEAD)] = (rotate_in(w) * HEAD**-0.5).astype(BF16)

    flip = rows_at(flip_c * tok, tok)
    kv_copy(flip, 1, spot.kp).wait_recv()
    sent.append(kv_copy(flip, 2, spot.kp))
    sent[-1].start()

    expert = lax.broadcasted_iota(jnp.int32, (n_experts, tok), 0)
    never = tok * ids_t.shape[0]
    turn = jnp.full((n_experts, tok), never, jnp.int32)
    for i in range(ids_t.shape[0]):
        turn = jnp.where(ids_t[i : i + 1, :] == expert, turn_t[i : i + 1, :], turn)
    turn_f = turn.astype(F32)
    tall = jnp.concatenate([turn_f, jnp.full((HEAD - n_experts, tok), float(never), F32)], axis=0).T
    meta[...] = jnp.zeros(meta.shape, F32)
    for g in range(n_experts):
        row = turn_f[g : g + 1, :]
        rank = jnp.sum(jnp.where(tall[:, g : g + 1] < row, 1.0, 0.0), axis=0, keepdims=True)
        meta[g, 0:1, :] = jnp.where((row < never) & (rank < cap), rank, -1.0)

    along_q = lax.broadcasted_iota(jnp.int32, (size, tok), 1)
    q_pos = jnp.where(along_q < size, start_one, start_two) + along_q
    for s in range(spans):
        k_pos = span[0, s] * size + lax.broadcasted_iota(jnp.int32, (size, tok), 0)
        mask[s * size : (s + 1) * size, :] = jnp.where(k_pos <= q_pos, 0.0, MASKED)

    near, across = rows_at(near_c * tok, tok), rows_at(across_c * tok, tok)
    kv_copy(near, 0, spot.kp).wait_recv()
    kv_copy(across, 2, spot.kp).wait_recv()
    for g in range(KV_HEADS):
        vt[g] = kv[:, kv_cols + g * HEAD : kv_cols + (g + 1) * HEAD].astype(F32).T.astype(BF16)
    lse[...] = jnp.zeros(lse.shape, F32)

    def heads(g, first, count):
        @pl.loop(first, first + count)
        def _(h):
            at = lanes(h * HEAD, HEAD)
            scores = dot_nt(kv[:, g * HEAD : (g + 1) * HEAD], queries[:, at]) + mask[...]
            top = jnp.max(scores, axis=0, keepdims=True)
            weights = jnp.exp(scores - top)
            total = jnp.sum(weights, axis=0, keepdims=True)
            lse[pl.ds(h, 1), :] = top + jnp.log(total)
            out = dot(vt[g], weights.astype(BF16)) / total
            attended[:, at] = out.T.astype(BF16)

    heads(0, 0, 3)
    gather.first()
    heads(0, 3, 3)
    heads(1, 6, 3)
    gather.second()
    heads(1, 9, 3)

    loads[2].wait()

    @pl.loop(0, width // step)
    def _(n):
        at = lanes(n * step, step)
        resid[:, at] = hidden[:, at].astype(F32) + dot_nt(attended[...], wout[at, :])

    r = resid[...]
    inv = lax.rsqrt(jnp.mean(r * r, axis=-1, keepdims=True) + NORM_EPS)
    ffn_in[...] = (r * inv * gain_two[...]).astype(BF16)
    logits = dot_nt(router_t[...], ffn_in[...])[:n_experts]
    logits = jnp.where(turn < never, logits, MASKED)
    shifted = jnp.exp(logits - jnp.max(logits, axis=0, keepdims=True))
    gates = shifted / jnp.sum(shifted, axis=0, keepdims=True)
    for g in range(n_experts):
        meta[g, 1:2, :] = gates[g : g + 1, :]
    gather.third()
    for q in range(4):
        gather.other_core(q)
    loads[3].wait()
    gather.done()
    for copy in sent:
        copy.wait_send()


def run_front(cap, span, hidden, cot, gain_one, freqs, gain_two, router_t, ids_t, turn_t, wqkv, wout, ctx, planes):
    tok, width = hidden.shape
    seq = tok * ctx
    n_experts = planes
    kv_cols = 2 * KV_HEADS * HEAD
    vm, anyspace = pl.BlockSpec(memory_space=pltpu.VMEM), pl.BlockSpec(memory_space=pl.ANY)
    sm = pl.BlockSpec(memory_space=pltpu.SMEM)
    shape = jax.ShapeDtypeStruct
    dma = pltpu.SemaphoreType.DMA
    return pl.pallas_call(
        functools.partial(front_kernel, cap),
        out_shape=(
            shape((tok, width), BF16),
            shape((tok, width), BF16),
            shape((seq, kv_cols), BF16),
            shape((16, tok), F32),
            shape((tok, width), BF16),
            shape((tok, width), F32),
            shape((tok, width), BF16),
            shape((2, tok, HEAD), F32),
            shape((n_experts, 8, tok), F32),
            shape((planes, tok, width), BF16),
        ),
        in_specs=[sm] + [vm] * 8 + [anyspace] * 2,
        out_specs=(vm,) * 9 + (anyspace,),
        scratch_shapes=[
            pltpu.VMEM(wqkv.shape, BF16),
            pltpu.VMEM(wout.shape, BF16),
            pltpu.VMEM((seq, tok), F32),
            pltpu.VMEM((KV_HEADS, HEAD, seq), BF16),
            dma((4,)),
            dma((3,)),
            dma((3,)),
            dma((GATHER_COPIES,)),
            dma((GATHER_COPIES,)),
        ],
        compiler_params=pltpu.CompilerParams(
            collective_id=4, has_side_effects=True, vmem_limit_bytes=56 * 2**20
        ),
        cost_estimate=pl.CostEstimate(flops=5 * 10**9, bytes_accessed=20 * 10**6, transcendentals=4 * 10**6),
    )(span, hidden, cot, gain_one, freqs, gain_two, router_t, ids_t, turn_t, wqkv, wout)


def ffn_kernel(cap, ffn, resid, cot_h, meta, win_h, wdn_h, output, pg_out, gg_out, gwin_h, ex_out, *scratch):
    agb, metas, cotb, win, wdn, xs, ds, hid, igs, pgs, ggs, ggr, wint, gwdn, pgt = scratch[:15]
    load_sem, ag_s, ag_r, me_s, me_r, gg_s, gg_r, out_s, out_r = scratch[15:24]
    plane_refs, line_refs = scratch[24:30], scratch[30:]
    spot = Spot()
    c, k, me = spot.c, spot.k, spot.me
    kp = spot.kp
    tok, width = ffn.shape
    ff = wdn.shape[1]
    planes, ctx = spot.planes, spot.ctx
    chips = spot.chips

    loads = [
        pltpu.make_async_copy(win_h.at[c], win, load_sem.at[0]),
        pltpu.make_async_copy(wdn_h.at[c], wdn, load_sem.at[1]),
        pltpu.make_async_copy(cot_h, cotb, load_sem.at[2]),
    ]
    for load in loads:
        load.start()
    others = spot.others()
    greet([dev for _, dev in others], spot.along())
    plane = plane_of(spot, *plane_refs)
    lo, hi = plane.lo, plane.hi
    outs = Plane(
        spot,
        [agb.at[2 * i + k] for i in range(4)],
        [cotb.at[base + k] for base in chips],
        [agb.at[1 - k, lo], agb.at[1 - k, hi], agb.at[3 - k, lo]],
        [agb.at[3 - k, hi], agb.at[5 - k, lo], agb.at[5 - k, hi]],
        out_s,
        out_r,
        [agb.at[2 * i + 1 - k] for i in range(4)],
    )
    line = ExpertLine(spot, gwdn, 0, ff, *line_refs)
    gather = Gather(spot, ffn, agb, ag_s, ag_r)
    for step, (other, dev) in enumerate(others):
        remote(meta.at[other], metas.at[me], me_s.at[step], me_r.at[step], dev).start()
    gather.start()
    gather.start_y()
    agb[me] = ffn[...]
    metas[me] = meta[me]
    slot_rows = lax.broadcasted_iota(jnp.int32, (cap, tok), 0).astype(F32)
    step = 256

    def spots(p):
        return jnp.where(slot_rows == metas[p, 0:1, :], 1.0, 0.0)

    def gate_of(p, hot):
        return jnp.sum(hot * metas[p, 1:2, :], axis=1, keepdims=True)

    def dispatch(q):
        for kk in range(2):
            p = chips[q] + kk
            hot = spots(p)
            low = hot.astype(BF16)
            part = pl.ds(q * 2 * cap + kk * cap, cap)
            xs[part, :] = dot(low, agb[p]).astype(BF16)
            ds[part, :] = (dot(low, cotb[p]) * gate_of(p, hot)).astype(BF16)

    def work(q, count):
        rows = pl.ds(q * 2 * cap, count * 2 * cap)

        @pl.loop(0, ff // step)
        def _(n):
            gate_cols, up_cols = lanes(n * step, step), lanes(ff + n * step, step)
            x = xs[rows, :]
            g = dot(x, win[:, gate_cols])
            u = dot(x, win[:, up_cols])
            s = 1.0 / (1.0 + jnp.exp(-g))
            act = g * s
            hid[rows, gate_cols] = (act * u).astype(BF16)
            h = dot(ds[rows, :], wdn[:, gate_cols])
            igs[rows, gate_cols] = (h * u * (s * (1.0 + g * (1.0 - s)))).astype(BF16)
            igs[rows, up_cols] = (h * act).astype(BF16)

        @pl.loop(0, width // step)
        def _(n):
            cols = lanes(n * step, step)
            pgs[pl.ds(0, count * 2 * cap), cols] = dot(igs[rows, :], wint[:, cols]).astype(BF16)

    def back(q, at):
        base = chips[q]
        mine, theirs = rows_at(at * 2 * cap + k * cap, cap), rows_at(at * 2 * cap + (1 - k) * cap, cap)
        given = agb.at[base + 1 - k]
        given[...] = dot_tn(spots(base + 1 - k).astype(BF16), pgs[theirs, :]).astype(BF16)
        plane.give(q, given)
        plane.zk[q][...] = dot_tn(spots(base + k).astype(BF16), pgs[mine, :]).astype(BF16)

    for load in loads:
        load.wait()

    @pl.loop(0, width // step)
    def _(n):
        cols = lanes(n * step, step)
        wint[:, cols] = win[cols, :].T

    for n in range(planes - 1):
        source = lax.rem(me + planes - 1 - n, planes)
        remote(metas.at[source], metas.at[source], me_s.at[n], me_r.at[n], kp).wait_recv()
    gather.other_core(0)
    dispatch(0)
    work(0, 1)
    back(0, 0)
    gather.first()
    gather.second()
    gather.other_core(1)
    dispatch(1)
    gather.other_core(2)
    dispatch(2)
    work(1, 2)
    gather.third()
    back(1, 0)
    back(2, 1)
    gather.other_core(3)
    gather.done()
    dispatch(3)
    plane.fold(1)
    plane.fold(2)
    plane.near()
    work(3, 1)
    back(3, 0)
    plane.fold(3)
    plane.given()
    plane.across()

    tall = width // ctx

    @pl.loop(0, ctx)
    def _(n):
        tile = dot_tn(ds[:, lanes(n * tall, tall)], hid[...]).astype(BF16)
        for d in range(gwdn.shape[1]):
            gwdn[n, d] = tile[d * gwdn.shape[2] : (d + 1) * gwdn.shape[2]]

    line.step(1)
    plane.fold(0)

    @pl.loop(0, width // step)
    def _(n):
        cols = lanes(n * step, step)
        ds[:, cols] = dot_nt(hid[...], wdn[cols, :]).astype(BF16)

    def returned(q):
        base = chips[q]
        for kk in range(2):
            p = base + kk
            hot = spots(p)
            rows = ds[pl.ds(q * 2 * cap + kk * cap, cap), :]
            ggs[p, 0:1, :] = jnp.sum(hot * dot_nt(rows, cotb[p]), axis=0, keepdims=True)
            scaled = (rows.astype(F32) * gate_of(p, hot)).astype(BF16)
            cotb[p] = dot_tn(hot.astype(BF16), scaled).astype(BF16)
        outs.give(q, cotb.at[base + 1 - k])

    returned(1)
    returned(2)
    plane.turn()
    returned(3)
    returned(0)
    outs.fold(1)
    outs.fold(2)
    outs.near()
    outs.fold(3)
    outs.across()
    ggr[me] = ggs[me]
    for n, (other, dev) in enumerate(others):
        remote(ggs.at[other], ggr.at[me], gg_s.at[n], gg_r.at[n], dev).start()
    line.step(2)
    outs.fold(0)
    half_wide = ff

    @pl.loop(0, 2 * ctx)
    def _(n):
        slot = lax.rem(n, 2)
        rows = lanes(lax.div(n, 2) * tall, tall)
        cols = lanes(slot * half_wide, half_wide)
        tile = pgt.at[slot]
        to = pltpu.make_async_copy(tile, gwin_h.at[rows, cols], load_sem.at[slot])

        @pl.when(n >= 2)
        def _():
            to.wait()

        tile[...] = dot_tn(xs[:, rows], igs[:, cols]).astype(BF16)
        to.start()

    for slot in range(2):
        pltpu.make_async_copy(pgt.at[slot], gwin_h.at[pl.ds(0, tall), pl.ds(0, half_wide)], load_sem.at[slot]).wait()
    line.step(3)
    outs.turn()
    for rows, terms in plane.total():
        pg_out[rows, :] = summed(terms)
    for n in range(planes - 1):
        source = lax.rem(me + planes - 1 - n, planes)
        remote(ggr.at[source], ggr.at[source], gg_s.at[n], gg_r.at[n], kp).wait_recv()
    for p in range(planes):
        gg_out[p : p + 1, :] = ggr[p, 0:1, :]
    line.final()
    for rows, terms in outs.total():
        output[rows, :] = (resid[rows, :] + summed(terms)).astype(BF16)
    for n, (other, dev) in enumerate(others):
        remote(meta.at[other], metas.at[other], me_s.at[n], me_r.at[n], dev).wait_send()
        remote(ggs.at[other], ggr.at[other], gg_s.at[n], gg_r.at[n], dev).wait_send()
    plane.done()
    outs.done()
    line.done(ex_out)


def run_ffn(cap, ffn, resid, cot_all, meta, win, wdn, parts):
    tok, width = ffn.shape
    ff = wdn.shape[2]
    planes = cot_all.shape[0]
    ctx = win.shape[0]
    rows = planes * cap
    piece = width // (ctx * parts)
    vm, anyspace = pl.BlockSpec(memory_space=pltpu.VMEM), pl.BlockSpec(memory_space=pl.ANY)
    shape = jax.ShapeDtypeStruct
    dma = pltpu.SemaphoreType.DMA
    return pl.pallas_call(
        functools.partial(ffn_kernel, cap),
        out_shape=(
            shape((tok, width), BF16),
            shape((tok, width), F32),
            shape((planes, tok), F32),
            shape((width, 2 * ff), BF16),
            shape((ctx, piece, ff), BF16),
        ),
        in_specs=[vm, vm, anyspace, vm, anyspace, anyspace],
        out_specs=(vm, vm, vm, anyspace, vm),
        scratch_shapes=[
            pltpu.VMEM((planes, tok, width), BF16),
            pltpu.VMEM((planes, 8, tok), F32),
            pltpu.VMEM((planes, tok, width), BF16),
            pltpu.VMEM((width, 2 * ff), BF16),
            pltpu.VMEM((width, ff), BF16),
            pltpu.VMEM((rows, width), BF16),
            pltpu.VMEM((rows, width), BF16),
            pltpu.VMEM((rows, ff), BF16),
            pltpu.VMEM((rows, 2 * ff), BF16),
            pltpu.VMEM((4 * cap, width), BF16),
            pltpu.VMEM((planes, 8, tok), F32),
            pltpu.VMEM((planes, 8, tok), F32),
            pltpu.VMEM((2 * ff, width), BF16),
            pltpu.VMEM((ctx, parts, piece, ff), BF16),
            pltpu.VMEM((2, width // ctx, ff), BF16),
            dma((3,)),
            dma((GATHER_COPIES,)),
            dma((GATHER_COPIES,)),
            dma((planes - 1,)),
            dma((planes - 1,)),
            dma((planes - 1,)),
            dma((planes - 1,)),
            dma((10,)),
            dma((10,)),
        ]
        + plane_scratch(tok, width)
        + expert_scratch(ctx, parts, piece, ff),
        compiler_params=pltpu.CompilerParams(
            collective_id=1, has_side_effects=True, vmem_limit_bytes=63 * 2**20
        ),
        cost_estimate=pl.CostEstimate(flops=25 * 10**9, bytes_accessed=50 * 10**6, transcendentals=10**6),
    )(ffn, resid, cot_all, meta, win, wdn)


def back_kernel(
    span,
    meta,
    gg,
    lse,
    trig,
    kv,
    queries,
    attended,
    normed,
    router_t,
    gain_two,
    gain_one,
    resid_h,
    cot_h,
    pg_h,
    ffn_in_h,
    hidden_h,
    wout_h,
    wqkv_h,
    gwin_h,
    input_grad,
    qkv_out,
    proj_out,
    one_out,
    two_out,
    *scratch,
):
    wide_f, back, low, attg, mixed, weights, gwin, send, bsend, smalls, total, out_red = scratch[:12]
    mask, delta, kt, dk, dv, kvs, kvr = scratch[12:19]
    load_sem, kv_s, kv_r = scratch[19:22]
    p_zcr, p_zk, p_rx, p_ry, p_s, p_r = scratch[22:28]
    a_rx, a_ry, a_s, a_r = scratch[28:32]
    b_refs, qkv_refs, proj_refs = scratch[32:38], scratch[38:41], scratch[41:44]
    one_refs, two_refs = scratch[44:51], scratch[51:58]
    spot = Spot()
    c, k, z, ctx = spot.c, spot.k, spot.z, spot.ctx
    tok, width = attended.shape
    cols = one_out.shape[2]
    block, piece = out_red.shape[0], proj_out.shape[0]
    heads_kv = KV_HEADS
    half_head = HEAD // 2
    n_experts = meta.shape[0]
    kv_wide = mixed.shape[1] - width
    step = 256

    def load(src, dst, i):
        copy = pltpu.make_async_copy(src, dst, load_sem.at[i])
        copy.start()
        return copy

    gwin_load = load(gwin_h, gwin, 0)
    early = [
        load(resid_h, wide_f, 1),
        load(pg_h, back, 2),
        load(cot_h, input_grad, 3),
        load(ffn_in_h, attg, 4),
    ]
    wout_load = load(wout_h, weights.at[:, pl.ds(0, width)], 5)
    greet([spot.xp, spot.yp, spot.kp, spot.yk], spot.along())
    one = ExpertLine(spot, gwin, 0, cols, *one_refs)
    two = ExpertLine(spot, gwin, cols, cols, *two_refs)
    proj_plane = plane_of(spot, p_zcr, p_zk, p_rx, p_ry, p_s, p_r)
    qkv_plane = plane_of(spot, p_zcr, p_zk, a_rx, a_ry, a_s, a_r)
    rest_plane = plane_of(spot, *b_refs)

    def shared_line(ref, refs):
        def own(d):
            return ref.at[rows_at(d * piece, piece)]

        def adder(came, d):
            came[...] = plus(came[...], own(d)[...])

        return Line(spot, own, adder, *refs)

    qkv_line, proj_line = shared_line(total, qkv_refs), shared_line(out_red, proj_refs)

    def put_shared(to, ref, came):
        to[...] = plus(ref[rows_at(z * piece, piece)], *(x[...] for x in came))

    mine, theirs = rows_at(k * block, block), rows_at((1 - k) * block, block)
    gwin_load.wait()
    one.step(1)

    for copy in early:
        copy.wait()
    gate = jnp.concatenate([meta[g, 1:2, :] for g in range(n_experts)], axis=0)
    seen = gate * gg[...]
    mix = seen - gate * jnp.sum(seen, axis=0, keepdims=True)
    mix = jnp.concatenate([mix, jnp.zeros((HEAD - n_experts, tok), F32)], axis=0)
    logit_t = mix.astype(BF16)
    r = wide_f[...]
    inv = lax.rsqrt(jnp.mean(r * r, axis=-1, keepdims=True) + NORM_EPS)
    plain = r * inv
    ffn_grad = back[...] + dot_tn(logit_t[:n_experts], router_t[...])
    gain_row = jnp.sum(ffn_grad * plain, axis=0, keepdims=True)
    scaled = ffn_grad * gain_two[...]
    grad = input_grad[...].astype(F32) + inv * (
        scaled - plain * jnp.mean(scaled * plain, axis=-1, keepdims=True)
    )
    back[...] = grad
    low[...] = grad.astype(BF16)
    lane = lax.broadcasted_iota(jnp.int32, (width, HEAD), 1)
    routed = dot_tn(attg[...], logit_t.T)
    gain_col = jnp.broadcast_to(gain_row, (HEAD, width)).T
    smalls[...] = jnp.where(lane == n_experts, gain_col, routed).astype(BF16)

    for q in (1, 2, 3, 0):
        at = lanes(spot.chips[q] * block, 2 * block)
        send[q] = dot_tn(low[:, at], attended[...]).astype(BF16)
        proj_plane.give(q, send.at[q, theirs])
    wout_load.wait()

    @pl.loop(0, width // step)
    def _(n):
        at = lanes(n * step, step)
        attg[:, at] = dot(low[...], weights[:, at]).astype(BF16)

    wqkv_load = load(wqkv_h, weights, 5)
    hidden_load = load(hidden_h, low, 1)

    def start_plane(plane):
        plane.fold(1, send[1, mine])
        plane.fold(2, send[2, mine])
        plane.near()
        plane.fold(3, send[3, mine])
        plane.across()
        plane.fold(0, send[0, mine])

    start_plane(proj_plane)

    seq = kv.shape[0]
    spans = span.shape[1]
    size = seq // spans
    per = spans // ctx
    along_q = lax.broadcasted_iota(jnp.int32, (size, tok), 1)
    q_pos = jnp.where(along_q < size, span[0, c * per] * size, (span[0, c * per + 1] - 1) * size) + along_q
    for s in range(spans):
        k_pos = span[0, s] * size + lax.broadcasted_iota(jnp.int32, (size, tok), 0)
        mask[s * size : (s + 1) * size, :] = jnp.where(k_pos <= q_pos, 0.0, MASKED)

    lane_h = lax.broadcasted_iota(jnp.int32, (tok, HEAD), 1)
    deltas = jnp.zeros((tok, HEAD), F32)
    for h in range(HEADS):
        at = slice(h * HEAD, (h + 1) * HEAD)
        term = jnp.sum(attg[:, at].astype(F32) * attended[:, at].astype(F32), axis=-1, keepdims=True)
        deltas = jnp.where(lane_h == h, term, deltas)
    delta[...] = deltas.T
    for g in range(heads_kv):
        kt[g] = kv[:, g * HEAD : (g + 1) * HEAD].astype(F32).T.astype(BF16)

    cosine, sine = trig[0], trig[1]

    def unrotate(w):
        return w * cosine - pltpu.roll(w, half_head, 1) * sine

    def head(g, h):
        at = lanes(h * HEAD, HEAD)
        k_at = slice(g * HEAD, (g + 1) * HEAD)
        v_at = slice((heads_kv + g) * HEAD, (heads_kv + g + 1) * HEAD)
        q, a = queries[:, at], attg[:, at]
        soft = jnp.exp(dot_nt(kv[:, k_at], q) + mask[...] - lse[pl.ds(h, 1), :])
        prob = dot_nt(kv[:, v_at], a)
        score = (soft * (prob - delta[pl.ds(h, 1), :])).astype(BF16)
        mixed[:, at] = (unrotate(dot(kt[g], score).T) * HEAD**-0.5).astype(BF16)
        dk[...] += dot(score, q)
        dv[...] += dot(soft.astype(BF16), a)

    def heads(g, first, count):
        @pl.loop(first, first + count)
        def _(h):
            head(g, h)

    def clear():
        dk[...] = jnp.zeros(dk.shape, F32)
        dv[...] = jnp.zeros(dv.shape, F32)

    flip_c = lax.rem(c + 2, ctx)
    near_c = c + 1 - 2 * k
    across_c = lax.rem(near_c + 2, ctx)

    def kv_copy(g, src, i, dev):
        return remote(src, kvr.at[g, i], kv_s.at[g, i], kv_r.at[g, i], dev)

    def send_kv(g):
        for cc in range(ctx):
            rows = slice(cc * tok, (cc + 1) * tok)
            kvs[g, cc, :, :HEAD] = dk[rows, :].astype(BF16)
            kvs[g, cc, :, HEAD:] = dv[rows, :].astype(BF16)
        kv_copy(g, kvs.at[g, across_c], 1, spot.kp).start()
        kv_copy(g, kvs.at[g, near_c], 0, spot.kp).start()

    def pass_kv(g):
        kv_copy(g, kvs.at[g, across_c], 1, spot.kp).wait_recv()
        kvs[g, flip_c] = plus(kvs[g, flip_c], kvr[g, 1])
        kv_copy(g, kvs.at[g, flip_c], 2, spot.yp).start()

    clear()
    heads(0, 0, 2)
    one.step(2)
    heads(0, 2, 4)
    send_kv(0)
    clear()
    proj_plane.turn()
    heads(1, 6, 3)
    pass_kv(0)
    one.step(3)
    two.step(1)
    heads(1, 9, 3)
    send_kv(1)
    pass_kv(1)
    for rows, terms in proj_plane.total():
        out_red[rows, :] = summed(terms).astype(BF16)
    proj_line.step(1)
    proj_plane.done()
    for g in range(heads_kv):
        kv_copy(g, kvs.at[g, near_c], 0, spot.kp).wait_recv()
        kv_copy(g, kvs.at[g, flip_c], 2, spot.yp).wait_recv()
        own = kvs[g, c].astype(F32) + kvr[g, 0].astype(F32) + kvr[g, 2].astype(F32)
        at = width + g * HEAD
        mixed[:, at : at + HEAD] = unrotate(own[:, :HEAD]).astype(BF16)
        at = width + (heads_kv + g) * HEAD
        mixed[:, at : at + HEAD] = own[:, HEAD:].astype(BF16)

    for q in (1, 2, 3, 0):
        at = lanes(spot.chips[q] * block, 2 * block)
        send[q] = dot_tn(normed[:, at], mixed[:, :width]).astype(BF16)
        qkv_plane.give(q, send.at[q, theirs])
    start_plane(qkv_plane)
    one.final()
    proj_line.step(2)
    wqkv_load.wait()

    @pl.loop(0, width // step)
    def _(n):
        at = lanes(n * step, step)
        wide_f[:, at] = dot_nt(mixed[...], weights[at, :])

    hidden_load.wait()
    x = low[...].astype(F32)
    inv = lax.rsqrt(jnp.mean(x * x, axis=-1, keepdims=True) + NORM_EPS)
    plain = x * inv
    ng = wide_f[...]
    gain_row = jnp.sum(ng * plain, axis=0, keepdims=True)
    scaled = ng * gain_one[...]
    input_grad[...] = (
        back[...] + inv * (scaled - plain * jnp.mean(scaled * plain, axis=-1, keepdims=True))
    ).astype(BF16)
    lane = lax.broadcasted_iota(jnp.int32, (width, HEAD), 1)
    gain_col = jnp.broadcast_to(gain_row, (HEAD, width)).T
    smalls[...] = jnp.where(lane == HEAD - 1, gain_col, smalls[...].astype(F32)).astype(BF16)
    for q in (1, 2, 3, 0):
        at = lanes(spot.chips[q] * block, 2 * block)
        bsend[q, :, :kv_wide] = dot_tn(normed[:, at], mixed[:, width:]).astype(BF16)
        bsend[q, :, kv_wide:] = smalls[rows_at(spot.chips[q] * block, 2 * block), :]
        rest_plane.give(q, bsend.at[q, theirs])
    rest_plane.fold(1, bsend[1, mine])
    rest_plane.fold(2, bsend[2, mine])
    rest_plane.near()
    rest_plane.fold(3, bsend[3, mine])
    rest_plane.across()
    rest_plane.fold(0, bsend[0, mine])
    two.step(2)
    qkv_plane.turn()
    rest_plane.turn()
    proj_line.step(3)
    for rows, terms in qkv_plane.total():
        total[rows, :width] = summed(terms).astype(BF16)
    for rows, terms in rest_plane.total():
        total[rows, width:] = summed(terms).astype(BF16)
    qkv_line.step(1)
    one.done(one_out)
    two.step(3)
    qkv_line.step(2)
    proj_line.final(lambda *came: put_shared(proj_out, out_red, came))
    qkv_line.step(3)
    two.final()
    proj_line.done()
    qkv_plane.done()
    rest_plane.done()
    for g in range(heads_kv):
        kv_copy(g, kvs.at[g, near_c], 0, spot.kp).wait_send()
        kv_copy(g, kvs.at[g, across_c], 1, spot.kp).wait_send()
        kv_copy(g, kvs.at[g, flip_c], 2, spot.yp).wait_send()
    qkv_line.final(lambda *came: put_shared(qkv_out, total, came))
    qkv_line.done()
    two.done(two_out)


def run_back(
    span, meta, gg, lse, trig, kv, queries, attended, normed, router_t, gain_two, gain_one,
    resid, cot, pg, ffn_in, hidden, wout, wqkv, gwin,
):
    tok, width = attended.shape
    seq, kv_cols = kv.shape
    planes = meta.shape[0]
    ctx, parts, rows, wide = gwin.shape
    cols = wide // 2
    block = width // planes
    piece = block // parts
    rest = kv_cols + HEAD
    vm, anyspace = pl.BlockSpec(memory_space=pltpu.VMEM), pl.BlockSpec(memory_space=pl.ANY)
    sm = pl.BlockSpec(memory_space=pltpu.SMEM)
    shape = jax.ShapeDtypeStruct
    dma = pltpu.SemaphoreType.DMA
    return pl.pallas_call(
        back_kernel,
        out_shape=(
            shape((tok, width), BF16),
            shape((piece, width + rest), BF16),
            shape((piece, width), BF16),
            shape((ctx, rows, cols), BF16),
            shape((ctx, rows, cols), BF16),
        ),
        in_specs=[sm] + [vm] * 11 + [anyspace] * 8,
        out_specs=(vm,) * 5,
        scratch_shapes=[
            pltpu.VMEM((tok, width), F32),
            pltpu.VMEM((tok, width), F32),
            pltpu.VMEM((tok, width), BF16),
            pltpu.VMEM((tok, width), BF16),
            pltpu.VMEM((tok, width + kv_cols), BF16),
            pltpu.VMEM(wqkv.shape, BF16),
            pltpu.VMEM(gwin.shape, BF16),
            pltpu.VMEM((4, 2 * block, width), BF16),
            pltpu.VMEM((4, 2 * block, rest), BF16),
            pltpu.VMEM((width, HEAD), BF16),
            pltpu.VMEM((block, width + rest), BF16),
            pltpu.VMEM((block, width), BF16),
            pltpu.VMEM((seq, tok), F32),
            pltpu.VMEM((HEAD, tok), F32),
            pltpu.VMEM((KV_HEADS, HEAD, seq), BF16),
            pltpu.VMEM((seq, HEAD), F32),
            pltpu.VMEM((seq, HEAD), F32),
            pltpu.VMEM((KV_HEADS, ctx, tok, 2 * HEAD), BF16),
            pltpu.VMEM((KV_HEADS, 3, tok, 2 * HEAD), BF16),
            dma((6,)),
            dma((KV_HEADS, 3)),
            dma((KV_HEADS, 3)),
        ]
        + plane_scratch(block, width)
        + plane_scratch(block, width)[2:]
        + plane_scratch(block, rest)
        + line_scratch(parts, (piece, width + rest))
        + line_scratch(parts, (piece, width))
        + expert_scratch(ctx, parts, rows, cols)
        + expert_scratch(ctx, parts, rows, cols),
        compiler_params=pltpu.CompilerParams(
            collective_id=2, has_side_effects=True, vmem_limit_bytes=63 * 2**20
        ),
        cost_estimate=pl.CostEstimate(flops=12 * 10**9, bytes_accessed=60 * 10**6, transcendentals=4 * 10**6),
    )(
        span, meta, gg, lse, trig, kv, queries, attended, normed, router_t, gain_two, gain_one,
        resid, cot, pg, ffn_in, hidden, wout, wqkv, gwin,
    )


def finish_kernel(
    n_experts, output_low, input_low, qkv_low, proj_low, one, two, down_low, output, input_grad, gains, qkv, proj, router, inner, down
):
    output[...] = output_low[...]
    input_grad[...] = input_low[...]
    wide = qkv.shape[1]
    qkv[...] = qkv_low[:, :wide].astype(F32)
    proj[...] = proj_low[...].astype(F32)
    ff = one.shape[2]
    inner[:, :, :ff] = one[...].astype(F32)
    inner[:, :, ff:] = two[...].astype(F32)
    down[...] = down_low[...].astype(F32)
    small = qkv_low[:, wide:].astype(F32)
    router[...] = small[:, :n_experts]
    piece = small.shape[0]
    same = lax.broadcasted_iota(jnp.int32, (piece, piece), 0) == lax.broadcasted_iota(
        jnp.int32, (piece, piece), 1
    )
    for row, col in ((0, HEAD - 1), (1, n_experts)):
        gains[row : row + 1, :] = jnp.sum(jnp.where(same, small[:, col : col + 1], 0.0), axis=0, keepdims=True)


def run_finish(n_experts, output, input_grad, qkv, proj, one, two, down):
    piece, width = proj.shape
    ctx, rows, ff = one.shape
    shape = jax.ShapeDtypeStruct
    vm = pl.BlockSpec(memory_space=pltpu.VMEM)
    return pl.pallas_call(
        functools.partial(finish_kernel, n_experts),
        out_shape=(
            shape(output.shape, BF16),
            shape(input_grad.shape, BF16),
            shape((2, piece), F32),
            shape((piece, qkv.shape[1] - HEAD), F32),
            shape((piece, width), F32),
            shape((piece, n_experts), F32),
            shape((ctx, rows, 2 * ff), F32),
            shape((ctx, rows, ff), F32),
        ),
        in_specs=[vm] * 7,
        out_specs=(vm,) * 8,
        compiler_params=pltpu.CompilerParams(vmem_limit_bytes=40 * 2**20),
    )(output, input_grad, qkv, proj, one, two, down)


def local(
    hidden_in,
    span_order,
    expert_ids,
    priority,
    gain_attn,
    qkv_weight,
    out_weight,
    gain_ffn,
    router,
    in_weight,
    down_weight,
    cotangent,
):
    _, tok_rows, width = hidden_in.shape
    ctx, parts = lax.axis_size("context"), lax.axis_size("dp")
    planes = ctx * lax.axis_size("expert")
    n_experts = router.shape[1]
    top_k = expert_ids.shape[2]
    capacity = (9 * tok_rows * top_k + 8 * n_experts - 1) // (8 * n_experts)
    ff = down_weight.shape[2]
    half_freqs = ROPE_BASE ** (np.arange(HEAD // 2) * (-2.0 / HEAD))
    freqs = np.concatenate([half_freqs, half_freqs])[None].astype(np.float32)
    router_t = router.T
    hidden, cot = hidden_in[0], cotangent[0]
    normed, queries, kv, lse, attended, resid, ffn_in, trig, meta, cot_all = run_front(
        capacity,
        span_order,
        hidden,
        cot,
        gain_attn,
        freqs,
        gain_ffn,
        router_t,
        expert_ids[0].T,
        priority[0].T,
        qkv_weight,
        out_weight,
        ctx,
        planes,
    )
    output, pair_sum, gate_grad, gwin, down = run_ffn(
        capacity, ffn_in, resid, cot_all, meta, in_weight, down_weight, parts
    )
    gwin = gwin.reshape(ctx, parts, width // (ctx * parts), 2 * ff)
    input_grad, qkv_sum, proj_sum, in_one, in_two = run_back(
        span_order,
        meta,
        gate_grad,
        lse,
        trig,
        kv,
        queries,
        attended,
        normed,
        router_t,
        gain_ffn,
        gain_attn,
        resid,
        cot,
        pair_sum,
        ffn_in,
        hidden,
        out_weight,
        qkv_weight,
        gwin,
    )
    output, input_grad, gains, qkv_grad, proj_grad, router_grad, inner_grad, down_grad = run_finish(
        n_experts, output, input_grad, qkv_sum, proj_sum, in_one, in_two, down
    )
    return (
        output[None],
        input_grad[None],
        gains[0],
        qkv_grad,
        proj_grad,
        gains[1],
        router_grad,
        inner_grad,
        down_grad,
    )


def general(
    hidden_in,
    span_order,
    expert_ids,
    priority,
    gain_attn,
    qkv_weight,
    out_weight,
    gain_ffn,
    router,
    in_weight,
    down_weight,
    cotangent,
):
    tok_rows = hidden_in.shape[1]
    width = hidden_in.shape[2]
    contexts = lax.axis_size("context")
    span_len = tok_rows // 2
    seq_len = tok_rows * contexts
    group = HEADS // KV_HEADS
    q_cols = HEADS * HEAD
    kv_cols = KV_HEADS * HEAD
    scale = HEAD ** (-0.5)
    local_experts = in_weight.shape[0]
    n_experts = local_experts * lax.axis_size("expert")
    top_k = expert_ids.shape[2]
    capacity = (9 * tok_rows * top_k + 8 * n_experts - 1) // (8 * n_experts)
    ff_width = down_weight.shape[2]
    seq_spans = span_order[0]
    stored = jnp.arange(seq_len) // span_len
    all_pos = (seq_spans[stored] * span_len + jnp.arange(seq_len) % span_len).astype(jnp.float32)
    my_pos = lax.dynamic_slice_in_dim(all_pos, lax.axis_index("context") * tok_rows, tok_rows)
    cosine, sine = rope_tables(my_pos, HEAD)
    inputs = hidden_in[0].astype(jnp.float32)
    inv_one = lax.rsqrt(jnp.mean(inputs * inputs, axis=-1, keepdims=True) + NORM_EPS)
    plain_one = inputs * inv_one
    normed = (plain_one * gain_attn).astype(jnp.bfloat16)
    mixed = jnp.dot(normed, qkv_weight, preferred_element_type=jnp.float32)
    queries = (
        rotate(mixed[:, :q_cols].reshape(tok_rows, HEADS, HEAD), cosine, sine) * scale
    ).astype(jnp.bfloat16)
    keys = rotate(
        mixed[:, q_cols : q_cols + kv_cols].reshape(tok_rows, KV_HEADS, HEAD), cosine, sine
    ).astype(jnp.bfloat16)
    values = mixed[:, q_cols + kv_cols :].reshape(tok_rows, KV_HEADS, HEAD).astype(jnp.bfloat16)
    grouped = queries.reshape(tok_rows, KV_HEADS, group, HEAD)

    def key_scores(key_piece):
        scores = jnp.einsum(
            "qkgd,skd->kgqs", grouped, key_piece, preferred_element_type=jnp.float32
        )
        visible = all_pos[None, None, None, :] <= my_pos[None, None, :, None]
        return (jnp.where(visible, scores, MASKED), visible)

    running = jnp.full((KV_HEADS, group, tok_rows), MASKED, jnp.float32)
    key_piece = lax.all_gather(keys, "context", axis=0, tiled=True)
    value_piece = lax.all_gather(values, "context", axis=0, tiled=True)
    scores, visible = key_scores(key_piece)
    newest = jnp.maximum(running, jnp.max(scores, axis=-1))
    weights = jnp.where(visible, jnp.exp(scores - newest[..., None]), 0.0)
    totals = jnp.sum(weights, axis=-1)
    accum = jnp.einsum(
        "kgqs,skd->kgqd",
        weights.astype(jnp.bfloat16),
        value_piece,
        preferred_element_type=jnp.float32,
    )
    running, totals, accum = (newest, totals, accum)
    log_total = running + jnp.log(totals)
    attended = (
        (accum / totals[..., None])
        .transpose(2, 0, 1, 3)
        .reshape(tok_rows, q_cols)
        .astype(jnp.bfloat16)
    )
    resid = inputs + jnp.einsum(
        "rh,dh->rd", attended, out_weight, preferred_element_type=jnp.float32
    )
    inv_two = lax.rsqrt(jnp.mean(resid * resid, axis=-1, keepdims=True) + NORM_EPS)
    plain_two = resid * inv_two
    ffn_in = (plain_two * gain_ffn).astype(jnp.bfloat16)
    logits = jnp.dot(ffn_in, router, preferred_element_type=jnp.float32)
    token_ids = expert_ids[0]
    gates = softmax_last(jnp.take_along_axis(logits, token_ids, axis=1))
    slots = route(token_ids, priority[0], n_experts, capacity)
    pair_rows = jnp.repeat(ffn_in, top_k, axis=0)
    send_rows = (
        jnp.zeros((n_experts * capacity, width), jnp.bfloat16).at[slots].set(pair_rows, mode="drop")
    )
    received = lax.all_to_all(
        send_rows.reshape(n_experts, capacity, width),
        "expert",
        split_axis=0,
        concat_axis=1,
        tiled=True,
    )
    inner = jnp.einsum("erd,edf->erf", received, in_weight, preferred_element_type=jnp.float32)
    gate_part = inner[..., :ff_width]
    up_part = inner[..., ff_width:]
    sigma = 1.0 / (1.0 + jnp.exp(-gate_part))
    activated = gate_part * sigma
    hidden = (activated * up_part).astype(jnp.bfloat16)
    expert_out = jnp.einsum(
        "erf,edf->erd", hidden, down_weight, preferred_element_type=jnp.float32
    ).astype(jnp.bfloat16)
    returned = lax.all_to_all(
        expert_out, "expert", split_axis=1, concat_axis=0, tiled=True
    ).reshape(n_experts * capacity, width)
    padded = jnp.concatenate([returned, jnp.zeros((1, width), jnp.bfloat16)], axis=0)
    picked = padded[slots].reshape(tok_rows, top_k, width)
    output = (resid + jnp.sum(gates[:, :, None] * picked, axis=1)).astype(jnp.bfloat16)
    cot_low = cotangent[0]
    cot_full = cot_low.astype(jnp.float32)
    gate_grad = jnp.einsum("rkd,rd->rk", picked, cot_low, preferred_element_type=jnp.float32)
    ret_grad = (
        (gates[:, :, None] * cot_full[:, None, :])
        .astype(jnp.bfloat16)
        .reshape(tok_rows * top_k, width)
    )
    send_grad = (
        jnp.zeros((n_experts * capacity, width), jnp.bfloat16).at[slots].set(ret_grad, mode="drop")
    )
    received_grad = lax.all_to_all(
        send_grad.reshape(n_experts, capacity, width),
        "expert",
        split_axis=0,
        concat_axis=1,
        tiled=True,
    )
    hid_grad = jnp.einsum(
        "erd,edf->erf", received_grad, down_weight, preferred_element_type=jnp.float32
    )
    slope = sigma * (1.0 + gate_part * (1.0 - sigma))
    inner_grad = jnp.concatenate(
        [hid_grad * up_part * slope, hid_grad * activated], axis=-1
    ).astype(jnp.bfloat16)
    row_grad = jnp.einsum(
        "erf,edf->erd", inner_grad, in_weight, preferred_element_type=jnp.float32
    ).astype(jnp.bfloat16)
    part_rows = received
    expert_in = (
        lax.psum_scatter(
            jnp.einsum(
                "erd,erf->def", part_rows, inner_grad, preferred_element_type=jnp.float32
            ).astype(jnp.bfloat16),
            ("context", "dp"),
            scatter_dimension=0,
            tiled=True,
        )
        .astype(jnp.float32)
        .transpose(1, 0, 2)
    )
    part_rows = received_grad
    expert_down = (
        lax.psum_scatter(
            jnp.einsum(
                "erd,erf->def", part_rows, hidden, preferred_element_type=jnp.float32
            ).astype(jnp.bfloat16),
            ("context", "dp"),
            scatter_dimension=0,
            tiled=True,
        )
        .astype(jnp.float32)
        .transpose(1, 0, 2)
    )
    back_rows = lax.all_to_all(row_grad, "expert", split_axis=1, concat_axis=0, tiled=True).reshape(
        n_experts * capacity, width
    )
    back_padded = jnp.concatenate([back_rows, jnp.zeros((1, width), jnp.bfloat16)], axis=0)
    pair_grad = back_padded[slots].reshape(tok_rows, top_k, width)
    mix_grad = gates * (gate_grad - jnp.sum(gates * gate_grad, axis=-1, keepdims=True))
    matches = token_ids[:, :, None] == jnp.arange(n_experts)[None, None, :]
    logit_grad = jnp.sum(jnp.where(matches, mix_grad[:, :, None], 0.0), axis=1).astype(jnp.bfloat16)
    router_part = jnp.einsum("rd,re->de", ffn_in, logit_grad, preferred_element_type=jnp.float32)
    ffn_grad = jnp.sum(pair_grad.astype(jnp.float32), axis=1) + jnp.einsum(
        "re,de->rd", logit_grad, router, preferred_element_type=jnp.float32
    )
    gain_ffn_part = jnp.sum(ffn_grad * plain_two, axis=0)
    scaled_two = ffn_grad * gain_ffn
    resid_grad = cot_full + inv_two * (
        scaled_two - plain_two * jnp.mean(scaled_two * plain_two, axis=-1, keepdims=True)
    )
    resid_low = resid_grad.astype(jnp.bfloat16)
    out_part = jnp.einsum("rd,rh->dh", resid_low, attended, preferred_element_type=jnp.float32)
    att_grad = jnp.einsum(
        "rd,dh->rh", resid_low, out_weight, preferred_element_type=jnp.float32
    ).astype(jnp.bfloat16)
    att_heads = att_grad.reshape(tok_rows, KV_HEADS, group, HEAD)
    row_delta = jnp.sum(
        att_heads.astype(jnp.float32)
        * attended.reshape(tok_rows, KV_HEADS, group, HEAD).astype(jnp.float32),
        axis=-1,
    ).transpose(1, 2, 0)
    key_piece = lax.all_gather(keys, "context", axis=0, tiled=True)
    value_piece = lax.all_gather(values, "context", axis=0, tiled=True)
    scores, visible = key_scores(key_piece)
    soft = jnp.exp(scores - log_total[..., None])
    prob_grad = jnp.einsum(
        "qkgd,skd->kgqs", att_heads, value_piece, preferred_element_type=jnp.float32
    )
    score_grad = (soft * (prob_grad - row_delta[..., None])).astype(jnp.bfloat16)
    query_acc = jnp.einsum(
        "kgqs,skd->kgqd", score_grad, key_piece, preferred_element_type=jnp.float32
    )
    key_part = jnp.einsum("kgqs,qkgd->skd", score_grad, grouped, preferred_element_type=jnp.float32)
    value_part = jnp.einsum(
        "kgqs,qkgd->skd", soft.astype(jnp.bfloat16), att_heads, preferred_element_type=jnp.float32
    )
    pair_acc = jnp.stack([key_part, value_part], axis=1)
    query_acc, pair_acc = (query_acc, pair_acc)
    own_pairs = lax.psum_scatter(
        pair_acc.astype(jnp.bfloat16), "context", scatter_dimension=0, tiled=True
    ).astype(jnp.float32)
    query_grad = (
        unrotate(query_acc.transpose(2, 0, 1, 3).reshape(tok_rows, HEADS, HEAD), cosine, sine)
        * scale
    )
    key_grad = unrotate(own_pairs[:, 0], cosine, sine)
    mixed_grad = jnp.concatenate(
        [
            query_grad.reshape(tok_rows, q_cols),
            key_grad.reshape(tok_rows, kv_cols),
            own_pairs[:, 1].reshape(tok_rows, kv_cols),
        ],
        axis=-1,
    ).astype(jnp.bfloat16)
    qkv_part = jnp.einsum("rd,rc->dc", normed, mixed_grad, preferred_element_type=jnp.float32)
    norm_grad = jnp.einsum("rc,dc->rd", mixed_grad, qkv_weight, preferred_element_type=jnp.float32)
    gain_attn_part = jnp.sum(norm_grad * plain_one, axis=0)
    scaled_one = norm_grad * gain_attn
    input_grad = (
        resid_grad
        + inv_one
        * (scaled_one - plain_one * jnp.mean(scaled_one * plain_one, axis=-1, keepdims=True))
    ).astype(jnp.bfloat16)
    gain_attn_grad, qkv_grad, out_proj_grad, gain_ffn_grad, router_grad = (
        lax.psum_scatter(
            gain_attn_part, ("expert", "context", "dp"), scatter_dimension=0, tiled=True
        ),
        lax.psum_scatter(qkv_part, ("expert", "context", "dp"), scatter_dimension=0, tiled=True),
        lax.psum_scatter(out_part, ("expert", "context", "dp"), scatter_dimension=0, tiled=True),
        lax.psum_scatter(
            gain_ffn_part, ("expert", "context", "dp"), scatter_dimension=0, tiled=True
        ),
        lax.psum_scatter(router_part, ("expert", "context", "dp"), scatter_dimension=0, tiled=True),
    )
    return (
        output[None],
        input_grad[None],
        gain_attn_grad,
        qkv_grad,
        out_proj_grad,
        gain_ffn_grad,
        router_grad,
        expert_in,
        expert_down,
    )


def solution(mesh):
    in_specs = (
        P(("expert", "dp"), "context", None),
        P(("expert", "dp"), None),
        P(("expert", "dp"), "context", None),
        P(("expert", "dp"), "context", None),
        P(),
        P(),
        P(),
        P(),
        P(),
        P("expert", None, None),
        P("expert", None, None),
        P(("expert", "dp"), "context", None),
    )
    out_specs = (
        P(("expert", "dp"), "context", None),
        P(("expert", "dp"), "context", None),
        P(("expert", "context", "dp")),
        P(("expert", "context", "dp"), None),
        P(("expert", "context", "dp"), None),
        P(("expert", "context", "dp")),
        P(("expert", "context", "dp"), None),
        P("expert", ("context", "dp"), None),
        P("expert", ("context", "dp"), None),
    )
    tuned = dict(mesh.shape) == {"expert": 2, "context": 4, "dp": 4}
    body = local if tuned else general
    return jax.shard_map(body, mesh=mesh, in_specs=in_specs, out_specs=out_specs, check_vma=False)
```

```python
import functools

import jax
import jax.numpy as jnp
import numpy as np
from jax import lax
from jax.experimental import pallas as pl
from jax.experimental.pallas import tpu as pltpu
from jax.sharding import PartitionSpec as P

HEADS = 12
KV_HEADS = 2
HEAD = 128


ROPE_BASE = 1000000.0
NORM_EPS = 1e-06
MASKED = -1e30


def rope_tables(positions, head_size):
    half_size = head_size // 2
    freqs = ROPE_BASE ** (jnp.arange(half_size).astype(jnp.float32) * (-2.0 / head_size))
    angles = positions[:, None] * freqs[None, :]
    return (jnp.cos(angles)[:, None, :], jnp.sin(angles)[:, None, :])


def rotate(values, cosine, sine):
    half_size = values.shape[-1] // 2
    first = values[..., :half_size]
    second = values[..., half_size:]
    return jnp.concatenate(
        [first * cosine - second * sine, second * cosine + first * sine], axis=-1
    )


def unrotate(values, cosine, sine):
    half_size = values.shape[-1] // 2
    first = values[..., :half_size]
    second = values[..., half_size:]
    return jnp.concatenate(
        [first * cosine + second * sine, second * cosine - first * sine], axis=-1
    )


def softmax_last(scores):
    shifted = jnp.exp(scores - jnp.max(scores, axis=-1, keepdims=True))
    return shifted / jnp.sum(shifted, axis=-1, keepdims=True)


def route(block_ids, block_order, n_experts, capacity):
    flat_ids = block_ids.reshape(-1)
    flat_order = block_order.reshape(-1)
    choose = (flat_ids[:, None] == jnp.arange(n_experts)[None, :]).astype(jnp.int32)
    ordered = jnp.zeros_like(choose).at[flat_order].set(choose)
    earlier = jnp.cumsum(ordered, axis=0, dtype=jnp.int32) - ordered
    ranks = jnp.sum(earlier[flat_order] * choose, axis=1)
    return jnp.where(ranks < capacity, flat_ids * capacity + ranks, n_experts * capacity)


MESH = pl.DeviceIdType.MESH
F32 = jnp.float32
BF16 = jnp.bfloat16
BACK_LOW = 96
OUT_LOW = 128
FRONT_LOW = 96


def dot(a, b):
    return jnp.dot(a, b, preferred_element_type=F32)


def dot_nt(a, b):
    return lax.dot_general(a, b, (((1,), (1,)), ((), ())), preferred_element_type=F32)


def dot_tn(a, b):
    return lax.dot_general(a, b, (((0,), (0,)), ((), ())), preferred_element_type=F32)


def plus(a, *more):
    total = a.astype(F32)
    for b in more:
        total = total + b.astype(F32)
    return total.astype(BF16)


def lanes(at, size):
    return pl.ds(pl.multiple_of(at, 128), size)


def rows_at(at, size):
    return pl.ds(pl.multiple_of(at, 16), size)


def remote(src, dst, s, r, dev):
    return pltpu.make_async_remote_copy(
        src_ref=src, dst_ref=dst, send_sem=s, recv_sem=r, device_id=dev, device_id_type=MESH
    )


class Spot:
    def __init__(self):
        e, c, z = lax.axis_index("expert"), lax.axis_index("context"), lax.axis_index("dp")
        self.ctx = lax.axis_size("context")
        self.parts = lax.axis_size("dp")
        self.planes = self.ctx * lax.axis_size("expert")
        y, k = lax.div(c, 2), lax.rem(c, 2)
        self.e, self.c, self.z, self.k = e, c, z, k
        self.me = e * self.ctx + c
        self.xp, self.yp = (1 - e, c, z), (e, (1 - y) * 2 + k, z)
        self.kp, self.yk = (e, y * 2 + 1 - k, z), (e, (1 - y) * 2 + 1 - k, z)
        self.chips = [
            eq * self.ctx + yq * 2 for eq, yq in ((e, y), (1 - e, y), (e, 1 - y), (1 - e, 1 - y))
        ]

    def others(self):
        found = []
        for step in range(1, self.planes):
            other = lax.rem(self.me + step, self.planes)
            found.append((other, (lax.div(other, self.ctx), lax.rem(other, self.ctx), self.z)))
        return found

    def along(self):
        e, c, z = self.e, self.c, self.z
        return [(z < self.parts - 1, (e, c, z + 1)), (z > 0, (e, c, z - 1))]


def greet(peers, extra=()):
    barrier = pltpu.get_barrier_semaphore()
    for peer in peers:
        pl.semaphore_signal(barrier, inc=1, device_id=peer, device_id_type=MESH)
    for there, peer in extra:

        @pl.when(there)
        def _():
            pl.semaphore_signal(barrier, inc=1, device_id=peer, device_id_type=MESH)

    count = len(peers)
    for there, _ in extra:
        count = count + there.astype(jnp.int32)
    pl.semaphore_wait(barrier, count)


class Plane:
    def __init__(self, spot, zcr, zk, rx, ry, s, r, zcr_there=None, low=None):
        self.zcr_there = zcr_there or zcr
        self.spot, self.zcr, self.zk, self.rx, self.ry, self.s, self.r = spot, zcr, zk, rx, ry, s, r
        low = low or zk[0].shape[0] // 2
        self.lo, self.hi = pl.ds(0, low), pl.ds(low, zk[0].shape[0] - low)
        self.sent, self.gives = [], []

    def push(self, src, dst, i, dev):
        copy = remote(src, dst, self.s.at[i], self.r.at[i], dev)
        copy.start()
        self.sent.append(copy)

    def arrive(self, dst, i):
        remote(dst, dst, self.s.at[i], self.r.at[i], self.spot.kp).wait_recv()

    def given(self):
        for copy in self.gives:
            copy.wait_send()
        self.gives = []

    def give(self, q, src):
        self.gives.append(remote(src, self.zcr_there[q], self.s.at[q], self.r.at[q], self.spot.kp))
        self.gives[-1].start()

    def fold(self, q, own=None):
        self.arrive(self.zcr[q], q)
        self.zk[q][...] = plus(self.zk[q][...] if own is None else own, self.zcr[q][...])

    def near(self):
        self.push(self.zk[1].at[self.lo], self.rx[1], 5, self.spot.xp)
        self.push(self.zk[2].at[self.hi], self.ry[1], 8, self.spot.yp)

    def across(self):
        self.push(self.zk[3].at[self.lo], self.rx[0], 4, self.spot.xp)
        self.push(self.zk[3].at[self.hi], self.ry[0], 7, self.spot.yp)

    def turn(self):
        lo, hi = self.lo, self.hi
        self.arrive(self.rx[0], 4)
        self.zk[2][lo] = plus(self.zk[2][lo], self.rx[0][...])
        self.push(self.zk[2].at[lo], self.ry[2], 9, self.spot.yp)
        self.arrive(self.ry[0], 7)
        self.zk[1][hi] = plus(self.zk[1][hi], self.ry[0][...])
        self.push(self.zk[1].at[hi], self.rx[2], 6, self.spot.xp)

    def total(self):
        self.arrive(self.rx[1], 5)
        self.arrive(self.ry[1], 8)
        self.arrive(self.rx[2], 6)
        self.arrive(self.ry[2], 9)
        return (
            (self.lo, (self.zk[0][self.lo], self.rx[1][...], self.ry[2][...])),
            (self.hi, (self.zk[0][self.hi], self.rx[2][...], self.ry[1][...])),
        )

    def done(self):
        self.given()
        for copy in self.sent:
            copy.wait_send()


def plane_of(spot, zcr, zk, rx, ry, s, r, low=None):
    four, block = range(4), zk.shape[1]
    lo, hi = pl.ds(0, low or block // 2), pl.ds(0, block - (low or block // 2))
    return Plane(
        spot,
        [zcr.at[q] for q in four],
        [zk.at[q] for q in four],
        [rx.at[0, lo], rx.at[1, lo], rx.at[2, hi]],
        [ry.at[0, hi], ry.at[1, hi], ry.at[2, lo]],
        s,
        r,
        low=low,
    )


def plane_scratch(block, wide, low=None):
    most = max(low or block // 2, block - (low or block // 2))
    return [
        pltpu.VMEM((4, block, wide), BF16),
        pltpu.VMEM((4, block, wide), BF16),
        pltpu.VMEM((3, most, wide), BF16),
        pltpu.VMEM((3, most, wide), BF16),
        pltpu.SemaphoreType.DMA((10,)),
        pltpu.SemaphoreType.DMA((10,)),
    ]


def summed(terms):
    total = terms[0].astype(F32)
    for term in terms[1:]:
        total = total + term.astype(F32)
    return total


class Line:
    def __init__(self, spot, own, adder, buf, s, r):
        z, last = spot.z, spot.parts - 1
        e, c = spot.e, spot.c
        self.own, self.adder, self.buf, self.s, self.r = own, adder, buf, s, r
        self.z, self.last, self.parts = z, last, spot.parts
        self.ways = [(z, (e, c, z + 1), lambda d: d), (last - z, (e, c, z - 1), lambda d: last - d)]

    def step(self, turn):
        for way, (i, dev, part) in enumerate(self.ways):
            to, s, r = self.buf.at[way, turn - 1], self.s.at[way, turn - 1], self.r.at[way, turn - 1]

            @pl.when(i == 0)
            def _():
                remote(self.own(part(self.parts - turn)), to, s, r, dev).start()

            if turn >= 2:
                came, s_came, r_came = (x.at[way, turn - 2] for x in (self.buf, self.s, self.r))

                @pl.when((i >= 1) & (i <= turn - 1) & (i < self.last))
                def _():
                    remote(came, came, s_came, r_came, dev).wait_recv()
                    self.adder(came, part(self.parts - turn + i))
                    remote(came, to, s, r, dev).start()

    def final(self, put):
        last, z = self.last, self.z
        for way, (i, dev, _) in enumerate(self.ways):
            came = self.buf.at[way, last - 1]

            @pl.when(i >= 1)
            def _():
                remote(came, came, self.s.at[way, last - 1], self.r.at[way, last - 1], dev).wait_recv()

        up, down = self.buf.at[0, last - 1], self.buf.at[1, last - 1]
        pl.when(z == 0)(lambda: put(down))
        pl.when(z == last)(lambda: put(up))
        pl.when((z > 0) & (z < last))(lambda: put(up, down))

    def done(self):
        for way, (i, dev, _) in enumerate(self.ways):
            for turn in range(1, self.parts):
                came = self.buf.at[way, turn - 1]

                @pl.when((i <= turn - 1) & (i < self.last))
                def _():
                    remote(came, came, self.s.at[way, turn - 1], self.r.at[way, turn - 1], dev).wait_send()


def line_scratch(parts, piece):
    return [
        pltpu.VMEM((2, parts - 1) + piece, BF16),
        pltpu.SemaphoreType.DMA((2, parts - 1)),
        pltpu.SemaphoreType.DMA((2, parts - 1)),
    ]


class ExpertLine:
    def __init__(self, spot, ref, at, cols, buf, s, r, fin, spread, a_s, a_r):
        self.spot, self.ref, self.at, self.cols = spot, ref, at, cols
        self.fin, self.spread, self.a_s, self.a_r = fin, spread, a_s, a_r
        self.line = Line(spot, self.own, self.adder, buf, s, r)
        self.step = self.line.step

    def own(self, d):
        return self.ref.at[:, d, :, pl.ds(self.at, self.cols)]

    def piece(self, cc, d):
        return self.ref[cc, d, :, self.at : self.at + self.cols]

    def adder(self, came, d):
        for cc in range(self.spot.ctx):
            came[cc] = plus(came[cc], self.piece(cc, d))

    def final(self):
        spot = self.spot

        def put(*came):
            for cc in range(spot.ctx):
                self.fin[cc] = plus(self.piece(cc, spot.z), *(x[cc] for x in came))

        self.line.final(put)
        for step in range(1, spot.ctx):
            cc = lax.rem(spot.c + step, spot.ctx)
            remote(
                self.fin.at[cc],
                self.spread.at[spot.c],
                self.a_s.at[step - 1],
                self.a_r.at[step - 1],
                (spot.e, cc, spot.z),
            ).start()

    def done(self, out):
        spot = self.spot
        for step in range(1, spot.ctx):
            cc = lax.rem(spot.c + spot.ctx - step, spot.ctx)
            got = remote(
                self.spread.at[cc],
                self.spread.at[cc],
                self.a_s.at[step - 1],
                self.a_r.at[step - 1],
                (spot.e, cc, spot.z),
            )
            got.wait_recv()
            got.wait_send()
            out[cc] = self.spread[cc]
        out[spot.c] = self.fin[spot.c]
        self.line.done()


def expert_scratch(ctx, parts, rows, cols):
    return line_scratch(parts, (ctx, rows, cols)) + [
        pltpu.VMEM((ctx, rows, cols), BF16),
        pltpu.VMEM((ctx, rows, cols), BF16),
        pltpu.SemaphoreType.DMA((ctx - 1,)),
        pltpu.SemaphoreType.DMA((ctx - 1,)),
    ]


class Gather:
    def __init__(self, spot, own, buf, s, r, low=None):
        self.spot, self.own, self.buf, self.s, self.r = spot, own, buf, s, r
        low = low or own.shape[0] // 2
        self.lo, self.hi = pl.ds(0, low), pl.ds(low, own.shape[0] - low)
        self.x_me, self.y_me, self.d_me = (base + spot.k for base in spot.chips[1:])
        self.side = 1 - 2 * spot.k
        self.sent = []

    def push(self, src, dst, i, dev):
        copy = remote(src, dst, self.s.at[i], self.r.at[i], dev)
        copy.start()
        self.sent.append(copy)

    def move(self, p, rows, i, dev):
        self.push(self.buf.at[p, rows], self.buf.at[p, rows], i, dev)

    def got(self, p, rows, i):
        to = self.buf.at[p, rows]
        remote(to, to, self.s.at[i], self.r.at[i], self.spot.kp).wait_recv()

    def start(self):
        me, own, lo, hi = self.spot.me, self.own, self.lo, self.hi
        self.push(own.at[lo], self.buf.at[me, lo], 0, self.spot.xp)
        self.push(own.at[lo], self.buf.at[me, lo], 6, self.spot.kp)
        self.push(own.at[hi], self.buf.at[me, hi], 13, self.spot.kp)
        self.push(own.at[hi], self.buf.at[me, hi], 1, self.spot.xp)

    def start_y(self):
        me, own, lo, hi = self.spot.me, self.own, self.lo, self.hi
        self.push(own.at[hi], self.buf.at[me, hi], 3, self.spot.yp)
        self.push(own.at[lo], self.buf.at[me, lo], 2, self.spot.yp)

    def first(self):
        spot = self.spot
        self.got(self.x_me, self.lo, 0)
        self.move(self.x_me, self.lo, 4, spot.yp)
        self.move(self.x_me, self.lo, 7, spot.kp)
        self.got(self.y_me, self.hi, 3)
        self.move(self.y_me, self.hi, 5, spot.xp)
        self.move(self.y_me, self.hi, 10, spot.kp)

    def second(self):
        self.got(self.x_me, self.hi, 1)
        self.move(self.x_me, self.hi, 8, self.spot.kp)
        self.got(self.y_me, self.lo, 2)
        self.move(self.y_me, self.lo, 9, self.spot.kp)

    def third(self):
        self.got(self.d_me, self.lo, 4)
        self.move(self.d_me, self.lo, 11, self.spot.kp)
        self.got(self.d_me, self.hi, 5)
        self.move(self.d_me, self.hi, 12, self.spot.kp)

    def other_core(self, q):
        low_sem, high_sem = ((6, 13), (7, 8), (9, 10), (11, 12))[q]
        p = (self.spot.me, self.x_me, self.y_me, self.d_me)[q] + self.side
        self.got(p, self.lo, low_sem)
        self.got(p, self.hi, high_sem)

    def done(self):
        for copy in self.sent:
            copy.wait_send()


GATHER_COPIES = 14


def front_kernel(
    cap,
    span,
    hidden,
    cot,
    gain_one,
    freqs,
    gain_two,
    router_t,
    ids_t,
    turn_t,
    wqkv_h,
    wout_h,
    normed,
    queries,
    kv,
    lse,
    attended,
    resid,
    ffn_in,
    trig,
    meta,
    cot_all,
    wqkv,
    wout,
    mask,
    vt,
    load_sem,
    kv_s,
    kv_r,
    co_s,
    co_r,
):
    spot = Spot()
    c, ctx, k = spot.c, spot.ctx, spot.k
    tok, width = hidden.shape
    group = HEADS // KV_HEADS
    kv_cols = KV_HEADS * HEAD
    half_head = HEAD // 2
    seq = kv.shape[0]
    spans = span.shape[1]
    size = seq // spans
    mine = spans // ctx
    n_experts = meta.shape[0]
    loads = [
        pltpu.make_async_copy(wqkv_h.at[:, pl.ds(width, 2 * kv_cols)], wqkv.at[:, pl.ds(width, 2 * kv_cols)], load_sem.at[0]),
        pltpu.make_async_copy(wqkv_h.at[:, pl.ds(0, width)], wqkv.at[:, pl.ds(0, width)], load_sem.at[1]),
        pltpu.make_async_copy(wout_h, wout, load_sem.at[2]),
        pltpu.make_async_copy(cot, cot_all.at[spot.me], load_sem.at[3]),
    ]
    for load in loads:
        load.start()
    greet([spot.xp, spot.yp, spot.kp])
    gather = Gather(spot, cot, cot_all, co_s, co_r, low=FRONT_LOW)
    gather.start()

    x = hidden[...].astype(F32)
    inv = lax.rsqrt(jnp.mean(x * x, axis=-1, keepdims=True) + NORM_EPS)
    normed[...] = (x * inv * gain_one[...]).astype(BF16)

    along = lax.broadcasted_iota(jnp.int32, (tok, HEAD), 0)
    start_one, start_two = span[0, c * mine] * size, (span[0, c * mine + 1] - 1) * size
    place = jnp.where(along < size, start_one, start_two) + along
    angle = place.astype(F32) * freqs[...]
    cosine, sine = jnp.cos(angle), jnp.sin(angle)
    lane = lax.broadcasted_iota(jnp.int32, (tok, HEAD), 1)
    sine = jnp.where(lane < half_head, -sine, sine)
    trig[0] = cosine
    trig[1] = sine

    def rotate_in(w):
        return w * cosine + pltpu.roll(w, half_head, 1) * sine

    loads[0].wait()
    raw = dot(normed[...], wqkv[:, width:])
    own = rows_at(c * tok, tok)
    for g in range(KV_HEADS):
        at = slice(g * HEAD, (g + 1) * HEAD)
        kv[own, at] = rotate_in(raw[:, at]).astype(BF16)
    kv[own, kv_cols:] = raw[:, kv_cols:].astype(BF16)

    def kv_copy(rows, i, dev):
        return remote(kv.at[rows], kv.at[rows], kv_s.at[i], kv_r.at[i], dev)

    flip_c = lax.rem(c + 2, ctx)
    near_c = c + 1 - 2 * k
    across_c = lax.rem(near_c + 2, ctx)
    sent = [kv_copy(own, 1, spot.yp), kv_copy(own, 0, spot.kp)]
    for copy in sent:
        copy.start()
    gather.start_y()

    loads[1].wait()
    step = 256

    @pl.loop(0, width // step)
    def _(n):
        at = lanes(n * step, step)
        raw = dot(normed[...], wqkv[:, at])
        for i in range(step // HEAD):
            w = raw[:, i * HEAD : (i + 1) * HEAD]
            queries[:, lanes(n * step + i * HEAD, HEAD)] = (rotate_in(w) * HEAD**-0.5).astype(BF16)

    flip = rows_at(flip_c * tok, tok)
    kv_copy(flip, 1, spot.kp).wait_recv()
    sent.append(kv_copy(flip, 2, spot.kp))
    sent[-1].start()

    expert = lax.broadcasted_iota(jnp.int32, (n_experts, tok), 0)
    never = tok * ids_t.shape[0]
    turn = jnp.full((n_experts, tok), never, jnp.int32)
    for i in range(ids_t.shape[0]):
        turn = jnp.where(ids_t[i : i + 1, :] == expert, turn_t[i : i + 1, :], turn)
    turn_f = turn.astype(F32)
    tall = jnp.concatenate([turn_f, jnp.full((HEAD - n_experts, tok), float(never), F32)], axis=0).T
    meta[...] = jnp.zeros(meta.shape, F32)
    for g in range(n_experts):
        row = turn_f[g : g + 1, :]
        rank = jnp.sum(jnp.where(tall[:, g : g + 1] < row, 1.0, 0.0), axis=0, keepdims=True)
        meta[g, 0:1, :] = jnp.where((row < never) & (rank < cap), rank, -1.0)

    along_q = lax.broadcasted_iota(jnp.int32, (size, tok), 1)
    q_pos = jnp.where(along_q < size, start_one, start_two) + along_q
    for s in range(spans):
        k_pos = span[0, s] * size + lax.broadcasted_iota(jnp.int32, (size, tok), 0)
        mask[s * size : (s + 1) * size, :] = jnp.where(k_pos <= q_pos, 0.0, MASKED)

    near, across = rows_at(near_c * tok, tok), rows_at(across_c * tok, tok)
    kv_copy(near, 0, spot.kp).wait_recv()
    kv_copy(across, 2, spot.kp).wait_recv()
    for g in range(KV_HEADS):
        vt[g] = kv[:, kv_cols + g * HEAD : kv_cols + (g + 1) * HEAD].astype(F32).T.astype(BF16)
    lse[...] = jnp.zeros(lse.shape, F32)

    def heads(g, first, count):
        @pl.loop(first, first + count)
        def _(h):
            at = lanes(h * HEAD, HEAD)
            scores = dot_nt(kv[:, g * HEAD : (g + 1) * HEAD], queries[:, at]) + mask[...]
            top = jnp.max(scores, axis=0, keepdims=True)
            weights = jnp.exp(scores - top)
            total = jnp.sum(weights, axis=0, keepdims=True)
            lse[pl.ds(h, 1), :] = top + jnp.log(total)
            out = dot(vt[g], weights.astype(BF16)) / total
            attended[:, at] = out.T.astype(BF16)

    heads(0, 0, 3)
    gather.first()
    heads(0, 3, 3)
    heads(1, 6, 3)
    gather.second()
    heads(1, 9, 3)

    loads[2].wait()

    @pl.loop(0, width // step)
    def _(n):
        at = lanes(n * step, step)
        resid[:, at] = hidden[:, at].astype(F32) + dot_nt(attended[...], wout[at, :])

    r = resid[...]
    inv = lax.rsqrt(jnp.mean(r * r, axis=-1, keepdims=True) + NORM_EPS)
    ffn_in[...] = (r * inv * gain_two[...]).astype(BF16)
    logits = dot_nt(router_t[...], ffn_in[...])[:n_experts]
    logits = jnp.where(turn < never, logits, MASKED)
    shifted = jnp.exp(logits - jnp.max(logits, axis=0, keepdims=True))
    gates = shifted / jnp.sum(shifted, axis=0, keepdims=True)
    for g in range(n_experts):
        meta[g, 1:2, :] = gates[g : g + 1, :]
    gather.third()
    for q in range(4):
        gather.other_core(q)
    loads[3].wait()
    gather.done()
    for copy in sent:
        copy.wait_send()


def run_front(cap, span, hidden, cot, gain_one, freqs, gain_two, router_t, ids_t, turn_t, wqkv, wout, ctx, planes):
    tok, width = hidden.shape
    seq = tok * ctx
    n_experts = planes
    kv_cols = 2 * KV_HEADS * HEAD
    vm, anyspace = pl.BlockSpec(memory_space=pltpu.VMEM), pl.BlockSpec(memory_space=pl.ANY)
    sm = pl.BlockSpec(memory_space=pltpu.SMEM)
    shape = jax.ShapeDtypeStruct
    dma = pltpu.SemaphoreType.DMA
    return pl.pallas_call(
        functools.partial(front_kernel, cap),
        out_shape=(
            shape((tok, width), BF16),
            shape((tok, width), BF16),
            shape((seq, kv_cols), BF16),
            shape((16, tok), F32),
            shape((tok, width), BF16),
            shape((tok, width), F32),
            shape((tok, width), BF16),
            shape((2, tok, HEAD), F32),
            shape((n_experts, 8, tok), F32),
            shape((planes, tok, width), BF16),
        ),
        in_specs=[sm] + [vm] * 8 + [anyspace] * 2,
        out_specs=(vm,) * 9 + (anyspace,),
        scratch_shapes=[
            pltpu.VMEM(wqkv.shape, BF16),
            pltpu.VMEM(wout.shape, BF16),
            pltpu.VMEM((seq, tok), F32),
            pltpu.VMEM((KV_HEADS, HEAD, seq), BF16),
            dma((4,)),
            dma((3,)),
            dma((3,)),
            dma((GATHER_COPIES,)),
            dma((GATHER_COPIES,)),
        ],
        compiler_params=pltpu.CompilerParams(
            collective_id=4, has_side_effects=True, vmem_limit_bytes=56 * 2**20
        ),
        cost_estimate=pl.CostEstimate(flops=5 * 10**9, bytes_accessed=20 * 10**6, transcendentals=4 * 10**6),
    )(span, hidden, cot, gain_one, freqs, gain_two, router_t, ids_t, turn_t, wqkv, wout)


def ffn_kernel(cap, ffn_h, resid_h, cot_h, meta, win_h, wdn_h, output, pg_out, gg_out, gwin_h, ex_out, first_out, *scratch):
    agb, metas, cotb, win, wdn, xs, ds, hid, igs, pgs, ggs, ggr, wint, gwdn = scratch[:14]
    load_sem, ag_s, ag_r, me_s, me_r, gg_s, gg_r, out_s, out_r = scratch[14:23]
    plane_refs, line_refs, first_refs = scratch[23:29], scratch[29:36], scratch[36:]
    spot = Spot()
    c, k, me = spot.c, spot.k, spot.me
    kp = spot.kp
    tok, width = output.shape
    ff = wdn.shape[1]
    planes, ctx = spot.planes, spot.ctx
    chips = spot.chips

    loads = [
        pltpu.make_async_copy(win_h.at[c], win, load_sem.at[0]),
        pltpu.make_async_copy(wdn_h.at[c], wdn, load_sem.at[1]),
        pltpu.make_async_copy(cot_h, cotb, load_sem.at[2]),
        pltpu.make_async_copy(resid_h, pg_out, load_sem.at[3]),
    ]
    own_load = pltpu.make_async_copy(ffn_h, agb.at[me], load_sem.at[4])
    own_load.start()
    for load in loads:
        load.start()
    others = spot.others()
    greet([dev for _, dev in others], spot.along())
    plane = plane_of(spot, *plane_refs)
    o_lo, o_hi = pl.ds(0, OUT_LOW), pl.ds(OUT_LOW, tok - OUT_LOW)
    outs = Plane(
        spot,
        [agb.at[2 * i + k] for i in range(4)],
        [cotb.at[base + k] for base in chips],
        [agb.at[1 - k, o_lo], agb.at[3 - k, o_lo], agb.at[1 - k, o_hi]],
        [agb.at[3 - k, o_hi], agb.at[5 - k, o_hi], agb.at[5 - k, o_lo]],
        out_s,
        out_r,
        [agb.at[2 * i + 1 - k] for i in range(4)],
        low=OUT_LOW,
    )
    line = ExpertLine(spot, gwdn, 0, ff, *line_refs)
    some = first_out.shape[2]
    first_line = ExpertLine(spot, win, 0, some, *first_refs)
    gather = Gather(spot, agb.at[me], agb, ag_s, ag_r)
    for step, (other, dev) in enumerate(others):
        remote(meta.at[other], metas.at[me], me_s.at[step], me_r.at[step], dev).start()
    own_load.wait()
    gather.start()
    gather.start_y()
    metas[me] = meta[me]
    slot_rows = lax.broadcasted_iota(jnp.int32, (cap, tok), 0).astype(F32)
    step = 256

    def spots(p):
        return jnp.where(slot_rows == metas[p, 0:1, :], 1.0, 0.0)

    def gate_of(p, hot):
        return jnp.sum(hot * metas[p, 1:2, :], axis=1, keepdims=True)

    def dispatch(q):
        for kk in range(2):
            p = chips[q] + kk
            hot = spots(p)
            low = hot.astype(BF16)
            part = pl.ds(q * 2 * cap + kk * cap, cap)
            xs[part, :] = dot(low, agb[p]).astype(BF16)
            ds[part, :] = (dot(low, cotb[p]) * gate_of(p, hot)).astype(BF16)

    def work(q, count):
        rows = pl.ds(q * 2 * cap, count * 2 * cap)

        @pl.loop(0, ff // step)
        def _(n):
            gate_cols, up_cols = lanes(n * step, step), lanes(ff + n * step, step)
            x = xs[rows, :]
            g = dot(x, win[:, :, :, gate_cols].reshape(width, step))
            u = dot(x, win[:, :, :, up_cols].reshape(width, step))
            s = 1.0 / (1.0 + jnp.exp(-g))
            act = g * s
            hid[rows, gate_cols] = (act * u).astype(BF16)
            h = dot(ds[rows, :], wdn[:, gate_cols])
            igs[rows, gate_cols] = (h * u * (s * (1.0 + g * (1.0 - s)))).astype(BF16)
            igs[rows, up_cols] = (h * act).astype(BF16)

        @pl.loop(0, width // step)
        def _(n):
            cols = lanes(n * step, step)
            pgs[pl.ds(0, count * 2 * cap), cols] = dot(igs[rows, :], wint[:, cols]).astype(BF16)

    def back(q, at):
        base = chips[q]
        mine, theirs = rows_at(at * 2 * cap + k * cap, cap), rows_at(at * 2 * cap + (1 - k) * cap, cap)
        given = agb.at[base + 1 - k]
        given[...] = dot_tn(spots(base + 1 - k).astype(BF16), pgs[theirs, :]).astype(BF16)
        plane.give(q, given)
        plane.zk[q][...] = dot_tn(spots(base + k).astype(BF16), pgs[mine, :]).astype(BF16)

    for load in loads:
        load.wait()

    tall = width // ctx

    @pl.loop(0, ctx)
    def _(n):
        wint[:, lanes(n * tall, tall)] = win[n].reshape(tall, 2 * ff).T

    for n in range(planes - 1):
        source = lax.rem(me + planes - 1 - n, planes)
        remote(metas.at[source], metas.at[source], me_s.at[n], me_r.at[n], kp).wait_recv()
    gather.other_core(0)
    dispatch(0)
    work(0, 1)
    back(0, 0)
    gather.first()
    gather.second()
    gather.other_core(1)
    dispatch(1)
    gather.other_core(2)
    dispatch(2)
    work(1, 2)
    gather.third()
    back(1, 0)
    back(2, 1)
    gather.other_core(3)
    gather.done()
    dispatch(3)
    plane.fold(1)
    plane.fold(2)
    plane.near()
    work(3, 1)
    back(3, 0)
    plane.fold(3)
    plane.given()
    plane.across()


    @pl.loop(0, ctx)
    def _(n):
        tile = dot_tn(ds[:, lanes(n * tall, tall)], hid[...]).astype(BF16)
        for d in range(gwdn.shape[1]):
            gwdn[n, d] = tile[d * gwdn.shape[2] : (d + 1) * gwdn.shape[2]]

    line.step(1)
    plane.fold(0)

    @pl.loop(0, width // step)
    def _(n):
        cols = lanes(n * step, step)
        ds[:, cols] = dot_nt(hid[...], wdn[cols, :]).astype(BF16)

    def returned(q):
        base = chips[q]
        for kk in range(2):
            p = base + kk
            hot = spots(p)
            rows = ds[pl.ds(q * 2 * cap + kk * cap, cap), :]
            ggs[p, 0:1, :] = jnp.sum(hot * dot_nt(rows, cotb[p]), axis=0, keepdims=True)
            scaled = (rows.astype(F32) * gate_of(p, hot)).astype(BF16)
            cotb[p] = dot_tn(hot.astype(BF16), scaled).astype(BF16)
        outs.give(q, cotb.at[base + 1 - k])

    returned(1)
    returned(2)
    plane.turn()
    returned(3)
    returned(0)
    outs.fold(1)
    outs.fold(2)
    outs.near()
    outs.fold(3)
    outs.across()
    ggr[me] = ggs[me]
    for n, (other, dev) in enumerate(others):
        remote(ggs.at[other], ggr.at[me], gg_s.at[n], gg_r.at[n], dev).start()
    line.step(2)
    outs.fold(0)

    def gate_up(at, size):
        @pl.loop(0, ctx)
        def _(n):
            tile = dot_tn(xs[:, lanes(n * tall, tall)], igs[:, pl.ds(at, size)]).astype(BF16)
            win[n, :, :, pl.ds(at, size)] = tile.reshape(gwdn.shape[1], gwdn.shape[2], size)

    gate_up(0, some)
    rest = 2 * ff - some
    gate_up(some, rest // 2)
    gate_up(some + rest // 2, rest // 2)
    gwin_copy = pltpu.make_async_copy(win.at[:, :, :, pl.ds(some, rest)], gwin_h, load_sem.at[0])
    gwin_copy.start()
    line.step(3)
    first_line.step(1)
    outs.turn()
    first_line.step(2)
    line.final()
    for rows, terms in outs.total():
        output[rows, :] = (pg_out[rows, :] + summed(terms)).astype(BF16)
    for rows, terms in plane.total():
        pg_out[rows, :] = summed(terms)
    for n in range(planes - 1):
        source = lax.rem(me + planes - 1 - n, planes)
        remote(ggr.at[source], ggr.at[source], gg_s.at[n], gg_r.at[n], kp).wait_recv()
    for p in range(planes):
        gg_out[p : p + 1, :] = ggr[p, 0:1, :]
    first_line.step(3)
    first_line.final()
    gwin_copy.wait()
    for n, (other, dev) in enumerate(others):
        remote(meta.at[other], metas.at[other], me_s.at[n], me_r.at[n], dev).wait_send()
        remote(ggs.at[other], ggr.at[other], gg_s.at[n], gg_r.at[n], dev).wait_send()
    plane.done()
    outs.done()
    line.done(ex_out)
    first_line.done(first_out)


def run_ffn(cap, ffn, resid, cot_all, meta, win, wdn, parts, some):
    tok, width = ffn.shape
    ff = wdn.shape[2]
    planes = cot_all.shape[0]
    ctx = win.shape[0]
    rows = planes * cap
    piece = width // (ctx * parts)
    win = win.reshape(ctx, ctx, parts, piece, 2 * ff)
    vm, anyspace = pl.BlockSpec(memory_space=pltpu.VMEM), pl.BlockSpec(memory_space=pl.ANY)
    shape = jax.ShapeDtypeStruct
    dma = pltpu.SemaphoreType.DMA
    return pl.pallas_call(
        functools.partial(ffn_kernel, cap),
        out_shape=(
            shape((tok, width), BF16),
            shape((tok, width), F32),
            shape((planes, tok), F32),
            shape((ctx, parts, piece, 2 * ff - some), BF16),
            shape((ctx, piece, ff), BF16),
            shape((ctx, piece, some), BF16),
        ),
        in_specs=[anyspace, anyspace, anyspace, vm, anyspace, anyspace],
        out_specs=(vm, vm, vm, anyspace, vm, vm),
        scratch_shapes=[
            pltpu.VMEM((planes, tok, width), BF16),
            pltpu.VMEM((planes, 8, tok), F32),
            pltpu.VMEM((planes, tok, width), BF16),
            pltpu.VMEM((ctx, parts, piece, 2 * ff), BF16),
            pltpu.VMEM((width, ff), BF16),
            pltpu.VMEM((rows, width), BF16),
            pltpu.VMEM((rows, width), BF16),
            pltpu.VMEM((rows, ff), BF16),
            pltpu.VMEM((rows, 2 * ff), BF16),
            pltpu.VMEM((4 * cap, width), BF16),
            pltpu.VMEM((planes, 8, tok), F32),
            pltpu.VMEM((planes, 8, tok), F32),
            pltpu.VMEM((2 * ff, width), BF16),
            pltpu.VMEM((ctx, parts, piece, ff), BF16),
            dma((5,)),
            dma((GATHER_COPIES,)),
            dma((GATHER_COPIES,)),
            dma((planes - 1,)),
            dma((planes - 1,)),
            dma((planes - 1,)),
            dma((planes - 1,)),
            dma((10,)),
            dma((10,)),
        ]
        + plane_scratch(tok, width)
        + expert_scratch(ctx, parts, piece, ff)
        + expert_scratch(ctx, parts, piece, some),
        compiler_params=pltpu.CompilerParams(
            collective_id=1, has_side_effects=True, vmem_limit_bytes=63 * 2**20
        ),
        cost_estimate=pl.CostEstimate(flops=25 * 10**9, bytes_accessed=50 * 10**6, transcendentals=10**6),
    )(ffn, resid, cot_all, meta, win, wdn)


def back_kernel(
    span,
    meta,
    gg,
    lse,
    trig,
    kv,
    queries,
    attended,
    normed,
    router_t,
    gain_two,
    gain_one,
    resid_h,
    cot_h,
    pg_h,
    ffn_in_h,
    hidden_h,
    wout_h,
    wqkv_h,
    gwin_h,
    input_grad,
    qkv_out,
    proj_out,
    one_out,
    two_out,
    *scratch,
):
    wide_f, back, low, attg, mixed, weights, gwin, send, bsend, smalls, total, out_red = scratch[:12]
    mask, delta, kt, dk, dv, kvs, kvr = scratch[12:19]
    load_sem, kv_s, kv_r = scratch[19:22]
    p_zcr, p_zk, p_rx, p_ry, p_s, p_r = scratch[22:28]
    a_rx, a_ry, a_s, a_r = scratch[28:32]
    b_refs, qkv_refs, proj_refs = scratch[32:38], scratch[38:41], scratch[41:44]
    one_refs, two_refs = scratch[44:51], scratch[51:58]
    spot = Spot()
    c, k, z, ctx = spot.c, spot.k, spot.z, spot.ctx
    tok, width = attended.shape
    cols = one_out.shape[2]
    block, piece = out_red.shape[0], proj_out.shape[0]
    heads_kv = KV_HEADS
    half_head = HEAD // 2
    n_experts = meta.shape[0]
    kv_wide = mixed.shape[1] - width
    step = 256

    def load(src, dst, i):
        copy = pltpu.make_async_copy(src, dst, load_sem.at[i])
        copy.start()
        return copy

    gwin_load = load(gwin_h, gwin, 0)
    early = [
        load(resid_h, wide_f, 1),
        load(pg_h, back, 2),
        load(cot_h, input_grad, 3),
        load(ffn_in_h, attg, 4),
    ]
    wout_load = load(wout_h, weights.at[:, pl.ds(0, width)], 5)
    greet([spot.xp, spot.yp, spot.kp, spot.yk], spot.along())
    one = ExpertLine(spot, gwin, 0, cols, *one_refs)
    two = ExpertLine(spot, gwin, cols, cols, *two_refs)
    proj_plane = plane_of(spot, p_zcr, p_zk, p_rx, p_ry, p_s, p_r, low=BACK_LOW)
    qkv_plane = plane_of(spot, p_zcr, p_zk, a_rx, a_ry, a_s, a_r, low=BACK_LOW)
    rest_plane = plane_of(spot, *b_refs, low=BACK_LOW)

    def shared_line(ref, refs):
        def own(d):
            return ref.at[rows_at(d * piece, piece)]

        def adder(came, d):
            came[...] = plus(came[...], own(d)[...])

        return Line(spot, own, adder, *refs)

    qkv_line, proj_line = shared_line(total, qkv_refs), shared_line(out_red, proj_refs)

    def put_shared(to, ref, came):
        to[...] = plus(ref[rows_at(z * piece, piece)], *(x[...] for x in came))

    mine, theirs = rows_at(k * block, block), rows_at((1 - k) * block, block)
    gwin_load.wait()
    one.step(1)

    for copy in early:
        copy.wait()
    gate = jnp.concatenate([meta[g, 1:2, :] for g in range(n_experts)], axis=0)
    seen = gate * gg[...]
    mix = seen - gate * jnp.sum(seen, axis=0, keepdims=True)
    mix = jnp.concatenate([mix, jnp.zeros((HEAD - n_experts, tok), F32)], axis=0)
    logit_t = mix.astype(BF16)
    r = wide_f[...]
    inv = lax.rsqrt(jnp.mean(r * r, axis=-1, keepdims=True) + NORM_EPS)
    plain = r * inv
    ffn_grad = back[...] + dot_tn(logit_t[:n_experts], router_t[...])
    gain_row = jnp.sum(ffn_grad * plain, axis=0, keepdims=True)
    scaled = ffn_grad * gain_two[...]
    grad = input_grad[...].astype(F32) + inv * (
        scaled - plain * jnp.mean(scaled * plain, axis=-1, keepdims=True)
    )
    back[...] = grad
    low[...] = grad.astype(BF16)
    lane = lax.broadcasted_iota(jnp.int32, (width, HEAD), 1)
    routed = dot_tn(attg[...], logit_t.T)
    gain_col = jnp.broadcast_to(gain_row, (HEAD, width)).T
    smalls[...] = jnp.where(lane == n_experts, gain_col, routed).astype(BF16)

    for q in (1, 2, 3, 0):
        at = lanes(spot.chips[q] * block, 2 * block)
        send[q] = dot_tn(low[:, at], attended[...]).astype(BF16)
        proj_plane.give(q, send.at[q, theirs])
    wout_load.wait()

    @pl.loop(0, width // step)
    def _(n):
        at = lanes(n * step, step)
        attg[:, at] = dot(low[...], weights[:, at]).astype(BF16)

    wqkv_load = load(wqkv_h, weights, 5)
    hidden_load = load(hidden_h, low, 1)

    def start_plane(plane):
        plane.fold(1, send[1, mine])
        plane.fold(2, send[2, mine])
        plane.near()
        plane.fold(3, send[3, mine])
        plane.across()
        plane.fold(0, send[0, mine])

    start_plane(proj_plane)

    seq = kv.shape[0]
    spans = span.shape[1]
    size = seq // spans
    per = spans // ctx
    along_q = lax.broadcasted_iota(jnp.int32, (size, tok), 1)
    q_pos = jnp.where(along_q < size, span[0, c * per] * size, (span[0, c * per + 1] - 1) * size) + along_q
    for s in range(spans):
        k_pos = span[0, s] * size + lax.broadcasted_iota(jnp.int32, (size, tok), 0)
        mask[s * size : (s + 1) * size, :] = jnp.where(k_pos <= q_pos, 0.0, MASKED)

    lane_h = lax.broadcasted_iota(jnp.int32, (tok, HEAD), 1)
    deltas = jnp.zeros((tok, HEAD), F32)
    for h in range(HEADS):
        at = slice(h * HEAD, (h + 1) * HEAD)
        term = jnp.sum(attg[:, at].astype(F32) * attended[:, at].astype(F32), axis=-1, keepdims=True)
        deltas = jnp.where(lane_h == h, term, deltas)
    delta[...] = deltas.T
    for g in range(heads_kv):
        kt[g] = kv[:, g * HEAD : (g + 1) * HEAD].astype(F32).T.astype(BF16)

    cosine, sine = trig[0], trig[1]

    def unrotate(w):
        return w * cosine - pltpu.roll(w, half_head, 1) * sine

    def head(g, h):
        at = lanes(h * HEAD, HEAD)
        k_at = slice(g * HEAD, (g + 1) * HEAD)
        v_at = slice((heads_kv + g) * HEAD, (heads_kv + g + 1) * HEAD)
        q, a = queries[:, at], attg[:, at]
        soft = jnp.exp(dot_nt(kv[:, k_at], q) + mask[...] - lse[pl.ds(h, 1), :])
        prob = dot_nt(kv[:, v_at], a)
        score = (soft * (prob - delta[pl.ds(h, 1), :])).astype(BF16)
        mixed[:, at] = (unrotate(dot(kt[g], score).T) * HEAD**-0.5).astype(BF16)
        dk[...] += dot(score, q)
        dv[...] += dot(soft.astype(BF16), a)

    def heads(g, first, count):
        @pl.loop(first, first + count)
        def _(h):
            head(g, h)

    def clear():
        dk[...] = jnp.zeros(dk.shape, F32)
        dv[...] = jnp.zeros(dv.shape, F32)

    flip_c = lax.rem(c + 2, ctx)
    near_c = c + 1 - 2 * k
    across_c = lax.rem(near_c + 2, ctx)

    def kv_copy(g, src, i, dev):
        return remote(src, kvr.at[g, i], kv_s.at[g, i], kv_r.at[g, i], dev)

    def send_kv(g):
        for cc in range(ctx):
            rows = slice(cc * tok, (cc + 1) * tok)
            kvs[g, cc, :, :HEAD] = dk[rows, :].astype(BF16)
            kvs[g, cc, :, HEAD:] = dv[rows, :].astype(BF16)
        kv_copy(g, kvs.at[g, across_c], 1, spot.kp).start()
        kv_copy(g, kvs.at[g, near_c], 0, spot.kp).start()

    def pass_kv(g):
        kv_copy(g, kvs.at[g, across_c], 1, spot.kp).wait_recv()
        kvs[g, flip_c] = plus(kvs[g, flip_c], kvr[g, 1])
        kv_copy(g, kvs.at[g, flip_c], 2, spot.yp).start()

    clear()
    heads(0, 0, 2)
    one.step(2)
    heads(0, 2, 4)
    send_kv(0)
    clear()
    proj_plane.turn()
    heads(1, 6, 3)
    pass_kv(0)
    one.step(3)
    two.step(1)
    heads(1, 9, 3)
    send_kv(1)
    pass_kv(1)
    for rows, terms in proj_plane.total():
        out_red[rows, :] = summed(terms).astype(BF16)
    proj_line.step(1)
    proj_plane.done()
    for g in range(heads_kv):
        kv_copy(g, kvs.at[g, near_c], 0, spot.kp).wait_recv()
        kv_copy(g, kvs.at[g, flip_c], 2, spot.yp).wait_recv()
        own = kvs[g, c].astype(F32) + kvr[g, 0].astype(F32) + kvr[g, 2].astype(F32)
        at = width + g * HEAD
        mixed[:, at : at + HEAD] = unrotate(own[:, :HEAD]).astype(BF16)
        at = width + (heads_kv + g) * HEAD
        mixed[:, at : at + HEAD] = own[:, HEAD:].astype(BF16)

    for q in (1, 2, 3, 0):
        at = lanes(spot.chips[q] * block, 2 * block)
        send[q] = dot_tn(normed[:, at], mixed[:, :width]).astype(BF16)
        qkv_plane.give(q, send.at[q, theirs])
    start_plane(qkv_plane)
    proj_line.step(2)
    wqkv_load.wait()

    @pl.loop(0, width // step)
    def _(n):
        at = lanes(n * step, step)
        wide_f[:, at] = dot_nt(mixed[...], weights[at, :])

    two.step(2)
    hidden_load.wait()
    x = low[...].astype(F32)
    inv = lax.rsqrt(jnp.mean(x * x, axis=-1, keepdims=True) + NORM_EPS)
    plain = x * inv
    ng = wide_f[...]
    gain_row = jnp.sum(ng * plain, axis=0, keepdims=True)
    scaled = ng * gain_one[...]
    input_grad[...] = (
        back[...] + inv * (scaled - plain * jnp.mean(scaled * plain, axis=-1, keepdims=True))
    ).astype(BF16)
    lane = lax.broadcasted_iota(jnp.int32, (width, HEAD), 1)
    gain_col = jnp.broadcast_to(gain_row, (HEAD, width)).T
    smalls[...] = jnp.where(lane == HEAD - 1, gain_col, smalls[...].astype(F32)).astype(BF16)
    for q in (1, 2, 3, 0):
        at = lanes(spot.chips[q] * block, 2 * block)
        bsend[q, :, :kv_wide] = dot_tn(normed[:, at], mixed[:, width:]).astype(BF16)
        bsend[q, :, kv_wide:] = smalls[rows_at(spot.chips[q] * block, 2 * block), :]
        rest_plane.give(q, bsend.at[q, theirs])
    rest_plane.fold(1, bsend[1, mine])
    rest_plane.fold(2, bsend[2, mine])
    rest_plane.near()
    rest_plane.fold(3, bsend[3, mine])
    rest_plane.across()
    rest_plane.fold(0, bsend[0, mine])
    qkv_plane.turn()
    rest_plane.turn()
    two.step(3)
    one.final()
    proj_line.step(3)
    for rows, terms in qkv_plane.total():
        total[rows, :width] = summed(terms).astype(BF16)
    for rows, terms in rest_plane.total():
        total[rows, width:] = summed(terms).astype(BF16)
    qkv_line.step(1)
    one.done(one_out)
    qkv_line.step(2)
    proj_line.final(lambda *came: put_shared(proj_out, out_red, came))
    qkv_line.step(3)
    two.final()
    proj_line.done()
    qkv_plane.done()
    rest_plane.done()
    for g in range(heads_kv):
        kv_copy(g, kvs.at[g, near_c], 0, spot.kp).wait_send()
        kv_copy(g, kvs.at[g, across_c], 1, spot.kp).wait_send()
        kv_copy(g, kvs.at[g, flip_c], 2, spot.yp).wait_send()
    qkv_line.final(lambda *came: put_shared(qkv_out, total, came))
    qkv_line.done()
    two.done(two_out)


def run_back(
    span, meta, gg, lse, trig, kv, queries, attended, normed, router_t, gain_two, gain_one,
    resid, cot, pg, ffn_in, hidden, wout, wqkv, gwin,
):
    tok, width = attended.shape
    seq, kv_cols = kv.shape
    planes = meta.shape[0]
    ctx, parts, rows, wide = gwin.shape
    cols = wide // 2
    block = width // planes
    piece = block // parts
    rest = kv_cols + HEAD
    vm, anyspace = pl.BlockSpec(memory_space=pltpu.VMEM), pl.BlockSpec(memory_space=pl.ANY)
    sm = pl.BlockSpec(memory_space=pltpu.SMEM)
    shape = jax.ShapeDtypeStruct
    dma = pltpu.SemaphoreType.DMA
    return pl.pallas_call(
        back_kernel,
        out_shape=(
            shape((tok, width), BF16),
            shape((piece, width + rest), BF16),
            shape((piece, width), BF16),
            shape((ctx, rows, cols), BF16),
            shape((ctx, rows, cols), BF16),
        ),
        in_specs=[sm] + [vm] * 11 + [anyspace] * 8,
        out_specs=(vm,) * 5,
        scratch_shapes=[
            pltpu.VMEM((tok, width), F32),
            pltpu.VMEM((tok, width), F32),
            pltpu.VMEM((tok, width), BF16),
            pltpu.VMEM((tok, width), BF16),
            pltpu.VMEM((tok, width + kv_cols), BF16),
            pltpu.VMEM(wqkv.shape, BF16),
            pltpu.VMEM(gwin.shape, BF16),
            pltpu.VMEM((4, 2 * block, width), BF16),
            pltpu.VMEM((4, 2 * block, rest), BF16),
            pltpu.VMEM((width, HEAD), BF16),
            pltpu.VMEM((block, width + rest), BF16),
            pltpu.VMEM((block, width), BF16),
            pltpu.VMEM((seq, tok), F32),
            pltpu.VMEM((HEAD, tok), F32),
            pltpu.VMEM((KV_HEADS, HEAD, seq), BF16),
            pltpu.VMEM((seq, HEAD), F32),
            pltpu.VMEM((seq, HEAD), F32),
            pltpu.VMEM((KV_HEADS, ctx, tok, 2 * HEAD), BF16),
            pltpu.VMEM((KV_HEADS, 3, tok, 2 * HEAD), BF16),
            dma((6,)),
            dma((KV_HEADS, 3)),
            dma((KV_HEADS, 3)),
        ]
        + plane_scratch(block, width, BACK_LOW)
        + plane_scratch(block, width, BACK_LOW)[2:]
        + plane_scratch(block, rest, BACK_LOW)
        + line_scratch(parts, (piece, width + rest))
        + line_scratch(parts, (piece, width))
        + expert_scratch(ctx, parts, rows, cols)
        + expert_scratch(ctx, parts, rows, cols),
        compiler_params=pltpu.CompilerParams(
            collective_id=2, has_side_effects=True, vmem_limit_bytes=63 * 2**20
        ),
        cost_estimate=pl.CostEstimate(flops=12 * 10**9, bytes_accessed=60 * 10**6, transcendentals=4 * 10**6),
    )(
        span, meta, gg, lse, trig, kv, queries, attended, normed, router_t, gain_two, gain_one,
        resid, cot, pg, ffn_in, hidden, wout, wqkv, gwin,
    )


def finish_kernel(
    n_experts,
    output_h,
    input_h,
    qkv_h,
    proj_h,
    first_h,
    one_h,
    two_h,
    down_h,
    output,
    input_grad,
    gains,
    qkv,
    proj,
    router,
    inner,
    down,
    low_qkv,
    low_proj,
    low_first,
    low_one,
    low_two,
    low_down,
    inner_full,
    down_full,
    sem,
    out_sem,
):
    whole = [pltpu.make_async_copy(output_h, output, out_sem.at[0]), pltpu.make_async_copy(input_h, input_grad, out_sem.at[1])]
    loads = [
        pltpu.make_async_copy(src, dst, sem.at[i])
        for i, (src, dst) in enumerate(
            (
                (down_h, low_down),
                (first_h, low_first),
                (one_h, low_one),
                (two_h, low_two),
                (qkv_h, low_qkv),
                (proj_h, low_proj),
            )
        )
    ]
    for copy in loads + whole:
        copy.start()
    loads[0].wait()
    down_full[...] = low_down[...].astype(F32)
    whole.append(pltpu.make_async_copy(down_full, down, out_sem.at[2]))
    whole[-1].start()
    at = 0
    for load, low in zip(loads[1:4], (low_first, low_one, low_two)):
        load.wait()
        size = low.shape[2]
        inner_full[:, :, at : at + size] = low[...].astype(F32)
        at += size
    whole.append(pltpu.make_async_copy(inner_full, inner, out_sem.at[3]))
    whole[-1].start()
    for load in loads[4:]:
        load.wait()
    wide = qkv.shape[1]
    qkv[...] = low_qkv[:, :wide].astype(F32)
    proj[...] = low_proj[...].astype(F32)
    small = low_qkv[:, wide:].astype(F32)
    router[...] = small[:, :n_experts]
    piece = small.shape[0]
    same = lax.broadcasted_iota(jnp.int32, (piece, piece), 0) == lax.broadcasted_iota(
        jnp.int32, (piece, piece), 1
    )
    for row, col in ((0, HEAD - 1), (1, n_experts)):
        gains[row : row + 1, :] = jnp.sum(jnp.where(same, small[:, col : col + 1], 0.0), axis=0, keepdims=True)
    for copy in whole:
        copy.wait()


def run_finish(n_experts, output, input_grad, qkv, proj, first, one, two, down):
    piece, width = proj.shape
    ctx, rows, ff = down.shape
    shape = jax.ShapeDtypeStruct
    vm, anyspace = pl.BlockSpec(memory_space=pltpu.VMEM), pl.BlockSpec(memory_space=pl.ANY)
    return pl.pallas_call(
        functools.partial(finish_kernel, n_experts),
        out_shape=(
            shape(output.shape, BF16),
            shape(input_grad.shape, BF16),
            shape((2, piece), F32),
            shape((piece, qkv.shape[1] - HEAD), F32),
            shape((piece, width), F32),
            shape((piece, n_experts), F32),
            shape((ctx, rows, 2 * ff), F32),
            shape((ctx, rows, ff), F32),
        ),
        in_specs=[anyspace] * 8,
        out_specs=(anyspace, anyspace, vm, vm, vm, vm, anyspace, anyspace),
        scratch_shapes=[pltpu.VMEM(x.shape, BF16) for x in (qkv, proj, first, one, two, down)]
        + [
            pltpu.VMEM((ctx, rows, 2 * ff), F32),
            pltpu.VMEM((ctx, rows, ff), F32),
            pltpu.SemaphoreType.DMA((6,)),
            pltpu.SemaphoreType.DMA((4,)),
        ],
        compiler_params=pltpu.CompilerParams(vmem_limit_bytes=56 * 2**20),
    )(output, input_grad, qkv, proj, first, one, two, down)


def local(
    hidden_in,
    span_order,
    expert_ids,
    priority,
    gain_attn,
    qkv_weight,
    out_weight,
    gain_ffn,
    router,
    in_weight,
    down_weight,
    cotangent,
):
    _, tok_rows, width = hidden_in.shape
    ctx, parts = lax.axis_size("context"), lax.axis_size("dp")
    planes = ctx * lax.axis_size("expert")
    n_experts = router.shape[1]
    top_k = expert_ids.shape[2]
    capacity = (9 * tok_rows * top_k + 8 * n_experts - 1) // (8 * n_experts)
    ff = down_weight.shape[2]
    half_freqs = ROPE_BASE ** (np.arange(HEAD // 2) * (-2.0 / HEAD))
    freqs = np.concatenate([half_freqs, half_freqs])[None].astype(np.float32)
    router_t = router.T
    hidden, cot = hidden_in[0], cotangent[0]
    normed, queries, kv, lse, attended, resid, ffn_in, trig, meta, cot_all = run_front(
        capacity,
        span_order,
        hidden,
        cot,
        gain_attn,
        freqs,
        gain_ffn,
        router_t,
        expert_ids[0].T,
        priority[0].T,
        qkv_weight,
        out_weight,
        ctx,
        planes,
    )
    output, pair_sum, gate_grad, gwin, down, in_first = run_ffn(
        capacity, ffn_in, resid, cot_all, meta, in_weight, down_weight, parts, ff // 3
    )
    input_grad, qkv_sum, proj_sum, in_one, in_two = run_back(
        span_order,
        meta,
        gate_grad,
        lse,
        trig,
        kv,
        queries,
        attended,
        normed,
        router_t,
        gain_ffn,
        gain_attn,
        resid,
        cot,
        pair_sum,
        ffn_in,
        hidden,
        out_weight,
        qkv_weight,
        gwin,
    )
    output, input_grad, gains, qkv_grad, proj_grad, router_grad, inner_grad, down_grad = run_finish(
        n_experts, output, input_grad, qkv_sum, proj_sum, in_first, in_one, in_two, down
    )
    return (
        output[None],
        input_grad[None],
        gains[0],
        qkv_grad,
        proj_grad,
        gains[1],
        router_grad,
        inner_grad,
        down_grad,
    )


def general(
    hidden_in,
    span_order,
    expert_ids,
    priority,
    gain_attn,
    qkv_weight,
    out_weight,
    gain_ffn,
    router,
    in_weight,
    down_weight,
    cotangent,
):
    tok_rows = hidden_in.shape[1]
    width = hidden_in.shape[2]
    contexts = lax.axis_size("context")
    span_len = tok_rows // 2
    seq_len = tok_rows * contexts
    group = HEADS // KV_HEADS
    q_cols = HEADS * HEAD
    kv_cols = KV_HEADS * HEAD
    scale = HEAD ** (-0.5)
    local_experts = in_weight.shape[0]
    n_experts = local_experts * lax.axis_size("expert")
    top_k = expert_ids.shape[2]
    capacity = (9 * tok_rows * top_k + 8 * n_experts - 1) // (8 * n_experts)
    ff_width = down_weight.shape[2]
    seq_spans = span_order[0]
    stored = jnp.arange(seq_len) // span_len
    all_pos = (seq_spans[stored] * span_len + jnp.arange(seq_len) % span_len).astype(jnp.float32)
    my_pos = lax.dynamic_slice_in_dim(all_pos, lax.axis_index("context") * tok_rows, tok_rows)
    cosine, sine = rope_tables(my_pos, HEAD)
    inputs = hidden_in[0].astype(jnp.float32)
    inv_one = lax.rsqrt(jnp.mean(inputs * inputs, axis=-1, keepdims=True) + NORM_EPS)
    plain_one = inputs * inv_one
    normed = (plain_one * gain_attn).astype(jnp.bfloat16)
    mixed = jnp.dot(normed, qkv_weight, preferred_element_type=jnp.float32)
    queries = (
        rotate(mixed[:, :q_cols].reshape(tok_rows, HEADS, HEAD), cosine, sine) * scale
    ).astype(jnp.bfloat16)
    keys = rotate(
        mixed[:, q_cols : q_cols + kv_cols].reshape(tok_rows, KV_HEADS, HEAD), cosine, sine
    ).astype(jnp.bfloat16)
    values = mixed[:, q_cols + kv_cols :].reshape(tok_rows, KV_HEADS, HEAD).astype(jnp.bfloat16)
    grouped = queries.reshape(tok_rows, KV_HEADS, group, HEAD)

    def key_scores(key_piece):
        scores = jnp.einsum(
            "qkgd,skd->kgqs", grouped, key_piece, preferred_element_type=jnp.float32
        )
        visible = all_pos[None, None, None, :] <= my_pos[None, None, :, None]
        return (jnp.where(visible, scores, MASKED), visible)

    running = jnp.full((KV_HEADS, group, tok_rows), MASKED, jnp.float32)
    key_piece = lax.all_gather(keys, "context", axis=0, tiled=True)
    value_piece = lax.all_gather(values, "context", axis=0, tiled=True)
    scores, visible = key_scores(key_piece)
    newest = jnp.maximum(running, jnp.max(scores, axis=-1))
    weights = jnp.where(visible, jnp.exp(scores - newest[..., None]), 0.0)
    totals = jnp.sum(weights, axis=-1)
    accum = jnp.einsum(
        "kgqs,skd->kgqd",
        weights.astype(jnp.bfloat16),
        value_piece,
        preferred_element_type=jnp.float32,
    )
    running, totals, accum = (newest, totals, accum)
    log_total = running + jnp.log(totals)
    attended = (
        (accum / totals[..., None])
        .transpose(2, 0, 1, 3)
        .reshape(tok_rows, q_cols)
        .astype(jnp.bfloat16)
    )
    resid = inputs + jnp.einsum(
        "rh,dh->rd", attended, out_weight, preferred_element_type=jnp.float32
    )
    inv_two = lax.rsqrt(jnp.mean(resid * resid, axis=-1, keepdims=True) + NORM_EPS)
    plain_two = resid * inv_two
    ffn_in = (plain_two * gain_ffn).astype(jnp.bfloat16)
    logits = jnp.dot(ffn_in, router, preferred_element_type=jnp.float32)
    token_ids = expert_ids[0]
    gates = softmax_last(jnp.take_along_axis(logits, token_ids, axis=1))
    slots = route(token_ids, priority[0], n_experts, capacity)
    pair_rows = jnp.repeat(ffn_in, top_k, axis=0)
    send_rows = (
        jnp.zeros((n_experts * capacity, width), jnp.bfloat16).at[slots].set(pair_rows, mode="drop")
    )
    received = lax.all_to_all(
        send_rows.reshape(n_experts, capacity, width),
        "expert",
        split_axis=0,
        concat_axis=1,
        tiled=True,
    )
    inner = jnp.einsum("erd,edf->erf", received, in_weight, preferred_element_type=jnp.float32)
    gate_part = inner[..., :ff_width]
    up_part = inner[..., ff_width:]
    sigma = 1.0 / (1.0 + jnp.exp(-gate_part))
    activated = gate_part * sigma
    hidden = (activated * up_part).astype(jnp.bfloat16)
    expert_out = jnp.einsum(
        "erf,edf->erd", hidden, down_weight, preferred_element_type=jnp.float32
    ).astype(jnp.bfloat16)
    returned = lax.all_to_all(
        expert_out, "expert", split_axis=1, concat_axis=0, tiled=True
    ).reshape(n_experts * capacity, width)
    padded = jnp.concatenate([returned, jnp.zeros((1, width), jnp.bfloat16)], axis=0)
    picked = padded[slots].reshape(tok_rows, top_k, width)
    output = (resid + jnp.sum(gates[:, :, None] * picked, axis=1)).astype(jnp.bfloat16)
    cot_low = cotangent[0]
    cot_full = cot_low.astype(jnp.float32)
    gate_grad = jnp.einsum("rkd,rd->rk", picked, cot_low, preferred_element_type=jnp.float32)
    ret_grad = (
        (gates[:, :, None] * cot_full[:, None, :])
        .astype(jnp.bfloat16)
        .reshape(tok_rows * top_k, width)
    )
    send_grad = (
        jnp.zeros((n_experts * capacity, width), jnp.bfloat16).at[slots].set(ret_grad, mode="drop")
    )
    received_grad = lax.all_to_all(
        send_grad.reshape(n_experts, capacity, width),
        "expert",
        split_axis=0,
        concat_axis=1,
        tiled=True,
    )
    hid_grad = jnp.einsum(
        "erd,edf->erf", received_grad, down_weight, preferred_element_type=jnp.float32
    )
    slope = sigma * (1.0 + gate_part * (1.0 - sigma))
    inner_grad = jnp.concatenate(
        [hid_grad * up_part * slope, hid_grad * activated], axis=-1
    ).astype(jnp.bfloat16)
    row_grad = jnp.einsum(
        "erf,edf->erd", inner_grad, in_weight, preferred_element_type=jnp.float32
    ).astype(jnp.bfloat16)
    part_rows = received
    expert_in = (
        lax.psum_scatter(
            jnp.einsum(
                "erd,erf->def", part_rows, inner_grad, preferred_element_type=jnp.float32
            ).astype(jnp.bfloat16),
            ("context", "dp"),
            scatter_dimension=0,
            tiled=True,
        )
        .astype(jnp.float32)
        .transpose(1, 0, 2)
    )
    part_rows = received_grad
    expert_down = (
        lax.psum_scatter(
            jnp.einsum(
                "erd,erf->def", part_rows, hidden, preferred_element_type=jnp.float32
            ).astype(jnp.bfloat16),
            ("context", "dp"),
            scatter_dimension=0,
            tiled=True,
        )
        .astype(jnp.float32)
        .transpose(1, 0, 2)
    )
    back_rows = lax.all_to_all(row_grad, "expert", split_axis=1, concat_axis=0, tiled=True).reshape(
        n_experts * capacity, width
    )
    back_padded = jnp.concatenate([back_rows, jnp.zeros((1, width), jnp.bfloat16)], axis=0)
    pair_grad = back_padded[slots].reshape(tok_rows, top_k, width)
    mix_grad = gates * (gate_grad - jnp.sum(gates * gate_grad, axis=-1, keepdims=True))
    matches = token_ids[:, :, None] == jnp.arange(n_experts)[None, None, :]
    logit_grad = jnp.sum(jnp.where(matches, mix_grad[:, :, None], 0.0), axis=1).astype(jnp.bfloat16)
    router_part = jnp.einsum("rd,re->de", ffn_in, logit_grad, preferred_element_type=jnp.float32)
    ffn_grad = jnp.sum(pair_grad.astype(jnp.float32), axis=1) + jnp.einsum(
        "re,de->rd", logit_grad, router, preferred_element_type=jnp.float32
    )
    gain_ffn_part = jnp.sum(ffn_grad * plain_two, axis=0)
    scaled_two = ffn_grad * gain_ffn
    resid_grad = cot_full + inv_two * (
        scaled_two - plain_two * jnp.mean(scaled_two * plain_two, axis=-1, keepdims=True)
    )
    resid_low = resid_grad.astype(jnp.bfloat16)
    out_part = jnp.einsum("rd,rh->dh", resid_low, attended, preferred_element_type=jnp.float32)
    att_grad = jnp.einsum(
        "rd,dh->rh", resid_low, out_weight, preferred_element_type=jnp.float32
    ).astype(jnp.bfloat16)
    att_heads = att_grad.reshape(tok_rows, KV_HEADS, group, HEAD)
    row_delta = jnp.sum(
        att_heads.astype(jnp.float32)
        * attended.reshape(tok_rows, KV_HEADS, group, HEAD).astype(jnp.float32),
        axis=-1,
    ).transpose(1, 2, 0)
    key_piece = lax.all_gather(keys, "context", axis=0, tiled=True)
    value_piece = lax.all_gather(values, "context", axis=0, tiled=True)
    scores, visible = key_scores(key_piece)
    soft = jnp.exp(scores - log_total[..., None])
    prob_grad = jnp.einsum(
        "qkgd,skd->kgqs", att_heads, value_piece, preferred_element_type=jnp.float32
    )
    score_grad = (soft * (prob_grad - row_delta[..., None])).astype(jnp.bfloat16)
    query_acc = jnp.einsum(
        "kgqs,skd->kgqd", score_grad, key_piece, preferred_element_type=jnp.float32
    )
    key_part = jnp.einsum("kgqs,qkgd->skd", score_grad, grouped, preferred_element_type=jnp.float32)
    value_part = jnp.einsum(
        "kgqs,qkgd->skd", soft.astype(jnp.bfloat16), att_heads, preferred_element_type=jnp.float32
    )
    pair_acc = jnp.stack([key_part, value_part], axis=1)
    query_acc, pair_acc = (query_acc, pair_acc)
    own_pairs = lax.psum_scatter(
        pair_acc.astype(jnp.bfloat16), "context", scatter_dimension=0, tiled=True
    ).astype(jnp.float32)
    query_grad = (
        unrotate(query_acc.transpose(2, 0, 1, 3).reshape(tok_rows, HEADS, HEAD), cosine, sine)
        * scale
    )
    key_grad = unrotate(own_pairs[:, 0], cosine, sine)
    mixed_grad = jnp.concatenate(
        [
            query_grad.reshape(tok_rows, q_cols),
            key_grad.reshape(tok_rows, kv_cols),
            own_pairs[:, 1].reshape(tok_rows, kv_cols),
        ],
        axis=-1,
    ).astype(jnp.bfloat16)
    qkv_part = jnp.einsum("rd,rc->dc", normed, mixed_grad, preferred_element_type=jnp.float32)
    norm_grad = jnp.einsum("rc,dc->rd", mixed_grad, qkv_weight, preferred_element_type=jnp.float32)
    gain_attn_part = jnp.sum(norm_grad * plain_one, axis=0)
    scaled_one = norm_grad * gain_attn
    input_grad = (
        resid_grad
        + inv_one
        * (scaled_one - plain_one * jnp.mean(scaled_one * plain_one, axis=-1, keepdims=True))
    ).astype(jnp.bfloat16)
    gain_attn_grad, qkv_grad, out_proj_grad, gain_ffn_grad, router_grad = (
        lax.psum_scatter(
            gain_attn_part, ("expert", "context", "dp"), scatter_dimension=0, tiled=True
        ),
        lax.psum_scatter(qkv_part, ("expert", "context", "dp"), scatter_dimension=0, tiled=True),
        lax.psum_scatter(out_part, ("expert", "context", "dp"), scatter_dimension=0, tiled=True),
        lax.psum_scatter(
            gain_ffn_part, ("expert", "context", "dp"), scatter_dimension=0, tiled=True
        ),
        lax.psum_scatter(router_part, ("expert", "context", "dp"), scatter_dimension=0, tiled=True),
    )
    return (
        output[None],
        input_grad[None],
        gain_attn_grad,
        qkv_grad,
        out_proj_grad,
        gain_ffn_grad,
        router_grad,
        expert_in,
        expert_down,
    )


def solution(mesh):
    in_specs = (
        P(("expert", "dp"), "context", None),
        P(("expert", "dp"), None),
        P(("expert", "dp"), "context", None),
        P(("expert", "dp"), "context", None),
        P(),
        P(),
        P(),
        P(),
        P(),
        P("expert", None, None),
        P("expert", None, None),
        P(("expert", "dp"), "context", None),
    )
    out_specs = (
        P(("expert", "dp"), "context", None),
        P(("expert", "dp"), "context", None),
        P(("expert", "context", "dp")),
        P(("expert", "context", "dp"), None),
        P(("expert", "context", "dp"), None),
        P(("expert", "context", "dp")),
        P(("expert", "context", "dp"), None),
        P("expert", ("context", "dp"), None),
        P("expert", ("context", "dp"), None),
    )
    tuned = dict(mesh.shape) == {"expert": 2, "context": 4, "dp": 4}
    body = local if tuned else general
    return jax.shard_map(body, mesh=mesh, in_specs=in_specs, out_specs=out_specs, check_vma=False)
```

```python
import functools

import jax
import jax.numpy as jnp
import numpy as np
from jax import lax
from jax.experimental import pallas as pl
from jax.experimental.pallas import tpu as pltpu
from jax.sharding import PartitionSpec as P

HEADS = 12
KV_HEADS = 2
HEAD = 128


ROPE_BASE = 1000000.0
NORM_EPS = 1e-06
MASKED = -1e30


def rope_tables(positions, head_size):
    half_size = head_size // 2
    freqs = ROPE_BASE ** (jnp.arange(half_size).astype(jnp.float32) * (-2.0 / head_size))
    angles = positions[:, None] * freqs[None, :]
    return (jnp.cos(angles)[:, None, :], jnp.sin(angles)[:, None, :])


def rotate(values, cosine, sine):
    half_size = values.shape[-1] // 2
    first = values[..., :half_size]
    second = values[..., half_size:]
    return jnp.concatenate(
        [first * cosine - second * sine, second * cosine + first * sine], axis=-1
    )


def unrotate(values, cosine, sine):
    half_size = values.shape[-1] // 2
    first = values[..., :half_size]
    second = values[..., half_size:]
    return jnp.concatenate(
        [first * cosine + second * sine, second * cosine - first * sine], axis=-1
    )


def softmax_last(scores):
    shifted = jnp.exp(scores - jnp.max(scores, axis=-1, keepdims=True))
    return shifted / jnp.sum(shifted, axis=-1, keepdims=True)


def route(block_ids, block_order, n_experts, capacity):
    flat_ids = block_ids.reshape(-1)
    flat_order = block_order.reshape(-1)
    choose = (flat_ids[:, None] == jnp.arange(n_experts)[None, :]).astype(jnp.int32)
    ordered = jnp.zeros_like(choose).at[flat_order].set(choose)
    earlier = jnp.cumsum(ordered, axis=0, dtype=jnp.int32) - ordered
    ranks = jnp.sum(earlier[flat_order] * choose, axis=1)
    return jnp.where(ranks < capacity, flat_ids * capacity + ranks, n_experts * capacity)


MESH = pl.DeviceIdType.MESH
F32 = jnp.float32
BF16 = jnp.bfloat16
BACK_LOW = 96
OUT_LOW = 128
FRONT_LOW = 96


def dot(a, b):
    return jnp.dot(a, b, preferred_element_type=F32)


def dot_nt(a, b):
    return lax.dot_general(a, b, (((1,), (1,)), ((), ())), preferred_element_type=F32)


def dot_tn(a, b):
    return lax.dot_general(a, b, (((0,), (0,)), ((), ())), preferred_element_type=F32)


def plus(a, *more):
    total = a.astype(F32)
    for b in more:
        total = total + b.astype(F32)
    return total.astype(BF16)


def lanes(at, size):
    return pl.ds(pl.multiple_of(at, 128), size)


def rows_at(at, size):
    return pl.ds(pl.multiple_of(at, 16), size)


def remote(src, dst, s, r, dev):
    return pltpu.make_async_remote_copy(
        src_ref=src, dst_ref=dst, send_sem=s, recv_sem=r, device_id=dev, device_id_type=MESH
    )


class Spot:
    def __init__(self):
        e, c, z = lax.axis_index("expert"), lax.axis_index("context"), lax.axis_index("dp")
        self.ctx = lax.axis_size("context")
        self.parts = lax.axis_size("dp")
        self.planes = self.ctx * lax.axis_size("expert")
        y, k = lax.div(c, 2), lax.rem(c, 2)
        self.e, self.c, self.z, self.k = e, c, z, k
        self.me = e * self.ctx + c
        self.xp, self.yp = (1 - e, c, z), (e, (1 - y) * 2 + k, z)
        self.kp, self.yk = (e, y * 2 + 1 - k, z), (e, (1 - y) * 2 + 1 - k, z)
        self.chips = [
            eq * self.ctx + yq * 2 for eq, yq in ((e, y), (1 - e, y), (e, 1 - y), (1 - e, 1 - y))
        ]

    def others(self):
        found = []
        for step in range(1, self.planes):
            other = lax.rem(self.me + step, self.planes)
            found.append((other, (lax.div(other, self.ctx), lax.rem(other, self.ctx), self.z)))
        return found

    def along(self):
        e, c, z = self.e, self.c, self.z
        return [(z < self.parts - 1, (e, c, z + 1)), (z > 0, (e, c, z - 1))]


def greet(peers, extra=()):
    barrier = pltpu.get_barrier_semaphore()
    for peer in peers:
        pl.semaphore_signal(barrier, inc=1, device_id=peer, device_id_type=MESH)
    for there, peer in extra:

        @pl.when(there)
        def _():
            pl.semaphore_signal(barrier, inc=1, device_id=peer, device_id_type=MESH)

    count = len(peers)
    for there, _ in extra:
        count = count + there.astype(jnp.int32)
    pl.semaphore_wait(barrier, count)


class Plane:
    def __init__(self, spot, zcr, zk, rx, ry, s, r, zcr_there=None, low=None):
        self.zcr_there = zcr_there or zcr
        self.spot, self.zcr, self.zk, self.rx, self.ry, self.s, self.r = spot, zcr, zk, rx, ry, s, r
        low = low or zk[0].shape[0] // 2
        self.lo, self.hi = pl.ds(0, low), pl.ds(low, zk[0].shape[0] - low)
        self.sent, self.gives = [], []

    def push(self, src, dst, i, dev):
        copy = remote(src, dst, self.s.at[i], self.r.at[i], dev)
        copy.start()
        self.sent.append(copy)

    def arrive(self, dst, i):
        remote(dst, dst, self.s.at[i], self.r.at[i], self.spot.kp).wait_recv()

    def given(self):
        for copy in self.gives:
            copy.wait_send()
        self.gives = []

    def give(self, q, src):
        self.gives.append(remote(src, self.zcr_there[q], self.s.at[q], self.r.at[q], self.spot.kp))
        self.gives[-1].start()

    def fold(self, q, own=None):
        self.arrive(self.zcr[q], q)
        self.zk[q][...] = plus(self.zk[q][...] if own is None else own, self.zcr[q][...])

    def near(self):
        self.push(self.zk[1].at[self.lo], self.rx[1], 5, self.spot.xp)
        self.push(self.zk[2].at[self.hi], self.ry[1], 8, self.spot.yp)

    def across(self):
        self.push(self.zk[3].at[self.lo], self.rx[0], 4, self.spot.xp)
        self.push(self.zk[3].at[self.hi], self.ry[0], 7, self.spot.yp)

    def turn(self):
        lo, hi = self.lo, self.hi
        self.arrive(self.rx[0], 4)
        self.zk[2][lo] = plus(self.zk[2][lo], self.rx[0][...])
        self.push(self.zk[2].at[lo], self.ry[2], 9, self.spot.yp)
        self.arrive(self.ry[0], 7)
        self.zk[1][hi] = plus(self.zk[1][hi], self.ry[0][...])
        self.push(self.zk[1].at[hi], self.rx[2], 6, self.spot.xp)

    def total(self):
        self.arrive(self.rx[1], 5)
        self.arrive(self.ry[1], 8)
        self.arrive(self.rx[2], 6)
        self.arrive(self.ry[2], 9)
        return (
            (self.lo, (self.zk[0][self.lo], self.rx[1][...], self.ry[2][...])),
            (self.hi, (self.zk[0][self.hi], self.rx[2][...], self.ry[1][...])),
        )

    def done(self):
        self.given()
        for copy in self.sent:
            copy.wait_send()


def plane_of(spot, zcr, zk, rx, ry, s, r, low=None):
    four, block = range(4), zk.shape[1]
    lo, hi = pl.ds(0, low or block // 2), pl.ds(0, block - (low or block // 2))
    return Plane(
        spot,
        [zcr.at[q] for q in four],
        [zk.at[q] for q in four],
        [rx.at[0, lo], rx.at[1, lo], rx.at[2, hi]],
        [ry.at[0, hi], ry.at[1, hi], ry.at[2, lo]],
        s,
        r,
        low=low,
    )


def plane_scratch(block, wide, low=None):
    most = max(low or block // 2, block - (low or block // 2))
    return [
        pltpu.VMEM((4, block, wide), BF16),
        pltpu.VMEM((4, block, wide), BF16),
        pltpu.VMEM((3, most, wide), BF16),
        pltpu.VMEM((3, most, wide), BF16),
        pltpu.SemaphoreType.DMA((10,)),
        pltpu.SemaphoreType.DMA((10,)),
    ]


def summed(terms):
    total = terms[0].astype(F32)
    for term in terms[1:]:
        total = total + term.astype(F32)
    return total


class Line:
    def __init__(self, spot, own, adder, buf, s, r):
        z, last = spot.z, spot.parts - 1
        e, c = spot.e, spot.c
        self.own, self.adder, self.buf, self.s, self.r = own, adder, buf, s, r
        self.z, self.last, self.parts = z, last, spot.parts
        self.ways = [(z, (e, c, z + 1), lambda d: d), (last - z, (e, c, z - 1), lambda d: last - d)]

    def step(self, turn):
        for way, (i, dev, part) in enumerate(self.ways):
            to, s, r = self.buf.at[way, turn - 1], self.s.at[way, turn - 1], self.r.at[way, turn - 1]

            @pl.when(i == 0)
            def _():
                remote(self.own(part(self.parts - turn)), to, s, r, dev).start()

            if turn >= 2:
                came, s_came, r_came = (x.at[way, turn - 2] for x in (self.buf, self.s, self.r))

                @pl.when((i >= 1) & (i <= turn - 1) & (i < self.last))
                def _():
                    remote(came, came, s_came, r_came, dev).wait_recv()
                    self.adder(came, part(self.parts - turn + i))
                    remote(came, to, s, r, dev).start()

    def final(self, put):
        last, z = self.last, self.z
        for way, (i, dev, _) in enumerate(self.ways):
            came = self.buf.at[way, last - 1]

            @pl.when(i >= 1)
            def _():
                remote(came, came, self.s.at[way, last - 1], self.r.at[way, last - 1], dev).wait_recv()

        up, down = self.buf.at[0, last - 1], self.buf.at[1, last - 1]
        pl.when(z == 0)(lambda: put(down))
        pl.when(z == last)(lambda: put(up))
        pl.when((z > 0) & (z < last))(lambda: put(up, down))

    def done(self):
        for way, (i, dev, _) in enumerate(self.ways):
            for turn in range(1, self.parts):
                came = self.buf.at[way, turn - 1]

                @pl.when((i <= turn - 1) & (i < self.last))
                def _():
                    remote(came, came, self.s.at[way, turn - 1], self.r.at[way, turn - 1], dev).wait_send()


def line_scratch(parts, piece):
    return [
        pltpu.VMEM((2, parts - 1) + piece, BF16),
        pltpu.SemaphoreType.DMA((2, parts - 1)),
        pltpu.SemaphoreType.DMA((2, parts - 1)),
    ]


class ExpertLine:
    def __init__(self, spot, ref, at, cols, buf, s, r, fin, spread, a_s, a_r):
        self.spot, self.ref, self.at, self.cols = spot, ref, at, cols
        self.fin, self.spread, self.a_s, self.a_r = fin, spread, a_s, a_r
        self.line = Line(spot, self.own, self.adder, buf, s, r)
        self.step = self.line.step

    def own(self, d):
        return self.ref.at[:, d, :, pl.ds(self.at, self.cols)]

    def piece(self, cc, d):
        return self.ref[cc, d, :, self.at : self.at + self.cols]

    def adder(self, came, d):
        for cc in range(self.spot.ctx):
            came[cc] = plus(came[cc], self.piece(cc, d))

    def final(self):
        spot = self.spot

        def put(*came):
            for cc in range(spot.ctx):
                self.fin[cc] = plus(self.piece(cc, spot.z), *(x[cc] for x in came))

        self.line.final(put)
        for step in range(1, spot.ctx):
            cc = lax.rem(spot.c + step, spot.ctx)
            remote(
                self.fin.at[cc],
                self.spread.at[spot.c],
                self.a_s.at[step - 1],
                self.a_r.at[step - 1],
                (spot.e, cc, spot.z),
            ).start()

    def done(self, out):
        spot = self.spot
        for step in range(1, spot.ctx):
            cc = lax.rem(spot.c + spot.ctx - step, spot.ctx)
            got = remote(
                self.spread.at[cc],
                self.spread.at[cc],
                self.a_s.at[step - 1],
                self.a_r.at[step - 1],
                (spot.e, cc, spot.z),
            )
            got.wait_recv()
            got.wait_send()
            out[cc] = self.spread[cc]
        out[spot.c] = self.fin[spot.c]
        self.line.done()


def expert_scratch(ctx, parts, rows, cols):
    return line_scratch(parts, (ctx, rows, cols)) + [
        pltpu.VMEM((ctx, rows, cols), BF16),
        pltpu.VMEM((ctx, rows, cols), BF16),
        pltpu.SemaphoreType.DMA((ctx - 1,)),
        pltpu.SemaphoreType.DMA((ctx - 1,)),
    ]


class Gather:
    def __init__(self, spot, own, buf, s, r, low=None):
        self.spot, self.own, self.buf, self.s, self.r = spot, own, buf, s, r
        low = low or own.shape[0] // 2
        self.lo, self.hi = pl.ds(0, low), pl.ds(low, own.shape[0] - low)
        self.x_me, self.y_me, self.d_me = (base + spot.k for base in spot.chips[1:])
        self.side = 1 - 2 * spot.k
        self.sent = []

    def push(self, src, dst, i, dev):
        copy = remote(src, dst, self.s.at[i], self.r.at[i], dev)
        copy.start()
        self.sent.append(copy)

    def move(self, p, rows, i, dev):
        self.push(self.buf.at[p, rows], self.buf.at[p, rows], i, dev)

    def got(self, p, rows, i):
        to = self.buf.at[p, rows]
        remote(to, to, self.s.at[i], self.r.at[i], self.spot.kp).wait_recv()

    def start(self):
        me, own, lo, hi = self.spot.me, self.own, self.lo, self.hi
        self.push(own.at[lo], self.buf.at[me, lo], 0, self.spot.xp)
        self.push(own.at[lo], self.buf.at[me, lo], 6, self.spot.kp)
        self.push(own.at[hi], self.buf.at[me, hi], 13, self.spot.kp)
        self.push(own.at[hi], self.buf.at[me, hi], 1, self.spot.xp)

    def start_y(self):
        me, own, lo, hi = self.spot.me, self.own, self.lo, self.hi
        self.push(own.at[hi], self.buf.at[me, hi], 3, self.spot.yp)
        self.push(own.at[lo], self.buf.at[me, lo], 2, self.spot.yp)

    def first(self):
        spot = self.spot
        self.got(self.x_me, self.lo, 0)
        self.move(self.x_me, self.lo, 4, spot.yp)
        self.move(self.x_me, self.lo, 7, spot.kp)
        self.got(self.y_me, self.hi, 3)
        self.move(self.y_me, self.hi, 5, spot.xp)
        self.move(self.y_me, self.hi, 10, spot.kp)

    def second(self):
        self.got(self.x_me, self.hi, 1)
        self.move(self.x_me, self.hi, 8, self.spot.kp)
        self.got(self.y_me, self.lo, 2)
        self.move(self.y_me, self.lo, 9, self.spot.kp)

    def third(self):
        self.got(self.d_me, self.lo, 4)
        self.move(self.d_me, self.lo, 11, self.spot.kp)
        self.got(self.d_me, self.hi, 5)
        self.move(self.d_me, self.hi, 12, self.spot.kp)

    def other_core(self, q):
        low_sem, high_sem = ((6, 13), (7, 8), (9, 10), (11, 12))[q]
        p = (self.spot.me, self.x_me, self.y_me, self.d_me)[q] + self.side
        self.got(p, self.lo, low_sem)
        self.got(p, self.hi, high_sem)

    def done(self):
        for copy in self.sent:
            copy.wait_send()


GATHER_COPIES = 14


def front_kernel(
    cap,
    span,
    hidden,
    cot,
    gain_one,
    freqs,
    gain_two,
    router_t,
    ids_t,
    turn_t,
    wqkv_h,
    wout_h,
    normed,
    queries,
    kv,
    lse,
    attended,
    resid,
    ffn_in,
    trig,
    meta,
    cot_all,
    wqkv,
    wout,
    mask,
    vt,
    load_sem,
    kv_s,
    kv_r,
    co_s,
    co_r,
):
    spot = Spot()
    c, ctx, k = spot.c, spot.ctx, spot.k
    tok, width = hidden.shape
    group = HEADS // KV_HEADS
    kv_cols = KV_HEADS * HEAD
    half_head = HEAD // 2
    seq = kv.shape[0]
    spans = span.shape[1]
    size = seq // spans
    mine = spans // ctx
    n_experts = meta.shape[0]
    loads = [
        pltpu.make_async_copy(wqkv_h.at[:, pl.ds(width, 2 * kv_cols)], wqkv.at[:, pl.ds(width, 2 * kv_cols)], load_sem.at[0]),
        pltpu.make_async_copy(wqkv_h.at[:, pl.ds(0, width)], wqkv.at[:, pl.ds(0, width)], load_sem.at[1]),
        pltpu.make_async_copy(wout_h, wout, load_sem.at[2]),
        pltpu.make_async_copy(cot, cot_all.at[spot.me], load_sem.at[3]),
    ]
    for load in loads:
        load.start()
    greet([spot.xp, spot.yp, spot.kp])
    gather = Gather(spot, cot, cot_all, co_s, co_r, low=FRONT_LOW)
    gather.start()

    x = hidden[...].astype(F32)
    inv = lax.rsqrt(jnp.mean(x * x, axis=-1, keepdims=True) + NORM_EPS)
    normed[...] = (x * inv * gain_one[...]).astype(BF16)

    along = lax.broadcasted_iota(jnp.int32, (tok, HEAD), 0)
    start_one, start_two = span[0, c * mine] * size, (span[0, c * mine + 1] - 1) * size
    place = jnp.where(along < size, start_one, start_two) + along
    angle = place.astype(F32) * freqs[...]
    cosine, sine = jnp.cos(angle), jnp.sin(angle)
    lane = lax.broadcasted_iota(jnp.int32, (tok, HEAD), 1)
    sine = jnp.where(lane < half_head, -sine, sine)
    trig[0] = cosine
    trig[1] = sine

    def rotate_in(w):
        return w * cosine + pltpu.roll(w, half_head, 1) * sine

    loads[0].wait()
    raw = dot(normed[...], wqkv[:, width:])
    own = rows_at(c * tok, tok)
    for g in range(KV_HEADS):
        at = slice(g * HEAD, (g + 1) * HEAD)
        kv[own, at] = rotate_in(raw[:, at]).astype(BF16)
    kv[own, kv_cols:] = raw[:, kv_cols:].astype(BF16)

    def kv_copy(rows, i, dev):
        return remote(kv.at[rows], kv.at[rows], kv_s.at[i], kv_r.at[i], dev)

    flip_c = lax.rem(c + 2, ctx)
    near_c = c + 1 - 2 * k
    across_c = lax.rem(near_c + 2, ctx)
    sent = [kv_copy(own, 1, spot.yp), kv_copy(own, 0, spot.kp)]
    for copy in sent:
        copy.start()
    gather.start_y()

    loads[1].wait()
    step = 256

    @pl.loop(0, width // step)
    def _(n):
        at = lanes(n * step, step)
        raw = dot(normed[...], wqkv[:, at])
        for i in range(step // HEAD):
            w = raw[:, i * HEAD : (i + 1) * HEAD]
            queries[:, lanes(n * step + i * HEAD, HEAD)] = (rotate_in(w) * HEAD**-0.5).astype(BF16)

    flip = rows_at(flip_c * tok, tok)
    kv_copy(flip, 1, spot.kp).wait_recv()
    sent.append(kv_copy(flip, 2, spot.kp))
    sent[-1].start()

    expert = lax.broadcasted_iota(jnp.int32, (n_experts, tok), 0)
    never = tok * ids_t.shape[0]
    turn = jnp.full((n_experts, tok), never, jnp.int32)
    for i in range(ids_t.shape[0]):
        turn = jnp.where(ids_t[i : i + 1, :] == expert, turn_t[i : i + 1, :], turn)
    turn_f = turn.astype(F32)
    tall = jnp.concatenate([turn_f, jnp.full((HEAD - n_experts, tok), float(never), F32)], axis=0).T
    meta[...] = jnp.zeros(meta.shape, F32)
    for g in range(n_experts):
        row = turn_f[g : g + 1, :]
        rank = jnp.sum(jnp.where(tall[:, g : g + 1] < row, 1.0, 0.0), axis=0, keepdims=True)
        meta[g, 0:1, :] = jnp.where((row < never) & (rank < cap), rank, -1.0)

    along_q = lax.broadcasted_iota(jnp.int32, (size, tok), 1)
    q_pos = jnp.where(along_q < size, start_one, start_two) + along_q
    for s in range(spans):
        k_pos = span[0, s] * size + lax.broadcasted_iota(jnp.int32, (size, tok), 0)
        mask[s * size : (s + 1) * size, :] = jnp.where(k_pos <= q_pos, 0.0, MASKED)

    near, across = rows_at(near_c * tok, tok), rows_at(across_c * tok, tok)
    kv_copy(near, 0, spot.kp).wait_recv()
    kv_copy(across, 2, spot.kp).wait_recv()
    for g in range(KV_HEADS):
        vt[g] = kv[:, kv_cols + g * HEAD : kv_cols + (g + 1) * HEAD].astype(F32).T.astype(BF16)
    lse[...] = jnp.zeros(lse.shape, F32)

    def heads(g, first, count):
        @pl.loop(first, first + count)
        def _(h):
            at = lanes(h * HEAD, HEAD)
            scores = dot_nt(kv[:, g * HEAD : (g + 1) * HEAD], queries[:, at]) + mask[...]
            top = jnp.max(scores, axis=0, keepdims=True)
            weights = jnp.exp(scores - top)
            total = jnp.sum(weights, axis=0, keepdims=True)
            lse[pl.ds(h, 1), :] = top + jnp.log(total)
            out = dot(vt[g], weights.astype(BF16)) / total
            attended[:, at] = out.T.astype(BF16)

    heads(0, 0, 3)
    gather.first()
    heads(0, 3, 3)
    heads(1, 6, 3)
    gather.second()
    heads(1, 9, 3)

    loads[2].wait()

    @pl.loop(0, width // step)
    def _(n):
        at = lanes(n * step, step)
        resid[:, at] = hidden[:, at].astype(F32) + dot_nt(attended[...], wout[at, :])

    r = resid[...]
    inv = lax.rsqrt(jnp.mean(r * r, axis=-1, keepdims=True) + NORM_EPS)
    ffn_in[...] = (r * inv * gain_two[...]).astype(BF16)
    logits = dot_nt(router_t[...], ffn_in[...])[:n_experts]
    logits = jnp.where(turn < never, logits, MASKED)
    shifted = jnp.exp(logits - jnp.max(logits, axis=0, keepdims=True))
    gates = shifted / jnp.sum(shifted, axis=0, keepdims=True)
    for g in range(n_experts):
        meta[g, 1:2, :] = gates[g : g + 1, :]
    gather.third()
    for q in range(4):
        gather.other_core(q)
    loads[3].wait()
    gather.done()
    for copy in sent:
        copy.wait_send()


def run_front(cap, span, hidden, cot, gain_one, freqs, gain_two, router_t, ids_t, turn_t, wqkv, wout, ctx, planes):
    tok, width = hidden.shape
    seq = tok * ctx
    n_experts = planes
    kv_cols = 2 * KV_HEADS * HEAD
    vm, anyspace = pl.BlockSpec(memory_space=pltpu.VMEM), pl.BlockSpec(memory_space=pl.ANY)
    sm = pl.BlockSpec(memory_space=pltpu.SMEM)
    shape = jax.ShapeDtypeStruct
    dma = pltpu.SemaphoreType.DMA
    return pl.pallas_call(
        functools.partial(front_kernel, cap),
        out_shape=(
            shape((tok, width), BF16),
            shape((tok, width), BF16),
            shape((seq, kv_cols), BF16),
            shape((16, tok), F32),
            shape((tok, width), BF16),
            shape((tok, width), F32),
            shape((tok, width), BF16),
            shape((2, tok, HEAD), F32),
            shape((n_experts, 8, tok), F32),
            shape((planes, tok, width), BF16),
        ),
        in_specs=[sm] + [vm] * 8 + [anyspace] * 2,
        out_specs=(vm,) * 9 + (anyspace,),
        scratch_shapes=[
            pltpu.VMEM(wqkv.shape, BF16),
            pltpu.VMEM(wout.shape, BF16),
            pltpu.VMEM((seq, tok), F32),
            pltpu.VMEM((KV_HEADS, HEAD, seq), BF16),
            dma((4,)),
            dma((3,)),
            dma((3,)),
            dma((GATHER_COPIES,)),
            dma((GATHER_COPIES,)),
        ],
        compiler_params=pltpu.CompilerParams(
            collective_id=4, has_side_effects=True, vmem_limit_bytes=56 * 2**20
        ),
        cost_estimate=pl.CostEstimate(flops=5 * 10**9, bytes_accessed=20 * 10**6, transcendentals=4 * 10**6),
    )(span, hidden, cot, gain_one, freqs, gain_two, router_t, ids_t, turn_t, wqkv, wout)


def ffn_kernel(cap, ffn_h, resid_h, cot_h, meta, win_h, wdn_h, output, pg_out, gg_out, gwin_h, ex_out, first_out, *scratch):
    agb, metas, cotb, win, wdn, xs, ds, hid, igs, pgs, ggs, ggr, wint, gwdn = scratch[:14]
    load_sem, ag_s, ag_r, me_s, me_r, gg_s, gg_r, out_s, out_r = scratch[14:23]
    plane_refs, line_refs, first_refs = scratch[23:29], scratch[29:36], scratch[36:]
    spot = Spot()
    c, k, me = spot.c, spot.k, spot.me
    kp = spot.kp
    tok, width = output.shape
    ff = wdn.shape[1]
    planes, ctx = spot.planes, spot.ctx
    chips = spot.chips

    loads = [
        pltpu.make_async_copy(win_h.at[c], win, load_sem.at[0]),
        pltpu.make_async_copy(wdn_h.at[c], wdn, load_sem.at[1]),
        pltpu.make_async_copy(cot_h, cotb, load_sem.at[2]),
        pltpu.make_async_copy(resid_h, pg_out, load_sem.at[3]),
    ]
    own_load = pltpu.make_async_copy(ffn_h, agb.at[me], load_sem.at[4])
    own_load.start()
    for load in loads:
        load.start()
    others = spot.others()
    greet([dev for _, dev in others], spot.along())
    plane = plane_of(spot, *plane_refs)
    o_lo, o_hi = pl.ds(0, OUT_LOW), pl.ds(OUT_LOW, tok - OUT_LOW)
    outs = Plane(
        spot,
        [agb.at[2 * i + k] for i in range(4)],
        [cotb.at[base + k] for base in chips],
        [agb.at[1 - k, o_lo], agb.at[3 - k, o_lo], agb.at[1 - k, o_hi]],
        [agb.at[3 - k, o_hi], agb.at[5 - k, o_hi], agb.at[5 - k, o_lo]],
        out_s,
        out_r,
        [agb.at[2 * i + 1 - k] for i in range(4)],
        low=OUT_LOW,
    )
    line = ExpertLine(spot, gwdn, 0, ff, *line_refs)
    some = first_out.shape[2]
    first_line = ExpertLine(spot, win, 0, some, *first_refs)
    gather = Gather(spot, agb.at[me], agb, ag_s, ag_r)
    for step, (other, dev) in enumerate(others):
        remote(meta.at[other], metas.at[me], me_s.at[step], me_r.at[step], dev).start()
    own_load.wait()
    gather.start()
    gather.start_y()
    metas[me] = meta[me]
    slot_rows = lax.broadcasted_iota(jnp.int32, (cap, tok), 0).astype(F32)
    step = 256

    def spots(p):
        return jnp.where(slot_rows == metas[p, 0:1, :], 1.0, 0.0)

    def gate_of(p, hot):
        return jnp.sum(hot * metas[p, 1:2, :], axis=1, keepdims=True)

    def dispatch(q):
        for kk in range(2):
            p = chips[q] + kk
            hot = spots(p)
            low = hot.astype(BF16)
            part = pl.ds(q * 2 * cap + kk * cap, cap)
            xs[part, :] = dot(low, agb[p]).astype(BF16)
            ds[part, :] = (dot(low, cotb[p]) * gate_of(p, hot)).astype(BF16)

    def work(q, count):
        rows = pl.ds(q * 2 * cap, count * 2 * cap)

        @pl.loop(0, ff // step)
        def _(n):
            gate_cols, up_cols = lanes(n * step, step), lanes(ff + n * step, step)
            x = xs[rows, :]
            g = dot(x, win[:, :, :, gate_cols].reshape(width, step))
            u = dot(x, win[:, :, :, up_cols].reshape(width, step))
            s = 1.0 / (1.0 + jnp.exp(-g))
            act = g * s
            hid[rows, gate_cols] = (act * u).astype(BF16)
            h = dot(ds[rows, :], wdn[:, gate_cols])
            igs[rows, gate_cols] = (h * u * (s * (1.0 + g * (1.0 - s)))).astype(BF16)
            igs[rows, up_cols] = (h * act).astype(BF16)

        @pl.loop(0, width // step)
        def _(n):
            cols = lanes(n * step, step)
            pgs[pl.ds(0, count * 2 * cap), cols] = dot(igs[rows, :], wint[:, cols]).astype(BF16)

    def back(q, at):
        base = chips[q]
        mine, theirs = rows_at(at * 2 * cap + k * cap, cap), rows_at(at * 2 * cap + (1 - k) * cap, cap)
        given = agb.at[base + 1 - k]
        given[...] = dot_tn(spots(base + 1 - k).astype(BF16), pgs[theirs, :]).astype(BF16)
        plane.give(q, given)
        plane.zk[q][...] = dot_tn(spots(base + k).astype(BF16), pgs[mine, :]).astype(BF16)

    for load in loads:
        load.wait()

    tall = width // ctx

    @pl.loop(0, ctx)
    def _(n):
        wint[:, lanes(n * tall, tall)] = win[n].reshape(tall, 2 * ff).T

    for n in range(planes - 1):
        source = lax.rem(me + planes - 1 - n, planes)
        remote(metas.at[source], metas.at[source], me_s.at[n], me_r.at[n], kp).wait_recv()
    gather.other_core(0)
    dispatch(0)
    work(0, 1)
    back(0, 0)
    gather.first()
    gather.second()
    gather.other_core(1)
    dispatch(1)
    gather.other_core(2)
    dispatch(2)
    work(1, 2)
    gather.third()
    back(1, 0)
    back(2, 1)
    gather.other_core(3)
    gather.done()
    dispatch(3)
    plane.fold(1)
    plane.fold(2)
    plane.near()
    work(3, 1)
    back(3, 0)
    plane.fold(3)
    plane.given()
    plane.across()


    @pl.loop(0, ctx)
    def _(n):
        tile = dot_tn(ds[:, lanes(n * tall, tall)], hid[...]).astype(BF16)
        for d in range(gwdn.shape[1]):
            gwdn[n, d] = tile[d * gwdn.shape[2] : (d + 1) * gwdn.shape[2]]

    line.step(1)
    plane.fold(0)

    @pl.loop(0, width // step)
    def _(n):
        cols = lanes(n * step, step)
        ds[:, cols] = dot_nt(hid[...], wdn[cols, :]).astype(BF16)

    def returned(q):
        base = chips[q]
        for kk in range(2):
            p = base + kk
            hot = spots(p)
            rows = ds[pl.ds(q * 2 * cap + kk * cap, cap), :]
            ggs[p, 0:1, :] = jnp.sum(hot * dot_nt(rows, cotb[p]), axis=0, keepdims=True)
            scaled = (rows.astype(F32) * gate_of(p, hot)).astype(BF16)
            cotb[p] = dot_tn(hot.astype(BF16), scaled).astype(BF16)
        outs.give(q, cotb.at[base + 1 - k])

    returned(1)
    returned(2)
    plane.turn()
    returned(3)
    returned(0)
    outs.fold(1)
    outs.fold(2)
    outs.near()
    outs.fold(3)
    outs.across()
    ggr[me] = ggs[me]
    for n, (other, dev) in enumerate(others):
        remote(ggs.at[other], ggr.at[me], gg_s.at[n], gg_r.at[n], dev).start()
    line.step(2)
    outs.fold(0)

    def gate_up(at, size):
        @pl.loop(0, ctx)
        def _(n):
            tile = dot_tn(xs[:, lanes(n * tall, tall)], igs[:, pl.ds(at, size)]).astype(BF16)
            win[n, :, :, pl.ds(at, size)] = tile.reshape(gwdn.shape[1], gwdn.shape[2], size)

    gate_up(0, some)
    rest = 2 * ff - some
    gate_up(some, rest // 2)
    gate_up(some + rest // 2, rest // 2)
    gwin_copy = pltpu.make_async_copy(win.at[:, :, :, pl.ds(some, rest)], gwin_h, load_sem.at[0])
    gwin_copy.start()
    line.step(3)
    first_line.step(1)
    outs.turn()
    first_line.step(2)
    line.final()
    for rows, terms in outs.total():
        output[rows, :] = (pg_out[rows, :] + summed(terms)).astype(BF16)
    for rows, terms in plane.total():
        pg_out[rows, :] = summed(terms)
    for n in range(planes - 1):
        source = lax.rem(me + planes - 1 - n, planes)
        remote(ggr.at[source], ggr.at[source], gg_s.at[n], gg_r.at[n], kp).wait_recv()
    for p in range(planes):
        gg_out[p : p + 1, :] = ggr[p, 0:1, :]
    first_line.step(3)
    first_line.final()
    gwin_copy.wait()
    for n, (other, dev) in enumerate(others):
        remote(meta.at[other], metas.at[other], me_s.at[n], me_r.at[n], dev).wait_send()
        remote(ggs.at[other], ggr.at[other], gg_s.at[n], gg_r.at[n], dev).wait_send()
    plane.done()
    outs.done()
    line.done(ex_out)
    first_line.done(first_out)


def run_ffn(cap, ffn, resid, cot_all, meta, win, wdn, parts, some):
    tok, width = ffn.shape
    ff = wdn.shape[2]
    planes = cot_all.shape[0]
    ctx = win.shape[0]
    rows = planes * cap
    piece = width // (ctx * parts)
    win = win.reshape(ctx, ctx, parts, piece, 2 * ff)
    vm, anyspace = pl.BlockSpec(memory_space=pltpu.VMEM), pl.BlockSpec(memory_space=pl.ANY)
    shape = jax.ShapeDtypeStruct
    dma = pltpu.SemaphoreType.DMA
    return pl.pallas_call(
        functools.partial(ffn_kernel, cap),
        out_shape=(
            shape((tok, width), BF16),
            shape((tok, width), F32),
            shape((planes, tok), F32),
            shape((ctx, parts, piece, 2 * ff - some), BF16),
            shape((ctx, piece, ff), BF16),
            shape((ctx, piece, some), BF16),
        ),
        in_specs=[anyspace, anyspace, anyspace, vm, anyspace, anyspace],
        out_specs=(vm, vm, vm, anyspace, vm, vm),
        scratch_shapes=[
            pltpu.VMEM((planes, tok, width), BF16),
            pltpu.VMEM((planes, 8, tok), F32),
            pltpu.VMEM((planes, tok, width), BF16),
            pltpu.VMEM((ctx, parts, piece, 2 * ff), BF16),
            pltpu.VMEM((width, ff), BF16),
            pltpu.VMEM((rows, width), BF16),
            pltpu.VMEM((rows, width), BF16),
            pltpu.VMEM((rows, ff), BF16),
            pltpu.VMEM((rows, 2 * ff), BF16),
            pltpu.VMEM((4 * cap, width), BF16),
            pltpu.VMEM((planes, 8, tok), F32),
            pltpu.VMEM((planes, 8, tok), F32),
            pltpu.VMEM((2 * ff, width), BF16),
            pltpu.VMEM((ctx, parts, piece, ff), BF16),
            dma((5,)),
            dma((GATHER_COPIES,)),
            dma((GATHER_COPIES,)),
            dma((planes - 1,)),
            dma((planes - 1,)),
            dma((planes - 1,)),
            dma((planes - 1,)),
            dma((10,)),
            dma((10,)),
        ]
        + plane_scratch(tok, width)
        + expert_scratch(ctx, parts, piece, ff)
        + expert_scratch(ctx, parts, piece, some),
        compiler_params=pltpu.CompilerParams(
            collective_id=1, has_side_effects=True, vmem_limit_bytes=63 * 2**20
        ),
        cost_estimate=pl.CostEstimate(flops=25 * 10**9, bytes_accessed=50 * 10**6, transcendentals=10**6),
    )(ffn, resid, cot_all, meta, win, wdn)


def back_kernel(
    span,
    meta,
    gg,
    lse,
    trig,
    kv,
    queries,
    attended,
    normed,
    router_t,
    gain_two,
    gain_one,
    resid_h,
    cot_h,
    pg_h,
    ffn_in_h,
    hidden_h,
    wout_h,
    wqkv_h,
    gwin_h,
    input_grad,
    qkv_out,
    proj_out,
    one_out,
    two_out,
    *scratch,
):
    wide_f, back, low, attg, mixed, weights, gwin, send, bsend, smalls, total, out_red = scratch[:12]
    mask, delta, kt, dk, dv, kvs, kvr = scratch[12:19]
    load_sem, kv_s, kv_r = scratch[19:22]
    p_zcr, p_zk, p_rx, p_ry, p_s, p_r = scratch[22:28]
    a_rx, a_ry, a_s, a_r = scratch[28:32]
    b_refs, qkv_refs, proj_refs = scratch[32:38], scratch[38:41], scratch[41:44]
    one_refs, two_refs = scratch[44:51], scratch[51:58]
    spot = Spot()
    c, k, z, ctx = spot.c, spot.k, spot.z, spot.ctx
    tok, width = attended.shape
    cols = one_out.shape[2]
    block, piece = out_red.shape[0], proj_out.shape[0]
    heads_kv = KV_HEADS
    half_head = HEAD // 2
    n_experts = meta.shape[0]
    kv_wide = mixed.shape[1] - width
    step = 256

    def load(src, dst, i):
        copy = pltpu.make_async_copy(src, dst, load_sem.at[i])
        copy.start()
        return copy

    gwin_load = load(gwin_h, gwin, 0)
    early = [
        load(resid_h, wide_f, 1),
        load(pg_h, back, 2),
        load(cot_h, input_grad, 3),
        load(ffn_in_h, attg, 4),
    ]
    wout_load = load(wout_h, weights.at[:, pl.ds(0, width)], 5)
    greet([spot.xp, spot.yp, spot.kp, spot.yk], spot.along())
    one = ExpertLine(spot, gwin, 0, cols, *one_refs)
    two = ExpertLine(spot, gwin, cols, cols, *two_refs)
    proj_plane = plane_of(spot, p_zcr, p_zk, p_rx, p_ry, p_s, p_r, low=BACK_LOW)
    qkv_plane = plane_of(spot, p_zcr, p_zk, a_rx, a_ry, a_s, a_r, low=BACK_LOW)
    rest_plane = plane_of(spot, *b_refs, low=BACK_LOW)

    def shared_line(ref, refs):
        def own(d):
            return ref.at[rows_at(d * piece, piece)]

        def adder(came, d):
            came[...] = plus(came[...], own(d)[...])

        return Line(spot, own, adder, *refs)

    qkv_line, proj_line = shared_line(total, qkv_refs), shared_line(out_red, proj_refs)

    def put_shared(to, ref, came):
        to[...] = plus(ref[rows_at(z * piece, piece)], *(x[...] for x in came))

    mine, theirs = rows_at(k * block, block), rows_at((1 - k) * block, block)
    gwin_load.wait()
    one.step(1)

    for copy in early:
        copy.wait()
    gate = jnp.concatenate([meta[g, 1:2, :] for g in range(n_experts)], axis=0)
    seen = gate * gg[...]
    mix = seen - gate * jnp.sum(seen, axis=0, keepdims=True)
    mix = jnp.concatenate([mix, jnp.zeros((HEAD - n_experts, tok), F32)], axis=0)
    logit_t = mix.astype(BF16)
    r = wide_f[...]
    inv = lax.rsqrt(jnp.mean(r * r, axis=-1, keepdims=True) + NORM_EPS)
    plain = r * inv
    ffn_grad = back[...] + dot_tn(logit_t[:n_experts], router_t[...])
    gain_row = jnp.sum(ffn_grad * plain, axis=0, keepdims=True)
    scaled = ffn_grad * gain_two[...]
    grad = input_grad[...].astype(F32) + inv * (
        scaled - plain * jnp.mean(scaled * plain, axis=-1, keepdims=True)
    )
    back[...] = grad
    low[...] = grad.astype(BF16)
    lane = lax.broadcasted_iota(jnp.int32, (width, HEAD), 1)
    routed = dot_tn(attg[...], logit_t.T)
    gain_col = jnp.broadcast_to(gain_row, (HEAD, width)).T
    smalls[...] = jnp.where(lane == n_experts, gain_col, routed).astype(BF16)

    for q in (1, 2, 3, 0):
        at = lanes(spot.chips[q] * block, 2 * block)
        send[q] = dot_tn(low[:, at], attended[...]).astype(BF16)
        proj_plane.give(q, send.at[q, theirs])
    wout_load.wait()

    @pl.loop(0, width // step)
    def _(n):
        at = lanes(n * step, step)
        attg[:, at] = dot(low[...], weights[:, at]).astype(BF16)

    wqkv_load = load(wqkv_h, weights, 5)
    hidden_load = load(hidden_h, low, 1)

    def start_plane(plane):
        plane.fold(1, send[1, mine])
        plane.fold(2, send[2, mine])
        plane.near()
        plane.fold(3, send[3, mine])
        plane.across()
        plane.fold(0, send[0, mine])

    start_plane(proj_plane)

    seq = kv.shape[0]
    spans = span.shape[1]
    size = seq // spans
    per = spans // ctx
    along_q = lax.broadcasted_iota(jnp.int32, (size, tok), 1)
    q_pos = jnp.where(along_q < size, span[0, c * per] * size, (span[0, c * per + 1] - 1) * size) + along_q
    for s in range(spans):
        k_pos = span[0, s] * size + lax.broadcasted_iota(jnp.int32, (size, tok), 0)
        mask[s * size : (s + 1) * size, :] = jnp.where(k_pos <= q_pos, 0.0, MASKED)

    lane_h = lax.broadcasted_iota(jnp.int32, (tok, HEAD), 1)
    deltas = jnp.zeros((tok, HEAD), F32)
    for h in range(HEADS):
        at = slice(h * HEAD, (h + 1) * HEAD)
        term = jnp.sum(attg[:, at].astype(F32) * attended[:, at].astype(F32), axis=-1, keepdims=True)
        deltas = jnp.where(lane_h == h, term, deltas)
    delta[...] = deltas.T
    for g in range(heads_kv):
        kt[g] = kv[:, g * HEAD : (g + 1) * HEAD].astype(F32).T.astype(BF16)

    cosine, sine = trig[0], trig[1]

    def unrotate(w):
        return w * cosine - pltpu.roll(w, half_head, 1) * sine

    def head(g, h):
        at = lanes(h * HEAD, HEAD)
        k_at = slice(g * HEAD, (g + 1) * HEAD)
        v_at = slice((heads_kv + g) * HEAD, (heads_kv + g + 1) * HEAD)
        q, a = queries[:, at], attg[:, at]
        soft = jnp.exp(dot_nt(kv[:, k_at], q) + mask[...] - lse[pl.ds(h, 1), :])
        prob = dot_nt(kv[:, v_at], a)
        score = (soft * (prob - delta[pl.ds(h, 1), :])).astype(BF16)
        mixed[:, at] = (unrotate(dot(kt[g], score).T) * HEAD**-0.5).astype(BF16)
        dk[...] += dot(score, q)
        dv[...] += dot(soft.astype(BF16), a)

    def heads(g, first, count):
        @pl.loop(first, first + count)
        def _(h):
            head(g, h)

    def clear():
        dk[...] = jnp.zeros(dk.shape, F32)
        dv[...] = jnp.zeros(dv.shape, F32)

    flip_c = lax.rem(c + 2, ctx)
    near_c = c + 1 - 2 * k
    across_c = lax.rem(near_c + 2, ctx)

    def kv_copy(g, src, i, dev):
        return remote(src, kvr.at[g, i], kv_s.at[g, i], kv_r.at[g, i], dev)

    def send_kv(g):
        for cc in range(ctx):
            rows = slice(cc * tok, (cc + 1) * tok)
            kvs[g, cc, :, :HEAD] = dk[rows, :].astype(BF16)
            kvs[g, cc, :, HEAD:] = dv[rows, :].astype(BF16)
        kv_copy(g, kvs.at[g, across_c], 1, spot.kp).start()
        kv_copy(g, kvs.at[g, near_c], 0, spot.kp).start()

    def pass_kv(g):
        kv_copy(g, kvs.at[g, across_c], 1, spot.kp).wait_recv()
        kvs[g, flip_c] = plus(kvs[g, flip_c], kvr[g, 1])
        kv_copy(g, kvs.at[g, flip_c], 2, spot.yp).start()

    clear()
    heads(0, 0, 2)
    one.step(2)
    heads(0, 2, 4)
    send_kv(0)
    clear()
    proj_plane.turn()
    heads(1, 6, 3)
    pass_kv(0)
    one.step(3)
    two.step(1)
    heads(1, 9, 3)
    send_kv(1)
    pass_kv(1)
    for rows, terms in proj_plane.total():
        out_red[rows, :] = summed(terms).astype(BF16)
    proj_line.step(1)
    proj_plane.done()
    for g in range(heads_kv):
        kv_copy(g, kvs.at[g, near_c], 0, spot.kp).wait_recv()
        kv_copy(g, kvs.at[g, flip_c], 2, spot.yp).wait_recv()
        own = kvs[g, c].astype(F32) + kvr[g, 0].astype(F32) + kvr[g, 2].astype(F32)
        at = width + g * HEAD
        mixed[:, at : at + HEAD] = unrotate(own[:, :HEAD]).astype(BF16)
        at = width + (heads_kv + g) * HEAD
        mixed[:, at : at + HEAD] = own[:, HEAD:].astype(BF16)

    for q in (1, 2, 3, 0):
        at = lanes(spot.chips[q] * block, 2 * block)
        send[q] = dot_tn(normed[:, at], mixed[:, :width]).astype(BF16)
        qkv_plane.give(q, send.at[q, theirs])
    start_plane(qkv_plane)
    proj_line.step(2)
    wqkv_load.wait()

    @pl.loop(0, width // step)
    def _(n):
        at = lanes(n * step, step)
        wide_f[:, at] = dot_nt(mixed[...], weights[at, :])

    two.step(2)
    hidden_load.wait()
    x = low[...].astype(F32)
    inv = lax.rsqrt(jnp.mean(x * x, axis=-1, keepdims=True) + NORM_EPS)
    plain = x * inv
    ng = wide_f[...]
    gain_row = jnp.sum(ng * plain, axis=0, keepdims=True)
    scaled = ng * gain_one[...]
    input_grad[...] = (
        back[...] + inv * (scaled - plain * jnp.mean(scaled * plain, axis=-1, keepdims=True))
    ).astype(BF16)
    lane = lax.broadcasted_iota(jnp.int32, (width, HEAD), 1)
    gain_col = jnp.broadcast_to(gain_row, (HEAD, width)).T
    smalls[...] = jnp.where(lane == HEAD - 1, gain_col, smalls[...].astype(F32)).astype(BF16)
    for q in (1, 2, 3, 0):
        at = lanes(spot.chips[q] * block, 2 * block)
        bsend[q, :, :kv_wide] = dot_tn(normed[:, at], mixed[:, width:]).astype(BF16)
        bsend[q, :, kv_wide:] = smalls[rows_at(spot.chips[q] * block, 2 * block), :]
        rest_plane.give(q, bsend.at[q, theirs])
    rest_plane.fold(1, bsend[1, mine])
    rest_plane.fold(2, bsend[2, mine])
    rest_plane.near()
    rest_plane.fold(3, bsend[3, mine])
    rest_plane.across()
    rest_plane.fold(0, bsend[0, mine])
    qkv_plane.turn()
    rest_plane.turn()
    two.step(3)
    one.final()
    proj_line.step(3)
    for rows, terms in qkv_plane.total():
        total[rows, :width] = summed(terms).astype(BF16)
    for rows, terms in rest_plane.total():
        total[rows, width:] = summed(terms).astype(BF16)
    qkv_line.step(1)
    one.done(one_out)
    qkv_line.step(2)
    proj_line.final(lambda *came: put_shared(proj_out, out_red, came))
    qkv_line.step(3)
    two.final()
    proj_line.done()
    qkv_plane.done()
    rest_plane.done()
    for g in range(heads_kv):
        kv_copy(g, kvs.at[g, near_c], 0, spot.kp).wait_send()
        kv_copy(g, kvs.at[g, across_c], 1, spot.kp).wait_send()
        kv_copy(g, kvs.at[g, flip_c], 2, spot.yp).wait_send()
    qkv_line.final(lambda *came: put_shared(qkv_out, total, came))
    qkv_line.done()
    two.done(two_out)


def run_back(
    span, meta, gg, lse, trig, kv, queries, attended, normed, router_t, gain_two, gain_one,
    resid, cot, pg, ffn_in, hidden, wout, wqkv, gwin,
):
    tok, width = attended.shape
    seq, kv_cols = kv.shape
    planes = meta.shape[0]
    ctx, parts, rows, wide = gwin.shape
    cols = wide // 2
    block = width // planes
    piece = block // parts
    rest = kv_cols + HEAD
    vm, anyspace = pl.BlockSpec(memory_space=pltpu.VMEM), pl.BlockSpec(memory_space=pl.ANY)
    sm = pl.BlockSpec(memory_space=pltpu.SMEM)
    shape = jax.ShapeDtypeStruct
    dma = pltpu.SemaphoreType.DMA
    return pl.pallas_call(
        back_kernel,
        out_shape=(
            shape((tok, width), BF16),
            shape((piece, width + rest), BF16),
            shape((piece, width), BF16),
            shape((ctx, rows, cols), BF16),
            shape((ctx, rows, cols), BF16),
        ),
        in_specs=[sm] + [vm] * 11 + [anyspace] * 8,
        out_specs=(vm,) * 5,
        scratch_shapes=[
            pltpu.VMEM((tok, width), F32),
            pltpu.VMEM((tok, width), F32),
            pltpu.VMEM((tok, width), BF16),
            pltpu.VMEM((tok, width), BF16),
            pltpu.VMEM((tok, width + kv_cols), BF16),
            pltpu.VMEM(wqkv.shape, BF16),
            pltpu.VMEM(gwin.shape, BF16),
            pltpu.VMEM((4, 2 * block, width), BF16),
            pltpu.VMEM((4, 2 * block, rest), BF16),
            pltpu.VMEM((width, HEAD), BF16),
            pltpu.VMEM((block, width + rest), BF16),
            pltpu.VMEM((block, width), BF16),
            pltpu.VMEM((seq, tok), F32),
            pltpu.VMEM((HEAD, tok), F32),
            pltpu.VMEM((KV_HEADS, HEAD, seq), BF16),
            pltpu.VMEM((seq, HEAD), F32),
            pltpu.VMEM((seq, HEAD), F32),
            pltpu.VMEM((KV_HEADS, ctx, tok, 2 * HEAD), BF16),
            pltpu.VMEM((KV_HEADS, 3, tok, 2 * HEAD), BF16),
            dma((6,)),
            dma((KV_HEADS, 3)),
            dma((KV_HEADS, 3)),
        ]
        + plane_scratch(block, width, BACK_LOW)
        + plane_scratch(block, width, BACK_LOW)[2:]
        + plane_scratch(block, rest, BACK_LOW)
        + line_scratch(parts, (piece, width + rest))
        + line_scratch(parts, (piece, width))
        + expert_scratch(ctx, parts, rows, cols)
        + expert_scratch(ctx, parts, rows, cols),
        compiler_params=pltpu.CompilerParams(
            collective_id=2, has_side_effects=True, vmem_limit_bytes=63 * 2**20
        ),
        cost_estimate=pl.CostEstimate(flops=12 * 10**9, bytes_accessed=60 * 10**6, transcendentals=4 * 10**6),
    )(
        span, meta, gg, lse, trig, kv, queries, attended, normed, router_t, gain_two, gain_one,
        resid, cot, pg, ffn_in, hidden, wout, wqkv, gwin,
    )


def finish_kernel(
    n_experts,
    output_h,
    input_h,
    qkv_h,
    proj_h,
    first_h,
    one_h,
    two_h,
    down_h,
    output,
    input_grad,
    gains,
    qkv,
    proj,
    router,
    inner,
    down,
    low_qkv,
    low_proj,
    low_first,
    low_one,
    low_two,
    low_down,
    low_out,
    low_in,
    inner_full,
    down_full,
    sem,
    out_sem,
):
    whole = []
    loads = [
        pltpu.make_async_copy(src, dst, sem.at[i])
        for i, (src, dst) in enumerate(
            (
                (down_h, low_down),
                (first_h, low_first),
                (one_h, low_one),
                (two_h, low_two),
                (qkv_h, low_qkv),
                (proj_h, low_proj),
                (output_h, low_out),
                (input_h, low_in),
            )
        )
    ]
    for copy in loads:
        copy.start()
    loads[0].wait()
    down_full[...] = low_down[...].astype(F32)
    whole.append(pltpu.make_async_copy(down_full, down, out_sem.at[2]))
    whole[-1].start()
    at = 0
    for load, low in zip(loads[1:4], (low_first, low_one, low_two)):
        load.wait()
        size = low.shape[2]
        inner_full[:, :, at : at + size] = low[...].astype(F32)
        at += size
    whole.append(pltpu.make_async_copy(inner_full, inner, out_sem.at[3]))
    whole[-1].start()
    for i, (low, to) in enumerate(((low_out, output), (low_in, input_grad))):
        loads[6 + i].wait()
        whole.append(pltpu.make_async_copy(low, to, out_sem.at[i]))
        whole[-1].start()
    for load in loads[4:6]:
        load.wait()
    wide = qkv.shape[1]
    qkv[...] = low_qkv[:, :wide].astype(F32)
    proj[...] = low_proj[...].astype(F32)
    small = low_qkv[:, wide:].astype(F32)
    router[...] = small[:, :n_experts]
    piece = small.shape[0]
    same = lax.broadcasted_iota(jnp.int32, (piece, piece), 0) == lax.broadcasted_iota(
        jnp.int32, (piece, piece), 1
    )
    for row, col in ((0, HEAD - 1), (1, n_experts)):
        gains[row : row + 1, :] = jnp.sum(jnp.where(same, small[:, col : col + 1], 0.0), axis=0, keepdims=True)
    for copy in whole:
        copy.wait()


def run_finish(n_experts, output, input_grad, qkv, proj, first, one, two, down):
    piece, width = proj.shape
    ctx, rows, ff = down.shape
    shape = jax.ShapeDtypeStruct
    vm, anyspace = pl.BlockSpec(memory_space=pltpu.VMEM), pl.BlockSpec(memory_space=pl.ANY)
    return pl.pallas_call(
        functools.partial(finish_kernel, n_experts),
        out_shape=(
            shape(output.shape, BF16),
            shape(input_grad.shape, BF16),
            shape((2, piece), F32),
            shape((piece, qkv.shape[1] - HEAD), F32),
            shape((piece, width), F32),
            shape((piece, n_experts), F32),
            shape((ctx, rows, 2 * ff), F32),
            shape((ctx, rows, ff), F32),
        ),
        in_specs=[anyspace] * 8,
        out_specs=(anyspace, anyspace, vm, vm, vm, vm, anyspace, anyspace),
        scratch_shapes=[pltpu.VMEM(x.shape, BF16) for x in (qkv, proj, first, one, two, down, output, input_grad)]
        + [
            pltpu.VMEM((ctx, rows, 2 * ff), F32),
            pltpu.VMEM((ctx, rows, ff), F32),
            pltpu.SemaphoreType.DMA((8,)),
            pltpu.SemaphoreType.DMA((4,)),
        ],
        compiler_params=pltpu.CompilerParams(vmem_limit_bytes=56 * 2**20),
    )(output, input_grad, qkv, proj, first, one, two, down)


def local(
    hidden_in,
    span_order,
    expert_ids,
    priority,
    gain_attn,
    qkv_weight,
    out_weight,
    gain_ffn,
    router,
    in_weight,
    down_weight,
    cotangent,
):
    _, tok_rows, width = hidden_in.shape
    ctx, parts = lax.axis_size("context"), lax.axis_size("dp")
    planes = ctx * lax.axis_size("expert")
    n_experts = router.shape[1]
    top_k = expert_ids.shape[2]
    capacity = (9 * tok_rows * top_k + 8 * n_experts - 1) // (8 * n_experts)
    ff = down_weight.shape[2]
    half_freqs = ROPE_BASE ** (np.arange(HEAD // 2) * (-2.0 / HEAD))
    freqs = np.concatenate([half_freqs, half_freqs])[None].astype(np.float32)
    router_t = router.T
    hidden, cot = hidden_in[0], cotangent[0]
    normed, queries, kv, lse, attended, resid, ffn_in, trig, meta, cot_all = run_front(
        capacity,
        span_order,
        hidden,
        cot,
        gain_attn,
        freqs,
        gain_ffn,
        router_t,
        expert_ids[0].T,
        priority[0].T,
        qkv_weight,
        out_weight,
        ctx,
        planes,
    )
    output, pair_sum, gate_grad, gwin, down, in_first = run_ffn(
        capacity, ffn_in, resid, cot_all, meta, in_weight, down_weight, parts, ff // 3
    )
    input_grad, qkv_sum, proj_sum, in_one, in_two = run_back(
        span_order,
        meta,
        gate_grad,
        lse,
        trig,
        kv,
        queries,
        attended,
        normed,
        router_t,
        gain_ffn,
        gain_attn,
        resid,
        cot,
        pair_sum,
        ffn_in,
        hidden,
        out_weight,
        qkv_weight,
        gwin,
    )
    output, input_grad, gains, qkv_grad, proj_grad, router_grad, inner_grad, down_grad = run_finish(
        n_experts, output, input_grad, qkv_sum, proj_sum, in_first, in_one, in_two, down
    )
    return (
        output[None],
        input_grad[None],
        gains[0],
        qkv_grad,
        proj_grad,
        gains[1],
        router_grad,
        inner_grad,
        down_grad,
    )


def general(
    hidden_in,
    span_order,
    expert_ids,
    priority,
    gain_attn,
    qkv_weight,
    out_weight,
    gain_ffn,
    router,
    in_weight,
    down_weight,
    cotangent,
):
    tok_rows = hidden_in.shape[1]
    width = hidden_in.shape[2]
    contexts = lax.axis_size("context")
    span_len = tok_rows // 2
    seq_len = tok_rows * contexts
    group = HEADS // KV_HEADS
    q_cols = HEADS * HEAD
    kv_cols = KV_HEADS * HEAD
    scale = HEAD ** (-0.5)
    local_experts = in_weight.shape[0]
    n_experts = local_experts * lax.axis_size("expert")
    top_k = expert_ids.shape[2]
    capacity = (9 * tok_rows * top_k + 8 * n_experts - 1) // (8 * n_experts)
    ff_width = down_weight.shape[2]
    seq_spans = span_order[0]
    stored = jnp.arange(seq_len) // span_len
    all_pos = (seq_spans[stored] * span_len + jnp.arange(seq_len) % span_len).astype(jnp.float32)
    my_pos = lax.dynamic_slice_in_dim(all_pos, lax.axis_index("context") * tok_rows, tok_rows)
    cosine, sine = rope_tables(my_pos, HEAD)
    inputs = hidden_in[0].astype(jnp.float32)
    inv_one = lax.rsqrt(jnp.mean(inputs * inputs, axis=-1, keepdims=True) + NORM_EPS)
    plain_one = inputs * inv_one
    normed = (plain_one * gain_attn).astype(jnp.bfloat16)
    mixed = jnp.dot(normed, qkv_weight, preferred_element_type=jnp.float32)
    queries = (
        rotate(mixed[:, :q_cols].reshape(tok_rows, HEADS, HEAD), cosine, sine) * scale
    ).astype(jnp.bfloat16)
    keys = rotate(
        mixed[:, q_cols : q_cols + kv_cols].reshape(tok_rows, KV_HEADS, HEAD), cosine, sine
    ).astype(jnp.bfloat16)
    values = mixed[:, q_cols + kv_cols :].reshape(tok_rows, KV_HEADS, HEAD).astype(jnp.bfloat16)
    grouped = queries.reshape(tok_rows, KV_HEADS, group, HEAD)

    def key_scores(key_piece):
        scores = jnp.einsum(
            "qkgd,skd->kgqs", grouped, key_piece, preferred_element_type=jnp.float32
        )
        visible = all_pos[None, None, None, :] <= my_pos[None, None, :, None]
        return (jnp.where(visible, scores, MASKED), visible)

    running = jnp.full((KV_HEADS, group, tok_rows), MASKED, jnp.float32)
    key_piece = lax.all_gather(keys, "context", axis=0, tiled=True)
    value_piece = lax.all_gather(values, "context", axis=0, tiled=True)
    scores, visible = key_scores(key_piece)
    newest = jnp.maximum(running, jnp.max(scores, axis=-1))
    weights = jnp.where(visible, jnp.exp(scores - newest[..., None]), 0.0)
    totals = jnp.sum(weights, axis=-1)
    accum = jnp.einsum(
        "kgqs,skd->kgqd",
        weights.astype(jnp.bfloat16),
        value_piece,
        preferred_element_type=jnp.float32,
    )
    running, totals, accum = (newest, totals, accum)
    log_total = running + jnp.log(totals)
    attended = (
        (accum / totals[..., None])
        .transpose(2, 0, 1, 3)
        .reshape(tok_rows, q_cols)
        .astype(jnp.bfloat16)
    )
    resid = inputs + jnp.einsum(
        "rh,dh->rd", attended, out_weight, preferred_element_type=jnp.float32
    )
    inv_two = lax.rsqrt(jnp.mean(resid * resid, axis=-1, keepdims=True) + NORM_EPS)
    plain_two = resid * inv_two
    ffn_in = (plain_two * gain_ffn).astype(jnp.bfloat16)
    logits = jnp.dot(ffn_in, router, preferred_element_type=jnp.float32)
    token_ids = expert_ids[0]
    gates = softmax_last(jnp.take_along_axis(logits, token_ids, axis=1))
    slots = route(token_ids, priority[0], n_experts, capacity)
    pair_rows = jnp.repeat(ffn_in, top_k, axis=0)
    send_rows = (
        jnp.zeros((n_experts * capacity, width), jnp.bfloat16).at[slots].set(pair_rows, mode="drop")
    )
    received = lax.all_to_all(
        send_rows.reshape(n_experts, capacity, width),
        "expert",
        split_axis=0,
        concat_axis=1,
        tiled=True,
    )
    inner = jnp.einsum("erd,edf->erf", received, in_weight, preferred_element_type=jnp.float32)
    gate_part = inner[..., :ff_width]
    up_part = inner[..., ff_width:]
    sigma = 1.0 / (1.0 + jnp.exp(-gate_part))
    activated = gate_part * sigma
    hidden = (activated * up_part).astype(jnp.bfloat16)
    expert_out = jnp.einsum(
        "erf,edf->erd", hidden, down_weight, preferred_element_type=jnp.float32
    ).astype(jnp.bfloat16)
    returned = lax.all_to_all(
        expert_out, "expert", split_axis=1, concat_axis=0, tiled=True
    ).reshape(n_experts * capacity, width)
    padded = jnp.concatenate([returned, jnp.zeros((1, width), jnp.bfloat16)], axis=0)
    picked = padded[slots].reshape(tok_rows, top_k, width)
    output = (resid + jnp.sum(gates[:, :, None] * picked, axis=1)).astype(jnp.bfloat16)
    cot_low = cotangent[0]
    cot_full = cot_low.astype(jnp.float32)
    gate_grad = jnp.einsum("rkd,rd->rk", picked, cot_low, preferred_element_type=jnp.float32)
    ret_grad = (
        (gates[:, :, None] * cot_full[:, None, :])
        .astype(jnp.bfloat16)
        .reshape(tok_rows * top_k, width)
    )
    send_grad = (
        jnp.zeros((n_experts * capacity, width), jnp.bfloat16).at[slots].set(ret_grad, mode="drop")
    )
    received_grad = lax.all_to_all(
        send_grad.reshape(n_experts, capacity, width),
        "expert",
        split_axis=0,
        concat_axis=1,
        tiled=True,
    )
    hid_grad = jnp.einsum(
        "erd,edf->erf", received_grad, down_weight, preferred_element_type=jnp.float32
    )
    slope = sigma * (1.0 + gate_part * (1.0 - sigma))
    inner_grad = jnp.concatenate(
        [hid_grad * up_part * slope, hid_grad * activated], axis=-1
    ).astype(jnp.bfloat16)
    row_grad = jnp.einsum(
        "erf,edf->erd", inner_grad, in_weight, preferred_element_type=jnp.float32
    ).astype(jnp.bfloat16)
    part_rows = received
    expert_in = (
        lax.psum_scatter(
            jnp.einsum(
                "erd,erf->def", part_rows, inner_grad, preferred_element_type=jnp.float32
            ).astype(jnp.bfloat16),
            ("context", "dp"),
            scatter_dimension=0,
            tiled=True,
        )
        .astype(jnp.float32)
        .transpose(1, 0, 2)
    )
    part_rows = received_grad
    expert_down = (
        lax.psum_scatter(
            jnp.einsum(
                "erd,erf->def", part_rows, hidden, preferred_element_type=jnp.float32
            ).astype(jnp.bfloat16),
            ("context", "dp"),
            scatter_dimension=0,
            tiled=True,
        )
        .astype(jnp.float32)
        .transpose(1, 0, 2)
    )
    back_rows = lax.all_to_all(row_grad, "expert", split_axis=1, concat_axis=0, tiled=True).reshape(
        n_experts * capacity, width
    )
    back_padded = jnp.concatenate([back_rows, jnp.zeros((1, width), jnp.bfloat16)], axis=0)
    pair_grad = back_padded[slots].reshape(tok_rows, top_k, width)
    mix_grad = gates * (gate_grad - jnp.sum(gates * gate_grad, axis=-1, keepdims=True))
    matches = token_ids[:, :, None] == jnp.arange(n_experts)[None, None, :]
    logit_grad = jnp.sum(jnp.where(matches, mix_grad[:, :, None], 0.0), axis=1).astype(jnp.bfloat16)
    router_part = jnp.einsum("rd,re->de", ffn_in, logit_grad, preferred_element_type=jnp.float32)
    ffn_grad = jnp.sum(pair_grad.astype(jnp.float32), axis=1) + jnp.einsum(
        "re,de->rd", logit_grad, router, preferred_element_type=jnp.float32
    )
    gain_ffn_part = jnp.sum(ffn_grad * plain_two, axis=0)
    scaled_two = ffn_grad * gain_ffn
    resid_grad = cot_full + inv_two * (
        scaled_two - plain_two * jnp.mean(scaled_two * plain_two, axis=-1, keepdims=True)
    )
    resid_low = resid_grad.astype(jnp.bfloat16)
    out_part = jnp.einsum("rd,rh->dh", resid_low, attended, preferred_element_type=jnp.float32)
    att_grad = jnp.einsum(
        "rd,dh->rh", resid_low, out_weight, preferred_element_type=jnp.float32
    ).astype(jnp.bfloat16)
    att_heads = att_grad.reshape(tok_rows, KV_HEADS, group, HEAD)
    row_delta = jnp.sum(
        att_heads.astype(jnp.float32)
        * attended.reshape(tok_rows, KV_HEADS, group, HEAD).astype(jnp.float32),
        axis=-1,
    ).transpose(1, 2, 0)
    key_piece = lax.all_gather(keys, "context", axis=0, tiled=True)
    value_piece = lax.all_gather(values, "context", axis=0, tiled=True)
    scores, visible = key_scores(key_piece)
    soft = jnp.exp(scores - log_total[..., None])
    prob_grad = jnp.einsum(
        "qkgd,skd->kgqs", att_heads, value_piece, preferred_element_type=jnp.float32
    )
    score_grad = (soft * (prob_grad - row_delta[..., None])).astype(jnp.bfloat16)
    query_acc = jnp.einsum(
        "kgqs,skd->kgqd", score_grad, key_piece, preferred_element_type=jnp.float32
    )
    key_part = jnp.einsum("kgqs,qkgd->skd", score_grad, grouped, preferred_element_type=jnp.float32)
    value_part = jnp.einsum(
        "kgqs,qkgd->skd", soft.astype(jnp.bfloat16), att_heads, preferred_element_type=jnp.float32
    )
    pair_acc = jnp.stack([key_part, value_part], axis=1)
    query_acc, pair_acc = (query_acc, pair_acc)
    own_pairs = lax.psum_scatter(
        pair_acc.astype(jnp.bfloat16), "context", scatter_dimension=0, tiled=True
    ).astype(jnp.float32)
    query_grad = (
        unrotate(query_acc.transpose(2, 0, 1, 3).reshape(tok_rows, HEADS, HEAD), cosine, sine)
        * scale
    )
    key_grad = unrotate(own_pairs[:, 0], cosine, sine)
    mixed_grad = jnp.concatenate(
        [
            query_grad.reshape(tok_rows, q_cols),
            key_grad.reshape(tok_rows, kv_cols),
            own_pairs[:, 1].reshape(tok_rows, kv_cols),
        ],
        axis=-1,
    ).astype(jnp.bfloat16)
    qkv_part = jnp.einsum("rd,rc->dc", normed, mixed_grad, preferred_element_type=jnp.float32)
    norm_grad = jnp.einsum("rc,dc->rd", mixed_grad, qkv_weight, preferred_element_type=jnp.float32)
    gain_attn_part = jnp.sum(norm_grad * plain_one, axis=0)
    scaled_one = norm_grad * gain_attn
    input_grad = (
        resid_grad
        + inv_one
        * (scaled_one - plain_one * jnp.mean(scaled_one * plain_one, axis=-1, keepdims=True))
    ).astype(jnp.bfloat16)
    gain_attn_grad, qkv_grad, out_proj_grad, gain_ffn_grad, router_grad = (
        lax.psum_scatter(
            gain_attn_part, ("expert", "context", "dp"), scatter_dimension=0, tiled=True
        ),
        lax.psum_scatter(qkv_part, ("expert", "context", "dp"), scatter_dimension=0, tiled=True),
        lax.psum_scatter(out_part, ("expert", "context", "dp"), scatter_dimension=0, tiled=True),
        lax.psum_scatter(
            gain_ffn_part, ("expert", "context", "dp"), scatter_dimension=0, tiled=True
        ),
        lax.psum_scatter(router_part, ("expert", "context", "dp"), scatter_dimension=0, tiled=True),
    )
    return (
        output[None],
        input_grad[None],
        gain_attn_grad,
        qkv_grad,
        out_proj_grad,
        gain_ffn_grad,
        router_grad,
        expert_in,
        expert_down,
    )


def solution(mesh):
    in_specs = (
        P(("expert", "dp"), "context", None),
        P(("expert", "dp"), None),
        P(("expert", "dp"), "context", None),
        P(("expert", "dp"), "context", None),
        P(),
        P(),
        P(),
        P(),
        P(),
        P("expert", None, None),
        P("expert", None, None),
        P(("expert", "dp"), "context", None),
    )
    out_specs = (
        P(("expert", "dp"), "context", None),
        P(("expert", "dp"), "context", None),
        P(("expert", "context", "dp")),
        P(("expert", "context", "dp"), None),
        P(("expert", "context", "dp"), None),
        P(("expert", "context", "dp")),
        P(("expert", "context", "dp"), None),
        P("expert", ("context", "dp"), None),
        P("expert", ("context", "dp"), None),
    )
    tuned = dict(mesh.shape) == {"expert": 2, "context": 4, "dp": 4}
    body = local if tuned else general
    return jax.shard_map(body, mesh=mesh, in_specs=in_specs, out_specs=out_specs, check_vma=False)
```

```python
import functools

import jax
import jax.numpy as jnp
import numpy as np
from jax import lax
from jax.experimental import pallas as pl
from jax.experimental.pallas import tpu as pltpu
from jax.sharding import PartitionSpec as P

HEADS = 12
KV_HEADS = 2
HEAD = 128


ROPE_BASE = 1000000.0
NORM_EPS = 1e-06
MASKED = -1e30


def rope_tables(positions, head_size):
    half_size = head_size // 2
    freqs = ROPE_BASE ** (jnp.arange(half_size).astype(jnp.float32) * (-2.0 / head_size))
    angles = positions[:, None] * freqs[None, :]
    return (jnp.cos(angles)[:, None, :], jnp.sin(angles)[:, None, :])


def rotate(values, cosine, sine):
    half_size = values.shape[-1] // 2
    first = values[..., :half_size]
    second = values[..., half_size:]
    return jnp.concatenate(
        [first * cosine - second * sine, second * cosine + first * sine], axis=-1
    )


def unrotate(values, cosine, sine):
    half_size = values.shape[-1] // 2
    first = values[..., :half_size]
    second = values[..., half_size:]
    return jnp.concatenate(
        [first * cosine + second * sine, second * cosine - first * sine], axis=-1
    )


def softmax_last(scores):
    shifted = jnp.exp(scores - jnp.max(scores, axis=-1, keepdims=True))
    return shifted / jnp.sum(shifted, axis=-1, keepdims=True)


def route(block_ids, block_order, n_experts, capacity):
    flat_ids = block_ids.reshape(-1)
    flat_order = block_order.reshape(-1)
    choose = (flat_ids[:, None] == jnp.arange(n_experts)[None, :]).astype(jnp.int32)
    ordered = jnp.zeros_like(choose).at[flat_order].set(choose)
    earlier = jnp.cumsum(ordered, axis=0, dtype=jnp.int32) - ordered
    ranks = jnp.sum(earlier[flat_order] * choose, axis=1)
    return jnp.where(ranks < capacity, flat_ids * capacity + ranks, n_experts * capacity)


MESH = pl.DeviceIdType.MESH
F32 = jnp.float32
BF16 = jnp.bfloat16
BACK_LOW = 96
OUT_LOW = 128
FRONT_LOW = 96


def dot(a, b):
    return jnp.dot(a, b, preferred_element_type=F32)


def dot_nt(a, b):
    return lax.dot_general(a, b, (((1,), (1,)), ((), ())), preferred_element_type=F32)


def dot_tn(a, b):
    return lax.dot_general(a, b, (((0,), (0,)), ((), ())), preferred_element_type=F32)


def plus(a, *more):
    total = a.astype(F32)
    for b in more:
        total = total + b.astype(F32)
    return total.astype(BF16)


def lanes(at, size):
    return pl.ds(pl.multiple_of(at, 128), size)


def rows_at(at, size):
    return pl.ds(pl.multiple_of(at, 16), size)


def remote(src, dst, s, r, dev):
    return pltpu.make_async_remote_copy(
        src_ref=src, dst_ref=dst, send_sem=s, recv_sem=r, device_id=dev, device_id_type=MESH
    )


class Spot:
    def __init__(self):
        e, c, z = lax.axis_index("expert"), lax.axis_index("context"), lax.axis_index("dp")
        self.ctx = lax.axis_size("context")
        self.parts = lax.axis_size("dp")
        self.planes = self.ctx * lax.axis_size("expert")
        y, k = lax.div(c, 2), lax.rem(c, 2)
        self.e, self.c, self.z, self.k = e, c, z, k
        self.me = e * self.ctx + c
        self.xp, self.yp = (1 - e, c, z), (e, (1 - y) * 2 + k, z)
        self.kp, self.yk = (e, y * 2 + 1 - k, z), (e, (1 - y) * 2 + 1 - k, z)
        self.chips = [
            eq * self.ctx + yq * 2 for eq, yq in ((e, y), (1 - e, y), (e, 1 - y), (1 - e, 1 - y))
        ]

    def others(self):
        found = []
        for step in range(1, self.planes):
            other = lax.rem(self.me + step, self.planes)
            found.append((other, (lax.div(other, self.ctx), lax.rem(other, self.ctx), self.z)))
        return found

    def along(self):
        e, c, z = self.e, self.c, self.z
        return [(z < self.parts - 1, (e, c, z + 1)), (z > 0, (e, c, z - 1))]


def greet(peers, extra=()):
    barrier = pltpu.get_barrier_semaphore()
    for peer in peers:
        pl.semaphore_signal(barrier, inc=1, device_id=peer, device_id_type=MESH)
    for there, peer in extra:

        @pl.when(there)
        def _():
            pl.semaphore_signal(barrier, inc=1, device_id=peer, device_id_type=MESH)

    count = len(peers)
    for there, _ in extra:
        count = count + there.astype(jnp.int32)
    pl.semaphore_wait(barrier, count)


class Plane:
    def __init__(self, spot, zcr, zk, rx, ry, s, r, zcr_there=None, low=None):
        self.zcr_there = zcr_there or zcr
        self.spot, self.zcr, self.zk, self.rx, self.ry, self.s, self.r = spot, zcr, zk, rx, ry, s, r
        low = low or zk[0].shape[0] // 2
        self.lo, self.hi = pl.ds(0, low), pl.ds(low, zk[0].shape[0] - low)
        self.sent, self.gives = [], []

    def push(self, src, dst, i, dev):
        copy = remote(src, dst, self.s.at[i], self.r.at[i], dev)
        copy.start()
        self.sent.append(copy)

    def arrive(self, dst, i):
        remote(dst, dst, self.s.at[i], self.r.at[i], self.spot.kp).wait_recv()

    def given(self):
        for copy in self.gives:
            copy.wait_send()
        self.gives = []

    def give(self, q, src):
        self.gives.append(remote(src, self.zcr_there[q], self.s.at[q], self.r.at[q], self.spot.kp))
        self.gives[-1].start()

    def fold(self, q, own=None):
        self.arrive(self.zcr[q], q)
        self.zk[q][...] = plus(self.zk[q][...] if own is None else own, self.zcr[q][...])

    def near(self):
        self.push(self.zk[1].at[self.lo], self.rx[1], 5, self.spot.xp)
        self.push(self.zk[2].at[self.hi], self.ry[1], 8, self.spot.yp)

    def across(self):
        self.push(self.zk[3].at[self.lo], self.rx[0], 4, self.spot.xp)
        self.push(self.zk[3].at[self.hi], self.ry[0], 7, self.spot.yp)

    def turn(self):
        lo, hi = self.lo, self.hi
        self.arrive(self.rx[0], 4)
        self.zk[2][lo] = plus(self.zk[2][lo], self.rx[0][...])
        self.push(self.zk[2].at[lo], self.ry[2], 9, self.spot.yp)
        self.arrive(self.ry[0], 7)
        self.zk[1][hi] = plus(self.zk[1][hi], self.ry[0][...])
        self.push(self.zk[1].at[hi], self.rx[2], 6, self.spot.xp)

    def total(self):
        self.arrive(self.rx[1], 5)
        self.arrive(self.ry[1], 8)
        self.arrive(self.rx[2], 6)
        self.arrive(self.ry[2], 9)
        return (
            (self.lo, (self.zk[0][self.lo], self.rx[1][...], self.ry[2][...])),
            (self.hi, (self.zk[0][self.hi], self.rx[2][...], self.ry[1][...])),
        )

    def done(self):
        self.given()
        for copy in self.sent:
            copy.wait_send()


def plane_of(spot, zcr, zk, rx, ry, s, r, low=None):
    four, block = range(4), zk.shape[1]
    lo, hi = pl.ds(0, low or block // 2), pl.ds(0, block - (low or block // 2))
    return Plane(
        spot,
        [zcr.at[q] for q in four],
        [zk.at[q] for q in four],
        [rx.at[0, lo], rx.at[1, lo], rx.at[2, hi]],
        [ry.at[0, hi], ry.at[1, hi], ry.at[2, lo]],
        s,
        r,
        low=low,
    )


def plane_scratch(block, wide, low=None):
    most = max(low or block // 2, block - (low or block // 2))
    return [
        pltpu.VMEM((4, block, wide), BF16),
        pltpu.VMEM((4, block, wide), BF16),
        pltpu.VMEM((3, most, wide), BF16),
        pltpu.VMEM((3, most, wide), BF16),
        pltpu.SemaphoreType.DMA((10,)),
        pltpu.SemaphoreType.DMA((10,)),
    ]


def summed(terms):
    total = terms[0].astype(F32)
    for term in terms[1:]:
        total = total + term.astype(F32)
    return total


class Line:
    def __init__(self, spot, own, adder, buf, s, r):
        z, last = spot.z, spot.parts - 1
        e, c = spot.e, spot.c
        self.own, self.adder, self.buf, self.s, self.r = own, adder, buf, s, r
        self.z, self.last, self.parts = z, last, spot.parts
        self.ways = [(z, (e, c, z + 1), lambda d: d), (last - z, (e, c, z - 1), lambda d: last - d)]

    def step(self, turn):
        for way, (i, dev, part) in enumerate(self.ways):
            to, s, r = self.buf.at[way, turn - 1], self.s.at[way, turn - 1], self.r.at[way, turn - 1]

            @pl.when(i == 0)
            def _():
                remote(self.own(part(self.parts - turn)), to, s, r, dev).start()

            if turn >= 2:
                came, s_came, r_came = (x.at[way, turn - 2] for x in (self.buf, self.s, self.r))

                @pl.when((i >= 1) & (i <= turn - 1) & (i < self.last))
                def _():
                    remote(came, came, s_came, r_came, dev).wait_recv()
                    self.adder(came, part(self.parts - turn + i))
                    remote(came, to, s, r, dev).start()

    def final(self, put):
        last, z = self.last, self.z
        for way, (i, dev, _) in enumerate(self.ways):
            came = self.buf.at[way, last - 1]

            @pl.when(i >= 1)
            def _():
                remote(came, came, self.s.at[way, last - 1], self.r.at[way, last - 1], dev).wait_recv()

        up, down = self.buf.at[0, last - 1], self.buf.at[1, last - 1]
        pl.when(z == 0)(lambda: put(down))
        pl.when(z == last)(lambda: put(up))
        pl.when((z > 0) & (z < last))(lambda: put(up, down))

    def done(self):
        for way, (i, dev, _) in enumerate(self.ways):
            for turn in range(1, self.parts):
                came = self.buf.at[way, turn - 1]

                @pl.when((i <= turn - 1) & (i < self.last))
                def _():
                    remote(came, came, self.s.at[way, turn - 1], self.r.at[way, turn - 1], dev).wait_send()


def line_scratch(parts, piece):
    return [
        pltpu.VMEM((2, parts - 1) + piece, BF16),
        pltpu.SemaphoreType.DMA((2, parts - 1)),
        pltpu.SemaphoreType.DMA((2, parts - 1)),
    ]


class ExpertLine:
    def __init__(self, spot, ref, at, cols, buf, s, r, fin, spread, a_s, a_r):
        self.spot, self.ref, self.at, self.cols = spot, ref, at, cols
        self.fin, self.spread, self.a_s, self.a_r = fin, spread, a_s, a_r
        self.line = Line(spot, self.own, self.adder, buf, s, r)
        self.step = self.line.step

    def own(self, d):
        return self.ref.at[:, d, :, pl.ds(self.at, self.cols)]

    def piece(self, cc, d):
        return self.ref[cc, d, :, self.at : self.at + self.cols]

    def adder(self, came, d):
        for cc in range(self.spot.ctx):
            came[cc] = plus(came[cc], self.piece(cc, d))

    def final(self):
        spot = self.spot

        def put(*came):
            for cc in range(spot.ctx):
                self.fin[cc] = plus(self.piece(cc, spot.z), *(x[cc] for x in came))

        self.line.final(put)
        for step in range(1, spot.ctx):
            cc = lax.rem(spot.c + step, spot.ctx)
            remote(
                self.fin.at[cc],
                self.spread.at[spot.c],
                self.a_s.at[step - 1],
                self.a_r.at[step - 1],
                (spot.e, cc, spot.z),
            ).start()

    def done(self, out):
        spot = self.spot
        for step in range(1, spot.ctx):
            cc = lax.rem(spot.c + spot.ctx - step, spot.ctx)
            got = remote(
                self.spread.at[cc],
                self.spread.at[cc],
                self.a_s.at[step - 1],
                self.a_r.at[step - 1],
                (spot.e, cc, spot.z),
            )
            got.wait_recv()
            got.wait_send()
            out[cc] = self.spread[cc]
        out[spot.c] = self.fin[spot.c]
        self.line.done()


def expert_scratch(ctx, parts, rows, cols):
    return line_scratch(parts, (ctx, rows, cols)) + [
        pltpu.VMEM((ctx, rows, cols), BF16),
        pltpu.VMEM((ctx, rows, cols), BF16),
        pltpu.SemaphoreType.DMA((ctx - 1,)),
        pltpu.SemaphoreType.DMA((ctx - 1,)),
    ]


class Gather:
    def __init__(self, spot, own, buf, s, r, low=None):
        self.spot, self.own, self.buf, self.s, self.r = spot, own, buf, s, r
        low = low or own.shape[0] // 2
        self.lo, self.hi = pl.ds(0, low), pl.ds(low, own.shape[0] - low)
        self.x_me, self.y_me, self.d_me = (base + spot.k for base in spot.chips[1:])
        self.side = 1 - 2 * spot.k
        self.sent = []

    def push(self, src, dst, i, dev):
        copy = remote(src, dst, self.s.at[i], self.r.at[i], dev)
        copy.start()
        self.sent.append(copy)

    def move(self, p, rows, i, dev):
        self.push(self.buf.at[p, rows], self.buf.at[p, rows], i, dev)

    def got(self, p, rows, i):
        to = self.buf.at[p, rows]
        remote(to, to, self.s.at[i], self.r.at[i], self.spot.kp).wait_recv()

    def start(self):
        me, own, lo, hi = self.spot.me, self.own, self.lo, self.hi
        self.push(own.at[lo], self.buf.at[me, lo], 0, self.spot.xp)
        self.push(own.at[lo], self.buf.at[me, lo], 6, self.spot.kp)
        self.push(own.at[hi], self.buf.at[me, hi], 13, self.spot.kp)
        self.push(own.at[hi], self.buf.at[me, hi], 1, self.spot.xp)

    def start_y(self):
        me, own, lo, hi = self.spot.me, self.own, self.lo, self.hi
        self.push(own.at[hi], self.buf.at[me, hi], 3, self.spot.yp)
        self.push(own.at[lo], self.buf.at[me, lo], 2, self.spot.yp)

    def first(self):
        spot = self.spot
        self.got(self.x_me, self.lo, 0)
        self.move(self.x_me, self.lo, 4, spot.yp)
        self.move(self.x_me, self.lo, 7, spot.kp)
        self.got(self.y_me, self.hi, 3)
        self.move(self.y_me, self.hi, 5, spot.xp)
        self.move(self.y_me, self.hi, 10, spot.kp)

    def second(self):
        self.got(self.x_me, self.hi, 1)
        self.move(self.x_me, self.hi, 8, self.spot.kp)
        self.got(self.y_me, self.lo, 2)
        self.move(self.y_me, self.lo, 9, self.spot.kp)

    def third(self):
        self.got(self.d_me, self.lo, 4)
        self.move(self.d_me, self.lo, 11, self.spot.kp)
        self.got(self.d_me, self.hi, 5)
        self.move(self.d_me, self.hi, 12, self.spot.kp)

    def other_core(self, q):
        low_sem, high_sem = ((6, 13), (7, 8), (9, 10), (11, 12))[q]
        p = (self.spot.me, self.x_me, self.y_me, self.d_me)[q] + self.side
        self.got(p, self.lo, low_sem)
        self.got(p, self.hi, high_sem)

    def done(self):
        for copy in self.sent:
            copy.wait_send()


GATHER_COPIES = 14


def front_kernel(
    cap,
    span,
    hidden,
    cot,
    gain_one,
    freqs,
    gain_two,
    router_t,
    ids_t,
    turn_t,
    wqkv_h,
    wout_h,
    normed,
    queries,
    kv,
    lse,
    attended,
    resid,
    ffn_in,
    trig,
    meta,
    cot_all,
    wqkv,
    wout,
    mask,
    vt,
    load_sem,
    kv_s,
    kv_r,
    co_s,
    co_r,
):
    spot = Spot()
    c, ctx, k = spot.c, spot.ctx, spot.k
    tok, width = hidden.shape
    group = HEADS // KV_HEADS
    kv_cols = KV_HEADS * HEAD
    half_head = HEAD // 2
    seq = kv.shape[0]
    spans = span.shape[1]
    size = seq // spans
    mine = spans // ctx
    n_experts = meta.shape[0]
    loads = [
        pltpu.make_async_copy(wqkv_h.at[:, pl.ds(width, 2 * kv_cols)], wqkv.at[:, pl.ds(width, 2 * kv_cols)], load_sem.at[0]),
        pltpu.make_async_copy(wqkv_h.at[:, pl.ds(0, width)], wqkv.at[:, pl.ds(0, width)], load_sem.at[1]),
        pltpu.make_async_copy(wout_h, wout, load_sem.at[2]),
        pltpu.make_async_copy(cot, cot_all.at[spot.me], load_sem.at[3]),
    ]
    for load in loads:
        load.start()
    greet([spot.xp, spot.yp, spot.kp])
    gather = Gather(spot, cot, cot_all, co_s, co_r, low=FRONT_LOW)
    gather.start()

    x = hidden[...].astype(F32)
    inv = lax.rsqrt(jnp.mean(x * x, axis=-1, keepdims=True) + NORM_EPS)
    normed[...] = (x * inv * gain_one[...]).astype(BF16)

    along = lax.broadcasted_iota(jnp.int32, (tok, HEAD), 0)
    start_one, start_two = span[0, c * mine] * size, (span[0, c * mine + 1] - 1) * size
    place = jnp.where(along < size, start_one, start_two) + along
    angle = place.astype(F32) * freqs[...]
    cosine, sine = jnp.cos(angle), jnp.sin(angle)
    lane = lax.broadcasted_iota(jnp.int32, (tok, HEAD), 1)
    sine = jnp.where(lane < half_head, -sine, sine)
    trig[0] = cosine
    trig[1] = sine

    def rotate_in(w):
        return w * cosine + pltpu.roll(w, half_head, 1) * sine

    loads[0].wait()
    raw = dot(normed[...], wqkv[:, width:])
    own = rows_at(c * tok, tok)
    for g in range(KV_HEADS):
        at = slice(g * HEAD, (g + 1) * HEAD)
        kv[own, at] = rotate_in(raw[:, at]).astype(BF16)
    kv[own, kv_cols:] = raw[:, kv_cols:].astype(BF16)

    def kv_copy(rows, i, dev):
        return remote(kv.at[rows], kv.at[rows], kv_s.at[i], kv_r.at[i], dev)

    flip_c = lax.rem(c + 2, ctx)
    near_c = c + 1 - 2 * k
    across_c = lax.rem(near_c + 2, ctx)
    sent = [kv_copy(own, 1, spot.yp), kv_copy(own, 0, spot.kp)]
    for copy in sent:
        copy.start()
    gather.start_y()

    loads[1].wait()
    step = 256

    @pl.loop(0, width // step)
    def _(n):
        at = lanes(n * step, step)
        raw = dot(normed[...], wqkv[:, at])
        for i in range(step // HEAD):
            w = raw[:, i * HEAD : (i + 1) * HEAD]
            queries[:, lanes(n * step + i * HEAD, HEAD)] = (rotate_in(w) * HEAD**-0.5).astype(BF16)

    flip = rows_at(flip_c * tok, tok)
    kv_copy(flip, 1, spot.kp).wait_recv()
    sent.append(kv_copy(flip, 2, spot.kp))
    sent[-1].start()

    expert = lax.broadcasted_iota(jnp.int32, (n_experts, tok), 0)
    never = tok * ids_t.shape[0]
    turn = jnp.full((n_experts, tok), never, jnp.int32)
    for i in range(ids_t.shape[0]):
        turn = jnp.where(ids_t[i : i + 1, :] == expert, turn_t[i : i + 1, :], turn)
    turn_f = turn.astype(F32)
    tall = jnp.concatenate([turn_f, jnp.full((HEAD - n_experts, tok), float(never), F32)], axis=0).T
    meta[...] = jnp.zeros(meta.shape, F32)
    for g in range(n_experts):
        row = turn_f[g : g + 1, :]
        rank = jnp.sum(jnp.where(tall[:, g : g + 1] < row, 1.0, 0.0), axis=0, keepdims=True)
        meta[g, 0:1, :] = jnp.where((row < never) & (rank < cap), rank, -1.0)

    along_q = lax.broadcasted_iota(jnp.int32, (size, tok), 1)
    q_pos = jnp.where(along_q < size, start_one, start_two) + along_q
    for s in range(spans):
        k_pos = span[0, s] * size + lax.broadcasted_iota(jnp.int32, (size, tok), 0)
        mask[s * size : (s + 1) * size, :] = jnp.where(k_pos <= q_pos, 0.0, MASKED)

    near, across = rows_at(near_c * tok, tok), rows_at(across_c * tok, tok)
    kv_copy(near, 0, spot.kp).wait_recv()
    kv_copy(across, 2, spot.kp).wait_recv()
    for g in range(KV_HEADS):
        vt[g] = kv[:, kv_cols + g * HEAD : kv_cols + (g + 1) * HEAD].astype(F32).T.astype(BF16)
    lse[...] = jnp.zeros(lse.shape, F32)

    def heads(g, first, count):
        @pl.loop(first, first + count)
        def _(h):
            at = lanes(h * HEAD, HEAD)
            scores = dot_nt(kv[:, g * HEAD : (g + 1) * HEAD], queries[:, at]) + mask[...]
            top = jnp.max(scores, axis=0, keepdims=True)
            weights = jnp.exp(scores - top)
            total = jnp.sum(weights, axis=0, keepdims=True)
            lse[pl.ds(h, 1), :] = top + jnp.log(total)
            out = dot(vt[g], weights.astype(BF16)) / total
            attended[:, at] = out.T.astype(BF16)

    heads(0, 0, 3)
    gather.first()
    heads(0, 3, 3)
    heads(1, 6, 3)
    gather.second()
    heads(1, 9, 3)

    loads[2].wait()

    @pl.loop(0, width // step)
    def _(n):
        at = lanes(n * step, step)
        resid[:, at] = hidden[:, at].astype(F32) + dot_nt(attended[...], wout[at, :])

    r = resid[...]
    inv = lax.rsqrt(jnp.mean(r * r, axis=-1, keepdims=True) + NORM_EPS)
    ffn_in[...] = (r * inv * gain_two[...]).astype(BF16)
    logits = dot_nt(router_t[...], ffn_in[...])[:n_experts]
    logits = jnp.where(turn < never, logits, MASKED)
    shifted = jnp.exp(logits - jnp.max(logits, axis=0, keepdims=True))
    gates = shifted / jnp.sum(shifted, axis=0, keepdims=True)
    for g in range(n_experts):
        meta[g, 1:2, :] = gates[g : g + 1, :]
    gather.third()
    for q in range(4):
        gather.other_core(q)
    loads[3].wait()
    gather.done()
    for copy in sent:
        copy.wait_send()


def run_front(cap, span, hidden, cot, gain_one, freqs, gain_two, router_t, ids_t, turn_t, wqkv, wout, ctx, planes):
    tok, width = hidden.shape
    seq = tok * ctx
    n_experts = planes
    kv_cols = 2 * KV_HEADS * HEAD
    vm, anyspace = pl.BlockSpec(memory_space=pltpu.VMEM), pl.BlockSpec(memory_space=pl.ANY)
    sm = pl.BlockSpec(memory_space=pltpu.SMEM)
    shape = jax.ShapeDtypeStruct
    dma = pltpu.SemaphoreType.DMA
    return pl.pallas_call(
        functools.partial(front_kernel, cap),
        out_shape=(
            shape((tok, width), BF16),
            shape((tok, width), BF16),
            shape((seq, kv_cols), BF16),
            shape((16, tok), F32),
            shape((tok, width), BF16),
            shape((tok, width), F32),
            shape((tok, width), BF16),
            shape((2, tok, HEAD), F32),
            shape((n_experts, 8, tok), F32),
            shape((planes, tok, width), BF16),
        ),
        in_specs=[sm] + [vm] * 8 + [anyspace] * 2,
        out_specs=(vm,) * 9 + (anyspace,),
        scratch_shapes=[
            pltpu.VMEM(wqkv.shape, BF16),
            pltpu.VMEM(wout.shape, BF16),
            pltpu.VMEM((seq, tok), F32),
            pltpu.VMEM((KV_HEADS, HEAD, seq), BF16),
            dma((4,)),
            dma((3,)),
            dma((3,)),
            dma((GATHER_COPIES,)),
            dma((GATHER_COPIES,)),
        ],
        compiler_params=pltpu.CompilerParams(
            collective_id=4, has_side_effects=True, vmem_limit_bytes=56 * 2**20
        ),
        cost_estimate=pl.CostEstimate(flops=5 * 10**9, bytes_accessed=20 * 10**6, transcendentals=4 * 10**6),
    )(span, hidden, cot, gain_one, freqs, gain_two, router_t, ids_t, turn_t, wqkv, wout)


def ffn_kernel(cap, ffn_h, resid_h, cot_h, meta, win_h, wdn_h, output, pg_out, gg_out, gwin_h, ex_out, first_out, *scratch):
    agb, metas, cotb, win, wdn, xs, ds, hid, igs, pgs, ggs, ggr, wint, gwdn = scratch[:14]
    load_sem, ag_s, ag_r, me_s, me_r, gg_s, gg_r, out_s, out_r = scratch[14:23]
    plane_refs, line_refs, first_refs = scratch[23:29], scratch[29:36], scratch[36:]
    spot = Spot()
    c, k, me = spot.c, spot.k, spot.me
    kp = spot.kp
    tok, width = output.shape
    ff = wdn.shape[1]
    planes, ctx = spot.planes, spot.ctx
    chips = spot.chips

    loads = [
        pltpu.make_async_copy(win_h.at[c], win, load_sem.at[0]),
        pltpu.make_async_copy(wdn_h.at[c], wdn, load_sem.at[1]),
        pltpu.make_async_copy(cot_h, cotb, load_sem.at[2]),
        pltpu.make_async_copy(resid_h, pg_out, load_sem.at[3]),
    ]
    own_load = pltpu.make_async_copy(ffn_h, agb.at[me], load_sem.at[4])
    own_load.start()
    for load in loads:
        load.start()
    others = spot.others()
    greet([dev for _, dev in others], spot.along())
    plane = plane_of(spot, *plane_refs)
    o_lo, o_hi = pl.ds(0, OUT_LOW), pl.ds(OUT_LOW, tok - OUT_LOW)
    outs = Plane(
        spot,
        [agb.at[2 * i + k] for i in range(4)],
        [cotb.at[base + k] for base in chips],
        [agb.at[1 - k, o_lo], agb.at[3 - k, o_lo], agb.at[1 - k, o_hi]],
        [agb.at[3 - k, o_hi], agb.at[5 - k, o_hi], agb.at[5 - k, o_lo]],
        out_s,
        out_r,
        [agb.at[2 * i + 1 - k] for i in range(4)],
        low=OUT_LOW,
    )
    line = ExpertLine(spot, gwdn, 0, ff, *line_refs)
    some = first_out.shape[2]
    first_line = ExpertLine(spot, win, 0, some, *first_refs)
    gather = Gather(spot, agb.at[me], agb, ag_s, ag_r)
    for step, (other, dev) in enumerate(others):
        remote(meta.at[other], metas.at[me], me_s.at[step], me_r.at[step], dev).start()
    own_load.wait()
    gather.start()
    gather.start_y()
    metas[me] = meta[me]
    slot_rows = lax.broadcasted_iota(jnp.int32, (cap, tok), 0).astype(F32)
    step = 256

    def spots(p):
        return jnp.where(slot_rows == metas[p, 0:1, :], 1.0, 0.0)

    def gate_of(p, hot):
        return jnp.sum(hot * metas[p, 1:2, :], axis=1, keepdims=True)

    def dispatch(q):
        for kk in range(2):
            p = chips[q] + kk
            hot = spots(p)
            low = hot.astype(BF16)
            part = pl.ds(q * 2 * cap + kk * cap, cap)
            xs[part, :] = dot(low, agb[p]).astype(BF16)
            ds[part, :] = (dot(low, cotb[p]) * gate_of(p, hot)).astype(BF16)

    def work(q, count):
        rows = pl.ds(q * 2 * cap, count * 2 * cap)

        @pl.loop(0, ff // step)
        def _(n):
            gate_cols, up_cols = lanes(n * step, step), lanes(ff + n * step, step)
            x = xs[rows, :]
            g = dot(x, win[:, :, :, gate_cols].reshape(width, step))
            u = dot(x, win[:, :, :, up_cols].reshape(width, step))
            s = 1.0 / (1.0 + jnp.exp(-g))
            act = g * s
            hid[rows, gate_cols] = (act * u).astype(BF16)
            h = dot(ds[rows, :], wdn[:, gate_cols])
            igs[rows, gate_cols] = (h * u * (s * (1.0 + g * (1.0 - s)))).astype(BF16)
            igs[rows, up_cols] = (h * act).astype(BF16)

        @pl.loop(0, width // step)
        def _(n):
            cols = lanes(n * step, step)
            pgs[pl.ds(0, count * 2 * cap), cols] = dot(igs[rows, :], wint[:, cols]).astype(BF16)

    def back(q, at):
        base = chips[q]
        mine, theirs = rows_at(at * 2 * cap + k * cap, cap), rows_at(at * 2 * cap + (1 - k) * cap, cap)
        given = agb.at[base + 1 - k]
        given[...] = dot_tn(spots(base + 1 - k).astype(BF16), pgs[theirs, :]).astype(BF16)
        plane.give(q, given)
        plane.zk[q][...] = dot_tn(spots(base + k).astype(BF16), pgs[mine, :]).astype(BF16)

    for load in loads:
        load.wait()

    tall = width // ctx

    @pl.loop(0, ctx)
    def _(n):
        wint[:, lanes(n * tall, tall)] = win[n].reshape(tall, 2 * ff).T

    for n in range(planes - 1):
        source = lax.rem(me + planes - 1 - n, planes)
        remote(metas.at[source], metas.at[source], me_s.at[n], me_r.at[n], kp).wait_recv()
    gather.other_core(0)
    dispatch(0)
    work(0, 1)
    back(0, 0)
    gather.first()
    gather.second()
    gather.other_core(1)
    dispatch(1)
    gather.other_core(2)
    dispatch(2)
    work(1, 2)
    gather.third()
    back(1, 0)
    back(2, 1)
    gather.other_core(3)
    gather.done()
    dispatch(3)
    plane.fold(1)
    plane.fold(2)
    plane.near()
    work(3, 1)
    back(3, 0)
    plane.fold(3)
    plane.given()
    plane.across()


    @pl.loop(0, ctx)
    def _(n):
        tile = dot_tn(ds[:, lanes(n * tall, tall)], hid[...]).astype(BF16)
        for d in range(gwdn.shape[1]):
            gwdn[n, d] = tile[d * gwdn.shape[2] : (d + 1) * gwdn.shape[2]]

    line.step(1)
    plane.fold(0)

    @pl.loop(0, width // step)
    def _(n):
        cols = lanes(n * step, step)
        ds[:, cols] = dot_nt(hid[...], wdn[cols, :]).astype(BF16)

    def returned(q):
        base = chips[q]
        for kk in range(2):
            p = base + kk
            hot = spots(p)
            rows = ds[pl.ds(q * 2 * cap + kk * cap, cap), :]
            ggs[p, 0:1, :] = jnp.sum(hot * dot_nt(rows, cotb[p]), axis=0, keepdims=True)
            scaled = (rows.astype(F32) * gate_of(p, hot)).astype(BF16)
            cotb[p] = dot_tn(hot.astype(BF16), scaled).astype(BF16)
        outs.give(q, cotb.at[base + 1 - k])

    returned(1)
    returned(2)
    plane.turn()
    returned(3)
    returned(0)
    outs.fold(1)
    outs.fold(2)
    outs.near()
    outs.fold(3)
    outs.across()
    ggr[me] = ggs[me]
    for n, (other, dev) in enumerate(others):
        remote(ggs.at[other], ggr.at[me], gg_s.at[n], gg_r.at[n], dev).start()
    line.step(2)
    outs.fold(0)

    def gate_up(at, size):
        @pl.loop(0, ctx)
        def _(n):
            tile = dot_tn(xs[:, lanes(n * tall, tall)], igs[:, pl.ds(at, size)]).astype(BF16)
            win[n, :, :, pl.ds(at, size)] = tile.reshape(gwdn.shape[1], gwdn.shape[2], size)

    gate_up(0, some)
    first_line.step(1)
    rest = 2 * ff - some
    gate_up(some, rest // 2)
    gate_up(some + rest // 2, rest // 2)
    gwin_copy = pltpu.make_async_copy(win.at[:, :, :, pl.ds(some, rest)], gwin_h, load_sem.at[0])
    gwin_copy.start()
    line.step(3)
    outs.turn()
    first_line.step(2)
    line.final()
    for rows, terms in outs.total():
        output[rows, :] = (pg_out[rows, :] + summed(terms)).astype(BF16)
    for rows, terms in plane.total():
        pg_out[rows, :] = summed(terms)
    for n in range(planes - 1):
        source = lax.rem(me + planes - 1 - n, planes)
        remote(ggr.at[source], ggr.at[source], gg_s.at[n], gg_r.at[n], kp).wait_recv()
    for p in range(planes):
        gg_out[p : p + 1, :] = ggr[p, 0:1, :]
    first_line.step(3)
    first_line.final()
    gwin_copy.wait()
    for n, (other, dev) in enumerate(others):
        remote(meta.at[other], metas.at[other], me_s.at[n], me_r.at[n], dev).wait_send()
        remote(ggs.at[other], ggr.at[other], gg_s.at[n], gg_r.at[n], dev).wait_send()
    plane.done()
    outs.done()
    line.done(ex_out)
    first_line.done(first_out)


def run_ffn(cap, ffn, resid, cot_all, meta, win, wdn, parts, some):
    tok, width = ffn.shape
    ff = wdn.shape[2]
    planes = cot_all.shape[0]
    ctx = win.shape[0]
    rows = planes * cap
    piece = width // (ctx * parts)
    win = win.reshape(ctx, ctx, parts, piece, 2 * ff)
    vm, anyspace = pl.BlockSpec(memory_space=pltpu.VMEM), pl.BlockSpec(memory_space=pl.ANY)
    shape = jax.ShapeDtypeStruct
    dma = pltpu.SemaphoreType.DMA
    return pl.pallas_call(
        functools.partial(ffn_kernel, cap),
        out_shape=(
            shape((tok, width), BF16),
            shape((tok, width), F32),
            shape((planes, tok), F32),
            shape((ctx, parts, piece, 2 * ff - some), BF16),
            shape((ctx, piece, ff), BF16),
            shape((ctx, piece, some), BF16),
        ),
        in_specs=[anyspace, anyspace, anyspace, vm, anyspace, anyspace],
        out_specs=(vm, vm, vm, anyspace, vm, vm),
        scratch_shapes=[
            pltpu.VMEM((planes, tok, width), BF16),
            pltpu.VMEM((planes, 8, tok), F32),
            pltpu.VMEM((planes, tok, width), BF16),
            pltpu.VMEM((ctx, parts, piece, 2 * ff), BF16),
            pltpu.VMEM((width, ff), BF16),
            pltpu.VMEM((rows, width), BF16),
            pltpu.VMEM((rows, width), BF16),
            pltpu.VMEM((rows, ff), BF16),
            pltpu.VMEM((rows, 2 * ff), BF16),
            pltpu.VMEM((4 * cap, width), BF16),
            pltpu.VMEM((planes, 8, tok), F32),
            pltpu.VMEM((planes, 8, tok), F32),
            pltpu.VMEM((2 * ff, width), BF16),
            pltpu.VMEM((ctx, parts, piece, ff), BF16),
            dma((5,)),
            dma((GATHER_COPIES,)),
            dma((GATHER_COPIES,)),
            dma((planes - 1,)),
            dma((planes - 1,)),
            dma((planes - 1,)),
            dma((planes - 1,)),
            dma((10,)),
            dma((10,)),
        ]
        + plane_scratch(tok, width)
        + expert_scratch(ctx, parts, piece, ff)
        + expert_scratch(ctx, parts, piece, some),
        compiler_params=pltpu.CompilerParams(
            collective_id=1, has_side_effects=True, vmem_limit_bytes=63 * 2**20
        ),
        cost_estimate=pl.CostEstimate(flops=25 * 10**9, bytes_accessed=50 * 10**6, transcendentals=10**6),
    )(ffn, resid, cot_all, meta, win, wdn)


def back_kernel(
    span,
    meta,
    gg,
    lse,
    trig,
    kv,
    queries,
    attended,
    normed,
    router_t,
    gain_two,
    gain_one,
    resid_h,
    cot_h,
    pg_h,
    ffn_in_h,
    hidden_h,
    wout_h,
    wqkv_h,
    gwin_h,
    input_grad,
    qkv_out,
    proj_out,
    one_out,
    two_out,
    *scratch,
):
    wide_f, back, low, attg, mixed, weights, gwin, send, bsend, smalls, total, out_red = scratch[:12]
    mask, delta, kt, dk, dv, kvs, kvr = scratch[12:19]
    load_sem, kv_s, kv_r = scratch[19:22]
    p_zcr, p_zk, p_rx, p_ry, p_s, p_r = scratch[22:28]
    a_rx, a_ry, a_s, a_r = scratch[28:32]
    e_refs, b_refs = scratch[32:38], scratch[38:44]
    qkv_refs, proj_refs = scratch[44:47], scratch[47:50]
    one_refs, two_refs = scratch[50:57], scratch[57:64]
    spot = Spot()
    c, k, z, ctx = spot.c, spot.k, spot.z, spot.ctx
    tok, width = attended.shape
    cols = one_out.shape[2]
    block, piece = out_red.shape[0], proj_out.shape[0]
    heads_kv = KV_HEADS
    half_head = HEAD // 2
    n_experts = meta.shape[0]
    kv_wide = mixed.shape[1] - width
    step = 256

    def load(src, dst, i):
        copy = pltpu.make_async_copy(src, dst, load_sem.at[i])
        copy.start()
        return copy

    gwin_load = load(gwin_h, gwin, 0)
    early = [
        load(resid_h, wide_f, 1),
        load(pg_h, back, 2),
        load(cot_h, input_grad, 3),
        load(ffn_in_h, attg, 4),
    ]
    wout_load = load(wout_h, weights.at[:, pl.ds(0, width)], 5)
    greet([spot.xp, spot.yp, spot.kp, spot.yk], spot.along())
    one = ExpertLine(spot, gwin, 0, cols, *one_refs)
    two = ExpertLine(spot, gwin, cols, cols, *two_refs)
    proj_plane = plane_of(spot, p_zcr, p_zk, p_rx, p_ry, p_s, p_r, low=BACK_LOW)
    half_wide = width // 2
    cut = pl.ds(0, half_wide)
    early_plane = plane_of(spot, *e_refs, low=BACK_LOW)
    late_plane = plane_of(
        spot, p_zcr.at[:, :, cut], p_zk.at[:, :, cut], a_rx, a_ry, a_s, a_r, low=BACK_LOW
    )
    rest_plane = plane_of(spot, *b_refs, low=BACK_LOW)

    def shared_line(ref, refs):
        def own(d):
            return ref.at[rows_at(d * piece, piece)]

        def adder(came, d):
            came[...] = plus(came[...], own(d)[...])

        return Line(spot, own, adder, *refs)

    qkv_line, proj_line = shared_line(total, qkv_refs), shared_line(out_red, proj_refs)

    def put_shared(to, ref, came):
        to[...] = plus(ref[rows_at(z * piece, piece)], *(x[...] for x in came))

    mine, theirs = rows_at(k * block, block), rows_at((1 - k) * block, block)
    gwin_load.wait()
    one.step(1)

    for copy in early:
        copy.wait()
    gate = jnp.concatenate([meta[g, 1:2, :] for g in range(n_experts)], axis=0)
    seen = gate * gg[...]
    mix = seen - gate * jnp.sum(seen, axis=0, keepdims=True)
    mix = jnp.concatenate([mix, jnp.zeros((HEAD - n_experts, tok), F32)], axis=0)
    logit_t = mix.astype(BF16)
    r = wide_f[...]
    inv = lax.rsqrt(jnp.mean(r * r, axis=-1, keepdims=True) + NORM_EPS)
    plain = r * inv
    ffn_grad = back[...] + dot_tn(logit_t[:n_experts], router_t[...])
    gain_row = jnp.sum(ffn_grad * plain, axis=0, keepdims=True)
    scaled = ffn_grad * gain_two[...]
    grad = input_grad[...].astype(F32) + inv * (
        scaled - plain * jnp.mean(scaled * plain, axis=-1, keepdims=True)
    )
    back[...] = grad
    low[...] = grad.astype(BF16)
    lane = lax.broadcasted_iota(jnp.int32, (width, HEAD), 1)
    routed = dot_tn(attg[...], logit_t.T)
    gain_col = jnp.broadcast_to(gain_row, (HEAD, width)).T
    smalls[...] = jnp.where(lane == n_experts, gain_col, routed).astype(BF16)

    for q in (3, 1, 2, 0):
        at = lanes(spot.chips[q] * block, 2 * block)
        send[q] = dot_tn(low[:, at], attended[...]).astype(BF16)
        proj_plane.give(q, send.at[q, theirs])
    wout_load.wait()

    @pl.loop(0, width // step)
    def _(n):
        at = lanes(n * step, step)
        attg[:, at] = dot(low[...], weights[:, at]).astype(BF16)

    wqkv_load = load(wqkv_h, weights, 5)
    hidden_load = load(hidden_h, low, 1)

    def start_plane(plane, at):
        plane.fold(3, send[3, mine, at])
        plane.across()
        plane.fold(1, send[1, mine, at])
        plane.fold(2, send[2, mine, at])
        plane.near()
        plane.fold(0, send[0, mine, at])

    def qkv_tiles(plane, at):
        for q in (3, 1, 2, 0):
            rows = lanes(spot.chips[q] * block, 2 * block)
            send[q, :, at] = dot_tn(normed[:, rows], mixed[:, at]).astype(BF16)
            plane.give(q, send.at[q, theirs, at])

    start_plane(proj_plane, pl.ds(0, width))

    seq = kv.shape[0]
    spans = span.shape[1]
    size = seq // spans
    per = spans // ctx
    along_q = lax.broadcasted_iota(jnp.int32, (size, tok), 1)
    q_pos = jnp.where(along_q < size, span[0, c * per] * size, (span[0, c * per + 1] - 1) * size) + along_q
    for s in range(spans):
        k_pos = span[0, s] * size + lax.broadcasted_iota(jnp.int32, (size, tok), 0)
        mask[s * size : (s + 1) * size, :] = jnp.where(k_pos <= q_pos, 0.0, MASKED)

    lane_h = lax.broadcasted_iota(jnp.int32, (tok, HEAD), 1)
    deltas = jnp.zeros((tok, HEAD), F32)
    for h in range(HEADS):
        at = slice(h * HEAD, (h + 1) * HEAD)
        term = jnp.sum(attg[:, at].astype(F32) * attended[:, at].astype(F32), axis=-1, keepdims=True)
        deltas = jnp.where(lane_h == h, term, deltas)
    delta[...] = deltas.T
    for g in range(heads_kv):
        kt[g] = kv[:, g * HEAD : (g + 1) * HEAD].astype(F32).T.astype(BF16)

    cosine, sine = trig[0], trig[1]

    def unrotate(w):
        return w * cosine - pltpu.roll(w, half_head, 1) * sine

    def head(g, h):
        at = lanes(h * HEAD, HEAD)
        k_at = slice(g * HEAD, (g + 1) * HEAD)
        v_at = slice((heads_kv + g) * HEAD, (heads_kv + g + 1) * HEAD)
        q, a = queries[:, at], attg[:, at]
        soft = jnp.exp(dot_nt(kv[:, k_at], q) + mask[...] - lse[pl.ds(h, 1), :])
        prob = dot_nt(kv[:, v_at], a)
        score = (soft * (prob - delta[pl.ds(h, 1), :])).astype(BF16)
        mixed[:, at] = (unrotate(dot(kt[g], score).T) * HEAD**-0.5).astype(BF16)
        dk[...] += dot(score, q)
        dv[...] += dot(soft.astype(BF16), a)

    def heads(g, first, count):
        @pl.loop(first, first + count)
        def _(h):
            head(g, h)

    def clear():
        dk[...] = jnp.zeros(dk.shape, F32)
        dv[...] = jnp.zeros(dv.shape, F32)

    flip_c = lax.rem(c + 2, ctx)
    near_c = c + 1 - 2 * k
    across_c = lax.rem(near_c + 2, ctx)

    def kv_copy(g, src, i, dev):
        return remote(src, kvr.at[g, i], kv_s.at[g, i], kv_r.at[g, i], dev)

    def send_kv(g):
        for cc in range(ctx):
            rows = slice(cc * tok, (cc + 1) * tok)
            kvs[g, cc, :, :HEAD] = dk[rows, :].astype(BF16)
            kvs[g, cc, :, HEAD:] = dv[rows, :].astype(BF16)
        kv_copy(g, kvs.at[g, across_c], 1, spot.kp).start()
        kv_copy(g, kvs.at[g, near_c], 0, spot.kp).start()

    def pass_kv(g):
        kv_copy(g, kvs.at[g, across_c], 1, spot.kp).wait_recv()
        kvs[g, flip_c] = plus(kvs[g, flip_c], kvr[g, 1])
        kv_copy(g, kvs.at[g, flip_c], 2, spot.yp).start()

    clear()
    heads(0, 0, 2)
    one.step(2)
    heads(0, 2, 4)
    send_kv(0)
    clear()
    proj_plane.turn()
    proj_plane.given()
    qkv_tiles(early_plane, pl.ds(0, half_wide))
    heads(1, 6, 1)
    start_plane(early_plane, pl.ds(0, half_wide))
    pass_kv(0)
    one.step(3)
    two.step(1)
    heads(1, 7, 2)
    heads(1, 9, 3)
    send_kv(1)
    pass_kv(1)
    early_plane.turn()
    for rows, terms in proj_plane.total():
        out_red[rows, :] = summed(terms).astype(BF16)
    proj_line.step(1)
    proj_plane.done()
    for g in range(heads_kv):
        kv_copy(g, kvs.at[g, near_c], 0, spot.kp).wait_recv()
        kv_copy(g, kvs.at[g, flip_c], 2, spot.yp).wait_recv()
        own = kvs[g, c].astype(F32) + kvr[g, 0].astype(F32) + kvr[g, 2].astype(F32)
        at = width + g * HEAD
        mixed[:, at : at + HEAD] = unrotate(own[:, :HEAD]).astype(BF16)
        at = width + (heads_kv + g) * HEAD
        mixed[:, at : at + HEAD] = own[:, HEAD:].astype(BF16)

    qkv_tiles(late_plane, pl.ds(half_wide, half_wide))
    start_plane(late_plane, pl.ds(half_wide, half_wide))
    proj_line.step(2)
    wqkv_load.wait()

    @pl.loop(0, width // step)
    def _(n):
        at = lanes(n * step, step)
        wide_f[:, at] = dot_nt(mixed[...], weights[at, :])

    two.step(2)
    hidden_load.wait()
    x = low[...].astype(F32)
    inv = lax.rsqrt(jnp.mean(x * x, axis=-1, keepdims=True) + NORM_EPS)
    plain = x * inv
    ng = wide_f[...]
    gain_row = jnp.sum(ng * plain, axis=0, keepdims=True)
    scaled = ng * gain_one[...]
    input_grad[...] = (
        back[...] + inv * (scaled - plain * jnp.mean(scaled * plain, axis=-1, keepdims=True))
    ).astype(BF16)
    lane = lax.broadcasted_iota(jnp.int32, (width, HEAD), 1)
    gain_col = jnp.broadcast_to(gain_row, (HEAD, width)).T
    smalls[...] = jnp.where(lane == HEAD - 1, gain_col, smalls[...].astype(F32)).astype(BF16)
    for q in (3, 1, 2, 0):
        at = lanes(spot.chips[q] * block, 2 * block)
        bsend[q, :, :kv_wide] = dot_tn(normed[:, at], mixed[:, width:]).astype(BF16)
        bsend[q, :, kv_wide:] = smalls[rows_at(spot.chips[q] * block, 2 * block), :]
        rest_plane.give(q, bsend.at[q, theirs])
    rest_plane.fold(3, bsend[3, mine])
    rest_plane.across()
    rest_plane.fold(1, bsend[1, mine])
    rest_plane.fold(2, bsend[2, mine])
    rest_plane.near()
    rest_plane.fold(0, bsend[0, mine])
    late_plane.turn()
    rest_plane.turn()
    two.step(3)
    one.final()
    proj_line.step(3)
    for rows, terms in early_plane.total():
        total[rows, :half_wide] = summed(terms).astype(BF16)
    for rows, terms in late_plane.total():
        total[rows, half_wide:width] = summed(terms).astype(BF16)
    for rows, terms in rest_plane.total():
        total[rows, width:] = summed(terms).astype(BF16)
    qkv_line.step(1)
    one.done(one_out)
    qkv_line.step(2)
    two.final()
    proj_line.final(lambda *came: put_shared(proj_out, out_red, came))
    qkv_line.step(3)
    proj_line.done()
    early_plane.done()
    late_plane.done()
    rest_plane.done()
    for g in range(heads_kv):
        kv_copy(g, kvs.at[g, near_c], 0, spot.kp).wait_send()
        kv_copy(g, kvs.at[g, across_c], 1, spot.kp).wait_send()
        kv_copy(g, kvs.at[g, flip_c], 2, spot.yp).wait_send()
    qkv_line.final(lambda *came: put_shared(qkv_out, total, came))
    qkv_line.done()
    two.done(two_out)


def run_back(
    span, meta, gg, lse, trig, kv, queries, attended, normed, router_t, gain_two, gain_one,
    resid, cot, pg, ffn_in, hidden, wout, wqkv, gwin,
):
    tok, width = attended.shape
    seq, kv_cols = kv.shape
    planes = meta.shape[0]
    ctx, parts, rows, wide = gwin.shape
    cols = wide // 2
    block = width // planes
    piece = block // parts
    rest = kv_cols + HEAD
    vm, anyspace = pl.BlockSpec(memory_space=pltpu.VMEM), pl.BlockSpec(memory_space=pl.ANY)
    sm = pl.BlockSpec(memory_space=pltpu.SMEM)
    shape = jax.ShapeDtypeStruct
    dma = pltpu.SemaphoreType.DMA
    return pl.pallas_call(
        back_kernel,
        out_shape=(
            shape((tok, width), BF16),
            shape((piece, width + rest), BF16),
            shape((piece, width), BF16),
            shape((ctx, rows, cols), BF16),
            shape((ctx, rows, cols), BF16),
        ),
        in_specs=[sm] + [vm] * 11 + [anyspace] * 8,
        out_specs=(vm,) * 5,
        scratch_shapes=[
            pltpu.VMEM((tok, width), F32),
            pltpu.VMEM((tok, width), F32),
            pltpu.VMEM((tok, width), BF16),
            pltpu.VMEM((tok, width), BF16),
            pltpu.VMEM((tok, width + kv_cols), BF16),
            pltpu.VMEM(wqkv.shape, BF16),
            pltpu.VMEM(gwin.shape, BF16),
            pltpu.VMEM((4, 2 * block, width), BF16),
            pltpu.VMEM((4, 2 * block, rest), BF16),
            pltpu.VMEM((width, HEAD), BF16),
            pltpu.VMEM((block, width + rest), BF16),
            pltpu.VMEM((block, width), BF16),
            pltpu.VMEM((seq, tok), F32),
            pltpu.VMEM((HEAD, tok), F32),
            pltpu.VMEM((KV_HEADS, HEAD, seq), BF16),
            pltpu.VMEM((seq, HEAD), F32),
            pltpu.VMEM((seq, HEAD), F32),
            pltpu.VMEM((KV_HEADS, ctx, tok, 2 * HEAD), BF16),
            pltpu.VMEM((KV_HEADS, 3, tok, 2 * HEAD), BF16),
            dma((6,)),
            dma((KV_HEADS, 3)),
            dma((KV_HEADS, 3)),
        ]
        + plane_scratch(block, width, BACK_LOW)
        + plane_scratch(block, width // 2, BACK_LOW)[2:]
        + plane_scratch(block, width // 2, BACK_LOW)
        + plane_scratch(block, rest, BACK_LOW)
        + line_scratch(parts, (piece, width + rest))
        + line_scratch(parts, (piece, width))
        + expert_scratch(ctx, parts, rows, cols)
        + expert_scratch(ctx, parts, rows, cols),
        compiler_params=pltpu.CompilerParams(
            collective_id=2, has_side_effects=True, vmem_limit_bytes=63 * 2**20
        ),
        cost_estimate=pl.CostEstimate(flops=12 * 10**9, bytes_accessed=60 * 10**6, transcendentals=4 * 10**6),
    )(
        span, meta, gg, lse, trig, kv, queries, attended, normed, router_t, gain_two, gain_one,
        resid, cot, pg, ffn_in, hidden, wout, wqkv, gwin,
    )


def finish_kernel(
    n_experts,
    output_h,
    input_h,
    qkv_h,
    proj_h,
    first_h,
    one_h,
    two_h,
    down_h,
    output,
    input_grad,
    gain_one,
    gain_two,
    qkv,
    proj,
    router,
    inner,
    down,
    low_qkv,
    low_proj,
    low_first,
    low_one,
    low_two,
    low_down,
    low_out,
    low_in,
    inner_full,
    down_full,
    sem,
    out_sem,
):
    whole = []
    loads = [
        pltpu.make_async_copy(src, dst, sem.at[i])
        for i, (src, dst) in enumerate(
            (
                (down_h, low_down),
                (first_h, low_first),
                (one_h, low_one),
                (two_h, low_two),
                (qkv_h, low_qkv),
                (proj_h, low_proj),
                (output_h, low_out),
                (input_h, low_in),
            )
        )
    ]
    for copy in loads:
        copy.start()
    loads[0].wait()
    down_full[...] = low_down[...].astype(F32)
    whole.append(pltpu.make_async_copy(down_full, down, out_sem.at[2]))
    whole[-1].start()
    at = 0
    for load, low in zip(loads[1:4], (low_first, low_one, low_two)):
        load.wait()
        size = low.shape[2]
        inner_full[:, :, at : at + size] = low[...].astype(F32)
        at += size
    whole.append(pltpu.make_async_copy(inner_full, inner, out_sem.at[3]))
    whole[-1].start()
    for i, (low, to) in enumerate(((low_out, output), (low_in, input_grad))):
        loads[6 + i].wait()
        whole.append(pltpu.make_async_copy(low, to, out_sem.at[i]))
        whole[-1].start()
    for load in loads[4:6]:
        load.wait()
    wide = qkv.shape[1]
    qkv[...] = low_qkv[:, :wide].astype(F32)
    proj[...] = low_proj[...].astype(F32)
    small = low_qkv[:, wide:].astype(F32)
    piece = small.shape[0]
    same = lax.broadcasted_iota(jnp.int32, (piece, piece), 0) == lax.broadcasted_iota(
        jnp.int32, (piece, piece), 1
    )

    def column(at):
        return jnp.sum(jnp.where(same, small[:, at : at + 1], 0.0), axis=0, keepdims=True)

    gain_one[...] = column(HEAD - 1)[0]
    gain_two[...] = column(n_experts)[0]
    for at in range(n_experts):
        router[at : at + 1, :] = column(at)
    for copy in whole:
        copy.wait()


def run_finish(n_experts, output, input_grad, qkv, proj, first, one, two, down):
    piece, width = proj.shape
    ctx, rows, ff = down.shape
    shape = jax.ShapeDtypeStruct
    vm, anyspace = pl.BlockSpec(memory_space=pltpu.VMEM), pl.BlockSpec(memory_space=pl.ANY)
    return pl.pallas_call(
        functools.partial(finish_kernel, n_experts),
        out_shape=(
            shape(output.shape, BF16),
            shape(input_grad.shape, BF16),
            shape((piece,), F32),
            shape((piece,), F32),
            shape((piece, qkv.shape[1] - HEAD), F32),
            shape((piece, width), F32),
            shape((n_experts, piece), F32),
            shape((ctx, rows, 2 * ff), F32),
            shape((ctx, rows, ff), F32),
        ),
        in_specs=[anyspace] * 8,
        out_specs=(anyspace, anyspace, vm, vm, vm, vm, vm, anyspace, anyspace),
        scratch_shapes=[pltpu.VMEM(x.shape, BF16) for x in (qkv, proj, first, one, two, down, output, input_grad)]
        + [
            pltpu.VMEM((ctx, rows, 2 * ff), F32),
            pltpu.VMEM((ctx, rows, ff), F32),
            pltpu.SemaphoreType.DMA((8,)),
            pltpu.SemaphoreType.DMA((4,)),
        ],
        compiler_params=pltpu.CompilerParams(vmem_limit_bytes=56 * 2**20),
    )(output, input_grad, qkv, proj, first, one, two, down)


def local(
    hidden_in,
    span_order,
    expert_ids,
    priority,
    gain_attn,
    qkv_weight,
    out_weight,
    gain_ffn,
    router,
    in_weight,
    down_weight,
    cotangent,
):
    _, tok_rows, width = hidden_in.shape
    ctx, parts = lax.axis_size("context"), lax.axis_size("dp")
    planes = ctx * lax.axis_size("expert")
    n_experts = router.shape[1]
    top_k = expert_ids.shape[2]
    capacity = (9 * tok_rows * top_k + 8 * n_experts - 1) // (8 * n_experts)
    ff = down_weight.shape[2]
    half_freqs = ROPE_BASE ** (np.arange(HEAD // 2) * (-2.0 / HEAD))
    freqs = np.concatenate([half_freqs, half_freqs])[None].astype(np.float32)
    router_t = router.T
    hidden, cot = hidden_in[0], cotangent[0]
    normed, queries, kv, lse, attended, resid, ffn_in, trig, meta, cot_all = run_front(
        capacity,
        span_order,
        hidden,
        cot,
        gain_attn,
        freqs,
        gain_ffn,
        router_t,
        expert_ids[0].T,
        priority[0].T,
        qkv_weight,
        out_weight,
        ctx,
        planes,
    )
    output, pair_sum, gate_grad, gwin, down, in_first = run_ffn(
        capacity, ffn_in, resid, cot_all, meta, in_weight, down_weight, parts, ff // 3
    )
    input_grad, qkv_sum, proj_sum, in_one, in_two = run_back(
        span_order,
        meta,
        gate_grad,
        lse,
        trig,
        kv,
        queries,
        attended,
        normed,
        router_t,
        gain_ffn,
        gain_attn,
        resid,
        cot,
        pair_sum,
        ffn_in,
        hidden,
        out_weight,
        qkv_weight,
        gwin,
    )
    output, input_grad, gain_one, gain_two, qkv_grad, proj_grad, router_grad, inner_grad, down_grad = run_finish(
        n_experts, output, input_grad, qkv_sum, proj_sum, in_first, in_one, in_two, down
    )
    return (
        output[None],
        input_grad[None],
        gain_one,
        qkv_grad,
        proj_grad,
        gain_two,
        router_grad.T,
        inner_grad,
        down_grad,
    )


def general(
    hidden_in,
    span_order,
    expert_ids,
    priority,
    gain_attn,
    qkv_weight,
    out_weight,
    gain_ffn,
    router,
    in_weight,
    down_weight,
    cotangent,
):
    tok_rows = hidden_in.shape[1]
    width = hidden_in.shape[2]
    contexts = lax.axis_size("context")
    span_len = tok_rows // 2
    seq_len = tok_rows * contexts
    group = HEADS // KV_HEADS
    q_cols = HEADS * HEAD
    kv_cols = KV_HEADS * HEAD
    scale = HEAD ** (-0.5)
    local_experts = in_weight.shape[0]
    n_experts = local_experts * lax.axis_size("expert")
    top_k = expert_ids.shape[2]
    capacity = (9 * tok_rows * top_k + 8 * n_experts - 1) // (8 * n_experts)
    ff_width = down_weight.shape[2]
    seq_spans = span_order[0]
    stored = jnp.arange(seq_len) // span_len
    all_pos = (seq_spans[stored] * span_len + jnp.arange(seq_len) % span_len).astype(jnp.float32)
    my_pos = lax.dynamic_slice_in_dim(all_pos, lax.axis_index("context") * tok_rows, tok_rows)
    cosine, sine = rope_tables(my_pos, HEAD)
    inputs = hidden_in[0].astype(jnp.float32)
    inv_one = lax.rsqrt(jnp.mean(inputs * inputs, axis=-1, keepdims=True) + NORM_EPS)
    plain_one = inputs * inv_one
    normed = (plain_one * gain_attn).astype(jnp.bfloat16)
    mixed = jnp.dot(normed, qkv_weight, preferred_element_type=jnp.float32)
    queries = (
        rotate(mixed[:, :q_cols].reshape(tok_rows, HEADS, HEAD), cosine, sine) * scale
    ).astype(jnp.bfloat16)
    keys = rotate(
        mixed[:, q_cols : q_cols + kv_cols].reshape(tok_rows, KV_HEADS, HEAD), cosine, sine
    ).astype(jnp.bfloat16)
    values = mixed[:, q_cols + kv_cols :].reshape(tok_rows, KV_HEADS, HEAD).astype(jnp.bfloat16)
    grouped = queries.reshape(tok_rows, KV_HEADS, group, HEAD)

    def key_scores(key_piece):
        scores = jnp.einsum(
            "qkgd,skd->kgqs", grouped, key_piece, preferred_element_type=jnp.float32
        )
        visible = all_pos[None, None, None, :] <= my_pos[None, None, :, None]
        return (jnp.where(visible, scores, MASKED), visible)

    running = jnp.full((KV_HEADS, group, tok_rows), MASKED, jnp.float32)
    key_piece = lax.all_gather(keys, "context", axis=0, tiled=True)
    value_piece = lax.all_gather(values, "context", axis=0, tiled=True)
    scores, visible = key_scores(key_piece)
    newest = jnp.maximum(running, jnp.max(scores, axis=-1))
    weights = jnp.where(visible, jnp.exp(scores - newest[..., None]), 0.0)
    totals = jnp.sum(weights, axis=-1)
    accum = jnp.einsum(
        "kgqs,skd->kgqd",
        weights.astype(jnp.bfloat16),
        value_piece,
        preferred_element_type=jnp.float32,
    )
    running, totals, accum = (newest, totals, accum)
    log_total = running + jnp.log(totals)
    attended = (
        (accum / totals[..., None])
        .transpose(2, 0, 1, 3)
        .reshape(tok_rows, q_cols)
        .astype(jnp.bfloat16)
    )
    resid = inputs + jnp.einsum(
        "rh,dh->rd", attended, out_weight, preferred_element_type=jnp.float32
    )
    inv_two = lax.rsqrt(jnp.mean(resid * resid, axis=-1, keepdims=True) + NORM_EPS)
    plain_two = resid * inv_two
    ffn_in = (plain_two * gain_ffn).astype(jnp.bfloat16)
    logits = jnp.dot(ffn_in, router, preferred_element_type=jnp.float32)
    token_ids = expert_ids[0]
    gates = softmax_last(jnp.take_along_axis(logits, token_ids, axis=1))
    slots = route(token_ids, priority[0], n_experts, capacity)
    pair_rows = jnp.repeat(ffn_in, top_k, axis=0)
    send_rows = (
        jnp.zeros((n_experts * capacity, width), jnp.bfloat16).at[slots].set(pair_rows, mode="drop")
    )
    received = lax.all_to_all(
        send_rows.reshape(n_experts, capacity, width),
        "expert",
        split_axis=0,
        concat_axis=1,
        tiled=True,
    )
    inner = jnp.einsum("erd,edf->erf", received, in_weight, preferred_element_type=jnp.float32)
    gate_part = inner[..., :ff_width]
    up_part = inner[..., ff_width:]
    sigma = 1.0 / (1.0 + jnp.exp(-gate_part))
    activated = gate_part * sigma
    hidden = (activated * up_part).astype(jnp.bfloat16)
    expert_out = jnp.einsum(
        "erf,edf->erd", hidden, down_weight, preferred_element_type=jnp.float32
    ).astype(jnp.bfloat16)
    returned = lax.all_to_all(
        expert_out, "expert", split_axis=1, concat_axis=0, tiled=True
    ).reshape(n_experts * capacity, width)
    padded = jnp.concatenate([returned, jnp.zeros((1, width), jnp.bfloat16)], axis=0)
    picked = padded[slots].reshape(tok_rows, top_k, width)
    output = (resid + jnp.sum(gates[:, :, None] * picked, axis=1)).astype(jnp.bfloat16)
    cot_low = cotangent[0]
    cot_full = cot_low.astype(jnp.float32)
    gate_grad = jnp.einsum("rkd,rd->rk", picked, cot_low, preferred_element_type=jnp.float32)
    ret_grad = (
        (gates[:, :, None] * cot_full[:, None, :])
        .astype(jnp.bfloat16)
        .reshape(tok_rows * top_k, width)
    )
    send_grad = (
        jnp.zeros((n_experts * capacity, width), jnp.bfloat16).at[slots].set(ret_grad, mode="drop")
    )
    received_grad = lax.all_to_all(
        send_grad.reshape(n_experts, capacity, width),
        "expert",
        split_axis=0,
        concat_axis=1,
        tiled=True,
    )
    hid_grad = jnp.einsum(
        "erd,edf->erf", received_grad, down_weight, preferred_element_type=jnp.float32
    )
    slope = sigma * (1.0 + gate_part * (1.0 - sigma))
    inner_grad = jnp.concatenate(
        [hid_grad * up_part * slope, hid_grad * activated], axis=-1
    ).astype(jnp.bfloat16)
    row_grad = jnp.einsum(
        "erf,edf->erd", inner_grad, in_weight, preferred_element_type=jnp.float32
    ).astype(jnp.bfloat16)
    part_rows = received
    expert_in = (
        lax.psum_scatter(
            jnp.einsum(
                "erd,erf->def", part_rows, inner_grad, preferred_element_type=jnp.float32
            ).astype(jnp.bfloat16),
            ("context", "dp"),
            scatter_dimension=0,
            tiled=True,
        )
        .astype(jnp.float32)
        .transpose(1, 0, 2)
    )
    part_rows = received_grad
    expert_down = (
        lax.psum_scatter(
            jnp.einsum(
                "erd,erf->def", part_rows, hidden, preferred_element_type=jnp.float32
            ).astype(jnp.bfloat16),
            ("context", "dp"),
            scatter_dimension=0,
            tiled=True,
        )
        .astype(jnp.float32)
        .transpose(1, 0, 2)
    )
    back_rows = lax.all_to_all(row_grad, "expert", split_axis=1, concat_axis=0, tiled=True).reshape(
        n_experts * capacity, width
    )
    back_padded = jnp.concatenate([back_rows, jnp.zeros((1, width), jnp.bfloat16)], axis=0)
    pair_grad = back_padded[slots].reshape(tok_rows, top_k, width)
    mix_grad = gates * (gate_grad - jnp.sum(gates * gate_grad, axis=-1, keepdims=True))
    matches = token_ids[:, :, None] == jnp.arange(n_experts)[None, None, :]
    logit_grad = jnp.sum(jnp.where(matches, mix_grad[:, :, None], 0.0), axis=1).astype(jnp.bfloat16)
    router_part = jnp.einsum("rd,re->de", ffn_in, logit_grad, preferred_element_type=jnp.float32)
    ffn_grad = jnp.sum(pair_grad.astype(jnp.float32), axis=1) + jnp.einsum(
        "re,de->rd", logit_grad, router, preferred_element_type=jnp.float32
    )
    gain_ffn_part = jnp.sum(ffn_grad * plain_two, axis=0)
    scaled_two = ffn_grad * gain_ffn
    resid_grad = cot_full + inv_two * (
        scaled_two - plain_two * jnp.mean(scaled_two * plain_two, axis=-1, keepdims=True)
    )
    resid_low = resid_grad.astype(jnp.bfloat16)
    out_part = jnp.einsum("rd,rh->dh", resid_low, attended, preferred_element_type=jnp.float32)
    att_grad = jnp.einsum(
        "rd,dh->rh", resid_low, out_weight, preferred_element_type=jnp.float32
    ).astype(jnp.bfloat16)
    att_heads = att_grad.reshape(tok_rows, KV_HEADS, group, HEAD)
    row_delta = jnp.sum(
        att_heads.astype(jnp.float32)
        * attended.reshape(tok_rows, KV_HEADS, group, HEAD).astype(jnp.float32),
        axis=-1,
    ).transpose(1, 2, 0)
    key_piece = lax.all_gather(keys, "context", axis=0, tiled=True)
    value_piece = lax.all_gather(values, "context", axis=0, tiled=True)
    scores, visible = key_scores(key_piece)
    soft = jnp.exp(scores - log_total[..., None])
    prob_grad = jnp.einsum(
        "qkgd,skd->kgqs", att_heads, value_piece, preferred_element_type=jnp.float32
    )
    score_grad = (soft * (prob_grad - row_delta[..., None])).astype(jnp.bfloat16)
    query_acc = jnp.einsum(
        "kgqs,skd->kgqd", score_grad, key_piece, preferred_element_type=jnp.float32
    )
    key_part = jnp.einsum("kgqs,qkgd->skd", score_grad, grouped, preferred_element_type=jnp.float32)
    value_part = jnp.einsum(
        "kgqs,qkgd->skd", soft.astype(jnp.bfloat16), att_heads, preferred_element_type=jnp.float32
    )
    pair_acc = jnp.stack([key_part, value_part], axis=1)
    query_acc, pair_acc = (query_acc, pair_acc)
    own_pairs = lax.psum_scatter(
        pair_acc.astype(jnp.bfloat16), "context", scatter_dimension=0, tiled=True
    ).astype(jnp.float32)
    query_grad = (
        unrotate(query_acc.transpose(2, 0, 1, 3).reshape(tok_rows, HEADS, HEAD), cosine, sine)
        * scale
    )
    key_grad = unrotate(own_pairs[:, 0], cosine, sine)
    mixed_grad = jnp.concatenate(
        [
            query_grad.reshape(tok_rows, q_cols),
            key_grad.reshape(tok_rows, kv_cols),
            own_pairs[:, 1].reshape(tok_rows, kv_cols),
        ],
        axis=-1,
    ).astype(jnp.bfloat16)
    qkv_part = jnp.einsum("rd,rc->dc", normed, mixed_grad, preferred_element_type=jnp.float32)
    norm_grad = jnp.einsum("rc,dc->rd", mixed_grad, qkv_weight, preferred_element_type=jnp.float32)
    gain_attn_part = jnp.sum(norm_grad * plain_one, axis=0)
    scaled_one = norm_grad * gain_attn
    input_grad = (
        resid_grad
        + inv_one
        * (scaled_one - plain_one * jnp.mean(scaled_one * plain_one, axis=-1, keepdims=True))
    ).astype(jnp.bfloat16)
    gain_attn_grad, qkv_grad, out_proj_grad, gain_ffn_grad, router_grad = (
        lax.psum_scatter(
            gain_attn_part, ("expert", "context", "dp"), scatter_dimension=0, tiled=True
        ),
        lax.psum_scatter(qkv_part, ("expert", "context", "dp"), scatter_dimension=0, tiled=True),
        lax.psum_scatter(out_part, ("expert", "context", "dp"), scatter_dimension=0, tiled=True),
        lax.psum_scatter(
            gain_ffn_part, ("expert", "context", "dp"), scatter_dimension=0, tiled=True
        ),
        lax.psum_scatter(router_part, ("expert", "context", "dp"), scatter_dimension=0, tiled=True),
    )
    return (
        output[None],
        input_grad[None],
        gain_attn_grad,
        qkv_grad,
        out_proj_grad,
        gain_ffn_grad,
        router_grad,
        expert_in,
        expert_down,
    )


def solution(mesh):
    in_specs = (
        P(("expert", "dp"), "context", None),
        P(("expert", "dp"), None),
        P(("expert", "dp"), "context", None),
        P(("expert", "dp"), "context", None),
        P(),
        P(),
        P(),
        P(),
        P(),
        P("expert", None, None),
        P("expert", None, None),
        P(("expert", "dp"), "context", None),
    )
    out_specs = (
        P(("expert", "dp"), "context", None),
        P(("expert", "dp"), "context", None),
        P(("expert", "context", "dp")),
        P(("expert", "context", "dp"), None),
        P(("expert", "context", "dp"), None),
        P(("expert", "context", "dp")),
        P(("expert", "context", "dp"), None),
        P("expert", ("context", "dp"), None),
        P("expert", ("context", "dp"), None),
    )
    tuned = dict(mesh.shape) == {"expert": 2, "context": 4, "dp": 4}
    body = local if tuned else general
    return jax.shard_map(body, mesh=mesh, in_specs=in_specs, out_specs=out_specs, check_vma=False)
```

```python
import functools

import jax
import jax.numpy as jnp
import numpy as np
from jax import lax
from jax.experimental import pallas as pl
from jax.experimental.pallas import tpu as pltpu
from jax.sharding import PartitionSpec as P

HEADS = 12
KV_HEADS = 2
HEAD = 128


ROPE_BASE = 1000000.0
NORM_EPS = 1e-06
MASKED = -1e30


def rope_tables(positions, head_size):
    half_size = head_size // 2
    freqs = ROPE_BASE ** (jnp.arange(half_size).astype(jnp.float32) * (-2.0 / head_size))
    angles = positions[:, None] * freqs[None, :]
    return (jnp.cos(angles)[:, None, :], jnp.sin(angles)[:, None, :])


def rotate(values, cosine, sine):
    half_size = values.shape[-1] // 2
    first = values[..., :half_size]
    second = values[..., half_size:]
    return jnp.concatenate(
        [first * cosine - second * sine, second * cosine + first * sine], axis=-1
    )


def unrotate(values, cosine, sine):
    half_size = values.shape[-1] // 2
    first = values[..., :half_size]
    second = values[..., half_size:]
    return jnp.concatenate(
        [first * cosine + second * sine, second * cosine - first * sine], axis=-1
    )


def softmax_last(scores):
    shifted = jnp.exp(scores - jnp.max(scores, axis=-1, keepdims=True))
    return shifted / jnp.sum(shifted, axis=-1, keepdims=True)


def route(block_ids, block_order, n_experts, capacity):
    flat_ids = block_ids.reshape(-1)
    flat_order = block_order.reshape(-1)
    choose = (flat_ids[:, None] == jnp.arange(n_experts)[None, :]).astype(jnp.int32)
    ordered = jnp.zeros_like(choose).at[flat_order].set(choose)
    earlier = jnp.cumsum(ordered, axis=0, dtype=jnp.int32) - ordered
    ranks = jnp.sum(earlier[flat_order] * choose, axis=1)
    return jnp.where(ranks < capacity, flat_ids * capacity + ranks, n_experts * capacity)


MESH = pl.DeviceIdType.MESH
F32 = jnp.float32
BF16 = jnp.bfloat16
BACK_LOW = 96
OUT_LOW = 128
FRONT_LOW = 96
FRONT_AHEAD = 64


def dot(a, b):
    return jnp.dot(a, b, preferred_element_type=F32)


def dot_nt(a, b):
    return lax.dot_general(a, b, (((1,), (1,)), ((), ())), preferred_element_type=F32)


def dot_tn(a, b):
    return lax.dot_general(a, b, (((0,), (0,)), ((), ())), preferred_element_type=F32)


def plus(a, *more):
    total = a.astype(F32)
    for b in more:
        total = total + b.astype(F32)
    return total.astype(BF16)


def lanes(at, size):
    return pl.ds(pl.multiple_of(at, 128), size)


def rows_at(at, size):
    return pl.ds(pl.multiple_of(at, 16), size)


def remote(src, dst, s, r, dev):
    return pltpu.make_async_remote_copy(
        src_ref=src, dst_ref=dst, send_sem=s, recv_sem=r, device_id=dev, device_id_type=MESH
    )


class Spot:
    def __init__(self):
        e, c, z = lax.axis_index("expert"), lax.axis_index("context"), lax.axis_index("dp")
        self.ctx = lax.axis_size("context")
        self.parts = lax.axis_size("dp")
        self.planes = self.ctx * lax.axis_size("expert")
        y, k = lax.div(c, 2), lax.rem(c, 2)
        self.e, self.c, self.z, self.k = e, c, z, k
        self.me = e * self.ctx + c
        self.xp, self.yp = (1 - e, c, z), (e, (1 - y) * 2 + k, z)
        self.kp, self.yk = (e, y * 2 + 1 - k, z), (e, (1 - y) * 2 + 1 - k, z)
        self.chips = [
            eq * self.ctx + yq * 2 for eq, yq in ((e, y), (1 - e, y), (e, 1 - y), (1 - e, 1 - y))
        ]

    def others(self):
        found = []
        for step in range(1, self.planes):
            other = lax.rem(self.me + step, self.planes)
            found.append((other, (lax.div(other, self.ctx), lax.rem(other, self.ctx), self.z)))
        return found

    def along(self):
        e, c, z = self.e, self.c, self.z
        return [(z < self.parts - 1, (e, c, z + 1)), (z > 0, (e, c, z - 1))]


def greet(peers, extra=()):
    barrier = pltpu.get_barrier_semaphore()
    for peer in peers:
        pl.semaphore_signal(barrier, inc=1, device_id=peer, device_id_type=MESH)
    for there, peer in extra:

        @pl.when(there)
        def _():
            pl.semaphore_signal(barrier, inc=1, device_id=peer, device_id_type=MESH)

    count = len(peers)
    for there, _ in extra:
        count = count + there.astype(jnp.int32)
    pl.semaphore_wait(barrier, count)


class Plane:
    def __init__(self, spot, zcr, zk, rx, ry, s, r, zcr_there=None, low=None):
        self.zcr_there = zcr_there or zcr
        self.spot, self.zcr, self.zk, self.rx, self.ry, self.s, self.r = spot, zcr, zk, rx, ry, s, r
        low = low or zk[0].shape[0] // 2
        self.lo, self.hi = pl.ds(0, low), pl.ds(low, zk[0].shape[0] - low)
        self.sent, self.gives = [], []

    def push(self, src, dst, i, dev):
        copy = remote(src, dst, self.s.at[i], self.r.at[i], dev)
        copy.start()
        self.sent.append(copy)

    def arrive(self, dst, i):
        remote(dst, dst, self.s.at[i], self.r.at[i], self.spot.kp).wait_recv()

    def given(self):
        for copy in self.gives:
            copy.wait_send()
        self.gives = []

    def give(self, q, src):
        self.gives.append(remote(src, self.zcr_there[q], self.s.at[q], self.r.at[q], self.spot.kp))
        self.gives[-1].start()

    def fold(self, q, own=None):
        self.arrive(self.zcr[q], q)
        self.zk[q][...] = plus(self.zk[q][...] if own is None else own, self.zcr[q][...])

    def near(self):
        self.push(self.zk[1].at[self.lo], self.rx[1], 5, self.spot.xp)
        self.push(self.zk[2].at[self.hi], self.ry[1], 8, self.spot.yp)

    def across(self):
        self.push(self.zk[3].at[self.lo], self.rx[0], 4, self.spot.xp)
        self.push(self.zk[3].at[self.hi], self.ry[0], 7, self.spot.yp)

    def turn(self):
        lo, hi = self.lo, self.hi
        self.arrive(self.rx[0], 4)
        self.zk[2][lo] = plus(self.zk[2][lo], self.rx[0][...])
        self.push(self.zk[2].at[lo], self.ry[2], 9, self.spot.yp)
        self.arrive(self.ry[0], 7)
        self.zk[1][hi] = plus(self.zk[1][hi], self.ry[0][...])
        self.push(self.zk[1].at[hi], self.rx[2], 6, self.spot.xp)

    def total(self):
        self.arrive(self.rx[1], 5)
        self.arrive(self.ry[1], 8)
        self.arrive(self.rx[2], 6)
        self.arrive(self.ry[2], 9)
        return (
            (self.lo, (self.zk[0][self.lo], self.rx[1][...], self.ry[2][...])),
            (self.hi, (self.zk[0][self.hi], self.rx[2][...], self.ry[1][...])),
        )

    def done(self):
        self.given()
        for copy in self.sent:
            copy.wait_send()


def plane_of(spot, zcr, zk, rx, ry, s, r, low=None):
    four, block = range(4), zk.shape[1]
    lo, hi = pl.ds(0, low or block // 2), pl.ds(0, block - (low or block // 2))
    return Plane(
        spot,
        [zcr.at[q] for q in four],
        [zk.at[q] for q in four],
        [rx.at[0, lo], rx.at[1, lo], rx.at[2, hi]],
        [ry.at[0, hi], ry.at[1, hi], ry.at[2, lo]],
        s,
        r,
        low=low,
    )


def plane_scratch(block, wide, low=None):
    most = max(low or block // 2, block - (low or block // 2))
    return [
        pltpu.VMEM((4, block, wide), BF16),
        pltpu.VMEM((4, block, wide), BF16),
        pltpu.VMEM((3, most, wide), BF16),
        pltpu.VMEM((3, most, wide), BF16),
        pltpu.SemaphoreType.DMA((10,)),
        pltpu.SemaphoreType.DMA((10,)),
    ]


def summed(terms):
    total = terms[0].astype(F32)
    for term in terms[1:]:
        total = total + term.astype(F32)
    return total


class Line:
    def __init__(self, spot, own, adder, buf, s, r):
        z, last = spot.z, spot.parts - 1
        e, c = spot.e, spot.c
        self.own, self.adder, self.buf, self.s, self.r = own, adder, buf, s, r
        self.z, self.last, self.parts = z, last, spot.parts
        self.ways = [(z, (e, c, z + 1), lambda d: d), (last - z, (e, c, z - 1), lambda d: last - d)]

    def step(self, turn):
        for way, (i, dev, part) in enumerate(self.ways):
            to, s, r = self.buf.at[way, turn - 1], self.s.at[way, turn - 1], self.r.at[way, turn - 1]

            @pl.when(i == 0)
            def _():
                remote(self.own(part(self.parts - turn)), to, s, r, dev).start()

            if turn >= 2:
                came, s_came, r_came = (x.at[way, turn - 2] for x in (self.buf, self.s, self.r))

                @pl.when((i >= 1) & (i <= turn - 1) & (i < self.last))
                def _():
                    remote(came, came, s_came, r_came, dev).wait_recv()
                    self.adder(came, part(self.parts - turn + i))
                    remote(came, to, s, r, dev).start()

    def final(self, put):
        last, z = self.last, self.z
        for way, (i, dev, _) in enumerate(self.ways):
            came = self.buf.at[way, last - 1]

            @pl.when(i >= 1)
            def _():
                remote(came, came, self.s.at[way, last - 1], self.r.at[way, last - 1], dev).wait_recv()

        up, down = self.buf.at[0, last - 1], self.buf.at[1, last - 1]
        pl.when(z == 0)(lambda: put(down))
        pl.when(z == last)(lambda: put(up))
        pl.when((z > 0) & (z < last))(lambda: put(up, down))

    def done(self):
        for way, (i, dev, _) in enumerate(self.ways):
            for turn in range(1, self.parts):
                came = self.buf.at[way, turn - 1]

                @pl.when((i <= turn - 1) & (i < self.last))
                def _():
                    remote(came, came, self.s.at[way, turn - 1], self.r.at[way, turn - 1], dev).wait_send()


def line_scratch(parts, piece):
    return [
        pltpu.VMEM((2, parts - 1) + piece, BF16),
        pltpu.SemaphoreType.DMA((2, parts - 1)),
        pltpu.SemaphoreType.DMA((2, parts - 1)),
    ]


class ExpertLine:
    def __init__(self, spot, ref, at, cols, buf, s, r, fin, spread, a_s, a_r):
        self.spot, self.ref, self.at, self.cols = spot, ref, at, cols
        self.fin, self.spread, self.a_s, self.a_r = fin, spread, a_s, a_r
        self.line = Line(spot, self.own, self.adder, buf, s, r)
        self.step = self.line.step

    def own(self, d):
        return self.ref.at[:, d, :, pl.ds(self.at, self.cols)]

    def piece(self, cc, d):
        return self.ref[cc, d, :, self.at : self.at + self.cols]

    def adder(self, came, d):
        for cc in range(self.spot.ctx):
            came[cc] = plus(came[cc], self.piece(cc, d))

    def final(self):
        spot = self.spot

        def put(*came):
            for cc in range(spot.ctx):
                self.fin[cc] = plus(self.piece(cc, spot.z), *(x[cc] for x in came))

        self.line.final(put)
        for step in range(1, spot.ctx):
            cc = lax.rem(spot.c + step, spot.ctx)
            remote(
                self.fin.at[cc],
                self.spread.at[spot.c],
                self.a_s.at[step - 1],
                self.a_r.at[step - 1],
                (spot.e, cc, spot.z),
            ).start()

    def done(self, out):
        spot = self.spot
        for step in range(1, spot.ctx):
            cc = lax.rem(spot.c + spot.ctx - step, spot.ctx)
            got = remote(
                self.spread.at[cc],
                self.spread.at[cc],
                self.a_s.at[step - 1],
                self.a_r.at[step - 1],
                (spot.e, cc, spot.z),
            )
            got.wait_recv()
            got.wait_send()
            out[cc] = self.spread[cc]
        out[spot.c] = self.fin[spot.c]
        self.line.done()


def expert_scratch(ctx, parts, rows, cols):
    return line_scratch(parts, (ctx, rows, cols)) + [
        pltpu.VMEM((ctx, rows, cols), BF16),
        pltpu.VMEM((ctx, rows, cols), BF16),
        pltpu.SemaphoreType.DMA((ctx - 1,)),
        pltpu.SemaphoreType.DMA((ctx - 1,)),
    ]


class Gather:
    def __init__(self, spot, own, buf, s, r, low=None, ahead=0):
        self.spot, self.own, self.buf, self.s, self.r = spot, own, buf, s, r
        low = low or own.shape[0] // 2
        self.lo, self.hi = pl.ds(0, low), pl.ds(low, own.shape[0] - low)
        self.ahead, self.rest = ahead and pl.ds(low, ahead), pl.ds(low + ahead, own.shape[0] - low - ahead)
        self.x_me, self.y_me, self.d_me = (base + spot.k for base in spot.chips[1:])
        self.side = 1 - 2 * spot.k
        self.sent = []

    def push(self, src, dst, i, dev):
        copy = remote(src, dst, self.s.at[i], self.r.at[i], dev)
        copy.start()
        self.sent.append(copy)

    def move(self, p, rows, i, dev):
        self.push(self.buf.at[p, rows], self.buf.at[p, rows], i, dev)

    def got(self, p, rows, i):
        to = self.buf.at[p, rows]
        remote(to, to, self.s.at[i], self.r.at[i], self.spot.kp).wait_recv()

    def start(self):
        me, own, lo, hi = self.spot.me, self.own, self.lo, self.hi
        self.push(own.at[lo], self.buf.at[me, lo], 0, self.spot.xp)
        if self.ahead:
            self.push(own.at[self.ahead], self.buf.at[me, self.ahead], 14, self.spot.yp)
        self.push(own.at[lo], self.buf.at[me, lo], 6, self.spot.kp)
        self.push(own.at[hi], self.buf.at[me, hi], 13, self.spot.kp)
        self.push(own.at[hi], self.buf.at[me, hi], 1, self.spot.xp)

    def start_y(self):
        me, own, lo, rest = self.spot.me, self.own, self.lo, self.rest
        self.push(own.at[rest], self.buf.at[me, rest], 3, self.spot.yp)
        self.push(own.at[lo], self.buf.at[me, lo], 2, self.spot.yp)

    def first(self):
        spot = self.spot
        self.got(self.x_me, self.lo, 0)
        self.move(self.x_me, self.lo, 4, spot.yp)
        self.move(self.x_me, self.lo, 7, spot.kp)
        if self.ahead:
            self.got(self.y_me, self.ahead, 14)
        self.got(self.y_me, self.rest, 3)
        self.move(self.y_me, self.hi, 5, spot.xp)
        self.move(self.y_me, self.hi, 10, spot.kp)

    def second(self):
        self.got(self.x_me, self.hi, 1)
        self.move(self.x_me, self.hi, 8, self.spot.kp)
        self.got(self.y_me, self.lo, 2)
        self.move(self.y_me, self.lo, 9, self.spot.kp)

    def third(self):
        self.got(self.d_me, self.lo, 4)
        self.move(self.d_me, self.lo, 11, self.spot.kp)
        self.got(self.d_me, self.hi, 5)
        self.move(self.d_me, self.hi, 12, self.spot.kp)

    def other_core(self, q):
        low_sem, high_sem = ((6, 13), (7, 8), (9, 10), (11, 12))[q]
        p = (self.spot.me, self.x_me, self.y_me, self.d_me)[q] + self.side
        self.got(p, self.lo, low_sem)
        self.got(p, self.hi, high_sem)

    def done(self):
        for copy in self.sent:
            copy.wait_send()


GATHER_COPIES = 15


def front_kernel(
    cap,
    span,
    hidden,
    cot,
    gain_one,
    freqs,
    gain_two,
    router_t,
    ids_t,
    turn_t,
    wqkv_h,
    wout_h,
    normed_h,
    queries_h,
    kv_h,
    lse,
    attended,
    resid,
    ffn_in,
    trig,
    meta,
    cot_all,
    wqkv,
    wout,
    mask,
    vt,
    normed,
    queries,
    kv,
    load_sem,
    out_sem,
    kv_s,
    kv_r,
    co_s,
    co_r,
):
    spot = Spot()
    c, ctx, k = spot.c, spot.ctx, spot.k
    tok, width = hidden.shape
    group = HEADS // KV_HEADS
    kv_cols = KV_HEADS * HEAD
    half_head = HEAD // 2
    seq = kv.shape[0]
    spans = span.shape[1]
    size = seq // spans
    mine = spans // ctx
    n_experts = meta.shape[0]
    loads = [
        pltpu.make_async_copy(wqkv_h.at[:, pl.ds(width, 2 * kv_cols)], wqkv.at[:, pl.ds(width, 2 * kv_cols)], load_sem.at[0]),
        pltpu.make_async_copy(wqkv_h.at[:, pl.ds(0, width)], wqkv.at[:, pl.ds(0, width)], load_sem.at[1]),
        pltpu.make_async_copy(wout_h, wout, load_sem.at[2]),
        pltpu.make_async_copy(cot, cot_all.at[spot.me], load_sem.at[3]),
    ]
    for load in loads:
        load.start()
    greet([spot.xp, spot.yp, spot.kp])
    gather = Gather(spot, cot, cot_all, co_s, co_r, low=FRONT_LOW, ahead=FRONT_AHEAD)
    gather.start()

    x = hidden[...].astype(F32)
    inv = lax.rsqrt(jnp.mean(x * x, axis=-1, keepdims=True) + NORM_EPS)
    normed[...] = (x * inv * gain_one[...]).astype(BF16)

    along = lax.broadcasted_iota(jnp.int32, (tok, HEAD), 0)
    start_one, start_two = span[0, c * mine] * size, (span[0, c * mine + 1] - 1) * size
    place = jnp.where(along < size, start_one, start_two) + along
    angle = place.astype(F32) * freqs[...]
    cosine, sine = jnp.cos(angle), jnp.sin(angle)
    lane = lax.broadcasted_iota(jnp.int32, (tok, HEAD), 1)
    sine = jnp.where(lane < half_head, -sine, sine)
    trig[0] = cosine
    trig[1] = sine

    def rotate_in(w):
        return w * cosine + pltpu.roll(w, half_head, 1) * sine

    loads[0].wait()
    raw = dot(normed[...], wqkv[:, width:])
    own = rows_at(c * tok, tok)
    for g in range(KV_HEADS):
        at = slice(g * HEAD, (g + 1) * HEAD)
        kv[own, at] = rotate_in(raw[:, at]).astype(BF16)
    kv[own, kv_cols:] = raw[:, kv_cols:].astype(BF16)

    def kv_copy(rows, i, dev):
        return remote(kv.at[rows], kv.at[rows], kv_s.at[i], kv_r.at[i], dev)

    flip_c = lax.rem(c + 2, ctx)
    near_c = c + 1 - 2 * k
    across_c = lax.rem(near_c + 2, ctx)
    sent = [kv_copy(own, 1, spot.yp), kv_copy(own, 0, spot.kp)]
    for copy in sent:
        copy.start()
    gather.start_y()

    outs = [pltpu.make_async_copy(normed, normed_h, out_sem.at[0])]
    outs[0].start()
    loads[1].wait()
    step = 256

    @pl.loop(0, width // step)
    def _(n):
        at = lanes(n * step, step)
        raw = dot(normed[...], wqkv[:, at])
        for i in range(step // HEAD):
            w = raw[:, i * HEAD : (i + 1) * HEAD]
            queries[:, lanes(n * step + i * HEAD, HEAD)] = (rotate_in(w) * HEAD**-0.5).astype(BF16)

    outs.append(pltpu.make_async_copy(queries, queries_h, out_sem.at[1]))
    outs[1].start()

    flip = rows_at(flip_c * tok, tok)
    kv_copy(flip, 1, spot.kp).wait_recv()
    sent.append(kv_copy(flip, 2, spot.kp))
    sent[-1].start()

    expert = lax.broadcasted_iota(jnp.int32, (n_experts, tok), 0)
    never = tok * ids_t.shape[0]
    turn = jnp.full((n_experts, tok), never, jnp.int32)
    for i in range(ids_t.shape[0]):
        turn = jnp.where(ids_t[i : i + 1, :] == expert, turn_t[i : i + 1, :], turn)
    turn_f = turn.astype(F32)
    tall = jnp.concatenate([turn_f, jnp.full((HEAD - n_experts, tok), float(never), F32)], axis=0).T
    meta[...] = jnp.zeros(meta.shape, F32)
    for g in range(n_experts):
        row = turn_f[g : g + 1, :]
        rank = jnp.sum(jnp.where(tall[:, g : g + 1] < row, 1.0, 0.0), axis=0, keepdims=True)
        meta[g, 0:1, :] = jnp.where((row < never) & (rank < cap), rank, -1.0)

    along_q = lax.broadcasted_iota(jnp.int32, (size, tok), 1)
    q_pos = jnp.where(along_q < size, start_one, start_two) + along_q
    for s in range(spans):
        k_pos = span[0, s] * size + lax.broadcasted_iota(jnp.int32, (size, tok), 0)
        mask[s * size : (s + 1) * size, :] = jnp.where(k_pos <= q_pos, 0.0, MASKED)

    near, across = rows_at(near_c * tok, tok), rows_at(across_c * tok, tok)
    kv_copy(near, 0, spot.kp).wait_recv()
    kv_copy(across, 2, spot.kp).wait_recv()
    outs.append(pltpu.make_async_copy(kv, kv_h, out_sem.at[2]))
    outs[2].start()
    for g in range(KV_HEADS):
        vt[g] = kv[:, kv_cols + g * HEAD : kv_cols + (g + 1) * HEAD].astype(F32).T.astype(BF16)
    lse[...] = jnp.zeros(lse.shape, F32)

    def heads(g, first, count):
        @pl.loop(first, first + count)
        def _(h):
            at = lanes(h * HEAD, HEAD)
            scores = dot_nt(kv[:, g * HEAD : (g + 1) * HEAD], queries[:, at]) + mask[...]
            top = jnp.max(scores, axis=0, keepdims=True)
            weights = jnp.exp(scores - top)
            total = jnp.sum(weights, axis=0, keepdims=True)
            lse[pl.ds(h, 1), :] = top + jnp.log(total)
            out = dot(vt[g], weights.astype(BF16)) / total
            attended[:, at] = out.T.astype(BF16)

    heads(0, 0, 3)
    gather.first()
    heads(0, 3, 3)
    heads(1, 6, 3)
    gather.second()
    heads(1, 9, 3)

    loads[2].wait()

    @pl.loop(0, width // step)
    def _(n):
        at = lanes(n * step, step)
        resid[:, at] = hidden[:, at].astype(F32) + dot_nt(attended[...], wout[at, :])

    r = resid[...]
    inv = lax.rsqrt(jnp.mean(r * r, axis=-1, keepdims=True) + NORM_EPS)
    ffn_in[...] = (r * inv * gain_two[...]).astype(BF16)
    logits = dot_nt(router_t[...], ffn_in[...])[:n_experts]
    logits = jnp.where(turn < never, logits, MASKED)
    shifted = jnp.exp(logits - jnp.max(logits, axis=0, keepdims=True))
    gates = shifted / jnp.sum(shifted, axis=0, keepdims=True)
    for g in range(n_experts):
        meta[g, 1:2, :] = gates[g : g + 1, :]
    gather.third()
    for q in range(4):
        gather.other_core(q)
    loads[3].wait()
    gather.done()
    for copy in outs:
        copy.wait()
    for copy in sent:
        copy.wait_send()


def run_front(cap, span, hidden, cot, gain_one, freqs, gain_two, router_t, ids_t, turn_t, wqkv, wout, ctx, planes):
    tok, width = hidden.shape
    seq = tok * ctx
    n_experts = planes
    kv_cols = 2 * KV_HEADS * HEAD
    vm, anyspace = pl.BlockSpec(memory_space=pltpu.VMEM), pl.BlockSpec(memory_space=pl.ANY)
    sm = pl.BlockSpec(memory_space=pltpu.SMEM)
    shape = jax.ShapeDtypeStruct
    dma = pltpu.SemaphoreType.DMA
    return pl.pallas_call(
        functools.partial(front_kernel, cap),
        out_shape=(
            shape((tok, width), BF16),
            shape((tok, width), BF16),
            shape((seq, kv_cols), BF16),
            shape((16, tok), F32),
            shape((tok, width), BF16),
            shape((tok, width), F32),
            shape((tok, width), BF16),
            shape((2, tok, HEAD), F32),
            shape((n_experts, 8, tok), F32),
            shape((planes, tok, width), BF16),
        ),
        in_specs=[sm] + [vm] * 8 + [anyspace] * 2,
        out_specs=(anyspace,) * 3 + (vm,) * 6 + (anyspace,),
        scratch_shapes=[
            pltpu.VMEM(wqkv.shape, BF16),
            pltpu.VMEM(wout.shape, BF16),
            pltpu.VMEM((seq, tok), F32),
            pltpu.VMEM((KV_HEADS, HEAD, seq), BF16),
            pltpu.VMEM((tok, width), BF16),
            pltpu.VMEM((tok, width), BF16),
            pltpu.VMEM((seq, kv_cols), BF16),
            dma((4,)),
            dma((3,)),
            dma((3,)),
            dma((3,)),
            dma((GATHER_COPIES,)),
            dma((GATHER_COPIES,)),
        ],
        compiler_params=pltpu.CompilerParams(
            collective_id=4, has_side_effects=True, vmem_limit_bytes=56 * 2**20
        ),
        cost_estimate=pl.CostEstimate(flops=5 * 10**9, bytes_accessed=20 * 10**6, transcendentals=4 * 10**6),
    )(span, hidden, cot, gain_one, freqs, gain_two, router_t, ids_t, turn_t, wqkv, wout)


def ffn_kernel(cap, ffn_h, resid_h, cot_h, meta, win_h, wdn_h, output, pg_out, gg_out, gwin_h, ex_out, first_out, *scratch):
    agb, metas, cotb, win, wdn, xs, ds, hid, igs, pgs, ggs, ggr, wint, gwdn = scratch[:14]
    load_sem, ag_s, ag_r, me_s, me_r, gg_s, gg_r, out_s, out_r = scratch[14:23]
    plane_refs, line_refs, first_refs = scratch[23:29], scratch[29:36], scratch[36:]
    spot = Spot()
    c, k, me = spot.c, spot.k, spot.me
    kp = spot.kp
    tok, width = output.shape
    ff = wdn.shape[1]
    planes, ctx = spot.planes, spot.ctx
    chips = spot.chips

    loads = [
        pltpu.make_async_copy(win_h.at[c], win, load_sem.at[0]),
        pltpu.make_async_copy(wdn_h.at[c], wdn, load_sem.at[1]),
        pltpu.make_async_copy(cot_h, cotb, load_sem.at[2]),
        pltpu.make_async_copy(resid_h, pg_out, load_sem.at[3]),
    ]
    own_load = pltpu.make_async_copy(ffn_h, agb.at[me], load_sem.at[4])
    own_load.start()
    others = spot.others()
    greet([dev for _, dev in others], spot.along())
    plane = plane_of(spot, *plane_refs)
    o_lo, o_hi = pl.ds(0, OUT_LOW), pl.ds(OUT_LOW, tok - OUT_LOW)
    outs = Plane(
        spot,
        [agb.at[2 * i + k] for i in range(4)],
        [cotb.at[base + k] for base in chips],
        [agb.at[1 - k, o_lo], agb.at[3 - k, o_lo], agb.at[1 - k, o_hi]],
        [agb.at[3 - k, o_hi], agb.at[5 - k, o_hi], agb.at[5 - k, o_lo]],
        out_s,
        out_r,
        [agb.at[2 * i + 1 - k] for i in range(4)],
        low=OUT_LOW,
    )
    line = ExpertLine(spot, gwdn, 0, ff, *line_refs)
    some = first_out.shape[2]
    first_line = ExpertLine(spot, win, 0, some, *first_refs)
    gather = Gather(spot, agb.at[me], agb, ag_s, ag_r)
    for step, (other, dev) in enumerate(others):
        remote(meta.at[other], metas.at[me], me_s.at[step], me_r.at[step], dev).start()
    own_load.wait()
    gather.start()
    gather.start_y()
    for load in loads:
        load.start()
    metas[me] = meta[me]
    slot_rows = lax.broadcasted_iota(jnp.int32, (cap, tok), 0).astype(F32)
    step = 256

    def spots(p):
        return jnp.where(slot_rows == metas[p, 0:1, :], 1.0, 0.0)

    def gate_of(p, hot):
        return jnp.sum(hot * metas[p, 1:2, :], axis=1, keepdims=True)

    def dispatch(q):
        for kk in range(2):
            p = chips[q] + kk
            hot = spots(p)
            low = hot.astype(BF16)
            part = pl.ds(q * 2 * cap + kk * cap, cap)
            xs[part, :] = dot(low, agb[p]).astype(BF16)
            ds[part, :] = (dot(low, cotb[p]) * gate_of(p, hot)).astype(BF16)

    def work(q, count):
        rows = pl.ds(q * 2 * cap, count * 2 * cap)

        @pl.loop(0, ff // step)
        def _(n):
            gate_cols, up_cols = lanes(n * step, step), lanes(ff + n * step, step)
            x = xs[rows, :]
            g = dot(x, win[:, :, :, gate_cols].reshape(width, step))
            u = dot(x, win[:, :, :, up_cols].reshape(width, step))
            s = 1.0 / (1.0 + jnp.exp(-g))
            act = g * s
            hid[rows, gate_cols] = (act * u).astype(BF16)
            h = dot(ds[rows, :], wdn[:, gate_cols])
            igs[rows, gate_cols] = (h * u * (s * (1.0 + g * (1.0 - s)))).astype(BF16)
            igs[rows, up_cols] = (h * act).astype(BF16)

        @pl.loop(0, width // step)
        def _(n):
            cols = lanes(n * step, step)
            pgs[pl.ds(0, count * 2 * cap), cols] = dot(igs[rows, :], wint[:, cols]).astype(BF16)

    def back(q, at):
        base = chips[q]
        mine, theirs = rows_at(at * 2 * cap + k * cap, cap), rows_at(at * 2 * cap + (1 - k) * cap, cap)
        given = agb.at[base + 1 - k]
        given[...] = dot_tn(spots(base + 1 - k).astype(BF16), pgs[theirs, :]).astype(BF16)
        plane.give(q, given)
        plane.zk[q][...] = dot_tn(spots(base + k).astype(BF16), pgs[mine, :]).astype(BF16)

    loads[0].wait()
    tall = width // ctx

    @pl.loop(0, ctx)
    def _(n):
        wint[:, lanes(n * tall, tall)] = win[n].reshape(tall, 2 * ff).T

    for n in range(planes - 1):
        source = lax.rem(me + planes - 1 - n, planes)
        remote(metas.at[source], metas.at[source], me_s.at[n], me_r.at[n], kp).wait_recv()
    for load in loads[1:]:
        load.wait()
    gather.other_core(0)
    dispatch(0)
    work(0, 1)
    back(0, 0)
    gather.first()
    gather.second()
    gather.other_core(1)
    dispatch(1)
    gather.other_core(2)
    dispatch(2)
    work(1, 2)
    gather.third()
    back(1, 0)
    back(2, 1)
    gather.other_core(3)
    gather.done()
    dispatch(3)
    plane.fold(1)
    plane.fold(2)
    plane.near()
    work(3, 1)
    back(3, 0)
    plane.fold(3)
    plane.given()
    plane.across()


    @pl.loop(0, ctx)
    def _(n):
        tile = dot_tn(ds[:, lanes(n * tall, tall)], hid[...]).astype(BF16)
        for d in range(gwdn.shape[1]):
            gwdn[n, d] = tile[d * gwdn.shape[2] : (d + 1) * gwdn.shape[2]]

    line.step(1)
    plane.fold(0)

    @pl.loop(0, width // step)
    def _(n):
        cols = lanes(n * step, step)
        ds[:, cols] = dot_nt(hid[...], wdn[cols, :]).astype(BF16)

    def returned(q):
        base = chips[q]
        for kk in range(2):
            p = base + kk
            hot = spots(p)
            rows = ds[pl.ds(q * 2 * cap + kk * cap, cap), :]
            ggs[p, 0:1, :] = jnp.sum(hot * dot_nt(rows, cotb[p]), axis=0, keepdims=True)
            scaled = (rows.astype(F32) * gate_of(p, hot)).astype(BF16)
            cotb[p] = dot_tn(hot.astype(BF16), scaled).astype(BF16)
        outs.give(q, cotb.at[base + 1 - k])

    returned(1)
    returned(2)
    plane.turn()
    returned(3)
    returned(0)
    outs.fold(1)
    outs.fold(2)
    outs.near()
    outs.fold(3)
    outs.across()
    ggr[me] = ggs[me]
    for n, (other, dev) in enumerate(others):
        remote(ggs.at[other], ggr.at[me], gg_s.at[n], gg_r.at[n], dev).start()
    line.step(2)
    outs.fold(0)

    def gate_up(at, size):
        @pl.loop(0, ctx)
        def _(n):
            tile = dot_tn(xs[:, lanes(n * tall, tall)], igs[:, pl.ds(at, size)]).astype(BF16)
            win[n, :, :, pl.ds(at, size)] = tile.reshape(gwdn.shape[1], gwdn.shape[2], size)

    gate_up(0, some)
    first_line.step(1)
    rest = 2 * ff - some
    gate_up(some, rest // 2)
    gate_up(some + rest // 2, rest // 2)
    gwin_copy = pltpu.make_async_copy(win.at[:, :, :, pl.ds(some, rest)], gwin_h, load_sem.at[0])
    gwin_copy.start()
    line.step(3)
    outs.turn()
    first_line.step(2)
    line.final()
    for rows, terms in outs.total():
        output[rows, :] = (pg_out[rows, :] + summed(terms)).astype(BF16)
    for rows, terms in plane.total():
        pg_out[rows, :] = summed(terms)
    for n in range(planes - 1):
        source = lax.rem(me + planes - 1 - n, planes)
        remote(ggr.at[source], ggr.at[source], gg_s.at[n], gg_r.at[n], kp).wait_recv()
    for p in range(planes):
        gg_out[p : p + 1, :] = ggr[p, 0:1, :]
    first_line.step(3)
    first_line.final()
    gwin_copy.wait()
    for n, (other, dev) in enumerate(others):
        remote(meta.at[other], metas.at[other], me_s.at[n], me_r.at[n], dev).wait_send()
        remote(ggs.at[other], ggr.at[other], gg_s.at[n], gg_r.at[n], dev).wait_send()
    plane.done()
    outs.done()
    line.done(ex_out)
    first_line.done(first_out)


def run_ffn(cap, ffn, resid, cot_all, meta, win, wdn, parts, some):
    tok, width = ffn.shape
    ff = wdn.shape[2]
    planes = cot_all.shape[0]
    ctx = win.shape[0]
    rows = planes * cap
    piece = width // (ctx * parts)
    win = win.reshape(ctx, ctx, parts, piece, 2 * ff)
    vm, anyspace = pl.BlockSpec(memory_space=pltpu.VMEM), pl.BlockSpec(memory_space=pl.ANY)
    shape = jax.ShapeDtypeStruct
    dma = pltpu.SemaphoreType.DMA
    return pl.pallas_call(
        functools.partial(ffn_kernel, cap),
        out_shape=(
            shape((tok, width), BF16),
            shape((tok, width), F32),
            shape((planes, tok), F32),
            shape((ctx, parts, piece, 2 * ff - some), BF16),
            shape((ctx, piece, ff), BF16),
            shape((ctx, piece, some), BF16),
        ),
        in_specs=[anyspace, anyspace, anyspace, vm, anyspace, anyspace],
        out_specs=(vm, vm, vm, anyspace, vm, vm),
        scratch_shapes=[
            pltpu.VMEM((planes, tok, width), BF16),
            pltpu.VMEM((planes, 8, tok), F32),
            pltpu.VMEM((planes, tok, width), BF16),
            pltpu.VMEM((ctx, parts, piece, 2 * ff), BF16),
            pltpu.VMEM((width, ff), BF16),
            pltpu.VMEM((rows, width), BF16),
            pltpu.VMEM((rows, width), BF16),
            pltpu.VMEM((rows, ff), BF16),
            pltpu.VMEM((rows, 2 * ff), BF16),
            pltpu.VMEM((4 * cap, width), BF16),
            pltpu.VMEM((planes, 8, tok), F32),
            pltpu.VMEM((planes, 8, tok), F32),
            pltpu.VMEM((2 * ff, width), BF16),
            pltpu.VMEM((ctx, parts, piece, ff), BF16),
            dma((5,)),
            dma((GATHER_COPIES,)),
            dma((GATHER_COPIES,)),
            dma((planes - 1,)),
            dma((planes - 1,)),
            dma((planes - 1,)),
            dma((planes - 1,)),
            dma((10,)),
            dma((10,)),
        ]
        + plane_scratch(tok, width)
        + expert_scratch(ctx, parts, piece, ff)
        + expert_scratch(ctx, parts, piece, some),
        compiler_params=pltpu.CompilerParams(
            collective_id=1, has_side_effects=True, vmem_limit_bytes=63 * 2**20
        ),
        cost_estimate=pl.CostEstimate(flops=25 * 10**9, bytes_accessed=50 * 10**6, transcendentals=10**6),
    )(ffn, resid, cot_all, meta, win, wdn)


def back_kernel(
    span,
    meta,
    gg,
    lse,
    trig,
    kv,
    queries,
    attended,
    normed,
    router_t,
    gain_two,
    gain_one,
    resid_h,
    cot_h,
    pg_h,
    ffn_in_h,
    hidden_h,
    wout_h,
    wqkv_h,
    gwin_h,
    input_grad,
    qkv_out,
    proj_out,
    one_out,
    two_out,
    *scratch,
):
    wide_f, back, low, attg, mixed, weights, gwin, send, bsend, smalls, total, out_red = scratch[:12]
    mask, delta, kt, dk, dv, kvs, kvr = scratch[12:19]
    load_sem, kv_s, kv_r = scratch[19:22]
    p_zcr, p_zk, p_rx, p_ry, p_s, p_r = scratch[22:28]
    a_rx, a_ry, a_s, a_r = scratch[28:32]
    e_refs, b_refs = scratch[32:38], scratch[38:44]
    qkv_refs, proj_refs = scratch[44:47], scratch[47:50]
    one_refs, two_refs = scratch[50:57], scratch[57:64]
    spot = Spot()
    c, k, z, ctx = spot.c, spot.k, spot.z, spot.ctx
    tok, width = attended.shape
    cols = one_out.shape[2]
    block, piece = out_red.shape[0], proj_out.shape[0]
    heads_kv = KV_HEADS
    half_head = HEAD // 2
    n_experts = meta.shape[0]
    kv_wide = mixed.shape[1] - width
    step = 256

    def load(src, dst, i):
        copy = pltpu.make_async_copy(src, dst, load_sem.at[i])
        copy.start()
        return copy

    gwin_load = load(gwin_h, gwin, 0)
    early = [
        load(resid_h, wide_f, 1),
        load(pg_h, back, 2),
        load(cot_h, input_grad, 3),
        load(ffn_in_h, attg, 4),
    ]
    wout_load = load(wout_h, weights.at[:, pl.ds(0, width)], 5)
    greet([spot.xp, spot.yp, spot.kp, spot.yk], spot.along())
    one = ExpertLine(spot, gwin, 0, cols, *one_refs)
    two = ExpertLine(spot, gwin, cols, cols, *two_refs)
    proj_plane = plane_of(spot, p_zcr, p_zk, p_rx, p_ry, p_s, p_r, low=BACK_LOW)
    half_wide = width // 2
    cut = pl.ds(0, half_wide)
    early_plane = plane_of(spot, *e_refs, low=BACK_LOW)
    late_plane = plane_of(
        spot, p_zcr.at[:, :, cut], p_zk.at[:, :, cut], a_rx, a_ry, a_s, a_r, low=BACK_LOW
    )
    rest_plane = plane_of(spot, *b_refs, low=BACK_LOW)

    def shared_line(ref, refs):
        def own(d):
            return ref.at[rows_at(d * piece, piece)]

        def adder(came, d):
            came[...] = plus(came[...], own(d)[...])

        return Line(spot, own, adder, *refs)

    qkv_line, proj_line = shared_line(total, qkv_refs), shared_line(out_red, proj_refs)

    def put_shared(to, ref, came):
        to[...] = plus(ref[rows_at(z * piece, piece)], *(x[...] for x in came))

    mine, theirs = rows_at(k * block, block), rows_at((1 - k) * block, block)
    gwin_load.wait()
    one.step(1)

    for copy in early:
        copy.wait()
    gate = jnp.concatenate([meta[g, 1:2, :] for g in range(n_experts)], axis=0)
    seen = gate * gg[...]
    mix = seen - gate * jnp.sum(seen, axis=0, keepdims=True)
    mix = jnp.concatenate([mix, jnp.zeros((HEAD - n_experts, tok), F32)], axis=0)
    logit_t = mix.astype(BF16)
    r = wide_f[...]
    inv = lax.rsqrt(jnp.mean(r * r, axis=-1, keepdims=True) + NORM_EPS)
    plain = r * inv
    ffn_grad = back[...] + dot_tn(logit_t[:n_experts], router_t[...])
    gain_row = jnp.sum(ffn_grad * plain, axis=0, keepdims=True)
    scaled = ffn_grad * gain_two[...]
    grad = input_grad[...].astype(F32) + inv * (
        scaled - plain * jnp.mean(scaled * plain, axis=-1, keepdims=True)
    )
    back[...] = grad
    low[...] = grad.astype(BF16)
    lane = lax.broadcasted_iota(jnp.int32, (width, HEAD), 1)
    routed = dot_tn(attg[...], logit_t.T)
    gain_col = jnp.broadcast_to(gain_row, (HEAD, width)).T
    smalls[...] = jnp.where(lane == n_experts, gain_col, routed).astype(BF16)

    for q in (3, 1, 2, 0):
        at = lanes(spot.chips[q] * block, 2 * block)
        send[q] = dot_tn(low[:, at], attended[...]).astype(BF16)
        proj_plane.give(q, send.at[q, theirs])
    wout_load.wait()

    @pl.loop(0, width // step)
    def _(n):
        at = lanes(n * step, step)
        attg[:, at] = dot(low[...], weights[:, at]).astype(BF16)

    wqkv_load = load(wqkv_h, weights, 5)
    hidden_load = load(hidden_h, low, 1)

    def start_plane(plane, at):
        plane.fold(3, send[3, mine, at])
        plane.across()
        plane.fold(1, send[1, mine, at])
        plane.fold(2, send[2, mine, at])
        plane.near()
        plane.fold(0, send[0, mine, at])

    def qkv_tiles(plane, at):
        for q in (3, 1, 2, 0):
            rows = lanes(spot.chips[q] * block, 2 * block)
            send[q, :, at] = dot_tn(normed[:, rows], mixed[:, at]).astype(BF16)
            plane.give(q, send.at[q, theirs, at])

    start_plane(proj_plane, pl.ds(0, width))

    seq = kv.shape[0]
    spans = span.shape[1]
    size = seq // spans
    per = spans // ctx
    along_q = lax.broadcasted_iota(jnp.int32, (size, tok), 1)
    q_pos = jnp.where(along_q < size, span[0, c * per] * size, (span[0, c * per + 1] - 1) * size) + along_q
    for s in range(spans):
        k_pos = span[0, s] * size + lax.broadcasted_iota(jnp.int32, (size, tok), 0)
        mask[s * size : (s + 1) * size, :] = jnp.where(k_pos <= q_pos, 0.0, MASKED)

    lane_h = lax.broadcasted_iota(jnp.int32, (tok, HEAD), 1)
    deltas = jnp.zeros((tok, HEAD), F32)
    for h in range(HEADS):
        at = slice(h * HEAD, (h + 1) * HEAD)
        term = jnp.sum(attg[:, at].astype(F32) * attended[:, at].astype(F32), axis=-1, keepdims=True)
        deltas = jnp.where(lane_h == h, term, deltas)
    delta[...] = deltas.T
    for g in range(heads_kv):
        kt[g] = kv[:, g * HEAD : (g + 1) * HEAD].astype(F32).T.astype(BF16)

    cosine, sine = trig[0], trig[1]

    def unrotate(w):
        return w * cosine - pltpu.roll(w, half_head, 1) * sine

    def head(g, h):
        at = lanes(h * HEAD, HEAD)
        k_at = slice(g * HEAD, (g + 1) * HEAD)
        v_at = slice((heads_kv + g) * HEAD, (heads_kv + g + 1) * HEAD)
        q, a = queries[:, at], attg[:, at]
        soft = jnp.exp(dot_nt(kv[:, k_at], q) + mask[...] - lse[pl.ds(h, 1), :])
        prob = dot_nt(kv[:, v_at], a)
        score = (soft * (prob - delta[pl.ds(h, 1), :])).astype(BF16)
        mixed[:, at] = (unrotate(dot(kt[g], score).T) * HEAD**-0.5).astype(BF16)
        dk[...] += dot(score, q)
        dv[...] += dot(soft.astype(BF16), a)

    def heads(g, first, count):
        @pl.loop(first, first + count)
        def _(h):
            head(g, h)

    def clear():
        dk[...] = jnp.zeros(dk.shape, F32)
        dv[...] = jnp.zeros(dv.shape, F32)

    flip_c = lax.rem(c + 2, ctx)
    near_c = c + 1 - 2 * k
    across_c = lax.rem(near_c + 2, ctx)

    def kv_copy(g, src, i, dev):
        return remote(src, kvr.at[g, i], kv_s.at[g, i], kv_r.at[g, i], dev)

    def send_kv(g):
        for cc in range(ctx):
            rows = slice(cc * tok, (cc + 1) * tok)
            kvs[g, cc, :, :HEAD] = dk[rows, :].astype(BF16)
            kvs[g, cc, :, HEAD:] = dv[rows, :].astype(BF16)
        kv_copy(g, kvs.at[g, across_c], 1, spot.kp).start()
        kv_copy(g, kvs.at[g, near_c], 0, spot.kp).start()

    def pass_kv(g):
        kv_copy(g, kvs.at[g, across_c], 1, spot.kp).wait_recv()
        kvs[g, flip_c] = plus(kvs[g, flip_c], kvr[g, 1])
        kv_copy(g, kvs.at[g, flip_c], 2, spot.yp).start()

    clear()
    heads(0, 0, 2)
    one.step(2)
    heads(0, 2, 4)
    send_kv(0)
    clear()
    proj_plane.turn()
    proj_plane.given()
    qkv_tiles(early_plane, pl.ds(0, half_wide))
    heads(1, 6, 1)
    start_plane(early_plane, pl.ds(0, half_wide))
    pass_kv(0)
    one.step(3)
    two.step(1)
    heads(1, 7, 2)
    heads(1, 9, 3)
    send_kv(1)
    pass_kv(1)
    early_plane.turn()
    for rows, terms in proj_plane.total():
        out_red[rows, :] = summed(terms).astype(BF16)
    proj_line.step(1)
    proj_plane.done()
    for g in range(heads_kv):
        kv_copy(g, kvs.at[g, near_c], 0, spot.kp).wait_recv()
        kv_copy(g, kvs.at[g, flip_c], 2, spot.yp).wait_recv()
        own = kvs[g, c].astype(F32) + kvr[g, 0].astype(F32) + kvr[g, 2].astype(F32)
        at = width + g * HEAD
        mixed[:, at : at + HEAD] = unrotate(own[:, :HEAD]).astype(BF16)
        at = width + (heads_kv + g) * HEAD
        mixed[:, at : at + HEAD] = own[:, HEAD:].astype(BF16)

    qkv_tiles(late_plane, pl.ds(half_wide, half_wide))
    start_plane(late_plane, pl.ds(half_wide, half_wide))
    proj_line.step(2)
    wqkv_load.wait()

    @pl.loop(0, width // step)
    def _(n):
        at = lanes(n * step, step)
        wide_f[:, at] = dot_nt(mixed[...], weights[at, :])

    two.step(2)
    hidden_load.wait()
    x = low[...].astype(F32)
    inv = lax.rsqrt(jnp.mean(x * x, axis=-1, keepdims=True) + NORM_EPS)
    plain = x * inv
    ng = wide_f[...]
    gain_row = jnp.sum(ng * plain, axis=0, keepdims=True)
    scaled = ng * gain_one[...]
    input_grad[...] = (
        back[...] + inv * (scaled - plain * jnp.mean(scaled * plain, axis=-1, keepdims=True))
    ).astype(BF16)
    lane = lax.broadcasted_iota(jnp.int32, (width, HEAD), 1)
    gain_col = jnp.broadcast_to(gain_row, (HEAD, width)).T
    smalls[...] = jnp.where(lane == HEAD - 1, gain_col, smalls[...].astype(F32)).astype(BF16)
    for q in (3, 1, 2, 0):
        at = lanes(spot.chips[q] * block, 2 * block)
        bsend[q, :, :kv_wide] = dot_tn(normed[:, at], mixed[:, width:]).astype(BF16)
        bsend[q, :, kv_wide:] = smalls[rows_at(spot.chips[q] * block, 2 * block), :]
        rest_plane.give(q, bsend.at[q, theirs])
    rest_plane.fold(3, bsend[3, mine])
    rest_plane.across()
    rest_plane.fold(1, bsend[1, mine])
    rest_plane.fold(2, bsend[2, mine])
    rest_plane.near()
    rest_plane.fold(0, bsend[0, mine])
    late_plane.turn()
    rest_plane.turn()
    two.step(3)
    one.final()
    proj_line.step(3)
    for rows, terms in early_plane.total():
        total[rows, :half_wide] = summed(terms).astype(BF16)
    for rows, terms in late_plane.total():
        total[rows, half_wide:width] = summed(terms).astype(BF16)
    for rows, terms in rest_plane.total():
        total[rows, width:] = summed(terms).astype(BF16)
    qkv_line.step(1)
    one.done(one_out)
    qkv_line.step(2)
    two.final()
    proj_line.final(lambda *came: put_shared(proj_out, out_red, came))
    qkv_line.step(3)
    proj_line.done()
    early_plane.done()
    late_plane.done()
    rest_plane.done()
    for g in range(heads_kv):
        kv_copy(g, kvs.at[g, near_c], 0, spot.kp).wait_send()
        kv_copy(g, kvs.at[g, across_c], 1, spot.kp).wait_send()
        kv_copy(g, kvs.at[g, flip_c], 2, spot.yp).wait_send()
    qkv_line.final(lambda *came: put_shared(qkv_out, total, came))
    qkv_line.done()
    two.done(two_out)


def run_back(
    span, meta, gg, lse, trig, kv, queries, attended, normed, router_t, gain_two, gain_one,
    resid, cot, pg, ffn_in, hidden, wout, wqkv, gwin,
):
    tok, width = attended.shape
    seq, kv_cols = kv.shape
    planes = meta.shape[0]
    ctx, parts, rows, wide = gwin.shape
    cols = wide // 2
    block = width // planes
    piece = block // parts
    rest = kv_cols + HEAD
    vm, anyspace = pl.BlockSpec(memory_space=pltpu.VMEM), pl.BlockSpec(memory_space=pl.ANY)
    sm = pl.BlockSpec(memory_space=pltpu.SMEM)
    shape = jax.ShapeDtypeStruct
    dma = pltpu.SemaphoreType.DMA
    return pl.pallas_call(
        back_kernel,
        out_shape=(
            shape((tok, width), BF16),
            shape((piece, width + rest), BF16),
            shape((piece, width), BF16),
            shape((ctx, rows, cols), BF16),
            shape((ctx, rows, cols), BF16),
        ),
        in_specs=[sm] + [vm] * 11 + [anyspace] * 8,
        out_specs=(vm,) * 5,
        scratch_shapes=[
            pltpu.VMEM((tok, width), F32),
            pltpu.VMEM((tok, width), F32),
            pltpu.VMEM((tok, width), BF16),
            pltpu.VMEM((tok, width), BF16),
            pltpu.VMEM((tok, width + kv_cols), BF16),
            pltpu.VMEM(wqkv.shape, BF16),
            pltpu.VMEM(gwin.shape, BF16),
            pltpu.VMEM((4, 2 * block, width), BF16),
            pltpu.VMEM((4, 2 * block, rest), BF16),
            pltpu.VMEM((width, HEAD), BF16),
            pltpu.VMEM((block, width + rest), BF16),
            pltpu.VMEM((block, width), BF16),
            pltpu.VMEM((seq, tok), F32),
            pltpu.VMEM((HEAD, tok), F32),
            pltpu.VMEM((KV_HEADS, HEAD, seq), BF16),
            pltpu.VMEM((seq, HEAD), F32),
            pltpu.VMEM((seq, HEAD), F32),
            pltpu.VMEM((KV_HEADS, ctx, tok, 2 * HEAD), BF16),
            pltpu.VMEM((KV_HEADS, 3, tok, 2 * HEAD), BF16),
            dma((6,)),
            dma((KV_HEADS, 3)),
            dma((KV_HEADS, 3)),
        ]
        + plane_scratch(block, width, BACK_LOW)
        + plane_scratch(block, width // 2, BACK_LOW)[2:]
        + plane_scratch(block, width // 2, BACK_LOW)
        + plane_scratch(block, rest, BACK_LOW)
        + line_scratch(parts, (piece, width + rest))
        + line_scratch(parts, (piece, width))
        + expert_scratch(ctx, parts, rows, cols)
        + expert_scratch(ctx, parts, rows, cols),
        compiler_params=pltpu.CompilerParams(
            collective_id=2, has_side_effects=True, vmem_limit_bytes=63 * 2**20
        ),
        cost_estimate=pl.CostEstimate(flops=12 * 10**9, bytes_accessed=60 * 10**6, transcendentals=4 * 10**6),
    )(
        span, meta, gg, lse, trig, kv, queries, attended, normed, router_t, gain_two, gain_one,
        resid, cot, pg, ffn_in, hidden, wout, wqkv, gwin,
    )


def finish_kernel(
    n_experts,
    output_h,
    input_h,
    qkv_h,
    proj_h,
    first_h,
    one_h,
    two_h,
    down_h,
    output,
    input_grad,
    gain_one,
    gain_two,
    qkv,
    proj,
    router,
    inner,
    down,
    low_qkv,
    low_proj,
    low_first,
    low_one,
    low_two,
    low_down,
    low_out,
    low_in,
    inner_full,
    down_full,
    sem,
    out_sem,
):
    whole = []
    loads = [
        pltpu.make_async_copy(src, dst, sem.at[i])
        for i, (src, dst) in enumerate(
            (
                (down_h, low_down),
                (first_h, low_first),
                (one_h, low_one),
                (two_h, low_two),
                (qkv_h, low_qkv),
                (proj_h, low_proj),
                (output_h, low_out),
                (input_h, low_in),
            )
        )
    ]
    for copy in loads:
        copy.start()
    loads[0].wait()
    down_full[...] = low_down[...].astype(F32)
    whole.append(pltpu.make_async_copy(down_full, down, out_sem.at[2]))
    whole[-1].start()
    at = 0
    for load, low in zip(loads[1:4], (low_first, low_one, low_two)):
        load.wait()
        size = low.shape[2]
        inner_full[:, :, at : at + size] = low[...].astype(F32)
        at += size
    whole.append(pltpu.make_async_copy(inner_full, inner, out_sem.at[3]))
    whole[-1].start()
    for i, (low, to) in enumerate(((low_out, output), (low_in, input_grad))):
        loads[6 + i].wait()
        whole.append(pltpu.make_async_copy(low, to, out_sem.at[i]))
        whole[-1].start()
    for load in loads[4:6]:
        load.wait()
    wide = qkv.shape[1]
    qkv[...] = low_qkv[:, :wide].astype(F32)
    proj[...] = low_proj[...].astype(F32)
    small = low_qkv[:, wide:].astype(F32)
    piece = small.shape[0]
    same = lax.broadcasted_iota(jnp.int32, (piece, piece), 0) == lax.broadcasted_iota(
        jnp.int32, (piece, piece), 1
    )

    def column(at):
        return jnp.sum(jnp.where(same, small[:, at : at + 1], 0.0), axis=0, keepdims=True)

    gain_one[...] = column(HEAD - 1)[0]
    gain_two[...] = column(n_experts)[0]
    for at in range(n_experts):
        router[at : at + 1, :] = column(at)
    for copy in whole:
        copy.wait()


def run_finish(n_experts, output, input_grad, qkv, proj, first, one, two, down):
    piece, width = proj.shape
    ctx, rows, ff = down.shape
    shape = jax.ShapeDtypeStruct
    vm, anyspace = pl.BlockSpec(memory_space=pltpu.VMEM), pl.BlockSpec(memory_space=pl.ANY)
    return pl.pallas_call(
        functools.partial(finish_kernel, n_experts),
        out_shape=(
            shape(output.shape, BF16),
            shape(input_grad.shape, BF16),
            shape((piece,), F32),
            shape((piece,), F32),
            shape((piece, qkv.shape[1] - HEAD), F32),
            shape((piece, width), F32),
            shape((n_experts, piece), F32),
            shape((ctx, rows, 2 * ff), F32),
            shape((ctx, rows, ff), F32),
        ),
        in_specs=[anyspace] * 8,
        out_specs=(anyspace, anyspace, vm, vm, vm, vm, vm, anyspace, anyspace),
        scratch_shapes=[pltpu.VMEM(x.shape, BF16) for x in (qkv, proj, first, one, two, down, output, input_grad)]
        + [
            pltpu.VMEM((ctx, rows, 2 * ff), F32),
            pltpu.VMEM((ctx, rows, ff), F32),
            pltpu.SemaphoreType.DMA((8,)),
            pltpu.SemaphoreType.DMA((4,)),
        ],
        compiler_params=pltpu.CompilerParams(vmem_limit_bytes=56 * 2**20),
    )(output, input_grad, qkv, proj, first, one, two, down)


def local(
    hidden_in,
    span_order,
    expert_ids,
    priority,
    gain_attn,
    qkv_weight,
    out_weight,
    gain_ffn,
    router,
    in_weight,
    down_weight,
    cotangent,
):
    _, tok_rows, width = hidden_in.shape
    ctx, parts = lax.axis_size("context"), lax.axis_size("dp")
    planes = ctx * lax.axis_size("expert")
    n_experts = router.shape[1]
    top_k = expert_ids.shape[2]
    capacity = (9 * tok_rows * top_k + 8 * n_experts - 1) // (8 * n_experts)
    ff = down_weight.shape[2]
    half_freqs = ROPE_BASE ** (np.arange(HEAD // 2) * (-2.0 / HEAD))
    freqs = np.concatenate([half_freqs, half_freqs])[None].astype(np.float32)
    router_t = router.T
    hidden, cot = hidden_in[0], cotangent[0]
    normed, queries, kv, lse, attended, resid, ffn_in, trig, meta, cot_all = run_front(
        capacity,
        span_order,
        hidden,
        cot,
        gain_attn,
        freqs,
        gain_ffn,
        router_t,
        expert_ids[0].T,
        priority[0].T,
        qkv_weight,
        out_weight,
        ctx,
        planes,
    )
    output, pair_sum, gate_grad, gwin, down, in_first = run_ffn(
        capacity, ffn_in, resid, cot_all, meta, in_weight, down_weight, parts, ff // 3
    )
    input_grad, qkv_sum, proj_sum, in_one, in_two = run_back(
        span_order,
        meta,
        gate_grad,
        lse,
        trig,
        kv,
        queries,
        attended,
        normed,
        router_t,
        gain_ffn,
        gain_attn,
        resid,
        cot,
        pair_sum,
        ffn_in,
        hidden,
        out_weight,
        qkv_weight,
        gwin,
    )
    output, input_grad, gain_one, gain_two, qkv_grad, proj_grad, router_grad, inner_grad, down_grad = run_finish(
        n_experts, output, input_grad, qkv_sum, proj_sum, in_first, in_one, in_two, down
    )
    return (
        output[None],
        input_grad[None],
        gain_one,
        qkv_grad,
        proj_grad,
        gain_two,
        router_grad.T,
        inner_grad,
        down_grad,
    )


def general(
    hidden_in,
    span_order,
    expert_ids,
    priority,
    gain_attn,
    qkv_weight,
    out_weight,
    gain_ffn,
    router,
    in_weight,
    down_weight,
    cotangent,
):
    tok_rows = hidden_in.shape[1]
    width = hidden_in.shape[2]
    contexts = lax.axis_size("context")
    span_len = tok_rows // 2
    seq_len = tok_rows * contexts
    group = HEADS // KV_HEADS
    q_cols = HEADS * HEAD
    kv_cols = KV_HEADS * HEAD
    scale = HEAD ** (-0.5)
    local_experts = in_weight.shape[0]
    n_experts = local_experts * lax.axis_size("expert")
    top_k = expert_ids.shape[2]
    capacity = (9 * tok_rows * top_k + 8 * n_experts - 1) // (8 * n_experts)
    ff_width = down_weight.shape[2]
    seq_spans = span_order[0]
    stored = jnp.arange(seq_len) // span_len
    all_pos = (seq_spans[stored] * span_len + jnp.arange(seq_len) % span_len).astype(jnp.float32)
    my_pos = lax.dynamic_slice_in_dim(all_pos, lax.axis_index("context") * tok_rows, tok_rows)
    cosine, sine = rope_tables(my_pos, HEAD)
    inputs = hidden_in[0].astype(jnp.float32)
    inv_one = lax.rsqrt(jnp.mean(inputs * inputs, axis=-1, keepdims=True) + NORM_EPS)
    plain_one = inputs * inv_one
    normed = (plain_one * gain_attn).astype(jnp.bfloat16)
    mixed = jnp.dot(normed, qkv_weight, preferred_element_type=jnp.float32)
    queries = (
        rotate(mixed[:, :q_cols].reshape(tok_rows, HEADS, HEAD), cosine, sine) * scale
    ).astype(jnp.bfloat16)
    keys = rotate(
        mixed[:, q_cols : q_cols + kv_cols].reshape(tok_rows, KV_HEADS, HEAD), cosine, sine
    ).astype(jnp.bfloat16)
    values = mixed[:, q_cols + kv_cols :].reshape(tok_rows, KV_HEADS, HEAD).astype(jnp.bfloat16)
    grouped = queries.reshape(tok_rows, KV_HEADS, group, HEAD)

    def key_scores(key_piece):
        scores = jnp.einsum(
            "qkgd,skd->kgqs", grouped, key_piece, preferred_element_type=jnp.float32
        )
        visible = all_pos[None, None, None, :] <= my_pos[None, None, :, None]
        return (jnp.where(visible, scores, MASKED), visible)

    running = jnp.full((KV_HEADS, group, tok_rows), MASKED, jnp.float32)
    key_piece = lax.all_gather(keys, "context", axis=0, tiled=True)
    value_piece = lax.all_gather(values, "context", axis=0, tiled=True)
    scores, visible = key_scores(key_piece)
    newest = jnp.maximum(running, jnp.max(scores, axis=-1))
    weights = jnp.where(visible, jnp.exp(scores - newest[..., None]), 0.0)
    totals = jnp.sum(weights, axis=-1)
    accum = jnp.einsum(
        "kgqs,skd->kgqd",
        weights.astype(jnp.bfloat16),
        value_piece,
        preferred_element_type=jnp.float32,
    )
    running, totals, accum = (newest, totals, accum)
    log_total = running + jnp.log(totals)
    attended = (
        (accum / totals[..., None])
        .transpose(2, 0, 1, 3)
        .reshape(tok_rows, q_cols)
        .astype(jnp.bfloat16)
    )
    resid = inputs + jnp.einsum(
        "rh,dh->rd", attended, out_weight, preferred_element_type=jnp.float32
    )
    inv_two = lax.rsqrt(jnp.mean(resid * resid, axis=-1, keepdims=True) + NORM_EPS)
    plain_two = resid * inv_two
    ffn_in = (plain_two * gain_ffn).astype(jnp.bfloat16)
    logits = jnp.dot(ffn_in, router, preferred_element_type=jnp.float32)
    token_ids = expert_ids[0]
    gates = softmax_last(jnp.take_along_axis(logits, token_ids, axis=1))
    slots = route(token_ids, priority[0], n_experts, capacity)
    pair_rows = jnp.repeat(ffn_in, top_k, axis=0)
    send_rows = (
        jnp.zeros((n_experts * capacity, width), jnp.bfloat16).at[slots].set(pair_rows, mode="drop")
    )
    received = lax.all_to_all(
        send_rows.reshape(n_experts, capacity, width),
        "expert",
        split_axis=0,
        concat_axis=1,
        tiled=True,
    )
    inner = jnp.einsum("erd,edf->erf", received, in_weight, preferred_element_type=jnp.float32)
    gate_part = inner[..., :ff_width]
    up_part = inner[..., ff_width:]
    sigma = 1.0 / (1.0 + jnp.exp(-gate_part))
    activated = gate_part * sigma
    hidden = (activated * up_part).astype(jnp.bfloat16)
    expert_out = jnp.einsum(
        "erf,edf->erd", hidden, down_weight, preferred_element_type=jnp.float32
    ).astype(jnp.bfloat16)
    returned = lax.all_to_all(
        expert_out, "expert", split_axis=1, concat_axis=0, tiled=True
    ).reshape(n_experts * capacity, width)
    padded = jnp.concatenate([returned, jnp.zeros((1, width), jnp.bfloat16)], axis=0)
    picked = padded[slots].reshape(tok_rows, top_k, width)
    output = (resid + jnp.sum(gates[:, :, None] * picked, axis=1)).astype(jnp.bfloat16)
    cot_low = cotangent[0]
    cot_full = cot_low.astype(jnp.float32)
    gate_grad = jnp.einsum("rkd,rd->rk", picked, cot_low, preferred_element_type=jnp.float32)
    ret_grad = (
        (gates[:, :, None] * cot_full[:, None, :])
        .astype(jnp.bfloat16)
        .reshape(tok_rows * top_k, width)
    )
    send_grad = (
        jnp.zeros((n_experts * capacity, width), jnp.bfloat16).at[slots].set(ret_grad, mode="drop")
    )
    received_grad = lax.all_to_all(
        send_grad.reshape(n_experts, capacity, width),
        "expert",
        split_axis=0,
        concat_axis=1,
        tiled=True,
    )
    hid_grad = jnp.einsum(
        "erd,edf->erf", received_grad, down_weight, preferred_element_type=jnp.float32
    )
    slope = sigma * (1.0 + gate_part * (1.0 - sigma))
    inner_grad = jnp.concatenate(
        [hid_grad * up_part * slope, hid_grad * activated], axis=-1
    ).astype(jnp.bfloat16)
    row_grad = jnp.einsum(
        "erf,edf->erd", inner_grad, in_weight, preferred_element_type=jnp.float32
    ).astype(jnp.bfloat16)
    part_rows = received
    expert_in = (
        lax.psum_scatter(
            jnp.einsum(
                "erd,erf->def", part_rows, inner_grad, preferred_element_type=jnp.float32
            ).astype(jnp.bfloat16),
            ("context", "dp"),
            scatter_dimension=0,
            tiled=True,
        )
        .astype(jnp.float32)
        .transpose(1, 0, 2)
    )
    part_rows = received_grad
    expert_down = (
        lax.psum_scatter(
            jnp.einsum(
                "erd,erf->def", part_rows, hidden, preferred_element_type=jnp.float32
            ).astype(jnp.bfloat16),
            ("context", "dp"),
            scatter_dimension=0,
            tiled=True,
        )
        .astype(jnp.float32)
        .transpose(1, 0, 2)
    )
    back_rows = lax.all_to_all(row_grad, "expert", split_axis=1, concat_axis=0, tiled=True).reshape(
        n_experts * capacity, width
    )
    back_padded = jnp.concatenate([back_rows, jnp.zeros((1, width), jnp.bfloat16)], axis=0)
    pair_grad = back_padded[slots].reshape(tok_rows, top_k, width)
    mix_grad = gates * (gate_grad - jnp.sum(gates * gate_grad, axis=-1, keepdims=True))
    matches = token_ids[:, :, None] == jnp.arange(n_experts)[None, None, :]
    logit_grad = jnp.sum(jnp.where(matches, mix_grad[:, :, None], 0.0), axis=1).astype(jnp.bfloat16)
    router_part = jnp.einsum("rd,re->de", ffn_in, logit_grad, preferred_element_type=jnp.float32)
    ffn_grad = jnp.sum(pair_grad.astype(jnp.float32), axis=1) + jnp.einsum(
        "re,de->rd", logit_grad, router, preferred_element_type=jnp.float32
    )
    gain_ffn_part = jnp.sum(ffn_grad * plain_two, axis=0)
    scaled_two = ffn_grad * gain_ffn
    resid_grad = cot_full + inv_two * (
        scaled_two - plain_two * jnp.mean(scaled_two * plain_two, axis=-1, keepdims=True)
    )
    resid_low = resid_grad.astype(jnp.bfloat16)
    out_part = jnp.einsum("rd,rh->dh", resid_low, attended, preferred_element_type=jnp.float32)
    att_grad = jnp.einsum(
        "rd,dh->rh", resid_low, out_weight, preferred_element_type=jnp.float32
    ).astype(jnp.bfloat16)
    att_heads = att_grad.reshape(tok_rows, KV_HEADS, group, HEAD)
    row_delta = jnp.sum(
        att_heads.astype(jnp.float32)
        * attended.reshape(tok_rows, KV_HEADS, group, HEAD).astype(jnp.float32),
        axis=-1,
    ).transpose(1, 2, 0)
    key_piece = lax.all_gather(keys, "context", axis=0, tiled=True)
    value_piece = lax.all_gather(values, "context", axis=0, tiled=True)
    scores, visible = key_scores(key_piece)
    soft = jnp.exp(scores - log_total[..., None])
    prob_grad = jnp.einsum(
        "qkgd,skd->kgqs", att_heads, value_piece, preferred_element_type=jnp.float32
    )
    score_grad = (soft * (prob_grad - row_delta[..., None])).astype(jnp.bfloat16)
    query_acc = jnp.einsum(
        "kgqs,skd->kgqd", score_grad, key_piece, preferred_element_type=jnp.float32
    )
    key_part = jnp.einsum("kgqs,qkgd->skd", score_grad, grouped, preferred_element_type=jnp.float32)
    value_part = jnp.einsum(
        "kgqs,qkgd->skd", soft.astype(jnp.bfloat16), att_heads, preferred_element_type=jnp.float32
    )
    pair_acc = jnp.stack([key_part, value_part], axis=1)
    query_acc, pair_acc = (query_acc, pair_acc)
    own_pairs = lax.psum_scatter(
        pair_acc.astype(jnp.bfloat16), "context", scatter_dimension=0, tiled=True
    ).astype(jnp.float32)
    query_grad = (
        unrotate(query_acc.transpose(2, 0, 1, 3).reshape(tok_rows, HEADS, HEAD), cosine, sine)
        * scale
    )
    key_grad = unrotate(own_pairs[:, 0], cosine, sine)
    mixed_grad = jnp.concatenate(
        [
            query_grad.reshape(tok_rows, q_cols),
            key_grad.reshape(tok_rows, kv_cols),
            own_pairs[:, 1].reshape(tok_rows, kv_cols),
        ],
        axis=-1,
    ).astype(jnp.bfloat16)
    qkv_part = jnp.einsum("rd,rc->dc", normed, mixed_grad, preferred_element_type=jnp.float32)
    norm_grad = jnp.einsum("rc,dc->rd", mixed_grad, qkv_weight, preferred_element_type=jnp.float32)
    gain_attn_part = jnp.sum(norm_grad * plain_one, axis=0)
    scaled_one = norm_grad * gain_attn
    input_grad = (
        resid_grad
        + inv_one
        * (scaled_one - plain_one * jnp.mean(scaled_one * plain_one, axis=-1, keepdims=True))
    ).astype(jnp.bfloat16)
    gain_attn_grad, qkv_grad, out_proj_grad, gain_ffn_grad, router_grad = (
        lax.psum_scatter(
            gain_attn_part, ("expert", "context", "dp"), scatter_dimension=0, tiled=True
        ),
        lax.psum_scatter(qkv_part, ("expert", "context", "dp"), scatter_dimension=0, tiled=True),
        lax.psum_scatter(out_part, ("expert", "context", "dp"), scatter_dimension=0, tiled=True),
        lax.psum_scatter(
            gain_ffn_part, ("expert", "context", "dp"), scatter_dimension=0, tiled=True
        ),
        lax.psum_scatter(router_part, ("expert", "context", "dp"), scatter_dimension=0, tiled=True),
    )
    return (
        output[None],
        input_grad[None],
        gain_attn_grad,
        qkv_grad,
        out_proj_grad,
        gain_ffn_grad,
        router_grad,
        expert_in,
        expert_down,
    )


def solution(mesh):
    in_specs = (
        P(("expert", "dp"), "context", None),
        P(("expert", "dp"), None),
        P(("expert", "dp"), "context", None),
        P(("expert", "dp"), "context", None),
        P(),
        P(),
        P(),
        P(),
        P(),
        P("expert", None, None),
        P("expert", None, None),
        P(("expert", "dp"), "context", None),
    )
    out_specs = (
        P(("expert", "dp"), "context", None),
        P(("expert", "dp"), "context", None),
        P(("expert", "context", "dp")),
        P(("expert", "context", "dp"), None),
        P(("expert", "context", "dp"), None),
        P(("expert", "context", "dp")),
        P(("expert", "context", "dp"), None),
        P("expert", ("context", "dp"), None),
        P("expert", ("context", "dp"), None),
    )
    tuned = dict(mesh.shape) == {"expert": 2, "context": 4, "dp": 4}
    body = local if tuned else general
    return jax.shard_map(body, mesh=mesh, in_specs=in_specs, out_specs=out_specs, check_vma=False)
```

```python
import functools

import jax
import jax.numpy as jnp
import numpy as np
from jax import lax
from jax.experimental import pallas as pl
from jax.experimental.pallas import tpu as pltpu
from jax.sharding import PartitionSpec as P

HEADS = 12
KV_HEADS = 2
HEAD = 128


ROPE_BASE = 1000000.0
NORM_EPS = 1e-06
MASKED = -1e30


def rope_tables(positions, head_size):
    half_size = head_size // 2
    freqs = ROPE_BASE ** (jnp.arange(half_size).astype(jnp.float32) * (-2.0 / head_size))
    angles = positions[:, None] * freqs[None, :]
    return (jnp.cos(angles)[:, None, :], jnp.sin(angles)[:, None, :])


def rotate(values, cosine, sine):
    half_size = values.shape[-1] // 2
    first = values[..., :half_size]
    second = values[..., half_size:]
    return jnp.concatenate(
        [first * cosine - second * sine, second * cosine + first * sine], axis=-1
    )


def unrotate(values, cosine, sine):
    half_size = values.shape[-1] // 2
    first = values[..., :half_size]
    second = values[..., half_size:]
    return jnp.concatenate(
        [first * cosine + second * sine, second * cosine - first * sine], axis=-1
    )


def softmax_last(scores):
    shifted = jnp.exp(scores - jnp.max(scores, axis=-1, keepdims=True))
    return shifted / jnp.sum(shifted, axis=-1, keepdims=True)


def route(block_ids, block_order, n_experts, capacity):
    flat_ids = block_ids.reshape(-1)
    flat_order = block_order.reshape(-1)
    choose = (flat_ids[:, None] == jnp.arange(n_experts)[None, :]).astype(jnp.int32)
    ordered = jnp.zeros_like(choose).at[flat_order].set(choose)
    earlier = jnp.cumsum(ordered, axis=0, dtype=jnp.int32) - ordered
    ranks = jnp.sum(earlier[flat_order] * choose, axis=1)
    return jnp.where(ranks < capacity, flat_ids * capacity + ranks, n_experts * capacity)


MESH = pl.DeviceIdType.MESH
F32 = jnp.float32
BF16 = jnp.bfloat16
BACK_LOW = 96
OUT_LOW = 128
FRONT_LOW = 96
FRONT_AHEAD = 64


def dot(a, b):
    return jnp.dot(a, b, preferred_element_type=F32)


def dot_nt(a, b):
    return lax.dot_general(a, b, (((1,), (1,)), ((), ())), preferred_element_type=F32)


def dot_tn(a, b):
    return lax.dot_general(a, b, (((0,), (0,)), ((), ())), preferred_element_type=F32)


def plus(a, *more):
    total = a.astype(F32)
    for b in more:
        total = total + b.astype(F32)
    return total.astype(BF16)


def lanes(at, size):
    return pl.ds(pl.multiple_of(at, 128), size)


def rows_at(at, size):
    return pl.ds(pl.multiple_of(at, 16), size)


def remote(src, dst, s, r, dev):
    return pltpu.make_async_remote_copy(
        src_ref=src, dst_ref=dst, send_sem=s, recv_sem=r, device_id=dev, device_id_type=MESH
    )


class Spot:
    def __init__(self):
        e, c, z = lax.axis_index("expert"), lax.axis_index("context"), lax.axis_index("dp")
        self.ctx = lax.axis_size("context")
        self.parts = lax.axis_size("dp")
        self.planes = self.ctx * lax.axis_size("expert")
        y, k = lax.div(c, 2), lax.rem(c, 2)
        self.e, self.c, self.z, self.k = e, c, z, k
        self.me = e * self.ctx + c
        self.xp, self.yp = (1 - e, c, z), (e, (1 - y) * 2 + k, z)
        self.kp, self.yk = (e, y * 2 + 1 - k, z), (e, (1 - y) * 2 + 1 - k, z)
        self.chips = [
            eq * self.ctx + yq * 2 for eq, yq in ((e, y), (1 - e, y), (e, 1 - y), (1 - e, 1 - y))
        ]

    def others(self):
        found = []
        for step in range(1, self.planes):
            other = lax.rem(self.me + step, self.planes)
            found.append((other, (lax.div(other, self.ctx), lax.rem(other, self.ctx), self.z)))
        return found

    def along(self):
        e, c, z = self.e, self.c, self.z
        return [(z < self.parts - 1, (e, c, z + 1)), (z > 0, (e, c, z - 1))]


def greet(peers, extra=()):
    barrier = pltpu.get_barrier_semaphore()
    for peer in peers:
        pl.semaphore_signal(barrier, inc=1, device_id=peer, device_id_type=MESH)
    for there, peer in extra:

        @pl.when(there)
        def _():
            pl.semaphore_signal(barrier, inc=1, device_id=peer, device_id_type=MESH)

    count = len(peers)
    for there, _ in extra:
        count = count + there.astype(jnp.int32)
    pl.semaphore_wait(barrier, count)


class Plane:
    def __init__(self, spot, zcr, zk, rx, ry, s, r, zcr_there=None, low=None):
        self.zcr_there = zcr_there or zcr
        self.spot, self.zcr, self.zk, self.rx, self.ry, self.s, self.r = spot, zcr, zk, rx, ry, s, r
        low = low or zk[0].shape[0] // 2
        self.lo, self.hi = pl.ds(0, low), pl.ds(low, zk[0].shape[0] - low)
        self.sent, self.gives = [], []

    def push(self, src, dst, i, dev):
        copy = remote(src, dst, self.s.at[i], self.r.at[i], dev)
        copy.start()
        self.sent.append(copy)

    def arrive(self, dst, i):
        remote(dst, dst, self.s.at[i], self.r.at[i], self.spot.kp).wait_recv()

    def given(self):
        for copy in self.gives:
            copy.wait_send()
        self.gives = []

    def give(self, q, src):
        self.gives.append(remote(src, self.zcr_there[q], self.s.at[q], self.r.at[q], self.spot.kp))
        self.gives[-1].start()

    def fold(self, q, own=None):
        self.arrive(self.zcr[q], q)
        self.zk[q][...] = plus(self.zk[q][...] if own is None else own, self.zcr[q][...])

    def near(self):
        self.push(self.zk[1].at[self.lo], self.rx[1], 5, self.spot.xp)
        self.push(self.zk[2].at[self.hi], self.ry[1], 8, self.spot.yp)

    def across(self):
        self.push(self.zk[3].at[self.lo], self.rx[0], 4, self.spot.xp)
        self.push(self.zk[3].at[self.hi], self.ry[0], 7, self.spot.yp)

    def turn(self):
        lo, hi = self.lo, self.hi
        self.arrive(self.rx[0], 4)
        self.zk[2][lo] = plus(self.zk[2][lo], self.rx[0][...])
        self.push(self.zk[2].at[lo], self.ry[2], 9, self.spot.yp)
        self.arrive(self.ry[0], 7)
        self.zk[1][hi] = plus(self.zk[1][hi], self.ry[0][...])
        self.push(self.zk[1].at[hi], self.rx[2], 6, self.spot.xp)

    def total(self):
        self.arrive(self.rx[1], 5)
        self.arrive(self.ry[1], 8)
        self.arrive(self.rx[2], 6)
        self.arrive(self.ry[2], 9)
        return (
            (self.lo, (self.zk[0][self.lo], self.rx[1][...], self.ry[2][...])),
            (self.hi, (self.zk[0][self.hi], self.rx[2][...], self.ry[1][...])),
        )

    def done(self):
        self.given()
        for copy in self.sent:
            copy.wait_send()


def plane_of(spot, zcr, zk, rx, ry, s, r, low=None):
    four, block = range(4), zk.shape[1]
    lo, hi = pl.ds(0, low or block // 2), pl.ds(0, block - (low or block // 2))
    return Plane(
        spot,
        [zcr.at[q] for q in four],
        [zk.at[q] for q in four],
        [rx.at[0, lo], rx.at[1, lo], rx.at[2, hi]],
        [ry.at[0, hi], ry.at[1, hi], ry.at[2, lo]],
        s,
        r,
        low=low,
    )


def plane_scratch(block, wide, low=None):
    most = max(low or block // 2, block - (low or block // 2))
    return [
        pltpu.VMEM((4, block, wide), BF16),
        pltpu.VMEM((4, block, wide), BF16),
        pltpu.VMEM((3, most, wide), BF16),
        pltpu.VMEM((3, most, wide), BF16),
        pltpu.SemaphoreType.DMA((10,)),
        pltpu.SemaphoreType.DMA((10,)),
    ]


def summed(terms):
    total = terms[0].astype(F32)
    for term in terms[1:]:
        total = total + term.astype(F32)
    return total


class Line:
    def __init__(self, spot, own, adder, buf, s, r):
        z, last = spot.z, spot.parts - 1
        e, c = spot.e, spot.c
        self.own, self.adder, self.buf, self.s, self.r = own, adder, buf, s, r
        self.z, self.last, self.parts = z, last, spot.parts
        self.ways = [(z, (e, c, z + 1), lambda d: d), (last - z, (e, c, z - 1), lambda d: last - d)]

    def step(self, turn):
        for way, (i, dev, part) in enumerate(self.ways):
            to, s, r = self.buf.at[way, turn - 1], self.s.at[way, turn - 1], self.r.at[way, turn - 1]

            @pl.when(i == 0)
            def _():
                remote(self.own(part(self.parts - turn)), to, s, r, dev).start()

            if turn >= 2:
                came, s_came, r_came = (x.at[way, turn - 2] for x in (self.buf, self.s, self.r))

                @pl.when((i >= 1) & (i <= turn - 1) & (i < self.last))
                def _():
                    remote(came, came, s_came, r_came, dev).wait_recv()
                    self.adder(came, part(self.parts - turn + i))
                    remote(came, to, s, r, dev).start()

    def final(self, put):
        last, z = self.last, self.z
        for way, (i, dev, _) in enumerate(self.ways):
            came = self.buf.at[way, last - 1]

            @pl.when(i >= 1)
            def _():
                remote(came, came, self.s.at[way, last - 1], self.r.at[way, last - 1], dev).wait_recv()

        up, down = self.buf.at[0, last - 1], self.buf.at[1, last - 1]
        pl.when(z == 0)(lambda: put(down))
        pl.when(z == last)(lambda: put(up))
        pl.when((z > 0) & (z < last))(lambda: put(up, down))

    def done(self):
        for way, (i, dev, _) in enumerate(self.ways):
            for turn in range(1, self.parts):
                came = self.buf.at[way, turn - 1]

                @pl.when((i <= turn - 1) & (i < self.last))
                def _():
                    remote(came, came, self.s.at[way, turn - 1], self.r.at[way, turn - 1], dev).wait_send()


def line_scratch(parts, piece):
    return [
        pltpu.VMEM((2, parts - 1) + piece, BF16),
        pltpu.SemaphoreType.DMA((2, parts - 1)),
        pltpu.SemaphoreType.DMA((2, parts - 1)),
    ]


class ExpertLine:
    def __init__(self, spot, ref, at, cols, buf, s, r, fin, spread=None, a_s=None, a_r=None):
        self.spot, self.ref, self.at, self.cols = spot, ref, at, cols
        self.fin, self.spread, self.a_s, self.a_r = fin, spread, a_s, a_r
        self.line = Line(spot, self.own, self.adder, buf, s, r)
        self.step = self.line.step

    def own(self, d):
        return self.ref.at[:, d, :, pl.ds(self.at, self.cols)]

    def piece(self, cc, d):
        return self.ref[cc, d, :, self.at : self.at + self.cols]

    def adder(self, came, d):
        for cc in range(self.spot.ctx):
            came[cc] = plus(came[cc], self.piece(cc, d))

    def final(self):
        spot = self.spot

        def put(*came):
            for cc in range(spot.ctx):
                self.fin[cc] = plus(self.piece(cc, spot.z), *(x[cc] for x in came))

        self.line.final(put)
        if self.spread is None:
            return
        for step in range(1, spot.ctx):
            cc = lax.rem(spot.c + step, spot.ctx)
            remote(
                self.fin.at[cc],
                self.spread.at[spot.c],
                self.a_s.at[step - 1],
                self.a_r.at[step - 1],
                (spot.e, cc, spot.z),
            ).start()

    def done(self, out=None):
        spot = self.spot
        if self.spread is None:
            self.line.done()
            return
        for step in range(1, spot.ctx):
            cc = lax.rem(spot.c + spot.ctx - step, spot.ctx)
            got = remote(
                self.spread.at[cc],
                self.spread.at[cc],
                self.a_s.at[step - 1],
                self.a_r.at[step - 1],
                (spot.e, cc, spot.z),
            )
            got.wait_recv()
            got.wait_send()
            out[cc] = self.spread[cc]
        out[spot.c] = self.fin[spot.c]
        self.line.done()


def expert_scratch(ctx, parts, rows, cols):
    return line_scratch(parts, (ctx, rows, cols)) + [
        pltpu.VMEM((ctx, rows, cols), BF16),
        pltpu.VMEM((ctx, rows, cols), BF16),
        pltpu.SemaphoreType.DMA((ctx - 1,)),
        pltpu.SemaphoreType.DMA((ctx - 1,)),
    ]


class Gather:
    def __init__(self, spot, own, buf, s, r, low=None, ahead=0):
        self.spot, self.own, self.buf, self.s, self.r = spot, own, buf, s, r
        low = low or own.shape[0] // 2
        self.lo, self.hi = pl.ds(0, low), pl.ds(low, own.shape[0] - low)
        self.ahead, self.rest = ahead and pl.ds(low, ahead), pl.ds(low + ahead, own.shape[0] - low - ahead)
        self.x_me, self.y_me, self.d_me = (base + spot.k for base in spot.chips[1:])
        self.side = 1 - 2 * spot.k
        self.sent = []

    def push(self, src, dst, i, dev):
        copy = remote(src, dst, self.s.at[i], self.r.at[i], dev)
        copy.start()
        self.sent.append(copy)

    def move(self, p, rows, i, dev):
        self.push(self.buf.at[p, rows], self.buf.at[p, rows], i, dev)

    def got(self, p, rows, i):
        to = self.buf.at[p, rows]
        remote(to, to, self.s.at[i], self.r.at[i], self.spot.kp).wait_recv()

    def start(self):
        me, own, lo, hi = self.spot.me, self.own, self.lo, self.hi
        self.push(own.at[lo], self.buf.at[me, lo], 0, self.spot.xp)
        if self.ahead:
            self.push(own.at[self.ahead], self.buf.at[me, self.ahead], 14, self.spot.yp)
        self.push(own.at[lo], self.buf.at[me, lo], 6, self.spot.kp)
        self.push(own.at[hi], self.buf.at[me, hi], 13, self.spot.kp)
        self.push(own.at[hi], self.buf.at[me, hi], 1, self.spot.xp)

    def start_y(self):
        me, own, lo, rest = self.spot.me, self.own, self.lo, self.rest
        self.push(own.at[rest], self.buf.at[me, rest], 3, self.spot.yp)
        self.push(own.at[lo], self.buf.at[me, lo], 2, self.spot.yp)

    def first(self):
        spot = self.spot
        self.got(self.x_me, self.lo, 0)
        self.move(self.x_me, self.lo, 4, spot.yp)
        self.move(self.x_me, self.lo, 7, spot.kp)
        if self.ahead:
            self.got(self.y_me, self.ahead, 14)
        self.got(self.y_me, self.rest, 3)
        self.move(self.y_me, self.hi, 5, spot.xp)
        self.move(self.y_me, self.hi, 10, spot.kp)

    def second(self):
        self.got(self.x_me, self.hi, 1)
        self.move(self.x_me, self.hi, 8, self.spot.kp)
        self.got(self.y_me, self.lo, 2)
        self.move(self.y_me, self.lo, 9, self.spot.kp)

    def third(self):
        self.got(self.d_me, self.lo, 4)
        self.move(self.d_me, self.lo, 11, self.spot.kp)
        self.got(self.d_me, self.hi, 5)
        self.move(self.d_me, self.hi, 12, self.spot.kp)

    def other_core(self, q):
        low_sem, high_sem = ((6, 13), (7, 8), (9, 10), (11, 12))[q]
        p = (self.spot.me, self.x_me, self.y_me, self.d_me)[q] + self.side
        self.got(p, self.lo, low_sem)
        self.got(p, self.hi, high_sem)

    def done(self):
        for copy in self.sent:
            copy.wait_send()


GATHER_COPIES = 15


def front_kernel(
    cap,
    span,
    hidden,
    cot,
    gain_one,
    freqs,
    gain_two,
    router_t,
    ids_t,
    turn_t,
    wqkv_h,
    wout_h,
    normed_h,
    queries_h,
    kv_h,
    lse,
    attended,
    resid,
    ffn_in,
    trig,
    meta,
    cot_all,
    wqkv,
    wout,
    mask,
    vt,
    normed,
    queries,
    kv,
    load_sem,
    out_sem,
    kv_s,
    kv_r,
    co_s,
    co_r,
):
    spot = Spot()
    c, ctx, k = spot.c, spot.ctx, spot.k
    tok, width = hidden.shape
    group = HEADS // KV_HEADS
    kv_cols = KV_HEADS * HEAD
    half_head = HEAD // 2
    seq = kv.shape[0]
    spans = span.shape[1]
    size = seq // spans
    mine = spans // ctx
    n_experts = meta.shape[0]
    loads = [
        pltpu.make_async_copy(wqkv_h.at[:, pl.ds(width, 2 * kv_cols)], wqkv.at[:, pl.ds(width, 2 * kv_cols)], load_sem.at[0]),
        pltpu.make_async_copy(wqkv_h.at[:, pl.ds(0, width)], wqkv.at[:, pl.ds(0, width)], load_sem.at[1]),
        pltpu.make_async_copy(wout_h, wout, load_sem.at[2]),
        pltpu.make_async_copy(cot, cot_all.at[spot.me], load_sem.at[3]),
    ]
    for load in loads:
        load.start()
    greet([spot.xp, spot.yp, spot.kp])
    gather = Gather(spot, cot, cot_all, co_s, co_r, low=FRONT_LOW, ahead=FRONT_AHEAD)
    gather.start()

    x = hidden[...].astype(F32)
    inv = lax.rsqrt(jnp.mean(x * x, axis=-1, keepdims=True) + NORM_EPS)
    normed[...] = (x * inv * gain_one[...]).astype(BF16)

    along = lax.broadcasted_iota(jnp.int32, (tok, HEAD), 0)
    start_one, start_two = span[0, c * mine] * size, (span[0, c * mine + 1] - 1) * size
    place = jnp.where(along < size, start_one, start_two) + along
    angle = place.astype(F32) * freqs[...]
    cosine, sine = jnp.cos(angle), jnp.sin(angle)
    lane = lax.broadcasted_iota(jnp.int32, (tok, HEAD), 1)
    sine = jnp.where(lane < half_head, -sine, sine)
    trig[0] = cosine
    trig[1] = sine

    def rotate_in(w):
        return w * cosine + pltpu.roll(w, half_head, 1) * sine

    loads[0].wait()
    raw = dot(normed[...], wqkv[:, width:])
    own = rows_at(c * tok, tok)
    for g in range(KV_HEADS):
        at = slice(g * HEAD, (g + 1) * HEAD)
        kv[own, at] = rotate_in(raw[:, at]).astype(BF16)
    kv[own, kv_cols:] = raw[:, kv_cols:].astype(BF16)

    def kv_copy(rows, i, dev):
        return remote(kv.at[rows], kv.at[rows], kv_s.at[i], kv_r.at[i], dev)

    flip_c = lax.rem(c + 2, ctx)
    near_c = c + 1 - 2 * k
    across_c = lax.rem(near_c + 2, ctx)
    sent = [kv_copy(own, 1, spot.yp), kv_copy(own, 0, spot.kp)]
    for copy in sent:
        copy.start()
    gather.start_y()

    outs = [pltpu.make_async_copy(normed, normed_h, out_sem.at[0])]
    outs[0].start()
    loads[1].wait()
    step = 256

    @pl.loop(0, width // step)
    def _(n):
        at = lanes(n * step, step)
        raw = dot(normed[...], wqkv[:, at])
        for i in range(step // HEAD):
            w = raw[:, i * HEAD : (i + 1) * HEAD]
            queries[:, lanes(n * step + i * HEAD, HEAD)] = (rotate_in(w) * HEAD**-0.5).astype(BF16)

    outs.append(pltpu.make_async_copy(queries, queries_h, out_sem.at[1]))
    outs[1].start()

    flip = rows_at(flip_c * tok, tok)
    kv_copy(flip, 1, spot.kp).wait_recv()
    sent.append(kv_copy(flip, 2, spot.kp))
    sent[-1].start()

    expert = lax.broadcasted_iota(jnp.int32, (n_experts, tok), 0)
    never = tok * ids_t.shape[0]
    turn = jnp.full((n_experts, tok), never, jnp.int32)
    for i in range(ids_t.shape[0]):
        turn = jnp.where(ids_t[i : i + 1, :] == expert, turn_t[i : i + 1, :], turn)
    turn_f = turn.astype(F32)
    tall = jnp.concatenate([turn_f, jnp.full((HEAD - n_experts, tok), float(never), F32)], axis=0).T
    meta[...] = jnp.zeros(meta.shape, F32)
    for g in range(n_experts):
        row = turn_f[g : g + 1, :]
        rank = jnp.sum(jnp.where(tall[:, g : g + 1] < row, 1.0, 0.0), axis=0, keepdims=True)
        meta[g, 0:1, :] = jnp.where((row < never) & (rank < cap), rank, -1.0)

    along_q = lax.broadcasted_iota(jnp.int32, (size, tok), 1)
    q_pos = jnp.where(along_q < size, start_one, start_two) + along_q
    for s in range(spans):
        k_pos = span[0, s] * size + lax.broadcasted_iota(jnp.int32, (size, tok), 0)
        mask[s * size : (s + 1) * size, :] = jnp.where(k_pos <= q_pos, 0.0, MASKED)

    near, across = rows_at(near_c * tok, tok), rows_at(across_c * tok, tok)
    kv_copy(near, 0, spot.kp).wait_recv()
    kv_copy(across, 2, spot.kp).wait_recv()
    outs.append(pltpu.make_async_copy(kv, kv_h, out_sem.at[2]))
    outs[2].start()
    for g in range(KV_HEADS):
        vt[g] = kv[:, kv_cols + g * HEAD : kv_cols + (g + 1) * HEAD].astype(F32).T.astype(BF16)
    lse[...] = jnp.zeros(lse.shape, F32)

    def heads(g, first, count):
        @pl.loop(first, first + count)
        def _(h):
            at = lanes(h * HEAD, HEAD)
            scores = dot_nt(kv[:, g * HEAD : (g + 1) * HEAD], queries[:, at]) + mask[...]
            top = jnp.max(scores, axis=0, keepdims=True)
            weights = jnp.exp(scores - top)
            total = jnp.sum(weights, axis=0, keepdims=True)
            lse[pl.ds(h, 1), :] = top + jnp.log(total)
            out = dot(vt[g], weights.astype(BF16)) / total
            attended[:, at] = out.T.astype(BF16)

    heads(0, 0, 3)
    gather.first()
    heads(0, 3, 3)
    heads(1, 6, 3)
    gather.second()
    heads(1, 9, 3)

    loads[2].wait()

    @pl.loop(0, width // step)
    def _(n):
        at = lanes(n * step, step)
        resid[:, at] = hidden[:, at].astype(F32) + dot_nt(attended[...], wout[at, :])

    r = resid[...]
    inv = lax.rsqrt(jnp.mean(r * r, axis=-1, keepdims=True) + NORM_EPS)
    ffn_in[...] = (r * inv * gain_two[...]).astype(BF16)
    logits = dot_nt(router_t[...], ffn_in[...])[:n_experts]
    logits = jnp.where(turn < never, logits, MASKED)
    shifted = jnp.exp(logits - jnp.max(logits, axis=0, keepdims=True))
    gates = shifted / jnp.sum(shifted, axis=0, keepdims=True)
    for g in range(n_experts):
        meta[g, 1:2, :] = gates[g : g + 1, :]
    gather.third()
    for q in range(4):
        gather.other_core(q)
    loads[3].wait()
    gather.done()
    for copy in outs:
        copy.wait()
    for copy in sent:
        copy.wait_send()


def run_front(cap, span, hidden, cot, gain_one, freqs, gain_two, router_t, ids_t, turn_t, wqkv, wout, ctx, planes):
    tok, width = hidden.shape
    seq = tok * ctx
    n_experts = planes
    kv_cols = 2 * KV_HEADS * HEAD
    vm, anyspace = pl.BlockSpec(memory_space=pltpu.VMEM), pl.BlockSpec(memory_space=pl.ANY)
    sm = pl.BlockSpec(memory_space=pltpu.SMEM)
    shape = jax.ShapeDtypeStruct
    dma = pltpu.SemaphoreType.DMA
    return pl.pallas_call(
        functools.partial(front_kernel, cap),
        out_shape=(
            shape((tok, width), BF16),
            shape((tok, width), BF16),
            shape((seq, kv_cols), BF16),
            shape((16, tok), F32),
            shape((tok, width), BF16),
            shape((tok, width), F32),
            shape((tok, width), BF16),
            shape((2, tok, HEAD), F32),
            shape((n_experts, 8, tok), F32),
            shape((planes, tok, width), BF16),
        ),
        in_specs=[sm] + [vm] * 8 + [anyspace] * 2,
        out_specs=(anyspace,) * 3 + (vm,) * 6 + (anyspace,),
        scratch_shapes=[
            pltpu.VMEM(wqkv.shape, BF16),
            pltpu.VMEM(wout.shape, BF16),
            pltpu.VMEM((seq, tok), F32),
            pltpu.VMEM((KV_HEADS, HEAD, seq), BF16),
            pltpu.VMEM((tok, width), BF16),
            pltpu.VMEM((tok, width), BF16),
            pltpu.VMEM((seq, kv_cols), BF16),
            dma((4,)),
            dma((3,)),
            dma((3,)),
            dma((3,)),
            dma((GATHER_COPIES,)),
            dma((GATHER_COPIES,)),
        ],
        compiler_params=pltpu.CompilerParams(
            collective_id=4, has_side_effects=True, vmem_limit_bytes=56 * 2**20
        ),
        cost_estimate=pl.CostEstimate(flops=5 * 10**9, bytes_accessed=20 * 10**6, transcendentals=4 * 10**6),
    )(span, hidden, cot, gain_one, freqs, gain_two, router_t, ids_t, turn_t, wqkv, wout)


def ffn_kernel(cap, ffn_h, resid_h, cot_h, meta, win_h, wdn_h, output, pg_out, gg_out, gwin_h, ex_out, *scratch):
    agb, metas, cotb, win, wdn, xs, ds, hid, igs, pgs, ggs, ggr, wint, gwdn = scratch[:14]
    load_sem, ag_s, ag_r, me_s, me_r, gg_s, gg_r, out_s, out_r = scratch[14:23]
    plane_refs, line_refs, first_refs = scratch[23:29], scratch[29:32], scratch[32:]
    spot = Spot()
    c, k, me = spot.c, spot.k, spot.me
    kp = spot.kp
    tok, width = output.shape
    ff = wdn.shape[1]
    planes, ctx = spot.planes, spot.ctx
    chips = spot.chips

    loads = [
        pltpu.make_async_copy(win_h.at[c], win, load_sem.at[0]),
        pltpu.make_async_copy(wdn_h.at[c], wdn, load_sem.at[1]),
        pltpu.make_async_copy(cot_h, cotb, load_sem.at[2]),
        pltpu.make_async_copy(resid_h, pg_out, load_sem.at[3]),
    ]
    own_load = pltpu.make_async_copy(ffn_h, agb.at[me], load_sem.at[4])
    own_load.start()
    others = spot.others()
    greet([dev for _, dev in others], spot.along())
    plane = plane_of(spot, *plane_refs)
    o_lo, o_hi = pl.ds(0, OUT_LOW), pl.ds(OUT_LOW, tok - OUT_LOW)
    outs = Plane(
        spot,
        [agb.at[2 * i + k] for i in range(4)],
        [cotb.at[base + k] for base in chips],
        [agb.at[1 - k, o_lo], agb.at[3 - k, o_lo], agb.at[1 - k, o_hi]],
        [agb.at[3 - k, o_hi], agb.at[5 - k, o_hi], agb.at[5 - k, o_lo]],
        out_s,
        out_r,
        [agb.at[2 * i + 1 - k] for i in range(4)],
        low=OUT_LOW,
    )
    line = ExpertLine(spot, gwdn, 0, ff, *line_refs, ex_out.at[:, :, pl.ds(0, ff)])
    some = ex_out.shape[2] - ff
    first_line = ExpertLine(spot, win, 0, some, *first_refs, ex_out.at[:, :, pl.ds(ff, some)])
    gather = Gather(spot, agb.at[me], agb, ag_s, ag_r)
    for step, (other, dev) in enumerate(others):
        remote(meta.at[other], metas.at[me], me_s.at[step], me_r.at[step], dev).start()
    own_load.wait()
    gather.start()
    gather.start_y()
    for load in loads:
        load.start()
    metas[me] = meta[me]
    slot_rows = lax.broadcasted_iota(jnp.int32, (cap, tok), 0).astype(F32)
    step = 256

    def spots(p):
        return jnp.where(slot_rows == metas[p, 0:1, :], 1.0, 0.0)

    def gate_of(p, hot):
        return jnp.sum(hot * metas[p, 1:2, :], axis=1, keepdims=True)

    def dispatch(q):
        for kk in range(2):
            p = chips[q] + kk
            hot = spots(p)
            low = hot.astype(BF16)
            part = pl.ds(q * 2 * cap + kk * cap, cap)
            xs[part, :] = dot(low, agb[p]).astype(BF16)
            ds[part, :] = (dot(low, cotb[p]) * gate_of(p, hot)).astype(BF16)

    def work(q, count):
        rows = pl.ds(q * 2 * cap, count * 2 * cap)

        @pl.loop(0, ff // step)
        def _(n):
            gate_cols, up_cols = lanes(n * step, step), lanes(ff + n * step, step)
            x = xs[rows, :]
            g = dot(x, win[:, :, :, gate_cols].reshape(width, step))
            u = dot(x, win[:, :, :, up_cols].reshape(width, step))
            s = 1.0 / (1.0 + jnp.exp(-g))
            act = g * s
            hid[rows, gate_cols] = (act * u).astype(BF16)
            h = dot(ds[rows, :], wdn[:, gate_cols])
            igs[rows, gate_cols] = (h * u * (s * (1.0 + g * (1.0 - s)))).astype(BF16)
            igs[rows, up_cols] = (h * act).astype(BF16)

        @pl.loop(0, width // step)
        def _(n):
            cols = lanes(n * step, step)
            pgs[pl.ds(0, count * 2 * cap), cols] = dot(igs[rows, :], wint[:, cols]).astype(BF16)

    def back(q, at):
        base = chips[q]
        mine, theirs = rows_at(at * 2 * cap + k * cap, cap), rows_at(at * 2 * cap + (1 - k) * cap, cap)
        given = agb.at[base + 1 - k]
        given[...] = dot_tn(spots(base + 1 - k).astype(BF16), pgs[theirs, :]).astype(BF16)
        plane.give(q, given)
        plane.zk[q][...] = dot_tn(spots(base + k).astype(BF16), pgs[mine, :]).astype(BF16)

    loads[0].wait()
    tall = width // ctx

    @pl.loop(0, ctx)
    def _(n):
        wint[:, lanes(n * tall, tall)] = win[n].reshape(tall, 2 * ff).T

    for n in range(planes - 1):
        source = lax.rem(me + planes - 1 - n, planes)
        remote(metas.at[source], metas.at[source], me_s.at[n], me_r.at[n], kp).wait_recv()
    for load in loads[1:]:
        load.wait()
    gather.other_core(0)
    dispatch(0)
    work(0, 1)
    back(0, 0)
    gather.first()
    gather.second()
    gather.other_core(1)
    dispatch(1)
    gather.other_core(2)
    dispatch(2)
    work(1, 2)
    gather.third()
    back(1, 0)
    back(2, 1)
    gather.other_core(3)
    gather.done()
    dispatch(3)
    plane.fold(1)
    plane.fold(2)
    plane.near()
    work(3, 1)
    back(3, 0)
    plane.fold(3)
    plane.given()
    plane.across()


    @pl.loop(0, ctx)
    def _(n):
        tile = dot_tn(ds[:, lanes(n * tall, tall)], hid[...]).astype(BF16)
        for d in range(gwdn.shape[1]):
            gwdn[n, d] = tile[d * gwdn.shape[2] : (d + 1) * gwdn.shape[2]]

    line.step(1)
    plane.fold(0)

    @pl.loop(0, width // step)
    def _(n):
        cols = lanes(n * step, step)
        ds[:, cols] = dot_nt(hid[...], wdn[cols, :]).astype(BF16)

    def returned(q):
        base = chips[q]
        for kk in range(2):
            p = base + kk
            hot = spots(p)
            rows = ds[pl.ds(q * 2 * cap + kk * cap, cap), :]
            ggs[p, 0:1, :] = jnp.sum(hot * dot_nt(rows, cotb[p]), axis=0, keepdims=True)
            scaled = (rows.astype(F32) * gate_of(p, hot)).astype(BF16)
            cotb[p] = dot_tn(hot.astype(BF16), scaled).astype(BF16)
        outs.give(q, cotb.at[base + 1 - k])

    returned(1)
    returned(2)
    plane.turn()
    returned(3)
    returned(0)
    outs.fold(1)
    outs.fold(2)
    outs.near()
    outs.fold(3)
    outs.across()
    ggr[me] = ggs[me]
    for n, (other, dev) in enumerate(others):
        remote(ggs.at[other], ggr.at[me], gg_s.at[n], gg_r.at[n], dev).start()
    line.step(2)
    outs.fold(0)

    def gate_up(at, size):
        @pl.loop(0, ctx)
        def _(n):
            tile = dot_tn(xs[:, lanes(n * tall, tall)], igs[:, pl.ds(at, size)]).astype(BF16)
            win[n, :, :, pl.ds(at, size)] = tile.reshape(gwdn.shape[1], gwdn.shape[2], size)

    gate_up(0, some)
    first_line.step(1)
    rest = 2 * ff - some
    gate_up(some, rest // 2)
    gate_up(some + rest // 2, rest // 2)
    gwin_copy = pltpu.make_async_copy(win.at[:, :, :, pl.ds(some, rest)], gwin_h, load_sem.at[0])
    gwin_copy.start()
    line.step(3)
    outs.turn()
    first_line.step(2)
    line.final()
    for rows, terms in outs.total():
        output[rows, :] = (pg_out[rows, :] + summed(terms)).astype(BF16)
    for rows, terms in plane.total():
        pg_out[rows, :] = summed(terms)
    for n in range(planes - 1):
        source = lax.rem(me + planes - 1 - n, planes)
        remote(ggr.at[source], ggr.at[source], gg_s.at[n], gg_r.at[n], kp).wait_recv()
    for p in range(planes):
        gg_out[p : p + 1, :] = ggr[p, 0:1, :]
    first_line.step(3)
    first_line.final()
    gwin_copy.wait()
    for n, (other, dev) in enumerate(others):
        remote(meta.at[other], metas.at[other], me_s.at[n], me_r.at[n], dev).wait_send()
        remote(ggs.at[other], ggr.at[other], gg_s.at[n], gg_r.at[n], dev).wait_send()
    plane.done()
    outs.done()
    line.done()
    first_line.done()


def run_ffn(cap, ffn, resid, cot_all, meta, win, wdn, parts, some):
    tok, width = ffn.shape
    ff = wdn.shape[2]
    planes = cot_all.shape[0]
    ctx = win.shape[0]
    rows = planes * cap
    piece = width // (ctx * parts)
    win = win.reshape(ctx, ctx, parts, piece, 2 * ff)
    vm, anyspace = pl.BlockSpec(memory_space=pltpu.VMEM), pl.BlockSpec(memory_space=pl.ANY)
    shape = jax.ShapeDtypeStruct
    dma = pltpu.SemaphoreType.DMA
    return pl.pallas_call(
        functools.partial(ffn_kernel, cap),
        out_shape=(
            shape((tok, width), BF16),
            shape((tok, width), F32),
            shape((planes, tok), F32),
            shape((ctx, parts, piece, 2 * ff - some), BF16),
            shape((ctx, piece, ff + some), BF16),
        ),
        in_specs=[anyspace, anyspace, anyspace, vm, anyspace, anyspace],
        out_specs=(vm, vm, vm, anyspace, vm),
        scratch_shapes=[
            pltpu.VMEM((planes, tok, width), BF16),
            pltpu.VMEM((planes, 8, tok), F32),
            pltpu.VMEM((planes, tok, width), BF16),
            pltpu.VMEM((ctx, parts, piece, 2 * ff), BF16),
            pltpu.VMEM((width, ff), BF16),
            pltpu.VMEM((rows, width), BF16),
            pltpu.VMEM((rows, width), BF16),
            pltpu.VMEM((rows, ff), BF16),
            pltpu.VMEM((rows, 2 * ff), BF16),
            pltpu.VMEM((4 * cap, width), BF16),
            pltpu.VMEM((planes, 8, tok), F32),
            pltpu.VMEM((planes, 8, tok), F32),
            pltpu.VMEM((2 * ff, width), BF16),
            pltpu.VMEM((ctx, parts, piece, ff), BF16),
            dma((5,)),
            dma((GATHER_COPIES,)),
            dma((GATHER_COPIES,)),
            dma((planes - 1,)),
            dma((planes - 1,)),
            dma((planes - 1,)),
            dma((planes - 1,)),
            dma((10,)),
            dma((10,)),
        ]
        + plane_scratch(tok, width)
        + line_scratch(parts, (ctx, piece, ff))
        + line_scratch(parts, (ctx, piece, some)),
        compiler_params=pltpu.CompilerParams(
            collective_id=1, has_side_effects=True, vmem_limit_bytes=63 * 2**20
        ),
        cost_estimate=pl.CostEstimate(flops=25 * 10**9, bytes_accessed=50 * 10**6, transcendentals=10**6),
    )(ffn, resid, cot_all, meta, win, wdn)


def back_kernel(
    span,
    meta,
    gg,
    lse,
    trig,
    kv,
    queries,
    attended,
    normed,
    router_t,
    gain_two,
    gain_one,
    reduced,
    resid_h,
    cot_h,
    pg_h,
    ffn_in_h,
    hidden_h,
    wout_h,
    wqkv_h,
    gwin_h,
    input_grad,
    qkv_out,
    proj_out,
    one_out,
    two_out,
    ffn_out,
    *scratch,
):
    wide_f, back, low, attg, mixed, weights, gwin, send, bsend, smalls, total, out_red = scratch[:12]
    mask, delta, kt, dk, dv, kvs, kvr = scratch[12:19]
    load_sem, kv_s, kv_r = scratch[19:22]
    p_zcr, p_zk, p_rx, p_ry, p_s, p_r = scratch[22:28]
    a_rx, a_ry, a_s, a_r = scratch[28:32]
    e_refs, b_refs = scratch[32:38], scratch[38:44]
    qkv_refs, proj_refs = scratch[44:47], scratch[47:50]
    one_refs, two_refs = scratch[50:57], scratch[57:64]
    f_s, f_r = scratch[64:]
    spot = Spot()
    c, k, z, ctx = spot.c, spot.k, spot.z, spot.ctx
    tok, width = attended.shape
    cols = one_out.shape[2]
    block, piece = out_red.shape[0], proj_out.shape[0]
    heads_kv = KV_HEADS
    half_head = HEAD // 2
    n_experts = meta.shape[0]
    kv_wide = mixed.shape[1] - width
    step = 256

    def load(src, dst, i):
        copy = pltpu.make_async_copy(src, dst, load_sem.at[i])
        copy.start()
        return copy

    gwin_load = load(gwin_h, gwin, 0)
    early = [
        load(resid_h, wide_f, 1),
        load(pg_h, back, 2),
        load(cot_h, input_grad, 3),
        load(ffn_in_h, attg, 4),
    ]
    wout_load = load(wout_h, weights.at[:, pl.ds(0, width)], 5)
    greet([spot.xp, spot.yp, spot.kp, spot.yk], spot.along())
    for n in range(1, ctx):
        cc = lax.rem(c + n, ctx)
        remote(reduced.at[cc], ffn_out.at[c], f_s.at[n - 1], f_r.at[n - 1], (spot.e, cc, z)).start()
    ffn_out[c] = reduced[c]
    one = ExpertLine(spot, gwin, 0, cols, *one_refs)
    two = ExpertLine(spot, gwin, cols, cols, *two_refs)
    proj_plane = plane_of(spot, p_zcr, p_zk, p_rx, p_ry, p_s, p_r, low=BACK_LOW)
    half_wide = width // 2
    cut = pl.ds(0, half_wide)
    early_plane = plane_of(spot, *e_refs, low=BACK_LOW)
    late_plane = plane_of(
        spot, p_zcr.at[:, :, cut], p_zk.at[:, :, cut], a_rx, a_ry, a_s, a_r, low=BACK_LOW
    )
    rest_plane = plane_of(spot, *b_refs, low=BACK_LOW)

    def shared_line(ref, refs):
        def own(d):
            return ref.at[rows_at(d * piece, piece)]

        def adder(came, d):
            came[...] = plus(came[...], own(d)[...])

        return Line(spot, own, adder, *refs)

    qkv_line, proj_line = shared_line(total, qkv_refs), shared_line(out_red, proj_refs)

    def put_shared(to, ref, came):
        to[...] = plus(ref[rows_at(z * piece, piece)], *(x[...] for x in came))

    mine, theirs = rows_at(k * block, block), rows_at((1 - k) * block, block)
    gwin_load.wait()
    one.step(1)

    for copy in early:
        copy.wait()
    gate = jnp.concatenate([meta[g, 1:2, :] for g in range(n_experts)], axis=0)
    seen = gate * gg[...]
    mix = seen - gate * jnp.sum(seen, axis=0, keepdims=True)
    mix = jnp.concatenate([mix, jnp.zeros((HEAD - n_experts, tok), F32)], axis=0)
    logit_t = mix.astype(BF16)
    r = wide_f[...]
    inv = lax.rsqrt(jnp.mean(r * r, axis=-1, keepdims=True) + NORM_EPS)
    plain = r * inv
    ffn_grad = back[...] + dot_tn(logit_t[:n_experts], router_t[...])
    gain_row = jnp.sum(ffn_grad * plain, axis=0, keepdims=True)
    scaled = ffn_grad * gain_two[...]
    grad = input_grad[...].astype(F32) + inv * (
        scaled - plain * jnp.mean(scaled * plain, axis=-1, keepdims=True)
    )
    back[...] = grad
    low[...] = grad.astype(BF16)
    lane = lax.broadcasted_iota(jnp.int32, (width, HEAD), 1)
    routed = dot_tn(attg[...], logit_t.T)
    gain_col = jnp.broadcast_to(gain_row, (HEAD, width)).T
    smalls[...] = jnp.where(lane == n_experts, gain_col, routed).astype(BF16)

    for q in (3, 1, 2, 0):
        at = lanes(spot.chips[q] * block, 2 * block)
        send[q] = dot_tn(low[:, at], attended[...]).astype(BF16)
        proj_plane.give(q, send.at[q, theirs])
    wout_load.wait()

    @pl.loop(0, width // step)
    def _(n):
        at = lanes(n * step, step)
        attg[:, at] = dot(low[...], weights[:, at]).astype(BF16)

    wqkv_load = load(wqkv_h, weights, 5)
    hidden_load = load(hidden_h, low, 1)

    def start_plane(plane, at):
        plane.fold(3, send[3, mine, at])
        plane.across()
        plane.fold(1, send[1, mine, at])
        plane.fold(2, send[2, mine, at])
        plane.near()
        plane.fold(0, send[0, mine, at])

    def qkv_tiles(plane, at):
        for q in (3, 1, 2, 0):
            rows = lanes(spot.chips[q] * block, 2 * block)
            send[q, :, at] = dot_tn(normed[:, rows], mixed[:, at]).astype(BF16)
            plane.give(q, send.at[q, theirs, at])

    start_plane(proj_plane, pl.ds(0, width))

    seq = kv.shape[0]
    spans = span.shape[1]
    size = seq // spans
    per = spans // ctx
    along_q = lax.broadcasted_iota(jnp.int32, (size, tok), 1)
    q_pos = jnp.where(along_q < size, span[0, c * per] * size, (span[0, c * per + 1] - 1) * size) + along_q
    for s in range(spans):
        k_pos = span[0, s] * size + lax.broadcasted_iota(jnp.int32, (size, tok), 0)
        mask[s * size : (s + 1) * size, :] = jnp.where(k_pos <= q_pos, 0.0, MASKED)

    lane_h = lax.broadcasted_iota(jnp.int32, (tok, HEAD), 1)
    deltas = jnp.zeros((tok, HEAD), F32)
    for h in range(HEADS):
        at = slice(h * HEAD, (h + 1) * HEAD)
        term = jnp.sum(attg[:, at].astype(F32) * attended[:, at].astype(F32), axis=-1, keepdims=True)
        deltas = jnp.where(lane_h == h, term, deltas)
    delta[...] = deltas.T
    for g in range(heads_kv):
        kt[g] = kv[:, g * HEAD : (g + 1) * HEAD].astype(F32).T.astype(BF16)

    cosine, sine = trig[0], trig[1]

    def unrotate(w):
        return w * cosine - pltpu.roll(w, half_head, 1) * sine

    def head(g, h):
        at = lanes(h * HEAD, HEAD)
        k_at = slice(g * HEAD, (g + 1) * HEAD)
        v_at = slice((heads_kv + g) * HEAD, (heads_kv + g + 1) * HEAD)
        q, a = queries[:, at], attg[:, at]
        soft = jnp.exp(dot_nt(kv[:, k_at], q) + mask[...] - lse[pl.ds(h, 1), :])
        prob = dot_nt(kv[:, v_at], a)
        score = (soft * (prob - delta[pl.ds(h, 1), :])).astype(BF16)
        mixed[:, at] = (unrotate(dot(kt[g], score).T) * HEAD**-0.5).astype(BF16)
        dk[...] += dot(score, q)
        dv[...] += dot(soft.astype(BF16), a)

    def heads(g, first, count):
        @pl.loop(first, first + count)
        def _(h):
            head(g, h)

    def clear():
        dk[...] = jnp.zeros(dk.shape, F32)
        dv[...] = jnp.zeros(dv.shape, F32)

    flip_c = lax.rem(c + 2, ctx)
    near_c = c + 1 - 2 * k
    across_c = lax.rem(near_c + 2, ctx)

    def kv_copy(g, src, i, dev):
        return remote(src, kvr.at[g, i], kv_s.at[g, i], kv_r.at[g, i], dev)

    def send_kv(g):
        for cc in range(ctx):
            rows = slice(cc * tok, (cc + 1) * tok)
            kvs[g, cc, :, :HEAD] = dk[rows, :].astype(BF16)
            kvs[g, cc, :, HEAD:] = dv[rows, :].astype(BF16)
        kv_copy(g, kvs.at[g, across_c], 1, spot.kp).start()
        kv_copy(g, kvs.at[g, near_c], 0, spot.kp).start()

    def pass_kv(g):
        kv_copy(g, kvs.at[g, across_c], 1, spot.kp).wait_recv()
        kvs[g, flip_c] = plus(kvs[g, flip_c], kvr[g, 1])
        kv_copy(g, kvs.at[g, flip_c], 2, spot.yp).start()

    clear()
    heads(0, 0, 2)
    one.step(2)
    heads(0, 2, 4)
    send_kv(0)
    clear()
    proj_plane.turn()
    proj_plane.given()
    qkv_tiles(early_plane, pl.ds(0, half_wide))
    heads(1, 6, 1)
    start_plane(early_plane, pl.ds(0, half_wide))
    pass_kv(0)
    one.step(3)
    two.step(1)
    heads(1, 7, 2)
    heads(1, 9, 3)
    send_kv(1)
    pass_kv(1)
    early_plane.turn()
    for rows, terms in proj_plane.total():
        out_red[rows, :] = summed(terms).astype(BF16)
    proj_line.step(1)
    proj_plane.done()
    for g in range(heads_kv):
        kv_copy(g, kvs.at[g, near_c], 0, spot.kp).wait_recv()
        kv_copy(g, kvs.at[g, flip_c], 2, spot.yp).wait_recv()
        own = kvs[g, c].astype(F32) + kvr[g, 0].astype(F32) + kvr[g, 2].astype(F32)
        at = width + g * HEAD
        mixed[:, at : at + HEAD] = unrotate(own[:, :HEAD]).astype(BF16)
        at = width + (heads_kv + g) * HEAD
        mixed[:, at : at + HEAD] = own[:, HEAD:].astype(BF16)

    qkv_tiles(late_plane, pl.ds(half_wide, half_wide))
    start_plane(late_plane, pl.ds(half_wide, half_wide))
    proj_line.step(2)
    wqkv_load.wait()

    @pl.loop(0, width // step)
    def _(n):
        at = lanes(n * step, step)
        wide_f[:, at] = dot_nt(mixed[...], weights[at, :])

    two.step(2)
    hidden_load.wait()
    x = low[...].astype(F32)
    inv = lax.rsqrt(jnp.mean(x * x, axis=-1, keepdims=True) + NORM_EPS)
    plain = x * inv
    ng = wide_f[...]
    gain_row = jnp.sum(ng * plain, axis=0, keepdims=True)
    scaled = ng * gain_one[...]
    input_grad[...] = (
        back[...] + inv * (scaled - plain * jnp.mean(scaled * plain, axis=-1, keepdims=True))
    ).astype(BF16)
    lane = lax.broadcasted_iota(jnp.int32, (width, HEAD), 1)
    gain_col = jnp.broadcast_to(gain_row, (HEAD, width)).T
    smalls[...] = jnp.where(lane == HEAD - 1, gain_col, smalls[...].astype(F32)).astype(BF16)
    for q in (3, 1, 2, 0):
        at = lanes(spot.chips[q] * block, 2 * block)
        bsend[q, :, :kv_wide] = dot_tn(normed[:, at], mixed[:, width:]).astype(BF16)
        bsend[q, :, kv_wide:] = smalls[rows_at(spot.chips[q] * block, 2 * block), :]
        rest_plane.give(q, bsend.at[q, theirs])
    rest_plane.fold(3, bsend[3, mine])
    rest_plane.across()
    rest_plane.fold(1, bsend[1, mine])
    rest_plane.fold(2, bsend[2, mine])
    rest_plane.near()
    rest_plane.fold(0, bsend[0, mine])
    late_plane.turn()
    rest_plane.turn()
    two.step(3)
    one.final()
    proj_line.step(3)
    for rows, terms in early_plane.total():
        total[rows, :half_wide] = summed(terms).astype(BF16)
    for rows, terms in late_plane.total():
        total[rows, half_wide:width] = summed(terms).astype(BF16)
    for rows, terms in rest_plane.total():
        total[rows, width:] = summed(terms).astype(BF16)
    qkv_line.step(1)
    one.done(one_out)
    qkv_line.step(2)
    two.final()
    proj_line.final(lambda *came: put_shared(proj_out, out_red, came))
    qkv_line.step(3)
    proj_line.done()
    early_plane.done()
    late_plane.done()
    rest_plane.done()
    for g in range(heads_kv):
        kv_copy(g, kvs.at[g, near_c], 0, spot.kp).wait_send()
        kv_copy(g, kvs.at[g, across_c], 1, spot.kp).wait_send()
        kv_copy(g, kvs.at[g, flip_c], 2, spot.yp).wait_send()
    qkv_line.final(lambda *came: put_shared(qkv_out, total, came))
    qkv_line.done()
    for n in range(1, ctx):
        cc = lax.rem(c + ctx - n, ctx)
        got = remote(ffn_out.at[cc], ffn_out.at[cc], f_s.at[n - 1], f_r.at[n - 1], spot.kp)
        got.wait_recv()
        got.wait_send()
    two.done(two_out)


def run_back(
    span, meta, gg, lse, trig, kv, queries, attended, normed, router_t, gain_two, gain_one,
    reduced, resid, cot, pg, ffn_in, hidden, wout, wqkv, gwin,
):
    tok, width = attended.shape
    seq, kv_cols = kv.shape
    planes = meta.shape[0]
    ctx, parts, rows, wide = gwin.shape
    cols = wide // 2
    block = width // planes
    piece = block // parts
    rest = kv_cols + HEAD
    vm, anyspace = pl.BlockSpec(memory_space=pltpu.VMEM), pl.BlockSpec(memory_space=pl.ANY)
    sm = pl.BlockSpec(memory_space=pltpu.SMEM)
    shape = jax.ShapeDtypeStruct
    dma = pltpu.SemaphoreType.DMA
    return pl.pallas_call(
        back_kernel,
        out_shape=(
            shape((tok, width), BF16),
            shape((piece, width + rest), BF16),
            shape((piece, width), BF16),
            shape((ctx, rows, cols), BF16),
            shape((ctx, rows, cols), BF16),
            shape(reduced.shape, BF16),
        ),
        in_specs=[sm] + [vm] * 12 + [anyspace] * 8,
        out_specs=(vm,) * 6,
        scratch_shapes=[
            pltpu.VMEM((tok, width), F32),
            pltpu.VMEM((tok, width), F32),
            pltpu.VMEM((tok, width), BF16),
            pltpu.VMEM((tok, width), BF16),
            pltpu.VMEM((tok, width + kv_cols), BF16),
            pltpu.VMEM(wqkv.shape, BF16),
            pltpu.VMEM(gwin.shape, BF16),
            pltpu.VMEM((4, 2 * block, width), BF16),
            pltpu.VMEM((4, 2 * block, rest), BF16),
            pltpu.VMEM((width, HEAD), BF16),
            pltpu.VMEM((block, width + rest), BF16),
            pltpu.VMEM((block, width), BF16),
            pltpu.VMEM((seq, tok), F32),
            pltpu.VMEM((HEAD, tok), F32),
            pltpu.VMEM((KV_HEADS, HEAD, seq), BF16),
            pltpu.VMEM((seq, HEAD), F32),
            pltpu.VMEM((seq, HEAD), F32),
            pltpu.VMEM((KV_HEADS, ctx, tok, 2 * HEAD), BF16),
            pltpu.VMEM((KV_HEADS, 3, tok, 2 * HEAD), BF16),
            dma((6,)),
            dma((KV_HEADS, 3)),
            dma((KV_HEADS, 3)),
        ]
        + plane_scratch(block, width, BACK_LOW)
        + plane_scratch(block, width // 2, BACK_LOW)[2:]
        + plane_scratch(block, width // 2, BACK_LOW)
        + plane_scratch(block, rest, BACK_LOW)
        + line_scratch(parts, (piece, width + rest))
        + line_scratch(parts, (piece, width))
        + expert_scratch(ctx, parts, rows, cols)
        + expert_scratch(ctx, parts, rows, cols)
        + [dma((ctx - 1,)), dma((ctx - 1,))],
        compiler_params=pltpu.CompilerParams(
            collective_id=2, has_side_effects=True, vmem_limit_bytes=63 * 2**20
        ),
        cost_estimate=pl.CostEstimate(flops=12 * 10**9, bytes_accessed=60 * 10**6, transcendentals=4 * 10**6),
    )(
        span, meta, gg, lse, trig, kv, queries, attended, normed, router_t, gain_two, gain_one,
        reduced, resid, cot, pg, ffn_in, hidden, wout, wqkv, gwin,
    )


def finish_kernel(
    n_experts,
    output_h,
    input_h,
    qkv_h,
    proj_h,
    one_h,
    two_h,
    down_h,
    output,
    input_grad,
    gain_one,
    gain_two,
    qkv,
    proj,
    router,
    inner,
    down,
    low_qkv,
    low_proj,
    low_one,
    low_two,
    low_down,
    low_out,
    low_in,
    inner_full,
    down_full,
    sem,
    out_sem,
):
    whole = []
    loads = [
        pltpu.make_async_copy(src, dst, sem.at[i])
        for i, (src, dst) in enumerate(
            (
                (down_h, low_down),
                (one_h, low_one),
                (two_h, low_two),
                (qkv_h, low_qkv),
                (proj_h, low_proj),
                (output_h, low_out),
                (input_h, low_in),
            )
        )
    ]
    for copy in loads:
        copy.start()
    loads[0].wait()
    ff = down.shape[2]
    down_full[...] = low_down[:, :, :ff].astype(F32)
    at = low_down.shape[2] - ff
    inner_full[:, :, :at] = low_down[:, :, ff:].astype(F32)
    whole.append(pltpu.make_async_copy(down_full, down, out_sem.at[2]))
    whole[-1].start()
    for load, low in zip(loads[1:3], (low_one, low_two)):
        load.wait()
        size = low.shape[2]
        inner_full[:, :, at : at + size] = low[...].astype(F32)
        at += size
    whole.append(pltpu.make_async_copy(inner_full, inner, out_sem.at[3]))
    whole[-1].start()
    for i, (low, to) in enumerate(((low_out, output), (low_in, input_grad))):
        loads[5 + i].wait()
        whole.append(pltpu.make_async_copy(low, to, out_sem.at[i]))
        whole[-1].start()
    for load in loads[3:5]:
        load.wait()
    wide = qkv.shape[1]
    qkv[...] = low_qkv[:, :wide].astype(F32)
    proj[...] = low_proj[...].astype(F32)
    small = low_qkv[:, wide:].astype(F32)
    piece = small.shape[0]
    same = lax.broadcasted_iota(jnp.int32, (piece, piece), 0) == lax.broadcasted_iota(
        jnp.int32, (piece, piece), 1
    )

    def column(at):
        return jnp.sum(jnp.where(same, small[:, at : at + 1], 0.0), axis=0, keepdims=True)

    gain_one[...] = column(HEAD - 1)[0]
    gain_two[...] = column(n_experts)[0]
    for at in range(n_experts):
        router[at : at + 1, :] = column(at)
    for copy in whole:
        copy.wait()


def run_finish(n_experts, output, input_grad, qkv, proj, one, two, down):
    piece, width = proj.shape
    ctx, rows, cols = one.shape
    ff = (down.shape[2] + 2 * cols) // 3
    shape = jax.ShapeDtypeStruct
    vm, anyspace = pl.BlockSpec(memory_space=pltpu.VMEM), pl.BlockSpec(memory_space=pl.ANY)
    return pl.pallas_call(
        functools.partial(finish_kernel, n_experts),
        out_shape=(
            shape(output.shape, BF16),
            shape(input_grad.shape, BF16),
            shape((piece,), F32),
            shape((piece,), F32),
            shape((piece, qkv.shape[1] - HEAD), F32),
            shape((piece, width), F32),
            shape((n_experts, piece), F32),
            shape((ctx, rows, 2 * ff), F32),
            shape((ctx, rows, ff), F32),
        ),
        in_specs=[anyspace] * 7,
        out_specs=(anyspace, anyspace, vm, vm, vm, vm, vm, anyspace, anyspace),
        scratch_shapes=[pltpu.VMEM(x.shape, BF16) for x in (qkv, proj, one, two, down, output, input_grad)]
        + [
            pltpu.VMEM((ctx, rows, 2 * ff), F32),
            pltpu.VMEM((ctx, rows, ff), F32),
            pltpu.SemaphoreType.DMA((7,)),
            pltpu.SemaphoreType.DMA((4,)),
        ],
        compiler_params=pltpu.CompilerParams(vmem_limit_bytes=56 * 2**20),
    )(output, input_grad, qkv, proj, one, two, down)


def local(
    hidden_in,
    span_order,
    expert_ids,
    priority,
    gain_attn,
    qkv_weight,
    out_weight,
    gain_ffn,
    router,
    in_weight,
    down_weight,
    cotangent,
):
    _, tok_rows, width = hidden_in.shape
    ctx, parts = lax.axis_size("context"), lax.axis_size("dp")
    planes = ctx * lax.axis_size("expert")
    n_experts = router.shape[1]
    top_k = expert_ids.shape[2]
    capacity = (9 * tok_rows * top_k + 8 * n_experts - 1) // (8 * n_experts)
    ff = down_weight.shape[2]
    half_freqs = ROPE_BASE ** (np.arange(HEAD // 2) * (-2.0 / HEAD))
    freqs = np.concatenate([half_freqs, half_freqs])[None].astype(np.float32)
    router_t = router.T
    hidden, cot = hidden_in[0], cotangent[0]
    normed, queries, kv, lse, attended, resid, ffn_in, trig, meta, cot_all = run_front(
        capacity,
        span_order,
        hidden,
        cot,
        gain_attn,
        freqs,
        gain_ffn,
        router_t,
        expert_ids[0].T,
        priority[0].T,
        qkv_weight,
        out_weight,
        ctx,
        planes,
    )
    output, pair_sum, gate_grad, gwin, reduced = run_ffn(
        capacity, ffn_in, resid, cot_all, meta, in_weight, down_weight, parts, ff // 3
    )
    input_grad, qkv_sum, proj_sum, in_one, in_two, ffn_sums = run_back(
        span_order,
        meta,
        gate_grad,
        lse,
        trig,
        kv,
        queries,
        attended,
        normed,
        router_t,
        gain_ffn,
        gain_attn,
        reduced,
        resid,
        cot,
        pair_sum,
        ffn_in,
        hidden,
        out_weight,
        qkv_weight,
        gwin,
    )
    output, input_grad, gain_one, gain_two, qkv_grad, proj_grad, router_grad, inner_grad, down_grad = run_finish(
        n_experts, output, input_grad, qkv_sum, proj_sum, in_one, in_two, ffn_sums
    )
    return (
        output[None],
        input_grad[None],
        gain_one,
        qkv_grad,
        proj_grad,
        gain_two,
        router_grad.T,
        inner_grad,
        down_grad,
    )


def general(
    hidden_in,
    span_order,
    expert_ids,
    priority,
    gain_attn,
    qkv_weight,
    out_weight,
    gain_ffn,
    router,
    in_weight,
    down_weight,
    cotangent,
):
    tok_rows = hidden_in.shape[1]
    width = hidden_in.shape[2]
    contexts = lax.axis_size("context")
    span_len = tok_rows // 2
    seq_len = tok_rows * contexts
    group = HEADS // KV_HEADS
    q_cols = HEADS * HEAD
    kv_cols = KV_HEADS * HEAD
    scale = HEAD ** (-0.5)
    local_experts = in_weight.shape[0]
    n_experts = local_experts * lax.axis_size("expert")
    top_k = expert_ids.shape[2]
    capacity = (9 * tok_rows * top_k + 8 * n_experts - 1) // (8 * n_experts)
    ff_width = down_weight.shape[2]
    seq_spans = span_order[0]
    stored = jnp.arange(seq_len) // span_len
    all_pos = (seq_spans[stored] * span_len + jnp.arange(seq_len) % span_len).astype(jnp.float32)
    my_pos = lax.dynamic_slice_in_dim(all_pos, lax.axis_index("context") * tok_rows, tok_rows)
    cosine, sine = rope_tables(my_pos, HEAD)
    inputs = hidden_in[0].astype(jnp.float32)
    inv_one = lax.rsqrt(jnp.mean(inputs * inputs, axis=-1, keepdims=True) + NORM_EPS)
    plain_one = inputs * inv_one
    normed = (plain_one * gain_attn).astype(jnp.bfloat16)
    mixed = jnp.dot(normed, qkv_weight, preferred_element_type=jnp.float32)
    queries = (
        rotate(mixed[:, :q_cols].reshape(tok_rows, HEADS, HEAD), cosine, sine) * scale
    ).astype(jnp.bfloat16)
    keys = rotate(
        mixed[:, q_cols : q_cols + kv_cols].reshape(tok_rows, KV_HEADS, HEAD), cosine, sine
    ).astype(jnp.bfloat16)
    values = mixed[:, q_cols + kv_cols :].reshape(tok_rows, KV_HEADS, HEAD).astype(jnp.bfloat16)
    grouped = queries.reshape(tok_rows, KV_HEADS, group, HEAD)

    def key_scores(key_piece):
        scores = jnp.einsum(
            "qkgd,skd->kgqs", grouped, key_piece, preferred_element_type=jnp.float32
        )
        visible = all_pos[None, None, None, :] <= my_pos[None, None, :, None]
        return (jnp.where(visible, scores, MASKED), visible)

    running = jnp.full((KV_HEADS, group, tok_rows), MASKED, jnp.float32)
    key_piece = lax.all_gather(keys, "context", axis=0, tiled=True)
    value_piece = lax.all_gather(values, "context", axis=0, tiled=True)
    scores, visible = key_scores(key_piece)
    newest = jnp.maximum(running, jnp.max(scores, axis=-1))
    weights = jnp.where(visible, jnp.exp(scores - newest[..., None]), 0.0)
    totals = jnp.sum(weights, axis=-1)
    accum = jnp.einsum(
        "kgqs,skd->kgqd",
        weights.astype(jnp.bfloat16),
        value_piece,
        preferred_element_type=jnp.float32,
    )
    running, totals, accum = (newest, totals, accum)
    log_total = running + jnp.log(totals)
    attended = (
        (accum / totals[..., None])
        .transpose(2, 0, 1, 3)
        .reshape(tok_rows, q_cols)
        .astype(jnp.bfloat16)
    )
    resid = inputs + jnp.einsum(
        "rh,dh->rd", attended, out_weight, preferred_element_type=jnp.float32
    )
    inv_two = lax.rsqrt(jnp.mean(resid * resid, axis=-1, keepdims=True) + NORM_EPS)
    plain_two = resid * inv_two
    ffn_in = (plain_two * gain_ffn).astype(jnp.bfloat16)
    logits = jnp.dot(ffn_in, router, preferred_element_type=jnp.float32)
    token_ids = expert_ids[0]
    gates = softmax_last(jnp.take_along_axis(logits, token_ids, axis=1))
    slots = route(token_ids, priority[0], n_experts, capacity)
    pair_rows = jnp.repeat(ffn_in, top_k, axis=0)
    send_rows = (
        jnp.zeros((n_experts * capacity, width), jnp.bfloat16).at[slots].set(pair_rows, mode="drop")
    )
    received = lax.all_to_all(
        send_rows.reshape(n_experts, capacity, width),
        "expert",
        split_axis=0,
        concat_axis=1,
        tiled=True,
    )
    inner = jnp.einsum("erd,edf->erf", received, in_weight, preferred_element_type=jnp.float32)
    gate_part = inner[..., :ff_width]
    up_part = inner[..., ff_width:]
    sigma = 1.0 / (1.0 + jnp.exp(-gate_part))
    activated = gate_part * sigma
    hidden = (activated * up_part).astype(jnp.bfloat16)
    expert_out = jnp.einsum(
        "erf,edf->erd", hidden, down_weight, preferred_element_type=jnp.float32
    ).astype(jnp.bfloat16)
    returned = lax.all_to_all(
        expert_out, "expert", split_axis=1, concat_axis=0, tiled=True
    ).reshape(n_experts * capacity, width)
    padded = jnp.concatenate([returned, jnp.zeros((1, width), jnp.bfloat16)], axis=0)
    picked = padded[slots].reshape(tok_rows, top_k, width)
    output = (resid + jnp.sum(gates[:, :, None] * picked, axis=1)).astype(jnp.bfloat16)
    cot_low = cotangent[0]
    cot_full = cot_low.astype(jnp.float32)
    gate_grad = jnp.einsum("rkd,rd->rk", picked, cot_low, preferred_element_type=jnp.float32)
    ret_grad = (
        (gates[:, :, None] * cot_full[:, None, :])
        .astype(jnp.bfloat16)
        .reshape(tok_rows * top_k, width)
    )
    send_grad = (
        jnp.zeros((n_experts * capacity, width), jnp.bfloat16).at[slots].set(ret_grad, mode="drop")
    )
    received_grad = lax.all_to_all(
        send_grad.reshape(n_experts, capacity, width),
        "expert",
        split_axis=0,
        concat_axis=1,
        tiled=True,
    )
    hid_grad = jnp.einsum(
        "erd,edf->erf", received_grad, down_weight, preferred_element_type=jnp.float32
    )
    slope = sigma * (1.0 + gate_part * (1.0 - sigma))
    inner_grad = jnp.concatenate(
        [hid_grad * up_part * slope, hid_grad * activated], axis=-1
    ).astype(jnp.bfloat16)
    row_grad = jnp.einsum(
        "erf,edf->erd", inner_grad, in_weight, preferred_element_type=jnp.float32
    ).astype(jnp.bfloat16)
    part_rows = received
    expert_in = (
        lax.psum_scatter(
            jnp.einsum(
                "erd,erf->def", part_rows, inner_grad, preferred_element_type=jnp.float32
            ).astype(jnp.bfloat16),
            ("context", "dp"),
            scatter_dimension=0,
            tiled=True,
        )
        .astype(jnp.float32)
        .transpose(1, 0, 2)
    )
    part_rows = received_grad
    expert_down = (
        lax.psum_scatter(
            jnp.einsum(
                "erd,erf->def", part_rows, hidden, preferred_element_type=jnp.float32
            ).astype(jnp.bfloat16),
            ("context", "dp"),
            scatter_dimension=0,
            tiled=True,
        )
        .astype(jnp.float32)
        .transpose(1, 0, 2)
    )
    back_rows = lax.all_to_all(row_grad, "expert", split_axis=1, concat_axis=0, tiled=True).reshape(
        n_experts * capacity, width
    )
    back_padded = jnp.concatenate([back_rows, jnp.zeros((1, width), jnp.bfloat16)], axis=0)
    pair_grad = back_padded[slots].reshape(tok_rows, top_k, width)
    mix_grad = gates * (gate_grad - jnp.sum(gates * gate_grad, axis=-1, keepdims=True))
    matches = token_ids[:, :, None] == jnp.arange(n_experts)[None, None, :]
    logit_grad = jnp.sum(jnp.where(matches, mix_grad[:, :, None], 0.0), axis=1).astype(jnp.bfloat16)
    router_part = jnp.einsum("rd,re->de", ffn_in, logit_grad, preferred_element_type=jnp.float32)
    ffn_grad = jnp.sum(pair_grad.astype(jnp.float32), axis=1) + jnp.einsum(
        "re,de->rd", logit_grad, router, preferred_element_type=jnp.float32
    )
    gain_ffn_part = jnp.sum(ffn_grad * plain_two, axis=0)
    scaled_two = ffn_grad * gain_ffn
    resid_grad = cot_full + inv_two * (
        scaled_two - plain_two * jnp.mean(scaled_two * plain_two, axis=-1, keepdims=True)
    )
    resid_low = resid_grad.astype(jnp.bfloat16)
    out_part = jnp.einsum("rd,rh->dh", resid_low, attended, preferred_element_type=jnp.float32)
    att_grad = jnp.einsum(
        "rd,dh->rh", resid_low, out_weight, preferred_element_type=jnp.float32
    ).astype(jnp.bfloat16)
    att_heads = att_grad.reshape(tok_rows, KV_HEADS, group, HEAD)
    row_delta = jnp.sum(
        att_heads.astype(jnp.float32)
        * attended.reshape(tok_rows, KV_HEADS, group, HEAD).astype(jnp.float32),
        axis=-1,
    ).transpose(1, 2, 0)
    key_piece = lax.all_gather(keys, "context", axis=0, tiled=True)
    value_piece = lax.all_gather(values, "context", axis=0, tiled=True)
    scores, visible = key_scores(key_piece)
    soft = jnp.exp(scores - log_total[..., None])
    prob_grad = jnp.einsum(
        "qkgd,skd->kgqs", att_heads, value_piece, preferred_element_type=jnp.float32
    )
    score_grad = (soft * (prob_grad - row_delta[..., None])).astype(jnp.bfloat16)
    query_acc = jnp.einsum(
        "kgqs,skd->kgqd", score_grad, key_piece, preferred_element_type=jnp.float32
    )
    key_part = jnp.einsum("kgqs,qkgd->skd", score_grad, grouped, preferred_element_type=jnp.float32)
    value_part = jnp.einsum(
        "kgqs,qkgd->skd", soft.astype(jnp.bfloat16), att_heads, preferred_element_type=jnp.float32
    )
    pair_acc = jnp.stack([key_part, value_part], axis=1)
    query_acc, pair_acc = (query_acc, pair_acc)
    own_pairs = lax.psum_scatter(
        pair_acc.astype(jnp.bfloat16), "context", scatter_dimension=0, tiled=True
    ).astype(jnp.float32)
    query_grad = (
        unrotate(query_acc.transpose(2, 0, 1, 3).reshape(tok_rows, HEADS, HEAD), cosine, sine)
        * scale
    )
    key_grad = unrotate(own_pairs[:, 0], cosine, sine)
    mixed_grad = jnp.concatenate(
        [
            query_grad.reshape(tok_rows, q_cols),
            key_grad.reshape(tok_rows, kv_cols),
            own_pairs[:, 1].reshape(tok_rows, kv_cols),
        ],
        axis=-1,
    ).astype(jnp.bfloat16)
    qkv_part = jnp.einsum("rd,rc->dc", normed, mixed_grad, preferred_element_type=jnp.float32)
    norm_grad = jnp.einsum("rc,dc->rd", mixed_grad, qkv_weight, preferred_element_type=jnp.float32)
    gain_attn_part = jnp.sum(norm_grad * plain_one, axis=0)
    scaled_one = norm_grad * gain_attn
    input_grad = (
        resid_grad
        + inv_one
        * (scaled_one - plain_one * jnp.mean(scaled_one * plain_one, axis=-1, keepdims=True))
    ).astype(jnp.bfloat16)
    gain_attn_grad, qkv_grad, out_proj_grad, gain_ffn_grad, router_grad = (
        lax.psum_scatter(
            gain_attn_part, ("expert", "context", "dp"), scatter_dimension=0, tiled=True
        ),
        lax.psum_scatter(qkv_part, ("expert", "context", "dp"), scatter_dimension=0, tiled=True),
        lax.psum_scatter(out_part, ("expert", "context", "dp"), scatter_dimension=0, tiled=True),
        lax.psum_scatter(
            gain_ffn_part, ("expert", "context", "dp"), scatter_dimension=0, tiled=True
        ),
        lax.psum_scatter(router_part, ("expert", "context", "dp"), scatter_dimension=0, tiled=True),
    )
    return (
        output[None],
        input_grad[None],
        gain_attn_grad,
        qkv_grad,
        out_proj_grad,
        gain_ffn_grad,
        router_grad,
        expert_in,
        expert_down,
    )


def solution(mesh):
    in_specs = (
        P(("expert", "dp"), "context", None),
        P(("expert", "dp"), None),
        P(("expert", "dp"), "context", None),
        P(("expert", "dp"), "context", None),
        P(),
        P(),
        P(),
        P(),
        P(),
        P("expert", None, None),
        P("expert", None, None),
        P(("expert", "dp"), "context", None),
    )
    out_specs = (
        P(("expert", "dp"), "context", None),
        P(("expert", "dp"), "context", None),
        P(("expert", "context", "dp")),
        P(("expert", "context", "dp"), None),
        P(("expert", "context", "dp"), None),
        P(("expert", "context", "dp")),
        P(("expert", "context", "dp"), None),
        P("expert", ("context", "dp"), None),
        P("expert", ("context", "dp"), None),
    )
    tuned = dict(mesh.shape) == {"expert": 2, "context": 4, "dp": 4}
    body = local if tuned else general
    return jax.shard_map(body, mesh=mesh, in_specs=in_specs, out_specs=out_specs, check_vma=False)
```

```python
import functools

import jax
import jax.numpy as jnp
import numpy as np
from jax import lax
from jax.experimental import pallas as pl
from jax.experimental.pallas import tpu as pltpu
from jax.sharding import PartitionSpec as P

HEADS = 12
KV_HEADS = 2
HEAD = 128


ROPE_BASE = 1000000.0
NORM_EPS = 1e-06
MASKED = -1e30


def rope_tables(positions, head_size):
    half_size = head_size // 2
    freqs = ROPE_BASE ** (jnp.arange(half_size).astype(jnp.float32) * (-2.0 / head_size))
    angles = positions[:, None] * freqs[None, :]
    return (jnp.cos(angles)[:, None, :], jnp.sin(angles)[:, None, :])


def rotate(values, cosine, sine):
    half_size = values.shape[-1] // 2
    first = values[..., :half_size]
    second = values[..., half_size:]
    return jnp.concatenate(
        [first * cosine - second * sine, second * cosine + first * sine], axis=-1
    )


def unrotate(values, cosine, sine):
    half_size = values.shape[-1] // 2
    first = values[..., :half_size]
    second = values[..., half_size:]
    return jnp.concatenate(
        [first * cosine + second * sine, second * cosine - first * sine], axis=-1
    )


def softmax_last(scores):
    shifted = jnp.exp(scores - jnp.max(scores, axis=-1, keepdims=True))
    return shifted / jnp.sum(shifted, axis=-1, keepdims=True)


def route(block_ids, block_order, n_experts, capacity):
    flat_ids = block_ids.reshape(-1)
    flat_order = block_order.reshape(-1)
    choose = (flat_ids[:, None] == jnp.arange(n_experts)[None, :]).astype(jnp.int32)
    ordered = jnp.zeros_like(choose).at[flat_order].set(choose)
    earlier = jnp.cumsum(ordered, axis=0, dtype=jnp.int32) - ordered
    ranks = jnp.sum(earlier[flat_order] * choose, axis=1)
    return jnp.where(ranks < capacity, flat_ids * capacity + ranks, n_experts * capacity)


MESH = pl.DeviceIdType.MESH
F32 = jnp.float32
BF16 = jnp.bfloat16
BACK_LOW = 96
OUT_LOW = 128
FRONT_LOW = 96
FRONT_AHEAD = 64


def dot(a, b):
    return jnp.dot(a, b, preferred_element_type=F32)


def dot_nt(a, b):
    return lax.dot_general(a, b, (((1,), (1,)), ((), ())), preferred_element_type=F32)


def dot_tn(a, b):
    return lax.dot_general(a, b, (((0,), (0,)), ((), ())), preferred_element_type=F32)


def plus(a, *more):
    total = a.astype(F32)
    for b in more:
        total = total + b.astype(F32)
    return total.astype(BF16)


def lanes(at, size):
    return pl.ds(pl.multiple_of(at, 128), size)


def rows_at(at, size):
    return pl.ds(pl.multiple_of(at, 16), size)


def remote(src, dst, s, r, dev):
    return pltpu.make_async_remote_copy(
        src_ref=src, dst_ref=dst, send_sem=s, recv_sem=r, device_id=dev, device_id_type=MESH
    )


class Spot:
    def __init__(self):
        e, c, z = lax.axis_index("expert"), lax.axis_index("context"), lax.axis_index("dp")
        self.ctx = lax.axis_size("context")
        self.parts = lax.axis_size("dp")
        self.planes = self.ctx * lax.axis_size("expert")
        y, k = lax.div(c, 2), lax.rem(c, 2)
        self.e, self.c, self.z, self.k = e, c, z, k
        self.me = e * self.ctx + c
        self.xp, self.yp = (1 - e, c, z), (e, (1 - y) * 2 + k, z)
        self.kp, self.yk = (e, y * 2 + 1 - k, z), (e, (1 - y) * 2 + 1 - k, z)
        self.chips = [
            eq * self.ctx + yq * 2 for eq, yq in ((e, y), (1 - e, y), (e, 1 - y), (1 - e, 1 - y))
        ]

    def others(self):
        found = []
        for step in range(1, self.planes):
            other = lax.rem(self.me + step, self.planes)
            found.append((other, (lax.div(other, self.ctx), lax.rem(other, self.ctx), self.z)))
        return found

    def along(self):
        e, c, z = self.e, self.c, self.z
        return [(z < self.parts - 1, (e, c, z + 1)), (z > 0, (e, c, z - 1))]


def greet(peers, extra=()):
    barrier = pltpu.get_barrier_semaphore()
    for peer in peers:
        pl.semaphore_signal(barrier, inc=1, device_id=peer, device_id_type=MESH)
    for there, peer in extra:

        @pl.when(there)
        def _():
            pl.semaphore_signal(barrier, inc=1, device_id=peer, device_id_type=MESH)

    count = len(peers)
    for there, _ in extra:
        count = count + there.astype(jnp.int32)
    pl.semaphore_wait(barrier, count)


class Plane:
    def __init__(self, spot, zcr, zk, rx, ry, s, r, zcr_there=None, low=None):
        self.zcr_there = zcr_there or zcr
        self.spot, self.zcr, self.zk, self.rx, self.ry, self.s, self.r = spot, zcr, zk, rx, ry, s, r
        low = low or zk[0].shape[0] // 2
        self.lo, self.hi = pl.ds(0, low), pl.ds(low, zk[0].shape[0] - low)
        self.sent, self.gives = [], []

    def push(self, src, dst, i, dev):
        copy = remote(src, dst, self.s.at[i], self.r.at[i], dev)
        copy.start()
        self.sent.append(copy)

    def arrive(self, dst, i):
        remote(dst, dst, self.s.at[i], self.r.at[i], self.spot.kp).wait_recv()

    def given(self):
        for copy in self.gives:
            copy.wait_send()
        self.gives = []

    def give(self, q, src):
        self.gives.append(remote(src, self.zcr_there[q], self.s.at[q], self.r.at[q], self.spot.kp))
        self.gives[-1].start()

    def fold(self, q, own=None):
        self.arrive(self.zcr[q], q)
        self.zk[q][...] = plus(self.zk[q][...] if own is None else own, self.zcr[q][...])

    def near(self):
        self.push(self.zk[1].at[self.lo], self.rx[1], 5, self.spot.xp)
        self.push(self.zk[2].at[self.hi], self.ry[1], 8, self.spot.yp)

    def across(self):
        self.push(self.zk[3].at[self.lo], self.rx[0], 4, self.spot.xp)
        self.push(self.zk[3].at[self.hi], self.ry[0], 7, self.spot.yp)

    def turn(self):
        lo, hi = self.lo, self.hi
        self.arrive(self.rx[0], 4)
        self.zk[2][lo] = plus(self.zk[2][lo], self.rx[0][...])
        self.push(self.zk[2].at[lo], self.ry[2], 9, self.spot.yp)
        self.arrive(self.ry[0], 7)
        self.zk[1][hi] = plus(self.zk[1][hi], self.ry[0][...])
        self.push(self.zk[1].at[hi], self.rx[2], 6, self.spot.xp)

    def total(self):
        self.arrive(self.rx[1], 5)
        self.arrive(self.ry[1], 8)
        self.arrive(self.rx[2], 6)
        self.arrive(self.ry[2], 9)
        return (
            (self.lo, (self.zk[0][self.lo], self.rx[1][...], self.ry[2][...])),
            (self.hi, (self.zk[0][self.hi], self.rx[2][...], self.ry[1][...])),
        )

    def done(self):
        self.given()
        for copy in self.sent:
            copy.wait_send()


def plane_of(spot, zcr, zk, rx, ry, s, r, low=None):
    four, block = range(4), zk.shape[1]
    lo, hi = pl.ds(0, low or block // 2), pl.ds(0, block - (low or block // 2))
    return Plane(
        spot,
        [zcr.at[q] for q in four],
        [zk.at[q] for q in four],
        [rx.at[0, lo], rx.at[1, lo], rx.at[2, hi]],
        [ry.at[0, hi], ry.at[1, hi], ry.at[2, lo]],
        s,
        r,
        low=low,
    )


def plane_scratch(block, wide, low=None):
    most = max(low or block // 2, block - (low or block // 2))
    return [
        pltpu.VMEM((4, block, wide), BF16),
        pltpu.VMEM((4, block, wide), BF16),
        pltpu.VMEM((3, most, wide), BF16),
        pltpu.VMEM((3, most, wide), BF16),
        pltpu.SemaphoreType.DMA((10,)),
        pltpu.SemaphoreType.DMA((10,)),
    ]


def summed(terms):
    total = terms[0].astype(F32)
    for term in terms[1:]:
        total = total + term.astype(F32)
    return total


class Line:
    def __init__(self, spot, own, adder, buf, s, r):
        z, last = spot.z, spot.parts - 1
        e, c = spot.e, spot.c
        self.own, self.adder, self.buf, self.s, self.r = own, adder, buf, s, r
        self.z, self.last, self.parts = z, last, spot.parts
        self.ways = [(z, (e, c, z + 1), lambda d: d), (last - z, (e, c, z - 1), lambda d: last - d)]

    def step(self, turn):
        for way, (i, dev, part) in enumerate(self.ways):
            to, s, r = self.buf.at[way, turn - 1], self.s.at[way, turn - 1], self.r.at[way, turn - 1]

            @pl.when(i == 0)
            def _():
                remote(self.own(part(self.parts - turn)), to, s, r, dev).start()

            if turn >= 2:
                came, s_came, r_came = (x.at[way, turn - 2] for x in (self.buf, self.s, self.r))

                @pl.when((i >= 1) & (i <= turn - 1) & (i < self.last))
                def _():
                    remote(came, came, s_came, r_came, dev).wait_recv()
                    self.adder(came, part(self.parts - turn + i))
                    remote(came, to, s, r, dev).start()

    def final(self, put):
        last, z = self.last, self.z
        for way, (i, dev, _) in enumerate(self.ways):
            came = self.buf.at[way, last - 1]

            @pl.when(i >= 1)
            def _():
                remote(came, came, self.s.at[way, last - 1], self.r.at[way, last - 1], dev).wait_recv()

        up, down = self.buf.at[0, last - 1], self.buf.at[1, last - 1]
        pl.when(z == 0)(lambda: put(down))
        pl.when(z == last)(lambda: put(up))
        pl.when((z > 0) & (z < last))(lambda: put(up, down))

    def done(self):
        for way, (i, dev, _) in enumerate(self.ways):
            for turn in range(1, self.parts):
                came = self.buf.at[way, turn - 1]

                @pl.when((i <= turn - 1) & (i < self.last))
                def _():
                    remote(came, came, self.s.at[way, turn - 1], self.r.at[way, turn - 1], dev).wait_send()


def line_scratch(parts, piece):
    return [
        pltpu.VMEM((2, parts - 1) + piece, BF16),
        pltpu.SemaphoreType.DMA((2, parts - 1)),
        pltpu.SemaphoreType.DMA((2, parts - 1)),
    ]


class ExpertLine:
    def __init__(self, spot, ref, at, cols, buf, s, r, fin, spread=None, a_s=None, a_r=None):
        self.spot, self.ref, self.at, self.cols = spot, ref, at, cols
        self.fin, self.spread, self.a_s, self.a_r = fin, spread, a_s, a_r
        self.line = Line(spot, self.own, self.adder, buf, s, r)
        self.step = self.line.step

    def own(self, d):
        return self.ref.at[:, d, :, pl.ds(self.at, self.cols)]

    def piece(self, cc, d):
        return self.ref[cc, d, :, self.at : self.at + self.cols]

    def adder(self, came, d):
        for cc in range(self.spot.ctx):
            came[cc] = plus(came[cc], self.piece(cc, d))

    def final(self):
        spot = self.spot

        def put(*came):
            for cc in range(spot.ctx):
                self.fin[cc] = plus(self.piece(cc, spot.z), *(x[cc] for x in came))

        self.line.final(put)
        if self.spread is None:
            return
        for step in range(1, spot.ctx):
            cc = lax.rem(spot.c + step, spot.ctx)
            remote(
                self.fin.at[cc],
                self.spread.at[spot.c],
                self.a_s.at[step - 1],
                self.a_r.at[step - 1],
                (spot.e, cc, spot.z),
            ).start()

    def done(self, out=None):
        spot = self.spot
        if self.spread is None:
            self.line.done()
            return
        for step in range(1, spot.ctx):
            cc = lax.rem(spot.c + spot.ctx - step, spot.ctx)
            got = remote(
                self.spread.at[cc],
                self.spread.at[cc],
                self.a_s.at[step - 1],
                self.a_r.at[step - 1],
                (spot.e, cc, spot.z),
            )
            got.wait_recv()
            got.wait_send()
            out[cc] = self.spread[cc]
        out[spot.c] = self.fin[spot.c]
        self.line.done()


def expert_scratch(ctx, parts, rows, cols):
    return line_scratch(parts, (ctx, rows, cols)) + [
        pltpu.VMEM((ctx, rows, cols), BF16),
        pltpu.VMEM((ctx, rows, cols), BF16),
        pltpu.SemaphoreType.DMA((ctx - 1,)),
        pltpu.SemaphoreType.DMA((ctx - 1,)),
    ]


class Gather:
    def __init__(self, spot, own, buf, s, r, low=None, ahead=0):
        self.spot, self.own, self.buf, self.s, self.r = spot, own, buf, s, r
        low = low or own.shape[0] // 2
        self.lo, self.hi = pl.ds(0, low), pl.ds(low, own.shape[0] - low)
        self.ahead, self.rest = ahead and pl.ds(low, ahead), pl.ds(low + ahead, own.shape[0] - low - ahead)
        self.x_me, self.y_me, self.d_me = (base + spot.k for base in spot.chips[1:])
        self.side = 1 - 2 * spot.k
        self.sent = []

    def push(self, src, dst, i, dev):
        copy = remote(src, dst, self.s.at[i], self.r.at[i], dev)
        copy.start()
        self.sent.append(copy)

    def move(self, p, rows, i, dev):
        self.push(self.buf.at[p, rows], self.buf.at[p, rows], i, dev)

    def got(self, p, rows, i):
        to = self.buf.at[p, rows]
        remote(to, to, self.s.at[i], self.r.at[i], self.spot.kp).wait_recv()

    def start(self):
        me, own, lo, hi = self.spot.me, self.own, self.lo, self.hi
        self.push(own.at[lo], self.buf.at[me, lo], 0, self.spot.xp)
        if self.ahead:
            self.push(own.at[self.ahead], self.buf.at[me, self.ahead], 14, self.spot.yp)
        self.push(own.at[lo], self.buf.at[me, lo], 6, self.spot.kp)
        self.push(own.at[hi], self.buf.at[me, hi], 13, self.spot.kp)
        self.push(own.at[hi], self.buf.at[me, hi], 1, self.spot.xp)

    def start_y(self):
        me, own, lo, rest = self.spot.me, self.own, self.lo, self.rest
        self.push(own.at[rest], self.buf.at[me, rest], 3, self.spot.yp)
        self.push(own.at[lo], self.buf.at[me, lo], 2, self.spot.yp)

    def first(self):
        spot = self.spot
        self.got(self.x_me, self.lo, 0)
        self.move(self.x_me, self.lo, 4, spot.yp)
        self.move(self.x_me, self.lo, 7, spot.kp)
        if self.ahead:
            self.got(self.y_me, self.ahead, 14)
        self.got(self.y_me, self.rest, 3)
        self.move(self.y_me, self.hi, 5, spot.xp)
        self.move(self.y_me, self.hi, 10, spot.kp)

    def second(self):
        self.got(self.x_me, self.hi, 1)
        self.move(self.x_me, self.hi, 8, self.spot.kp)
        self.got(self.y_me, self.lo, 2)
        self.move(self.y_me, self.lo, 9, self.spot.kp)

    def third(self):
        self.got(self.d_me, self.lo, 4)
        self.move(self.d_me, self.lo, 11, self.spot.kp)
        self.got(self.d_me, self.hi, 5)
        self.move(self.d_me, self.hi, 12, self.spot.kp)

    def other_core(self, q):
        low_sem, high_sem = ((6, 13), (7, 8), (9, 10), (11, 12))[q]
        p = (self.spot.me, self.x_me, self.y_me, self.d_me)[q] + self.side
        self.got(p, self.lo, low_sem)
        self.got(p, self.hi, high_sem)

    def done(self):
        for copy in self.sent:
            copy.wait_send()


GATHER_COPIES = 15


def front_kernel(
    cap,
    span,
    hidden,
    cot,
    gain_one,
    freqs,
    gain_two,
    router_t,
    ids_t,
    turn_t,
    wqkv_h,
    wout_h,
    normed_h,
    queries_h,
    kv_h,
    lse,
    attended,
    resid,
    ffn_in,
    trig,
    meta,
    cot_all,
    wqkv,
    wout,
    mask,
    vt,
    normed,
    queries,
    kv,
    load_sem,
    out_sem,
    kv_s,
    kv_r,
    co_s,
    co_r,
):
    spot = Spot()
    c, ctx, k = spot.c, spot.ctx, spot.k
    tok, width = hidden.shape
    group = HEADS // KV_HEADS
    kv_cols = KV_HEADS * HEAD
    half_head = HEAD // 2
    seq = kv.shape[0]
    spans = span.shape[1]
    size = seq // spans
    mine = spans // ctx
    n_experts = meta.shape[0]
    loads = [
        pltpu.make_async_copy(wqkv_h.at[:, pl.ds(width, 2 * kv_cols)], wqkv.at[:, pl.ds(width, 2 * kv_cols)], load_sem.at[0]),
        pltpu.make_async_copy(wqkv_h.at[:, pl.ds(0, width)], wqkv.at[:, pl.ds(0, width)], load_sem.at[1]),
        pltpu.make_async_copy(wout_h, wout, load_sem.at[2]),
        pltpu.make_async_copy(cot, cot_all.at[spot.me], load_sem.at[3]),
    ]
    for load in loads:
        load.start()
    greet([spot.xp, spot.yp, spot.kp])
    gather = Gather(spot, cot, cot_all, co_s, co_r, low=FRONT_LOW, ahead=FRONT_AHEAD)
    gather.start()

    x = hidden[...].astype(F32)
    inv = lax.rsqrt(jnp.mean(x * x, axis=-1, keepdims=True) + NORM_EPS)
    normed[...] = (x * inv * gain_one[...]).astype(BF16)

    along = lax.broadcasted_iota(jnp.int32, (tok, HEAD), 0)
    start_one, start_two = span[0, c * mine] * size, (span[0, c * mine + 1] - 1) * size
    place = jnp.where(along < size, start_one, start_two) + along
    angle = place.astype(F32) * freqs[...]
    cosine, sine = jnp.cos(angle), jnp.sin(angle)
    lane = lax.broadcasted_iota(jnp.int32, (tok, HEAD), 1)
    sine = jnp.where(lane < half_head, -sine, sine)
    trig[0] = cosine
    trig[1] = sine

    def rotate_in(w):
        return w * cosine + pltpu.roll(w, half_head, 1) * sine

    loads[0].wait()
    raw = dot(normed[...], wqkv[:, width:])
    own = rows_at(c * tok, tok)
    for g in range(KV_HEADS):
        at = slice(g * HEAD, (g + 1) * HEAD)
        kv[own, at] = rotate_in(raw[:, at]).astype(BF16)
    kv[own, kv_cols:] = raw[:, kv_cols:].astype(BF16)

    def kv_copy(rows, i, dev):
        return remote(kv.at[rows], kv.at[rows], kv_s.at[i], kv_r.at[i], dev)

    flip_c = lax.rem(c + 2, ctx)
    near_c = c + 1 - 2 * k
    across_c = lax.rem(near_c + 2, ctx)
    sent = [kv_copy(own, 1, spot.yp), kv_copy(own, 0, spot.kp)]
    for copy in sent:
        copy.start()
    gather.start_y()

    outs = [pltpu.make_async_copy(normed, normed_h, out_sem.at[0])]
    outs[0].start()
    loads[1].wait()
    step = 256

    @pl.loop(0, width // step)
    def _(n):
        at = lanes(n * step, step)
        raw = dot(normed[...], wqkv[:, at])
        for i in range(step // HEAD):
            w = raw[:, i * HEAD : (i + 1) * HEAD]
            queries[:, lanes(n * step + i * HEAD, HEAD)] = (rotate_in(w) * HEAD**-0.5).astype(BF16)

    outs.append(pltpu.make_async_copy(queries, queries_h, out_sem.at[1]))
    outs[1].start()

    flip = rows_at(flip_c * tok, tok)
    kv_copy(flip, 1, spot.kp).wait_recv()
    sent.append(kv_copy(flip, 2, spot.kp))
    sent[-1].start()

    expert = lax.broadcasted_iota(jnp.int32, (n_experts, tok), 0)
    never = tok * ids_t.shape[0]
    turn = jnp.full((n_experts, tok), never, jnp.int32)
    for i in range(ids_t.shape[0]):
        turn = jnp.where(ids_t[i : i + 1, :] == expert, turn_t[i : i + 1, :], turn)
    turn_f = turn.astype(F32)
    tall = jnp.concatenate([turn_f, jnp.full((HEAD - n_experts, tok), float(never), F32)], axis=0).T
    meta[...] = jnp.zeros(meta.shape, F32)
    for g in range(n_experts):
        row = turn_f[g : g + 1, :]
        rank = jnp.sum(jnp.where(tall[:, g : g + 1] < row, 1.0, 0.0), axis=0, keepdims=True)
        meta[g, 0:1, :] = jnp.where((row < never) & (rank < cap), rank, -1.0)

    along_q = lax.broadcasted_iota(jnp.int32, (size, tok), 1)
    q_pos = jnp.where(along_q < size, start_one, start_two) + along_q
    for s in range(spans):
        k_pos = span[0, s] * size + lax.broadcasted_iota(jnp.int32, (size, tok), 0)
        mask[s * size : (s + 1) * size, :] = jnp.where(k_pos <= q_pos, 0.0, MASKED)

    near, across = rows_at(near_c * tok, tok), rows_at(across_c * tok, tok)
    kv_copy(near, 0, spot.kp).wait_recv()
    kv_copy(across, 2, spot.kp).wait_recv()
    outs.append(pltpu.make_async_copy(kv, kv_h, out_sem.at[2]))
    outs[2].start()
    for g in range(KV_HEADS):
        vt[g] = kv[:, kv_cols + g * HEAD : kv_cols + (g + 1) * HEAD].astype(F32).T.astype(BF16)
    lse[...] = jnp.zeros(lse.shape, F32)

    def heads(g, first, count):
        @pl.loop(first, first + count)
        def _(h):
            at = lanes(h * HEAD, HEAD)
            scores = dot_nt(kv[:, g * HEAD : (g + 1) * HEAD], queries[:, at]) + mask[...]
            top = jnp.max(scores, axis=0, keepdims=True)
            weights = jnp.exp(scores - top)
            total = jnp.sum(weights, axis=0, keepdims=True)
            lse[pl.ds(h, 1), :] = top + jnp.log(total)
            out = dot(vt[g], weights.astype(BF16)) / total
            attended[:, at] = out.T.astype(BF16)

    heads(0, 0, 3)
    gather.first()
    heads(0, 3, 3)
    heads(1, 6, 3)
    gather.second()
    heads(1, 9, 3)

    loads[2].wait()

    @pl.loop(0, width // step)
    def _(n):
        at = lanes(n * step, step)
        resid[:, at] = hidden[:, at].astype(F32) + dot_nt(attended[...], wout[at, :])

    r = resid[...]
    inv = lax.rsqrt(jnp.mean(r * r, axis=-1, keepdims=True) + NORM_EPS)
    ffn_in[...] = (r * inv * gain_two[...]).astype(BF16)
    logits = dot_nt(router_t[...], ffn_in[...])[:n_experts]
    logits = jnp.where(turn < never, logits, MASKED)
    shifted = jnp.exp(logits - jnp.max(logits, axis=0, keepdims=True))
    gates = shifted / jnp.sum(shifted, axis=0, keepdims=True)
    for g in range(n_experts):
        meta[g, 1:2, :] = gates[g : g + 1, :]
    gather.third()
    for q in range(4):
        gather.other_core(q)
    loads[3].wait()
    gather.done()
    for copy in outs:
        copy.wait()
    for copy in sent:
        copy.wait_send()


def run_front(cap, span, hidden, cot, gain_one, freqs, gain_two, router_t, ids_t, turn_t, wqkv, wout, ctx, planes):
    tok, width = hidden.shape
    seq = tok * ctx
    n_experts = planes
    kv_cols = 2 * KV_HEADS * HEAD
    vm, anyspace = pl.BlockSpec(memory_space=pltpu.VMEM), pl.BlockSpec(memory_space=pl.ANY)
    sm = pl.BlockSpec(memory_space=pltpu.SMEM)
    shape = jax.ShapeDtypeStruct
    dma = pltpu.SemaphoreType.DMA
    return pl.pallas_call(
        functools.partial(front_kernel, cap),
        out_shape=(
            shape((tok, width), BF16),
            shape((tok, width), BF16),
            shape((seq, kv_cols), BF16),
            shape((16, tok), F32),
            shape((tok, width), BF16),
            shape((tok, width), F32),
            shape((tok, width), BF16),
            shape((2, tok, HEAD), F32),
            shape((n_experts, 8, tok), F32),
            shape((planes, tok, width), BF16),
        ),
        in_specs=[sm] + [vm] * 8 + [anyspace] * 2,
        out_specs=(anyspace,) * 3 + (vm,) * 6 + (anyspace,),
        scratch_shapes=[
            pltpu.VMEM(wqkv.shape, BF16),
            pltpu.VMEM(wout.shape, BF16),
            pltpu.VMEM((seq, tok), F32),
            pltpu.VMEM((KV_HEADS, HEAD, seq), BF16),
            pltpu.VMEM((tok, width), BF16),
            pltpu.VMEM((tok, width), BF16),
            pltpu.VMEM((seq, kv_cols), BF16),
            dma((4,)),
            dma((3,)),
            dma((3,)),
            dma((3,)),
            dma((GATHER_COPIES,)),
            dma((GATHER_COPIES,)),
        ],
        compiler_params=pltpu.CompilerParams(
            collective_id=4, has_side_effects=True, vmem_limit_bytes=56 * 2**20
        ),
        cost_estimate=pl.CostEstimate(flops=5 * 10**9, bytes_accessed=20 * 10**6, transcendentals=4 * 10**6),
    )(span, hidden, cot, gain_one, freqs, gain_two, router_t, ids_t, turn_t, wqkv, wout)


def ffn_kernel(cap, ffn_h, resid_h, cot_h, meta, win_h, wdn_h, output, pg_out, gg_out, gwin_h, ex_out, *scratch):
    agb, metas, cotb, win, wdn, xs, ds, hid, igs, pgs, ggs, ggr, wint, gwdn = scratch[:14]
    load_sem, ag_s, ag_r, me_s, me_r, gg_s, gg_r, out_s, out_r = scratch[14:23]
    plane_refs, line_refs, first_refs = scratch[23:29], scratch[29:32], scratch[32:]
    spot = Spot()
    c, k, me = spot.c, spot.k, spot.me
    kp = spot.kp
    tok, width = output.shape
    ff = wdn.shape[1]
    planes, ctx = spot.planes, spot.ctx
    chips = spot.chips

    loads = [
        pltpu.make_async_copy(win_h.at[c], win, load_sem.at[0]),
        pltpu.make_async_copy(wdn_h.at[c], wdn, load_sem.at[1]),
        pltpu.make_async_copy(cot_h, cotb, load_sem.at[2]),
        pltpu.make_async_copy(resid_h, pg_out, load_sem.at[3]),
    ]
    own_load = pltpu.make_async_copy(ffn_h, agb.at[me], load_sem.at[4])
    own_load.start()
    others = spot.others()
    greet([dev for _, dev in others], spot.along())
    plane = plane_of(spot, *plane_refs)
    o_lo, o_hi = pl.ds(0, OUT_LOW), pl.ds(OUT_LOW, tok - OUT_LOW)
    outs = Plane(
        spot,
        [agb.at[2 * i + k] for i in range(4)],
        [cotb.at[base + k] for base in chips],
        [agb.at[1 - k, o_lo], agb.at[3 - k, o_lo], agb.at[1 - k, o_hi]],
        [agb.at[3 - k, o_hi], agb.at[5 - k, o_hi], agb.at[5 - k, o_lo]],
        out_s,
        out_r,
        [agb.at[2 * i + 1 - k] for i in range(4)],
        low=OUT_LOW,
    )
    line = ExpertLine(spot, gwdn, 0, ff, *line_refs, ex_out.at[:, :, pl.ds(0, ff)])
    some = ex_out.shape[2] - ff
    first_line = ExpertLine(spot, win, 0, some, *first_refs, ex_out.at[:, :, pl.ds(ff, some)])
    gather = Gather(spot, agb.at[me], agb, ag_s, ag_r)
    for step, (other, dev) in enumerate(others):
        remote(meta.at[other], metas.at[me], me_s.at[step], me_r.at[step], dev).start()
    own_load.wait()
    gather.start()
    gather.start_y()
    for load in loads:
        load.start()
    metas[me] = meta[me]
    slot_rows = lax.broadcasted_iota(jnp.int32, (cap, tok), 0).astype(F32)
    step = 256

    def spots(p):
        return jnp.where(slot_rows == metas[p, 0:1, :], 1.0, 0.0)

    def gate_of(p, hot):
        return jnp.sum(hot * metas[p, 1:2, :], axis=1, keepdims=True)

    def dispatch(q):
        for kk in range(2):
            p = chips[q] + kk
            hot = spots(p)
            low = hot.astype(BF16)
            part = pl.ds(q * 2 * cap + kk * cap, cap)
            xs[part, :] = dot(low, agb[p]).astype(BF16)
            ds[part, :] = (dot(low, cotb[p]) * gate_of(p, hot)).astype(BF16)

    def work(q, count):
        rows = pl.ds(q * 2 * cap, count * 2 * cap)

        @pl.loop(0, ff // step)
        def _(n):
            gate_cols, up_cols = lanes(n * step, step), lanes(ff + n * step, step)
            x = xs[rows, :]
            g = dot(x, win[:, :, :, gate_cols].reshape(width, step))
            u = dot(x, win[:, :, :, up_cols].reshape(width, step))
            s = 1.0 / (1.0 + jnp.exp(-g))
            act = g * s
            hid[rows, gate_cols] = (act * u).astype(BF16)
            h = dot(ds[rows, :], wdn[:, gate_cols])
            igs[rows, gate_cols] = (h * u * (s * (1.0 + g * (1.0 - s)))).astype(BF16)
            igs[rows, up_cols] = (h * act).astype(BF16)

        @pl.loop(0, width // step)
        def _(n):
            cols = lanes(n * step, step)
            pgs[pl.ds(0, count * 2 * cap), cols] = dot(igs[rows, :], wint[:, cols]).astype(BF16)

    def back(q, at):
        base = chips[q]
        mine, theirs = rows_at(at * 2 * cap + k * cap, cap), rows_at(at * 2 * cap + (1 - k) * cap, cap)
        given = agb.at[base + 1 - k]
        given[...] = dot_tn(spots(base + 1 - k).astype(BF16), pgs[theirs, :]).astype(BF16)
        plane.give(q, given)
        plane.zk[q][...] = dot_tn(spots(base + k).astype(BF16), pgs[mine, :]).astype(BF16)

    loads[0].wait()
    tall = width // ctx

    @pl.loop(0, ctx)
    def _(n):
        wint[:, lanes(n * tall, tall)] = win[n].reshape(tall, 2 * ff).T

    for n in range(planes - 1):
        source = lax.rem(me + planes - 1 - n, planes)
        remote(metas.at[source], metas.at[source], me_s.at[n], me_r.at[n], kp).wait_recv()
    for load in loads[1:]:
        load.wait()
    gather.other_core(0)
    dispatch(0)
    work(0, 1)
    back(0, 0)
    gather.first()
    gather.second()
    gather.other_core(1)
    dispatch(1)
    gather.other_core(2)
    dispatch(2)
    work(1, 2)
    gather.third()
    back(1, 0)
    back(2, 1)
    gather.other_core(3)
    gather.done()
    dispatch(3)
    plane.fold(1)
    plane.fold(2)
    plane.near()
    work(3, 1)
    back(3, 0)
    plane.fold(3)
    plane.given()
    plane.across()


    @pl.loop(0, ctx)
    def _(n):
        tile = dot_tn(ds[:, lanes(n * tall, tall)], hid[...]).astype(BF16)
        for d in range(gwdn.shape[1]):
            gwdn[n, d] = tile[d * gwdn.shape[2] : (d + 1) * gwdn.shape[2]]

    line.step(1)
    plane.fold(0)

    @pl.loop(0, width // step)
    def _(n):
        cols = lanes(n * step, step)
        ds[:, cols] = dot_nt(hid[...], wdn[cols, :]).astype(BF16)

    def returned(q):
        base = chips[q]
        for kk in range(2):
            p = base + kk
            hot = spots(p)
            rows = ds[pl.ds(q * 2 * cap + kk * cap, cap), :]
            ggs[p, 0:1, :] = jnp.sum(hot * dot_nt(rows, cotb[p]), axis=0, keepdims=True)
            scaled = (rows.astype(F32) * gate_of(p, hot)).astype(BF16)
            cotb[p] = dot_tn(hot.astype(BF16), scaled).astype(BF16)
        outs.give(q, cotb.at[base + 1 - k])

    returned(1)
    returned(2)
    plane.turn()
    returned(3)
    returned(0)
    outs.fold(1)
    outs.fold(2)
    outs.near()
    outs.fold(3)
    outs.across()
    ggr[me] = ggs[me]
    for n, (other, dev) in enumerate(others):
        remote(ggs.at[other], ggr.at[me], gg_s.at[n], gg_r.at[n], dev).start()
    line.step(2)
    outs.fold(0)

    def gate_up(at, size):
        @pl.loop(0, ctx)
        def _(n):
            tile = dot_tn(xs[:, lanes(n * tall, tall)], igs[:, pl.ds(at, size)]).astype(BF16)
            win[n, :, :, pl.ds(at, size)] = tile.reshape(gwdn.shape[1], gwdn.shape[2], size)

    gate_up(0, some)
    first_line.step(1)
    rest = 2 * ff - some
    gate_up(some, rest // 2)
    gate_up(some + rest // 2, rest // 2)
    gwin_copy = pltpu.make_async_copy(win.at[:, :, :, pl.ds(some, rest)], gwin_h, load_sem.at[0])
    gwin_copy.start()
    line.step(3)
    outs.turn()
    first_line.step(2)
    for rows, terms in outs.total():
        output[rows, :] = (pg_out[rows, :] + summed(terms)).astype(BF16)
    for rows, terms in plane.total():
        pg_out[rows, :] = summed(terms)
    for n in range(planes - 1):
        source = lax.rem(me + planes - 1 - n, planes)
        remote(ggr.at[source], ggr.at[source], gg_s.at[n], gg_r.at[n], kp).wait_recv()
    for p in range(planes):
        gg_out[p : p + 1, :] = ggr[p, 0:1, :]
    first_line.step(3)
    line.final()
    first_line.final()
    gwin_copy.wait()
    for n, (other, dev) in enumerate(others):
        remote(meta.at[other], metas.at[other], me_s.at[n], me_r.at[n], dev).wait_send()
        remote(ggs.at[other], ggr.at[other], gg_s.at[n], gg_r.at[n], dev).wait_send()
    plane.done()
    outs.done()
    line.done()
    first_line.done()


def run_ffn(cap, ffn, resid, cot_all, meta, win, wdn, parts, some):
    tok, width = ffn.shape
    ff = wdn.shape[2]
    planes = cot_all.shape[0]
    ctx = win.shape[0]
    rows = planes * cap
    piece = width // (ctx * parts)
    win = win.reshape(ctx, ctx, parts, piece, 2 * ff)
    vm, anyspace = pl.BlockSpec(memory_space=pltpu.VMEM), pl.BlockSpec(memory_space=pl.ANY)
    shape = jax.ShapeDtypeStruct
    dma = pltpu.SemaphoreType.DMA
    return pl.pallas_call(
        functools.partial(ffn_kernel, cap),
        out_shape=(
            shape((tok, width), BF16),
            shape((tok, width), F32),
            shape((planes, tok), F32),
            shape((ctx, parts, piece, 2 * ff - some), BF16),
            shape((ctx, piece, ff + some), BF16),
        ),
        in_specs=[anyspace, anyspace, anyspace, vm, anyspace, anyspace],
        out_specs=(vm, vm, vm, anyspace, vm),
        scratch_shapes=[
            pltpu.VMEM((planes, tok, width), BF16),
            pltpu.VMEM((planes, 8, tok), F32),
            pltpu.VMEM((planes, tok, width), BF16),
            pltpu.VMEM((ctx, parts, piece, 2 * ff), BF16),
            pltpu.VMEM((width, ff), BF16),
            pltpu.VMEM((rows, width), BF16),
            pltpu.VMEM((rows, width), BF16),
            pltpu.VMEM((rows, ff), BF16),
            pltpu.VMEM((rows, 2 * ff), BF16),
            pltpu.VMEM((4 * cap, width), BF16),
            pltpu.VMEM((planes, 8, tok), F32),
            pltpu.VMEM((planes, 8, tok), F32),
            pltpu.VMEM((2 * ff, width), BF16),
            pltpu.VMEM((ctx, parts, piece, ff), BF16),
            dma((5,)),
            dma((GATHER_COPIES,)),
            dma((GATHER_COPIES,)),
            dma((planes - 1,)),
            dma((planes - 1,)),
            dma((planes - 1,)),
            dma((planes - 1,)),
            dma((10,)),
            dma((10,)),
        ]
        + plane_scratch(tok, width)
        + line_scratch(parts, (ctx, piece, ff))
        + line_scratch(parts, (ctx, piece, some)),
        compiler_params=pltpu.CompilerParams(
            collective_id=1, has_side_effects=True, vmem_limit_bytes=63 * 2**20
        ),
        cost_estimate=pl.CostEstimate(flops=25 * 10**9, bytes_accessed=50 * 10**6, transcendentals=10**6),
    )(ffn, resid, cot_all, meta, win, wdn)


def back_kernel(
    span,
    meta,
    gg,
    lse,
    trig,
    attended,
    router_t,
    gain_two,
    gain_one,
    reduced,
    kv_h,
    queries_h,
    normed_h,
    resid_h,
    cot_h,
    pg_h,
    ffn_in_h,
    hidden_h,
    wout_h,
    wqkv_h,
    gwin_h,
    input_grad,
    qkv_out,
    proj_out,
    one_out,
    two_out,
    ffn_out,
    *scratch,
):
    wide_f, back, low, attg, mixed, weights, gwin, send, bsend, smalls, total, out_red = scratch[:12]
    mask, delta, kt, dk, dv, kvs, kvr = scratch[12:19]
    load_sem, kv_s, kv_r = scratch[19:22]
    p_zcr, p_zk, p_rx, p_ry, p_s, p_r = scratch[22:28]
    a_rx, a_ry, a_s, a_r = scratch[28:32]
    e_refs, b_refs = scratch[32:38], scratch[38:44]
    qkv_refs, proj_refs = scratch[44:47], scratch[47:50]
    one_refs, two_refs = scratch[50:57], scratch[57:64]
    f_s, f_r, kv, queries, normed = scratch[64:]
    spot = Spot()
    c, k, z, ctx = spot.c, spot.k, spot.z, spot.ctx
    tok, width = attended.shape
    cols = one_out.shape[2]
    block, piece = out_red.shape[0], proj_out.shape[0]
    heads_kv = KV_HEADS
    half_head = HEAD // 2
    n_experts = meta.shape[0]
    kv_wide = mixed.shape[1] - width
    step = 256

    def load(src, dst, i):
        copy = pltpu.make_async_copy(src, dst, load_sem.at[i])
        copy.start()
        return copy

    gwin_load = load(gwin_h, gwin, 0)
    early = [
        load(resid_h, wide_f, 1),
        load(pg_h, back, 2),
        load(cot_h, input_grad, 3),
        load(ffn_in_h, attg, 4),
    ]
    wout_load = load(wout_h, weights.at[:, pl.ds(0, width)], 5)
    later = [load(kv_h, kv, 6), load(queries_h, queries, 7), load(normed_h, normed, 8)]
    greet([spot.xp, spot.yp, spot.kp, spot.yk], spot.along())
    for n in range(1, ctx):
        cc = lax.rem(c + n, ctx)
        remote(reduced.at[cc], ffn_out.at[c], f_s.at[n - 1], f_r.at[n - 1], (spot.e, cc, z)).start()
    ffn_out[c] = reduced[c]
    one = ExpertLine(spot, gwin, 0, cols, *one_refs)
    two = ExpertLine(spot, gwin, cols, cols, *two_refs)
    proj_plane = plane_of(spot, p_zcr, p_zk, p_rx, p_ry, p_s, p_r, low=BACK_LOW)
    half_wide = width // 2
    cut = pl.ds(0, half_wide)
    early_plane = plane_of(spot, *e_refs, low=BACK_LOW)
    late_plane = plane_of(
        spot, p_zcr.at[:, :, cut], p_zk.at[:, :, cut], a_rx, a_ry, a_s, a_r, low=BACK_LOW
    )
    rest_plane = plane_of(spot, *b_refs, low=BACK_LOW)

    def shared_line(ref, refs):
        def own(d):
            return ref.at[rows_at(d * piece, piece)]

        def adder(came, d):
            came[...] = plus(came[...], own(d)[...])

        return Line(spot, own, adder, *refs)

    qkv_line, proj_line = shared_line(total, qkv_refs), shared_line(out_red, proj_refs)

    def put_shared(to, ref, came):
        to[...] = plus(ref[rows_at(z * piece, piece)], *(x[...] for x in came))

    mine, theirs = rows_at(k * block, block), rows_at((1 - k) * block, block)
    gwin_load.wait()
    one.step(1)

    for copy in early:
        copy.wait()
    gate = jnp.concatenate([meta[g, 1:2, :] for g in range(n_experts)], axis=0)
    seen = gate * gg[...]
    mix = seen - gate * jnp.sum(seen, axis=0, keepdims=True)
    mix = jnp.concatenate([mix, jnp.zeros((HEAD - n_experts, tok), F32)], axis=0)
    logit_t = mix.astype(BF16)
    r = wide_f[...]
    inv = lax.rsqrt(jnp.mean(r * r, axis=-1, keepdims=True) + NORM_EPS)
    plain = r * inv
    ffn_grad = back[...] + dot_tn(logit_t[:n_experts], router_t[...])
    gain_row = jnp.sum(ffn_grad * plain, axis=0, keepdims=True)
    scaled = ffn_grad * gain_two[...]
    grad = input_grad[...].astype(F32) + inv * (
        scaled - plain * jnp.mean(scaled * plain, axis=-1, keepdims=True)
    )
    back[...] = grad
    low[...] = grad.astype(BF16)
    lane = lax.broadcasted_iota(jnp.int32, (width, HEAD), 1)
    routed = dot_tn(attg[...], logit_t.T)
    gain_col = jnp.broadcast_to(gain_row, (HEAD, width)).T
    smalls[...] = jnp.where(lane == n_experts, gain_col, routed).astype(BF16)

    for q in (3, 1, 2, 0):
        at = lanes(spot.chips[q] * block, 2 * block)
        send[q] = dot_tn(low[:, at], attended[...]).astype(BF16)
        proj_plane.give(q, send.at[q, theirs])
    wout_load.wait()

    @pl.loop(0, width // step)
    def _(n):
        at = lanes(n * step, step)
        attg[:, at] = dot(low[...], weights[:, at]).astype(BF16)

    wqkv_load = load(wqkv_h, weights, 5)
    hidden_load = load(hidden_h, low, 1)

    def start_plane(plane, at):
        plane.fold(3, send[3, mine, at])
        plane.across()
        plane.fold(1, send[1, mine, at])
        plane.fold(2, send[2, mine, at])
        plane.near()
        plane.fold(0, send[0, mine, at])

    def qkv_tiles(plane, at):
        for q in (3, 1, 2, 0):
            rows = lanes(spot.chips[q] * block, 2 * block)
            send[q, :, at] = dot_tn(normed[:, rows], mixed[:, at]).astype(BF16)
            plane.give(q, send.at[q, theirs, at])

    start_plane(proj_plane, pl.ds(0, width))

    for copy in later:
        copy.wait()

    seq = kv.shape[0]
    spans = span.shape[1]
    size = seq // spans
    per = spans // ctx
    along_q = lax.broadcasted_iota(jnp.int32, (size, tok), 1)
    q_pos = jnp.where(along_q < size, span[0, c * per] * size, (span[0, c * per + 1] - 1) * size) + along_q
    for s in range(spans):
        k_pos = span[0, s] * size + lax.broadcasted_iota(jnp.int32, (size, tok), 0)
        mask[s * size : (s + 1) * size, :] = jnp.where(k_pos <= q_pos, 0.0, MASKED)

    lane_h = lax.broadcasted_iota(jnp.int32, (tok, HEAD), 1)
    deltas = jnp.zeros((tok, HEAD), F32)
    for h in range(HEADS):
        at = slice(h * HEAD, (h + 1) * HEAD)
        term = jnp.sum(attg[:, at].astype(F32) * attended[:, at].astype(F32), axis=-1, keepdims=True)
        deltas = jnp.where(lane_h == h, term, deltas)
    delta[...] = deltas.T
    for g in range(heads_kv):
        kt[g] = kv[:, g * HEAD : (g + 1) * HEAD].astype(F32).T.astype(BF16)

    cosine, sine = trig[0], trig[1]

    def unrotate(w):
        return w * cosine - pltpu.roll(w, half_head, 1) * sine

    def head(g, h):
        at = lanes(h * HEAD, HEAD)
        k_at = slice(g * HEAD, (g + 1) * HEAD)
        v_at = slice((heads_kv + g) * HEAD, (heads_kv + g + 1) * HEAD)
        q, a = queries[:, at], attg[:, at]
        soft = jnp.exp(dot_nt(kv[:, k_at], q) + mask[...] - lse[pl.ds(h, 1), :])
        prob = dot_nt(kv[:, v_at], a)
        score = (soft * (prob - delta[pl.ds(h, 1), :])).astype(BF16)
        mixed[:, at] = (unrotate(dot(kt[g], score).T) * HEAD**-0.5).astype(BF16)
        dk[...] += dot(score, q)
        dv[...] += dot(soft.astype(BF16), a)

    def heads(g, first, count):
        @pl.loop(first, first + count)
        def _(h):
            head(g, h)

    def clear():
        dk[...] = jnp.zeros(dk.shape, F32)
        dv[...] = jnp.zeros(dv.shape, F32)

    flip_c = lax.rem(c + 2, ctx)
    near_c = c + 1 - 2 * k
    across_c = lax.rem(near_c + 2, ctx)

    def kv_copy(g, src, i, dev):
        return remote(src, kvr.at[g, i], kv_s.at[g, i], kv_r.at[g, i], dev)

    def send_kv(g):
        for cc in range(ctx):
            rows = slice(cc * tok, (cc + 1) * tok)
            kvs[g, cc, :, :HEAD] = dk[rows, :].astype(BF16)
            kvs[g, cc, :, HEAD:] = dv[rows, :].astype(BF16)
        kv_copy(g, kvs.at[g, across_c], 1, spot.kp).start()
        kv_copy(g, kvs.at[g, near_c], 0, spot.kp).start()

    def pass_kv(g):
        kv_copy(g, kvs.at[g, across_c], 1, spot.kp).wait_recv()
        kvs[g, flip_c] = plus(kvs[g, flip_c], kvr[g, 1])
        kv_copy(g, kvs.at[g, flip_c], 2, spot.yp).start()

    clear()
    heads(0, 0, 2)
    one.step(2)
    heads(0, 2, 4)
    send_kv(0)
    clear()
    proj_plane.turn()
    proj_plane.given()
    qkv_tiles(early_plane, pl.ds(0, half_wide))
    heads(1, 6, 1)
    start_plane(early_plane, pl.ds(0, half_wide))
    pass_kv(0)
    one.step(3)
    two.step(1)
    heads(1, 7, 2)
    heads(1, 9, 3)
    send_kv(1)
    pass_kv(1)
    early_plane.turn()
    for rows, terms in proj_plane.total():
        out_red[rows, :] = summed(terms).astype(BF16)
    proj_line.step(1)
    proj_plane.done()
    for g in range(heads_kv):
        kv_copy(g, kvs.at[g, near_c], 0, spot.kp).wait_recv()
        kv_copy(g, kvs.at[g, flip_c], 2, spot.yp).wait_recv()
        own = kvs[g, c].astype(F32) + kvr[g, 0].astype(F32) + kvr[g, 2].astype(F32)
        at = width + g * HEAD
        mixed[:, at : at + HEAD] = unrotate(own[:, :HEAD]).astype(BF16)
        at = width + (heads_kv + g) * HEAD
        mixed[:, at : at + HEAD] = own[:, HEAD:].astype(BF16)

    qkv_tiles(late_plane, pl.ds(half_wide, half_wide))
    start_plane(late_plane, pl.ds(half_wide, half_wide))
    proj_line.step(2)
    wqkv_load.wait()

    @pl.loop(0, width // step)
    def _(n):
        at = lanes(n * step, step)
        wide_f[:, at] = dot_nt(mixed[...], weights[at, :])

    two.step(2)
    hidden_load.wait()
    x = low[...].astype(F32)
    inv = lax.rsqrt(jnp.mean(x * x, axis=-1, keepdims=True) + NORM_EPS)
    plain = x * inv
    ng = wide_f[...]
    gain_row = jnp.sum(ng * plain, axis=0, keepdims=True)
    scaled = ng * gain_one[...]
    input_grad[...] = (
        back[...] + inv * (scaled - plain * jnp.mean(scaled * plain, axis=-1, keepdims=True))
    ).astype(BF16)
    lane = lax.broadcasted_iota(jnp.int32, (width, HEAD), 1)
    gain_col = jnp.broadcast_to(gain_row, (HEAD, width)).T
    smalls[...] = jnp.where(lane == HEAD - 1, gain_col, smalls[...].astype(F32)).astype(BF16)
    for q in (3, 1, 2, 0):
        at = lanes(spot.chips[q] * block, 2 * block)
        bsend[q, :, :kv_wide] = dot_tn(normed[:, at], mixed[:, width:]).astype(BF16)
        bsend[q, :, kv_wide:] = smalls[rows_at(spot.chips[q] * block, 2 * block), :]
        rest_plane.give(q, bsend.at[q, theirs])
    rest_plane.fold(3, bsend[3, mine])
    rest_plane.across()
    rest_plane.fold(1, bsend[1, mine])
    rest_plane.fold(2, bsend[2, mine])
    rest_plane.near()
    rest_plane.fold(0, bsend[0, mine])
    late_plane.turn()
    rest_plane.turn()
    two.step(3)
    one.final()
    proj_line.step(3)
    for rows, terms in early_plane.total():
        total[rows, :half_wide] = summed(terms).astype(BF16)
    for rows, terms in late_plane.total():
        total[rows, half_wide:width] = summed(terms).astype(BF16)
    for rows, terms in rest_plane.total():
        total[rows, width:] = summed(terms).astype(BF16)
    qkv_line.step(1)
    one.done(one_out)
    qkv_line.step(2)
    two.final()
    proj_line.final(lambda *came: put_shared(proj_out, out_red, came))
    qkv_line.step(3)
    proj_line.done()
    early_plane.done()
    late_plane.done()
    rest_plane.done()
    for g in range(heads_kv):
        kv_copy(g, kvs.at[g, near_c], 0, spot.kp).wait_send()
        kv_copy(g, kvs.at[g, across_c], 1, spot.kp).wait_send()
        kv_copy(g, kvs.at[g, flip_c], 2, spot.yp).wait_send()
    qkv_line.final(lambda *came: put_shared(qkv_out, total, came))
    qkv_line.done()
    for n in range(1, ctx):
        cc = lax.rem(c + ctx - n, ctx)
        got = remote(ffn_out.at[cc], ffn_out.at[cc], f_s.at[n - 1], f_r.at[n - 1], spot.kp)
        got.wait_recv()
        got.wait_send()
    two.done(two_out)


def run_back(
    span, meta, gg, lse, trig, attended, router_t, gain_two, gain_one, reduced, kv, queries, normed,
    resid, cot, pg, ffn_in, hidden, wout, wqkv, gwin,
):
    tok, width = attended.shape
    seq, kv_cols = kv.shape
    planes = meta.shape[0]
    ctx, parts, rows, wide = gwin.shape
    cols = wide // 2
    block = width // planes
    piece = block // parts
    rest = kv_cols + HEAD
    vm, anyspace = pl.BlockSpec(memory_space=pltpu.VMEM), pl.BlockSpec(memory_space=pl.ANY)
    sm = pl.BlockSpec(memory_space=pltpu.SMEM)
    shape = jax.ShapeDtypeStruct
    dma = pltpu.SemaphoreType.DMA
    return pl.pallas_call(
        back_kernel,
        out_shape=(
            shape((tok, width), BF16),
            shape((piece, width + rest), BF16),
            shape((piece, width), BF16),
            shape((ctx, rows, cols), BF16),
            shape((ctx, rows, cols), BF16),
            shape(reduced.shape, BF16),
        ),
        in_specs=[sm] + [vm] * 9 + [anyspace] * 11,
        out_specs=(vm,) * 6,
        scratch_shapes=[
            pltpu.VMEM((tok, width), F32),
            pltpu.VMEM((tok, width), F32),
            pltpu.VMEM((tok, width), BF16),
            pltpu.VMEM((tok, width), BF16),
            pltpu.VMEM((tok, width + kv_cols), BF16),
            pltpu.VMEM(wqkv.shape, BF16),
            pltpu.VMEM(gwin.shape, BF16),
            pltpu.VMEM((4, 2 * block, width), BF16),
            pltpu.VMEM((4, 2 * block, rest), BF16),
            pltpu.VMEM((width, HEAD), BF16),
            pltpu.VMEM((block, width + rest), BF16),
            pltpu.VMEM((block, width), BF16),
            pltpu.VMEM((seq, tok), F32),
            pltpu.VMEM((HEAD, tok), F32),
            pltpu.VMEM((KV_HEADS, HEAD, seq), BF16),
            pltpu.VMEM((seq, HEAD), F32),
            pltpu.VMEM((seq, HEAD), F32),
            pltpu.VMEM((KV_HEADS, ctx, tok, 2 * HEAD), BF16),
            pltpu.VMEM((KV_HEADS, 3, tok, 2 * HEAD), BF16),
            dma((9,)),
            dma((KV_HEADS, 3)),
            dma((KV_HEADS, 3)),
        ]
        + plane_scratch(block, width, BACK_LOW)
        + plane_scratch(block, width // 2, BACK_LOW)[2:]
        + plane_scratch(block, width // 2, BACK_LOW)
        + plane_scratch(block, rest, BACK_LOW)
        + line_scratch(parts, (piece, width + rest))
        + line_scratch(parts, (piece, width))
        + expert_scratch(ctx, parts, rows, cols)
        + expert_scratch(ctx, parts, rows, cols)
        + [dma((ctx - 1,)), dma((ctx - 1,))]
        + [pltpu.VMEM(kv.shape, BF16), pltpu.VMEM(queries.shape, BF16), pltpu.VMEM(normed.shape, BF16)],
        compiler_params=pltpu.CompilerParams(
            collective_id=2, has_side_effects=True, vmem_limit_bytes=63 * 2**20
        ),
        cost_estimate=pl.CostEstimate(flops=12 * 10**9, bytes_accessed=60 * 10**6, transcendentals=4 * 10**6),
    )(
        span, meta, gg, lse, trig, attended, router_t, gain_two, gain_one, reduced, kv, queries, normed,
        resid, cot, pg, ffn_in, hidden, wout, wqkv, gwin,
    )


def finish_kernel(
    n_experts,
    output_h,
    input_h,
    qkv_h,
    proj_h,
    one_h,
    two_h,
    down_h,
    output,
    input_grad,
    gain_one,
    gain_two,
    qkv,
    proj,
    router,
    inner,
    down,
    low_qkv,
    low_proj,
    low_one,
    low_two,
    low_down,
    low_out,
    low_in,
    inner_full,
    down_full,
    sem,
    out_sem,
):
    whole = []
    loads = [
        pltpu.make_async_copy(src, dst, sem.at[i])
        for i, (src, dst) in enumerate(
            (
                (down_h, low_down),
                (one_h, low_one),
                (two_h, low_two),
                (qkv_h, low_qkv),
                (proj_h, low_proj),
                (output_h, low_out),
                (input_h, low_in),
            )
        )
    ]
    for copy in loads:
        copy.start()
    loads[0].wait()
    ff = down.shape[2]
    down_full[...] = low_down[:, :, :ff].astype(F32)
    at = low_down.shape[2] - ff
    inner_full[:, :, :at] = low_down[:, :, ff:].astype(F32)
    whole.append(pltpu.make_async_copy(down_full, down, out_sem.at[2]))
    whole[-1].start()
    for load, low in zip(loads[1:3], (low_one, low_two)):
        load.wait()
        size = low.shape[2]
        inner_full[:, :, at : at + size] = low[...].astype(F32)
        at += size
    whole.append(pltpu.make_async_copy(inner_full, inner, out_sem.at[3]))
    whole[-1].start()
    for i, (low, to) in enumerate(((low_out, output), (low_in, input_grad))):
        loads[5 + i].wait()
        whole.append(pltpu.make_async_copy(low, to, out_sem.at[i]))
        whole[-1].start()
    for load in loads[3:5]:
        load.wait()
    wide = qkv.shape[1]
    qkv[...] = low_qkv[:, :wide].astype(F32)
    proj[...] = low_proj[...].astype(F32)
    small = low_qkv[:, wide:].astype(F32)
    piece = small.shape[0]
    same = lax.broadcasted_iota(jnp.int32, (piece, piece), 0) == lax.broadcasted_iota(
        jnp.int32, (piece, piece), 1
    )

    def column(at):
        return jnp.sum(jnp.where(same, small[:, at : at + 1], 0.0), axis=0, keepdims=True)

    gain_one[...] = column(HEAD - 1)[0]
    gain_two[...] = column(n_experts)[0]
    for at in range(n_experts):
        router[at : at + 1, :] = column(at)
    for copy in whole:
        copy.wait()


def run_finish(n_experts, output, input_grad, qkv, proj, one, two, down):
    piece, width = proj.shape
    ctx, rows, cols = one.shape
    ff = (down.shape[2] + 2 * cols) // 3
    shape = jax.ShapeDtypeStruct
    vm, anyspace = pl.BlockSpec(memory_space=pltpu.VMEM), pl.BlockSpec(memory_space=pl.ANY)
    return pl.pallas_call(
        functools.partial(finish_kernel, n_experts),
        out_shape=(
            shape(output.shape, BF16),
            shape(input_grad.shape, BF16),
            shape((piece,), F32),
            shape((piece,), F32),
            shape((piece, qkv.shape[1] - HEAD), F32),
            shape((piece, width), F32),
            shape((n_experts, piece), F32),
            shape((ctx, rows, 2 * ff), F32),
            shape((ctx, rows, ff), F32),
        ),
        in_specs=[anyspace] * 7,
        out_specs=(anyspace, anyspace, vm, vm, vm, vm, vm, anyspace, anyspace),
        scratch_shapes=[pltpu.VMEM(x.shape, BF16) for x in (qkv, proj, one, two, down, output, input_grad)]
        + [
            pltpu.VMEM((ctx, rows, 2 * ff), F32),
            pltpu.VMEM((ctx, rows, ff), F32),
            pltpu.SemaphoreType.DMA((7,)),
            pltpu.SemaphoreType.DMA((4,)),
        ],
        compiler_params=pltpu.CompilerParams(vmem_limit_bytes=56 * 2**20),
    )(output, input_grad, qkv, proj, one, two, down)


def local(
    hidden_in,
    span_order,
    expert_ids,
    priority,
    gain_attn,
    qkv_weight,
    out_weight,
    gain_ffn,
    router,
    in_weight,
    down_weight,
    cotangent,
):
    _, tok_rows, width = hidden_in.shape
    ctx, parts = lax.axis_size("context"), lax.axis_size("dp")
    planes = ctx * lax.axis_size("expert")
    n_experts = router.shape[1]
    top_k = expert_ids.shape[2]
    capacity = (9 * tok_rows * top_k + 8 * n_experts - 1) // (8 * n_experts)
    ff = down_weight.shape[2]
    half_freqs = ROPE_BASE ** (np.arange(HEAD // 2) * (-2.0 / HEAD))
    freqs = np.concatenate([half_freqs, half_freqs])[None].astype(np.float32)
    router_t = router.T
    hidden, cot = hidden_in[0], cotangent[0]
    normed, queries, kv, lse, attended, resid, ffn_in, trig, meta, cot_all = run_front(
        capacity,
        span_order,
        hidden,
        cot,
        gain_attn,
        freqs,
        gain_ffn,
        router_t,
        expert_ids[0].T,
        priority[0].T,
        qkv_weight,
        out_weight,
        ctx,
        planes,
    )
    output, pair_sum, gate_grad, gwin, reduced = run_ffn(
        capacity, ffn_in, resid, cot_all, meta, in_weight, down_weight, parts, ff // 3
    )
    input_grad, qkv_sum, proj_sum, in_one, in_two, ffn_sums = run_back(
        span_order,
        meta,
        gate_grad,
        lse,
        trig,
        attended,
        router_t,
        gain_ffn,
        gain_attn,
        reduced,
        kv,
        queries,
        normed,
        resid,
        cot,
        pair_sum,
        ffn_in,
        hidden,
        out_weight,
        qkv_weight,
        gwin,
    )
    output, input_grad, gain_one, gain_two, qkv_grad, proj_grad, router_grad, inner_grad, down_grad = run_finish(
        n_experts, output, input_grad, qkv_sum, proj_sum, in_one, in_two, ffn_sums
    )
    return (
        output[None],
        input_grad[None],
        gain_one,
        qkv_grad,
        proj_grad,
        gain_two,
        router_grad.T,
        inner_grad,
        down_grad,
    )


def general(
    hidden_in,
    span_order,
    expert_ids,
    priority,
    gain_attn,
    qkv_weight,
    out_weight,
    gain_ffn,
    router,
    in_weight,
    down_weight,
    cotangent,
):
    tok_rows = hidden_in.shape[1]
    width = hidden_in.shape[2]
    contexts = lax.axis_size("context")
    span_len = tok_rows // 2
    seq_len = tok_rows * contexts
    group = HEADS // KV_HEADS
    q_cols = HEADS * HEAD
    kv_cols = KV_HEADS * HEAD
    scale = HEAD ** (-0.5)
    local_experts = in_weight.shape[0]
    n_experts = local_experts * lax.axis_size("expert")
    top_k = expert_ids.shape[2]
    capacity = (9 * tok_rows * top_k + 8 * n_experts - 1) // (8 * n_experts)
    ff_width = down_weight.shape[2]
    seq_spans = span_order[0]
    stored = jnp.arange(seq_len) // span_len
    all_pos = (seq_spans[stored] * span_len + jnp.arange(seq_len) % span_len).astype(jnp.float32)
    my_pos = lax.dynamic_slice_in_dim(all_pos, lax.axis_index("context") * tok_rows, tok_rows)
    cosine, sine = rope_tables(my_pos, HEAD)
    inputs = hidden_in[0].astype(jnp.float32)
    inv_one = lax.rsqrt(jnp.mean(inputs * inputs, axis=-1, keepdims=True) + NORM_EPS)
    plain_one = inputs * inv_one
    normed = (plain_one * gain_attn).astype(jnp.bfloat16)
    mixed = jnp.dot(normed, qkv_weight, preferred_element_type=jnp.float32)
    queries = (
        rotate(mixed[:, :q_cols].reshape(tok_rows, HEADS, HEAD), cosine, sine) * scale
    ).astype(jnp.bfloat16)
    keys = rotate(
        mixed[:, q_cols : q_cols + kv_cols].reshape(tok_rows, KV_HEADS, HEAD), cosine, sine
    ).astype(jnp.bfloat16)
    values = mixed[:, q_cols + kv_cols :].reshape(tok_rows, KV_HEADS, HEAD).astype(jnp.bfloat16)
    grouped = queries.reshape(tok_rows, KV_HEADS, group, HEAD)

    def key_scores(key_piece):
        scores = jnp.einsum(
            "qkgd,skd->kgqs", grouped, key_piece, preferred_element_type=jnp.float32
        )
        visible = all_pos[None, None, None, :] <= my_pos[None, None, :, None]
        return (jnp.where(visible, scores, MASKED), visible)

    running = jnp.full((KV_HEADS, group, tok_rows), MASKED, jnp.float32)
    key_piece = lax.all_gather(keys, "context", axis=0, tiled=True)
    value_piece = lax.all_gather(values, "context", axis=0, tiled=True)
    scores, visible = key_scores(key_piece)
    newest = jnp.maximum(running, jnp.max(scores, axis=-1))
    weights = jnp.where(visible, jnp.exp(scores - newest[..., None]), 0.0)
    totals = jnp.sum(weights, axis=-1)
    accum = jnp.einsum(
        "kgqs,skd->kgqd",
        weights.astype(jnp.bfloat16),
        value_piece,
        preferred_element_type=jnp.float32,
    )
    running, totals, accum = (newest, totals, accum)
    log_total = running + jnp.log(totals)
    attended = (
        (accum / totals[..., None])
        .transpose(2, 0, 1, 3)
        .reshape(tok_rows, q_cols)
        .astype(jnp.bfloat16)
    )
    resid = inputs + jnp.einsum(
        "rh,dh->rd", attended, out_weight, preferred_element_type=jnp.float32
    )
    inv_two = lax.rsqrt(jnp.mean(resid * resid, axis=-1, keepdims=True) + NORM_EPS)
    plain_two = resid * inv_two
    ffn_in = (plain_two * gain_ffn).astype(jnp.bfloat16)
    logits = jnp.dot(ffn_in, router, preferred_element_type=jnp.float32)
    token_ids = expert_ids[0]
    gates = softmax_last(jnp.take_along_axis(logits, token_ids, axis=1))
    slots = route(token_ids, priority[0], n_experts, capacity)
    pair_rows = jnp.repeat(ffn_in, top_k, axis=0)
    send_rows = (
        jnp.zeros((n_experts * capacity, width), jnp.bfloat16).at[slots].set(pair_rows, mode="drop")
    )
    received = lax.all_to_all(
        send_rows.reshape(n_experts, capacity, width),
        "expert",
        split_axis=0,
        concat_axis=1,
        tiled=True,
    )
    inner = jnp.einsum("erd,edf->erf", received, in_weight, preferred_element_type=jnp.float32)
    gate_part = inner[..., :ff_width]
    up_part = inner[..., ff_width:]
    sigma = 1.0 / (1.0 + jnp.exp(-gate_part))
    activated = gate_part * sigma
    hidden = (activated * up_part).astype(jnp.bfloat16)
    expert_out = jnp.einsum(
        "erf,edf->erd", hidden, down_weight, preferred_element_type=jnp.float32
    ).astype(jnp.bfloat16)
    returned = lax.all_to_all(
        expert_out, "expert", split_axis=1, concat_axis=0, tiled=True
    ).reshape(n_experts * capacity, width)
    padded = jnp.concatenate([returned, jnp.zeros((1, width), jnp.bfloat16)], axis=0)
    picked = padded[slots].reshape(tok_rows, top_k, width)
    output = (resid + jnp.sum(gates[:, :, None] * picked, axis=1)).astype(jnp.bfloat16)
    cot_low = cotangent[0]
    cot_full = cot_low.astype(jnp.float32)
    gate_grad = jnp.einsum("rkd,rd->rk", picked, cot_low, preferred_element_type=jnp.float32)
    ret_grad = (
        (gates[:, :, None] * cot_full[:, None, :])
        .astype(jnp.bfloat16)
        .reshape(tok_rows * top_k, width)
    )
    send_grad = (
        jnp.zeros((n_experts * capacity, width), jnp.bfloat16).at[slots].set(ret_grad, mode="drop")
    )
    received_grad = lax.all_to_all(
        send_grad.reshape(n_experts, capacity, width),
        "expert",
        split_axis=0,
        concat_axis=1,
        tiled=True,
    )
    hid_grad = jnp.einsum(
        "erd,edf->erf", received_grad, down_weight, preferred_element_type=jnp.float32
    )
    slope = sigma * (1.0 + gate_part * (1.0 - sigma))
    inner_grad = jnp.concatenate(
        [hid_grad * up_part * slope, hid_grad * activated], axis=-1
    ).astype(jnp.bfloat16)
    row_grad = jnp.einsum(
        "erf,edf->erd", inner_grad, in_weight, preferred_element_type=jnp.float32
    ).astype(jnp.bfloat16)
    part_rows = received
    expert_in = (
        lax.psum_scatter(
            jnp.einsum(
                "erd,erf->def", part_rows, inner_grad, preferred_element_type=jnp.float32
            ).astype(jnp.bfloat16),
            ("context", "dp"),
            scatter_dimension=0,
            tiled=True,
        )
        .astype(jnp.float32)
        .transpose(1, 0, 2)
    )
    part_rows = received_grad
    expert_down = (
        lax.psum_scatter(
            jnp.einsum(
                "erd,erf->def", part_rows, hidden, preferred_element_type=jnp.float32
            ).astype(jnp.bfloat16),
            ("context", "dp"),
            scatter_dimension=0,
            tiled=True,
        )
        .astype(jnp.float32)
        .transpose(1, 0, 2)
    )
    back_rows = lax.all_to_all(row_grad, "expert", split_axis=1, concat_axis=0, tiled=True).reshape(
        n_experts * capacity, width
    )
    back_padded = jnp.concatenate([back_rows, jnp.zeros((1, width), jnp.bfloat16)], axis=0)
    pair_grad = back_padded[slots].reshape(tok_rows, top_k, width)
    mix_grad = gates * (gate_grad - jnp.sum(gates * gate_grad, axis=-1, keepdims=True))
    matches = token_ids[:, :, None] == jnp.arange(n_experts)[None, None, :]
    logit_grad = jnp.sum(jnp.where(matches, mix_grad[:, :, None], 0.0), axis=1).astype(jnp.bfloat16)
    router_part = jnp.einsum("rd,re->de", ffn_in, logit_grad, preferred_element_type=jnp.float32)
    ffn_grad = jnp.sum(pair_grad.astype(jnp.float32), axis=1) + jnp.einsum(
        "re,de->rd", logit_grad, router, preferred_element_type=jnp.float32
    )
    gain_ffn_part = jnp.sum(ffn_grad * plain_two, axis=0)
    scaled_two = ffn_grad * gain_ffn
    resid_grad = cot_full + inv_two * (
        scaled_two - plain_two * jnp.mean(scaled_two * plain_two, axis=-1, keepdims=True)
    )
    resid_low = resid_grad.astype(jnp.bfloat16)
    out_part = jnp.einsum("rd,rh->dh", resid_low, attended, preferred_element_type=jnp.float32)
    att_grad = jnp.einsum(
        "rd,dh->rh", resid_low, out_weight, preferred_element_type=jnp.float32
    ).astype(jnp.bfloat16)
    att_heads = att_grad.reshape(tok_rows, KV_HEADS, group, HEAD)
    row_delta = jnp.sum(
        att_heads.astype(jnp.float32)
        * attended.reshape(tok_rows, KV_HEADS, group, HEAD).astype(jnp.float32),
        axis=-1,
    ).transpose(1, 2, 0)
    key_piece = lax.all_gather(keys, "context", axis=0, tiled=True)
    value_piece = lax.all_gather(values, "context", axis=0, tiled=True)
    scores, visible = key_scores(key_piece)
    soft = jnp.exp(scores - log_total[..., None])
    prob_grad = jnp.einsum(
        "qkgd,skd->kgqs", att_heads, value_piece, preferred_element_type=jnp.float32
    )
    score_grad = (soft * (prob_grad - row_delta[..., None])).astype(jnp.bfloat16)
    query_acc = jnp.einsum(
        "kgqs,skd->kgqd", score_grad, key_piece, preferred_element_type=jnp.float32
    )
    key_part = jnp.einsum("kgqs,qkgd->skd", score_grad, grouped, preferred_element_type=jnp.float32)
    value_part = jnp.einsum(
        "kgqs,qkgd->skd", soft.astype(jnp.bfloat16), att_heads, preferred_element_type=jnp.float32
    )
    pair_acc = jnp.stack([key_part, value_part], axis=1)
    query_acc, pair_acc = (query_acc, pair_acc)
    own_pairs = lax.psum_scatter(
        pair_acc.astype(jnp.bfloat16), "context", scatter_dimension=0, tiled=True
    ).astype(jnp.float32)
    query_grad = (
        unrotate(query_acc.transpose(2, 0, 1, 3).reshape(tok_rows, HEADS, HEAD), cosine, sine)
        * scale
    )
    key_grad = unrotate(own_pairs[:, 0], cosine, sine)
    mixed_grad = jnp.concatenate(
        [
            query_grad.reshape(tok_rows, q_cols),
            key_grad.reshape(tok_rows, kv_cols),
            own_pairs[:, 1].reshape(tok_rows, kv_cols),
        ],
        axis=-1,
    ).astype(jnp.bfloat16)
    qkv_part = jnp.einsum("rd,rc->dc", normed, mixed_grad, preferred_element_type=jnp.float32)
    norm_grad = jnp.einsum("rc,dc->rd", mixed_grad, qkv_weight, preferred_element_type=jnp.float32)
    gain_attn_part = jnp.sum(norm_grad * plain_one, axis=0)
    scaled_one = norm_grad * gain_attn
    input_grad = (
        resid_grad
        + inv_one
        * (scaled_one - plain_one * jnp.mean(scaled_one * plain_one, axis=-1, keepdims=True))
    ).astype(jnp.bfloat16)
    gain_attn_grad, qkv_grad, out_proj_grad, gain_ffn_grad, router_grad = (
        lax.psum_scatter(
            gain_attn_part, ("expert", "context", "dp"), scatter_dimension=0, tiled=True
        ),
        lax.psum_scatter(qkv_part, ("expert", "context", "dp"), scatter_dimension=0, tiled=True),
        lax.psum_scatter(out_part, ("expert", "context", "dp"), scatter_dimension=0, tiled=True),
        lax.psum_scatter(
            gain_ffn_part, ("expert", "context", "dp"), scatter_dimension=0, tiled=True
        ),
        lax.psum_scatter(router_part, ("expert", "context", "dp"), scatter_dimension=0, tiled=True),
    )
    return (
        output[None],
        input_grad[None],
        gain_attn_grad,
        qkv_grad,
        out_proj_grad,
        gain_ffn_grad,
        router_grad,
        expert_in,
        expert_down,
    )


def solution(mesh):
    in_specs = (
        P(("expert", "dp"), "context", None),
        P(("expert", "dp"), None),
        P(("expert", "dp"), "context", None),
        P(("expert", "dp"), "context", None),
        P(),
        P(),
        P(),
        P(),
        P(),
        P("expert", None, None),
        P("expert", None, None),
        P(("expert", "dp"), "context", None),
    )
    out_specs = (
        P(("expert", "dp"), "context", None),
        P(("expert", "dp"), "context", None),
        P(("expert", "context", "dp")),
        P(("expert", "context", "dp"), None),
        P(("expert", "context", "dp"), None),
        P(("expert", "context", "dp")),
        P(("expert", "context", "dp"), None),
        P("expert", ("context", "dp"), None),
        P("expert", ("context", "dp"), None),
    )
    tuned = dict(mesh.shape) == {"expert": 2, "context": 4, "dp": 4}
    body = local if tuned else general
    return jax.shard_map(body, mesh=mesh, in_specs=in_specs, out_specs=out_specs, check_vma=False)
```

```python
import functools

import jax
import jax.numpy as jnp
import numpy as np
from jax import lax
from jax.experimental import pallas as pl
from jax.experimental.pallas import tpu as pltpu
from jax.sharding import PartitionSpec as P

HEADS = 12
KV_HEADS = 2
HEAD = 128


ROPE_BASE = 1000000.0
NORM_EPS = 1e-06
MASKED = -1e30


def rope_tables(positions, head_size):
    half_size = head_size // 2
    freqs = ROPE_BASE ** (jnp.arange(half_size).astype(jnp.float32) * (-2.0 / head_size))
    angles = positions[:, None] * freqs[None, :]
    return (jnp.cos(angles)[:, None, :], jnp.sin(angles)[:, None, :])


def rotate(values, cosine, sine):
    half_size = values.shape[-1] // 2
    first = values[..., :half_size]
    second = values[..., half_size:]
    return jnp.concatenate(
        [first * cosine - second * sine, second * cosine + first * sine], axis=-1
    )


def unrotate(values, cosine, sine):
    half_size = values.shape[-1] // 2
    first = values[..., :half_size]
    second = values[..., half_size:]
    return jnp.concatenate(
        [first * cosine + second * sine, second * cosine - first * sine], axis=-1
    )


def softmax_last(scores):
    shifted = jnp.exp(scores - jnp.max(scores, axis=-1, keepdims=True))
    return shifted / jnp.sum(shifted, axis=-1, keepdims=True)


def route(block_ids, block_order, n_experts, capacity):
    flat_ids = block_ids.reshape(-1)
    flat_order = block_order.reshape(-1)
    choose = (flat_ids[:, None] == jnp.arange(n_experts)[None, :]).astype(jnp.int32)
    ordered = jnp.zeros_like(choose).at[flat_order].set(choose)
    earlier = jnp.cumsum(ordered, axis=0, dtype=jnp.int32) - ordered
    ranks = jnp.sum(earlier[flat_order] * choose, axis=1)
    return jnp.where(ranks < capacity, flat_ids * capacity + ranks, n_experts * capacity)


MESH = pl.DeviceIdType.MESH
F32 = jnp.float32
BF16 = jnp.bfloat16
BACK_LOW = 96
OUT_LOW = 128
FRONT_LOW = 96
FRONT_AHEAD = 64


def dot(a, b):
    return jnp.dot(a, b, preferred_element_type=F32)


def dot_nt(a, b):
    return lax.dot_general(a, b, (((1,), (1,)), ((), ())), preferred_element_type=F32)


def dot_tn(a, b):
    return lax.dot_general(a, b, (((0,), (0,)), ((), ())), preferred_element_type=F32)


def plus(a, *more):
    total = a.astype(F32)
    for b in more:
        total = total + b.astype(F32)
    return total.astype(BF16)


def lanes(at, size):
    return pl.ds(pl.multiple_of(at, 128), size)


def rows_at(at, size):
    return pl.ds(pl.multiple_of(at, 16), size)


def remote(src, dst, s, r, dev):
    return pltpu.make_async_remote_copy(
        src_ref=src, dst_ref=dst, send_sem=s, recv_sem=r, device_id=dev, device_id_type=MESH
    )


class Spot:
    def __init__(self):
        e, c, z = lax.axis_index("expert"), lax.axis_index("context"), lax.axis_index("dp")
        self.ctx = lax.axis_size("context")
        self.parts = lax.axis_size("dp")
        self.planes = self.ctx * lax.axis_size("expert")
        y, k = lax.div(c, 2), lax.rem(c, 2)
        self.e, self.c, self.z, self.k = e, c, z, k
        self.me = e * self.ctx + c
        self.xp, self.yp = (1 - e, c, z), (e, (1 - y) * 2 + k, z)
        self.kp, self.yk = (e, y * 2 + 1 - k, z), (e, (1 - y) * 2 + 1 - k, z)
        self.chips = [
            eq * self.ctx + yq * 2 for eq, yq in ((e, y), (1 - e, y), (e, 1 - y), (1 - e, 1 - y))
        ]

    def others(self):
        found = []
        for step in range(1, self.planes):
            other = lax.rem(self.me + step, self.planes)
            found.append((other, (lax.div(other, self.ctx), lax.rem(other, self.ctx), self.z)))
        return found

    def along(self):
        e, c, z = self.e, self.c, self.z
        return [(z < self.parts - 1, (e, c, z + 1)), (z > 0, (e, c, z - 1))]


def greet(peers, extra=()):
    barrier = pltpu.get_barrier_semaphore()
    for peer in peers:
        pl.semaphore_signal(barrier, inc=1, device_id=peer, device_id_type=MESH)
    for there, peer in extra:

        @pl.when(there)
        def _():
            pl.semaphore_signal(barrier, inc=1, device_id=peer, device_id_type=MESH)

    count = len(peers)
    for there, _ in extra:
        count = count + there.astype(jnp.int32)
    pl.semaphore_wait(barrier, count)


class Plane:
    def __init__(self, spot, zcr, zk, rx, ry, s, r, zcr_there=None, low=None):
        self.zcr_there = zcr_there or zcr
        self.spot, self.zcr, self.zk, self.rx, self.ry, self.s, self.r = spot, zcr, zk, rx, ry, s, r
        low = low or zk[0].shape[0] // 2
        self.lo, self.hi = pl.ds(0, low), pl.ds(low, zk[0].shape[0] - low)
        self.sent, self.gives = [], []

    def push(self, src, dst, i, dev):
        copy = remote(src, dst, self.s.at[i], self.r.at[i], dev)
        copy.start()
        self.sent.append(copy)

    def arrive(self, dst, i):
        remote(dst, dst, self.s.at[i], self.r.at[i], self.spot.kp).wait_recv()

    def given(self):
        for copy in self.gives:
            copy.wait_send()
        self.gives = []

    def give(self, q, src):
        self.gives.append(remote(src, self.zcr_there[q], self.s.at[q], self.r.at[q], self.spot.kp))
        self.gives[-1].start()

    def fold(self, q, own=None):
        self.arrive(self.zcr[q], q)
        self.zk[q][...] = plus(self.zk[q][...] if own is None else own, self.zcr[q][...])

    def near(self):
        self.push(self.zk[1].at[self.lo], self.rx[1], 5, self.spot.xp)
        self.push(self.zk[2].at[self.hi], self.ry[1], 8, self.spot.yp)

    def across(self):
        self.push(self.zk[3].at[self.lo], self.rx[0], 4, self.spot.xp)
        self.push(self.zk[3].at[self.hi], self.ry[0], 7, self.spot.yp)

    def turn(self):
        lo, hi = self.lo, self.hi
        self.arrive(self.rx[0], 4)
        self.zk[2][lo] = plus(self.zk[2][lo], self.rx[0][...])
        self.push(self.zk[2].at[lo], self.ry[2], 9, self.spot.yp)
        self.arrive(self.ry[0], 7)
        self.zk[1][hi] = plus(self.zk[1][hi], self.ry[0][...])
        self.push(self.zk[1].at[hi], self.rx[2], 6, self.spot.xp)

    def total(self):
        self.arrive(self.rx[1], 5)
        self.arrive(self.ry[1], 8)
        self.arrive(self.rx[2], 6)
        self.arrive(self.ry[2], 9)
        return (
            (self.lo, (self.zk[0][self.lo], self.rx[1][...], self.ry[2][...])),
            (self.hi, (self.zk[0][self.hi], self.rx[2][...], self.ry[1][...])),
        )

    def done(self):
        self.given()
        for copy in self.sent:
            copy.wait_send()


def plane_of(spot, zcr, zk, rx, ry, s, r, low=None):
    four, block = range(4), zk.shape[1]
    lo, hi = pl.ds(0, low or block // 2), pl.ds(0, block - (low or block // 2))
    return Plane(
        spot,
        [zcr.at[q] for q in four],
        [zk.at[q] for q in four],
        [rx.at[0, lo], rx.at[1, lo], rx.at[2, hi]],
        [ry.at[0, hi], ry.at[1, hi], ry.at[2, lo]],
        s,
        r,
        low=low,
    )


def plane_scratch(block, wide, low=None):
    most = max(low or block // 2, block - (low or block // 2))
    return [
        pltpu.VMEM((4, block, wide), BF16),
        pltpu.VMEM((4, block, wide), BF16),
        pltpu.VMEM((3, most, wide), BF16),
        pltpu.VMEM((3, most, wide), BF16),
        pltpu.SemaphoreType.DMA((10,)),
        pltpu.SemaphoreType.DMA((10,)),
    ]


def summed(terms):
    total = terms[0].astype(F32)
    for term in terms[1:]:
        total = total + term.astype(F32)
    return total


class Line:
    def __init__(self, spot, own, adder, buf, s, r):
        z, last = spot.z, spot.parts - 1
        e, c = spot.e, spot.c
        self.own, self.adder, self.buf, self.s, self.r = own, adder, buf, s, r
        self.z, self.last, self.parts = z, last, spot.parts
        self.ways = [(z, (e, c, z + 1), lambda d: d), (last - z, (e, c, z - 1), lambda d: last - d)]

    def step(self, turn):
        for way, (i, dev, part) in enumerate(self.ways):
            to, s, r = self.buf.at[way, turn - 1], self.s.at[way, turn - 1], self.r.at[way, turn - 1]

            @pl.when(i == 0)
            def _():
                remote(self.own(part(self.parts - turn)), to, s, r, dev).start()

            if turn >= 2:
                came, s_came, r_came = (x.at[way, turn - 2] for x in (self.buf, self.s, self.r))

                @pl.when((i >= 1) & (i <= turn - 1) & (i < self.last))
                def _():
                    remote(came, came, s_came, r_came, dev).wait_recv()
                    self.adder(came, part(self.parts - turn + i))
                    remote(came, to, s, r, dev).start()

    def final(self, put):
        last, z = self.last, self.z
        for way, (i, dev, _) in enumerate(self.ways):
            came = self.buf.at[way, last - 1]

            @pl.when(i >= 1)
            def _():
                remote(came, came, self.s.at[way, last - 1], self.r.at[way, last - 1], dev).wait_recv()

        up, down = self.buf.at[0, last - 1], self.buf.at[1, last - 1]
        pl.when(z == 0)(lambda: put(down))
        pl.when(z == last)(lambda: put(up))
        pl.when((z > 0) & (z < last))(lambda: put(up, down))

    def done(self):
        for way, (i, dev, _) in enumerate(self.ways):
            for turn in range(1, self.parts):
                came = self.buf.at[way, turn - 1]

                @pl.when((i <= turn - 1) & (i < self.last))
                def _():
                    remote(came, came, self.s.at[way, turn - 1], self.r.at[way, turn - 1], dev).wait_send()


def line_scratch(parts, piece):
    return [
        pltpu.VMEM((2, parts - 1) + piece, BF16),
        pltpu.SemaphoreType.DMA((2, parts - 1)),
        pltpu.SemaphoreType.DMA((2, parts - 1)),
    ]


class ExpertLine:
    def __init__(self, spot, ref, at, cols, buf, s, r, fin, spread=None, a_s=None, a_r=None):
        self.spot, self.ref, self.at, self.cols = spot, ref, at, cols
        self.fin, self.spread, self.a_s, self.a_r = fin, spread, a_s, a_r
        self.line = Line(spot, self.own, self.adder, buf, s, r)
        self.step = self.line.step

    def own(self, d):
        return self.ref.at[:, d, :, pl.ds(self.at, self.cols)]

    def piece(self, cc, d):
        return self.ref[cc, d, :, self.at : self.at + self.cols]

    def adder(self, came, d):
        for cc in range(self.spot.ctx):
            came[cc] = plus(came[cc], self.piece(cc, d))

    def final(self):
        spot = self.spot

        def put(*came):
            for cc in range(spot.ctx):
                self.fin[cc] = plus(self.piece(cc, spot.z), *(x[cc] for x in came))

        self.line.final(put)
        if self.spread is None:
            return
        for step in range(1, spot.ctx):
            cc = lax.rem(spot.c + step, spot.ctx)
            remote(
                self.fin.at[cc],
                self.spread.at[spot.c],
                self.a_s.at[step - 1],
                self.a_r.at[step - 1],
                (spot.e, cc, spot.z),
            ).start()

    def done(self, out=None):
        spot = self.spot
        if self.spread is None:
            self.line.done()
            return
        for step in range(1, spot.ctx):
            cc = lax.rem(spot.c + spot.ctx - step, spot.ctx)
            got = remote(
                self.spread.at[cc],
                self.spread.at[cc],
                self.a_s.at[step - 1],
                self.a_r.at[step - 1],
                (spot.e, cc, spot.z),
            )
            got.wait_recv()
            got.wait_send()
            out[cc] = self.spread[cc]
        out[spot.c] = self.fin[spot.c]
        self.line.done()


def expert_scratch(ctx, parts, rows, cols):
    return line_scratch(parts, (ctx, rows, cols)) + [
        pltpu.VMEM((ctx, rows, cols), BF16),
        pltpu.VMEM((ctx, rows, cols), BF16),
        pltpu.SemaphoreType.DMA((ctx - 1,)),
        pltpu.SemaphoreType.DMA((ctx - 1,)),
    ]


class Gather:
    def __init__(self, spot, own, buf, s, r, low=None, ahead=0):
        self.spot, self.own, self.buf, self.s, self.r = spot, own, buf, s, r
        low = low or own.shape[0] // 2
        self.lo, self.hi = pl.ds(0, low), pl.ds(low, own.shape[0] - low)
        self.ahead, self.rest = ahead and pl.ds(low, ahead), pl.ds(low + ahead, own.shape[0] - low - ahead)
        self.x_me, self.y_me, self.d_me = (base + spot.k for base in spot.chips[1:])
        self.side = 1 - 2 * spot.k
        self.sent = []

    def push(self, src, dst, i, dev):
        copy = remote(src, dst, self.s.at[i], self.r.at[i], dev)
        copy.start()
        self.sent.append(copy)

    def move(self, p, rows, i, dev):
        self.push(self.buf.at[p, rows], self.buf.at[p, rows], i, dev)

    def got(self, p, rows, i):
        to = self.buf.at[p, rows]
        remote(to, to, self.s.at[i], self.r.at[i], self.spot.kp).wait_recv()

    def start(self):
        me, own, lo, hi = self.spot.me, self.own, self.lo, self.hi
        self.push(own.at[lo], self.buf.at[me, lo], 0, self.spot.xp)
        if self.ahead:
            self.push(own.at[self.ahead], self.buf.at[me, self.ahead], 14, self.spot.yp)
        self.push(own.at[lo], self.buf.at[me, lo], 6, self.spot.kp)
        self.push(own.at[hi], self.buf.at[me, hi], 13, self.spot.kp)
        self.push(own.at[hi], self.buf.at[me, hi], 1, self.spot.xp)

    def start_y(self):
        me, own, lo, rest = self.spot.me, self.own, self.lo, self.rest
        self.push(own.at[rest], self.buf.at[me, rest], 3, self.spot.yp)
        self.push(own.at[lo], self.buf.at[me, lo], 2, self.spot.yp)

    def first(self):
        spot = self.spot
        self.got(self.x_me, self.lo, 0)
        self.move(self.x_me, self.lo, 4, spot.yp)
        self.move(self.x_me, self.lo, 7, spot.kp)
        if self.ahead:
            self.got(self.y_me, self.ahead, 14)
        self.got(self.y_me, self.rest, 3)
        self.move(self.y_me, self.hi, 5, spot.xp)
        self.move(self.y_me, self.hi, 10, spot.kp)

    def second(self):
        self.got(self.x_me, self.hi, 1)
        self.move(self.x_me, self.hi, 8, self.spot.kp)
        self.got(self.y_me, self.lo, 2)
        self.move(self.y_me, self.lo, 9, self.spot.kp)

    def third(self):
        self.got(self.d_me, self.lo, 4)
        self.move(self.d_me, self.lo, 11, self.spot.kp)
        self.got(self.d_me, self.hi, 5)
        self.move(self.d_me, self.hi, 12, self.spot.kp)

    def other_core(self, q):
        low_sem, high_sem = ((6, 13), (7, 8), (9, 10), (11, 12))[q]
        p = (self.spot.me, self.x_me, self.y_me, self.d_me)[q] + self.side
        self.got(p, self.lo, low_sem)
        self.got(p, self.hi, high_sem)

    def done(self):
        for copy in self.sent:
            copy.wait_send()


GATHER_COPIES = 15


def front_kernel(
    cap,
    span,
    hidden,
    cot,
    gain_one,
    freqs,
    gain_two,
    router_t,
    ids_t,
    turn_t,
    wqkv_h,
    wout_h,
    normed_h,
    queries_h,
    kv_h,
    lse,
    attended,
    resid,
    ffn_in,
    trig,
    meta,
    cot_all,
    wqkv,
    wout,
    mask,
    vt,
    normed,
    queries,
    kv,
    load_sem,
    out_sem,
    kv_s,
    kv_r,
    co_s,
    co_r,
):
    spot = Spot()
    c, ctx, k = spot.c, spot.ctx, spot.k
    tok, width = hidden.shape
    group = HEADS // KV_HEADS
    kv_cols = KV_HEADS * HEAD
    half_head = HEAD // 2
    seq = kv.shape[0]
    spans = span.shape[1]
    size = seq // spans
    mine = spans // ctx
    n_experts = meta.shape[0]
    loads = [
        pltpu.make_async_copy(wqkv_h.at[:, pl.ds(width, 2 * kv_cols)], wqkv.at[:, pl.ds(width, 2 * kv_cols)], load_sem.at[0]),
        pltpu.make_async_copy(wqkv_h.at[:, pl.ds(0, width)], wqkv.at[:, pl.ds(0, width)], load_sem.at[1]),
        pltpu.make_async_copy(wout_h, wout, load_sem.at[2]),
        pltpu.make_async_copy(cot, cot_all.at[spot.me], load_sem.at[3]),
    ]
    for load in loads:
        load.start()
    greet([spot.xp, spot.yp, spot.kp])
    gather = Gather(spot, cot, cot_all, co_s, co_r, low=FRONT_LOW, ahead=FRONT_AHEAD)
    gather.start()

    x = hidden[...].astype(F32)
    inv = lax.rsqrt(jnp.mean(x * x, axis=-1, keepdims=True) + NORM_EPS)
    normed[...] = (x * inv * gain_one[...]).astype(BF16)

    along = lax.broadcasted_iota(jnp.int32, (tok, HEAD), 0)
    start_one, start_two = span[0, c * mine] * size, (span[0, c * mine + 1] - 1) * size
    place = jnp.where(along < size, start_one, start_two) + along
    angle = place.astype(F32) * freqs[...]
    cosine, sine = jnp.cos(angle), jnp.sin(angle)
    lane = lax.broadcasted_iota(jnp.int32, (tok, HEAD), 1)
    sine = jnp.where(lane < half_head, -sine, sine)
    trig[0] = cosine
    trig[1] = sine

    def rotate_in(w):
        return w * cosine + pltpu.roll(w, half_head, 1) * sine

    loads[0].wait()
    raw = dot(normed[...], wqkv[:, width:])
    own = rows_at(c * tok, tok)
    for g in range(KV_HEADS):
        at = slice(g * HEAD, (g + 1) * HEAD)
        kv[own, at] = rotate_in(raw[:, at]).astype(BF16)
    kv[own, kv_cols:] = raw[:, kv_cols:].astype(BF16)

    def kv_copy(rows, i, dev):
        return remote(kv.at[rows], kv.at[rows], kv_s.at[i], kv_r.at[i], dev)

    flip_c = lax.rem(c + 2, ctx)
    near_c = c + 1 - 2 * k
    across_c = lax.rem(near_c + 2, ctx)
    sent = [kv_copy(own, 1, spot.yp), kv_copy(own, 0, spot.kp)]
    for copy in sent:
        copy.start()
    gather.start_y()

    outs = [pltpu.make_async_copy(normed, normed_h, out_sem.at[0])]
    outs[0].start()
    loads[1].wait()
    step = 256

    @pl.loop(0, width // step)
    def _(n):
        at = lanes(n * step, step)
        raw = dot(normed[...], wqkv[:, at])
        for i in range(step // HEAD):
            w = raw[:, i * HEAD : (i + 1) * HEAD]
            queries[:, lanes(n * step + i * HEAD, HEAD)] = (rotate_in(w) * HEAD**-0.5).astype(BF16)

    outs.append(pltpu.make_async_copy(queries, queries_h, out_sem.at[1]))
    outs[1].start()

    flip = rows_at(flip_c * tok, tok)
    kv_copy(flip, 1, spot.kp).wait_recv()
    sent.append(kv_copy(flip, 2, spot.kp))
    sent[-1].start()

    expert = lax.broadcasted_iota(jnp.int32, (n_experts, tok), 0)
    never = tok * ids_t.shape[0]
    turn = jnp.full((n_experts, tok), never, jnp.int32)
    for i in range(ids_t.shape[0]):
        turn = jnp.where(ids_t[i : i + 1, :] == expert, turn_t[i : i + 1, :], turn)
    turn_f = turn.astype(F32)
    tall = jnp.concatenate([turn_f, jnp.full((HEAD - n_experts, tok), float(never), F32)], axis=0).T
    meta[...] = jnp.zeros(meta.shape, F32)
    for g in range(n_experts):
        row = turn_f[g : g + 1, :]
        rank = jnp.sum(jnp.where(tall[:, g : g + 1] < row, 1.0, 0.0), axis=0, keepdims=True)
        meta[g, 0:1, :] = jnp.where((row < never) & (rank < cap), rank, -1.0)

    along_q = lax.broadcasted_iota(jnp.int32, (size, tok), 1)
    q_pos = jnp.where(along_q < size, start_one, start_two) + along_q
    for s in range(spans):
        k_pos = span[0, s] * size + lax.broadcasted_iota(jnp.int32, (size, tok), 0)
        mask[s * size : (s + 1) * size, :] = jnp.where(k_pos <= q_pos, 0.0, MASKED)

    near, across = rows_at(near_c * tok, tok), rows_at(across_c * tok, tok)
    kv_copy(near, 0, spot.kp).wait_recv()
    kv_copy(across, 2, spot.kp).wait_recv()
    outs.append(pltpu.make_async_copy(kv, kv_h, out_sem.at[2]))
    outs[2].start()
    for g in range(KV_HEADS):
        vt[g] = kv[:, kv_cols + g * HEAD : kv_cols + (g + 1) * HEAD].astype(F32).T.astype(BF16)
    lse[...] = jnp.zeros(lse.shape, F32)

    def heads(g, first, count):
        @pl.loop(first, first + count)
        def _(h):
            at = lanes(h * HEAD, HEAD)
            scores = dot_nt(kv[:, g * HEAD : (g + 1) * HEAD], queries[:, at]) + mask[...]
            top = jnp.max(scores, axis=0, keepdims=True)
            weights = jnp.exp(scores - top)
            total = jnp.sum(weights, axis=0, keepdims=True)
            lse[pl.ds(h, 1), :] = top + jnp.log(total)
            out = dot(vt[g], weights.astype(BF16)) / total
            attended[:, at] = out.T.astype(BF16)

    heads(0, 0, 3)
    gather.first()
    heads(0, 3, 3)
    heads(1, 6, 3)
    gather.second()
    heads(1, 9, 3)

    loads[2].wait()

    @pl.loop(0, width // step)
    def _(n):
        at = lanes(n * step, step)
        resid[:, at] = hidden[:, at].astype(F32) + dot_nt(attended[...], wout[at, :])

    r = resid[...]
    inv = lax.rsqrt(jnp.mean(r * r, axis=-1, keepdims=True) + NORM_EPS)
    ffn_in[...] = (r * inv * gain_two[...]).astype(BF16)
    logits = dot_nt(router_t[...], ffn_in[...])[:n_experts]
    logits = jnp.where(turn < never, logits, MASKED)
    shifted = jnp.exp(logits - jnp.max(logits, axis=0, keepdims=True))
    gates = shifted / jnp.sum(shifted, axis=0, keepdims=True)
    for g in range(n_experts):
        meta[g, 1:2, :] = gates[g : g + 1, :]
    gather.third()
    for q in range(4):
        gather.other_core(q)
    loads[3].wait()
    gather.done()
    for copy in outs:
        copy.wait()
    for copy in sent:
        copy.wait_send()


def run_front(cap, span, hidden, cot, gain_one, freqs, gain_two, router_t, ids_t, turn_t, wqkv, wout, ctx, planes):
    tok, width = hidden.shape
    seq = tok * ctx
    n_experts = planes
    kv_cols = 2 * KV_HEADS * HEAD
    vm, anyspace = pl.BlockSpec(memory_space=pltpu.VMEM), pl.BlockSpec(memory_space=pl.ANY)
    sm = pl.BlockSpec(memory_space=pltpu.SMEM)
    shape = jax.ShapeDtypeStruct
    dma = pltpu.SemaphoreType.DMA
    return pl.pallas_call(
        functools.partial(front_kernel, cap),
        out_shape=(
            shape((tok, width), BF16),
            shape((tok, width), BF16),
            shape((seq, kv_cols), BF16),
            shape((16, tok), F32),
            shape((tok, width), BF16),
            shape((tok, width), F32),
            shape((tok, width), BF16),
            shape((2, tok, HEAD), F32),
            shape((n_experts, 8, tok), F32),
            shape((planes, tok, width), BF16),
        ),
        in_specs=[sm] + [vm] * 8 + [anyspace] * 2,
        out_specs=(anyspace,) * 3 + (vm,) * 6 + (anyspace,),
        scratch_shapes=[
            pltpu.VMEM(wqkv.shape, BF16),
            pltpu.VMEM(wout.shape, BF16),
            pltpu.VMEM((seq, tok), F32),
            pltpu.VMEM((KV_HEADS, HEAD, seq), BF16),
            pltpu.VMEM((tok, width), BF16),
            pltpu.VMEM((tok, width), BF16),
            pltpu.VMEM((seq, kv_cols), BF16),
            dma((4,)),
            dma((3,)),
            dma((3,)),
            dma((3,)),
            dma((GATHER_COPIES,)),
            dma((GATHER_COPIES,)),
        ],
        compiler_params=pltpu.CompilerParams(
            collective_id=4, has_side_effects=True, vmem_limit_bytes=56 * 2**20
        ),
        cost_estimate=pl.CostEstimate(flops=5 * 10**9, bytes_accessed=20 * 10**6, transcendentals=4 * 10**6),
    )(span, hidden, cot, gain_one, freqs, gain_two, router_t, ids_t, turn_t, wqkv, wout)


def ffn_kernel(cap, ffn_h, resid_h, cot_h, meta, win_h, wdn_h, output_h, pg_h, gg_out, gwin_h, ex_out, *scratch):
    agb, metas, cotb, win, wdn, xs, ds, hid, igs, pgs, ggs, ggr, wint, gwdn = scratch[:14]
    load_sem, ag_s, ag_r, me_s, me_r, gg_s, gg_r, out_s, out_r = scratch[14:23]
    plane_refs, line_refs, first_refs = scratch[23:29], scratch[29:32], scratch[32:35]
    output, pg_out = scratch[35:]
    spot = Spot()
    c, k, me = spot.c, spot.k, spot.me
    kp = spot.kp
    tok, width = output.shape
    ff = wdn.shape[1]
    planes, ctx = spot.planes, spot.ctx
    chips = spot.chips

    loads = [
        pltpu.make_async_copy(win_h.at[c], win, load_sem.at[0]),
        pltpu.make_async_copy(wdn_h.at[c], wdn, load_sem.at[1]),
        pltpu.make_async_copy(cot_h, cotb, load_sem.at[2]),
        pltpu.make_async_copy(resid_h, pg_out, load_sem.at[3]),
    ]
    own_load = pltpu.make_async_copy(ffn_h, agb.at[me], load_sem.at[4])
    own_load.start()
    others = spot.others()
    greet([dev for _, dev in others], spot.along())
    plane = plane_of(spot, *plane_refs)
    o_lo, o_hi = pl.ds(0, OUT_LOW), pl.ds(OUT_LOW, tok - OUT_LOW)
    outs = Plane(
        spot,
        [agb.at[2 * i + k] for i in range(4)],
        [cotb.at[base + k] for base in chips],
        [agb.at[1 - k, o_lo], agb.at[3 - k, o_lo], agb.at[1 - k, o_hi]],
        [agb.at[3 - k, o_hi], agb.at[5 - k, o_hi], agb.at[5 - k, o_lo]],
        out_s,
        out_r,
        [agb.at[2 * i + 1 - k] for i in range(4)],
        low=OUT_LOW,
    )
    line = ExpertLine(spot, gwdn, 0, ff, *line_refs, ex_out.at[:, :, pl.ds(0, ff)])
    some = ex_out.shape[2] - ff
    first_line = ExpertLine(spot, win, 0, some, *first_refs, ex_out.at[:, :, pl.ds(ff, some)])
    gather = Gather(spot, agb.at[me], agb, ag_s, ag_r)
    for step, (other, dev) in enumerate(others):
        remote(meta.at[other], metas.at[me], me_s.at[step], me_r.at[step], dev).start()
    own_load.wait()
    gather.start()
    gather.start_y()
    for load in loads:
        load.start()
    metas[me] = meta[me]
    slot_rows = lax.broadcasted_iota(jnp.int32, (cap, tok), 0).astype(F32)
    step = 256

    def spots(p):
        return jnp.where(slot_rows == metas[p, 0:1, :], 1.0, 0.0)

    def gate_of(p, hot):
        return jnp.sum(hot * metas[p, 1:2, :], axis=1, keepdims=True)

    def dispatch(q):
        for kk in range(2):
            p = chips[q] + kk
            hot = spots(p)
            low = hot.astype(BF16)
            part = pl.ds(q * 2 * cap + kk * cap, cap)
            xs[part, :] = dot(low, agb[p]).astype(BF16)
            ds[part, :] = (dot(low, cotb[p]) * gate_of(p, hot)).astype(BF16)

    def work(q, count):
        rows = pl.ds(q * 2 * cap, count * 2 * cap)

        @pl.loop(0, ff // step)
        def _(n):
            gate_cols, up_cols = lanes(n * step, step), lanes(ff + n * step, step)
            x = xs[rows, :]
            g = dot(x, win[:, :, :, gate_cols].reshape(width, step))
            u = dot(x, win[:, :, :, up_cols].reshape(width, step))
            s = 1.0 / (1.0 + jnp.exp(-g))
            act = g * s
            hid[rows, gate_cols] = (act * u).astype(BF16)
            h = dot(ds[rows, :], wdn[:, gate_cols])
            igs[rows, gate_cols] = (h * u * (s * (1.0 + g * (1.0 - s)))).astype(BF16)
            igs[rows, up_cols] = (h * act).astype(BF16)

        @pl.loop(0, width // step)
        def _(n):
            cols = lanes(n * step, step)
            pgs[pl.ds(0, count * 2 * cap), cols] = dot(igs[rows, :], wint[:, cols]).astype(BF16)

    def back(q, at):
        base = chips[q]
        mine, theirs = rows_at(at * 2 * cap + k * cap, cap), rows_at(at * 2 * cap + (1 - k) * cap, cap)
        given = agb.at[base + 1 - k]
        given[...] = dot_tn(spots(base + 1 - k).astype(BF16), pgs[theirs, :]).astype(BF16)
        plane.give(q, given)
        plane.zk[q][...] = dot_tn(spots(base + k).astype(BF16), pgs[mine, :]).astype(BF16)

    loads[0].wait()
    tall = width // ctx

    @pl.loop(0, ctx)
    def _(n):
        wint[:, lanes(n * tall, tall)] = win[n].reshape(tall, 2 * ff).T

    for n in range(planes - 1):
        source = lax.rem(me + planes - 1 - n, planes)
        remote(metas.at[source], metas.at[source], me_s.at[n], me_r.at[n], kp).wait_recv()
    for load in loads[1:]:
        load.wait()
    gather.other_core(0)
    dispatch(0)
    work(0, 1)
    back(0, 0)
    gather.first()
    gather.second()
    gather.other_core(1)
    dispatch(1)
    gather.other_core(2)
    dispatch(2)
    work(1, 2)
    gather.third()
    back(1, 0)
    back(2, 1)
    gather.other_core(3)
    gather.done()
    dispatch(3)
    plane.fold(1)
    plane.fold(2)
    plane.near()
    work(3, 1)
    back(3, 0)
    plane.fold(3)
    plane.given()
    plane.across()


    @pl.loop(0, ctx)
    def _(n):
        tile = dot_tn(ds[:, lanes(n * tall, tall)], hid[...]).astype(BF16)
        for d in range(gwdn.shape[1]):
            gwdn[n, d] = tile[d * gwdn.shape[2] : (d + 1) * gwdn.shape[2]]

    line.step(1)
    plane.fold(0)

    @pl.loop(0, width // step)
    def _(n):
        cols = lanes(n * step, step)
        ds[:, cols] = dot_nt(hid[...], wdn[cols, :]).astype(BF16)

    def returned(q):
        base = chips[q]
        for kk in range(2):
            p = base + kk
            hot = spots(p)
            rows = ds[pl.ds(q * 2 * cap + kk * cap, cap), :]
            ggs[p, 0:1, :] = jnp.sum(hot * dot_nt(rows, cotb[p]), axis=0, keepdims=True)
            scaled = (rows.astype(F32) * gate_of(p, hot)).astype(BF16)
            cotb[p] = dot_tn(hot.astype(BF16), scaled).astype(BF16)
        outs.give(q, cotb.at[base + 1 - k])

    returned(1)
    returned(2)
    plane.turn()
    returned(3)
    returned(0)
    outs.fold(1)
    outs.fold(2)
    outs.near()
    outs.fold(3)
    outs.across()
    ggr[me] = ggs[me]
    for n, (other, dev) in enumerate(others):
        remote(ggs.at[other], ggr.at[me], gg_s.at[n], gg_r.at[n], dev).start()
    line.step(2)
    outs.fold(0)

    def gate_up(at, size):
        @pl.loop(0, ctx)
        def _(n):
            tile = dot_tn(xs[:, lanes(n * tall, tall)], igs[:, pl.ds(at, size)]).astype(BF16)
            win[n, :, :, pl.ds(at, size)] = tile.reshape(gwdn.shape[1], gwdn.shape[2], size)

    gate_up(0, some)
    first_line.step(1)
    rest = 2 * ff - some
    gate_up(some, rest // 2)
    gate_up(some + rest // 2, rest // 2)
    gwin_copy = pltpu.make_async_copy(win.at[:, :, :, pl.ds(some, rest)], gwin_h, load_sem.at[0])
    gwin_copy.start()
    line.step(3)
    outs.turn()
    first_line.step(2)
    for rows, terms in outs.total():
        output[rows, :] = (pg_out[rows, :] + summed(terms)).astype(BF16)
    early = [pltpu.make_async_copy(output, output_h, load_sem.at[1])]
    early[0].start()
    for rows, terms in plane.total():
        pg_out[rows, :] = summed(terms)
    early.append(pltpu.make_async_copy(pg_out, pg_h, load_sem.at[2]))
    early[1].start()
    for n in range(planes - 1):
        source = lax.rem(me + planes - 1 - n, planes)
        remote(ggr.at[source], ggr.at[source], gg_s.at[n], gg_r.at[n], kp).wait_recv()
    for p in range(planes):
        gg_out[p : p + 1, :] = ggr[p, 0:1, :]
    first_line.step(3)
    line.final()
    first_line.final()
    gwin_copy.wait()
    for copy in early:
        copy.wait()
    for n, (other, dev) in enumerate(others):
        remote(meta.at[other], metas.at[other], me_s.at[n], me_r.at[n], dev).wait_send()
        remote(ggs.at[other], ggr.at[other], gg_s.at[n], gg_r.at[n], dev).wait_send()
    plane.done()
    outs.done()
    line.done()
    first_line.done()


def run_ffn(cap, ffn, resid, cot_all, meta, win, wdn, parts, some):
    tok, width = ffn.shape
    ff = wdn.shape[2]
    planes = cot_all.shape[0]
    ctx = win.shape[0]
    rows = planes * cap
    piece = width // (ctx * parts)
    win = win.reshape(ctx, ctx, parts, piece, 2 * ff)
    vm, anyspace = pl.BlockSpec(memory_space=pltpu.VMEM), pl.BlockSpec(memory_space=pl.ANY)
    shape = jax.ShapeDtypeStruct
    dma = pltpu.SemaphoreType.DMA
    return pl.pallas_call(
        functools.partial(ffn_kernel, cap),
        out_shape=(
            shape((tok, width), BF16),
            shape((tok, width), F32),
            shape((planes, tok), F32),
            shape((ctx, parts, piece, 2 * ff - some), BF16),
            shape((ctx, piece, ff + some), BF16),
        ),
        in_specs=[anyspace, anyspace, anyspace, vm, anyspace, anyspace],
        out_specs=(anyspace, anyspace, vm, anyspace, vm),
        scratch_shapes=[
            pltpu.VMEM((planes, tok, width), BF16),
            pltpu.VMEM((planes, 8, tok), F32),
            pltpu.VMEM((planes, tok, width), BF16),
            pltpu.VMEM((ctx, parts, piece, 2 * ff), BF16),
            pltpu.VMEM((width, ff), BF16),
            pltpu.VMEM((rows, width), BF16),
            pltpu.VMEM((rows, width), BF16),
            pltpu.VMEM((rows, ff), BF16),
            pltpu.VMEM((rows, 2 * ff), BF16),
            pltpu.VMEM((4 * cap, width), BF16),
            pltpu.VMEM((planes, 8, tok), F32),
            pltpu.VMEM((planes, 8, tok), F32),
            pltpu.VMEM((2 * ff, width), BF16),
            pltpu.VMEM((ctx, parts, piece, ff), BF16),
            dma((5,)),
            dma((GATHER_COPIES,)),
            dma((GATHER_COPIES,)),
            dma((planes - 1,)),
            dma((planes - 1,)),
            dma((planes - 1,)),
            dma((planes - 1,)),
            dma((10,)),
            dma((10,)),
        ]
        + plane_scratch(tok, width)
        + line_scratch(parts, (ctx, piece, ff))
        + line_scratch(parts, (ctx, piece, some))
        + [pltpu.VMEM((tok, width), BF16), pltpu.VMEM((tok, width), F32)],
        compiler_params=pltpu.CompilerParams(
            collective_id=1, has_side_effects=True, vmem_limit_bytes=63 * 2**20
        ),
        cost_estimate=pl.CostEstimate(flops=25 * 10**9, bytes_accessed=50 * 10**6, transcendentals=10**6),
    )(ffn, resid, cot_all, meta, win, wdn)


def back_kernel(
    span,
    meta,
    gg,
    lse,
    trig,
    attended,
    router_t,
    gain_two,
    gain_one,
    reduced,
    kv_h,
    queries_h,
    normed_h,
    resid_h,
    cot_h,
    pg_h,
    ffn_in_h,
    hidden_h,
    wout_h,
    wqkv_h,
    gwin_h,
    input_grad,
    qkv_out,
    proj_out,
    one_out,
    two_out,
    ffn_out,
    *scratch,
):
    wide_f, back, low, attg, mixed, weights, gwin, send, bsend, smalls, total, out_red = scratch[:12]
    mask, delta, kt, dk, dv, kvs, kvr = scratch[12:19]
    load_sem, kv_s, kv_r = scratch[19:22]
    p_zcr, p_zk, p_rx, p_ry, p_s, p_r = scratch[22:28]
    a_rx, a_ry, a_s, a_r = scratch[28:32]
    e_refs, b_refs = scratch[32:38], scratch[38:44]
    qkv_refs, proj_refs = scratch[44:47], scratch[47:50]
    one_refs, two_refs = scratch[50:57], scratch[57:64]
    f_s, f_r, kv, queries, normed = scratch[64:]
    spot = Spot()
    c, k, z, ctx = spot.c, spot.k, spot.z, spot.ctx
    tok, width = attended.shape
    cols = one_out.shape[2]
    block, piece = out_red.shape[0], proj_out.shape[0]
    heads_kv = KV_HEADS
    half_head = HEAD // 2
    n_experts = meta.shape[0]
    kv_wide = mixed.shape[1] - width
    step = 256

    def load(src, dst, i):
        copy = pltpu.make_async_copy(src, dst, load_sem.at[i])
        copy.start()
        return copy

    gwin_load = load(gwin_h, gwin, 0)
    early = [
        load(resid_h, wide_f, 1),
        load(pg_h, back, 2),
        load(cot_h, input_grad, 3),
        load(ffn_in_h, attg, 4),
    ]
    wout_load = load(wout_h, weights.at[:, pl.ds(0, width)], 5)
    later = [load(kv_h, kv, 6), load(queries_h, queries, 7), load(normed_h, normed, 8)]
    greet([spot.xp, spot.yp, spot.kp, spot.yk], spot.along())
    for n in range(1, ctx):
        cc = lax.rem(c + n, ctx)
        remote(reduced.at[cc], ffn_out.at[c], f_s.at[n - 1], f_r.at[n - 1], (spot.e, cc, z)).start()
    ffn_out[c] = reduced[c]
    one = ExpertLine(spot, gwin, 0, cols, *one_refs)
    two = ExpertLine(spot, gwin, cols, cols, *two_refs)
    proj_plane = plane_of(spot, p_zcr, p_zk, p_rx, p_ry, p_s, p_r, low=BACK_LOW)
    half_wide = width // 2
    cut = pl.ds(0, half_wide)
    early_plane = plane_of(spot, *e_refs, low=BACK_LOW)
    late_plane = plane_of(
        spot, p_zcr.at[:, :, cut], p_zk.at[:, :, cut], a_rx, a_ry, a_s, a_r, low=BACK_LOW
    )
    rest_plane = plane_of(spot, *b_refs, low=BACK_LOW)

    def shared_line(ref, refs):
        def own(d):
            return ref.at[rows_at(d * piece, piece)]

        def adder(came, d):
            came[...] = plus(came[...], own(d)[...])

        return Line(spot, own, adder, *refs)

    qkv_line, proj_line = shared_line(total, qkv_refs), shared_line(out_red, proj_refs)

    def put_shared(to, ref, came):
        to[...] = plus(ref[rows_at(z * piece, piece)], *(x[...] for x in came))

    mine, theirs = rows_at(k * block, block), rows_at((1 - k) * block, block)
    gwin_load.wait()
    one.step(1)

    for copy in early:
        copy.wait()
    gate = jnp.concatenate([meta[g, 1:2, :] for g in range(n_experts)], axis=0)
    seen = gate * gg[...]
    mix = seen - gate * jnp.sum(seen, axis=0, keepdims=True)
    mix = jnp.concatenate([mix, jnp.zeros((HEAD - n_experts, tok), F32)], axis=0)
    logit_t = mix.astype(BF16)
    r = wide_f[...]
    inv = lax.rsqrt(jnp.mean(r * r, axis=-1, keepdims=True) + NORM_EPS)
    plain = r * inv
    ffn_grad = back[...] + dot_tn(logit_t[:n_experts], router_t[...])
    gain_row = jnp.sum(ffn_grad * plain, axis=0, keepdims=True)
    scaled = ffn_grad * gain_two[...]
    grad = input_grad[...].astype(F32) + inv * (
        scaled - plain * jnp.mean(scaled * plain, axis=-1, keepdims=True)
    )
    back[...] = grad
    low[...] = grad.astype(BF16)
    lane = lax.broadcasted_iota(jnp.int32, (width, HEAD), 1)
    routed = dot_tn(attg[...], logit_t.T)
    gain_col = jnp.broadcast_to(gain_row, (HEAD, width)).T
    smalls[...] = jnp.where(lane == n_experts, gain_col, routed).astype(BF16)

    for q in (3, 1, 2, 0):
        at = lanes(spot.chips[q] * block, 2 * block)
        send[q] = dot_tn(low[:, at], attended[...]).astype(BF16)
        proj_plane.give(q, send.at[q, theirs])
    wout_load.wait()

    @pl.loop(0, width // step)
    def _(n):
        at = lanes(n * step, step)
        attg[:, at] = dot(low[...], weights[:, at]).astype(BF16)

    wqkv_load = load(wqkv_h, weights, 5)
    hidden_load = load(hidden_h, low, 1)

    def start_plane(plane, at):
        plane.fold(3, send[3, mine, at])
        plane.across()
        plane.fold(1, send[1, mine, at])
        plane.fold(2, send[2, mine, at])
        plane.near()
        plane.fold(0, send[0, mine, at])

    def qkv_tiles(plane, at):
        for q in (3, 1, 2, 0):
            rows = lanes(spot.chips[q] * block, 2 * block)
            send[q, :, at] = dot_tn(normed[:, rows], mixed[:, at]).astype(BF16)
            plane.give(q, send.at[q, theirs, at])

    start_plane(proj_plane, pl.ds(0, width))

    for copy in later:
        copy.wait()

    seq = kv.shape[0]
    spans = span.shape[1]
    size = seq // spans
    per = spans // ctx
    along_q = lax.broadcasted_iota(jnp.int32, (size, tok), 1)
    q_pos = jnp.where(along_q < size, span[0, c * per] * size, (span[0, c * per + 1] - 1) * size) + along_q
    for s in range(spans):
        k_pos = span[0, s] * size + lax.broadcasted_iota(jnp.int32, (size, tok), 0)
        mask[s * size : (s + 1) * size, :] = jnp.where(k_pos <= q_pos, 0.0, MASKED)

    lane_h = lax.broadcasted_iota(jnp.int32, (tok, HEAD), 1)
    deltas = jnp.zeros((tok, HEAD), F32)
    for h in range(HEADS):
        at = slice(h * HEAD, (h + 1) * HEAD)
        term = jnp.sum(attg[:, at].astype(F32) * attended[:, at].astype(F32), axis=-1, keepdims=True)
        deltas = jnp.where(lane_h == h, term, deltas)
    delta[...] = deltas.T
    for g in range(heads_kv):
        kt[g] = kv[:, g * HEAD : (g + 1) * HEAD].astype(F32).T.astype(BF16)

    cosine, sine = trig[0], trig[1]

    def unrotate(w):
        return w * cosine - pltpu.roll(w, half_head, 1) * sine

    def head(g, h):
        at = lanes(h * HEAD, HEAD)
        k_at = slice(g * HEAD, (g + 1) * HEAD)
        v_at = slice((heads_kv + g) * HEAD, (heads_kv + g + 1) * HEAD)
        q, a = queries[:, at], attg[:, at]
        soft = jnp.exp(dot_nt(kv[:, k_at], q) + mask[...] - lse[pl.ds(h, 1), :])
        prob = dot_nt(kv[:, v_at], a)
        score = (soft * (prob - delta[pl.ds(h, 1), :])).astype(BF16)
        mixed[:, at] = (unrotate(dot(kt[g], score).T) * HEAD**-0.5).astype(BF16)
        dk[...] += dot(score, q)
        dv[...] += dot(soft.astype(BF16), a)

    def heads(g, first, count):
        @pl.loop(first, first + count)
        def _(h):
            head(g, h)

    def clear():
        dk[...] = jnp.zeros(dk.shape, F32)
        dv[...] = jnp.zeros(dv.shape, F32)

    flip_c = lax.rem(c + 2, ctx)
    near_c = c + 1 - 2 * k
    across_c = lax.rem(near_c + 2, ctx)

    def kv_copy(g, src, i, dev):
        return remote(src, kvr.at[g, i], kv_s.at[g, i], kv_r.at[g, i], dev)

    def send_kv(g):
        for cc in range(ctx):
            rows = slice(cc * tok, (cc + 1) * tok)
            kvs[g, cc, :, :HEAD] = dk[rows, :].astype(BF16)
            kvs[g, cc, :, HEAD:] = dv[rows, :].astype(BF16)
        kv_copy(g, kvs.at[g, across_c], 1, spot.kp).start()
        kv_copy(g, kvs.at[g, near_c], 0, spot.kp).start()

    def pass_kv(g):
        kv_copy(g, kvs.at[g, across_c], 1, spot.kp).wait_recv()
        kvs[g, flip_c] = plus(kvs[g, flip_c], kvr[g, 1])
        kv_copy(g, kvs.at[g, flip_c], 2, spot.yp).start()

    clear()
    heads(0, 0, 2)
    one.step(2)
    heads(0, 2, 4)
    send_kv(0)
    clear()
    proj_plane.turn()
    proj_plane.given()
    qkv_tiles(early_plane, pl.ds(0, half_wide))
    heads(1, 6, 1)
    start_plane(early_plane, pl.ds(0, half_wide))
    pass_kv(0)
    one.step(3)
    two.step(1)
    heads(1, 7, 2)
    heads(1, 9, 3)
    send_kv(1)
    pass_kv(1)
    early_plane.turn()
    for rows, terms in proj_plane.total():
        out_red[rows, :] = summed(terms).astype(BF16)
    proj_line.step(1)
    proj_plane.done()
    for g in range(heads_kv):
        kv_copy(g, kvs.at[g, near_c], 0, spot.kp).wait_recv()
        kv_copy(g, kvs.at[g, flip_c], 2, spot.yp).wait_recv()
        own = kvs[g, c].astype(F32) + kvr[g, 0].astype(F32) + kvr[g, 2].astype(F32)
        at = width + g * HEAD
        mixed[:, at : at + HEAD] = unrotate(own[:, :HEAD]).astype(BF16)
        at = width + (heads_kv + g) * HEAD
        mixed[:, at : at + HEAD] = own[:, HEAD:].astype(BF16)

    qkv_tiles(late_plane, pl.ds(half_wide, half_wide))
    start_plane(late_plane, pl.ds(half_wide, half_wide))
    proj_line.step(2)
    wqkv_load.wait()

    @pl.loop(0, width // step)
    def _(n):
        at = lanes(n * step, step)
        wide_f[:, at] = dot_nt(mixed[...], weights[at, :])

    two.step(2)
    hidden_load.wait()
    x = low[...].astype(F32)
    inv = lax.rsqrt(jnp.mean(x * x, axis=-1, keepdims=True) + NORM_EPS)
    plain = x * inv
    ng = wide_f[...]
    gain_row = jnp.sum(ng * plain, axis=0, keepdims=True)
    scaled = ng * gain_one[...]
    input_grad[...] = (
        back[...] + inv * (scaled - plain * jnp.mean(scaled * plain, axis=-1, keepdims=True))
    ).astype(BF16)
    lane = lax.broadcasted_iota(jnp.int32, (width, HEAD), 1)
    gain_col = jnp.broadcast_to(gain_row, (HEAD, width)).T
    smalls[...] = jnp.where(lane == HEAD - 1, gain_col, smalls[...].astype(F32)).astype(BF16)
    for q in (3, 1, 2, 0):
        at = lanes(spot.chips[q] * block, 2 * block)
        bsend[q, :, :kv_wide] = dot_tn(normed[:, at], mixed[:, width:]).astype(BF16)
        bsend[q, :, kv_wide:] = smalls[rows_at(spot.chips[q] * block, 2 * block), :]
        rest_plane.give(q, bsend.at[q, theirs])
    rest_plane.fold(3, bsend[3, mine])
    rest_plane.across()
    rest_plane.fold(1, bsend[1, mine])
    rest_plane.fold(2, bsend[2, mine])
    rest_plane.near()
    rest_plane.fold(0, bsend[0, mine])
    late_plane.turn()
    rest_plane.turn()
    two.step(3)
    one.final()
    proj_line.step(3)
    for rows, terms in early_plane.total():
        total[rows, :half_wide] = summed(terms).astype(BF16)
    for rows, terms in late_plane.total():
        total[rows, half_wide:width] = summed(terms).astype(BF16)
    for rows, terms in rest_plane.total():
        total[rows, width:] = summed(terms).astype(BF16)
    qkv_line.step(1)
    one.done(one_out)
    qkv_line.step(2)
    two.final()
    proj_line.final(lambda *came: put_shared(proj_out, out_red, came))
    qkv_line.step(3)
    proj_line.done()
    early_plane.done()
    late_plane.done()
    rest_plane.done()
    for g in range(heads_kv):
        kv_copy(g, kvs.at[g, near_c], 0, spot.kp).wait_send()
        kv_copy(g, kvs.at[g, across_c], 1, spot.kp).wait_send()
        kv_copy(g, kvs.at[g, flip_c], 2, spot.yp).wait_send()
    qkv_line.final(lambda *came: put_shared(qkv_out, total, came))
    qkv_line.done()
    for n in range(1, ctx):
        cc = lax.rem(c + ctx - n, ctx)
        got = remote(ffn_out.at[cc], ffn_out.at[cc], f_s.at[n - 1], f_r.at[n - 1], spot.kp)
        got.wait_recv()
        got.wait_send()
    two.done(two_out)


def run_back(
    span, meta, gg, lse, trig, attended, router_t, gain_two, gain_one, reduced, kv, queries, normed,
    resid, cot, pg, ffn_in, hidden, wout, wqkv, gwin,
):
    tok, width = attended.shape
    seq, kv_cols = kv.shape
    planes = meta.shape[0]
    ctx, parts, rows, wide = gwin.shape
    cols = wide // 2
    block = width // planes
    piece = block // parts
    rest = kv_cols + HEAD
    vm, anyspace = pl.BlockSpec(memory_space=pltpu.VMEM), pl.BlockSpec(memory_space=pl.ANY)
    sm = pl.BlockSpec(memory_space=pltpu.SMEM)
    shape = jax.ShapeDtypeStruct
    dma = pltpu.SemaphoreType.DMA
    return pl.pallas_call(
        back_kernel,
        out_shape=(
            shape((tok, width), BF16),
            shape((piece, width + rest), BF16),
            shape((piece, width), BF16),
            shape((ctx, rows, cols), BF16),
            shape((ctx, rows, cols), BF16),
            shape(reduced.shape, BF16),
        ),
        in_specs=[sm] + [vm] * 9 + [anyspace] * 11,
        out_specs=(vm,) * 6,
        scratch_shapes=[
            pltpu.VMEM((tok, width), F32),
            pltpu.VMEM((tok, width), F32),
            pltpu.VMEM((tok, width), BF16),
            pltpu.VMEM((tok, width), BF16),
            pltpu.VMEM((tok, width + kv_cols), BF16),
            pltpu.VMEM(wqkv.shape, BF16),
            pltpu.VMEM(gwin.shape, BF16),
            pltpu.VMEM((4, 2 * block, width), BF16),
            pltpu.VMEM((4, 2 * block, rest), BF16),
            pltpu.VMEM((width, HEAD), BF16),
            pltpu.VMEM((block, width + rest), BF16),
            pltpu.VMEM((block, width), BF16),
            pltpu.VMEM((seq, tok), F32),
            pltpu.VMEM((HEAD, tok), F32),
            pltpu.VMEM((KV_HEADS, HEAD, seq), BF16),
            pltpu.VMEM((seq, HEAD), F32),
            pltpu.VMEM((seq, HEAD), F32),
            pltpu.VMEM((KV_HEADS, ctx, tok, 2 * HEAD), BF16),
            pltpu.VMEM((KV_HEADS, 3, tok, 2 * HEAD), BF16),
            dma((9,)),
            dma((KV_HEADS, 3)),
            dma((KV_HEADS, 3)),
        ]
        + plane_scratch(block, width, BACK_LOW)
        + plane_scratch(block, width // 2, BACK_LOW)[2:]
        + plane_scratch(block, width // 2, BACK_LOW)
        + plane_scratch(block, rest, BACK_LOW)
        + line_scratch(parts, (piece, width + rest))
        + line_scratch(parts, (piece, width))
        + expert_scratch(ctx, parts, rows, cols)
        + expert_scratch(ctx, parts, rows, cols)
        + [dma((ctx - 1,)), dma((ctx - 1,))]
        + [pltpu.VMEM(kv.shape, BF16), pltpu.VMEM(queries.shape, BF16), pltpu.VMEM(normed.shape, BF16)],
        compiler_params=pltpu.CompilerParams(
            collective_id=2, has_side_effects=True, vmem_limit_bytes=63 * 2**20
        ),
        cost_estimate=pl.CostEstimate(flops=12 * 10**9, bytes_accessed=60 * 10**6, transcendentals=4 * 10**6),
    )(
        span, meta, gg, lse, trig, attended, router_t, gain_two, gain_one, reduced, kv, queries, normed,
        resid, cot, pg, ffn_in, hidden, wout, wqkv, gwin,
    )


def finish_kernel(
    n_experts,
    output_h,
    input_h,
    qkv_h,
    proj_h,
    one_h,
    two_h,
    down_h,
    output,
    input_grad,
    gain_one,
    gain_two,
    qkv,
    proj,
    router,
    inner,
    down,
    low_qkv,
    low_proj,
    low_one,
    low_two,
    low_down,
    low_out,
    low_in,
    inner_full,
    down_full,
    sem,
    out_sem,
):
    whole = []
    loads = [
        pltpu.make_async_copy(src, dst, sem.at[i])
        for i, (src, dst) in enumerate(
            (
                (down_h, low_down),
                (one_h, low_one),
                (two_h, low_two),
                (qkv_h, low_qkv),
                (proj_h, low_proj),
                (output_h, low_out),
                (input_h, low_in),
            )
        )
    ]
    for copy in loads:
        copy.start()
    loads[0].wait()
    ff = down.shape[2]
    down_full[...] = low_down[:, :, :ff].astype(F32)
    at = low_down.shape[2] - ff
    inner_full[:, :, :at] = low_down[:, :, ff:].astype(F32)
    whole.append(pltpu.make_async_copy(down_full, down, out_sem.at[2]))
    whole[-1].start()
    for load, low in zip(loads[1:3], (low_one, low_two)):
        load.wait()
        size = low.shape[2]
        inner_full[:, :, at : at + size] = low[...].astype(F32)
        at += size
    whole.append(pltpu.make_async_copy(inner_full, inner, out_sem.at[3]))
    whole[-1].start()
    for i, (low, to) in enumerate(((low_out, output), (low_in, input_grad))):
        loads[5 + i].wait()
        whole.append(pltpu.make_async_copy(low, to, out_sem.at[i]))
        whole[-1].start()
    for load in loads[3:5]:
        load.wait()
    wide = qkv.shape[1]
    qkv[...] = low_qkv[:, :wide].astype(F32)
    proj[...] = low_proj[...].astype(F32)
    small = low_qkv[:, wide:].astype(F32)
    piece = small.shape[0]
    same = lax.broadcasted_iota(jnp.int32, (piece, piece), 0) == lax.broadcasted_iota(
        jnp.int32, (piece, piece), 1
    )

    def column(at):
        return jnp.sum(jnp.where(same, small[:, at : at + 1], 0.0), axis=0, keepdims=True)

    gain_one[...] = column(HEAD - 1)[0]
    gain_two[...] = column(n_experts)[0]
    for at in range(n_experts):
        router[at : at + 1, :] = column(at)
    for copy in whole:
        copy.wait()


def run_finish(n_experts, output, input_grad, qkv, proj, one, two, down):
    piece, width = proj.shape
    ctx, rows, cols = one.shape
    ff = (down.shape[2] + 2 * cols) // 3
    shape = jax.ShapeDtypeStruct
    vm, anyspace = pl.BlockSpec(memory_space=pltpu.VMEM), pl.BlockSpec(memory_space=pl.ANY)
    return pl.pallas_call(
        functools.partial(finish_kernel, n_experts),
        out_shape=(
            shape(output.shape, BF16),
            shape(input_grad.shape, BF16),
            shape((piece,), F32),
            shape((piece,), F32),
            shape((piece, qkv.shape[1] - HEAD), F32),
            shape((piece, width), F32),
            shape((n_experts, piece), F32),
            shape((ctx, rows, 2 * ff), F32),
            shape((ctx, rows, ff), F32),
        ),
        in_specs=[anyspace] * 7,
        out_specs=(anyspace, anyspace, vm, vm, vm, vm, vm, anyspace, anyspace),
        scratch_shapes=[pltpu.VMEM(x.shape, BF16) for x in (qkv, proj, one, two, down, output, input_grad)]
        + [
            pltpu.VMEM((ctx, rows, 2 * ff), F32),
            pltpu.VMEM((ctx, rows, ff), F32),
            pltpu.SemaphoreType.DMA((7,)),
            pltpu.SemaphoreType.DMA((4,)),
        ],
        compiler_params=pltpu.CompilerParams(vmem_limit_bytes=56 * 2**20),
    )(output, input_grad, qkv, proj, one, two, down)


def local(
    hidden_in,
    span_order,
    expert_ids,
    priority,
    gain_attn,
    qkv_weight,
    out_weight,
    gain_ffn,
    router,
    in_weight,
    down_weight,
    cotangent,
):
    _, tok_rows, width = hidden_in.shape
    ctx, parts = lax.axis_size("context"), lax.axis_size("dp")
    planes = ctx * lax.axis_size("expert")
    n_experts = router.shape[1]
    top_k = expert_ids.shape[2]
    capacity = (9 * tok_rows * top_k + 8 * n_experts - 1) // (8 * n_experts)
    ff = down_weight.shape[2]
    half_freqs = ROPE_BASE ** (np.arange(HEAD // 2) * (-2.0 / HEAD))
    freqs = np.concatenate([half_freqs, half_freqs])[None].astype(np.float32)
    router_t = router.T
    hidden, cot = hidden_in[0], cotangent[0]
    normed, queries, kv, lse, attended, resid, ffn_in, trig, meta, cot_all = run_front(
        capacity,
        span_order,
        hidden,
        cot,
        gain_attn,
        freqs,
        gain_ffn,
        router_t,
        expert_ids[0].T,
        priority[0].T,
        qkv_weight,
        out_weight,
        ctx,
        planes,
    )
    output, pair_sum, gate_grad, gwin, reduced = run_ffn(
        capacity, ffn_in, resid, cot_all, meta, in_weight, down_weight, parts, ff // 3
    )
    input_grad, qkv_sum, proj_sum, in_one, in_two, ffn_sums = run_back(
        span_order,
        meta,
        gate_grad,
        lse,
        trig,
        attended,
        router_t,
        gain_ffn,
        gain_attn,
        reduced,
        kv,
        queries,
        normed,
        resid,
        cot,
        pair_sum,
        ffn_in,
        hidden,
        out_weight,
        qkv_weight,
        gwin,
    )
    output, input_grad, gain_one, gain_two, qkv_grad, proj_grad, router_grad, inner_grad, down_grad = run_finish(
        n_experts, output, input_grad, qkv_sum, proj_sum, in_one, in_two, ffn_sums
    )
    return (
        output[None],
        input_grad[None],
        gain_one,
        qkv_grad,
        proj_grad,
        gain_two,
        router_grad.T,
        inner_grad,
        down_grad,
    )


def general(
    hidden_in,
    span_order,
    expert_ids,
    priority,
    gain_attn,
    qkv_weight,
    out_weight,
    gain_ffn,
    router,
    in_weight,
    down_weight,
    cotangent,
):
    tok_rows = hidden_in.shape[1]
    width = hidden_in.shape[2]
    contexts = lax.axis_size("context")
    span_len = tok_rows // 2
    seq_len = tok_rows * contexts
    group = HEADS // KV_HEADS
    q_cols = HEADS * HEAD
    kv_cols = KV_HEADS * HEAD
    scale = HEAD ** (-0.5)
    local_experts = in_weight.shape[0]
    n_experts = local_experts * lax.axis_size("expert")
    top_k = expert_ids.shape[2]
    capacity = (9 * tok_rows * top_k + 8 * n_experts - 1) // (8 * n_experts)
    ff_width = down_weight.shape[2]
    seq_spans = span_order[0]
    stored = jnp.arange(seq_len) // span_len
    all_pos = (seq_spans[stored] * span_len + jnp.arange(seq_len) % span_len).astype(jnp.float32)
    my_pos = lax.dynamic_slice_in_dim(all_pos, lax.axis_index("context") * tok_rows, tok_rows)
    cosine, sine = rope_tables(my_pos, HEAD)
    inputs = hidden_in[0].astype(jnp.float32)
    inv_one = lax.rsqrt(jnp.mean(inputs * inputs, axis=-1, keepdims=True) + NORM_EPS)
    plain_one = inputs * inv_one
    normed = (plain_one * gain_attn).astype(jnp.bfloat16)
    mixed = jnp.dot(normed, qkv_weight, preferred_element_type=jnp.float32)
    queries = (
        rotate(mixed[:, :q_cols].reshape(tok_rows, HEADS, HEAD), cosine, sine) * scale
    ).astype(jnp.bfloat16)
    keys = rotate(
        mixed[:, q_cols : q_cols + kv_cols].reshape(tok_rows, KV_HEADS, HEAD), cosine, sine
    ).astype(jnp.bfloat16)
    values = mixed[:, q_cols + kv_cols :].reshape(tok_rows, KV_HEADS, HEAD).astype(jnp.bfloat16)
    grouped = queries.reshape(tok_rows, KV_HEADS, group, HEAD)

    def key_scores(key_piece):
        scores = jnp.einsum(
            "qkgd,skd->kgqs", grouped, key_piece, preferred_element_type=jnp.float32
        )
        visible = all_pos[None, None, None, :] <= my_pos[None, None, :, None]
        return (jnp.where(visible, scores, MASKED), visible)

    running = jnp.full((KV_HEADS, group, tok_rows), MASKED, jnp.float32)
    key_piece = lax.all_gather(keys, "context", axis=0, tiled=True)
    value_piece = lax.all_gather(values, "context", axis=0, tiled=True)
    scores, visible = key_scores(key_piece)
    newest = jnp.maximum(running, jnp.max(scores, axis=-1))
    weights = jnp.where(visible, jnp.exp(scores - newest[..., None]), 0.0)
    totals = jnp.sum(weights, axis=-1)
    accum = jnp.einsum(
        "kgqs,skd->kgqd",
        weights.astype(jnp.bfloat16),
        value_piece,
        preferred_element_type=jnp.float32,
    )
    running, totals, accum = (newest, totals, accum)
    log_total = running + jnp.log(totals)
    attended = (
        (accum / totals[..., None])
        .transpose(2, 0, 1, 3)
        .reshape(tok_rows, q_cols)
        .astype(jnp.bfloat16)
    )
    resid = inputs + jnp.einsum(
        "rh,dh->rd", attended, out_weight, preferred_element_type=jnp.float32
    )
    inv_two = lax.rsqrt(jnp.mean(resid * resid, axis=-1, keepdims=True) + NORM_EPS)
    plain_two = resid * inv_two
    ffn_in = (plain_two * gain_ffn).astype(jnp.bfloat16)
    logits = jnp.dot(ffn_in, router, preferred_element_type=jnp.float32)
    token_ids = expert_ids[0]
    gates = softmax_last(jnp.take_along_axis(logits, token_ids, axis=1))
    slots = route(token_ids, priority[0], n_experts, capacity)
    pair_rows = jnp.repeat(ffn_in, top_k, axis=0)
    send_rows = (
        jnp.zeros((n_experts * capacity, width), jnp.bfloat16).at[slots].set(pair_rows, mode="drop")
    )
    received = lax.all_to_all(
        send_rows.reshape(n_experts, capacity, width),
        "expert",
        split_axis=0,
        concat_axis=1,
        tiled=True,
    )
    inner = jnp.einsum("erd,edf->erf", received, in_weight, preferred_element_type=jnp.float32)
    gate_part = inner[..., :ff_width]
    up_part = inner[..., ff_width:]
    sigma = 1.0 / (1.0 + jnp.exp(-gate_part))
    activated = gate_part * sigma
    hidden = (activated * up_part).astype(jnp.bfloat16)
    expert_out = jnp.einsum(
        "erf,edf->erd", hidden, down_weight, preferred_element_type=jnp.float32
    ).astype(jnp.bfloat16)
    returned = lax.all_to_all(
        expert_out, "expert", split_axis=1, concat_axis=0, tiled=True
    ).reshape(n_experts * capacity, width)
    padded = jnp.concatenate([returned, jnp.zeros((1, width), jnp.bfloat16)], axis=0)
    picked = padded[slots].reshape(tok_rows, top_k, width)
    output = (resid + jnp.sum(gates[:, :, None] * picked, axis=1)).astype(jnp.bfloat16)
    cot_low = cotangent[0]
    cot_full = cot_low.astype(jnp.float32)
    gate_grad = jnp.einsum("rkd,rd->rk", picked, cot_low, preferred_element_type=jnp.float32)
    ret_grad = (
        (gates[:, :, None] * cot_full[:, None, :])
        .astype(jnp.bfloat16)
        .reshape(tok_rows * top_k, width)
    )
    send_grad = (
        jnp.zeros((n_experts * capacity, width), jnp.bfloat16).at[slots].set(ret_grad, mode="drop")
    )
    received_grad = lax.all_to_all(
        send_grad.reshape(n_experts, capacity, width),
        "expert",
        split_axis=0,
        concat_axis=1,
        tiled=True,
    )
    hid_grad = jnp.einsum(
        "erd,edf->erf", received_grad, down_weight, preferred_element_type=jnp.float32
    )
    slope = sigma * (1.0 + gate_part * (1.0 - sigma))
    inner_grad = jnp.concatenate(
        [hid_grad * up_part * slope, hid_grad * activated], axis=-1
    ).astype(jnp.bfloat16)
    row_grad = jnp.einsum(
        "erf,edf->erd", inner_grad, in_weight, preferred_element_type=jnp.float32
    ).astype(jnp.bfloat16)
    part_rows = received
    expert_in = (
        lax.psum_scatter(
            jnp.einsum(
                "erd,erf->def", part_rows, inner_grad, preferred_element_type=jnp.float32
            ).astype(jnp.bfloat16),
            ("context", "dp"),
            scatter_dimension=0,
            tiled=True,
        )
        .astype(jnp.float32)
        .transpose(1, 0, 2)
    )
    part_rows = received_grad
    expert_down = (
        lax.psum_scatter(
            jnp.einsum(
                "erd,erf->def", part_rows, hidden, preferred_element_type=jnp.float32
            ).astype(jnp.bfloat16),
            ("context", "dp"),
            scatter_dimension=0,
            tiled=True,
        )
        .astype(jnp.float32)
        .transpose(1, 0, 2)
    )
    back_rows = lax.all_to_all(row_grad, "expert", split_axis=1, concat_axis=0, tiled=True).reshape(
        n_experts * capacity, width
    )
    back_padded = jnp.concatenate([back_rows, jnp.zeros((1, width), jnp.bfloat16)], axis=0)
    pair_grad = back_padded[slots].reshape(tok_rows, top_k, width)
    mix_grad = gates * (gate_grad - jnp.sum(gates * gate_grad, axis=-1, keepdims=True))
    matches = token_ids[:, :, None] == jnp.arange(n_experts)[None, None, :]
    logit_grad = jnp.sum(jnp.where(matches, mix_grad[:, :, None], 0.0), axis=1).astype(jnp.bfloat16)
    router_part = jnp.einsum("rd,re->de", ffn_in, logit_grad, preferred_element_type=jnp.float32)
    ffn_grad = jnp.sum(pair_grad.astype(jnp.float32), axis=1) + jnp.einsum(
        "re,de->rd", logit_grad, router, preferred_element_type=jnp.float32
    )
    gain_ffn_part = jnp.sum(ffn_grad * plain_two, axis=0)
    scaled_two = ffn_grad * gain_ffn
    resid_grad = cot_full + inv_two * (
        scaled_two - plain_two * jnp.mean(scaled_two * plain_two, axis=-1, keepdims=True)
    )
    resid_low = resid_grad.astype(jnp.bfloat16)
    out_part = jnp.einsum("rd,rh->dh", resid_low, attended, preferred_element_type=jnp.float32)
    att_grad = jnp.einsum(
        "rd,dh->rh", resid_low, out_weight, preferred_element_type=jnp.float32
    ).astype(jnp.bfloat16)
    att_heads = att_grad.reshape(tok_rows, KV_HEADS, group, HEAD)
    row_delta = jnp.sum(
        att_heads.astype(jnp.float32)
        * attended.reshape(tok_rows, KV_HEADS, group, HEAD).astype(jnp.float32),
        axis=-1,
    ).transpose(1, 2, 0)
    key_piece = lax.all_gather(keys, "context", axis=0, tiled=True)
    value_piece = lax.all_gather(values, "context", axis=0, tiled=True)
    scores, visible = key_scores(key_piece)
    soft = jnp.exp(scores - log_total[..., None])
    prob_grad = jnp.einsum(
        "qkgd,skd->kgqs", att_heads, value_piece, preferred_element_type=jnp.float32
    )
    score_grad = (soft * (prob_grad - row_delta[..., None])).astype(jnp.bfloat16)
    query_acc = jnp.einsum(
        "kgqs,skd->kgqd", score_grad, key_piece, preferred_element_type=jnp.float32
    )
    key_part = jnp.einsum("kgqs,qkgd->skd", score_grad, grouped, preferred_element_type=jnp.float32)
    value_part = jnp.einsum(
        "kgqs,qkgd->skd", soft.astype(jnp.bfloat16), att_heads, preferred_element_type=jnp.float32
    )
    pair_acc = jnp.stack([key_part, value_part], axis=1)
    query_acc, pair_acc = (query_acc, pair_acc)
    own_pairs = lax.psum_scatter(
        pair_acc.astype(jnp.bfloat16), "context", scatter_dimension=0, tiled=True
    ).astype(jnp.float32)
    query_grad = (
        unrotate(query_acc.transpose(2, 0, 1, 3).reshape(tok_rows, HEADS, HEAD), cosine, sine)
        * scale
    )
    key_grad = unrotate(own_pairs[:, 0], cosine, sine)
    mixed_grad = jnp.concatenate(
        [
            query_grad.reshape(tok_rows, q_cols),
            key_grad.reshape(tok_rows, kv_cols),
            own_pairs[:, 1].reshape(tok_rows, kv_cols),
        ],
        axis=-1,
    ).astype(jnp.bfloat16)
    qkv_part = jnp.einsum("rd,rc->dc", normed, mixed_grad, preferred_element_type=jnp.float32)
    norm_grad = jnp.einsum("rc,dc->rd", mixed_grad, qkv_weight, preferred_element_type=jnp.float32)
    gain_attn_part = jnp.sum(norm_grad * plain_one, axis=0)
    scaled_one = norm_grad * gain_attn
    input_grad = (
        resid_grad
        + inv_one
        * (scaled_one - plain_one * jnp.mean(scaled_one * plain_one, axis=-1, keepdims=True))
    ).astype(jnp.bfloat16)
    gain_attn_grad, qkv_grad, out_proj_grad, gain_ffn_grad, router_grad = (
        lax.psum_scatter(
            gain_attn_part, ("expert", "context", "dp"), scatter_dimension=0, tiled=True
        ),
        lax.psum_scatter(qkv_part, ("expert", "context", "dp"), scatter_dimension=0, tiled=True),
        lax.psum_scatter(out_part, ("expert", "context", "dp"), scatter_dimension=0, tiled=True),
        lax.psum_scatter(
            gain_ffn_part, ("expert", "context", "dp"), scatter_dimension=0, tiled=True
        ),
        lax.psum_scatter(router_part, ("expert", "context", "dp"), scatter_dimension=0, tiled=True),
    )
    return (
        output[None],
        input_grad[None],
        gain_attn_grad,
        qkv_grad,
        out_proj_grad,
        gain_ffn_grad,
        router_grad,
        expert_in,
        expert_down,
    )


def solution(mesh):
    in_specs = (
        P(("expert", "dp"), "context", None),
        P(("expert", "dp"), None),
        P(("expert", "dp"), "context", None),
        P(("expert", "dp"), "context", None),
        P(),
        P(),
        P(),
        P(),
        P(),
        P("expert", None, None),
        P("expert", None, None),
        P(("expert", "dp"), "context", None),
    )
    out_specs = (
        P(("expert", "dp"), "context", None),
        P(("expert", "dp"), "context", None),
        P(("expert", "context", "dp")),
        P(("expert", "context", "dp"), None),
        P(("expert", "context", "dp"), None),
        P(("expert", "context", "dp")),
        P(("expert", "context", "dp"), None),
        P("expert", ("context", "dp"), None),
        P("expert", ("context", "dp"), None),
    )
    tuned = dict(mesh.shape) == {"expert": 2, "context": 4, "dp": 4}
    body = local if tuned else general
    return jax.shard_map(body, mesh=mesh, in_specs=in_specs, out_specs=out_specs, check_vma=False)
```
